32 devices in a mesh: section: 2 (over x), row: 4 (over z), col: 4 (over y, core).
Axes of the slice: x: 2, y: 2, z: 4, core: 2. Of those that a mesh axis runs over, the one named last changes fastest.
Arguments:
- tokens: bfloat16 [8192, 1280], P('row', 'col'), may hold values from -6 to 6
- cotangent: bfloat16 [8192, 1280], P('row', 'col'), may hold values from -6 to 6
- first_gain: bfloat16 [2, 1280], P('section', 'col'), may hold values from 0.5 to 1.5
- first_shift: bfloat16 [2, 1280], P('section', 'col'), may hold values from -1.1953125 to 1.1953125
- attend_weight: bfloat16 [2, 1280, 3, 1280], P('section', 'row', None, 'col'), may hold values from -0.15625 to 0.15625
- attend_bias: bfloat16 [2, 2, 1280], P('section', None, 'col'), may hold values from -1.1953125 to 1.1953125
- output_weight: bfloat16 [2, 1280, 1280], P('section', 'col', 'row'), may hold values from -2.5 to 2.5
- output_bias: bfloat16 [2, 1280], P('section', 'col'), may hold values from -1.1953125 to 1.1953125
- second_gain: bfloat16 [2, 1280], P('section', 'col'), may hold values from 0.5 to 1.5
- second_shift: bfloat16 [2, 1280], P('section', 'col'), may hold values from -1.1953125 to 1.1953125
- expand_weight: bfloat16 [2, 1280, 5120], P('section', 'row', 'col'), may hold values from -0.15625 to 0.15625
- expand_bias: bfloat16 [2, 5120], P('section', 'col'), may hold values from -1.1953125 to 1.1953125
- contract_weight: bfloat16 [2, 5120, 1280], P('section', 'col', 'row'), may hold values from -0.078125 to 0.078125
- contract_bias: bfloat16 [2, 1280], P('section', 'col'), may hold values from -1.1953125 to 1.1953125
Outputs:
- layer_outputs: bfloat16 [2, 8192, 1280], P('section', 'row', 'col')
- input_grads: float32 [2, 8192, 1280], P('section', 'row', 'col')
- grad_first_gain: float32 [2, 1280], P('section', 'col')
- grad_first_shift: float32 [2, 1280], P('section', 'col')
- grad_attend_weight: float32 [2, 1280, 3, 1280], P('section', 'row', None, 'col')
- grad_attend_bias: float32 [2, 2, 1280], P('section', None, 'col')
- grad_output_weight: float32 [2, 1280, 1280], P('section', 'col', 'row')
- grad_output_bias: float32 [2, 1280], P('section', 'col')
- grad_second_gain: float32 [2, 1280], P('section', 'col')
- grad_second_shift: float32 [2, 1280], P('section', 'col')
- grad_expand_weight: float32 [2, 1280, 5120], P('section', 'row', 'col')
- grad_expand_bias: float32 [2, 5120], P('section', 'col')
- grad_contract_weight: float32 [2, 5120, 1280], P('section', 'col', 'row')
- grad_contract_bias: float32 [2, 1280], P('section', 'col')
The draws below stay inside these ranges and needn't reach their ends.
All inputs are finite; a program needn't handle non-finite values.
Results may differ from the reference program's by a relative error of at most 0.019.
Values may be sent and summed in bfloat16 or wider, within the bound.
A program may use at most 256 MiB of HBM per device.

```python
import jax
import jax.numpy as jnp
from jax import lax

D = 1280
HEADS = 20
HEAD = 64
FF = 5120
LENGTH = 1024
TOKENS = 8192
N_SECTION = 2


def steps_of(stream_key, shape, pieces, smallest, high):
    level, own = 1.0, jax.random.fold_in(stream_key, 6)
    for position, blocks in pieces:
        draws = jnp.exp(jax.random.uniform(jax.random.fold_in(own, position), (blocks,), jnp.float32, smallest / len(pieces), high / len(pieces)))
        level = level * jnp.repeat(draws, shape[position] // blocks).reshape([-1 if axis == position else 1 for axis in range(len(shape))])
    return level


def noise(key, extent, scale, most, shards=(), kind=jnp.bfloat16):
    loudness = steps_of(key, extent, shards, -0.22, 0.18) if shards else 1.0
    values = jax.random.normal(key, extent, jnp.float32) * scale * loudness
    return jnp.minimum(jnp.maximum(values, -most), most).astype(kind)


def setup_inputs(seed: int = 0) -> dict:
    splits = jax.random.split(jax.random.key(seed), 15)
    return {
        "tokens": noise(splits[0], (TOKENS, D), 1.0, 6.0, ((0, 4), (1, 4))),
        "cotangent": noise(splits[1], (TOKENS, D), 1.0, 6.0, ((0, 4), (1, 4))),
        "first_gain": jnp.clip(1.0 + 0.1 * jax.random.normal(splits[2], (N_SECTION, D), jnp.float32), 0.5, 1.5).astype(jnp.bfloat16),
        "first_shift": noise(splits[3], (N_SECTION, D), 0.2, 1.1953125, ((0, 2), (1, 4))),
        "attend_weight": noise(splits[4], (N_SECTION, D, 3, D), D ** -0.5, 0.15625, ((0, 2), (1, 4), (3, 4))),
        "attend_bias": noise(splits[5], (N_SECTION, 2, D), 0.2, 1.1953125, ((0, 2), (2, 4))),
        "output_weight": noise(splits[6], (N_SECTION, D, D), (D * 4 // LENGTH) ** -0.5, 2.5, ((0, 2), (1, 4), (2, 4))),
        "output_bias": noise(splits[7], (N_SECTION, D), 0.2, 1.1953125, ((0, 2), (1, 4))),
        "second_gain": jnp.clip(1.0 + 0.1 * jax.random.normal(splits[8], (N_SECTION, D), jnp.float32), 0.5, 1.5).astype(jnp.bfloat16),
        "second_shift": noise(splits[9], (N_SECTION, D), 0.2, 1.1953125, ((0, 2), (1, 4))),
        "expand_weight": noise(splits[10], (N_SECTION, D, FF), D ** -0.5, 0.15625, ((0, 2), (1, 4), (2, 4))),
        "expand_bias": noise(splits[11], (N_SECTION, FF), 0.2, 1.1953125, ((0, 2), (1, 4))),
        "contract_weight": noise(splits[12], (N_SECTION, FF, D), FF ** -0.5, 0.078125, ((0, 2), (1, 4), (2, 4))),
        "contract_bias": noise(splits[13], (N_SECTION, D), 0.2, 1.1953125, ((0, 2), (1, 4))),
    }


@jax.custom_vjp
def low(v):
    return lax.optimization_barrier(v.astype(jnp.bfloat16)).astype(jnp.float32)

@jax.custom_vjp
def low_back(v):
    return v

def low_keep(v):
    return (low(v), None)

def low_pass(kept, grad):
    return (grad,)

def back_keep(v):
    return (v, None)

def back_low(kept, grad):
    return (low(grad),)
low.defvjp(low_keep, low_pass)
low_back.defvjp(back_keep, back_low)
eps = 1e-05

def matmul(left, right):
    return jnp.dot(left, right, precision=lax.Precision.HIGHEST)

def layer_norm(values, gain, shift):
    center = lax.optimization_barrier(jnp.mean(values, axis=-1, keepdims=True))
    spread = lax.optimization_barrier(jnp.mean(jnp.square(values - center), axis=-1, keepdims=True))
    return (values - center) * lax.rsqrt(spread + eps) * gain + shift

def gelu(values):
    return 0.5 * values * (1.0 + jnp.tanh(0.7978845608028654 * (values + 0.044715 * values * values * values)))

def attend(triple):
    query_heads, key_heads, value_heads = triple
    scores = jnp.einsum('qhd,khd->hqk', query_heads, key_heads, precision=lax.Precision.HIGHEST) * HEAD ** (-0.5)
    scores = low_back(scores)
    length = scores.shape[1]
    causal = lax.broadcasted_iota(jnp.int32, (length, length), 0) >= lax.broadcasted_iota(jnp.int32, (length, length), 1)
    scores = jnp.where(causal[None], scores, -1000000000.0)
    probs = low(jax.nn.softmax(scores, axis=-1))
    return jnp.einsum('hqk,khd->qhd', probs, value_heads, precision=lax.Precision.HIGHEST)

def layer(inputs, first_gain, first_shift, attend_weight, attend_bias, output_weight, output_bias, second_gain, second_shift, expand_weight, expand_bias, contract_weight, contract_bias):
    normed = low(layer_norm(inputs, first_gain, first_shift))
    queries = low_back(low(matmul(normed, attend_weight[:, 0]) + attend_bias[0]))
    key_rows = low_back(low(matmul(normed, attend_weight[:, 1])))
    value_rows = low_back(low(matmul(normed, attend_weight[:, 2]) + attend_bias[1]))
    shaped = (-1, LENGTH, HEADS, HEAD)
    mixed = lax.map(jax.checkpoint(attend), (queries.reshape(shaped), key_rows.reshape(shaped), value_rows.reshape(shaped)))
    mixed = low_back(low(mixed.reshape(inputs.shape)))
    hidden = inputs + low_back(matmul(mixed, output_weight)) + output_bias
    second = low(layer_norm(hidden, second_gain, second_shift))
    before = low_back(matmul(second, expand_weight) + expand_bias)
    activated = low(gelu(before))
    return hidden + low_back(matmul(activated, contract_weight)) + contract_bias

def reference(tokens, cotangent, first_gain, first_shift, attend_weight, attend_bias, output_weight, output_bias, second_gain, second_shift, expand_weight, expand_bias, contract_weight, contract_bias):
    params = [member.astype(jnp.float32) for member in (first_gain, first_shift, attend_weight, attend_bias, output_weight, output_bias, second_gain, second_shift, expand_weight, expand_bias, contract_weight, contract_bias)]
    inputs = tokens.astype(jnp.float32)
    probe = jnp.zeros_like(inputs)

    def forward(layer_input, probe_input, *weights):
        first_out = layer(layer_input, *[member[0] for member in weights])
        sent = low_back(low(first_out))
        second_out = layer(sent + probe_input, *[member[1] for member in weights])
        return (second_out, first_out)
    result, pullback, first_out = jax.vjp(forward, inputs, probe, *params, has_aux=True)
    grads = pullback(cotangent.astype(jnp.float32))
    layer_outputs = jnp.stack([first_out, result]).astype(jnp.bfloat16)
    input_grads = jnp.stack([grads[0], grads[1]])
    return (layer_outputs, input_grads, grads[2], grads[3], grads[4], grads[5], grads[6], grads[7], grads[8], grads[9], grads[10], grads[11], grads[12], grads[13])
```

```python
import jax
import jax.numpy as jnp
from jax import lax
from jax.sharding import PartitionSpec as P

HEAD = 64
LENGTH = 1024
EPS = 1e-05
LOW = jnp.bfloat16
WIDE = jnp.float32


def gelu(t):
    return 0.5 * t * (1.0 + jnp.tanh(0.7978845608028654 * (t + 0.044715 * t * t * t)))


def nn(left, right):
    return jnp.dot(left, right, preferred_element_type=WIDE)


def nt(left, right):
    return lax.dot_general(left, right, (((1,), (1,)), ((), ())), preferred_element_type=WIDE)


def tn(left, right):
    return lax.dot_general(left, right, (((0,), (0,)), ((), ())), preferred_element_type=WIDE)


def gather_rows(own):
    return lax.all_gather(own, "col", axis=0, tiled=True)


def scatter_rows(partial):
    return lax.psum_scatter(
        partial.astype(LOW), "col", scatter_dimension=0, tiled=True
    ).astype(WIDE)


def swap_sections(value):
    return lax.ppermute(value, "section", [(0, 1), (1, 0)])


def normalise(values):
    center = jnp.mean(values, axis=1, keepdims=True)
    centred = values - center
    scale = lax.rsqrt(jnp.mean(centred * centred, axis=1, keepdims=True) + EPS)
    return centred * scale, scale


def norm_backward(grad, hat, scale, gain):
    scaled = grad * gain
    mean_one = jnp.mean(scaled, axis=1, keepdims=True)
    mean_two = jnp.mean(scaled * hat, axis=1, keepdims=True)
    return (
        scale * (scaled - mean_one - hat * mean_two),
        jnp.sum(grad * hat, axis=0),
        jnp.sum(grad, axis=0),
    )


def split_heads(values):
    return values.reshape(values.shape[0], values.shape[1] // HEAD, HEAD)


def block_scores(query_heads, key_heads, begin, finish):
    scores = jnp.einsum(
        "qhd,khd->hqk",
        query_heads[begin:finish],
        key_heads[:finish],
        preferred_element_type=WIDE,
    ) * HEAD ** (-0.5)
    rows = begin + lax.broadcasted_iota(jnp.int32, (finish - begin, finish), 0)
    cols = lax.broadcasted_iota(jnp.int32, (finish - begin, finish), 1)
    return jnp.where((rows >= cols)[None], scores, -1000000000.0)


def attention_forward(queries, keys, values):
    length = queries.shape[0]
    block = min(512, length)
    qh, kh, vh = split_heads(queries), split_heads(keys), split_heads(values)
    outputs, totals = [], []
    for begin in range(0, length, block):
        finish = begin + block
        scores = block_scores(qh, kh, begin, finish)
        highest = jnp.max(scores, axis=-1, keepdims=True)
        powers = jnp.exp(scores - highest)
        summed = jnp.sum(powers, axis=-1, keepdims=True)
        probs = (powers / summed).astype(LOW)
        outputs.append(
            jnp.einsum("hqk,khd->qhd", probs, vh[:finish], preferred_element_type=WIDE)
        )
        totals.append((highest + jnp.log(summed))[:, :, 0])
    return (
        jnp.concatenate(outputs, 0).astype(LOW).reshape(length, -1),
        jnp.concatenate(totals, 1),
    )


def attention_backward(queries, keys, values, totals, grad):
    length = queries.shape[0]
    block = min(512, length)
    qh, kh, vh = split_heads(queries), split_heads(keys), split_heads(values)
    gh = split_heads(grad)
    query_grads = []
    key_grad = jnp.zeros(kh.shape, WIDE)
    value_grad = jnp.zeros(vh.shape, WIDE)
    for begin in range(0, length, block):
        finish = begin + block
        scores = block_scores(qh, kh, begin, finish)
        probs = jnp.exp(scores - totals[:, begin:finish, None])
        grad_probs = jnp.einsum(
            "qhd,khd->hqk", gh[begin:finish], vh[:finish], preferred_element_type=WIDE
        )
        grad_scores = (
            probs
            * (grad_probs - jnp.sum(probs * grad_probs, axis=-1, keepdims=True))
            * HEAD ** (-0.5)
        ).astype(LOW)
        query_grads.append(
            jnp.einsum("hqk,khd->qhd", grad_scores, kh[:finish], preferred_element_type=WIDE)
        )
        padding = ((0, length - finish), (0, 0), (0, 0))
        key_grad = key_grad + jnp.pad(
            jnp.einsum(
                "hqk,qhd->khd", grad_scores, qh[begin:finish], preferred_element_type=WIDE
            ),
            padding,
        )
        value_grad = value_grad + jnp.pad(
            jnp.einsum(
                "hqk,qhd->khd", probs.astype(LOW), gh[begin:finish], preferred_element_type=WIDE
            ),
            padding,
        )
    return (
        jnp.concatenate(query_grads, 0).astype(LOW).reshape(length, -1),
        key_grad.astype(LOW).reshape(length, -1),
        value_grad.astype(LOW).reshape(length, -1),
    )


def layer_forward(x_full, x_own, small, mats):
    attend, out_t, expand, contract_t = mats
    width = out_t.shape[1]
    hat, _ = normalise(x_full.astype(WIDE))
    normed = (hat * small["gain_one"] + small["shift_one"]).astype(LOW)
    projected = nn(normed, attend)
    queries = (projected[:, :width] + small["query_bias"]).astype(LOW)
    keys = projected[:, width : 2 * width].astype(LOW)
    values = (projected[:, 2 * width :] + small["value_bias"]).astype(LOW)
    attended, totals = attention_forward(queries, keys, values)
    hidden = x_own + scatter_rows(nt(attended, out_t)) + small["out_bias"]
    hat_two, scale_two = normalise(hidden)
    second_own = (hat_two * small["gain_two"] + small["shift_two"]).astype(LOW)
    second = gather_rows(second_own)
    before = nn(second, expand) + small["expand_bias"]
    active = gelu(before).astype(LOW)
    result = hidden + scatter_rows(nt(active, contract_t)) + small["contract_bias"]
    kept = (normed, queries, keys, values, attended, totals, hat_two, scale_two, second, before, active)
    return result, kept


def layer_backward(grad_full, grad_own, x_own, kept, small, mats):
    attend, out_t, expand, contract_t = mats
    normed, queries, keys, values, attended, totals, hat_two, scale_two, second, before, active = kept
    grad_active = nn(grad_full, contract_t)
    contract_grad = tn(grad_full, active).astype(LOW)
    contract_bias_grad = jnp.sum(grad_own, axis=0)
    _, pullback = jax.vjp(gelu, before)
    grad_before = pullback(grad_active)[0].astype(LOW)
    expand_grad = tn(second, grad_before).astype(LOW)
    expand_bias_grad = jnp.sum(grad_before.astype(WIDE), axis=0)
    grad_second = scatter_rows(nt(grad_before, expand))
    through, gain_two_grad, shift_two_grad = norm_backward(
        grad_second, hat_two, scale_two, small["gain_two"]
    )
    grad_hidden = grad_own + through
    hidden_full = gather_rows(grad_hidden.astype(LOW))
    out_grad = tn(hidden_full, attended).astype(LOW)
    out_bias_grad = jnp.sum(grad_hidden, axis=0)
    grad_attended = nn(hidden_full, out_t).astype(LOW)
    gq, gk, gv = attention_backward(queries, keys, values, totals, grad_attended)
    mixed = jnp.concatenate([gq, gk, gv], 1)
    attend_grad = tn(normed, mixed).astype(LOW)
    attend_bias_grad = jnp.stack(
        [jnp.sum(gq.astype(WIDE), axis=0), jnp.sum(gv.astype(WIDE), axis=0)]
    )
    grad_first = scatter_rows(nt(mixed, attend))
    hat, scale = normalise(x_own)
    through, gain_one_grad, shift_one_grad = norm_backward(
        grad_first, hat, scale, small["gain_one"]
    )
    grad_input = grad_hidden + through
    wide_vectors = jnp.stack(
        [
            gain_one_grad,
            shift_one_grad,
            out_bias_grad,
            gain_two_grad,
            shift_two_grad,
            contract_bias_grad,
        ]
    )
    own_vectors = (attend_bias_grad, expand_bias_grad)
    return grad_input, (attend_grad, out_grad, expand_grad, contract_grad), wide_vectors, own_vectors


def on_device(
    tokens,
    cotangent,
    first_gain,
    first_shift,
    attend_weight,
    attend_bias,
    output_weight,
    output_bias,
    second_gain,
    second_shift,
    expand_weight,
    expand_bias,
    contract_weight,
    contract_bias,
):
    section = lax.axis_index("section")
    column = lax.axis_index("col")
    first_section = section == 0
    columns = lax.axis_size("col")
    width = tokens.shape[1]
    rows = LENGTH // columns
    hidden_width = expand_bias.shape[1]

    def pick(early, later):
        return jnp.where(first_section, early, later)

    def both(own):
        other = swap_sections(own)
        return pick(own, other), pick(other, own)

    packed = jnp.concatenate(
        [
            first_gain[0],
            first_shift[0],
            output_bias[0],
            second_gain[0],
            second_shift[0],
            contract_bias[0],
        ]
    )
    wide_small = lax.all_gather(packed, ("section", "col"), axis=0, tiled=False)
    wide_small = wide_small.reshape(2, columns, 6, width).astype(WIDE)
    wide_small = jnp.swapaxes(wide_small, 1, 2).reshape(2, 6, columns * width)
    own_small = both(
        jnp.concatenate([attend_bias[0, 0], attend_bias[0, 1], expand_bias[0]]).astype(WIDE)
    )
    small = []
    for layer in range(2):
        names = ("gain_one", "shift_one", "out_bias", "gain_two", "shift_two", "contract_bias")
        entry = {name: wide_small[layer, i] for i, name in enumerate(names)}
        entry["query_bias"] = own_small[layer][:width]
        entry["value_bias"] = own_small[layer][width : 2 * width]
        entry["expand_bias"] = own_small[layer][2 * width :]
        small.append(entry)

    x0_full = lax.all_gather(
        lax.dynamic_slice_in_dim(tokens, section * LENGTH, LENGTH, 0), "col", axis=1, tiled=True
    )
    gy_full = lax.all_gather(
        lax.dynamic_slice_in_dim(cotangent, section * LENGTH, LENGTH, 0), "col", axis=1, tiled=True
    )

    def fetch(block):
        own = lax.all_gather(block, "row", axis=0, tiled=True)
        return both(own)

    block_rows = attend_weight.shape[1]
    attend = fetch(attend_weight[0].reshape(block_rows, -1))
    out_t = fetch(output_weight[0].T)
    expand = fetch(expand_weight[0])
    contract_t = fetch(contract_weight[0].T)
    mats = [(attend[i], out_t[i], expand[i], contract_t[i]) for i in range(2)]

    def own_rows(full):
        return lax.dynamic_slice_in_dim(full, column * rows, rows, 0).astype(WIDE)

    def own_features(full):
        return lax.dynamic_slice_in_dim(full, column * width, width, 1)

    x0_own = own_rows(x0_full)
    y0, kept0 = layer_forward(x0_full, x0_own, small[0], mats[0])
    y0_low = y0.astype(LOW)
    x1_full = gather_rows(y0_low)
    x1_own = y0_low.astype(WIDE)
    y1, kept1 = layer_forward(x1_full, x1_own, small[1], mats[1])
    y1_full = gather_rows(y1.astype(LOW))

    gx1, mat_grads1, wide1, own1 = layer_backward(
        gy_full, own_rows(gy_full), x1_own, kept1, small[1], mats[1]
    )
    gx1_low = gx1.astype(LOW)
    gx1_full = gather_rows(gx1_low)
    gx0, mat_grads0, wide0, own0 = layer_backward(
        gx1_full, gx1_low.astype(WIDE), x0_own, kept0, small[0], mats[0]
    )
    gx0_full = gather_rows(gx0.astype(LOW))

    def to_sections(layer0, layer1):
        kept = pick(layer0, layer1)
        got = swap_sections(pick(layer1, layer0))
        return jnp.concatenate([pick(kept, got), pick(got, kept)], 0)

    layer_outputs = to_sections(own_features(x1_full), own_features(y1_full))
    input_grads = to_sections(own_features(gx0_full), own_features(gx1_full)).astype(WIDE)

    def reduce_grad(layer0, layer1):
        kept = pick(layer0, layer1)
        got = swap_sections(pick(layer1, layer0))
        total = (kept.astype(WIDE) + got.astype(WIDE)).astype(LOW)
        return lax.psum_scatter(total, "row", scatter_dimension=0, tiled=True).astype(WIDE)

    attend_part, out_part, expand_part, contract_part = [
        reduce_grad(a, b) for a, b in zip(mat_grads0, mat_grads1)
    ]

    wide_sum = lax.psum(jnp.stack([wide0, wide1]), ("section", "row", "col"))
    own_sum = lax.psum(
        jnp.stack([jnp.concatenate([a.reshape(-1), b]) for a, b in (own0, own1)]),
        ("section", "row"),
    )
    wide_mine = lax.dynamic_slice_in_dim(pick(wide_sum[0], wide_sum[1]), column * width, width, 1)
    own_mine = pick(own_sum[0], own_sum[1])
    return (
        layer_outputs[None],
        input_grads[None],
        wide_mine[0][None],
        wide_mine[1][None],
        attend_part.reshape(block_rows, 3, width)[None],
        own_mine[: 2 * width].reshape(1, 2, width),
        out_part.T[None],
        wide_mine[2][None],
        wide_mine[3][None],
        wide_mine[4][None],
        expand_part[None],
        own_mine[2 * width :][None],
        contract_part.T[None],
        wide_mine[5][None],
    )


def solution(mesh):
    return jax.shard_map(
        on_device,
        mesh=mesh,
        in_specs=(
            P("row", "col"),
            P("row", "col"),
            P("section", "col"),
            P("section", "col"),
            P("section", "row", None, "col"),
            P("section", None, "col"),
            P("section", "col", "row"),
            P("section", "col"),
            P("section", "col"),
            P("section", "col"),
            P("section", "row", "col"),
            P("section", "col"),
            P("section", "col", "row"),
            P("section", "col"),
        ),
        out_specs=(
            P("section", "row", "col"),
            P("section", "row", "col"),
            P("section", "col"),
            P("section", "col"),
            P("section", "row", None, "col"),
            P("section", None, "col"),
            P("section", "col", "row"),
            P("section", "col"),
            P("section", "col"),
            P("section", "col"),
            P("section", "row", "col"),
            P("section", "col"),
            P("section", "col", "row"),
            P("section", "col"),
        ),
        check_vma=False,
    )
```

```python
import functools

import jax
import jax.numpy as jnp
from jax import lax
from jax.experimental import pallas as pl
from jax.experimental.pallas import tpu as pltpu
from jax.sharding import PartitionSpec as P

HEAD = 64
LENGTH = 1024
EPS = 1e-05
LOW = jnp.bfloat16
WIDE = jnp.float32
MESH = pl.DeviceIdType.MESH
PARTS = 2
TILE = 256
MEBI = 1024 * 1024


def nn(left, right):
    return lax.dot_general(left, right, (((1,), (0,)), ((), ())), preferred_element_type=WIDE)


def nt(left, right):
    return lax.dot_general(left, right, (((1,), (1,)), ((), ())), preferred_element_type=WIDE)


def tn(left, right):
    return lax.dot_general(left, right, (((0,), (0,)), ((), ())), preferred_element_type=WIDE)


def normalise(values):
    center = jnp.mean(values, axis=1, keepdims=True)
    centred = values - center
    scale = lax.rsqrt(jnp.mean(centred * centred, axis=1, keepdims=True) + EPS)
    return centred * scale, scale


def norm_backward(grad, hat, scale, gain):
    scaled = grad * gain
    mean_one = jnp.mean(scaled, axis=1, keepdims=True)
    mean_two = jnp.mean(scaled * hat, axis=1, keepdims=True)
    return scale * (scaled - mean_one - hat * mean_two)


class Group:
    def __init__(self, rows):
        self.me = lax.axis_index("col")
        chip, core = self.me // 2, self.me % 2
        self.sib = chip * 2 + 1 - core
        self.peer = (1 - chip) * 2 + core
        self.diag = (1 - chip) * 2 + 1 - core
        self.rows = rows
        self.part = rows // PARTS

    def greet(self):
        barrier = pltpu.get_barrier_semaphore()
        for other in (self.sib, self.peer):
            pl.semaphore_signal(barrier, inc=1, device_id={"col": other}, device_id_type=MESH)
        pl.semaphore_wait(barrier, 2)

    def slab(self, owner, j):
        return pl.ds(pl.multiple_of(owner * self.rows + j * self.part, self.part), self.part)

    def chunk(self, owner):
        return pl.ds(pl.multiple_of(owner * self.rows, self.rows), self.rows)


def push(src, dst, sems, slot, target):
    return pltpu.make_async_remote_copy(
        src_ref=src,
        dst_ref=dst,
        send_sem=sems.at[0, slot],
        recv_sem=sems.at[1, slot],
        device_id={"col": target},
        device_id_type=MESH,
    )


class Gather:
    def __init__(self, group, full, sems):
        self.group, self.full, self.sems = group, full, sems

    def start(self):
        g = self.group
        self.over, self.near, self.relayed = [], [], []
        for j in range(PARTS):
            piece = self.full.at[g.slab(g.me, j)]
            self.over.append(push(piece, piece, self.sems, j, g.peer))
            self.over[-1].start()
        for j in range(PARTS):
            piece = self.full.at[g.slab(g.me, j)]
            self.near.append(push(piece, piece, self.sems, PARTS + j, g.sib))
            self.near[-1].start()

    def sibling(self):
        for copy in self.near:
            copy.wait_recv()

    def relay(self):
        g = self.group
        for j in range(PARTS):
            self.over[j].wait_recv()
            piece = self.full.at[g.slab(g.peer, j)]
            self.relayed.append(push(piece, piece, self.sems, 2 * PARTS + j, g.sib))
            self.relayed[-1].start()

    def diagonal(self):
        for copy in self.relayed:
            copy.wait_recv()

    def done(self):
        for copy in self.over + self.near + self.relayed:
            copy.wait_send()

    def each(self, body):
        g = self.group
        self.start()
        body(g.chunk(g.me))
        self.sibling()
        body(g.chunk(g.sib))
        self.relay()
        body(g.chunk(g.peer))
        self.diagonal()
        body(g.chunk(g.diag))
        self.done()


class Scatter:
    def __init__(self, group, stage, land, total, sems):
        self.group, self.stage, self.land, self.total, self.sems = group, stage, land, total, sems

    def start(self, part):
        g, stage, land = self.group, self.stage, self.land
        self.first, self.over, self.near = [], [], []
        for j in range(PARTS):
            stage[0, j] = part(g.slab(g.diag, j)).astype(LOW)
            self.first.append(push(stage.at[0, j], land.at[0, j], self.sems, j, g.sib))
            self.first[-1].start()
        for j in range(PARTS):
            mine = part(g.slab(g.peer, j))
            self.first[j].wait_recv()
            stage[1, j] = (mine + land[0, j].astype(WIDE)).astype(LOW)
            self.over.append(push(stage.at[1, j], land.at[1, j], self.sems, PARTS + j, g.peer))
            self.over[-1].start()
        for j in range(PARTS):
            stage[2, j] = part(g.slab(g.sib, j)).astype(LOW)
            self.near.append(push(stage.at[2, j], land.at[2, j], self.sems, 2 * PARTS + j, g.sib))
            self.near[-1].start()
        for j in range(PARTS):
            self.total[j] = part(g.slab(g.me, j))

    def take(self, j):
        self.near[j].wait_recv()
        self.over[j].wait_recv()
        land = self.land
        return self.total[j] + (land[1, j].astype(WIDE) + land[2, j].astype(WIDE))

    def done(self):
        for copy in self.first + self.over + self.near:
            copy.wait_send()


def scatter_scratch(rows, width):
    part = rows // PARTS
    return [
        pltpu.VMEM((3, PARTS, part, width), LOW),
        pltpu.VMEM((3, PARTS, part, width), LOW),
        pltpu.VMEM((PARTS, part, width), WIDE),
        pltpu.SemaphoreType.DMA((2, 3 * PARTS)),
    ]


class Halves:
    def __init__(self, pair, whole, sems, slot):
        section = lax.axis_index("section")
        half = whole.shape[1] // 2
        self.copies = []
        for n, place in enumerate((section, 1 - section)):
            columns = pl.ds(pl.multiple_of(place * half, half), half)
            self.copies.append(
                pltpu.make_async_copy(pair[n], whole.at[:, columns], sems.at[slot + n])
            )

    def start(self):
        for copy in self.copies:
            copy.start()

    def wait(self):
        for copy in self.copies:
            copy.wait()


def attention_out(heads_ref, o3, lse_ref, heads):
    length = heads_ref.shape[1]
    size = min(TILE, length)

    @pl.loop(0, heads)
    def _(h):
        for i in range(length // size):
            rows = slice(i * size, (i + 1) * size)
            finish = (i + 1) * size
            queries = heads_ref[h, rows, :]
            scores = nt(heads_ref[heads + h, :finish, :], queries)
            keep = lax.broadcasted_iota(jnp.int32, (size, size), 0) <= lax.broadcasted_iota(
                jnp.int32, (size, size), 1
            )
            last = jnp.where(keep, scores[finish - size :], -1000000000.0)
            scores = last if i == 0 else jnp.concatenate([scores[: finish - size], last], 0)
            highest = jnp.max(scores, axis=0, keepdims=True)
            powers = jnp.exp(scores - highest)
            summed = jnp.sum(powers, axis=0, keepdims=True)
            mixed = tn(heads_ref[2 * heads + h, :finish, :], powers.astype(LOW))
            o3[h, rows, :] = (mixed / summed).T.astype(LOW)
            lse_ref[pl.ds(h, 1), rows] = highest + jnp.log(summed)


def attention_back(heads_ref, go3, lse_ref, dots_ref, g3, key_acc, value_acc, heads):
    length = heads_ref.shape[1]
    size = min(TILE, length)

    @pl.loop(0, heads)
    def _(h):
        for i in reversed(range(length // size)):
            rows = slice(i * size, (i + 1) * size)
            finish = (i + 1) * size
            queries = heads_ref[h, rows, :]
            keys = heads_ref[heads + h, :finish, :]
            grads = go3[h, rows, :]
            scores = nt(keys, queries) - lse_ref[pl.ds(h, 1), rows]
            keep = lax.broadcasted_iota(jnp.int32, (size, size), 0) <= lax.broadcasted_iota(
                jnp.int32, (size, size), 1
            )
            last = jnp.where(keep, scores[finish - size :], -1000000000.0)
            scores = last if i == 0 else jnp.concatenate([scores[: finish - size], last], 0)
            probs = jnp.exp(scores)
            grad_probs = nt(heads_ref[2 * heads + h, :finish, :], grads)
            grad_scores = (probs * (grad_probs - dots_ref[pl.ds(h, 1), rows])).astype(LOW)
            g3[h, rows, :] = (tn(grad_scores, keys) * HEAD ** (-0.5)).astype(LOW)
            key_part = nn(grad_scores, queries)
            value_part = nn(probs.astype(LOW), grads)
            if finish == length:
                key_acc[...] = key_part
                value_acc[...] = value_part
            else:
                key_acc[:finish, :] += key_part
                value_acc[:finish, :] += value_part
        g3[heads + h] = key_acc[...].astype(LOW)
        g3[2 * heads + h] = value_acc[...].astype(LOW)


def attend_kernel(
    gathered, heads, x_ref, mine_ref, other_ref, vec_ref, bias_ref,
    full_ref, normed_ref, heads_ref, o_ref, lse_ref, hidden_ref, second_ref,
    weight, o3, stage, land, total, scatter_sems, gather_sems, local_sems,
):
    width = o_ref.shape[1]
    group = Group(hidden_ref.shape[0])
    halves = Halves((mine_ref, other_ref), weight, local_sems, 0)
    halves.start()
    group.greet()
    if not gathered:
        full_ref[group.chunk(group.me), :] = x_ref[...]
    halves.wait()

    def project(rows):
        values = (x_ref if gathered else full_ref)[rows, :].astype(WIDE)
        hat, _ = normalise(values)
        normed = (hat * vec_ref[0:1, :] + vec_ref[1:2, :]).astype(LOW)
        normed_ref[rows, :] = normed
        mixed = nn(normed, weight[:, : 3 * width]) + bias_ref[...]
        for j in range(3 * heads):
            piece = mixed[:, j * HEAD : (j + 1) * HEAD]
            if j < heads:
                piece = piece * HEAD ** (-0.5)
            heads_ref[j, rows, :] = piece.astype(LOW)

    if gathered:
        full_ref[...] = jnp.zeros_like(full_ref)

        @pl.loop(0, LENGTH // group.rows)
        def _(n):
            project(group.chunk(n))
    else:
        Gather(group, full_ref, gather_sems).each(project)

    attention_out(heads_ref, o3, lse_ref, heads)
    for h in range(heads):
        o_ref[:, h * HEAD : (h + 1) * HEAD] = o3[h]

    scatter = Scatter(group, stage, land, total, scatter_sems)
    scatter.start(lambda rows: nt(o_ref[rows, :], weight[:, 3 * width :]))
    for j in range(PARTS):
        rows = slice(j * group.part, (j + 1) * group.part)
        residual = (x_ref if gathered else full_ref)[group.slab(group.me, j), :].astype(WIDE)
        hidden = residual + scatter.take(j) + vec_ref[2:3, :]
        hidden_ref[rows, :] = hidden
        hat, _ = normalise(hidden)
        second_ref[rows, :] = (hat * vec_ref[3:4, :] + vec_ref[4:5, :]).astype(LOW)
    scatter.done()


def expand_kernel(
    second_ref, hidden_ref, em_ref, eo_ref, cm_ref, co_ref, vec_ref, bias_ref,
    full_ref, active_ref, slope_ref, result_ref,
    expand, contract, stage, land, total, scatter_sems, gather_sems, local_sems,
):
    group = Group(hidden_ref.shape[0])
    first = Halves((em_ref, eo_ref), expand, local_sems, 0)
    then = Halves((cm_ref, co_ref), contract, local_sems, 2)
    first.start()
    then.start()
    group.greet()
    full_ref[group.chunk(group.me), :] = second_ref[...]
    first.wait()

    def widen(rows):
        t = nn(full_ref[rows, :], expand[...]) + bias_ref[...]
        square = t * t
        bent = jnp.tanh(0.7978845608028654 * t * (1.0 + 0.044715 * square))
        active_ref[rows, :] = (0.5 * t * (1.0 + bent)).astype(LOW)
        slope_ref[rows, :] = (
            0.5 * (1.0 + bent)
            + (0.5 * 0.7978845608028654) * t * (1.0 - bent * bent) * (1.0 + 3 * 0.044715 * square)
        ).astype(LOW)

    Gather(group, full_ref, gather_sems).each(widen)
    then.wait()
    scatter = Scatter(group, stage, land, total, scatter_sems)
    scatter.start(lambda rows: nt(active_ref[rows, :], contract[...]))
    for j in range(PARTS):
        rows = slice(j * group.part, (j + 1) * group.part)
        result = hidden_ref[rows, :] + scatter.take(j) + vec_ref[5:6, :]
        result_ref[rows, :] = result.astype(LOW)
    scatter.done()


def outer_halves(left_ref, right_ref, keep_ref, send_ref):
    section = lax.axis_index("section")
    half = right_ref.shape[1] // 2
    for place, out in ((section, keep_ref), (1 - section, send_ref)):
        columns = pl.ds(pl.multiple_of(place * half, half), half)

        @pl.loop(0, left_ref.shape[1] // TILE)
        def _(n):
            rows = pl.ds(pl.multiple_of(n * TILE, TILE), TILE)
            out[rows, :] = tn(left_ref[:, rows], right_ref[:, columns]).astype(LOW)


def expand_back_kernel(
    gathered, g_ref, em_ref, eo_ref, cm_ref, co_ref, active_ref, slope_ref, second_ref, hidden_ref, vec_ref,
    full_ref, ek_ref, es_ref, ck_ref, cs_ref, grad_ref, low_ref, sums_ref,
    expand, contract, before, stage, land, total, scatter_sems, gather_sems, local_sems,
):
    group = Group(hidden_ref.shape[0])
    first = Halves((cm_ref, co_ref), contract, local_sems, 0)
    then = Halves((em_ref, eo_ref), expand, local_sems, 2)
    first.start()
    then.start()
    group.greet()
    sums_ref[...] = jnp.zeros_like(sums_ref)
    if gathered:
        full_ref[...] = g_ref[...]
    else:
        full_ref[group.chunk(group.me), :] = g_ref[...]
    first.wait()

    def bend(rows):
        grad = (nn(full_ref[rows, :], contract[...]) * slope_ref[rows, :].astype(WIDE)).astype(LOW)
        before[rows, :] = grad
        sums_ref[4:5, :] += jnp.sum(grad.astype(WIDE), axis=0, keepdims=True)

    if gathered:

        @pl.loop(0, LENGTH // group.rows)
        def _(n):
            bend(group.chunk(n))
    else:
        Gather(group, full_ref, gather_sems).each(bend)
    then.wait()
    scatter = Scatter(group, stage, land, total, scatter_sems)
    scatter.start(lambda rows: nt(before[rows, :], expand[...]))
    outer_halves(full_ref, active_ref, ck_ref, cs_ref)
    outer_halves(second_ref, before, ek_ref, es_ref)
    for j in range(PARTS):
        rows = slice(j * group.part, (j + 1) * group.part)
        grad = scatter.take(j)
        hat, scale = normalise(hidden_ref[rows, :])
        own = full_ref[group.slab(group.me, j), :].astype(WIDE)
        out = own + norm_backward(grad, hat, scale, vec_ref[3:4, :])
        grad_ref[rows, :] = out
        low_ref[rows, :] = out.astype(LOW)
        for n, term in enumerate((grad * hat, grad, own, out)):
            sums_ref[n : n + 1, :] += jnp.sum(term, axis=0, keepdims=True)
    scatter.done()


def attend_back_kernel(
    heads, low_ref, grad_ref, x_ref, mine_ref, other_ref, normed_ref, heads_ref, o_ref, lse_ref, vec_ref,
    wk_ref, ws_ref, out_ref, sums_ref,
    weight, full, go3, dots, g3, key_acc, value_acc, mixed, outer,
    stage, land, total, scatter_sems, gather_sems, local_sems,
):
    width = o_ref.shape[1]
    group = Group(grad_ref.shape[0])
    section = lax.axis_index("section")
    halves = Halves((mine_ref, other_ref), weight, local_sems, 0)
    halves.start()
    group.greet()
    sums_ref[...] = jnp.zeros_like(sums_ref)
    full[group.chunk(group.me), :] = low_ref[...]
    halves.wait()
    picks = (
        lax.broadcasted_iota(jnp.int32, (8, width), 1) // HEAD
        == lax.broadcasted_iota(jnp.int32, (8, width), 0)
    ).astype(WIDE)

    def spread(rows):
        grads = nn(full[rows, :], weight[:, 3 * width :]).astype(LOW)
        for h in range(heads):
            go3[h, rows, :] = grads[:, h * HEAD : (h + 1) * HEAD]
        term = grads.astype(WIDE) * o_ref[rows, :].astype(WIDE)
        dots[:, rows] = lax.dot_general(
            picks,
            term,
            (((1,), (1,)), ((), ())),
            precision=lax.Precision.HIGHEST,
            preferred_element_type=WIDE,
        )

    Gather(group, full, gather_sems).each(spread)
    attention_back(heads_ref, go3, lse_ref, dots, g3, key_acc, value_acc, heads)
    for j in range(3 * heads):
        mixed[:, j * HEAD : (j + 1) * HEAD] = g3[j]

    scatter = Scatter(group, stage, land, total, scatter_sems)
    scatter.start(lambda rows: nt(mixed[rows, :], weight[:, : 3 * width]))

    half = weight.shape[1] // 2

    @pl.loop(0, weight.shape[0] // TILE)
    def _(n):
        rows = pl.ds(pl.multiple_of(n * TILE, TILE), TILE)
        outer[section, rows, :] = tn(normed_ref[:, rows], mixed[:, :half]).astype(LOW)
        outer[1 - section, rows, : 3 * width - half] = tn(
            normed_ref[:, rows], mixed[:, half:]
        ).astype(LOW)
        outer[1 - section, rows, 3 * width - half :] = tn(full[:, rows], o_ref[...]).astype(LOW)

    keep = pltpu.make_async_copy(outer.at[0], wk_ref, local_sems.at[2])
    send = pltpu.make_async_copy(outer.at[1], ws_ref, local_sems.at[3])
    keep.start()
    send.start()
    sums_ref[2:3, : 3 * width] = jnp.sum(mixed[...].astype(WIDE), axis=0, keepdims=True)
    for j in range(PARTS):
        rows = slice(j * group.part, (j + 1) * group.part)
        grad = scatter.take(j)
        hat, scale = normalise(x_ref[rows, :].astype(WIDE))
        out = grad_ref[rows, :] + norm_backward(grad, hat, scale, vec_ref[0:1, :])
        out_ref[rows, :] = out.astype(LOW)
        for n, term in enumerate((grad * hat, grad)):
            sums_ref[n : n + 1, :] += jnp.sum(term, axis=0, keepdims=True)
    scatter.done()
    keep.wait()
    send.wait()


VM = pl.BlockSpec(memory_space=pltpu.VMEM)
ANY = pl.BlockSpec(memory_space=pl.ANY)


def shape(dims, kind=LOW):
    return jax.ShapeDtypeStruct(dims, kind)


def launch(kernel, number, in_specs, outs, out_specs, scratch, flops):
    return pl.pallas_call(
        kernel,
        out_shape=outs,
        in_specs=in_specs,
        out_specs=out_specs,
        scratch_shapes=scratch,
        compiler_params=pltpu.CompilerParams(
            collective_id=number, has_side_effects=True, vmem_limit_bytes=56 * MEBI
        ),
        cost_estimate=pl.CostEstimate(
            flops=int(flops), bytes_accessed=30 * MEBI, transcendentals=0
        ),
    )


def attend_call(number, gathered, x, pair, vec, bias, rows, width):
    size = vec.shape[1]
    heads = width // HEAD
    outs = (
        shape((LENGTH, size) if not gathered else (16, 128)),
        shape((LENGTH, size)),
        shape((3 * heads, LENGTH, HEAD)),
        shape((LENGTH, width)),
        shape((8, LENGTH), WIDE),
        shape((rows, size), WIDE),
        shape((rows, size)),
    )
    scratch = [
        pltpu.VMEM((size, 4 * width), LOW),
        pltpu.VMEM((heads, LENGTH, HEAD), LOW),
        *scatter_scratch(rows, size),
        pltpu.SemaphoreType.DMA((2, 3 * PARTS)),
        pltpu.SemaphoreType.DMA((4,)),
    ]
    return launch(
        functools.partial(attend_kernel, gathered, heads),
        number, [VM, ANY, ANY, VM, VM], outs, (VM,) * 7, scratch, 3e10,
    )(x, *pair, vec, bias)


def expand_call(number, second, hidden, expand, contract, vec, bias):
    rows, size = hidden.shape
    wide = bias.shape[1]
    outs = (
        shape((LENGTH, size)),
        shape((LENGTH, wide)),
        shape((LENGTH, wide)),
        shape((rows, size)),
    )
    scratch = [
        pltpu.VMEM((size, wide), LOW),
        pltpu.VMEM((size, wide), LOW),
        *scatter_scratch(rows, size),
        pltpu.SemaphoreType.DMA((2, 3 * PARTS)),
        pltpu.SemaphoreType.DMA((4,)),
    ]
    return launch(
        expand_kernel, number, [VM, VM, ANY, ANY, ANY, ANY, VM, VM], outs, (VM,) * 4, scratch, 3e10
    )(second, hidden, *expand, *contract, vec, bias)


def expand_back_call(number, gathered, grad, expand, contract, active, slope, second, hidden, vec):
    rows, size = hidden.shape
    wide = active.shape[1]
    half = wide // 2
    outs = (
        shape((LENGTH, size)),
        *[shape((size, half))] * 4,
        shape((rows, size), WIDE),
        shape((rows, size)),
        shape((8, wide), WIDE),
    )
    scratch = [
        pltpu.VMEM((size, wide), LOW),
        pltpu.VMEM((size, wide), LOW),
        pltpu.VMEM((LENGTH, wide), LOW),
        *scatter_scratch(rows, size),
        pltpu.SemaphoreType.DMA((2, 3 * PARTS)),
        pltpu.SemaphoreType.DMA((4,)),
    ]
    return launch(
        functools.partial(expand_back_kernel, gathered),
        number, [VM, ANY, ANY, ANY, ANY, VM, VM, VM, VM, VM], outs, (VM,) * 8, scratch, 3e10,
    )(grad, *expand, *contract, active, slope, second, hidden, vec)


def attend_back_call(number, low, grad, x_own, pair, normed, heads_all, o, lse, vec):
    rows, size = grad.shape
    width = o.shape[1]
    heads = width // HEAD
    half = 2 * width
    outs = (shape((size, half)), shape((size, half)), shape((rows, size)), shape((8, size), WIDE))
    scratch = [
        pltpu.VMEM((size, 4 * width), LOW),
        pltpu.VMEM((LENGTH, size), LOW),
        pltpu.VMEM((heads, LENGTH, HEAD), LOW),
        pltpu.VMEM((8, LENGTH), WIDE),
        pltpu.VMEM((3 * heads, LENGTH, HEAD), LOW),
        pltpu.VMEM((LENGTH, HEAD), WIDE),
        pltpu.VMEM((LENGTH, HEAD), WIDE),
        pltpu.VMEM((LENGTH, 3 * width), LOW),
        pltpu.VMEM((2, size, half), LOW),
        *scatter_scratch(rows, size),
        pltpu.SemaphoreType.DMA((2, 3 * PARTS)),
        pltpu.SemaphoreType.DMA((4,)),
    ]
    return launch(
        functools.partial(attend_back_kernel, heads),
        number, [VM, VM, VM, ANY, ANY, VM, VM, VM, VM, VM], outs, (ANY, ANY, VM, VM), scratch, 3e10,
    )(low, grad, x_own, *pair, normed, heads_all, o, lse, vec)


def swap_sections(value):
    return lax.ppermute(value, "section", [(0, 1), (1, 0)])


def on_device(
    tokens,
    cotangent,
    first_gain,
    first_shift,
    attend_weight,
    attend_bias,
    output_weight,
    output_bias,
    second_gain,
    second_shift,
    expand_weight,
    expand_bias,
    contract_weight,
    contract_bias,
):
    section = lax.axis_index("section")
    column = lax.axis_index("col")
    first_section = section == 0
    columns = lax.axis_size("col")
    width = tokens.shape[1]
    size = width * columns
    rows = LENGTH // columns

    def pick(early, later):
        return jnp.where(first_section, early, later)

    block_rows = attend_weight.shape[1]
    units = (
        jnp.concatenate(
            [attend_weight[0].reshape(block_rows, 3 * width), output_weight[0].T], axis=1
        ),
        expand_weight[0],
        contract_weight[0].T,
    )
    mine, theirs = [], []
    for unit in units:
        half = unit.shape[1] // 2
        low, high = unit[:, :half], unit[:, half:]
        mine.append(pick(low, high))
        theirs.append(swap_sections(pick(high, low)))
    mats = []
    for layer in range(2):
        entry = []
        for own, got in zip(mine, theirs):
            block = pick(own, got) if layer == 0 else pick(got, own)
            gathered = lax.all_gather(block, "row", axis=0, tiled=True)
            entry.append((gathered, swap_sections(gathered)))
        mats.append(entry)

    packed = jnp.concatenate(
        [
            first_gain[0],
            first_shift[0],
            output_bias[0],
            second_gain[0],
            second_shift[0],
            contract_bias[0],
        ]
    )
    vectors = lax.all_gather(packed, ("section", "col"), axis=0, tiled=False)
    vectors = vectors.reshape(2, columns, 6, width).astype(WIDE)
    vectors = jnp.swapaxes(vectors, 1, 2).reshape(2, 6, size)
    vectors = jnp.pad(vectors, ((0, 0), (0, 2), (0, 0)))
    own_small = jnp.concatenate(
        [
            attend_bias[0, 0],
            jnp.zeros_like(attend_bias[0, 0]),
            attend_bias[0, 1],
            expand_bias[0],
        ]
    )[None].astype(WIDE)
    other_small = swap_sections(own_small)
    biases = (pick(own_small, other_small), pick(other_small, own_small))
    biases = [(b[:, : 3 * width], b[:, 3 * width :]) for b in biases]

    x0_full = lax.all_gather(
        lax.dynamic_slice_in_dim(tokens, section * LENGTH, LENGTH, 0), "col", axis=1, tiled=True
    )
    gy_full = lax.all_gather(
        lax.dynamic_slice_in_dim(cotangent, section * LENGTH, LENGTH, 0), "col", axis=1, tiled=True
    )

    def own_rows(full):
        return lax.dynamic_slice_in_dim(full, column * rows, rows, 0)

    def own_features(full):
        return lax.dynamic_slice_in_dim(full, column * width, width, 1)

    def gather_rows(own):
        return lax.all_gather(own, "col", axis=0, tiled=True)

    kept = []
    x = x0_full
    fulls = []
    owns = [own_rows(x0_full)]
    for layer in range(2):
        attn, expand, contract = mats[layer]
        full, normed, heads, o, lse, hidden, second_own = attend_call(
            1 + 2 * layer, layer == 0, x, attn, vectors[layer], biases[layer][0], rows, width
        )
        second, active, slope, result = expand_call(
            2 + 2 * layer, second_own, hidden, expand, contract, vectors[layer], biases[layer][1]
        )
        kept.append((normed, heads, o, lse, hidden, second, active, slope))
        fulls.append(full)
        owns.append(result)
        x = result
    x1_full = fulls[1]
    y1_full = gather_rows(owns[2])

    grad = gy_full
    unit_grads, sums, grads = [None, None], [None, None], []
    for layer in (1, 0):
        attn, expand, contract = mats[layer]
        normed, heads, o, lse, hidden, second, active, slope = kept[layer]
        grad_full, ek, es, ck, cs, grad_hidden, low, ff_sums = expand_back_call(
            9 - 2 * layer, layer == 1, grad, expand, contract, active, slope, second, hidden, vectors[layer]
        )
        wk, ws, grad, attn_sums = attend_back_call(
            10 - 2 * layer, low, grad_hidden, owns[layer], attn, normed, heads, o, lse, vectors[layer]
        )
        unit_grads[layer] = ((wk, ws), (ek, es), (ck, cs))
        sums[layer] = (ff_sums, attn_sums)
        grads.append(grad_full)
    gx1_full = grads[1]
    gx0_full = gather_rows(grad)

    def to_sections(layer0, layer1):
        stays = pick(layer0, layer1)
        got = swap_sections(pick(layer1, layer0))
        return jnp.concatenate([pick(stays, got), pick(got, stays)], 0)

    layer_outputs = to_sections(own_features(x1_full), own_features(y1_full))
    input_grads = to_sections(own_features(gx0_full), own_features(gx1_full)).astype(WIDE)

    reduced = []
    for layer in (1, 0):
        entry = []
        for keep, send in unit_grads[layer]:
            total = (keep.astype(WIDE) + swap_sections(send).astype(WIDE)).astype(LOW)
            entry.append(lax.psum_scatter(total, "row", scatter_dimension=0, tiled=True))
        reduced.append(entry)
    units = []
    for late, early in zip(*reduced):
        stays = pick(early, late)
        got = swap_sections(pick(late, early))
        units.append(jnp.concatenate([pick(stays, got), pick(got, stays)], 1).astype(WIDE))
    attn_part, expand_part, contract_part = units

    wide_sum, own_sum = [], []
    for layer in range(2):
        ff_sums, attn_sums = sums[layer]
        wide_sum.append(
            jnp.stack(
                [attn_sums[0], attn_sums[1], ff_sums[3], ff_sums[0], ff_sums[1], ff_sums[2]]
            )
        )
        own_sum.append(
            jnp.concatenate(
                [attn_sums[2, :width], attn_sums[2, 2 * width : 3 * width], ff_sums[4]]
            )
        )
    wide_sum = lax.psum(jnp.stack(wide_sum), ("section", "row", "col"))
    own_sum = lax.psum(jnp.stack(own_sum), ("section", "row"))
    wide_mine = lax.dynamic_slice_in_dim(pick(wide_sum[0], wide_sum[1]), column * width, width, 1)
    own_mine = pick(own_sum[0], own_sum[1])
    return (
        layer_outputs[None],
        input_grads[None],
        wide_mine[0][None],
        wide_mine[1][None],
        attn_part[:, : 3 * width].reshape(block_rows, 3, width)[None],
        own_mine[: 2 * width].reshape(1, 2, width),
        attn_part[:, 3 * width :].T[None],
        wide_mine[2][None],
        wide_mine[3][None],
        wide_mine[4][None],
        expand_part[None],
        own_mine[2 * width :][None],
        contract_part.T[None],
        wide_mine[5][None],
    )


def solution(mesh):
    return jax.shard_map(
        on_device,
        mesh=mesh,
        in_specs=(
            P("row", "col"),
            P("row", "col"),
            P("section", "col"),
            P("section", "col"),
            P("section", "row", None, "col"),
            P("section", None, "col"),
            P("section", "col", "row"),
            P("section", "col"),
            P("section", "col"),
            P("section", "col"),
            P("section", "row", "col"),
            P("section", "col"),
            P("section", "col", "row"),
            P("section", "col"),
        ),
        out_specs=(
            P("section", "row", "col"),
            P("section", "row", "col"),
            P("section", "col"),
            P("section", "col"),
            P("section", "row", None, "col"),
            P("section", None, "col"),
            P("section", "col", "row"),
            P("section", "col"),
            P("section", "col"),
            P("section", "col"),
            P("section", "row", "col"),
            P("section", "col"),
            P("section", "col", "row"),
            P("section", "col"),
        ),
        check_vma=False,
    )
```

```python
import functools

import jax
import jax.numpy as jnp
from jax import lax
from jax.experimental import pallas as pl
from jax.experimental.pallas import tpu as pltpu
from jax.sharding import PartitionSpec as P

HEAD = 64
LENGTH = 1024
EPS = 1e-05
LOW = jnp.bfloat16
WIDE = jnp.float32
MESH = pl.DeviceIdType.MESH
PARTS = 2
TILE = 256
MEBI = 1024 * 1024


def nn(left, right):
    return lax.dot_general(left, right, (((1,), (0,)), ((), ())), preferred_element_type=WIDE)


def nt(left, right):
    return lax.dot_general(left, right, (((1,), (1,)), ((), ())), preferred_element_type=WIDE)


def tn(left, right):
    return lax.dot_general(left, right, (((0,), (0,)), ((), ())), preferred_element_type=WIDE)


def normalise(values):
    center = jnp.mean(values, axis=1, keepdims=True)
    centred = values - center
    scale = lax.rsqrt(jnp.mean(centred * centred, axis=1, keepdims=True) + EPS)
    return centred * scale, scale


def norm_backward(grad, hat, scale, gain):
    scaled = grad * gain
    mean_one = jnp.mean(scaled, axis=1, keepdims=True)
    mean_two = jnp.mean(scaled * hat, axis=1, keepdims=True)
    return scale * (scaled - mean_one - hat * mean_two)


class Group:
    def __init__(self, rows):
        self.me = lax.axis_index("col")
        chip, core = self.me // 2, self.me % 2
        self.sib = chip * 2 + 1 - core
        self.peer = (1 - chip) * 2 + core
        self.diag = (1 - chip) * 2 + 1 - core
        self.rows = rows
        self.part = rows // PARTS

    def greet(self, swaps, diagonal):
        barrier = pltpu.get_barrier_semaphore()
        others = [{"col": self.sib}, {"col": self.peer}]
        if diagonal:
            others.append({"col": self.diag})
        if swaps:
            others.append({"section": 1 - lax.axis_index("section")})
        for other in others:
            pl.semaphore_signal(barrier, inc=1, device_id=other, device_id_type=MESH)
        pl.semaphore_wait(barrier, len(others))

    def slab(self, owner, j):
        return pl.ds(pl.multiple_of(owner * self.rows + j * self.part, self.part), self.part)

    def chunk(self, owner):
        return pl.ds(pl.multiple_of(owner * self.rows, self.rows), self.rows)


def push(src, dst, sems, slot, target, axis="col"):
    return pltpu.make_async_remote_copy(
        src_ref=src,
        dst_ref=dst,
        send_sem=sems.at[0, slot],
        recv_sem=sems.at[1, slot],
        device_id={axis: target},
        device_id_type=MESH,
    )


class Gather:
    def __init__(self, group, full, sems, blocks=False):
        self.group, self.full, self.sems, self.blocks = group, full, sems, blocks

    def piece(self, owner, j):
        if not self.blocks:
            return self.full.at[self.group.slab(owner, j)]
        part = self.full.shape[1] // PARTS
        return self.full.at[owner, pl.ds(j * part, part)]

    def start(self):
        g = self.group
        self.over, self.near, self.relayed = [], [], []
        for j in range(PARTS):
            piece = self.piece(g.me, j)
            self.over.append(push(piece, piece, self.sems, j, g.peer))
            self.over[-1].start()
        for j in range(PARTS):
            piece = self.piece(g.me, j)
            self.near.append(push(piece, piece, self.sems, PARTS + j, g.sib))
            self.near[-1].start()

    def sibling(self):
        for copy in self.near:
            copy.wait_recv()

    def relay(self):
        g = self.group
        for j in range(PARTS):
            self.over[j].wait_recv()
            piece = self.piece(g.peer, j)
            self.relayed.append(push(piece, piece, self.sems, 2 * PARTS + j, g.sib))
            self.relayed[-1].start()

    def diagonal(self):
        for copy in self.relayed:
            copy.wait_recv()

    def done(self):
        for copy in self.over + self.near + self.relayed:
            copy.wait_send()

    def each(self, body):
        g = self.group
        self.start()
        body(g.chunk(g.me))
        self.sibling()
        body(g.chunk(g.sib))
        self.relay()
        body(g.chunk(g.peer))
        self.diagonal()
        body(g.chunk(g.diag))
        self.done()


class Scatter:
    def __init__(self, group, stage, land, total, sems):
        self.group, self.stage, self.land, self.total, self.sems = group, stage, land, total, sems

    def start(self, part):
        g, stage, land = self.group, self.stage, self.land
        self.first, self.over, self.near = [], [], []
        for j in range(PARTS):
            stage[0, j] = part(g.slab(g.diag, j)).astype(LOW)
            self.first.append(push(stage.at[0, j], land.at[0, j], self.sems, j, g.sib))
            self.first[-1].start()
        for j in range(PARTS):
            mine = part(g.slab(g.peer, j))
            self.first[j].wait_recv()
            stage[1, j] = (mine + land[0, j].astype(WIDE)).astype(LOW)
            self.over.append(push(stage.at[1, j], land.at[1, j], self.sems, PARTS + j, g.peer))
            self.over[-1].start()
        for j in range(PARTS):
            stage[2, j] = part(g.slab(g.sib, j)).astype(LOW)
            self.near.append(push(stage.at[2, j], land.at[2, j], self.sems, 2 * PARTS + j, g.sib))
            self.near[-1].start()
        for j in range(PARTS):
            self.total[j] = part(g.slab(g.me, j))

    def take(self, j):
        self.near[j].wait_recv()
        self.over[j].wait_recv()
        land = self.land
        return self.total[j] + (land[1, j].astype(WIDE) + land[2, j].astype(WIDE))

    def done(self):
        for copy in self.first + self.over + self.near:
            copy.wait_send()


class Deliver:
    def __init__(self, group, stage, out, sems):
        self.group, self.stage, self.out, self.sems = group, stage, out, sems

    def start(self, rows_ref):
        g, width = self.group, self.out.shape[1]
        for c in range(self.stage.shape[0]):
            self.stage[c] = rows_ref[:, c * width : (c + 1) * width]
        place = self.out.at[g.chunk(g.me)]
        self.copies = [
            push(self.stage.at[other], place, self.sems, n, other)
            for n, other in enumerate((g.peer, g.diag, g.sib))
        ]
        for copy in self.copies:
            copy.start()
        self.out[g.chunk(g.me), :] = self.stage[g.me]

    def done(self):
        for copy in self.copies:
            copy.wait()


def scatter_scratch(rows, width):
    part = rows // PARTS
    return [
        pltpu.VMEM((3, PARTS, part, width), LOW),
        pltpu.VMEM((3, PARTS, part, width), LOW),
        pltpu.VMEM((PARTS, part, width), WIDE),
        pltpu.SemaphoreType.DMA((2, 3 * PARTS)),
    ]


class Halves:
    def __init__(self, pair, whole, sems, slot):
        section = lax.axis_index("section")
        half = whole.shape[1] // 2
        self.copies = []
        for n, place in enumerate((section, 1 - section)):
            columns = pl.ds(pl.multiple_of(place * half, half), half)
            self.copies.append(
                pltpu.make_async_copy(pair[n], whole.at[:, columns], sems.at[slot + n])
            )

    def start(self):
        for copy in self.copies:
            copy.start()

    def wait(self):
        for copy in self.copies:
            copy.wait()


def attention_out(heads_ref, o3, lse_ref, heads):
    length = heads_ref.shape[1]
    size = min(TILE, length)

    @pl.loop(0, heads)
    def _(h):
        for i in range(length // size):
            rows = slice(i * size, (i + 1) * size)
            finish = (i + 1) * size
            queries = heads_ref[h, rows, :]
            scores = nt(heads_ref[heads + h, :finish, :], queries)
            keep = lax.broadcasted_iota(jnp.int32, (size, size), 0) <= lax.broadcasted_iota(
                jnp.int32, (size, size), 1
            )
            last = jnp.where(keep, scores[finish - size :], -1000000000.0)
            scores = last if i == 0 else jnp.concatenate([scores[: finish - size], last], 0)
            highest = jnp.max(scores, axis=0, keepdims=True)
            powers = jnp.exp(scores - highest)
            summed = jnp.sum(powers, axis=0, keepdims=True)
            mixed = tn(heads_ref[2 * heads + h, :finish, :], powers.astype(LOW))
            o3[h, rows, :] = (mixed / summed).T.astype(LOW)
            lse_ref[pl.ds(h, 1), rows] = highest + jnp.log(summed)


def attention_back(heads_ref, go3, lse_ref, dots_ref, g3, key_acc, value_acc, heads):
    length = heads_ref.shape[1]
    size = min(TILE, length)

    @pl.loop(0, heads)
    def _(h):
        for i in reversed(range(length // size)):
            rows = slice(i * size, (i + 1) * size)
            finish = (i + 1) * size
            queries = heads_ref[h, rows, :]
            keys = heads_ref[heads + h, :finish, :]
            grads = go3[h, rows, :]
            scores = nt(keys, queries) - lse_ref[pl.ds(h, 1), rows]
            keep = lax.broadcasted_iota(jnp.int32, (size, size), 0) <= lax.broadcasted_iota(
                jnp.int32, (size, size), 1
            )
            last = jnp.where(keep, scores[finish - size :], -1000000000.0)
            scores = last if i == 0 else jnp.concatenate([scores[: finish - size], last], 0)
            probs = jnp.exp(scores)
            grad_probs = nt(heads_ref[2 * heads + h, :finish, :], grads)
            grad_scores = (probs * (grad_probs - dots_ref[pl.ds(h, 1), rows])).astype(LOW)
            g3[h, rows, :] = (tn(grad_scores, keys) * HEAD ** (-0.5)).astype(LOW)
            key_part = nn(grad_scores, queries)
            value_part = nn(probs.astype(LOW), grads)
            if finish == length:
                key_acc[...] = key_part
                value_acc[...] = value_part
            else:
                key_acc[:finish, :] += key_part
                value_acc[:finish, :] += value_part
        g3[heads + h] = key_acc[...].astype(LOW)
        g3[2 * heads + h] = value_acc[...].astype(LOW)


def start_kernel(
    tokens_ref, cotangent_ref, small_ref, x_ref, g_ref, vectors_ref,
    x4, g4, s4, other4, x_sems, g_sems, s_sems, local_sems,
):
    section = lax.axis_index("section")
    group = Group(x_ref.shape[0] // 4)
    length = x_ref.shape[0]
    loads = []
    rows = pl.ds(pl.multiple_of(section * length, length), length)
    for n, (source, into) in enumerate(((tokens_ref.at[rows], x4), (cotangent_ref.at[rows], g4), (small_ref, s4))):
        loads.append(pltpu.make_async_copy(source, into.at[group.me], local_sems.at[n]))
        loads[-1].start()
    group.greet(True, False)
    gathers = [Gather(group, x4, x_sems, True), Gather(group, s4, s_sems, True), Gather(group, g4, g_sems, True)]
    for gather, load in zip(gathers, (loads[0], loads[2], loads[1])):
        load.wait()
        gather.start()
    for gather in gathers:
        gather.sibling()
        gather.relay()
        gather.diagonal()
    swap = push(s4, other4, s_sems, 3 * PARTS, 1 - section, "section")
    swap.start()
    width = x4.shape[2]
    for c in range(x4.shape[0]):
        x_ref[:, c * width : (c + 1) * width] = x4[c]
        g_ref[:, c * width : (c + 1) * width] = g4[c]
    swap.wait()
    vectors_ref[section] = s4[...]
    vectors_ref[1 - section] = other4[...]
    for gather in gathers:
        gather.done()


def attend_kernel(
    gathered, heads, group, x_ref, mine_ref, other_ref, vec_ref, bias_ref,
    full_ref, normed_ref, heads_ref, o_ref, lse_ref, hidden_ref, second_ref,
    weight, o3, stage, land, total, scatter_sems, gather_sems, local_sems,
):
    width = o_ref.shape[1]
    halves = Halves((mine_ref, other_ref), weight, local_sems, 0)
    halves.start()
    if not gathered:
        full_ref[group.chunk(group.me), :] = x_ref[...]
    halves.wait()

    def project(rows):
        values = (x_ref if gathered else full_ref)[rows, :].astype(WIDE)
        hat, _ = normalise(values)
        normed = (hat * vec_ref[0:1, :] + vec_ref[1:2, :]).astype(LOW)
        normed_ref[rows, :] = normed
        mixed = nn(normed, weight[:, : 3 * width]) + bias_ref[...]
        for j in range(3 * heads):
            piece = mixed[:, j * HEAD : (j + 1) * HEAD]
            if j < heads:
                piece = piece * HEAD ** (-0.5)
            heads_ref[j, rows, :] = piece.astype(LOW)

    if gathered:
        full_ref[...] = jnp.zeros_like(full_ref)

        @pl.loop(0, LENGTH // group.rows)
        def _(n):
            project(group.chunk(n))
    else:
        Gather(group, full_ref, gather_sems).each(project)

    attention_out(heads_ref, o3, lse_ref, heads)
    for h in range(heads):
        o_ref[:, h * HEAD : (h + 1) * HEAD] = o3[h]

    scatter = Scatter(group, stage, land, total, scatter_sems)
    scatter.start(lambda rows: nt(o_ref[rows, :], weight[:, 3 * width :]))
    for j in range(PARTS):
        rows = slice(j * group.part, (j + 1) * group.part)
        residual = (x_ref if gathered else full_ref)[group.slab(group.me, j), :].astype(WIDE)
        hidden = residual + scatter.take(j) + vec_ref[2:3, :]
        hidden_ref[rows, :] = hidden
        hat, _ = normalise(hidden)
        second_ref[rows, :] = (hat * vec_ref[3:4, :] + vec_ref[4:5, :]).astype(LOW)
    scatter.done()


def widen_kernel(
    group, second_ref, em_ref, eo_ref, bias_ref,
    full_ref, active_ref, slope_ref,
    expand, gather_sems, local_sems,
):
    halves = Halves((em_ref, eo_ref), expand, local_sems, 0)
    halves.start()
    full_ref[group.chunk(group.me), :] = second_ref[...]
    halves.wait()

    def widen(rows):
        t = nn(full_ref[rows, :], expand[...]) + bias_ref[...]
        square = t * t
        bent = jnp.tanh(0.7978845608028654 * t * (1.0 + 0.044715 * square))
        active_ref[rows, :] = (0.5 * t * (1.0 + bent)).astype(LOW)
        slope_ref[rows, :] = (
            0.5 * (1.0 + bent)
            + (0.5 * 0.7978845608028654) * t * (1.0 - bent * bent) * (1.0 + 3 * 0.044715 * square)
        ).astype(LOW)

    Gather(group, full_ref, gather_sems).each(widen)


def outer_halves(left_ref, right_ref, keep_ref, send_ref):
    section = lax.axis_index("section")
    half = right_ref.shape[1] // 2
    for place, out in ((section, keep_ref), (1 - section, send_ref)):
        columns = pl.ds(pl.multiple_of(place * half, half), half)

        @pl.loop(0, left_ref.shape[1] // TILE)
        def _(n):
            rows = pl.ds(pl.multiple_of(n * TILE, TILE), TILE)
            out[rows, :] = tn(left_ref[:, rows], right_ref[:, columns]).astype(LOW)


def contract_kernel(last, group, *refs):
    active_ref, hidden_ref, cm_ref, co_ref, vec_ref, *refs = refs
    if last:
        g_ref, *refs = refs
    result_ref, *refs = refs
    if last:
        out_ref, ck_ref, cs_ref, *refs = refs
    contract, stage, land, total, scatter_sems, local_sems, *refs = refs
    if last:
        stage4, deliver_sems = refs
    halves = Halves((cm_ref, co_ref), contract, local_sems, 0)
    halves.start()
    halves.wait()
    scatter = Scatter(group, stage, land, total, scatter_sems)
    scatter.start(lambda rows: nt(active_ref[rows, :], contract[...]))
    if last:
        outer_halves(g_ref, active_ref, ck_ref, cs_ref)
    for j in range(PARTS):
        rows = slice(j * group.part, (j + 1) * group.part)
        result = hidden_ref[rows, :] + scatter.take(j) + vec_ref[5:6, :]
        result_ref[rows, :] = result.astype(LOW)
    if last:
        deliver = Deliver(group, stage4, out_ref, deliver_sems)
        deliver.start(result_ref)
        deliver.done()
    scatter.done()


def bend_kernel(last, group, g_ref, cm_ref, co_ref, active_ref, slope_ref, *refs):
    before, sums_ref, *refs = refs
    if not last:
        full_ref, ck_ref, cs_ref, *refs = refs
    contract, gather_sems, local_sems = refs
    halves = Halves((cm_ref, co_ref), contract, local_sems, 0)
    halves.start()
    sums_ref[...] = jnp.zeros_like(sums_ref)
    if not last:
        full_ref[group.chunk(group.me), :] = g_ref[...]
    halves.wait()

    def bend(rows):
        rows_grad = (g_ref if last else full_ref)[rows, :]
        grad = (nn(rows_grad, contract[...]) * slope_ref[rows, :].astype(WIDE)).astype(LOW)
        before[rows, :] = grad
        sums_ref[0:1, :] += jnp.sum(grad.astype(WIDE), axis=0, keepdims=True)

    if last:

        @pl.loop(0, LENGTH // group.rows)
        def _(n):
            bend(group.chunk(n))
    else:
        Gather(group, full_ref, gather_sems).each(bend)
        outer_halves(full_ref, active_ref, ck_ref, cs_ref)


def narrow_kernel(
    group, before, g_ref, em_ref, eo_ref, second_ref, hidden_ref, vec_ref,
    ek_ref, es_ref, grad_ref, low_ref, sums_ref,
    expand, stage, land, total, scatter_sems, local_sems,
):
    halves = Halves((em_ref, eo_ref), expand, local_sems, 0)
    halves.start()
    sums_ref[...] = jnp.zeros_like(sums_ref)
    halves.wait()
    scatter = Scatter(group, stage, land, total, scatter_sems)
    scatter.start(lambda rows: nt(before[rows, :], expand[...]))
    outer_halves(second_ref, before, ek_ref, es_ref)
    for j in range(PARTS):
        rows = slice(j * group.part, (j + 1) * group.part)
        grad = scatter.take(j)
        hat, scale = normalise(hidden_ref[rows, :])
        own = g_ref[rows, :].astype(WIDE)
        out = own + norm_backward(grad, hat, scale, vec_ref[3:4, :])
        grad_ref[rows, :] = out
        low_ref[rows, :] = out.astype(LOW)
        for n, term in enumerate((grad * hat, grad, own, out)):
            sums_ref[n : n + 1, :] += jnp.sum(term, axis=0, keepdims=True)
    scatter.done()


def attend_back_kernel(
    last, heads, group, low_ref, grad_ref, x_ref, mine_ref, other_ref, normed_ref, heads_ref, o_ref, lse_ref, vec_ref,
    *refs,
):
    wk_ref, ws_ref, out_ref, sums_ref, *refs = refs
    if not last:
        spread_ref, *refs = refs
    weight, full, go3, dots, g3, key_acc, value_acc, mixed, outer, *refs = refs
    stage, land, total, scatter_sems, gather_sems, local_sems, *refs = refs
    if not last:
        stage4, deliver_sems = refs
    width = o_ref.shape[1]
    section = lax.axis_index("section")
    halves = Halves((mine_ref, other_ref), weight, local_sems, 0)
    halves.start()
    sums_ref[...] = jnp.zeros_like(sums_ref)
    full[group.chunk(group.me), :] = low_ref[...]
    halves.wait()
    picks = (
        lax.broadcasted_iota(jnp.int32, (8, width), 1) // HEAD
        == lax.broadcasted_iota(jnp.int32, (8, width), 0)
    ).astype(WIDE)

    def spread(rows):
        grads = nn(full[rows, :], weight[:, 3 * width :]).astype(LOW)
        for h in range(heads):
            go3[h, rows, :] = grads[:, h * HEAD : (h + 1) * HEAD]
        term = grads.astype(WIDE) * o_ref[rows, :].astype(WIDE)
        dots[:, rows] = lax.dot_general(
            picks,
            term,
            (((1,), (1,)), ((), ())),
            precision=lax.Precision.HIGHEST,
            preferred_element_type=WIDE,
        )

    Gather(group, full, gather_sems).each(spread)
    attention_back(heads_ref, go3, lse_ref, dots, g3, key_acc, value_acc, heads)
    for j in range(3 * heads):
        mixed[:, j * HEAD : (j + 1) * HEAD] = g3[j]

    scatter = Scatter(group, stage, land, total, scatter_sems)
    scatter.start(lambda rows: nt(mixed[rows, :], weight[:, : 3 * width]))

    half = weight.shape[1] // 2

    @pl.loop(0, weight.shape[0] // TILE)
    def _(n):
        rows = pl.ds(pl.multiple_of(n * TILE, TILE), TILE)
        outer[section, rows, :] = tn(normed_ref[:, rows], mixed[:, :half]).astype(LOW)
        outer[1 - section, rows, : 3 * width - half] = tn(
            normed_ref[:, rows], mixed[:, half:]
        ).astype(LOW)
        outer[1 - section, rows, 3 * width - half :] = tn(full[:, rows], o_ref[...]).astype(LOW)

    keep = pltpu.make_async_copy(outer.at[0], wk_ref, local_sems.at[2])
    send = pltpu.make_async_copy(outer.at[1], ws_ref, local_sems.at[3])
    keep.start()
    send.start()
    sums_ref[2:3, : 3 * width] = jnp.sum(mixed[...].astype(WIDE), axis=0, keepdims=True)
    for j in range(PARTS):
        rows = slice(j * group.part, (j + 1) * group.part)
        grad = scatter.take(j)
        hat, scale = normalise(x_ref[rows, :].astype(WIDE))
        out = grad_ref[rows, :] + norm_backward(grad, hat, scale, vec_ref[0:1, :])
        out_ref[rows, :] = out.astype(LOW)
        for n, term in enumerate((grad * hat, grad)):
            sums_ref[n : n + 1, :] += jnp.sum(term, axis=0, keepdims=True)
    if not last:
        deliver = Deliver(group, stage4, spread_ref, deliver_sems)
        deliver.start(out_ref)
        deliver.done()
    scatter.done()
    keep.wait()
    send.wait()


VM = pl.BlockSpec(memory_space=pltpu.VMEM)
ANY = pl.BlockSpec(memory_space=pl.ANY)
PAIRS = pltpu.SemaphoreType.DMA((2, 3 * PARTS))
LOCAL = pltpu.SemaphoreType.DMA((4,))


def shape(dims, kind=LOW):
    return jax.ShapeDtypeStruct(dims, kind)


def launch(body, number, rows, in_specs, ins, outs, out_specs, scratch, swaps=(), diagonal=False, flops=3e10):
    def kernel(*refs):
        n_in, n_out, n = len(in_specs), len(outs), len(swaps)
        group = Group(rows)
        group.greet(n, diagonal)
        sources, lands = refs[n_in : n_in + n], refs[n_in + n + n_out : n_in + 2 * n + n_out]
        other = 1 - lax.axis_index("section")
        copies = [
            push(source, land, refs[-1], i, other, "section")
            for i, (source, land) in enumerate(zip(sources, lands))
        ]
        for copy in copies:
            copy.start()
        rest = refs[n_in + 2 * n + n_out :]
        body(group, *refs[:n_in], *refs[n_in + n : n_in + n + n_out], *(rest[:-1] if n else rest))
        for copy in copies:
            copy.wait()

    extra = [pltpu.SemaphoreType.DMA((2, len(swaps)))] if swaps else []
    results = pl.pallas_call(
        kernel,
        out_shape=(*outs, *[shape(s.shape, s.dtype) for s in swaps]),
        in_specs=[*in_specs, *[ANY] * len(swaps)],
        out_specs=(*out_specs, *[ANY] * len(swaps)),
        scratch_shapes=[*scratch, *extra],
        compiler_params=pltpu.CompilerParams(
            collective_id=number, has_side_effects=True, vmem_limit_bytes=56 * MEBI
        ),
        cost_estimate=pl.CostEstimate(
            flops=int(flops), bytes_accessed=30 * MEBI, transcendentals=0
        ),
    )(*ins, *swaps)
    return results[: len(outs)], results[len(outs) :]


def start_call(number, tokens, cotangent, small, columns):
    width = tokens.shape[1]
    size = width * columns
    kinds = small.shape[0]
    outs = (shape((LENGTH, size)), shape((LENGTH, size)), shape((2, columns, kinds, width)))
    blocks = pltpu.VMEM((columns, LENGTH, width), LOW)
    vectors = pltpu.VMEM((columns, kinds, width), LOW)
    return pl.pallas_call(
        start_kernel,
        out_shape=outs,
        in_specs=[ANY] * 3,
        out_specs=(VM,) * 3,
        scratch_shapes=[
            blocks, blocks, vectors, vectors, PAIRS, PAIRS,
            pltpu.SemaphoreType.DMA((2, 3 * PARTS + 1)), LOCAL,
        ],
        compiler_params=pltpu.CompilerParams(
            collective_id=number, has_side_effects=True, vmem_limit_bytes=56 * MEBI
        ),
        cost_estimate=pl.CostEstimate(flops=int(3e10), bytes_accessed=30 * MEBI, transcendentals=0),
    )(tokens, cotangent, small)


def attend_call(number, gathered, x, pair, vec, bias, rows, width, swaps):
    size = vec.shape[1]
    heads = width // HEAD
    outs = (
        shape((LENGTH, size) if not gathered else (16, 128)),
        shape((LENGTH, size)),
        shape((3 * heads, LENGTH, HEAD)),
        shape((LENGTH, width)),
        shape((8, LENGTH), WIDE),
        shape((rows, size), WIDE),
        shape((rows, size)),
    )
    scratch = [
        pltpu.VMEM((size, 4 * width), LOW),
        pltpu.VMEM((heads, LENGTH, HEAD), LOW),
        *scatter_scratch(rows, size), PAIRS, LOCAL,
    ]
    return launch(
        functools.partial(attend_kernel, gathered, heads),
        number, rows, [VM, ANY, ANY, VM, VM], (x, *pair, vec, bias), outs, (VM,) * 7, scratch, swaps,
    )


def widen_call(number, second, pair, bias, swaps):
    rows, size = second.shape
    wide = bias.shape[1]
    outs = (shape((LENGTH, size)), shape((LENGTH, wide)), shape((LENGTH, wide)))
    scratch = [pltpu.VMEM((size, wide), LOW), PAIRS, LOCAL]
    return launch(
        widen_kernel, number, rows, [VM, ANY, ANY, VM], (second, *pair, bias), outs, (VM,) * 3, scratch, swaps
    )


def contract_call(number, active, hidden, pair, vec, grad, swaps):
    rows, size = hidden.shape
    wide = active.shape[1]
    last = grad is not None
    outs = [shape((rows, size))]
    scratch = [pltpu.VMEM((size, wide), LOW), *scatter_scratch(rows, size), LOCAL]
    in_specs, ins = [VM, VM, ANY, ANY, VM], [active, hidden, *pair, vec]
    if last:
        in_specs, ins = in_specs + [VM], ins + [grad]
        columns = LENGTH // rows
        outs += [shape((LENGTH, size // columns)), *[shape((size, wide // 2))] * 2]
        scratch += [pltpu.VMEM((columns, rows, size // columns), LOW), pltpu.SemaphoreType.DMA((2, 3))]
    return launch(
        functools.partial(contract_kernel, last),
        number, rows, in_specs, ins, outs, (VM,) * len(outs), scratch, swaps, last,
    )


def bend_call(number, last, grad, pair, active, slope, size, rows, swaps):
    wide = active.shape[1]
    outs = [shape((LENGTH, wide)), shape((8, wide), WIDE)]
    if not last:
        outs += [shape((LENGTH, size)), *[shape((size, wide // 2))] * 2]
    scratch = [pltpu.VMEM((size, wide), LOW), PAIRS, LOCAL]
    return launch(
        functools.partial(bend_kernel, last),
        number, rows, [VM, ANY, ANY, VM, VM], (grad, *pair, active, slope), outs, (VM,) * len(outs), scratch, swaps,
    )


def narrow_call(number, before, grad_own, pair, second, hidden, vec, swaps):
    rows, size = hidden.shape
    wide = before.shape[1]
    outs = (
        *[shape((size, wide // 2))] * 2,
        shape((rows, size), WIDE),
        shape((rows, size)),
        shape((8, size), WIDE),
    )
    scratch = [pltpu.VMEM((size, wide), LOW), *scatter_scratch(rows, size), LOCAL]
    return launch(
        narrow_kernel,
        number, rows, [VM, VM, ANY, ANY, VM, VM, VM], (before, grad_own, *pair, second, hidden, vec),
        outs, (VM,) * 5, scratch, swaps,
    )


def attend_back_call(number, last, low, grad, x_own, pair, normed, heads_all, o, lse, vec, swaps):
    rows, size = grad.shape
    width = o.shape[1]
    heads = width // HEAD
    half = 2 * width
    outs = [shape((size, half)), shape((size, half)), shape((rows, size)), shape((8, size), WIDE)]
    scratch = [
        pltpu.VMEM((size, 4 * width), LOW),
        pltpu.VMEM((LENGTH, size), LOW),
        pltpu.VMEM((heads, LENGTH, HEAD), LOW),
        pltpu.VMEM((8, LENGTH), WIDE),
        pltpu.VMEM((3 * heads, LENGTH, HEAD), LOW),
        pltpu.VMEM((LENGTH, HEAD), WIDE),
        pltpu.VMEM((LENGTH, HEAD), WIDE),
        pltpu.VMEM((LENGTH, 3 * width), LOW),
        pltpu.VMEM((2, size, half), LOW),
        *scatter_scratch(rows, size), PAIRS, LOCAL,
    ]
    out_specs = [ANY, ANY, VM, VM]
    if not last:
        outs, out_specs = outs + [shape((LENGTH, width))], out_specs + [VM]
        scratch += [pltpu.VMEM((LENGTH // rows, rows, width), LOW), pltpu.SemaphoreType.DMA((2, 3))]
    return launch(
        functools.partial(attend_back_kernel, last, heads),
        number, rows, [VM, VM, VM, ANY, ANY, VM, VM, VM, VM, VM],
        (low, grad, x_own, *pair, normed, heads_all, o, lse, vec), outs, out_specs, scratch, swaps, not last,
    )


def swap_sections(value):
    return lax.ppermute(value, "section", [(0, 1), (1, 0)])


def on_device(
    tokens,
    cotangent,
    first_gain,
    first_shift,
    attend_weight,
    attend_bias,
    output_weight,
    output_bias,
    second_gain,
    second_shift,
    expand_weight,
    expand_bias,
    contract_weight,
    contract_bias,
):
    section = lax.axis_index("section")
    column = lax.axis_index("col")
    first_section = section == 0
    columns = lax.axis_size("col")
    width = tokens.shape[1]
    size = width * columns
    rows = LENGTH // columns

    def pick(early, later):
        return jnp.where(first_section, early, later)

    block_rows = attend_weight.shape[1]
    units = (
        jnp.concatenate(
            [attend_weight[0].reshape(block_rows, 3 * width), output_weight[0].T], axis=1
        ),
        expand_weight[0],
        contract_weight[0].T,
    )
    mats = [[], []]
    for unit in units:
        half = unit.shape[1] // 2
        low, high = unit[:, :half], unit[:, half:]
        own = pick(low, high)
        got = swap_sections(pick(high, low))
        for layer, block in enumerate((pick(own, got), pick(got, own))):
            mats[layer].append(lax.all_gather(block, "row", axis=0, tiled=True))

    small = jnp.concatenate(
        [
            first_gain,
            first_shift,
            output_bias,
            second_gain,
            second_shift,
            contract_bias,
            attend_bias[0],
            expand_bias[0].reshape(-1, width),
        ],
        0,
    )
    filled = small.shape[0]
    small = jnp.pad(small, ((0, -filled % 16), (0, 0)))
    x0_full, gy_full, vectors = start_call(1, tokens, cotangent, small, columns)
    vectors = vectors.astype(WIDE)
    wide_vectors = jnp.swapaxes(vectors[:, :, :6], 1, 2).reshape(2, 6, size)
    wide_vectors = jnp.pad(wide_vectors, ((0, 0), (0, 2), (0, 0)))
    own_vectors = lax.dynamic_index_in_dim(vectors, column, 1, keepdims=False)
    attend_biases = jnp.stack(
        [own_vectors[:, 6], jnp.zeros_like(own_vectors[:, 6]), own_vectors[:, 7]], 1
    ).reshape(2, 1, 3 * width)
    expand_biases = own_vectors[:, 8:filled].reshape(2, 1, -1)

    def own_rows(full):
        return lax.dynamic_slice_in_dim(full, column * rows, rows, 0)

    def own_features(full):
        return lax.dynamic_slice_in_dim(full, column * width, width, 1)

    attn = (mats[0][0], swap_sections(mats[0][0]))
    x = x0_full
    kept, pairs = [], []
    owns = [own_rows(x0_full)]
    for layer in range(2):
        last = layer == 1
        vec = wide_vectors[layer]
        (full, normed, heads, o, lse, hidden, second_own), (other,) = attend_call(
            2 + 3 * layer, not last, x, attn, vec, attend_biases[layer], rows, width, [mats[layer][1]]
        )
        expand = (mats[layer][1], other)
        (second, active, slope), (other,) = widen_call(
            3 + 3 * layer, second_own, expand, expand_biases[layer], [mats[layer][2]]
        )
        contract = (mats[layer][2], other)
        outs, others = contract_call(
            4 + 3 * layer, active, hidden, contract, vec,
            gy_full if last else None, [] if last else [mats[1][0]],
        )
        pairs.append((attn, expand, contract))
        kept.append((normed, heads, o, lse, hidden, second, active, slope))
        x = outs[0]
        owns.append(x)
        if last:
            y1, ck1, cs1 = outs[1:]
        else:
            attn = (mats[1][0], others[0])
    y0 = own_features(full)
    layer_low, layer_high = pick(y0, y1), pick(y1, y0)

    attn, expand, contract = pairs[1]
    normed, heads, o, lse, hidden, second, active, slope = kept[1]
    (before, bend_sums1), _ = bend_call(8, True, gy_full, contract, active, slope, size, rows, [])
    (ek1, es1, grad_hidden, low, narrow_sums1), (ct1,) = narrow_call(
        9, before, own_rows(gy_full), expand, second, hidden, wide_vectors[1], [cs1]
    )
    (wk1, ws1, gx1_own, attend_sums1), (et1, layer_got) = attend_back_call(
        10, True, low, grad_hidden, owns[1], attn, normed, heads, o, lse, wide_vectors[1], [es1, layer_high]
    )
    layer_outputs = jnp.concatenate([pick(layer_low, layer_got), pick(layer_got, layer_low)], 0)

    attn, expand, contract = pairs[0]
    normed, heads, o, lse, hidden, second, active, slope = kept[0]
    (before, bend_sums0, gx1_full, ck0, cs0), (wt1,) = bend_call(
        11, False, gx1_own, contract, active, slope, size, rows, [ws1]
    )
    (ek0, es0, grad_hidden, low, narrow_sums0), (ct0,) = narrow_call(
        12, before, gx1_own, expand, second, hidden, wide_vectors[0], [cs0]
    )
    (wk0, ws0, _, attend_sums0, gx0), (et0,) = attend_back_call(
        13, False, low, grad_hidden, owns[0], attn, normed, heads, o, lse, wide_vectors[0], [es0]
    )
    wt0 = swap_sections(ws0)

    gx1 = own_features(gx1_full)
    gx_low, gx_got = pick(gx0, gx1), swap_sections(pick(gx1, gx0))
    input_grads = jnp.concatenate([pick(gx_low, gx_got), pick(gx_got, gx_low)], 0).astype(WIDE)

    def reduce_grad(keep, got):
        total = (keep.astype(WIDE) + got.astype(WIDE)).astype(LOW)
        return lax.psum_scatter(total, "row", scatter_dimension=0, tiled=True)

    late = [reduce_grad(*pair) for pair in ((wk1, wt1), (ek1, et1), (ck1, ct1))]
    early = [reduce_grad(*pair) for pair in ((wk0, wt0), (ek0, et0), (ck0, ct0))]
    units = []
    for second_layer, first_layer in zip(late, early):
        stays = pick(first_layer, second_layer)
        got = swap_sections(pick(second_layer, first_layer))
        units.append(jnp.concatenate([pick(stays, got), pick(got, stays)], 1).astype(WIDE))
    attn_part, expand_part, contract_part = units

    wide_sum, own_sum = [], []
    for attend_sums, narrow_sums, bend_sums in (
        (attend_sums0, narrow_sums0, bend_sums0),
        (attend_sums1, narrow_sums1, bend_sums1),
    ):
        wide_sum.append(
            jnp.concatenate([attend_sums[:2], narrow_sums[3:4], narrow_sums[:3]], 0)
        )
        own_sum.append(
            jnp.concatenate(
                [attend_sums[2, :width], attend_sums[2, 2 * width : 3 * width], bend_sums[0]]
            )
        )
    wide_sum = lax.psum(jnp.stack(wide_sum), ("section", "row", "col"))
    own_sum = lax.psum(jnp.stack(own_sum), ("section", "row"))
    wide_mine = lax.dynamic_slice_in_dim(pick(wide_sum[0], wide_sum[1]), column * width, width, 1)
    own_mine = pick(own_sum[0], own_sum[1])
    return (
        layer_outputs[None],
        input_grads[None],
        wide_mine[0][None],
        wide_mine[1][None],
        attn_part[:, : 3 * width].reshape(block_rows, 3, width)[None],
        own_mine[: 2 * width].reshape(1, 2, width),
        attn_part[:, 3 * width :].T[None],
        wide_mine[2][None],
        wide_mine[3][None],
        wide_mine[4][None],
        expand_part[None],
        own_mine[2 * width :][None],
        contract_part.T[None],
        wide_mine[5][None],
    )


def solution(mesh):
    return jax.shard_map(
        on_device,
        mesh=mesh,
        in_specs=(
            P("row", "col"),
            P("row", "col"),
            P("section", "col"),
            P("section", "col"),
            P("section", "row", None, "col"),
            P("section", None, "col"),
            P("section", "col", "row"),
            P("section", "col"),
            P("section", "col"),
            P("section", "col"),
            P("section", "row", "col"),
            P("section", "col"),
            P("section", "col", "row"),
            P("section", "col"),
        ),
        out_specs=(
            P("section", "row", "col"),
            P("section", "row", "col"),
            P("section", "col"),
            P("section", "col"),
            P("section", "row", None, "col"),
            P("section", None, "col"),
            P("section", "col", "row"),
            P("section", "col"),
            P("section", "col"),
            P("section", "col"),
            P("section", "row", "col"),
            P("section", "col"),
            P("section", "col", "row"),
            P("section", "col"),
        ),
        check_vma=False,
    )
```

```python
import functools
import math

import jax
import jax.numpy as jnp
from jax import lax
from jax.experimental import pallas as pl
from jax.experimental.pallas import tpu as pltpu
from jax.sharding import PartitionSpec as P

HEAD = 64
LENGTH = 1024
EPS = 1e-05
LOW = jnp.bfloat16
WIDE = jnp.float32
MESH = pl.DeviceIdType.MESH
PARTS = 2
TILE = 256
MEBI = 1024 * 1024
SPARE = 14 * MEBI


def nn(left, right):
    return lax.dot_general(left, right, (((1,), (0,)), ((), ())), preferred_element_type=WIDE)


def nt(left, right):
    return lax.dot_general(left, right, (((1,), (1,)), ((), ())), preferred_element_type=WIDE)


def tn(left, right):
    return lax.dot_general(left, right, (((0,), (0,)), ((), ())), preferred_element_type=WIDE)


def normalise(values):
    center = jnp.mean(values, axis=1, keepdims=True)
    centred = values - center
    scale = lax.rsqrt(jnp.mean(centred * centred, axis=1, keepdims=True) + EPS)
    return centred * scale, scale


def norm_backward(grad, hat, scale, gain):
    scaled = grad * gain
    mean_one = jnp.mean(scaled, axis=1, keepdims=True)
    mean_two = jnp.mean(scaled * hat, axis=1, keepdims=True)
    return scale * (scaled - mean_one - hat * mean_two)


class Group:
    def __init__(self, rows):
        self.me = lax.axis_index("col")
        chip, core = self.me // 2, self.me % 2
        self.sib = chip * 2 + 1 - core
        self.peer = (1 - chip) * 2 + core
        self.diag = (1 - chip) * 2 + 1 - core
        self.rows = rows
        self.part = rows // PARTS

    def greet(self, swaps, diagonal, rows=()):
        barrier = pltpu.get_barrier_semaphore()
        others = [{"col": self.sib}, {"col": self.peer}]
        if diagonal:
            others.append({"col": self.diag})
        if swaps:
            others.append({"section": 1 - lax.axis_index("section")})
        others += [{"row": row} for row in rows]
        for other in others:
            pl.semaphore_signal(barrier, inc=1, device_id=other, device_id_type=MESH)
        pl.semaphore_wait(barrier, len(others))

    def slab(self, owner, j):
        return pl.ds(pl.multiple_of(owner * self.rows + j * self.part, self.part), self.part)

    def chunk(self, owner):
        return pl.ds(pl.multiple_of(owner * self.rows, self.rows), self.rows)


def push(src, dst, sems, slot, target, axis="col"):
    return pltpu.make_async_remote_copy(
        src_ref=src,
        dst_ref=dst,
        send_sem=sems.at[0, slot],
        recv_sem=sems.at[1, slot],
        device_id={axis: target},
        device_id_type=MESH,
    )


class Gather:
    def __init__(self, group, full, sems, blocks=False):
        self.group, self.full, self.sems, self.blocks = group, full, sems, blocks

    def piece(self, owner, j):
        if not self.blocks:
            return self.full.at[self.group.slab(owner, j)]
        part = self.full.shape[1] // PARTS
        return self.full.at[owner, pl.ds(j * part, part)]

    def start(self):
        g = self.group
        self.over, self.near, self.relayed = [], [], []
        for j in range(PARTS):
            piece = self.piece(g.me, j)
            self.over.append(push(piece, piece, self.sems, j, g.peer))
            self.over[-1].start()
        for j in range(PARTS):
            piece = self.piece(g.me, j)
            self.near.append(push(piece, piece, self.sems, PARTS + j, g.sib))
            self.near[-1].start()

    def sibling(self):
        for copy in self.near:
            copy.wait_recv()

    def relay(self):
        g = self.group
        for j in range(PARTS):
            self.over[j].wait_recv()
            piece = self.piece(g.peer, j)
            self.relayed.append(push(piece, piece, self.sems, 2 * PARTS + j, g.sib))
            self.relayed[-1].start()

    def diagonal(self):
        for copy in self.relayed:
            copy.wait_recv()

    def done(self):
        for copy in self.over + self.near + self.relayed:
            copy.wait_send()

    def each(self, body):
        g = self.group
        self.start()
        body(g.chunk(g.me))
        self.sibling()
        body(g.chunk(g.sib))
        self.relay()
        body(g.chunk(g.peer))
        self.diagonal()
        body(g.chunk(g.diag))
        self.done()


class Scatter:
    def __init__(self, group, stage, land, total, sems):
        self.group, self.stage, self.land, self.total, self.sems = group, stage, land, total, sems

    def start(self, part):
        g, stage, land = self.group, self.stage, self.land
        self.first, self.over, self.near = [], [], []
        def split(owner):
            whole = part(g.chunk(owner))
            return [whole[j * g.part : (j + 1) * g.part] for j in range(PARTS)]

        for j, mine in enumerate(split(g.diag)):
            stage[0, j] = mine.astype(LOW)
            self.first.append(push(stage.at[0, j], land.at[0, j], self.sems, j, g.sib))
            self.first[-1].start()
        for j, mine in enumerate(split(g.peer)):
            self.first[j].wait_recv()
            stage[1, j] = (mine + land[0, j].astype(WIDE)).astype(LOW)
            self.over.append(push(stage.at[1, j], land.at[1, j], self.sems, PARTS + j, g.peer))
            self.over[-1].start()
        for j, mine in enumerate(split(g.sib)):
            stage[2, j] = mine.astype(LOW)
            self.near.append(push(stage.at[2, j], land.at[2, j], self.sems, 2 * PARTS + j, g.sib))
            self.near[-1].start()
        for j, mine in enumerate(split(g.me)):
            self.total[j] = mine

    def take(self, j):
        self.near[j].wait_recv()
        self.over[j].wait_recv()
        land = self.land
        return self.total[j] + (land[1, j].astype(WIDE) + land[2, j].astype(WIDE))

    def done(self):
        for copy in self.first + self.over + self.near:
            copy.wait_send()


class Deliver:
    def __init__(self, group, stage, out, sems):
        self.group, self.stage, self.out, self.sems = group, stage, out, sems

    def start(self, rows_ref):
        g, width = self.group, self.out.shape[1]
        for c in range(self.stage.shape[0]):
            self.stage[c] = rows_ref[:, c * width : (c + 1) * width]
        place = self.out.at[g.chunk(g.me)]
        self.copies = [
            push(self.stage.at[other], place, self.sems, n, other)
            for n, other in enumerate((g.peer, g.diag, g.sib))
        ]
        for copy in self.copies:
            copy.start()
        self.out[g.chunk(g.me), :] = self.stage[g.me]

    def done(self):
        for copy in self.copies:
            copy.wait()


def scatter_scratch(rows, width):
    part = rows // PARTS
    return [
        pltpu.VMEM((3, PARTS, part, width), LOW),
        pltpu.VMEM((3, PARTS, part, width), LOW),
        pltpu.VMEM((PARTS, part, width), WIDE),
        pltpu.SemaphoreType.DMA((2, 3 * PARTS)),
    ]


class Halves:
    def __init__(self, pair, whole, sems, slot):
        section = lax.axis_index("section")
        half = whole.shape[1] // 2
        self.copies = []
        for n, place in enumerate((section, 1 - section)):
            columns = pl.ds(pl.multiple_of(place * half, half), half)
            self.copies.append(
                pltpu.make_async_copy(pair[n], whole.at[:, columns], sems.at[slot + n])
            )

    def start(self):
        for copy in self.copies:
            copy.start()

    def wait(self):
        for copy in self.copies:
            copy.wait()


def attention_out(heads_ref, o3, lse_ref, heads):
    length = heads_ref.shape[1]
    size = min(TILE, length)

    @pl.loop(0, heads)
    def _(h):
        for i in range(length // size):
            rows = slice(i * size, (i + 1) * size)
            finish = (i + 1) * size
            queries = heads_ref[h, rows, :]
            scores = nt(heads_ref[heads + h, :finish, :], queries)
            keep = lax.broadcasted_iota(jnp.int32, (size, size), 0) <= lax.broadcasted_iota(
                jnp.int32, (size, size), 1
            )
            last = jnp.where(keep, scores[finish - size :], -1000000000.0)
            scores = last if i == 0 else jnp.concatenate([scores[: finish - size], last], 0)
            highest = jnp.max(scores, axis=0, keepdims=True)
            powers = jnp.exp(scores - highest)
            summed = jnp.sum(powers, axis=0, keepdims=True)
            mixed = tn(heads_ref[2 * heads + h, :finish, :], powers.astype(LOW))
            o3[h, rows, :] = (mixed / summed).T.astype(LOW)
            lse_ref[pl.ds(h, 1), rows] = highest + jnp.log(summed)


def attention_back(heads_ref, go3, lse_ref, dots_ref, g3, key_acc, value_acc, heads):
    length = heads_ref.shape[1]
    size = min(TILE, length)

    @pl.loop(0, heads)
    def _(h):
        for i in reversed(range(length // size)):
            rows = slice(i * size, (i + 1) * size)
            finish = (i + 1) * size
            queries = heads_ref[h, rows, :]
            keys = heads_ref[heads + h, :finish, :]
            grads = go3[h, rows, :]
            scores = nt(keys, queries) - lse_ref[pl.ds(h, 1), rows]
            keep = lax.broadcasted_iota(jnp.int32, (size, size), 0) <= lax.broadcasted_iota(
                jnp.int32, (size, size), 1
            )
            last = jnp.where(keep, scores[finish - size :], -1000000000.0)
            scores = last if i == 0 else jnp.concatenate([scores[: finish - size], last], 0)
            probs = jnp.exp(scores)
            grad_probs = nt(heads_ref[2 * heads + h, :finish, :], grads)
            grad_scores = (probs * (grad_probs - dots_ref[pl.ds(h, 1), rows])).astype(LOW)
            g3[h, rows, :] = (tn(grad_scores, keys) * HEAD ** (-0.5)).astype(LOW)
            key_part = nn(grad_scores, queries)
            value_part = nn(probs.astype(LOW), grads)
            if finish == length:
                key_acc[...] = key_part
                value_acc[...] = value_part
            else:
                key_acc[:finish, :] += key_part
                value_acc[:finish, :] += value_part
        g3[heads + h] = key_acc[...].astype(LOW)
        g3[2 * heads + h] = value_acc[...].astype(LOW)


def start_kernel(
    tokens_ref, cotangent_ref, small_ref, raw_ref, x_ref, g_ref, vectors_ref, got_ref,
    x4, g4, s4, other4, x_sems, g_sems, s_sems, local_sems,
):
    section = lax.axis_index("section")
    group = Group(x_ref.shape[0] // 4)
    length = x_ref.shape[0]
    loads = []
    rows = pl.ds(pl.multiple_of(section * length, length), length)
    for n, (source, into) in enumerate(((tokens_ref.at[rows], x4), (cotangent_ref.at[rows], g4), (small_ref, s4))):
        loads.append(pltpu.make_async_copy(source, into.at[group.me], local_sems.at[n]))
        loads[-1].start()
    group.greet(True, False)
    blocks = push(raw_ref, got_ref, s_sems, 3 * PARTS + 1, 1 - section, "section")
    blocks.start()
    gathers = [Gather(group, x4, x_sems, True), Gather(group, s4, s_sems, True), Gather(group, g4, g_sems, True)]
    for gather, load in zip(gathers, (loads[0], loads[2], loads[1])):
        load.wait()
        gather.start()
    for gather in gathers:
        gather.sibling()
        gather.relay()
        gather.diagonal()
    swap = push(s4, other4, s_sems, 3 * PARTS, 1 - section, "section")
    swap.start()
    width = x4.shape[2]
    for c in range(x4.shape[0]):
        x_ref[:, c * width : (c + 1) * width] = x4[c]
        g_ref[:, c * width : (c + 1) * width] = g4[c]
    swap.wait()
    blocks.wait()
    vectors_ref[section] = s4[...]
    vectors_ref[1 - section] = other4[...]
    for gather in gathers:
        gather.done()


def attend_kernel(
    gathered, heads, group, x_ref, mine_ref, other_ref, vec_ref, bias_ref,
    full_ref, normed_ref, heads_ref, o_ref, lse_ref, hidden_ref, second_ref,
    weight, o3, stage, land, total, scatter_sems, gather_sems, local_sems,
):
    width = o_ref.shape[1]
    halves = Halves((mine_ref, other_ref), weight, local_sems, 0)
    halves.start()
    if not gathered:
        full_ref[group.chunk(group.me), :] = x_ref[...]
    halves.wait()

    def project(rows):
        values = (x_ref if gathered else full_ref)[rows, :].astype(WIDE)
        hat, _ = normalise(values)
        normed = (hat * vec_ref[0:1, :] + vec_ref[1:2, :]).astype(LOW)
        normed_ref[rows, :] = normed
        mixed = nn(normed, weight[:, : 3 * width]) + bias_ref[...]
        for j in range(3 * heads):
            piece = mixed[:, j * HEAD : (j + 1) * HEAD]
            if j < heads:
                piece = piece * HEAD ** (-0.5)
            heads_ref[j, rows, :] = piece.astype(LOW)

    if gathered:
        full_ref[...] = jnp.zeros_like(full_ref)

        @pl.loop(0, LENGTH // group.rows)
        def _(n):
            project(group.chunk(n))
    else:
        Gather(group, full_ref, gather_sems).each(project)

    attention_out(heads_ref, o3, lse_ref, heads)
    for h in range(heads):
        o_ref[:, h * HEAD : (h + 1) * HEAD] = o3[h]

    scatter = Scatter(group, stage, land, total, scatter_sems)
    scatter.start(lambda rows: nt(o_ref[rows, :], weight[:, 3 * width :]))
    for j in range(PARTS):
        rows = slice(j * group.part, (j + 1) * group.part)
        residual = (x_ref if gathered else full_ref)[group.slab(group.me, j), :].astype(WIDE)
        hidden = residual + scatter.take(j) + vec_ref[2:3, :]
        hidden_ref[rows, :] = hidden
        hat, _ = normalise(hidden)
        second_ref[rows, :] = (hat * vec_ref[3:4, :] + vec_ref[4:5, :]).astype(LOW)
    scatter.done()


def widen_kernel(
    group, second_ref, em_ref, eo_ref, bias_ref,
    full_ref, active_ref, slope_ref,
    expand, gather_sems, local_sems,
):
    halves = Halves((em_ref, eo_ref), expand, local_sems, 0)
    halves.start()
    full_ref[group.chunk(group.me), :] = second_ref[...]
    halves.wait()

    def widen(rows):
        t = nn(full_ref[rows, :], expand[...]) + bias_ref[...]
        square = t * t
        bent = jnp.tanh(0.7978845608028654 * t * (1.0 + 0.044715 * square))
        active_ref[rows, :] = (0.5 * t * (1.0 + bent)).astype(LOW)
        slope_ref[rows, :] = (
            0.5 * (1.0 + bent)
            + (0.5 * 0.7978845608028654) * t * (1.0 - bent * bent) * (1.0 + 3 * 0.044715 * square)
        ).astype(LOW)

    Gather(group, full_ref, gather_sems).each(widen)


def outer_halves(left_ref, right_ref, keep_ref, send_ref):
    section = lax.axis_index("section")
    half = right_ref.shape[1] // 2
    for place, out in ((section, keep_ref), (1 - section, send_ref)):
        columns = pl.ds(pl.multiple_of(place * half, half), half)

        @pl.loop(0, left_ref.shape[1] // TILE)
        def _(n):
            rows = pl.ds(pl.multiple_of(n * TILE, TILE), TILE)
            out[rows, :] = tn(left_ref[:, rows], right_ref[:, columns]).astype(LOW)


def contract_kernel(last, group, *refs):
    active_ref, hidden_ref, cm_ref, co_ref, vec_ref, *refs = refs
    if last:
        g_ref, *refs = refs
    result_ref, *refs = refs
    if last:
        ck_ref, cs_ref, *refs = refs
    contract, stage, land, total, scatter_sems, local_sems = refs
    halves = Halves((cm_ref, co_ref), contract, local_sems, 0)
    halves.start()
    halves.wait()
    scatter = Scatter(group, stage, land, total, scatter_sems)
    scatter.start(lambda rows: nt(active_ref[rows, :], contract[...]))
    if last:
        outer_halves(g_ref, active_ref, ck_ref, cs_ref)
    for j in range(PARTS):
        rows = slice(j * group.part, (j + 1) * group.part)
        result = hidden_ref[rows, :] + scatter.take(j) + vec_ref[5:6, :]
        result_ref[rows, :] = result.astype(LOW)
    scatter.done()


def bend_kernel(last, group, g_ref, cm_ref, co_ref, slope_ref, extra_ref, *refs):
    before, sums_ref, *refs = refs
    if last:
        out_ref, *refs = refs
    else:
        full_ref, ck_ref, cs_ref, *refs = refs
    contract, gather_sems, local_sems, *refs = refs
    if last:
        stage4, deliver_sems = refs
        deliver = Deliver(group, stage4, out_ref, deliver_sems)
    halves = Halves((cm_ref, co_ref), contract, local_sems, 0)
    halves.start()
    sums_ref[...] = jnp.zeros_like(sums_ref)
    if last:
        deliver.start(extra_ref)
    else:
        full_ref[group.chunk(group.me), :] = g_ref[...]
    halves.wait()

    def bend(rows):
        rows_grad = (g_ref if last else full_ref)[rows, :]
        grad = (nn(rows_grad, contract[...]) * slope_ref[rows, :].astype(WIDE)).astype(LOW)
        before[rows, :] = grad
        sums_ref[0:1, :] += jnp.sum(grad.astype(WIDE), axis=0, keepdims=True)

    if last:

        @pl.loop(0, LENGTH // group.rows)
        def _(n):
            bend(group.chunk(n))

        deliver.done()
    else:
        Gather(group, full_ref, gather_sems).each(bend)
        outer_halves(full_ref, extra_ref, ck_ref, cs_ref)


def narrow_kernel(
    group, before, g_ref, em_ref, eo_ref, second_ref, hidden_ref, vec_ref,
    ek_ref, es_ref, grad_ref, low_ref, sums_ref,
    expand, stage, land, total, scatter_sems, local_sems,
):
    halves = Halves((em_ref, eo_ref), expand, local_sems, 0)
    halves.start()
    sums_ref[...] = jnp.zeros_like(sums_ref)
    halves.wait()
    scatter = Scatter(group, stage, land, total, scatter_sems)
    scatter.start(lambda rows: nt(before[rows, :], expand[...]))
    outer_halves(second_ref, before, ek_ref, es_ref)
    for j in range(PARTS):
        rows = slice(j * group.part, (j + 1) * group.part)
        grad = scatter.take(j)
        hat, scale = normalise(hidden_ref[rows, :])
        own = g_ref[rows, :].astype(WIDE)
        out = own + norm_backward(grad, hat, scale, vec_ref[3:4, :])
        grad_ref[rows, :] = out
        low_ref[rows, :] = out.astype(LOW)
        for n, term in enumerate((grad * hat, grad, own, out)):
            sums_ref[n : n + 1, :] += jnp.sum(term, axis=0, keepdims=True)
    scatter.done()


def scores_back_kernel(
    heads, group, low_ref, mine_ref, other_ref, heads_ref, o_ref, lse_ref,
    mixed, outer_ref,
    weight, full, go3, dots, g3, key_acc, value_acc, gather_sems, local_sems,
):
    width = o_ref.shape[1]
    halves = Halves((mine_ref, other_ref), weight, local_sems, 0)
    halves.start()
    full[group.chunk(group.me), :] = low_ref[...]
    halves.wait()
    picks = (
        lax.broadcasted_iota(jnp.int32, (8, width), 1) // HEAD
        == lax.broadcasted_iota(jnp.int32, (8, width), 0)
    ).astype(WIDE)

    def spread(rows):
        grads = nn(full[rows, :], weight[:, 3 * width :]).astype(LOW)
        for h in range(heads):
            go3[h, rows, :] = grads[:, h * HEAD : (h + 1) * HEAD]
        term = grads.astype(WIDE) * o_ref[rows, :].astype(WIDE)
        dots[:, rows] = lax.dot_general(
            picks,
            term,
            (((1,), (1,)), ((), ())),
            precision=lax.Precision.HIGHEST,
            preferred_element_type=WIDE,
        )

    Gather(group, full, gather_sems).each(spread)
    attention_back(heads_ref, go3, lse_ref, dots, g3, key_acc, value_acc, heads)
    for j in range(3 * heads):
        mixed[:, j * HEAD : (j + 1) * HEAD] = g3[j]

    @pl.loop(0, outer_ref.shape[0] // TILE)
    def _(n):
        rows = pl.ds(pl.multiple_of(n * TILE, TILE), TILE)
        outer_ref[rows, :] = tn(full[:, rows], o_ref[...]).astype(LOW)


def attend_back_kernel(
    last, group, mixed, outer_ref, grad_ref, x_ref, mine_ref, other_ref, normed_ref, vec_ref,
    wk_ref, ws_ref, out_ref, sums_ref, *refs,
):
    if not last:
        got_ref, *refs = refs
    weight, outer, stage, land, total, scatter_sems, local_sems, *refs = refs
    width = outer_ref.shape[1]
    section = lax.axis_index("section")
    halves = Halves((mine_ref, other_ref), weight, local_sems, 0)
    halves.start()
    sums_ref[...] = jnp.zeros_like(sums_ref)

    half = weight.shape[1] // 2

    def products():
        @pl.loop(0, weight.shape[0] // TILE)
        def _(n):
            rows = pl.ds(pl.multiple_of(n * TILE, TILE), TILE)
            outer[section, rows, :] = tn(normed_ref[:, rows], mixed[:, :half]).astype(LOW)
            outer[1 - section, rows, : 3 * width - half] = tn(
                normed_ref[:, rows], mixed[:, half:]
            ).astype(LOW)
            outer[1 - section, rows, 3 * width - half :] = outer_ref[rows, :]

    scatter = Scatter(group, stage, land, total, scatter_sems)
    if not last:
        products()
        swap = push(outer.at[1], got_ref, refs[0], 0, 1 - section, "section")
        swap.start()
    halves.wait()
    scatter.start(lambda rows: nt(mixed[rows, :], weight[:, : 3 * width]))
    if last:
        products()
    copies = [pltpu.make_async_copy(outer.at[0], wk_ref, local_sems.at[2])]
    if last:
        copies.append(pltpu.make_async_copy(outer.at[1], ws_ref, local_sems.at[3]))
    for copy in copies:
        copy.start()
    sums_ref[2:3, : 3 * width] = jnp.sum(mixed[...].astype(WIDE), axis=0, keepdims=True)
    for j in range(PARTS):
        rows = slice(j * group.part, (j + 1) * group.part)
        grad = scatter.take(j)
        hat, scale = normalise(x_ref[rows, :].astype(WIDE))
        out = grad_ref[rows, :] + norm_backward(grad, hat, scale, vec_ref[0:1, :])
        out_ref[rows, :] = out.astype(LOW)
        for n, term in enumerate((grad * hat, grad)):
            sums_ref[n : n + 1, :] += jnp.sum(term, axis=0, keepdims=True)
    scatter.done()
    for copy in copies:
        copy.wait()
    if not last:
        swap.wait()


def finish_kernel(
    near_ref, far_ref, a0, n0, b0, a1, n1, b1, grads_ref, sums_ref,
    mine, stage4, block, land_col, land_x, land_z, send, land,
    deliver_sems, col_sems, x_sems, z_sems,
):
    section, row = lax.axis_index("section"), lax.axis_index("row")
    group = Group(near_ref.shape[0])
    length, width = far_ref.shape
    others = [lax.rem(row + d, land_z.shape[0]) for d in range(1, land_z.shape[0])]
    group.greet(True, True, others)
    deliver = Deliver(group, stage4, mine, deliver_sems)
    deliver.start(near_ref)

    block[...] = jnp.zeros_like(block)
    for layer, (attn, narrow, bend) in enumerate(((a0, n0, b0), (a1, n1, b1))):
        wide = [attn[0:1, :], attn[1:2, :], narrow[3:4, :], narrow[0:1, :], narrow[1:2, :], narrow[2:3, :]]
        for c in range(block.shape[0]):
            columns = slice(c * width, (c + 1) * width)
            for n, term in enumerate(wide):
                block[c, layer, n : n + 1, :] = term[:, columns]
            for n, term in enumerate((attn[2:3, :width], attn[2:3, 2 * width : 3 * width])):
                block[c, layer, 8 + n : 9 + n, :] = term
            for n in range(bend.shape[1] // width):
                block[c, layer, 10 + n : 11 + n, :] = bend[0:1, n * width : (n + 1) * width]
    copies = [
        push(block.at[other, :, pl.ds(0, 8)], land_col.at[n], col_sems, n, other)
        for n, other in enumerate((group.peer, group.diag, group.sib))
    ]
    for copy in copies:
        copy.start()
    for copy in copies:
        copy.wait()
    me = group.me
    block[me, :, :8] = block[me, :, :8] + (land_col[0] + (land_col[1] + land_col[2]))
    swap = push(block.at[me, 1 - section], land_x, x_sems, 0, 1 - section, "section")
    swap.start()
    swap.wait()
    land_z[row] = block[me, section] + land_x[...]
    copies = [
        push(land_z.at[row], land_z.at[row], z_sems, n, other, "row")
        for n, other in enumerate(others)
    ]
    for copy in copies:
        copy.start()

    deliver.done()

    @pl.when(section == 0)
    def _():
        send[...] = far_ref[...]

    @pl.when(section == 1)
    def _():
        send[...] = mine[...]

    swap = push(send, land, x_sems, 1, 1 - section, "section")
    swap.start()
    own = pl.ds(pl.multiple_of(section * length, length), length)
    away = pl.ds(pl.multiple_of((1 - section) * length, length), length)

    @pl.when(section == 0)
    def _():
        grads_ref[own, :] = mine[...].astype(WIDE)

    @pl.when(section == 1)
    def _():
        grads_ref[own, :] = far_ref[...].astype(WIDE)

    for copy in copies:
        copy.wait()
    result = land_z[0]
    for n in range(1, land_z.shape[0]):
        result = result + land_z[n]
    sums_ref[...] = result
    swap.wait()
    grads_ref[away, :] = land[...].astype(WIDE)


VM = pl.BlockSpec(memory_space=pltpu.VMEM)
ANY = pl.BlockSpec(memory_space=pl.ANY)
PAIRS = pltpu.SemaphoreType.DMA((2, 3 * PARTS))
LOCAL = pltpu.SemaphoreType.DMA((4,))


def shape(dims, kind=LOW):
    return jax.ShapeDtypeStruct(dims, kind)


def launch(body, number, rows, in_specs, ins, outs, out_specs, scratch, swaps=(), diagonal=False, across=False, flops=3e10):
    def kernel(*refs):
        n_in, n_out, n = len(in_specs), len(outs), len(swaps)
        group = Group(rows)
        group.greet(n or across, diagonal)
        sources, lands = refs[n_in : n_in + n], refs[n_in + n + n_out : n_in + 2 * n + n_out]
        other = 1 - lax.axis_index("section")
        copies = [
            push(source, land, refs[-1], i, other, "section")
            for i, (source, land) in enumerate(zip(sources, lands))
        ]
        for copy in copies:
            copy.start()
        rest = refs[n_in + 2 * n + n_out :]
        body(group, *refs[:n_in], *refs[n_in + n : n_in + n + n_out], *(rest[:-1] if n else rest))
        for copy in copies:
            copy.wait()

    extra = [pltpu.SemaphoreType.DMA((2, len(swaps)))] if swaps else []
    held = [a for a, spec in zip((*ins, *outs), (*in_specs, *out_specs)) if spec is VM]
    held += [s for s in scratch if s.memory_space == pltpu.VMEM]
    need = sum(math.prod(s.shape[:-1]) * (-(-s.shape[-1] // 128) * 128) * s.dtype.itemsize for s in held)
    results = pl.pallas_call(
        kernel,
        out_shape=(*outs, *[shape(s.shape, s.dtype) for s in swaps]),
        in_specs=[*in_specs, *[ANY] * len(swaps)],
        out_specs=(*out_specs, *[ANY] * len(swaps)),
        scratch_shapes=[*scratch, *extra],
        compiler_params=pltpu.CompilerParams(
            collective_id=number, has_side_effects=True, vmem_limit_bytes=min(need + SPARE, 58 * MEBI)
        ),
        cost_estimate=pl.CostEstimate(
            flops=int(flops), bytes_accessed=30 * MEBI, transcendentals=0
        ),
    )(*ins, *swaps)
    return results[: len(outs)], results[len(outs) :]


def start_call(number, tokens, cotangent, small, raw, columns):
    width = tokens.shape[1]
    size = width * columns
    kinds = small.shape[0]
    outs = (shape((LENGTH, size)), shape((LENGTH, size)), shape((2, columns, kinds, width)), shape(raw.shape))
    blocks = pltpu.VMEM((columns, LENGTH, width), LOW)
    vectors = pltpu.VMEM((columns, kinds, width), LOW)
    return pl.pallas_call(
        start_kernel,
        out_shape=outs,
        in_specs=[ANY] * 4,
        out_specs=(VM, VM, VM, ANY),
        scratch_shapes=[
            blocks, blocks, vectors, vectors, PAIRS, PAIRS,
            pltpu.SemaphoreType.DMA((2, 3 * PARTS + 2)), LOCAL,
        ],
        compiler_params=pltpu.CompilerParams(
            collective_id=number, has_side_effects=True, vmem_limit_bytes=56 * MEBI
        ),
        cost_estimate=pl.CostEstimate(flops=int(3e10), bytes_accessed=30 * MEBI, transcendentals=0),
    )(tokens, cotangent, small, raw)


def attend_call(number, gathered, x, pair, vec, bias, rows, width, swaps):
    size = vec.shape[1]
    heads = width // HEAD
    outs = (
        shape((LENGTH, size) if not gathered else (16, 128)),
        shape((LENGTH, size)),
        shape((3 * heads, LENGTH, HEAD)),
        shape((LENGTH, width)),
        shape((8, LENGTH), WIDE),
        shape((rows, size), WIDE),
        shape((rows, size)),
    )
    scratch = [
        pltpu.VMEM((size, 4 * width), LOW),
        pltpu.VMEM((heads, LENGTH, HEAD), LOW),
        *scatter_scratch(rows, size), PAIRS, LOCAL,
    ]
    return launch(
        functools.partial(attend_kernel, gathered, heads),
        number, rows, [VM, ANY, ANY, VM, VM], (x, *pair, vec, bias), outs, (VM,) * 7, scratch, swaps,
    )


def widen_call(number, second, pair, bias, swaps):
    rows, size = second.shape
    wide = bias.shape[1]
    outs = (shape((LENGTH, size)), shape((LENGTH, wide)), shape((LENGTH, wide)))
    scratch = [pltpu.VMEM((size, wide), LOW), PAIRS, LOCAL]
    return launch(
        widen_kernel, number, rows, [VM, ANY, ANY, VM], (second, *pair, bias), outs, (VM,) * 3, scratch, swaps
    )


def contract_call(number, active, hidden, pair, vec, grad, swaps):
    rows, size = hidden.shape
    wide = active.shape[1]
    last = grad is not None
    outs = [shape((rows, size))]
    scratch = [pltpu.VMEM((size, wide), LOW), *scatter_scratch(rows, size), LOCAL]
    in_specs, ins = [VM, VM, ANY, ANY, VM], [active, hidden, *pair, vec]
    if last:
        in_specs, ins = in_specs + [VM], ins + [grad]
        outs += [shape((size, wide // 2))] * 2
    return launch(
        functools.partial(contract_kernel, last),
        number, rows, in_specs, ins, outs, (VM,) * len(outs), scratch, swaps,
    )


def bend_call(number, last, grad, pair, slope, extra, size, rows, swaps):
    wide = slope.shape[1]
    columns = LENGTH // rows
    outs = [shape((LENGTH, wide)), shape((8, wide), WIDE)]
    scratch = [pltpu.VMEM((size, wide), LOW), PAIRS, LOCAL]
    if last:
        outs += [shape((LENGTH, size // columns))]
        scratch += [pltpu.VMEM((columns, rows, size // columns), LOW), pltpu.SemaphoreType.DMA((2, 3))]
    else:
        outs += [shape((LENGTH, size)), *[shape((size, wide // 2))] * 2]
    return launch(
        functools.partial(bend_kernel, last),
        number, rows, [VM, ANY, ANY, VM, VM], (grad, *pair, slope, extra),
        outs, (VM,) * len(outs), scratch, swaps, last,
    )


def narrow_call(number, before, grad_own, pair, second, hidden, vec, swaps):
    rows, size = hidden.shape
    wide = before.shape[1]
    outs = (
        *[shape((size, wide // 2))] * 2,
        shape((rows, size), WIDE),
        shape((rows, size)),
        shape((8, size), WIDE),
    )
    scratch = [pltpu.VMEM((size, wide), LOW), *scatter_scratch(rows, size), LOCAL]
    return launch(
        narrow_kernel,
        number, rows, [VM, VM, ANY, ANY, VM, VM, VM], (before, grad_own, *pair, second, hidden, vec),
        outs, (VM,) * 5, scratch, swaps,
    )


def scores_back_call(number, low, pair, heads_all, o, lse, swaps):
    rows, size = low.shape
    width = o.shape[1]
    heads = width // HEAD
    outs = (shape((LENGTH, 3 * width)), shape((size, width)))
    scratch = [
        pltpu.VMEM((size, 4 * width), LOW),
        pltpu.VMEM((LENGTH, size), LOW),
        pltpu.VMEM((heads, LENGTH, HEAD), LOW),
        pltpu.VMEM((8, LENGTH), WIDE),
        pltpu.VMEM((3 * heads, LENGTH, HEAD), LOW),
        pltpu.VMEM((LENGTH, HEAD), WIDE),
        pltpu.VMEM((LENGTH, HEAD), WIDE),
        PAIRS, LOCAL,
    ]
    return launch(
        functools.partial(scores_back_kernel, heads),
        number, rows, [VM, ANY, ANY, VM, VM, VM], (low, *pair, heads_all, o, lse),
        outs, (VM,) * 2, scratch, swaps,
    )


def attend_back_call(number, last, mixed, outer, grad, x_own, pair, normed, vec, swaps):
    rows, size = grad.shape
    width = outer.shape[1]
    half = 2 * width
    outs = [shape((size, half)), shape((size, half)), shape((rows, size)), shape((8, size), WIDE)]
    out_specs = [ANY, ANY, VM, VM]
    scratch = [
        pltpu.VMEM((size, 4 * width), LOW),
        pltpu.VMEM((2, size, half), LOW),
        *scatter_scratch(rows, size), LOCAL,
    ]
    if not last:
        outs[1] = shape((16, 128))
        outs, out_specs = outs + [shape((size, half))], out_specs + [ANY]
        scratch += [pltpu.SemaphoreType.DMA((2, 1))]
    return launch(
        functools.partial(attend_back_kernel, last),
        number, rows, [VM, VM, VM, VM, ANY, ANY, VM, VM],
        (mixed, outer, grad, x_own, *pair, normed, vec), outs, out_specs, scratch, swaps, False, True,
    )


def finish_call(number, near, far, sums, row_count):
    rows, size = near.shape
    length, width = far.shape
    columns = length // rows
    outs = (shape((2 * length, width), WIDE), shape((16, width), WIDE))
    scratch = [
        pltpu.VMEM((length, width), LOW),
        pltpu.VMEM((columns, rows, width), LOW),
        pltpu.VMEM((columns, 2, 16, width), WIDE),
        pltpu.VMEM((3, 2, 8, width), WIDE),
        pltpu.VMEM((16, width), WIDE),
        pltpu.VMEM((row_count, 16, width), WIDE),
        pltpu.VMEM((length, width), LOW),
        pltpu.VMEM((length, width), LOW),
        pltpu.SemaphoreType.DMA((2, 3)),
        pltpu.SemaphoreType.DMA((2, 3)),
        pltpu.SemaphoreType.DMA((2, 2)),
        pltpu.SemaphoreType.DMA((2, row_count)),
    ]
    return pl.pallas_call(
        finish_kernel,
        out_shape=outs,
        in_specs=[VM] * 8,
        out_specs=(VM, VM),
        scratch_shapes=scratch,
        compiler_params=pltpu.CompilerParams(
            collective_id=number, has_side_effects=True, vmem_limit_bytes=32 * MEBI
        ),
        cost_estimate=pl.CostEstimate(flops=int(3e10), bytes_accessed=30 * MEBI, transcendentals=0),
    )(near, far, *sums)


def swap_sections(value):
    return lax.ppermute(value, "section", [(0, 1), (1, 0)])


def on_device(
    tokens,
    cotangent,
    first_gain,
    first_shift,
    attend_weight,
    attend_bias,
    output_weight,
    output_bias,
    second_gain,
    second_shift,
    expand_weight,
    expand_bias,
    contract_weight,
    contract_bias,
):
    section = lax.axis_index("section")
    column = lax.axis_index("col")
    first_section = section == 0
    columns = lax.axis_size("col")
    width = tokens.shape[1]
    size = width * columns
    rows = LENGTH // columns

    def pick(early, later):
        return jnp.where(first_section, early, later)

    block_rows = attend_weight.shape[1]
    units = (
        jnp.concatenate(
            [attend_weight[0].reshape(block_rows, 3 * width), output_weight[0].T], axis=1
        ),
        expand_weight[0],
        contract_weight[0].T,
    )
    kept_blocks, sent_blocks = [], []
    for unit in units:
        half = unit.shape[1] // 2
        low, high = unit[:, :half], unit[:, half:]
        kept_blocks.append(pick(low, high))
        sent_blocks.append(pick(high, low))

    small = jnp.concatenate(
        [
            first_gain,
            first_shift,
            output_bias,
            second_gain,
            second_shift,
            contract_bias,
            attend_bias[0],
            expand_bias[0].reshape(-1, width),
        ],
        0,
    )
    filled = small.shape[0]
    small = jnp.pad(small, ((0, -filled % 16), (0, 0)))
    got_attend = swap_sections(sent_blocks[0])
    raw = jnp.stack(sent_blocks[1:])
    got_attend, raw = lax.optimization_barrier((got_attend, raw))
    x0_full, gy_full, vectors, got_blocks = start_call(1, tokens, cotangent, small, raw, columns)
    mats = [[], []]
    for own, got in zip(kept_blocks, (got_attend, got_blocks[0], got_blocks[1])):
        for layer, block in enumerate((pick(own, got), pick(got, own))):
            mats[layer].append(lax.all_gather(block, "row", axis=0, tiled=True))
    vectors = vectors.astype(WIDE)
    wide_vectors = jnp.swapaxes(vectors[:, :, :6], 1, 2).reshape(2, 6, size)
    wide_vectors = jnp.pad(wide_vectors, ((0, 0), (0, 2), (0, 0)))
    own_vectors = lax.dynamic_index_in_dim(vectors, column, 1, keepdims=False)
    attend_biases = jnp.stack(
        [own_vectors[:, 6], jnp.zeros_like(own_vectors[:, 6]), own_vectors[:, 7]], 1
    ).reshape(2, 1, 3 * width)
    expand_biases = own_vectors[:, 8:filled].reshape(2, 1, -1)

    def own_rows(full):
        return lax.dynamic_slice_in_dim(full, column * rows, rows, 0)

    def own_features(full):
        return lax.dynamic_slice_in_dim(full, column * width, width, 1)

    attn = (mats[0][0], swap_sections(mats[0][0]))
    x = x0_full
    kept, pairs = [], []
    owns = [own_rows(x0_full)]
    for layer in range(2):
        last = layer == 1
        vec = wide_vectors[layer]
        (full, normed, heads, o, lse, hidden, second_own), (other,) = attend_call(
            2 + 3 * layer, not last, x, attn, vec, attend_biases[layer], rows, width, [mats[layer][1]]
        )
        expand = (mats[layer][1], other)
        (second, active, slope), (other,) = widen_call(
            3 + 3 * layer, second_own, expand, expand_biases[layer], [mats[layer][2]]
        )
        contract = (mats[layer][2], other)
        outs, others = contract_call(
            4 + 3 * layer, active, hidden, contract, vec,
            gy_full if last else None, [] if last else [mats[1][0]],
        )
        pairs.append((attn, expand, contract))
        kept.append((normed, heads, o, lse, hidden, second, active, slope))
        x = outs[0]
        owns.append(x)
        if last:
            ck1, cs1 = outs[1:]
        else:
            attn = (mats[1][0], others[0])
    y0 = own_features(full)

    def add(keep, got, then):
        total = (keep.astype(WIDE) + got.astype(WIDE)).astype(LOW)
        return lax.optimization_barrier((total, then))

    def scatter(total):
        return lax.psum_scatter(total, "row", scatter_dimension=0, tiled=True)

    def tie(value, then):
        return lax.optimization_barrier((value, then))

    attn, expand, contract = pairs[1]
    normed, heads, o, lse, hidden, second, active, slope = kept[1]
    (before, bend_sums1, y1), _ = bend_call(8, True, gy_full, contract, slope, owns[2], size, rows, [])
    layer_low, layer_high = pick(y0, y1), pick(y1, y0)
    (ek1, es1, grad_hidden, low, narrow_sums1), (ct1,) = narrow_call(
        9, before, own_rows(gy_full), expand, second, hidden, wide_vectors[1], [cs1]
    )
    total_c1, low = add(ck1, ct1, low)
    (mixed, outer), (et1,) = scores_back_call(10, low, attn, heads, o, lse, [es1])
    total_e1, mixed = add(ek1, et1, mixed)
    part_c1, mixed = tie(scatter(total_c1), mixed)
    (wk1, ws1, gx1_own, attend_sums1), (layer_got,) = attend_back_call(
        11, True, mixed, outer, grad_hidden, owns[1], attn, normed, wide_vectors[1], [layer_high]
    )
    layer_outputs = jnp.concatenate([pick(layer_low, layer_got), pick(layer_got, layer_low)], 0)

    attn, expand, contract = pairs[0]
    normed, heads, o, lse, hidden, second, active, slope = kept[0]
    (before, bend_sums0, gx1_full, ck0, cs0), (wt1,) = bend_call(
        12, False, gx1_own, contract, slope, active, size, rows, [ws1]
    )
    total_w1, before = add(wk1, wt1, before)
    part_e1, before = tie(scatter(total_e1), before)
    (ek0, es0, grad_hidden, low, narrow_sums0), (ct0,) = narrow_call(
        13, before, gx1_own, expand, second, hidden, wide_vectors[0], [cs0]
    )
    total_c0, low = add(ck0, ct0, low)
    part_w1, low = tie(scatter(total_w1), low)
    (mixed, outer), (et0,) = scores_back_call(14, low, attn, heads, o, lse, [es0])
    total_e0, mixed = add(ek0, et0, mixed)
    part_c0, mixed = tie(scatter(total_c0), mixed)
    (wk0, _, gx0_own, attend_sums0, wt0), _ = attend_back_call(
        15, False, mixed, outer, grad_hidden, owns[0], attn, normed, wide_vectors[0], []
    )
    total_w0, gx0_own = add(wk0, wt0, gx0_own)
    part_e0, gx0_own = tie(scatter(total_e0), gx0_own)
    input_grads, small_grads = finish_call(
        16,
        gx0_own,
        own_features(gx1_full),
        (attend_sums0, narrow_sums0, bend_sums0, attend_sums1, narrow_sums1, bend_sums1),
        lax.axis_size("row"),
    )

    late = [part_w1, part_e1, part_c1]
    part_w0, small_grads = tie(scatter(total_w0), small_grads)
    early = [part_w0, part_e0, part_c0]
    units = []
    for second_layer, first_layer in zip(late, early):
        stays = pick(first_layer, second_layer)
        got = swap_sections(pick(second_layer, first_layer))
        units.append(jnp.concatenate([pick(stays, got), pick(got, stays)], 1).astype(WIDE))
    attn_part, expand_part, contract_part = units

    return (
        layer_outputs[None],
        input_grads[None],
        small_grads[0:1],
        small_grads[1:2],
        attn_part[:, : 3 * width].reshape(block_rows, 3, width)[None],
        small_grads[8:10][None],
        attn_part[:, 3 * width :].T[None],
        small_grads[2:3],
        small_grads[3:4],
        small_grads[4:5],
        expand_part[None],
        small_grads[10 : 10 + expand_bias.shape[1] // width].reshape(1, -1),
        contract_part.T[None],
        small_grads[5:6],
    )


def solution(mesh):
    return jax.shard_map(
        on_device,
        mesh=mesh,
        in_specs=(
            P("row", "col"),
            P("row", "col"),
            P("section", "col"),
            P("section", "col"),
            P("section", "row", None, "col"),
            P("section", None, "col"),
            P("section", "col", "row"),
            P("section", "col"),
            P("section", "col"),
            P("section", "col"),
            P("section", "row", "col"),
            P("section", "col"),
            P("section", "col", "row"),
            P("section", "col"),
        ),
        out_specs=(
            P("section", "row", "col"),
            P("section", "row", "col"),
            P("section", "col"),
            P("section", "col"),
            P("section", "row", None, "col"),
            P("section", None, "col"),
            P("section", "col", "row"),
            P("section", "col"),
            P("section", "col"),
            P("section", "col"),
            P("section", "row", "col"),
            P("section", "col"),
            P("section", "col", "row"),
            P("section", "col"),
        ),
        check_vma=False,
    )
```

```python
import functools

import jax
import jax.numpy as jnp
from jax import lax
from jax.experimental import pallas as pl
from jax.experimental.pallas import tpu as pltpu
from jax.sharding import PartitionSpec as P

HEAD = 64
LENGTH = 1024
EPS = 1e-05
LOW = jnp.bfloat16
WIDE = jnp.float32
MESH = pl.DeviceIdType.MESH
PARTS = 2
TILE = 256
MEBI = 1024 * 1024
GRANT = 58 * MEBI


def nn(left, right):
    return lax.dot_general(left, right, (((1,), (0,)), ((), ())), preferred_element_type=WIDE)


def nt(left, right):
    return lax.dot_general(left, right, (((1,), (1,)), ((), ())), preferred_element_type=WIDE)


def tn(left, right):
    return lax.dot_general(left, right, (((0,), (0,)), ((), ())), preferred_element_type=WIDE)


def normalise(values):
    center = jnp.mean(values, axis=1, keepdims=True)
    centred = values - center
    scale = lax.rsqrt(jnp.mean(centred * centred, axis=1, keepdims=True) + EPS)
    return centred * scale, scale


def norm_backward(grad, hat, scale, gain):
    scaled = grad * gain
    mean_one = jnp.mean(scaled, axis=1, keepdims=True)
    mean_two = jnp.mean(scaled * hat, axis=1, keepdims=True)
    return scale * (scaled - mean_one - hat * mean_two)


class Group:
    def __init__(self, rows):
        self.me = lax.axis_index("col")
        chip, core = self.me // 2, self.me % 2
        self.sib = chip * 2 + 1 - core
        self.peer = (1 - chip) * 2 + core
        self.diag = (1 - chip) * 2 + 1 - core
        self.rows = rows
        self.part = rows // PARTS
        self.loads, self.stores, self.begun = {}, {}, set()

    def need(self, *places):
        for place in places:
            self.loads[place].wait()

    def emit(self, *places):
        for place in places:
            self.stores[place].start()
            self.begun.add(place)

    def greet(self, swaps, diagonal, rows=()):
        barrier = pltpu.get_barrier_semaphore()
        others = [{"col": self.sib}, {"col": self.peer}]
        if diagonal:
            others.append({"col": self.diag})
        if swaps:
            others.append({"section": 1 - lax.axis_index("section")})
        others += [{"row": row} for row in rows]
        for other in others:
            pl.semaphore_signal(barrier, inc=1, device_id=other, device_id_type=MESH)
        pl.semaphore_wait(barrier, len(others))

    def slab(self, owner, j):
        return pl.ds(pl.multiple_of(owner * self.rows + j * self.part, self.part), self.part)

    def chunk(self, owner):
        return pl.ds(pl.multiple_of(owner * self.rows, self.rows), self.rows)


def push(src, dst, sems, slot, target, axis="col"):
    return pltpu.make_async_remote_copy(
        src_ref=src,
        dst_ref=dst,
        send_sem=sems.at[0, slot],
        recv_sem=sems.at[1, slot],
        device_id={axis: target},
        device_id_type=MESH,
    )


class Gather:
    def __init__(self, group, full, sems, blocks=False):
        self.group, self.full, self.sems, self.blocks = group, full, sems, blocks

    def piece(self, owner, j):
        if not self.blocks:
            return self.full.at[self.group.slab(owner, j)]
        part = self.full.shape[1] // PARTS
        return self.full.at[owner, pl.ds(j * part, part)]

    def start(self):
        g = self.group
        self.over, self.near, self.relayed = [], [], []
        for j in range(PARTS):
            piece = self.piece(g.me, j)
            self.over.append(push(piece, piece, self.sems, j, g.peer))
            self.over[-1].start()
        for j in range(PARTS):
            piece = self.piece(g.me, j)
            self.near.append(push(piece, piece, self.sems, PARTS + j, g.sib))
            self.near[-1].start()

    def sibling(self):
        for copy in self.near:
            copy.wait_recv()

    def relay(self):
        g = self.group
        for j in range(PARTS):
            self.over[j].wait_recv()
            piece = self.piece(g.peer, j)
            self.relayed.append(push(piece, piece, self.sems, 2 * PARTS + j, g.sib))
            self.relayed[-1].start()

    def diagonal(self):
        for copy in self.relayed:
            copy.wait_recv()

    def done(self):
        for copy in self.over + self.near + self.relayed:
            copy.wait_send()

    def each(self, body, first=None):
        g = self.group
        self.start()
        if first is not None:
            first()
        body(g.chunk(g.me))
        self.sibling()
        body(g.chunk(g.sib))
        self.relay()
        body(g.chunk(g.peer))
        self.diagonal()
        body(g.chunk(g.diag))
        self.done()


class Scatter:
    def __init__(self, group, stage, land, total, sems):
        self.group, self.stage, self.land, self.total, self.sems = group, stage, land, total, sems

    def start(self, part):
        g, stage, land = self.group, self.stage, self.land
        self.first, self.over, self.near = [], [], []
        def split(owner):
            whole = part(g.chunk(owner))
            return [whole[j * g.part : (j + 1) * g.part] for j in range(PARTS)]

        for j, mine in enumerate(split(g.diag)):
            stage[0, j] = mine.astype(LOW)
            self.first.append(push(stage.at[0, j], land.at[0, j], self.sems, j, g.sib))
            self.first[-1].start()
        for j, mine in enumerate(split(g.peer)):
            self.first[j].wait_recv()
            stage[1, j] = (mine + land[0, j].astype(WIDE)).astype(LOW)
            self.over.append(push(stage.at[1, j], land.at[1, j], self.sems, PARTS + j, g.peer))
            self.over[-1].start()
        for j, mine in enumerate(split(g.sib)):
            stage[2, j] = mine.astype(LOW)
            self.near.append(push(stage.at[2, j], land.at[2, j], self.sems, 2 * PARTS + j, g.sib))
            self.near[-1].start()
        for j, mine in enumerate(split(g.me)):
            self.total[j] = mine

    def take(self, j):
        self.near[j].wait_recv()
        self.over[j].wait_recv()
        land = self.land
        return self.total[j] + (land[1, j].astype(WIDE) + land[2, j].astype(WIDE))

    def done(self):
        for copy in self.first + self.over + self.near:
            copy.wait_send()


class Deliver:
    def __init__(self, group, stage, out, sems):
        self.group, self.stage, self.out, self.sems = group, stage, out, sems

    def start(self, rows_ref):
        g, width = self.group, self.out.shape[1]
        for c in range(self.stage.shape[0]):
            self.stage[c] = rows_ref[:, c * width : (c + 1) * width]
        place = self.out.at[g.chunk(g.me)]
        self.copies = [
            push(self.stage.at[other], place, self.sems, n, other)
            for n, other in enumerate((g.peer, g.diag, g.sib))
        ]
        for copy in self.copies:
            copy.start()
        self.out[g.chunk(g.me), :] = self.stage[g.me]

    def done(self):
        for copy in self.copies:
            copy.wait()


def scatter_scratch(rows, width):
    part = rows // PARTS
    return [
        pltpu.VMEM((3, PARTS, part, width), LOW),
        pltpu.VMEM((3, PARTS, part, width), LOW),
        pltpu.VMEM((PARTS, part, width), WIDE),
        pltpu.SemaphoreType.DMA((2, 3 * PARTS)),
    ]


class Halves:
    def __init__(self, pair, whole, sems, slot):
        section = lax.axis_index("section")
        half = whole.shape[1] // 2
        self.copies = []
        for n, place in enumerate((section, 1 - section)):
            columns = pl.ds(pl.multiple_of(place * half, half), half)
            self.copies.append(
                pltpu.make_async_copy(pair[n], whole.at[:, columns], sems.at[slot + n])
            )

    def start(self):
        for copy in self.copies:
            copy.start()

    def wait(self):
        for copy in self.copies:
            copy.wait()


def attention_out(heads_ref, o3, lse_ref, heads):
    length = heads_ref.shape[1]
    size = min(TILE, length)

    @pl.loop(0, heads)
    def _(h):
        for i in range(length // size):
            rows = slice(i * size, (i + 1) * size)
            finish = (i + 1) * size
            queries = heads_ref[h, rows, :]
            scores = nt(heads_ref[heads + h, :finish, :], queries)
            keep = lax.broadcasted_iota(jnp.int32, (size, size), 0) <= lax.broadcasted_iota(
                jnp.int32, (size, size), 1
            )
            last = jnp.where(keep, scores[finish - size :], -1000000000.0)
            scores = last if i == 0 else jnp.concatenate([scores[: finish - size], last], 0)
            highest = jnp.max(scores, axis=0, keepdims=True)
            powers = jnp.exp(scores - highest)
            summed = jnp.sum(powers, axis=0, keepdims=True)
            mixed = tn(heads_ref[2 * heads + h, :finish, :], powers.astype(LOW))
            o3[h, rows, :] = (mixed / summed).T.astype(LOW)
            lse_ref[pl.ds(h, 1), rows] = highest + jnp.log(summed)


def attention_back(heads_ref, go3, lse_ref, dots_ref, g3, key_acc, value_acc, heads):
    length = heads_ref.shape[1]
    size = min(TILE, length)

    @pl.loop(0, heads)
    def _(h):
        for i in reversed(range(length // size)):
            rows = slice(i * size, (i + 1) * size)
            finish = (i + 1) * size
            queries = heads_ref[h, rows, :]
            keys = heads_ref[heads + h, :finish, :]
            grads = go3[h, rows, :]
            scores = nt(keys, queries) - lse_ref[pl.ds(h, 1), rows]
            keep = lax.broadcasted_iota(jnp.int32, (size, size), 0) <= lax.broadcasted_iota(
                jnp.int32, (size, size), 1
            )
            last = jnp.where(keep, scores[finish - size :], -1000000000.0)
            scores = last if i == 0 else jnp.concatenate([scores[: finish - size], last], 0)
            probs = jnp.exp(scores)
            grad_probs = nt(heads_ref[2 * heads + h, :finish, :], grads)
            grad_scores = (probs * (grad_probs - dots_ref[pl.ds(h, 1), rows])).astype(LOW)
            g3[h, rows, :] = (tn(grad_scores, keys) * HEAD ** (-0.5)).astype(LOW)
            key_part = nn(grad_scores, queries)
            value_part = nn(probs.astype(LOW), grads)
            if finish == length:
                key_acc[...] = key_part
                value_acc[...] = value_part
            else:
                key_acc[:finish, :] += key_part
                value_acc[:finish, :] += value_part
        g3[heads + h] = key_acc[...].astype(LOW)
        g3[2 * heads + h] = value_acc[...].astype(LOW)


def start_kernel(
    tokens_ref, cotangent_ref, small_ref, raw_ref, x_ref, g_ref, vectors_ref, got_ref,
    x4, g4, s4, other4, x_sems, g_sems, s_sems, local_sems,
):
    section = lax.axis_index("section")
    group = Group(x_ref.shape[0] // 4)
    length = x_ref.shape[0]
    loads = []
    rows = pl.ds(pl.multiple_of(section * length, length), length)
    for n, (source, into) in enumerate(((tokens_ref.at[rows], x4), (cotangent_ref.at[rows], g4), (small_ref, s4))):
        loads.append(pltpu.make_async_copy(source, into.at[group.me], local_sems.at[n]))
        loads[-1].start()
    group.greet(True, False)
    blocks = push(raw_ref, got_ref, s_sems, 3 * PARTS + 1, 1 - section, "section")
    blocks.start()
    gathers = [Gather(group, x4, x_sems, True), Gather(group, s4, s_sems, True), Gather(group, g4, g_sems, True)]
    for gather, load in zip(gathers, (loads[0], loads[2], loads[1])):
        load.wait()
        gather.start()
    for gather in gathers:
        gather.sibling()
        gather.relay()
        gather.diagonal()
    swap = push(s4, other4, s_sems, 3 * PARTS, 1 - section, "section")
    swap.start()
    width = x4.shape[2]
    for c in range(x4.shape[0]):
        x_ref[:, c * width : (c + 1) * width] = x4[c]
        g_ref[:, c * width : (c + 1) * width] = g4[c]
    swap.wait()
    blocks.wait()
    vectors_ref[section] = s4[...]
    vectors_ref[1 - section] = other4[...]
    for gather in gathers:
        gather.done()


def attend_kernel(
    gathered, heads, group, x_ref, mine_ref, other_ref, vec_ref, bias_ref,
    full_ref, normed_ref, heads_ref, o_ref, lse_ref, hidden_ref, second_ref,
    weight, o3, stage, land, total, scatter_sems, gather_sems, local_sems,
):
    width = o_ref.shape[1]
    halves = Halves((mine_ref, other_ref), weight, local_sems, 0)
    halves.start()
    if not gathered:
        full_ref[group.chunk(group.me), :] = x_ref[...]
    halves.wait()

    def project(rows):
        values = (x_ref if gathered else full_ref)[rows, :].astype(WIDE)
        hat, _ = normalise(values)
        normed = (hat * vec_ref[0:1, :] + vec_ref[1:2, :]).astype(LOW)
        normed_ref[rows, :] = normed
        mixed = nn(normed, weight[:, : 3 * width]) + bias_ref[...]
        for j in range(3 * heads):
            piece = mixed[:, j * HEAD : (j + 1) * HEAD]
            if j < heads:
                piece = piece * HEAD ** (-0.5)
            heads_ref[j, rows, :] = piece.astype(LOW)

    if gathered:
        full_ref[...] = jnp.zeros_like(full_ref)

        @pl.loop(0, LENGTH // group.rows)
        def _(n):
            project(group.chunk(n))
    else:
        Gather(group, full_ref, gather_sems).each(project)
    group.emit(0, 1, 2)

    attention_out(heads_ref, o3, lse_ref, heads)
    for h in range(heads):
        o_ref[:, h * HEAD : (h + 1) * HEAD] = o3[h]
    group.emit(3, 4)

    scatter = Scatter(group, stage, land, total, scatter_sems)
    scatter.start(lambda rows: nt(o_ref[rows, :], weight[:, 3 * width :]))
    for j in range(PARTS):
        rows = slice(j * group.part, (j + 1) * group.part)
        residual = (x_ref if gathered else full_ref)[group.slab(group.me, j), :].astype(WIDE)
        hidden = residual + scatter.take(j) + vec_ref[2:3, :]
        hidden_ref[rows, :] = hidden
        hat, _ = normalise(hidden)
        second_ref[rows, :] = (hat * vec_ref[3:4, :] + vec_ref[4:5, :]).astype(LOW)
    scatter.done()


def widen_kernel(
    group, second_ref, em_ref, eo_ref, bias_ref,
    full_ref, active_ref, slope_ref,
    expand, gather_sems, local_sems,
):
    halves = Halves((em_ref, eo_ref), expand, local_sems, 0)
    halves.start()
    full_ref[group.chunk(group.me), :] = second_ref[...]
    halves.wait()

    def widen(rows):
        t = nn(full_ref[rows, :], expand[...]) + bias_ref[...]
        square = t * t
        bent = jnp.tanh(0.7978845608028654 * t * (1.0 + 0.044715 * square))
        active_ref[rows, :] = (0.5 * t * (1.0 + bent)).astype(LOW)
        slope_ref[rows, :] = (
            0.5 * (1.0 + bent)
            + (0.5 * 0.7978845608028654) * t * (1.0 - bent * bent) * (1.0 + 3 * 0.044715 * square)
        ).astype(LOW)

    Gather(group, full_ref, gather_sems).each(widen)


def outer_halves(left_ref, right_ref, keep_ref, send_ref):
    section = lax.axis_index("section")
    half = right_ref.shape[1] // 2
    for place, out in ((section, keep_ref), (1 - section, send_ref)):
        columns = pl.ds(pl.multiple_of(place * half, half), half)

        @pl.loop(0, left_ref.shape[1] // TILE)
        def _(n):
            rows = pl.ds(pl.multiple_of(n * TILE, TILE), TILE)
            out[rows, :] = tn(left_ref[:, rows], right_ref[:, columns]).astype(LOW)


def contract_kernel(last, group, *refs):
    active_ref, hidden_ref, cm_ref, co_ref, vec_ref, *refs = refs
    if last:
        g_ref, *refs = refs
    result_ref, *refs = refs
    if last:
        ck_ref, cs_ref, *refs = refs
    contract, stage, land, total, scatter_sems, local_sems = refs
    halves = Halves((cm_ref, co_ref), contract, local_sems, 0)
    halves.start()
    halves.wait()
    scatter = Scatter(group, stage, land, total, scatter_sems)
    scatter.start(lambda rows: nt(active_ref[rows, :], contract[...]))
    if last:
        group.need(5)
        outer_halves(g_ref, active_ref, ck_ref, cs_ref)
        group.emit(1, 2)
    group.need(1)
    for j in range(PARTS):
        rows = slice(j * group.part, (j + 1) * group.part)
        result = hidden_ref[rows, :] + scatter.take(j) + vec_ref[5:6, :]
        result_ref[rows, :] = result.astype(LOW)
    scatter.done()


def bend_kernel(last, group, g_ref, cm_ref, co_ref, slope_ref, extra_ref, *refs):
    before, sums_ref, *refs = refs
    if last:
        out_ref, *refs = refs
    else:
        full_ref, ck_ref, cs_ref, *refs = refs
    contract, gather_sems, local_sems, *refs = refs
    if last:
        stage4, deliver_sems = refs
        deliver = Deliver(group, stage4, out_ref, deliver_sems)
    halves = Halves((cm_ref, co_ref), contract, local_sems, 0)
    halves.start()
    sums_ref[...] = jnp.zeros_like(sums_ref)
    if last:
        deliver.start(extra_ref)
    else:
        full_ref[group.chunk(group.me), :] = g_ref[...]
    halves.wait()

    if last:
        group.need(3)

    def bend(rows):
        rows_grad = (g_ref if last else full_ref)[rows, :]
        grad = (nn(rows_grad, contract[...]) * slope_ref[rows, :].astype(WIDE)).astype(LOW)
        before[rows, :] = grad
        sums_ref[0:1, :] += jnp.sum(grad.astype(WIDE), axis=0, keepdims=True)

    if last:

        @pl.loop(0, LENGTH // group.rows)
        def _(n):
            bend(group.chunk(n))

        deliver.done()
    else:
        Gather(group, full_ref, gather_sems).each(bend, lambda: group.need(3))
        group.emit(0, 2)
        group.need(4)
        outer_halves(full_ref, extra_ref, ck_ref, cs_ref)


def narrow_kernel(
    group, before, g_ref, em_ref, eo_ref, second_ref, hidden_ref, vec_ref,
    ek_ref, es_ref, grad_ref, low_ref, sums_ref,
    expand, stage, land, total, scatter_sems, local_sems,
):
    halves = Halves((em_ref, eo_ref), expand, local_sems, 0)
    halves.start()
    sums_ref[...] = jnp.zeros_like(sums_ref)
    halves.wait()
    scatter = Scatter(group, stage, land, total, scatter_sems)
    scatter.start(lambda rows: nt(before[rows, :], expand[...]))
    group.need(4)
    outer_halves(second_ref, before, ek_ref, es_ref)
    group.emit(0, 1)
    group.need(1, 5)
    for j in range(PARTS):
        rows = slice(j * group.part, (j + 1) * group.part)
        grad = scatter.take(j)
        hat, scale = normalise(hidden_ref[rows, :])
        own = g_ref[rows, :].astype(WIDE)
        out = own + norm_backward(grad, hat, scale, vec_ref[3:4, :])
        grad_ref[rows, :] = out
        low_ref[rows, :] = out.astype(LOW)
        for n, term in enumerate((grad * hat, grad, own, out)):
            sums_ref[n : n + 1, :] += jnp.sum(term, axis=0, keepdims=True)
    scatter.done()


def scores_back_kernel(
    heads, group, low_ref, mine_ref, other_ref, heads_ref, o_ref, lse_ref,
    mixed, outer_ref,
    weight, full, go3, dots, g3, key_acc, value_acc, gather_sems, local_sems,
):
    width = o_ref.shape[1]
    halves = Halves((mine_ref, other_ref), weight, local_sems, 0)
    halves.start()
    full[group.chunk(group.me), :] = low_ref[...]
    halves.wait()
    picks = (
        lax.broadcasted_iota(jnp.int32, (8, width), 1) // HEAD
        == lax.broadcasted_iota(jnp.int32, (8, width), 0)
    ).astype(WIDE)

    def spread(rows):
        grads = nn(full[rows, :], weight[:, 3 * width :]).astype(LOW)
        for h in range(heads):
            go3[h, rows, :] = grads[:, h * HEAD : (h + 1) * HEAD]
        term = grads.astype(WIDE) * o_ref[rows, :].astype(WIDE)
        dots[:, rows] = lax.dot_general(
            picks,
            term,
            (((1,), (1,)), ((), ())),
            precision=lax.Precision.HIGHEST,
            preferred_element_type=WIDE,
        )

    Gather(group, full, gather_sems).each(spread, lambda: group.need(4))
    group.need(3, 5)
    attention_back(heads_ref, go3, lse_ref, dots, g3, key_acc, value_acc, heads)
    for j in range(3 * heads):
        mixed[:, j * HEAD : (j + 1) * HEAD] = g3[j]
    group.emit(0)

    @pl.loop(0, outer_ref.shape[0] // TILE)
    def _(n):
        rows = pl.ds(pl.multiple_of(n * TILE, TILE), TILE)
        outer_ref[rows, :] = tn(full[:, rows], o_ref[...]).astype(LOW)


def attend_back_kernel(
    last, group, mixed, outer_ref, grad_ref, x_ref, mine_ref, other_ref, normed_ref, vec_ref,
    wk_ref, ws_ref, out_ref, sums_ref, *refs,
):
    if not last:
        got_ref, *refs = refs
    weight, outer, stage, land, total, scatter_sems, local_sems, *refs = refs
    width = outer_ref.shape[1]
    section = lax.axis_index("section")
    halves = Halves((mine_ref, other_ref), weight, local_sems, 0)
    halves.start()
    sums_ref[...] = jnp.zeros_like(sums_ref)

    half = weight.shape[1] // 2

    def products():
        @pl.loop(0, weight.shape[0] // TILE)
        def _(n):
            rows = pl.ds(pl.multiple_of(n * TILE, TILE), TILE)
            outer[section, rows, :] = tn(normed_ref[:, rows], mixed[:, :half]).astype(LOW)
            outer[1 - section, rows, : 3 * width - half] = tn(
                normed_ref[:, rows], mixed[:, half:]
            ).astype(LOW)
            outer[1 - section, rows, 3 * width - half :] = outer_ref[rows, :]

    scatter = Scatter(group, stage, land, total, scatter_sems)
    if not last:
        group.need(1, 6)
        products()
        swap = push(outer.at[1], got_ref, refs[0], 0, 1 - section, "section")
        swap.start()
    halves.wait()
    scatter.start(lambda rows: nt(mixed[rows, :], weight[:, : 3 * width]))
    if last:
        group.need(1, 6)
        products()
    copies = [pltpu.make_async_copy(outer.at[0], wk_ref, local_sems.at[2])]
    if last:
        copies.append(pltpu.make_async_copy(outer.at[1], ws_ref, local_sems.at[3]))
    for copy in copies:
        copy.start()
    group.need(2, 3)
    sums_ref[2:3, : 3 * width] = jnp.sum(mixed[...].astype(WIDE), axis=0, keepdims=True)
    for j in range(PARTS):
        rows = slice(j * group.part, (j + 1) * group.part)
        grad = scatter.take(j)
        hat, scale = normalise(x_ref[rows, :].astype(WIDE))
        out = grad_ref[rows, :] + norm_backward(grad, hat, scale, vec_ref[0:1, :])
        out_ref[rows, :] = out.astype(LOW)
        for n, term in enumerate((grad * hat, grad)):
            sums_ref[n : n + 1, :] += jnp.sum(term, axis=0, keepdims=True)
    scatter.done()
    for copy in copies:
        copy.wait()
    if not last:
        swap.wait()


def finish_kernel(
    near_ref, far_ref, a0, n0, b0, a1, n1, b1, grads_ref, sums_ref,
    mine, stage4, block, land_col, land_x, land_z, send, land,
    deliver_sems, col_sems, x_sems, z_sems,
):
    section, row = lax.axis_index("section"), lax.axis_index("row")
    group = Group(near_ref.shape[0])
    length, width = far_ref.shape
    others = [lax.rem(row + d, land_z.shape[0]) for d in range(1, land_z.shape[0])]
    group.greet(True, True, others)
    deliver = Deliver(group, stage4, mine, deliver_sems)
    deliver.start(near_ref)

    block[...] = jnp.zeros_like(block)
    for layer, (attn, narrow, bend) in enumerate(((a0, n0, b0), (a1, n1, b1))):
        wide = [attn[0:1, :], attn[1:2, :], narrow[3:4, :], narrow[0:1, :], narrow[1:2, :], narrow[2:3, :]]
        for c in range(block.shape[0]):
            columns = slice(c * width, (c + 1) * width)
            for n, term in enumerate(wide):
                block[c, layer, n : n + 1, :] = term[:, columns]
            for n, term in enumerate((attn[2:3, :width], attn[2:3, 2 * width : 3 * width])):
                block[c, layer, 8 + n : 9 + n, :] = term
            for n in range(bend.shape[1] // width):
                block[c, layer, 10 + n : 11 + n, :] = bend[0:1, n * width : (n + 1) * width]
    copies = [
        push(block.at[other, :, pl.ds(0, 8)], land_col.at[n], col_sems, n, other)
        for n, other in enumerate((group.peer, group.diag, group.sib))
    ]
    for copy in copies:
        copy.start()
    for copy in copies:
        copy.wait()
    me = group.me
    block[me, :, :8] = block[me, :, :8] + (land_col[0] + (land_col[1] + land_col[2]))
    swap = push(block.at[me, 1 - section], land_x, x_sems, 0, 1 - section, "section")
    swap.start()
    swap.wait()
    land_z[row] = block[me, section] + land_x[...]
    copies = [
        push(land_z.at[row], land_z.at[row], z_sems, n, other, "row")
        for n, other in enumerate(others)
    ]
    for copy in copies:
        copy.start()

    deliver.done()

    @pl.when(section == 0)
    def _():
        send[...] = far_ref[...]

    @pl.when(section == 1)
    def _():
        send[...] = mine[...]

    swap = push(send, land, x_sems, 1, 1 - section, "section")
    swap.start()
    own = pl.ds(pl.multiple_of(section * length, length), length)
    away = pl.ds(pl.multiple_of((1 - section) * length, length), length)

    @pl.when(section == 0)
    def _():
        grads_ref[own, :] = mine[...].astype(WIDE)

    @pl.when(section == 1)
    def _():
        grads_ref[own, :] = far_ref[...].astype(WIDE)

    for copy in copies:
        copy.wait()
    result = land_z[0]
    for n in range(1, land_z.shape[0]):
        result = result + land_z[n]
    sums_ref[...] = result
    swap.wait()
    grads_ref[away, :] = land[...].astype(WIDE)


VM = pl.BlockSpec(memory_space=pltpu.VMEM)
ANY = pl.BlockSpec(memory_space=pl.ANY)
PAIRS = pltpu.SemaphoreType.DMA((2, 3 * PARTS))
LOCAL = pltpu.SemaphoreType.DMA((4,))


def shape(dims, kind=LOW):
    return jax.ShapeDtypeStruct(dims, kind)


def launch(
    body, number, rows, in_specs, ins, outs, out_specs, scratch, swaps=(), diagonal=False, across=False, late=(),
):
    n_in, n_out, n = len(ins), len(outs), len(swaps)
    held_in = [i for i in range(n_in) if in_specs[i] is VM]
    held_out = [i for i in range(n_out) if out_specs[i] is VM]

    def kernel(*refs):
        refs = list(refs)
        takes, sources = refs[:n_in], refs[n_in : n_in + n]
        gives = refs[n_in + n : n_in + n + n_out]
        lands = refs[n_in + n + n_out : n_in + 2 * n + n_out]
        rest = refs[n_in + 2 * n + n_out :]
        own, rest = rest[: len(scratch)], rest[len(scratch) :]
        in_held, rest = rest[: len(held_in)], rest[len(held_in) :]
        out_held, rest = rest[: len(held_out)], rest[len(held_out) :]
        in_sems, out_sems, swap_sems = rest
        group = Group(rows)
        for k, i in enumerate(held_in):
            group.loads[i] = pltpu.make_async_copy(takes[i], in_held[k], in_sems.at[k])
            group.loads[i].start()
            takes[i] = in_held[k]
        for k, i in enumerate(held_out):
            group.stores[i] = pltpu.make_async_copy(out_held[k], gives[i], out_sems.at[k])
            gives[i] = out_held[k]
        group.greet(n or across, diagonal)
        other = 1 - lax.axis_index("section")
        copies = [
            push(source, land, swap_sems, i, other, "section")
            for i, (source, land) in enumerate(zip(sources, lands))
        ]
        for copy in copies:
            copy.start()
        group.need(*[i for i in held_in if i not in late])
        body(group, *takes, *gives, *own)
        group.emit(*[i for i in held_out if i not in group.begun])
        for copy in copies:
            copy.wait()
        for i in held_out:
            group.stores[i].wait()

    results = pl.pallas_call(
        kernel,
        out_shape=(*outs, *[shape(s.shape, s.dtype) for s in swaps]),
        in_specs=[ANY] * (n_in + n),
        out_specs=(ANY,) * (n_out + n),
        scratch_shapes=[
            *scratch,
            *[pltpu.VMEM(ins[i].shape, ins[i].dtype) for i in held_in],
            *[pltpu.VMEM(outs[i].shape, outs[i].dtype) for i in held_out],
            pltpu.SemaphoreType.DMA((len(held_in),)),
            pltpu.SemaphoreType.DMA((len(held_out),)),
            pltpu.SemaphoreType.DMA((2, max(n, 1))),
        ],
        compiler_params=pltpu.CompilerParams(
            collective_id=number, has_side_effects=True, vmem_limit_bytes=GRANT
        ),
        cost_estimate=pl.CostEstimate(flops=int(3e10), bytes_accessed=30 * MEBI, transcendentals=0),
    )(*ins, *swaps)
    return results[:n_out], results[n_out:]


def start_call(number, tokens, cotangent, small, raw, columns):
    width = tokens.shape[1]
    size = width * columns
    kinds = small.shape[0]
    outs = (shape((LENGTH, size)), shape((LENGTH, size)), shape((2, columns, kinds, width)), shape(raw.shape))
    blocks = pltpu.VMEM((columns, LENGTH, width), LOW)
    vectors = pltpu.VMEM((columns, kinds, width), LOW)
    return pl.pallas_call(
        start_kernel,
        out_shape=outs,
        in_specs=[ANY] * 4,
        out_specs=(VM, VM, VM, ANY),
        scratch_shapes=[
            blocks, blocks, vectors, vectors, PAIRS, PAIRS,
            pltpu.SemaphoreType.DMA((2, 3 * PARTS + 2)), LOCAL,
        ],
        compiler_params=pltpu.CompilerParams(
            collective_id=number, has_side_effects=True, vmem_limit_bytes=GRANT
        ),
        cost_estimate=pl.CostEstimate(flops=int(3e10), bytes_accessed=30 * MEBI, transcendentals=0),
    )(tokens, cotangent, small, raw)


def attend_call(number, gathered, x, pair, vec, bias, rows, width, swaps):
    size = vec.shape[1]
    heads = width // HEAD
    outs = (
        shape((LENGTH, size) if not gathered else (16, 128)),
        shape((LENGTH, size)),
        shape((3 * heads, LENGTH, HEAD)),
        shape((LENGTH, width)),
        shape((8, LENGTH), WIDE),
        shape((rows, size), WIDE),
        shape((rows, size)),
    )
    scratch = [
        pltpu.VMEM((size, 4 * width), LOW),
        pltpu.VMEM((heads, LENGTH, HEAD), LOW),
        *scatter_scratch(rows, size), PAIRS, LOCAL,
    ]
    return launch(
        functools.partial(attend_kernel, gathered, heads),
        number, rows, [VM, ANY, ANY, VM, VM], (x, *pair, vec, bias), outs, (VM,) * 7, scratch, swaps,
    )


def widen_call(number, second, pair, bias, swaps):
    rows, size = second.shape
    wide = bias.shape[1]
    outs = (shape((LENGTH, size)), shape((LENGTH, wide)), shape((LENGTH, wide)))
    scratch = [pltpu.VMEM((size, wide), LOW), PAIRS, LOCAL]
    return launch(
        widen_kernel, number, rows, [VM, ANY, ANY, VM], (second, *pair, bias), outs, (VM,) * 3, scratch, swaps
    )


def contract_call(number, active, hidden, pair, vec, grad, swaps):
    rows, size = hidden.shape
    wide = active.shape[1]
    last = grad is not None
    outs = [shape((rows, size))]
    scratch = [pltpu.VMEM((size, wide), LOW), *scatter_scratch(rows, size), LOCAL]
    in_specs, ins = [VM, VM, ANY, ANY, VM], [active, hidden, *pair, vec]
    if last:
        in_specs, ins = in_specs + [VM], ins + [grad]
        outs += [shape((size, wide // 2))] * 2
    return launch(
        functools.partial(contract_kernel, last),
        number, rows, in_specs, ins, outs, (VM,) * len(outs), scratch, swaps, late=(1, 5),
    )


def bend_call(number, last, grad, pair, slope, extra, size, rows, swaps):
    wide = slope.shape[1]
    columns = LENGTH // rows
    outs = [shape((LENGTH, wide)), shape((8, wide), WIDE)]
    scratch = [pltpu.VMEM((size, wide), LOW), PAIRS, LOCAL]
    if last:
        outs += [shape((LENGTH, size // columns))]
        scratch += [pltpu.VMEM((columns, rows, size // columns), LOW), pltpu.SemaphoreType.DMA((2, 3))]
    else:
        outs += [shape((LENGTH, size)), *[shape((size, wide // 2))] * 2]
    return launch(
        functools.partial(bend_kernel, last),
        number, rows, [VM, ANY, ANY, VM, VM], (grad, *pair, slope, extra),
        outs, (VM,) * len(outs), scratch, swaps, last, late=(3,) if last else (3, 4),
    )


def narrow_call(number, before, grad_own, pair, second, hidden, vec, swaps):
    rows, size = hidden.shape
    wide = before.shape[1]
    outs = (
        *[shape((size, wide // 2))] * 2,
        shape((rows, size), WIDE),
        shape((rows, size)),
        shape((8, size), WIDE),
    )
    scratch = [pltpu.VMEM((size, wide), LOW), *scatter_scratch(rows, size), LOCAL]
    return launch(
        narrow_kernel,
        number, rows, [VM, VM, ANY, ANY, VM, VM, VM], (before, grad_own, *pair, second, hidden, vec),
        outs, (VM,) * 5, scratch, swaps, late=(1, 4, 5),
    )


def scores_back_call(number, low, pair, heads_all, o, lse, swaps):
    rows, size = low.shape
    width = o.shape[1]
    heads = width // HEAD
    outs = (shape((LENGTH, 3 * width)), shape((size, width)))
    scratch = [
        pltpu.VMEM((size, 4 * width), LOW),
        pltpu.VMEM((LENGTH, size), LOW),
        pltpu.VMEM((heads, LENGTH, HEAD), LOW),
        pltpu.VMEM((8, LENGTH), WIDE),
        pltpu.VMEM((3 * heads, LENGTH, HEAD), LOW),
        pltpu.VMEM((LENGTH, HEAD), WIDE),
        pltpu.VMEM((LENGTH, HEAD), WIDE),
        PAIRS, LOCAL,
    ]
    return launch(
        functools.partial(scores_back_kernel, heads),
        number, rows, [VM, ANY, ANY, VM, VM, VM], (low, *pair, heads_all, o, lse),
        outs, (VM,) * 2, scratch, swaps, late=(3, 4, 5),
    )


def attend_back_call(number, last, mixed, outer, grad, x_own, pair, normed, vec, swaps):
    rows, size = grad.shape
    width = outer.shape[1]
    half = 2 * width
    outs = [shape((size, half)), shape((size, half)), shape((rows, size)), shape((8, size), WIDE)]
    out_specs = [ANY, ANY, VM, VM]
    scratch = [
        pltpu.VMEM((size, 4 * width), LOW),
        pltpu.VMEM((2, size, half), LOW),
        *scatter_scratch(rows, size), LOCAL,
    ]
    if not last:
        outs[1] = shape((16, 128))
        outs, out_specs = outs + [shape((size, half))], out_specs + [ANY]
        scratch += [pltpu.SemaphoreType.DMA((2, 1))]
    return launch(
        functools.partial(attend_back_kernel, last),
        number, rows, [VM, VM, VM, VM, ANY, ANY, VM, VM],
        (mixed, outer, grad, x_own, *pair, normed, vec), outs, out_specs, scratch, swaps, False, True, late=(1, 2, 3, 6),
    )


def finish_call(number, near, far, sums, row_count):
    rows, size = near.shape
    length, width = far.shape
    columns = length // rows
    outs = (shape((2 * length, width), WIDE), shape((16, width), WIDE))
    scratch = [
        pltpu.VMEM((length, width), LOW),
        pltpu.VMEM((columns, rows, width), LOW),
        pltpu.VMEM((columns, 2, 16, width), WIDE),
        pltpu.VMEM((3, 2, 8, width), WIDE),
        pltpu.VMEM((16, width), WIDE),
        pltpu.VMEM((row_count, 16, width), WIDE),
        pltpu.VMEM((length, width), LOW),
        pltpu.VMEM((length, width), LOW),
        pltpu.SemaphoreType.DMA((2, 3)),
        pltpu.SemaphoreType.DMA((2, 3)),
        pltpu.SemaphoreType.DMA((2, 2)),
        pltpu.SemaphoreType.DMA((2, row_count)),
    ]
    return pl.pallas_call(
        finish_kernel,
        out_shape=outs,
        in_specs=[VM] * 8,
        out_specs=(VM, VM),
        scratch_shapes=scratch,
        compiler_params=pltpu.CompilerParams(
            collective_id=number, has_side_effects=True, vmem_limit_bytes=GRANT
        ),
        cost_estimate=pl.CostEstimate(flops=int(3e10), bytes_accessed=30 * MEBI, transcendentals=0),
    )(near, far, *sums)


def swap_sections(value):
    return lax.ppermute(value, "section", [(0, 1), (1, 0)])


def on_device(
    tokens,
    cotangent,
    first_gain,
    first_shift,
    attend_weight,
    attend_bias,
    output_weight,
    output_bias,
    second_gain,
    second_shift,
    expand_weight,
    expand_bias,
    contract_weight,
    contract_bias,
):
    section = lax.axis_index("section")
    column = lax.axis_index("col")
    first_section = section == 0
    columns = lax.axis_size("col")
    width = tokens.shape[1]
    size = width * columns
    rows = LENGTH // columns

    def pick(early, later):
        return jnp.where(first_section, early, later)

    block_rows = attend_weight.shape[1]
    units = (
        jnp.concatenate(
            [attend_weight[0].reshape(block_rows, 3 * width), output_weight[0].T], axis=1
        ),
        expand_weight[0],
        contract_weight[0].T,
    )
    kept_blocks, sent_blocks = [], []
    for unit in units:
        half = unit.shape[1] // 2
        low, high = unit[:, :half], unit[:, half:]
        kept_blocks.append(pick(low, high))
        sent_blocks.append(pick(high, low))

    small = jnp.concatenate(
        [
            first_gain,
            first_shift,
            output_bias,
            second_gain,
            second_shift,
            contract_bias,
            attend_bias[0],
            expand_bias[0].reshape(-1, width),
        ],
        0,
    )
    filled = small.shape[0]
    small = jnp.pad(small, ((0, -filled % 16), (0, 0)))
    got_attend = swap_sections(sent_blocks[0])
    raw = jnp.stack(sent_blocks[1:])
    got_attend, raw = lax.optimization_barrier((got_attend, raw))
    x0_full, gy_full, vectors, got_blocks = start_call(1, tokens, cotangent, small, raw, columns)
    mats = [[], []]
    for own, got in zip(kept_blocks, (got_attend, got_blocks[0], got_blocks[1])):
        for layer, block in enumerate((pick(own, got), pick(got, own))):
            mats[layer].append(lax.all_gather(block, "row", axis=0, tiled=True))
    vectors = vectors.astype(WIDE)
    wide_vectors = jnp.swapaxes(vectors[:, :, :6], 1, 2).reshape(2, 6, size)
    wide_vectors = jnp.pad(wide_vectors, ((0, 0), (0, 2), (0, 0)))
    own_vectors = lax.dynamic_index_in_dim(vectors, column, 1, keepdims=False)
    attend_biases = jnp.stack(
        [own_vectors[:, 6], jnp.zeros_like(own_vectors[:, 6]), own_vectors[:, 7]], 1
    ).reshape(2, 1, 3 * width)
    expand_biases = own_vectors[:, 8:filled].reshape(2, 1, -1)

    def own_rows(full):
        return lax.dynamic_slice_in_dim(full, column * rows, rows, 0)

    def own_features(full):
        return lax.dynamic_slice_in_dim(full, column * width, width, 1)

    attn = (mats[0][0], swap_sections(mats[0][0]))
    x = x0_full
    kept, pairs = [], []
    owns = [own_rows(x0_full)]
    for layer in range(2):
        last = layer == 1
        vec = wide_vectors[layer]
        (full, normed, heads, o, lse, hidden, second_own), (other,) = attend_call(
            2 + 3 * layer, not last, x, attn, vec, attend_biases[layer], rows, width, [mats[layer][1]]
        )
        expand = (mats[layer][1], other)
        (second, active, slope), (other,) = widen_call(
            3 + 3 * layer, second_own, expand, expand_biases[layer], [mats[layer][2]]
        )
        contract = (mats[layer][2], other)
        outs, others = contract_call(
            4 + 3 * layer, active, hidden, contract, vec,
            gy_full if last else None, [] if last else [mats[1][0]],
        )
        pairs.append((attn, expand, contract))
        kept.append((normed, heads, o, lse, hidden, second, active, slope))
        x = outs[0]
        owns.append(x)
        if last:
            ck1, cs1 = outs[1:]
        else:
            attn = (mats[1][0], others[0])
    y0 = own_features(full)

    def add(keep, got, then):
        total = (keep.astype(WIDE) + got.astype(WIDE)).astype(LOW)
        return lax.optimization_barrier((total, then))

    def scatter(total):
        return lax.psum_scatter(total, "row", scatter_dimension=0, tiled=True)

    def tie(value, then):
        return lax.optimization_barrier((value, then))

    attn, expand, contract = pairs[1]
    normed, heads, o, lse, hidden, second, active, slope = kept[1]
    (before, bend_sums1, y1), _ = bend_call(8, True, gy_full, contract, slope, owns[2], size, rows, [])
    layer_low, layer_high = pick(y0, y1), pick(y1, y0)
    (ek1, es1, grad_hidden, low, narrow_sums1), (ct1,) = narrow_call(
        9, before, own_rows(gy_full), expand, second, hidden, wide_vectors[1], [cs1]
    )
    total_c1, low = add(ck1, ct1, low)
    (mixed, outer), (et1,) = scores_back_call(10, low, attn, heads, o, lse, [es1])
    total_e1, mixed = add(ek1, et1, mixed)
    part_c1, mixed = tie(scatter(total_c1), mixed)
    (wk1, ws1, gx1_own, attend_sums1), (layer_got,) = attend_back_call(
        11, True, mixed, outer, grad_hidden, owns[1], attn, normed, wide_vectors[1], [layer_high]
    )
    layer_outputs = jnp.concatenate([pick(layer_low, layer_got), pick(layer_got, layer_low)], 0)

    attn, expand, contract = pairs[0]
    normed, heads, o, lse, hidden, second, active, slope = kept[0]
    (before, bend_sums0, gx1_full, ck0, cs0), (wt1,) = bend_call(
        12, False, gx1_own, contract, slope, active, size, rows, [ws1]
    )
    total_w1, before = add(wk1, wt1, before)
    part_e1, before = tie(scatter(total_e1), before)
    (ek0, es0, grad_hidden, low, narrow_sums0), (ct0,) = narrow_call(
        13, before, gx1_own, expand, second, hidden, wide_vectors[0], [cs0]
    )
    total_c0, low = add(ck0, ct0, low)
    part_w1, low = tie(scatter(total_w1), low)
    (mixed, outer), (et0,) = scores_back_call(14, low, attn, heads, o, lse, [es0])
    total_e0, mixed = add(ek0, et0, mixed)
    part_c0, mixed = tie(scatter(total_c0), mixed)
    (wk0, _, gx0_own, attend_sums0, wt0), _ = attend_back_call(
        15, False, mixed, outer, grad_hidden, owns[0], attn, normed, wide_vectors[0], []
    )
    total_w0, gx0_own = add(wk0, wt0, gx0_own)
    part_e0, gx0_own = tie(scatter(total_e0), gx0_own)
    input_grads, small_grads = finish_call(
        16,
        gx0_own,
        own_features(gx1_full),
        (attend_sums0, narrow_sums0, bend_sums0, attend_sums1, narrow_sums1, bend_sums1),
        lax.axis_size("row"),
    )

    late = [part_w1, part_e1, part_c1]
    part_w0, small_grads = tie(scatter(total_w0), small_grads)
    early = [part_w0, part_e0, part_c0]
    units = []
    for second_layer, first_layer in zip(late, early):
        stays = pick(first_layer, second_layer)
        got = swap_sections(pick(second_layer, first_layer))
        units.append(jnp.concatenate([pick(stays, got), pick(got, stays)], 1).astype(WIDE))
    attn_part, expand_part, contract_part = units

    return (
        layer_outputs[None],
        input_grads[None],
        small_grads[0:1],
        small_grads[1:2],
        attn_part[:, : 3 * width].reshape(block_rows, 3, width)[None],
        small_grads[8:10][None],
        attn_part[:, 3 * width :].T[None],
        small_grads[2:3],
        small_grads[3:4],
        small_grads[4:5],
        expand_part[None],
        small_grads[10 : 10 + expand_bias.shape[1] // width].reshape(1, -1),
        contract_part.T[None],
        small_grads[5:6],
    )


def solution(mesh):
    return jax.shard_map(
        on_device,
        mesh=mesh,
        in_specs=(
            P("row", "col"),
            P("row", "col"),
            P("section", "col"),
            P("section", "col"),
            P("section", "row", None, "col"),
            P("section", None, "col"),
            P("section", "col", "row"),
            P("section", "col"),
            P("section", "col"),
            P("section", "col"),
            P("section", "row", "col"),
            P("section", "col"),
            P("section", "col", "row"),
            P("section", "col"),
        ),
        out_specs=(
            P("section", "row", "col"),
            P("section", "row", "col"),
            P("section", "col"),
            P("section", "col"),
            P("section", "row", None, "col"),
            P("section", None, "col"),
            P("section", "col", "row"),
            P("section", "col"),
            P("section", "col"),
            P("section", "col"),
            P("section", "row", "col"),
            P("section", "col"),
            P("section", "col", "row"),
            P("section", "col"),
        ),
        check_vma=False,
    )
```

```python
import functools

import jax
import jax.numpy as jnp
from jax import lax
from jax.experimental import pallas as pl
from jax.experimental.pallas import tpu as pltpu
from jax.sharding import PartitionSpec as P

HEAD = 64
LENGTH = 1024
EPS = 1e-05
LOW = jnp.bfloat16
WIDE = jnp.float32
MESH = pl.DeviceIdType.MESH
PARTS = 2
TILE = 256
MEBI = 1024 * 1024
GRANT = 58 * MEBI


def nn(left, right):
    return lax.dot_general(left, right, (((1,), (0,)), ((), ())), preferred_element_type=WIDE)


def nt(left, right):
    return lax.dot_general(left, right, (((1,), (1,)), ((), ())), preferred_element_type=WIDE)


def tn(left, right):
    return lax.dot_general(left, right, (((0,), (0,)), ((), ())), preferred_element_type=WIDE)


def normalise(values):
    center = jnp.mean(values, axis=1, keepdims=True)
    centred = values - center
    scale = lax.rsqrt(jnp.mean(centred * centred, axis=1, keepdims=True) + EPS)
    return centred * scale, scale


def norm_backward(grad, hat, scale, gain):
    scaled = grad * gain
    mean_one = jnp.mean(scaled, axis=1, keepdims=True)
    mean_two = jnp.mean(scaled * hat, axis=1, keepdims=True)
    return scale * (scaled - mean_one - hat * mean_two)


class Group:
    def __init__(self, rows):
        self.me = lax.axis_index("col")
        chip, core = self.me // 2, self.me % 2
        self.sib = chip * 2 + 1 - core
        self.peer = (1 - chip) * 2 + core
        self.diag = (1 - chip) * 2 + 1 - core
        self.rows = rows
        self.part = rows // PARTS
        self.loads, self.stores, self.begun = {}, {}, set()

    def need(self, *places):
        for place in places:
            self.loads[place].wait()

    def emit(self, *places):
        for place in places:
            self.stores[place].start()
            self.begun.add(place)

    def greet(self, swaps, diagonal, rows=()):
        barrier = pltpu.get_barrier_semaphore()
        others = [{"col": self.sib}, {"col": self.peer}]
        if diagonal:
            others.append({"col": self.diag})
        if swaps:
            others.append({"section": 1 - lax.axis_index("section")})
        others += [{"row": row} for row in rows]
        for other in others:
            pl.semaphore_signal(barrier, inc=1, device_id=other, device_id_type=MESH)
        pl.semaphore_wait(barrier, len(others))

    def slab(self, owner, j):
        return pl.ds(pl.multiple_of(owner * self.rows + j * self.part, self.part), self.part)

    def chunk(self, owner):
        return pl.ds(pl.multiple_of(owner * self.rows, self.rows), self.rows)


def push(src, dst, sems, slot, target, axis="col"):
    return pltpu.make_async_remote_copy(
        src_ref=src,
        dst_ref=dst,
        send_sem=sems.at[0, slot],
        recv_sem=sems.at[1, slot],
        device_id={axis: target},
        device_id_type=MESH,
    )


class Gather:
    def __init__(self, group, full, sems, blocks=False):
        self.group, self.full, self.sems, self.blocks = group, full, sems, blocks

    def piece(self, owner, j):
        if not self.blocks:
            return self.full.at[self.group.slab(owner, j)]
        part = self.full.shape[1] // PARTS
        return self.full.at[owner, pl.ds(j * part, part)]

    def start(self):
        g = self.group
        self.over, self.near, self.relayed = [], [], []
        for j in range(PARTS):
            piece = self.piece(g.me, j)
            self.over.append(push(piece, piece, self.sems, j, g.peer))
            self.over[-1].start()
        for j in range(PARTS):
            piece = self.piece(g.me, j)
            self.near.append(push(piece, piece, self.sems, PARTS + j, g.sib))
            self.near[-1].start()

    def sibling(self):
        for copy in self.near:
            copy.wait_recv()

    def relay(self):
        g = self.group
        for j in range(PARTS):
            self.over[j].wait_recv()
            piece = self.piece(g.peer, j)
            self.relayed.append(push(piece, piece, self.sems, 2 * PARTS + j, g.sib))
            self.relayed[-1].start()

    def diagonal(self):
        for copy in self.relayed:
            copy.wait_recv()

    def done(self):
        for copy in self.over + self.near + self.relayed:
            copy.wait_send()

    def each(self, body, first=None):
        g = self.group
        self.start()
        if first is not None:
            first()
        body(g.chunk(g.me))
        self.sibling()
        body(g.chunk(g.sib))
        self.relay()
        body(g.chunk(g.peer))
        self.diagonal()
        body(g.chunk(g.diag))
        self.done()


class Scatter:
    def __init__(self, group, stage, land, total, sems):
        self.group, self.stage, self.land, self.total, self.sems = group, stage, land, total, sems

    def start(self, part):
        g, stage, land = self.group, self.stage, self.land
        self.first, self.over, self.near = [], [], []
        def split(owner):
            whole = part(g.chunk(owner))
            return [whole[j * g.part : (j + 1) * g.part] for j in range(PARTS)]

        for j, mine in enumerate(split(g.diag)):
            stage[0, j] = mine.astype(LOW)
            self.first.append(push(stage.at[0, j], land.at[0, j], self.sems, j, g.sib))
            self.first[-1].start()
        for j, mine in enumerate(split(g.peer)):
            self.first[j].wait_recv()
            stage[1, j] = (mine + land[0, j].astype(WIDE)).astype(LOW)
            self.over.append(push(stage.at[1, j], land.at[1, j], self.sems, PARTS + j, g.peer))
            self.over[-1].start()
        for j, mine in enumerate(split(g.sib)):
            stage[2, j] = mine.astype(LOW)
            self.near.append(push(stage.at[2, j], land.at[2, j], self.sems, 2 * PARTS + j, g.sib))
            self.near[-1].start()
        for j, mine in enumerate(split(g.me)):
            self.total[j] = mine

    def take(self, j):
        self.near[j].wait_recv()
        self.over[j].wait_recv()
        land = self.land
        return self.total[j] + (land[1, j].astype(WIDE) + land[2, j].astype(WIDE))

    def done(self):
        for copy in self.first + self.over + self.near:
            copy.wait_send()


class Deliver:
    def __init__(self, group, stage, out, sems):
        self.group, self.stage, self.out, self.sems = group, stage, out, sems

    def start(self, rows_ref):
        g, width = self.group, self.out.shape[1]
        for c in range(self.stage.shape[0]):
            self.stage[c] = rows_ref[:, c * width : (c + 1) * width]
        place = self.out.at[g.chunk(g.me)]
        self.copies = [
            push(self.stage.at[other], place, self.sems, n, other)
            for n, other in enumerate((g.peer, g.diag, g.sib))
        ]
        for copy in self.copies:
            copy.start()
        self.out[g.chunk(g.me), :] = self.stage[g.me]

    def done(self):
        for copy in self.copies:
            copy.wait()


def scatter_scratch(rows, width):
    part = rows // PARTS
    return [
        pltpu.VMEM((3, PARTS, part, width), LOW),
        pltpu.VMEM((3, PARTS, part, width), LOW),
        pltpu.VMEM((PARTS, part, width), WIDE),
        pltpu.SemaphoreType.DMA((2, 3 * PARTS)),
    ]


class Halves:
    def __init__(self, pair, whole, sems, slot):
        section = lax.axis_index("section")
        half = whole.shape[1] // 2
        self.copies = []
        for n, place in enumerate((section, 1 - section)):
            columns = pl.ds(pl.multiple_of(place * half, half), half)
            self.copies.append(
                pltpu.make_async_copy(pair[n], whole.at[:, columns], sems.at[slot + n])
            )

    def start(self):
        for copy in self.copies:
            copy.start()

    def wait(self):
        for copy in self.copies:
            copy.wait()


def attention_out(heads_ref, o3, lse_ref, heads):
    length = heads_ref.shape[1]
    size = min(TILE, length)

    @pl.loop(0, heads)
    def _(h):
        for i in range(length // size):
            rows = slice(i * size, (i + 1) * size)
            finish = (i + 1) * size
            queries = heads_ref[h, rows, :]
            scores = nt(heads_ref[heads + h, :finish, :], queries)
            keep = lax.broadcasted_iota(jnp.int32, (size, size), 0) <= lax.broadcasted_iota(
                jnp.int32, (size, size), 1
            )
            last = jnp.where(keep, scores[finish - size :], -1000000000.0)
            scores = last if i == 0 else jnp.concatenate([scores[: finish - size], last], 0)
            highest = jnp.max(scores, axis=0, keepdims=True)
            powers = jnp.exp(scores - highest)
            summed = jnp.sum(powers, axis=0, keepdims=True)
            mixed = tn(heads_ref[2 * heads + h, :finish, :], powers.astype(LOW))
            o3[h, rows, :] = (mixed / summed).T.astype(LOW)
            lse_ref[pl.ds(h, 1), rows] = highest + jnp.log(summed)


def attention_back(heads_ref, go3, lse_ref, dots_ref, g3, key_acc, value_acc, heads):
    length = heads_ref.shape[1]
    size = min(TILE, length)

    @pl.loop(0, heads)
    def _(h):
        for i in reversed(range(length // size)):
            rows = slice(i * size, (i + 1) * size)
            finish = (i + 1) * size
            queries = heads_ref[h, rows, :]
            keys = heads_ref[heads + h, :finish, :]
            grads = go3[h, rows, :]
            scores = nt(keys, queries) - lse_ref[pl.ds(h, 1), rows]
            keep = lax.broadcasted_iota(jnp.int32, (size, size), 0) <= lax.broadcasted_iota(
                jnp.int32, (size, size), 1
            )
            last = jnp.where(keep, scores[finish - size :], -1000000000.0)
            scores = last if i == 0 else jnp.concatenate([scores[: finish - size], last], 0)
            probs = jnp.exp(scores)
            grad_probs = nt(heads_ref[2 * heads + h, :finish, :], grads)
            grad_scores = (probs * (grad_probs - dots_ref[pl.ds(h, 1), rows])).astype(LOW)
            g3[h, rows, :] = (tn(grad_scores, keys) * HEAD ** (-0.5)).astype(LOW)
            key_part = nn(grad_scores, queries)
            value_part = nn(probs.astype(LOW), grads)
            if finish == length:
                key_acc[...] = key_part
                value_acc[...] = value_part
            else:
                key_acc[:finish, :] += key_part
                value_acc[:finish, :] += value_part
        g3[heads + h] = key_acc[...].astype(LOW)
        g3[2 * heads + h] = value_acc[...].astype(LOW)


def start_kernel(
    tokens_ref, cotangent_ref, small_ref, raw_ref, x_ref, g_ref, vectors_ref, got_ref,
    x4, g4, s4, other4, x_sems, g_sems, s_sems, local_sems,
):
    section = lax.axis_index("section")
    group = Group(x_ref.shape[0] // 4)
    length = x_ref.shape[0]
    loads = []
    rows = pl.ds(pl.multiple_of(section * length, length), length)
    for n, (source, into) in enumerate(((tokens_ref.at[rows], x4), (cotangent_ref.at[rows], g4), (small_ref, s4))):
        loads.append(pltpu.make_async_copy(source, into.at[group.me], local_sems.at[n]))
        loads[-1].start()
    group.greet(True, False)
    blocks = push(raw_ref, got_ref, s_sems, 3 * PARTS + 1, 1 - section, "section")
    blocks.start()
    gathers = [Gather(group, x4, x_sems, True), Gather(group, s4, s_sems, True), Gather(group, g4, g_sems, True)]
    for gather, load in zip(gathers, (loads[0], loads[2], loads[1])):
        load.wait()
        gather.start()
    for gather in gathers:
        gather.sibling()
        gather.relay()
        gather.diagonal()
    swap = push(s4, other4, s_sems, 3 * PARTS, 1 - section, "section")
    swap.start()
    width = x4.shape[2]
    for c in range(x4.shape[0]):
        x_ref[:, c * width : (c + 1) * width] = x4[c]
        g_ref[:, c * width : (c + 1) * width] = g4[c]
    swap.wait()
    blocks.wait()
    vectors_ref[section] = s4[...]
    vectors_ref[1 - section] = other4[...]
    for gather in gathers:
        gather.done()


def attend_kernel(
    gathered, heads, group, x_ref, mine_ref, other_ref, vec_ref, bias_ref,
    full_ref, normed_ref, heads_ref, o_ref, lse_ref, hidden_ref, second_ref,
    weight, o3, stage, land, total, scatter_sems, gather_sems, local_sems,
):
    width = o_ref.shape[1]
    halves = Halves((mine_ref, other_ref), weight, local_sems, 0)
    halves.start()
    if not gathered:
        full_ref[group.chunk(group.me), :] = x_ref[...]
    halves.wait()

    def project(rows):
        values = (x_ref if gathered else full_ref)[rows, :].astype(WIDE)
        hat, _ = normalise(values)
        normed = (hat * vec_ref[0:1, :] + vec_ref[1:2, :]).astype(LOW)
        normed_ref[rows, :] = normed
        mixed = nn(normed, weight[:, : 3 * width]) + bias_ref[...]
        for j in range(3 * heads):
            piece = mixed[:, j * HEAD : (j + 1) * HEAD]
            if j < heads:
                piece = piece * HEAD ** (-0.5)
            heads_ref[j, rows, :] = piece.astype(LOW)

    if gathered:
        full_ref[...] = jnp.zeros_like(full_ref)

        @pl.loop(0, LENGTH // group.rows)
        def _(n):
            project(group.chunk(n))
    else:
        Gather(group, full_ref, gather_sems).each(project)
    group.emit(0, 1, 2)

    attention_out(heads_ref, o3, lse_ref, heads)
    for h in range(heads):
        o_ref[:, h * HEAD : (h + 1) * HEAD] = o3[h]
    group.emit(3, 4)

    scatter = Scatter(group, stage, land, total, scatter_sems)
    scatter.start(lambda rows: nt(o_ref[rows, :], weight[:, 3 * width :]))
    for j in range(PARTS):
        rows = slice(j * group.part, (j + 1) * group.part)
        residual = (x_ref if gathered else full_ref)[group.slab(group.me, j), :].astype(WIDE)
        hidden = residual + scatter.take(j) + vec_ref[2:3, :]
        hidden_ref[rows, :] = hidden
        hat, _ = normalise(hidden)
        second_ref[rows, :] = (hat * vec_ref[3:4, :] + vec_ref[4:5, :]).astype(LOW)
    scatter.done()


def outer_whole(left_ref, right_ref, out_ref):
    @pl.loop(0, left_ref.shape[1] // TILE)
    def _(n):
        rows = pl.ds(pl.multiple_of(n * TILE, TILE), TILE)
        out_ref[rows, :] = tn(left_ref[:, rows], right_ref[...]).astype(LOW)


def widen_kernel(last, group, second_ref, em_ref, eo_ref, bias_ref, *refs):
    if last:
        g_ref, *refs = refs
    full_ref, active_ref, slope_ref, *refs = refs
    if last:
        c_ref, *refs = refs
    expand, gather_sems, local_sems = refs
    halves = Halves((em_ref, eo_ref), expand, local_sems, 0)
    halves.start()
    full_ref[group.chunk(group.me), :] = second_ref[...]
    halves.wait()

    def widen(rows):
        t = nn(full_ref[rows, :], expand[...]) + bias_ref[...]
        square = t * t
        bent = jnp.tanh(0.7978845608028654 * t * (1.0 + 0.044715 * square))
        active_ref[rows, :] = (0.5 * t * (1.0 + bent)).astype(LOW)
        slope_ref[rows, :] = (
            0.5 * (1.0 + bent)
            + (0.5 * 0.7978845608028654) * t * (1.0 - bent * bent) * (1.0 + 3 * 0.044715 * square)
        ).astype(LOW)

    Gather(group, full_ref, gather_sems).each(widen)
    if last:
        group.emit(0, 1, 2)
        group.need(4)
        outer_whole(g_ref, active_ref, c_ref)


def outer_halves(left_ref, right_ref, keep_ref, send_ref):
    section = lax.axis_index("section")
    half = right_ref.shape[1] // 2
    for place, out in ((section, keep_ref), (1 - section, send_ref)):
        columns = pl.ds(pl.multiple_of(place * half, half), half)

        @pl.loop(0, left_ref.shape[1] // TILE)
        def _(n):
            rows = pl.ds(pl.multiple_of(n * TILE, TILE), TILE)
            out[rows, :] = tn(left_ref[:, rows], right_ref[:, columns]).astype(LOW)


def contract_kernel(
    group, active_ref, hidden_ref, cm_ref, co_ref, vec_ref, result_ref,
    contract, stage, land, total, scatter_sems, local_sems,
):
    halves = Halves((cm_ref, co_ref), contract, local_sems, 0)
    halves.start()
    halves.wait()
    scatter = Scatter(group, stage, land, total, scatter_sems)
    scatter.start(lambda rows: nt(active_ref[rows, :], contract[...]))
    group.need(1)
    for j in range(PARTS):
        rows = slice(j * group.part, (j + 1) * group.part)
        result = hidden_ref[rows, :] + scatter.take(j) + vec_ref[5:6, :]
        result_ref[rows, :] = result.astype(LOW)
    scatter.done()


def bend_kernel(last, group, g_ref, cm_ref, co_ref, slope_ref, extra_ref, *refs):
    before, sums_ref, *refs = refs
    if last:
        out_ref, *refs = refs
    else:
        full_ref, ck_ref, cs_ref, *refs = refs
    contract, gather_sems, local_sems, *refs = refs
    if last:
        stage4, deliver_sems = refs
        deliver = Deliver(group, stage4, out_ref, deliver_sems)
    halves = Halves((cm_ref, co_ref), contract, local_sems, 0)
    halves.start()
    sums_ref[...] = jnp.zeros_like(sums_ref)
    if last:
        deliver.start(extra_ref)
    else:
        full_ref[group.chunk(group.me), :] = g_ref[...]
    halves.wait()

    if last:
        group.need(3)

    def bend(rows):
        rows_grad = (g_ref if last else full_ref)[rows, :]
        grad = (nn(rows_grad, contract[...]) * slope_ref[rows, :].astype(WIDE)).astype(LOW)
        before[rows, :] = grad
        sums_ref[0:1, :] += jnp.sum(grad.astype(WIDE), axis=0, keepdims=True)

    if last:

        @pl.loop(0, LENGTH // group.rows)
        def _(n):
            bend(group.chunk(n))

        deliver.done()
    else:
        Gather(group, full_ref, gather_sems).each(bend, lambda: group.need(3))
        group.emit(0, 2)
        group.need(4)
        outer_halves(full_ref, extra_ref, ck_ref, cs_ref)


def narrow_kernel(
    last, group, before, g_ref, em_ref, eo_ref, second_ref, hidden_ref, vec_ref,
    grad_ref, low_ref, sums_ref, ek_ref, es_ref,
    expand, stage, land, total, scatter_sems, local_sems,
):
    halves = Halves((em_ref, eo_ref), expand, local_sems, 0)
    halves.start()
    sums_ref[...] = jnp.zeros_like(sums_ref)
    halves.wait()
    scatter = Scatter(group, stage, land, total, scatter_sems)
    scatter.start(lambda rows: nt(before[rows, :], expand[...]))
    group.need(4)
    if last:
        outer_whole(second_ref, before, ek_ref)
        group.emit(3)
    else:
        outer_halves(second_ref, before, ek_ref, es_ref)
        group.emit(3, 4)
    group.need(1, 5)
    for j in range(PARTS):
        rows = slice(j * group.part, (j + 1) * group.part)
        grad = scatter.take(j)
        hat, scale = normalise(hidden_ref[rows, :])
        own = g_ref[rows, :].astype(WIDE)
        out = own + norm_backward(grad, hat, scale, vec_ref[3:4, :])
        grad_ref[rows, :] = out
        low_ref[rows, :] = out.astype(LOW)
        for n, term in enumerate((grad * hat, grad, own, out)):
            sums_ref[n : n + 1, :] += jnp.sum(term, axis=0, keepdims=True)
    scatter.done()


def scores_back_kernel(
    heads, group, low_ref, mine_ref, other_ref, heads_ref, o_ref, lse_ref,
    mixed, outer_ref,
    weight, full, go3, dots, g3, key_acc, value_acc, gather_sems, local_sems,
):
    width = o_ref.shape[1]
    halves = Halves((mine_ref, other_ref), weight, local_sems, 0)
    halves.start()
    full[group.chunk(group.me), :] = low_ref[...]
    halves.wait()
    picks = (
        lax.broadcasted_iota(jnp.int32, (8, width), 1) // HEAD
        == lax.broadcasted_iota(jnp.int32, (8, width), 0)
    ).astype(WIDE)

    def spread(rows):
        grads = nn(full[rows, :], weight[:, 3 * width :]).astype(LOW)
        for h in range(heads):
            go3[h, rows, :] = grads[:, h * HEAD : (h + 1) * HEAD]
        term = grads.astype(WIDE) * o_ref[rows, :].astype(WIDE)
        dots[:, rows] = lax.dot_general(
            picks,
            term,
            (((1,), (1,)), ((), ())),
            precision=lax.Precision.HIGHEST,
            preferred_element_type=WIDE,
        )

    Gather(group, full, gather_sems).each(spread, lambda: group.need(4))
    group.need(3, 5)
    attention_back(heads_ref, go3, lse_ref, dots, g3, key_acc, value_acc, heads)
    for j in range(3 * heads):
        mixed[:, j * HEAD : (j + 1) * HEAD] = g3[j]
    group.emit(0)

    @pl.loop(0, outer_ref.shape[0] // TILE)
    def _(n):
        rows = pl.ds(pl.multiple_of(n * TILE, TILE), TILE)
        outer_ref[rows, :] = tn(full[:, rows], o_ref[...]).astype(LOW)


def attend_back_kernel(
    last, group, mixed, outer_ref, grad_ref, x_ref, mine_ref, other_ref, normed_ref, vec_ref,
    wk_ref, out_ref, sums_ref, *refs,
):
    if not last:
        got_ref, *refs = refs
    weight, outer, stage, land, total, scatter_sems, local_sems, *refs = refs
    width = outer_ref.shape[1]
    section = lax.axis_index("section")
    halves = Halves((mine_ref, other_ref), weight, local_sems, 0)
    halves.start()
    sums_ref[...] = jnp.zeros_like(sums_ref)

    half = weight.shape[1] // 2

    def products():
        @pl.loop(0, weight.shape[0] // TILE)
        def _(n):
            rows = pl.ds(pl.multiple_of(n * TILE, TILE), TILE)
            if last:
                outer[rows, : 3 * width] = tn(normed_ref[:, rows], mixed[...]).astype(LOW)
                outer[rows, 3 * width :] = outer_ref[rows, :]
            else:
                outer[section, rows, :] = tn(normed_ref[:, rows], mixed[:, :half]).astype(LOW)
                outer[1 - section, rows, : 3 * width - half] = tn(
                    normed_ref[:, rows], mixed[:, half:]
                ).astype(LOW)
                outer[1 - section, rows, 3 * width - half :] = outer_ref[rows, :]

    scatter = Scatter(group, stage, land, total, scatter_sems)
    if not last:
        group.need(1, 6)
        products()
        swap = push(outer.at[1], got_ref, refs[0], 0, 1 - section, "section")
        swap.start()
    halves.wait()
    scatter.start(lambda rows: nt(mixed[rows, :], weight[:, : 3 * width]))
    if last:
        group.need(1, 6)
        products()
    store = pltpu.make_async_copy(outer if last else outer.at[0], wk_ref, local_sems.at[2])
    store.start()
    group.need(2, 3)
    sums_ref[2:3, : 3 * width] = jnp.sum(mixed[...].astype(WIDE), axis=0, keepdims=True)
    for j in range(PARTS):
        rows = slice(j * group.part, (j + 1) * group.part)
        grad = scatter.take(j)
        hat, scale = normalise(x_ref[rows, :].astype(WIDE))
        out = grad_ref[rows, :] + norm_backward(grad, hat, scale, vec_ref[0:1, :])
        out_ref[rows, :] = out.astype(LOW)
        for n, term in enumerate((grad * hat, grad)):
            sums_ref[n : n + 1, :] += jnp.sum(term, axis=0, keepdims=True)
    scatter.done()
    store.wait()
    if not last:
        swap.wait()


def finish_kernel(
    late_ref, early1_ref, early2_ref, near_ref, far_ref, a0, n0, b0, a1, n1, b1,
    grads_ref, sums_ref, got_late, got_early1, got_early2,
    mine, stage4, block, land_col, land_x, land_z, send, land,
    deliver_sems, col_sems, x_sems, z_sems, part_sems,
):
    section, row = lax.axis_index("section"), lax.axis_index("row")
    group = Group(near_ref.shape[0])
    length, width = far_ref.shape
    others = [lax.rem(row + d, land_z.shape[0]) for d in range(1, land_z.shape[0])]
    group.greet(True, True, others)
    parts = [
        push(source, into, part_sems, n, 1 - section, "section")
        for n, (source, into) in enumerate(
            ((late_ref, got_late), (early1_ref, got_early1), (early2_ref, got_early2))
        )
    ]

    @pl.when(section == 0)
    def _():
        parts[0].start()

    @pl.when(section == 1)
    def _():
        parts[1].start()
        parts[2].start()

    deliver = Deliver(group, stage4, mine, deliver_sems)
    deliver.start(near_ref)

    block[...] = jnp.zeros_like(block)
    for layer, (attn, narrow, bend) in enumerate(((a0, n0, b0), (a1, n1, b1))):
        wide = [attn[0:1, :], attn[1:2, :], narrow[3:4, :], narrow[0:1, :], narrow[1:2, :], narrow[2:3, :]]
        for c in range(block.shape[0]):
            columns = slice(c * width, (c + 1) * width)
            for n, term in enumerate(wide):
                block[c, layer, n : n + 1, :] = term[:, columns]
            for n, term in enumerate((attn[2:3, :width], attn[2:3, 2 * width : 3 * width])):
                block[c, layer, 8 + n : 9 + n, :] = term
            for n in range(bend.shape[1] // width):
                block[c, layer, 10 + n : 11 + n, :] = bend[0:1, n * width : (n + 1) * width]
    copies = [
        push(block.at[other, :, pl.ds(0, 8)], land_col.at[n], col_sems, n, other)
        for n, other in enumerate((group.peer, group.diag, group.sib))
    ]
    for copy in copies:
        copy.start()
    for copy in copies:
        copy.wait()
    me = group.me
    block[me, :, :8] = block[me, :, :8] + (land_col[0] + (land_col[1] + land_col[2]))
    swap = push(block.at[me, 1 - section], land_x, x_sems, 0, 1 - section, "section")
    swap.start()
    swap.wait()
    land_z[row] = block[me, section] + land_x[...]
    copies = [
        push(land_z.at[row], land_z.at[row], z_sems, n, other, "row")
        for n, other in enumerate(others)
    ]
    for copy in copies:
        copy.start()

    deliver.done()

    @pl.when(section == 0)
    def _():
        send[...] = far_ref[...]

    @pl.when(section == 1)
    def _():
        send[...] = mine[...]

    swap = push(send, land, x_sems, 1, 1 - section, "section")
    swap.start()
    own = pl.ds(pl.multiple_of(section * length, length), length)
    away = pl.ds(pl.multiple_of((1 - section) * length, length), length)

    @pl.when(section == 0)
    def _():
        grads_ref[own, :] = mine[...].astype(WIDE)

    @pl.when(section == 1)
    def _():
        grads_ref[own, :] = far_ref[...].astype(WIDE)

    for copy in copies:
        copy.wait()
    result = land_z[0]
    for n in range(1, land_z.shape[0]):
        result = result + land_z[n]
    sums_ref[...] = result
    swap.wait()
    grads_ref[away, :] = land[...].astype(WIDE)

    @pl.when(section == 0)
    def _():
        parts[0].wait_send()
        parts[1].wait_recv()
        parts[2].wait_recv()

    @pl.when(section == 1)
    def _():
        parts[1].wait_send()
        parts[2].wait_send()
        parts[0].wait_recv()


VM = pl.BlockSpec(memory_space=pltpu.VMEM)
ANY = pl.BlockSpec(memory_space=pl.ANY)
PAIRS = pltpu.SemaphoreType.DMA((2, 3 * PARTS))
LOCAL = pltpu.SemaphoreType.DMA((4,))


def shape(dims, kind=LOW):
    return jax.ShapeDtypeStruct(dims, kind)


def launch(
    body, number, rows, in_specs, ins, outs, out_specs, scratch, swaps=(), diagonal=False, across=False, late=(),
):
    n_in, n_out, n = len(ins), len(outs), len(swaps)
    held_in = [i for i in range(n_in) if in_specs[i] is VM]
    held_out = [i for i in range(n_out) if out_specs[i] is VM]

    def kernel(*refs):
        refs = list(refs)
        takes, sources = refs[:n_in], refs[n_in : n_in + n]
        gives = refs[n_in + n : n_in + n + n_out]
        lands = refs[n_in + n + n_out : n_in + 2 * n + n_out]
        rest = refs[n_in + 2 * n + n_out :]
        own, rest = rest[: len(scratch)], rest[len(scratch) :]
        in_held, rest = rest[: len(held_in)], rest[len(held_in) :]
        out_held, rest = rest[: len(held_out)], rest[len(held_out) :]
        in_sems, out_sems, swap_sems = rest
        group = Group(rows)
        for k, i in enumerate(held_in):
            group.loads[i] = pltpu.make_async_copy(takes[i], in_held[k], in_sems.at[k])
            group.loads[i].start()
            takes[i] = in_held[k]
        for k, i in enumerate(held_out):
            group.stores[i] = pltpu.make_async_copy(out_held[k], gives[i], out_sems.at[k])
            gives[i] = out_held[k]
        group.greet(n or across, diagonal)
        other = 1 - lax.axis_index("section")
        copies = [
            push(source, land, swap_sems, i, other, "section")
            for i, (source, land) in enumerate(zip(sources, lands))
        ]
        for copy in copies:
            copy.start()
        group.need(*[i for i in held_in if i not in late])
        body(group, *takes, *gives, *own)
        group.emit(*[i for i in held_out if i not in group.begun])
        for copy in copies:
            copy.wait()
        for i in held_out:
            group.stores[i].wait()

    results = pl.pallas_call(
        kernel,
        out_shape=(*outs, *[shape(s.shape, s.dtype) for s in swaps]),
        in_specs=[ANY] * (n_in + n),
        out_specs=(ANY,) * (n_out + n),
        scratch_shapes=[
            *scratch,
            *[pltpu.VMEM(ins[i].shape, ins[i].dtype) for i in held_in],
            *[pltpu.VMEM(outs[i].shape, outs[i].dtype) for i in held_out],
            pltpu.SemaphoreType.DMA((len(held_in),)),
            pltpu.SemaphoreType.DMA((len(held_out),)),
            pltpu.SemaphoreType.DMA((2, max(n, 1))),
        ],
        compiler_params=pltpu.CompilerParams(
            collective_id=number, has_side_effects=True, vmem_limit_bytes=GRANT
        ),
        cost_estimate=pl.CostEstimate(flops=int(3e10), bytes_accessed=30 * MEBI, transcendentals=0),
    )(*ins, *swaps)
    return results[:n_out], results[n_out:]


def start_call(number, tokens, cotangent, small, raw, columns):
    width = tokens.shape[1]
    size = width * columns
    kinds = small.shape[0]
    outs = (shape((LENGTH, size)), shape((LENGTH, size)), shape((2, columns, kinds, width)), shape(raw.shape))
    blocks = pltpu.VMEM((columns, LENGTH, width), LOW)
    vectors = pltpu.VMEM((columns, kinds, width), LOW)
    return pl.pallas_call(
        start_kernel,
        out_shape=outs,
        in_specs=[ANY] * 4,
        out_specs=(VM, VM, VM, ANY),
        scratch_shapes=[
            blocks, blocks, vectors, vectors, PAIRS, PAIRS,
            pltpu.SemaphoreType.DMA((2, 3 * PARTS + 2)), LOCAL,
        ],
        compiler_params=pltpu.CompilerParams(
            collective_id=number, has_side_effects=True, vmem_limit_bytes=GRANT
        ),
        cost_estimate=pl.CostEstimate(flops=int(3e10), bytes_accessed=30 * MEBI, transcendentals=0),
    )(tokens, cotangent, small, raw)


def attend_call(number, gathered, x, pair, vec, bias, rows, width, swaps):
    size = vec.shape[1]
    heads = width // HEAD
    outs = (
        shape((LENGTH, size) if not gathered else (16, 128)),
        shape((LENGTH, size)),
        shape((3 * heads, LENGTH, HEAD)),
        shape((LENGTH, width)),
        shape((8, LENGTH), WIDE),
        shape((rows, size), WIDE),
        shape((rows, size)),
    )
    scratch = [
        pltpu.VMEM((size, 4 * width), LOW),
        pltpu.VMEM((heads, LENGTH, HEAD), LOW),
        *scatter_scratch(rows, size), PAIRS, LOCAL,
    ]
    return launch(
        functools.partial(attend_kernel, gathered, heads),
        number, rows, [VM, ANY, ANY, VM, VM], (x, *pair, vec, bias), outs, (VM,) * 7, scratch, swaps,
    )


def widen_call(number, second, pair, bias, grad, swaps):
    rows, size = second.shape
    wide = bias.shape[1]
    last = grad is not None
    ins, in_specs = [second, *pair, bias], [VM, ANY, ANY, VM]
    outs = [shape((LENGTH, size)), shape((LENGTH, wide)), shape((LENGTH, wide))]
    if last:
        ins, in_specs, outs = ins + [grad], in_specs + [VM], outs + [shape((size, wide))]
    scratch = [pltpu.VMEM((size, wide), LOW), PAIRS, LOCAL]
    return launch(
        functools.partial(widen_kernel, last),
        number, rows, in_specs, ins, outs, (VM,) * len(outs), scratch, swaps, late=(4,),
    )


def contract_call(number, active, hidden, pair, vec, swaps):
    rows, size = hidden.shape
    wide = active.shape[1]
    scratch = [pltpu.VMEM((size, wide), LOW), *scatter_scratch(rows, size), LOCAL]
    return launch(
        contract_kernel, number, rows, [VM, VM, ANY, ANY, VM], (active, hidden, *pair, vec),
        [shape((rows, size))], (VM,), scratch, swaps, late=(1,),
    )


def bend_call(number, last, grad, pair, slope, extra, size, rows, swaps):
    wide = slope.shape[1]
    columns = LENGTH // rows
    outs = [shape((LENGTH, wide)), shape((8, wide), WIDE)]
    scratch = [pltpu.VMEM((size, wide), LOW), PAIRS, LOCAL]
    if last:
        outs += [shape((LENGTH, size // columns))]
        scratch += [pltpu.VMEM((columns, rows, size // columns), LOW), pltpu.SemaphoreType.DMA((2, 3))]
    else:
        outs += [shape((LENGTH, size)), *[shape((size, wide // 2))] * 2]
    return launch(
        functools.partial(bend_kernel, last),
        number, rows, [VM, ANY, ANY, VM, VM], (grad, *pair, slope, extra),
        outs, (VM,) * len(outs), scratch, swaps, last, late=(3,) if last else (3, 4),
    )


def narrow_call(number, last, before, grad_own, pair, second, hidden, vec, swaps):
    rows, size = hidden.shape
    wide = before.shape[1]
    outs = (
        shape((rows, size), WIDE),
        shape((rows, size)),
        shape((8, size), WIDE),
        shape((size, wide if last else wide // 2)),
        shape((16, 128) if last else (size, wide // 2)),
    )
    scratch = [pltpu.VMEM((size, wide), LOW), *scatter_scratch(rows, size), LOCAL]
    return launch(
        functools.partial(narrow_kernel, last),
        number, rows, [VM, VM, ANY, ANY, VM, VM, VM], (before, grad_own, *pair, second, hidden, vec),
        outs, (VM, VM, VM, VM, ANY if last else VM), scratch, swaps, late=(1, 4, 5),
    )


def scores_back_call(number, low, pair, heads_all, o, lse, swaps):
    rows, size = low.shape
    width = o.shape[1]
    heads = width // HEAD
    outs = (shape((LENGTH, 3 * width)), shape((size, width)))
    scratch = [
        pltpu.VMEM((size, 4 * width), LOW),
        pltpu.VMEM((LENGTH, size), LOW),
        pltpu.VMEM((heads, LENGTH, HEAD), LOW),
        pltpu.VMEM((8, LENGTH), WIDE),
        pltpu.VMEM((3 * heads, LENGTH, HEAD), LOW),
        pltpu.VMEM((LENGTH, HEAD), WIDE),
        pltpu.VMEM((LENGTH, HEAD), WIDE),
        PAIRS, LOCAL,
    ]
    return launch(
        functools.partial(scores_back_kernel, heads),
        number, rows, [VM, ANY, ANY, VM, VM, VM], (low, *pair, heads_all, o, lse),
        outs, (VM,) * 2, scratch, swaps, late=(3, 4, 5),
    )


def attend_back_call(number, last, mixed, outer, grad, x_own, pair, normed, vec, swaps):
    rows, size = grad.shape
    width = outer.shape[1]
    half = 2 * width
    outs = [shape((size, 2 * half if last else half)), shape((rows, size)), shape((8, size), WIDE)]
    out_specs = [ANY, VM, VM]
    scratch = [
        pltpu.VMEM((size, 4 * width), LOW),
        pltpu.VMEM((size, 2 * half) if last else (2, size, half), LOW),
        *scatter_scratch(rows, size), LOCAL,
    ]
    if not last:
        outs, out_specs = outs + [shape((size, half))], out_specs + [ANY]
        scratch += [pltpu.SemaphoreType.DMA((2, 1))]
    return launch(
        functools.partial(attend_back_kernel, last),
        number, rows, [VM, VM, VM, VM, ANY, ANY, VM, VM],
        (mixed, outer, grad, x_own, *pair, normed, vec), outs, out_specs, scratch, swaps, False, True, late=(1, 2, 3, 6),
    )


def finish_call(number, late, early1, early2, near, far, sums, row_count):
    rows, size = near.shape
    length, width = far.shape
    columns = length // rows
    outs = (
        shape((2 * length, width), WIDE),
        shape((16, width), WIDE),
        *[shape(part.shape) for part in (late, early1, early2)],
    )
    scratch = [
        pltpu.VMEM((length, width), LOW),
        pltpu.VMEM((columns, rows, width), LOW),
        pltpu.VMEM((columns, 2, 16, width), WIDE),
        pltpu.VMEM((3, 2, 8, width), WIDE),
        pltpu.VMEM((16, width), WIDE),
        pltpu.VMEM((row_count, 16, width), WIDE),
        pltpu.VMEM((length, width), LOW),
        pltpu.VMEM((length, width), LOW),
        pltpu.SemaphoreType.DMA((2, 3)),
        pltpu.SemaphoreType.DMA((2, 3)),
        pltpu.SemaphoreType.DMA((2, 2)),
        pltpu.SemaphoreType.DMA((2, row_count)),
        pltpu.SemaphoreType.DMA((2, 3)),
    ]
    return pl.pallas_call(
        finish_kernel,
        out_shape=outs,
        in_specs=[ANY] * 3 + [VM] * 8,
        out_specs=(VM, VM, ANY, ANY, ANY),
        scratch_shapes=scratch,
        compiler_params=pltpu.CompilerParams(
            collective_id=number, has_side_effects=True, vmem_limit_bytes=GRANT
        ),
        cost_estimate=pl.CostEstimate(flops=int(3e10), bytes_accessed=30 * MEBI, transcendentals=0),
    )(late, early1, early2, near, far, *sums)


def swap_sections(value):
    return lax.ppermute(value, "section", [(0, 1), (1, 0)])


def on_device(
    tokens,
    cotangent,
    first_gain,
    first_shift,
    attend_weight,
    attend_bias,
    output_weight,
    output_bias,
    second_gain,
    second_shift,
    expand_weight,
    expand_bias,
    contract_weight,
    contract_bias,
):
    section = lax.axis_index("section")
    column = lax.axis_index("col")
    first_section = section == 0
    columns = lax.axis_size("col")
    width = tokens.shape[1]
    size = width * columns
    rows = LENGTH // columns

    def pick(early, later):
        return jnp.where(first_section, early, later)

    block_rows = attend_weight.shape[1]
    units = (
        jnp.concatenate(
            [attend_weight[0].reshape(block_rows, 3 * width), output_weight[0].T], axis=1
        ),
        expand_weight[0],
        contract_weight[0].T,
    )
    kept_blocks, sent_blocks = [], []
    for unit in units:
        half = unit.shape[1] // 2
        low, high = unit[:, :half], unit[:, half:]
        kept_blocks.append(pick(low, high))
        sent_blocks.append(pick(high, low))

    small = jnp.concatenate(
        [
            first_gain,
            first_shift,
            output_bias,
            second_gain,
            second_shift,
            contract_bias,
            attend_bias[0],
            expand_bias[0].reshape(-1, width),
        ],
        0,
    )
    filled = small.shape[0]
    small = jnp.pad(small, ((0, -filled % 16), (0, 0)))
    got_attend = swap_sections(sent_blocks[0])
    raw = jnp.stack(sent_blocks[1:])
    got_attend, raw = lax.optimization_barrier((got_attend, raw))
    x0_full, gy_full, vectors, got_blocks = start_call(1, tokens, cotangent, small, raw, columns)
    mats = [[], []]
    for own, got in zip(kept_blocks, (got_attend, got_blocks[0], got_blocks[1])):
        for layer, block in enumerate((pick(own, got), pick(got, own))):
            mats[layer].append(lax.all_gather(block, "row", axis=0, tiled=True))
    vectors = vectors.astype(WIDE)
    wide_vectors = jnp.swapaxes(vectors[:, :, :6], 1, 2).reshape(2, 6, size)
    wide_vectors = jnp.pad(wide_vectors, ((0, 0), (0, 2), (0, 0)))
    own_vectors = lax.dynamic_index_in_dim(vectors, column, 1, keepdims=False)
    attend_biases = jnp.stack(
        [own_vectors[:, 6], jnp.zeros_like(own_vectors[:, 6]), own_vectors[:, 7]], 1
    ).reshape(2, 1, 3 * width)
    expand_biases = own_vectors[:, 8:filled].reshape(2, 1, -1)

    def own_rows(full):
        return lax.dynamic_slice_in_dim(full, column * rows, rows, 0)

    def own_features(full):
        return lax.dynamic_slice_in_dim(full, column * width, width, 1)

    attn = (mats[0][0], swap_sections(mats[0][0]))
    x = x0_full
    kept, pairs = [], []
    owns = [own_rows(x0_full)]
    for layer in range(2):
        last = layer == 1
        vec = wide_vectors[layer]
        (full, normed, heads, o, lse, hidden, second_own), (other,) = attend_call(
            2 + 3 * layer, not last, x, attn, vec, attend_biases[layer], rows, width, [mats[layer][1]]
        )
        expand = (mats[layer][1], other)
        outs, (other,) = widen_call(
            3 + 3 * layer, second_own, expand, expand_biases[layer],
            gy_full if last else None, [mats[layer][2]],
        )
        second, active, slope = outs[:3]
        contract = (mats[layer][2], other)
        if last:
            c1 = outs[3]
        outs, others = contract_call(
            4 + 3 * layer, active, hidden, contract, vec, [] if last else [mats[1][0]]
        )
        pairs.append((attn, expand, contract))
        kept.append((normed, heads, o, lse, hidden, second, active, slope))
        x = outs[0]
        owns.append(x)
        if not last:
            attn = (mats[1][0], others[0])
    y0 = own_features(full)

    def add(keep, got, then):
        total = (keep.astype(WIDE) + got.astype(WIDE)).astype(LOW)
        return lax.optimization_barrier((total, then))

    def scatter(total):
        return lax.psum_scatter(total, "row", scatter_dimension=0, tiled=True)

    def tie(value, then):
        return lax.optimization_barrier((value, then))

    attn, expand, contract = pairs[1]
    normed, heads, o, lse, hidden, second, active, slope = kept[1]
    (before, bend_sums1, y1), _ = bend_call(8, True, gy_full, contract, slope, owns[2], size, rows, [])
    layer_low, layer_high = pick(y0, y1), pick(y1, y0)
    (grad_hidden, low, narrow_sums1, e1, _), _ = narrow_call(
        9, True, before, own_rows(gy_full), expand, second, hidden, wide_vectors[1], []
    )
    (mixed, outer), (layer_got,) = scores_back_call(10, low, attn, heads, o, lse, [layer_high])
    part_c1, mixed = tie(scatter(c1), mixed)
    (w1, gx1_own, attend_sums1), (far_c1,) = attend_back_call(
        11, True, mixed, outer, grad_hidden, owns[1], attn, normed, wide_vectors[1], [part_c1]
    )
    layer_outputs = jnp.concatenate([pick(layer_low, layer_got), pick(layer_got, layer_low)], 0)

    attn, expand, contract = pairs[0]
    normed, heads, o, lse, hidden, second, active, slope = kept[0]
    part_e1 = scatter(e1)
    (before, bend_sums0, gx1_full, ck0, cs0), (far_e1,) = bend_call(
        12, False, gx1_own, contract, slope, active, size, rows, [part_e1]
    )
    (grad_hidden, low, narrow_sums0, ek0, es0), (ct0,) = narrow_call(
        13, False, before, gx1_own, expand, second, hidden, wide_vectors[0], [cs0]
    )
    total_c0, low = add(ck0, ct0, low)
    (mixed, outer), (et0,) = scores_back_call(14, low, attn, heads, o, lse, [es0])
    total_e0, mixed = add(ek0, et0, mixed)
    part_w1, mixed = tie(scatter(w1), mixed)
    part_c0, mixed = tie(scatter(total_c0), mixed)
    (wk0, gx0_own, attend_sums0, wt0), _ = attend_back_call(
        15, False, mixed, outer, grad_hidden, owns[0], attn, normed, wide_vectors[0], []
    )
    total_w0, gx0_own = add(wk0, wt0, gx0_own)
    part_e0 = scatter(total_e0)
    input_grads, small_grads, far_w1, far_c0, far_e0 = finish_call(
        16,
        part_w1,
        part_c0,
        part_e0,
        gx0_own,
        own_features(gx1_full),
        (attend_sums0, narrow_sums0, bend_sums0, attend_sums1, narrow_sums1, bend_sums1),
        lax.axis_size("row"),
    )

    late = [part_w1, part_e1, part_c1]
    part_w0, small_grads = tie(scatter(total_w0), small_grads)
    far_w0 = lax.ppermute(part_w0, "section", [(1, 0)])

    units = []
    for late, far_late, early, far_early in (
        (part_w1, far_w1, part_w0, far_w0),
        (part_e1, far_e1, part_e0, far_e0),
        (part_c1, far_c1, part_c0, far_c0),
    ):
        whole = jnp.concatenate([early, far_early], 1).astype(WIDE)
        units.append(pick(whole, late.astype(WIDE) + far_late.astype(WIDE)))
    attn_part, expand_part, contract_part = units

    return (
        layer_outputs[None],
        input_grads[None],
        small_grads[0:1],
        small_grads[1:2],
        attn_part[:, : 3 * width].reshape(block_rows, 3, width)[None],
        small_grads[8:10][None],
        attn_part[:, 3 * width :].T[None],
        small_grads[2:3],
        small_grads[3:4],
        small_grads[4:5],
        expand_part[None],
        small_grads[10 : 10 + expand_bias.shape[1] // width].reshape(1, -1),
        contract_part.T[None],
        small_grads[5:6],
    )


def solution(mesh):
    return jax.shard_map(
        on_device,
        mesh=mesh,
        in_specs=(
            P("row", "col"),
            P("row", "col"),
            P("section", "col"),
            P("section", "col"),
            P("section", "row", None, "col"),
            P("section", None, "col"),
            P("section", "col", "row"),
            P("section", "col"),
            P("section", "col"),
            P("section", "col"),
            P("section", "row", "col"),
            P("section", "col"),
            P("section", "col", "row"),
            P("section", "col"),
        ),
        out_specs=(
            P("section", "row", "col"),
            P("section", "row", "col"),
            P("section", "col"),
            P("section", "col"),
            P("section", "row", None, "col"),
            P("section", None, "col"),
            P("section", "col", "row"),
            P("section", "col"),
            P("section", "col"),
            P("section", "col"),
            P("section", "row", "col"),
            P("section", "col"),
            P("section", "col", "row"),
            P("section", "col"),
        ),
        check_vma=False,
    )
```

```python
import functools

import jax
import jax.numpy as jnp
from jax import lax
from jax.experimental import pallas as pl
from jax.experimental.pallas import tpu as pltpu
from jax.sharding import PartitionSpec as P

HEAD = 64
LENGTH = 1024
EPS = 1e-05
LOW = jnp.bfloat16
WIDE = jnp.float32
MESH = pl.DeviceIdType.MESH
PARTS = 2
TILE = 256
MEBI = 1024 * 1024
GRANT = 58 * MEBI


def nn(left, right):
    return lax.dot_general(left, right, (((1,), (0,)), ((), ())), preferred_element_type=WIDE)


def nt(left, right):
    return lax.dot_general(left, right, (((1,), (1,)), ((), ())), preferred_element_type=WIDE)


def tn(left, right):
    return lax.dot_general(left, right, (((0,), (0,)), ((), ())), preferred_element_type=WIDE)


def normalise(values):
    center = jnp.mean(values, axis=1, keepdims=True)
    centred = values - center
    scale = lax.rsqrt(jnp.mean(centred * centred, axis=1, keepdims=True) + EPS)
    return centred * scale, scale


def norm_backward(grad, hat, scale, gain):
    scaled = grad * gain
    mean_one = jnp.mean(scaled, axis=1, keepdims=True)
    mean_two = jnp.mean(scaled * hat, axis=1, keepdims=True)
    return scale * (scaled - mean_one - hat * mean_two)


class Group:
    def __init__(self, rows):
        self.me = lax.axis_index("col")
        chip, core = self.me // 2, self.me % 2
        self.sib = chip * 2 + 1 - core
        self.peer = (1 - chip) * 2 + core
        self.diag = (1 - chip) * 2 + 1 - core
        self.rows = rows
        self.part = rows // PARTS
        self.loads, self.stores, self.begun = {}, {}, set()

    def need(self, *places):
        for place in places:
            self.loads[place].wait()

    def emit(self, *places):
        for place in places:
            self.stores[place].start()
            self.begun.add(place)

    def greet(self, swaps, diagonal, rows=()):
        barrier = pltpu.get_barrier_semaphore()
        others = [{"col": self.sib}, {"col": self.peer}]
        if diagonal:
            others.append({"col": self.diag})
        if swaps:
            others.append({"section": 1 - lax.axis_index("section")})
        others += [{"row": row} for row in rows]
        for other in others:
            pl.semaphore_signal(barrier, inc=1, device_id=other, device_id_type=MESH)
        pl.semaphore_wait(barrier, len(others))

    def slab(self, owner, j):
        return pl.ds(pl.multiple_of(owner * self.rows + j * self.part, self.part), self.part)

    def chunk(self, owner):
        return pl.ds(pl.multiple_of(owner * self.rows, self.rows), self.rows)


def push(src, dst, sems, slot, target, axis="col"):
    return pltpu.make_async_remote_copy(
        src_ref=src,
        dst_ref=dst,
        send_sem=sems.at[0, slot],
        recv_sem=sems.at[1, slot],
        device_id={axis: target},
        device_id_type=MESH,
    )


class Gather:
    def __init__(self, group, full, sems, blocks=False):
        self.group, self.full, self.sems, self.blocks = group, full, sems, blocks

    def piece(self, owner, j):
        if not self.blocks:
            return self.full.at[self.group.slab(owner, j)]
        part = self.full.shape[1] // PARTS
        return self.full.at[owner, pl.ds(j * part, part)]

    def start(self):
        g = self.group
        self.over, self.near, self.relayed = [], [], []
        for j in range(PARTS):
            piece = self.piece(g.me, j)
            self.over.append(push(piece, piece, self.sems, j, g.peer))
            self.over[-1].start()
        for j in range(PARTS):
            piece = self.piece(g.me, j)
            self.near.append(push(piece, piece, self.sems, PARTS + j, g.sib))
            self.near[-1].start()

    def sibling(self):
        for copy in self.near:
            copy.wait_recv()

    def relay(self):
        g = self.group
        for j in range(PARTS):
            self.over[j].wait_recv()
            piece = self.piece(g.peer, j)
            self.relayed.append(push(piece, piece, self.sems, 2 * PARTS + j, g.sib))
            self.relayed[-1].start()

    def diagonal(self):
        for copy in self.relayed:
            copy.wait_recv()

    def done(self):
        for copy in self.over + self.near + self.relayed:
            copy.wait_send()

    def each(self, body, first=None):
        g = self.group
        self.start()
        if first is not None:
            first()
        body(g.chunk(g.me))
        self.sibling()
        body(g.chunk(g.sib))
        self.relay()
        body(g.chunk(g.peer))
        self.diagonal()
        body(g.chunk(g.diag))
        self.done()


class Scatter:
    def __init__(self, group, stage, land, total, sems):
        self.group, self.stage, self.land, self.total, self.sems = group, stage, land, total, sems

    def start(self, part):
        g, stage, land = self.group, self.stage, self.land
        self.first, self.over, self.near = [], [], []
        def split(owner):
            whole = part(g.chunk(owner))
            return [whole[j * g.part : (j + 1) * g.part] for j in range(PARTS)]

        for j, mine in enumerate(split(g.diag)):
            stage[0, j] = mine.astype(LOW)
            self.first.append(push(stage.at[0, j], land.at[0, j], self.sems, j, g.sib))
            self.first[-1].start()
        for j, mine in enumerate(split(g.peer)):
            self.first[j].wait_recv()
            stage[1, j] = (mine + land[0, j].astype(WIDE)).astype(LOW)
            self.over.append(push(stage.at[1, j], land.at[1, j], self.sems, PARTS + j, g.peer))
            self.over[-1].start()
        for j, mine in enumerate(split(g.sib)):
            stage[2, j] = mine.astype(LOW)
            self.near.append(push(stage.at[2, j], land.at[2, j], self.sems, 2 * PARTS + j, g.sib))
            self.near[-1].start()
        for j, mine in enumerate(split(g.me)):
            self.total[j] = mine

    def take(self, j):
        self.near[j].wait_recv()
        self.over[j].wait_recv()
        land = self.land
        return self.total[j] + (land[1, j].astype(WIDE) + land[2, j].astype(WIDE))

    def done(self):
        for copy in self.first + self.over + self.near:
            copy.wait_send()


class Deliver:
    def __init__(self, group, stage, out, sems):
        self.group, self.stage, self.out, self.sems = group, stage, out, sems

    def start(self, rows_ref):
        g, width = self.group, self.out.shape[1]
        for c in range(self.stage.shape[0]):
            self.stage[c] = rows_ref[:, c * width : (c + 1) * width]
        place = self.out.at[g.chunk(g.me)]
        self.copies = [
            push(self.stage.at[other], place, self.sems, n, other)
            for n, other in enumerate((g.peer, g.diag, g.sib))
        ]
        for copy in self.copies:
            copy.start()
        self.out[g.chunk(g.me), :] = self.stage[g.me]

    def done(self):
        for copy in self.copies:
            copy.wait()


def scatter_scratch(rows, width):
    part = rows // PARTS
    return [
        pltpu.VMEM((3, PARTS, part, width), LOW),
        pltpu.VMEM((3, PARTS, part, width), LOW),
        pltpu.VMEM((PARTS, part, width), WIDE),
        pltpu.SemaphoreType.DMA((2, 3 * PARTS)),
    ]


class Halves:
    def __init__(self, pair, whole, sems, slot):
        if pair[0].shape[1] == whole.shape[1]:
            self.copies = [pltpu.make_async_copy(pair[0], whole, sems.at[slot])]
            return
        section = lax.axis_index("section")
        half = whole.shape[1] // 2
        self.copies = []
        for n, place in enumerate((section, 1 - section)):
            columns = pl.ds(pl.multiple_of(place * half, half), half)
            self.copies.append(
                pltpu.make_async_copy(pair[n], whole.at[:, columns], sems.at[slot + n])
            )

    def start(self):
        for copy in self.copies:
            copy.start()

    def wait(self):
        for copy in self.copies:
            copy.wait()


def attention_out(heads_ref, o3, lse_ref, heads):
    length = heads_ref.shape[1]
    size = min(TILE, length)

    @pl.loop(0, heads)
    def _(h):
        for i in range(length // size):
            rows = slice(i * size, (i + 1) * size)
            finish = (i + 1) * size
            queries = heads_ref[h, rows, :]
            scores = nt(heads_ref[heads + h, :finish, :], queries)
            keep = lax.broadcasted_iota(jnp.int32, (size, size), 0) <= lax.broadcasted_iota(
                jnp.int32, (size, size), 1
            )
            last = jnp.where(keep, scores[finish - size :], -1000000000.0)
            scores = last if i == 0 else jnp.concatenate([scores[: finish - size], last], 0)
            highest = jnp.max(scores, axis=0, keepdims=True)
            powers = jnp.exp(scores - highest)
            summed = jnp.sum(powers, axis=0, keepdims=True)
            mixed = tn(heads_ref[2 * heads + h, :finish, :], powers.astype(LOW))
            o3[h, rows, :] = (mixed / summed).T.astype(LOW)
            lse_ref[pl.ds(h, 1), rows] = highest + jnp.log(summed)


def attention_back(heads_ref, go3, lse_ref, dots_ref, g3, key_acc, value_acc, heads):
    length = heads_ref.shape[1]
    size = min(TILE, length)

    @pl.loop(0, heads)
    def _(h):
        for i in reversed(range(length // size)):
            rows = slice(i * size, (i + 1) * size)
            finish = (i + 1) * size
            queries = heads_ref[h, rows, :]
            keys = heads_ref[heads + h, :finish, :]
            grads = go3[h, rows, :]
            scores = nt(keys, queries) - lse_ref[pl.ds(h, 1), rows]
            keep = lax.broadcasted_iota(jnp.int32, (size, size), 0) <= lax.broadcasted_iota(
                jnp.int32, (size, size), 1
            )
            last = jnp.where(keep, scores[finish - size :], -1000000000.0)
            scores = last if i == 0 else jnp.concatenate([scores[: finish - size], last], 0)
            probs = jnp.exp(scores)
            grad_probs = nt(heads_ref[2 * heads + h, :finish, :], grads)
            grad_scores = (probs * (grad_probs - dots_ref[pl.ds(h, 1), rows])).astype(LOW)
            g3[h, rows, :] = (tn(grad_scores, keys) * HEAD ** (-0.5)).astype(LOW)
            key_part = nn(grad_scores, queries)
            value_part = nn(probs.astype(LOW), grads)
            if finish == length:
                key_acc[...] = key_part
                value_acc[...] = value_part
            else:
                key_acc[:finish, :] += key_part
                value_acc[:finish, :] += value_part
        g3[heads + h] = key_acc[...].astype(LOW)
        g3[2 * heads + h] = value_acc[...].astype(LOW)


def start_kernel(
    tokens_ref, cotangent_ref, small_ref, keep_ref, sent_ref, contract_ref,
    x_ref, g_ref, vectors_ref, got_ref, got_contract_ref, mine_ref, far_ref,
    x4, g4, s4, other4, x_sems, g_sems, s_sems, row_sems, far_sems, local_sems,
):
    section, row = lax.axis_index("section"), lax.axis_index("row")
    away = 1 - section
    group = Group(x_ref.shape[0] // 4)
    length, block = x_ref.shape[0], keep_ref.shape[0]
    count = mine_ref.shape[0] // block
    others = [lax.rem(row + d, count) for d in range(1, count)]
    loads = []
    rows = pl.ds(pl.multiple_of(section * length, length), length)
    for n, (source, into) in enumerate(((tokens_ref.at[rows], x4), (cotangent_ref.at[rows], g4), (small_ref, s4))):
        loads.append(pltpu.make_async_copy(source, into.at[group.me], local_sems.at[n]))
        loads[-1].start()
    group.greet(True, False, others)

    def place(owner):
        return pl.ds(pl.multiple_of(owner * block, block), block)

    raw = push(sent_ref, got_ref, s_sems, 3 * PARTS + 1, away, "section")
    raw.start()
    gathers = [Gather(group, x4, x_sems, True), Gather(group, s4, s_sems, True), Gather(group, g4, g_sems, True)]
    for gather, load in zip(gathers, (loads[0], loads[2], loads[1])):
        load.wait()
        gather.start()
    own = mine_ref.at[place(row)]

    @pl.when(section == 0)
    def _():
        copy = pltpu.make_async_copy(keep_ref, own, local_sems.at[3])
        copy.start()
        copy.wait()

    raw.wait_recv()

    @pl.when(section == 1)
    def _():
        copy = pltpu.make_async_copy(got_ref, own, local_sems.at[3])
        copy.start()
        copy.wait()

    spread = [push(own, own, row_sems, n, other, "row") for n, other in enumerate(others)]
    for copy in spread:
        copy.start()
    passed = [push(own, far_ref.at[place(row)], far_sems, 0, away, "section")]
    passed[0].start()
    for gather in gathers:
        gather.sibling()
        gather.relay()
    swap = None
    for d in range(1, count):
        spread[d - 1].wait_recv()
        piece = place(lax.rem(row + count - d, count))
        passed.append(push(mine_ref.at[piece], far_ref.at[piece], far_sems, d, away, "section"))
        passed[-1].start()
    for gather in gathers:
        gather.diagonal()
    swap = push(s4, other4, s_sems, 3 * PARTS, away, "section")
    swap.start()
    contract = push(contract_ref, got_contract_ref, s_sems, 3 * PARTS + 2, away, "section")
    contract.start()
    width = x4.shape[2]
    for c in range(x4.shape[0]):
        x_ref[:, c * width : (c + 1) * width] = x4[c]
        g_ref[:, c * width : (c + 1) * width] = g4[c]
    swap.wait()
    vectors_ref[section] = s4[...]
    vectors_ref[away] = other4[...]
    for gather in gathers:
        gather.done()
    for copy in spread:
        copy.wait_send()
    for copy in passed:
        copy.wait()
    raw.wait_send()
    contract.wait()


def attend_kernel(
    gathered, heads, group, x_ref, mine_ref, other_ref, vec_ref, bias_ref,
    full_ref, normed_ref, heads_ref, o_ref, lse_ref, hidden_ref, second_ref,
    weight, o3, stage, land, total, scatter_sems, gather_sems, local_sems,
):
    width = o_ref.shape[1]
    halves = Halves((mine_ref, other_ref), weight, local_sems, 0)
    halves.start()
    if not gathered:
        full_ref[group.chunk(group.me), :] = x_ref[...]
    halves.wait()

    def project(rows):
        values = (x_ref if gathered else full_ref)[rows, :].astype(WIDE)
        hat, _ = normalise(values)
        normed = (hat * vec_ref[0:1, :] + vec_ref[1:2, :]).astype(LOW)
        normed_ref[rows, :] = normed
        mixed = nn(normed, weight[:, : 3 * width]) + bias_ref[...]
        for j in range(3 * heads):
            piece = mixed[:, j * HEAD : (j + 1) * HEAD]
            if j < heads:
                piece = piece * HEAD ** (-0.5)
            heads_ref[j, rows, :] = piece.astype(LOW)

    if gathered:
        full_ref[...] = jnp.zeros_like(full_ref)

        @pl.loop(0, LENGTH // group.rows)
        def _(n):
            project(group.chunk(n))
    else:
        Gather(group, full_ref, gather_sems).each(project)
    group.emit(0, 1, 2)

    attention_out(heads_ref, o3, lse_ref, heads)
    for h in range(heads):
        o_ref[:, h * HEAD : (h + 1) * HEAD] = o3[h]
    group.emit(3, 4)

    scatter = Scatter(group, stage, land, total, scatter_sems)
    scatter.start(lambda rows: nt(o_ref[rows, :], weight[:, 3 * width :]))
    for j in range(PARTS):
        rows = slice(j * group.part, (j + 1) * group.part)
        residual = (x_ref if gathered else full_ref)[group.slab(group.me, j), :].astype(WIDE)
        hidden = residual + scatter.take(j) + vec_ref[2:3, :]
        hidden_ref[rows, :] = hidden
        hat, _ = normalise(hidden)
        second_ref[rows, :] = (hat * vec_ref[3:4, :] + vec_ref[4:5, :]).astype(LOW)
    scatter.done()


def outer_whole(left_ref, right_ref, out_ref):
    @pl.loop(0, left_ref.shape[1] // TILE)
    def _(n):
        rows = pl.ds(pl.multiple_of(n * TILE, TILE), TILE)
        out_ref[rows, :] = tn(left_ref[:, rows], right_ref[...]).astype(LOW)


def widen_kernel(last, group, second_ref, em_ref, eo_ref, bias_ref, *refs):
    if last:
        g_ref, *refs = refs
    full_ref, active_ref, slope_ref, *refs = refs
    if last:
        c_ref, *refs = refs
    expand, gather_sems, local_sems = refs
    halves = Halves((em_ref, eo_ref), expand, local_sems, 0)
    halves.start()
    full_ref[group.chunk(group.me), :] = second_ref[...]
    halves.wait()

    def widen(rows):
        t = nn(full_ref[rows, :], expand[...]) + bias_ref[...]
        square = t * t
        bent = jnp.tanh(0.7978845608028654 * t * (1.0 + 0.044715 * square))
        active_ref[rows, :] = (0.5 * t * (1.0 + bent)).astype(LOW)
        slope_ref[rows, :] = (
            0.5 * (1.0 + bent)
            + (0.5 * 0.7978845608028654) * t * (1.0 - bent * bent) * (1.0 + 3 * 0.044715 * square)
        ).astype(LOW)

    Gather(group, full_ref, gather_sems).each(widen)
    if last:
        group.emit(0, 1, 2)
        group.need(4)
        outer_whole(g_ref, active_ref, c_ref)


def outer_halves(left_ref, right_ref, keep_ref, send_ref):
    section = lax.axis_index("section")
    half = right_ref.shape[1] // 2
    for place, out in ((section, keep_ref), (1 - section, send_ref)):
        columns = pl.ds(pl.multiple_of(place * half, half), half)

        @pl.loop(0, left_ref.shape[1] // TILE)
        def _(n):
            rows = pl.ds(pl.multiple_of(n * TILE, TILE), TILE)
            out[rows, :] = tn(left_ref[:, rows], right_ref[:, columns]).astype(LOW)


def contract_kernel(
    group, active_ref, hidden_ref, cm_ref, co_ref, vec_ref, result_ref,
    contract, stage, land, total, scatter_sems, local_sems,
):
    halves = Halves((cm_ref, co_ref), contract, local_sems, 0)
    halves.start()
    halves.wait()
    scatter = Scatter(group, stage, land, total, scatter_sems)
    scatter.start(lambda rows: nt(active_ref[rows, :], contract[...]))
    group.need(1)
    for j in range(PARTS):
        rows = slice(j * group.part, (j + 1) * group.part)
        result = hidden_ref[rows, :] + scatter.take(j) + vec_ref[5:6, :]
        result_ref[rows, :] = result.astype(LOW)
    scatter.done()


def bend_kernel(last, group, g_ref, cm_ref, co_ref, slope_ref, extra_ref, *refs):
    before, sums_ref, *refs = refs
    if last:
        out_ref, *refs = refs
    else:
        full_ref, ck_ref, cs_ref, *refs = refs
    contract, gather_sems, local_sems, *refs = refs
    if last:
        stage4, deliver_sems = refs
        deliver = Deliver(group, stage4, out_ref, deliver_sems)
    halves = Halves((cm_ref, co_ref), contract, local_sems, 0)
    halves.start()
    sums_ref[...] = jnp.zeros_like(sums_ref)
    if last:
        deliver.start(extra_ref)
    else:
        full_ref[group.chunk(group.me), :] = g_ref[...]
    halves.wait()

    if last:
        group.need(3)

    def bend(rows):
        rows_grad = (g_ref if last else full_ref)[rows, :]
        grad = (nn(rows_grad, contract[...]) * slope_ref[rows, :].astype(WIDE)).astype(LOW)
        before[rows, :] = grad
        sums_ref[0:1, :] += jnp.sum(grad.astype(WIDE), axis=0, keepdims=True)

    if last:

        @pl.loop(0, LENGTH // group.rows)
        def _(n):
            bend(group.chunk(n))

        deliver.done()
    else:
        Gather(group, full_ref, gather_sems).each(bend, lambda: group.need(3))
        group.emit(0, 2)
        group.need(4)
        outer_halves(full_ref, extra_ref, ck_ref, cs_ref)


def narrow_kernel(
    last, group, before, g_ref, em_ref, eo_ref, second_ref, hidden_ref, vec_ref,
    grad_ref, low_ref, sums_ref, ek_ref, es_ref,
    expand, stage, land, total, scatter_sems, local_sems,
):
    halves = Halves((em_ref, eo_ref), expand, local_sems, 0)
    halves.start()
    sums_ref[...] = jnp.zeros_like(sums_ref)
    halves.wait()
    scatter = Scatter(group, stage, land, total, scatter_sems)
    scatter.start(lambda rows: nt(before[rows, :], expand[...]))
    group.need(4)
    if last:
        outer_whole(second_ref, before, ek_ref)
        group.emit(3)
    else:
        outer_halves(second_ref, before, ek_ref, es_ref)
        group.emit(3, 4)
    group.need(1, 5)
    for j in range(PARTS):
        rows = slice(j * group.part, (j + 1) * group.part)
        grad = scatter.take(j)
        hat, scale = normalise(hidden_ref[rows, :])
        own = g_ref[rows, :].astype(WIDE)
        out = own + norm_backward(grad, hat, scale, vec_ref[3:4, :])
        grad_ref[rows, :] = out
        low_ref[rows, :] = out.astype(LOW)
        for n, term in enumerate((grad * hat, grad, own, out)):
            sums_ref[n : n + 1, :] += jnp.sum(term, axis=0, keepdims=True)
    scatter.done()


def scores_back_kernel(
    heads, group, low_ref, mine_ref, other_ref, heads_ref, o_ref, lse_ref,
    mixed, outer_ref,
    weight, full, go3, dots, g3, key_acc, value_acc, gather_sems, local_sems,
):
    width = o_ref.shape[1]
    halves = Halves((mine_ref, other_ref), weight, local_sems, 0)
    halves.start()
    full[group.chunk(group.me), :] = low_ref[...]
    halves.wait()
    picks = (
        lax.broadcasted_iota(jnp.int32, (8, width), 1) // HEAD
        == lax.broadcasted_iota(jnp.int32, (8, width), 0)
    ).astype(WIDE)

    def spread(rows):
        grads = nn(full[rows, :], weight[:, 3 * width :]).astype(LOW)
        for h in range(heads):
            go3[h, rows, :] = grads[:, h * HEAD : (h + 1) * HEAD]
        term = grads.astype(WIDE) * o_ref[rows, :].astype(WIDE)
        dots[:, rows] = lax.dot_general(
            picks,
            term,
            (((1,), (1,)), ((), ())),
            precision=lax.Precision.HIGHEST,
            preferred_element_type=WIDE,
        )

    Gather(group, full, gather_sems).each(spread, lambda: group.need(4))
    group.need(3, 5)
    attention_back(heads_ref, go3, lse_ref, dots, g3, key_acc, value_acc, heads)
    for j in range(3 * heads):
        mixed[:, j * HEAD : (j + 1) * HEAD] = g3[j]
    group.emit(0)

    @pl.loop(0, outer_ref.shape[0] // TILE)
    def _(n):
        rows = pl.ds(pl.multiple_of(n * TILE, TILE), TILE)
        outer_ref[rows, :] = tn(full[:, rows], o_ref[...]).astype(LOW)


def attend_back_kernel(
    last, group, mixed, outer_ref, grad_ref, x_ref, mine_ref, other_ref, normed_ref, vec_ref,
    wk_ref, out_ref, sums_ref, *refs,
):
    if not last:
        got_ref, *refs = refs
    weight, outer, stage, land, total, scatter_sems, local_sems, *refs = refs
    width = outer_ref.shape[1]
    section = lax.axis_index("section")
    halves = Halves((mine_ref, other_ref), weight, local_sems, 0)
    halves.start()
    sums_ref[...] = jnp.zeros_like(sums_ref)

    half = weight.shape[1] // 2

    def products():
        @pl.loop(0, weight.shape[0] // TILE)
        def _(n):
            rows = pl.ds(pl.multiple_of(n * TILE, TILE), TILE)
            if last:
                outer[rows, : 3 * width] = tn(normed_ref[:, rows], mixed[...]).astype(LOW)
                outer[rows, 3 * width :] = outer_ref[rows, :]
            else:
                outer[section, rows, :] = tn(normed_ref[:, rows], mixed[:, :half]).astype(LOW)
                outer[1 - section, rows, : 3 * width - half] = tn(
                    normed_ref[:, rows], mixed[:, half:]
                ).astype(LOW)
                outer[1 - section, rows, 3 * width - half :] = outer_ref[rows, :]

    scatter = Scatter(group, stage, land, total, scatter_sems)
    if not last:
        group.need(1, 6)
        products()
        swap = push(outer.at[1], got_ref, refs[0], 0, 1 - section, "section")
        swap.start()
    halves.wait()
    scatter.start(lambda rows: nt(mixed[rows, :], weight[:, : 3 * width]))
    if last:
        group.need(1, 6)
        products()
    store = pltpu.make_async_copy(outer if last else outer.at[0], wk_ref, local_sems.at[2])
    store.start()
    group.need(2, 3)
    sums_ref[2:3, : 3 * width] = jnp.sum(mixed[...].astype(WIDE), axis=0, keepdims=True)
    for j in range(PARTS):
        rows = slice(j * group.part, (j + 1) * group.part)
        grad = scatter.take(j)
        hat, scale = normalise(x_ref[rows, :].astype(WIDE))
        out = grad_ref[rows, :] + norm_backward(grad, hat, scale, vec_ref[0:1, :])
        out_ref[rows, :] = out.astype(LOW)
        for n, term in enumerate((grad * hat, grad)):
            sums_ref[n : n + 1, :] += jnp.sum(term, axis=0, keepdims=True)
    scatter.done()
    store.wait()
    if not last:
        swap.wait()


def finish_kernel(
    late_ref, early1_ref, early2_ref, near_ref, far_ref, a0, n0, b0, a1, n1, b1,
    grads_ref, sums_ref, got_late, got_early1, got_early2,
    mine, stage4, block, land_col, land_x, land_z, send, land,
    deliver_sems, col_sems, x_sems, z_sems, part_sems,
):
    section, row = lax.axis_index("section"), lax.axis_index("row")
    group = Group(near_ref.shape[0])
    length, width = far_ref.shape
    others = [lax.rem(row + d, land_z.shape[0]) for d in range(1, land_z.shape[0])]
    group.greet(True, True, others)
    parts = [
        push(source, into, part_sems, n, 1 - section, "section")
        for n, (source, into) in enumerate(
            ((late_ref, got_late), (early1_ref, got_early1), (early2_ref, got_early2))
        )
    ]

    @pl.when(section == 0)
    def _():
        parts[0].start()

    @pl.when(section == 1)
    def _():
        parts[1].start()
        parts[2].start()

    deliver = Deliver(group, stage4, mine, deliver_sems)
    deliver.start(near_ref)

    block[...] = jnp.zeros_like(block)
    for layer, (attn, narrow, bend) in enumerate(((a0, n0, b0), (a1, n1, b1))):
        wide = [attn[0:1, :], attn[1:2, :], narrow[3:4, :], narrow[0:1, :], narrow[1:2, :], narrow[2:3, :]]
        for c in range(block.shape[0]):
            columns = slice(c * width, (c + 1) * width)
            for n, term in enumerate(wide):
                block[c, layer, n : n + 1, :] = term[:, columns]
            for n, term in enumerate((attn[2:3, :width], attn[2:3, 2 * width : 3 * width])):
                block[c, layer, 8 + n : 9 + n, :] = term
            for n in range(bend.shape[1] // width):
                block[c, layer, 10 + n : 11 + n, :] = bend[0:1, n * width : (n + 1) * width]
    copies = [
        push(block.at[other, :, pl.ds(0, 8)], land_col.at[n], col_sems, n, other)
        for n, other in enumerate((group.peer, group.diag, group.sib))
    ]
    for copy in copies:
        copy.start()
    for copy in copies:
        copy.wait()
    me = group.me
    block[me, :, :8] = block[me, :, :8] + (land_col[0] + (land_col[1] + land_col[2]))
    swap = push(block.at[me, 1 - section], land_x, x_sems, 0, 1 - section, "section")
    swap.start()
    swap.wait()
    land_z[row] = block[me, section] + land_x[...]
    copies = [
        push(land_z.at[row], land_z.at[row], z_sems, n, other, "row")
        for n, other in enumerate(others)
    ]
    for copy in copies:
        copy.start()

    deliver.done()

    @pl.when(section == 0)
    def _():
        send[...] = far_ref[...]

    @pl.when(section == 1)
    def _():
        send[...] = mine[...]

    swap = push(send, land, x_sems, 1, 1 - section, "section")
    swap.start()
    own = pl.ds(pl.multiple_of(section * length, length), length)
    away = pl.ds(pl.multiple_of((1 - section) * length, length), length)

    @pl.when(section == 0)
    def _():
        grads_ref[own, :] = mine[...].astype(WIDE)

    @pl.when(section == 1)
    def _():
        grads_ref[own, :] = far_ref[...].astype(WIDE)

    for copy in copies:
        copy.wait()
    result = land_z[0]
    for n in range(1, land_z.shape[0]):
        result = result + land_z[n]
    sums_ref[...] = result
    swap.wait()
    grads_ref[away, :] = land[...].astype(WIDE)

    @pl.when(section == 0)
    def _():
        parts[0].wait_send()
        parts[1].wait_recv()
        parts[2].wait_recv()

    @pl.when(section == 1)
    def _():
        parts[1].wait_send()
        parts[2].wait_send()
        parts[0].wait_recv()


VM = pl.BlockSpec(memory_space=pltpu.VMEM)
ANY = pl.BlockSpec(memory_space=pl.ANY)
PAIRS = pltpu.SemaphoreType.DMA((2, 3 * PARTS))
LOCAL = pltpu.SemaphoreType.DMA((4,))


def shape(dims, kind=LOW):
    return jax.ShapeDtypeStruct(dims, kind)


def launch(
    body, number, rows, in_specs, ins, outs, out_specs, scratch, swaps=(), diagonal=False, across=False, late=(),
):
    n_in, n_out, n = len(ins), len(outs), len(swaps)
    held_in = [i for i in range(n_in) if in_specs[i] is VM]
    held_out = [i for i in range(n_out) if out_specs[i] is VM]

    def kernel(*refs):
        refs = list(refs)
        takes, sources = refs[:n_in], refs[n_in : n_in + n]
        gives = refs[n_in + n : n_in + n + n_out]
        lands = refs[n_in + n + n_out : n_in + 2 * n + n_out]
        rest = refs[n_in + 2 * n + n_out :]
        own, rest = rest[: len(scratch)], rest[len(scratch) :]
        in_held, rest = rest[: len(held_in)], rest[len(held_in) :]
        out_held, rest = rest[: len(held_out)], rest[len(held_out) :]
        in_sems, out_sems, swap_sems = rest
        group = Group(rows)
        for k, i in enumerate(held_in):
            group.loads[i] = pltpu.make_async_copy(takes[i], in_held[k], in_sems.at[k])
            group.loads[i].start()
            takes[i] = in_held[k]
        for k, i in enumerate(held_out):
            group.stores[i] = pltpu.make_async_copy(out_held[k], gives[i], out_sems.at[k])
            gives[i] = out_held[k]
        group.greet(n or across, diagonal)
        other = 1 - lax.axis_index("section")
        copies = [
            push(source, land, swap_sems, i, other, "section")
            for i, (source, land) in enumerate(zip(sources, lands))
        ]
        for copy in copies:
            copy.start()
        group.need(*[i for i in held_in if i not in late])
        body(group, *takes, *gives, *own)
        group.emit(*[i for i in held_out if i not in group.begun])
        for copy in copies:
            copy.wait()
        for i in held_out:
            group.stores[i].wait()

    results = pl.pallas_call(
        kernel,
        out_shape=(*outs, *[shape(s.shape, s.dtype) for s in swaps]),
        in_specs=[ANY] * (n_in + n),
        out_specs=(ANY,) * (n_out + n),
        scratch_shapes=[
            *scratch,
            *[pltpu.VMEM(ins[i].shape, ins[i].dtype) for i in held_in],
            *[pltpu.VMEM(outs[i].shape, outs[i].dtype) for i in held_out],
            pltpu.SemaphoreType.DMA((len(held_in),)),
            pltpu.SemaphoreType.DMA((len(held_out),)),
            pltpu.SemaphoreType.DMA((2, max(n, 1))),
        ],
        compiler_params=pltpu.CompilerParams(
            collective_id=number, has_side_effects=True, vmem_limit_bytes=GRANT
        ),
        cost_estimate=pl.CostEstimate(flops=int(3e10), bytes_accessed=30 * MEBI, transcendentals=0),
    )(*ins, *swaps)
    return results[:n_out], results[n_out:]


def start_call(number, tokens, cotangent, small, keep, sent, contract, columns, row_count):
    width = tokens.shape[1]
    size = width * columns
    kinds = small.shape[0]
    half = shape((keep.shape[0] * row_count, keep.shape[1]))
    outs = (
        shape((LENGTH, size)), shape((LENGTH, size)), shape((2, columns, kinds, width)),
        shape(sent.shape), shape(contract.shape), half, half,
    )
    blocks = pltpu.VMEM((columns, LENGTH, width), LOW)
    vectors = pltpu.VMEM((columns, kinds, width), LOW)
    many = pltpu.SemaphoreType.DMA((2, row_count))
    return pl.pallas_call(
        start_kernel,
        out_shape=outs,
        in_specs=[ANY] * 6,
        out_specs=(VM,) * 3 + (ANY,) * 4,
        scratch_shapes=[
            blocks, blocks, vectors, vectors, PAIRS, PAIRS,
            pltpu.SemaphoreType.DMA((2, 3 * PARTS + 3)), many, many, LOCAL,
        ],
        compiler_params=pltpu.CompilerParams(
            collective_id=number, has_side_effects=True, vmem_limit_bytes=GRANT
        ),
        cost_estimate=pl.CostEstimate(flops=int(3e10), bytes_accessed=30 * MEBI, transcendentals=0),
    )(tokens, cotangent, small, keep, sent, contract)


def attend_call(number, gathered, x, pair, vec, bias, rows, width, swaps):
    size = vec.shape[1]
    heads = width // HEAD
    outs = (
        shape((LENGTH, size) if not gathered else (16, 128)),
        shape((LENGTH, size)),
        shape((3 * heads, LENGTH, HEAD)),
        shape((LENGTH, width)),
        shape((8, LENGTH), WIDE),
        shape((rows, size), WIDE),
        shape((rows, size)),
    )
    scratch = [
        pltpu.VMEM((size, 4 * width), LOW),
        pltpu.VMEM((heads, LENGTH, HEAD), LOW),
        *scatter_scratch(rows, size), PAIRS, LOCAL,
    ]
    return launch(
        functools.partial(attend_kernel, gathered, heads),
        number, rows, [VM, ANY, ANY, VM, VM], (x, *pair, vec, bias), outs, (VM,) * 7, scratch, swaps,
    )


def widen_call(number, second, pair, bias, grad, swaps):
    rows, size = second.shape
    wide = bias.shape[1]
    last = grad is not None
    ins, in_specs = [second, *pair, bias], [VM, ANY, ANY, VM]
    outs = [shape((LENGTH, size)), shape((LENGTH, wide)), shape((LENGTH, wide))]
    if last:
        ins, in_specs, outs = ins + [grad], in_specs + [VM], outs + [shape((size, wide))]
    scratch = [pltpu.VMEM((size, wide), LOW), PAIRS, LOCAL]
    return launch(
        functools.partial(widen_kernel, last),
        number, rows, in_specs, ins, outs, (VM,) * len(outs), scratch, swaps, late=(4,),
    )


def contract_call(number, active, hidden, pair, vec, swaps):
    rows, size = hidden.shape
    wide = active.shape[1]
    scratch = [pltpu.VMEM((size, wide), LOW), *scatter_scratch(rows, size), LOCAL]
    return launch(
        contract_kernel, number, rows, [VM, VM, ANY, ANY, VM], (active, hidden, *pair, vec),
        [shape((rows, size))], (VM,), scratch, swaps, late=(1,),
    )


def bend_call(number, last, grad, pair, slope, extra, size, rows, swaps):
    wide = slope.shape[1]
    columns = LENGTH // rows
    outs = [shape((LENGTH, wide)), shape((8, wide), WIDE)]
    scratch = [pltpu.VMEM((size, wide), LOW), PAIRS, LOCAL]
    if last:
        outs += [shape((LENGTH, size // columns))]
        scratch += [pltpu.VMEM((columns, rows, size // columns), LOW), pltpu.SemaphoreType.DMA((2, 3))]
    else:
        outs += [shape((LENGTH, size)), *[shape((size, wide // 2))] * 2]
    return launch(
        functools.partial(bend_kernel, last),
        number, rows, [VM, ANY, ANY, VM, VM], (grad, *pair, slope, extra),
        outs, (VM,) * len(outs), scratch, swaps, last, late=(3,) if last else (3, 4),
    )


def narrow_call(number, last, before, grad_own, pair, second, hidden, vec, swaps):
    rows, size = hidden.shape
    wide = before.shape[1]
    outs = (
        shape((rows, size), WIDE),
        shape((rows, size)),
        shape((8, size), WIDE),
        shape((size, wide if last else wide // 2)),
        shape((16, 128) if last else (size, wide // 2)),
    )
    scratch = [pltpu.VMEM((size, wide), LOW), *scatter_scratch(rows, size), LOCAL]
    return launch(
        functools.partial(narrow_kernel, last),
        number, rows, [VM, VM, ANY, ANY, VM, VM, VM], (before, grad_own, *pair, second, hidden, vec),
        outs, (VM, VM, VM, VM, ANY if last else VM), scratch, swaps, late=(1, 4, 5),
    )


def scores_back_call(number, low, pair, heads_all, o, lse, swaps):
    rows, size = low.shape
    width = o.shape[1]
    heads = width // HEAD
    outs = (shape((LENGTH, 3 * width)), shape((size, width)))
    scratch = [
        pltpu.VMEM((size, 4 * width), LOW),
        pltpu.VMEM((LENGTH, size), LOW),
        pltpu.VMEM((heads, LENGTH, HEAD), LOW),
        pltpu.VMEM((8, LENGTH), WIDE),
        pltpu.VMEM((3 * heads, LENGTH, HEAD), LOW),
        pltpu.VMEM((LENGTH, HEAD), WIDE),
        pltpu.VMEM((LENGTH, HEAD), WIDE),
        PAIRS, LOCAL,
    ]
    return launch(
        functools.partial(scores_back_kernel, heads),
        number, rows, [VM, ANY, ANY, VM, VM, VM], (low, *pair, heads_all, o, lse),
        outs, (VM,) * 2, scratch, swaps, late=(3, 4, 5),
    )


def attend_back_call(number, last, mixed, outer, grad, x_own, pair, normed, vec, swaps):
    rows, size = grad.shape
    width = outer.shape[1]
    half = 2 * width
    outs = [shape((size, 2 * half if last else half)), shape((rows, size)), shape((8, size), WIDE)]
    out_specs = [ANY, VM, VM]
    scratch = [
        pltpu.VMEM((size, 4 * width), LOW),
        pltpu.VMEM((size, 2 * half) if last else (2, size, half), LOW),
        *scatter_scratch(rows, size), LOCAL,
    ]
    if not last:
        outs, out_specs = outs + [shape((size, half))], out_specs + [ANY]
        scratch += [pltpu.SemaphoreType.DMA((2, 1))]
    return launch(
        functools.partial(attend_back_kernel, last),
        number, rows, [VM, VM, VM, VM, ANY, ANY, VM, VM],
        (mixed, outer, grad, x_own, *pair, normed, vec), outs, out_specs, scratch, swaps, False, True, late=(1, 2, 3, 6),
    )


def finish_call(number, late, early1, early2, near, far, sums, row_count):
    rows, size = near.shape
    length, width = far.shape
    columns = length // rows
    outs = (
        shape((2 * length, width), WIDE),
        shape((16, width), WIDE),
        *[shape(part.shape) for part in (late, early1, early2)],
    )
    scratch = [
        pltpu.VMEM((length, width), LOW),
        pltpu.VMEM((columns, rows, width), LOW),
        pltpu.VMEM((columns, 2, 16, width), WIDE),
        pltpu.VMEM((3, 2, 8, width), WIDE),
        pltpu.VMEM((16, width), WIDE),
        pltpu.VMEM((row_count, 16, width), WIDE),
        pltpu.VMEM((length, width), LOW),
        pltpu.VMEM((length, width), LOW),
        pltpu.SemaphoreType.DMA((2, 3)),
        pltpu.SemaphoreType.DMA((2, 3)),
        pltpu.SemaphoreType.DMA((2, 2)),
        pltpu.SemaphoreType.DMA((2, row_count)),
        pltpu.SemaphoreType.DMA((2, 3)),
    ]
    return pl.pallas_call(
        finish_kernel,
        out_shape=outs,
        in_specs=[ANY] * 3 + [VM] * 8,
        out_specs=(VM, VM, ANY, ANY, ANY),
        scratch_shapes=scratch,
        compiler_params=pltpu.CompilerParams(
            collective_id=number, has_side_effects=True, vmem_limit_bytes=GRANT
        ),
        cost_estimate=pl.CostEstimate(flops=int(3e10), bytes_accessed=30 * MEBI, transcendentals=0),
    )(late, early1, early2, near, far, *sums)


def swap_sections(value):
    return lax.ppermute(value, "section", [(0, 1), (1, 0)])


def on_device(
    tokens,
    cotangent,
    first_gain,
    first_shift,
    attend_weight,
    attend_bias,
    output_weight,
    output_bias,
    second_gain,
    second_shift,
    expand_weight,
    expand_bias,
    contract_weight,
    contract_bias,
):
    section = lax.axis_index("section")
    column = lax.axis_index("col")
    first_section = section == 0
    columns = lax.axis_size("col")
    width = tokens.shape[1]
    size = width * columns
    rows = LENGTH // columns

    def pick(early, later):
        return jnp.where(first_section, early, later)

    block_rows = attend_weight.shape[1]
    units = (
        jnp.concatenate(
            [attend_weight[0].reshape(block_rows, 3 * width), output_weight[0].T], axis=1
        ),
        expand_weight[0],
        contract_weight[0].T,
    )
    kept_blocks, sent_blocks = [], []
    for unit in units:
        half = unit.shape[1] // 2
        low, high = unit[:, :half], unit[:, half:]
        kept_blocks.append(pick(low, high))
        sent_blocks.append(pick(high, low))

    small = jnp.concatenate(
        [
            first_gain,
            first_shift,
            output_bias,
            second_gain,
            second_shift,
            contract_bias,
            attend_bias[0],
            expand_bias[0].reshape(-1, width),
        ],
        0,
    )
    filled = small.shape[0]
    small = jnp.pad(small, ((0, -filled % 16), (0, 0)))
    got_expand = swap_sections(sent_blocks[1])
    sent_attend, got_expand = lax.optimization_barrier((sent_blocks[0], got_expand))
    x0_full, gy_full, vectors, got_attend, got_contract, mine, far = start_call(
        1, tokens, cotangent, small, kept_blocks[0], sent_attend, units[2], columns, lax.axis_size("row")
    )

    def gather_blocks(block):
        return lax.all_gather(block, "row", axis=0, tiled=True)

    half = units[2].shape[1] // 2
    mats = [
        [None, gather_blocks(pick(kept_blocks[1], got_expand)), None],
        [gather_blocks(pick(got_attend, kept_blocks[0])), gather_blocks(pick(got_expand, kept_blocks[1])), None],
    ]
    mats[0][2] = gather_blocks(pick(kept_blocks[2], got_contract[:, half:]))
    mats[1][2] = gather_blocks(pick(got_contract, units[2]))
    vectors = vectors.astype(WIDE)
    wide_vectors = jnp.swapaxes(vectors[:, :, :6], 1, 2).reshape(2, 6, size)
    wide_vectors = jnp.pad(wide_vectors, ((0, 0), (0, 2), (0, 0)))
    own_vectors = lax.dynamic_index_in_dim(vectors, column, 1, keepdims=False)
    attend_biases = jnp.stack(
        [own_vectors[:, 6], jnp.zeros_like(own_vectors[:, 6]), own_vectors[:, 7]], 1
    ).reshape(2, 1, 3 * width)
    expand_biases = own_vectors[:, 8:filled].reshape(2, 1, -1)

    def own_rows(full):
        return lax.dynamic_slice_in_dim(full, column * rows, rows, 0)

    def own_features(full):
        return lax.dynamic_slice_in_dim(full, column * width, width, 1)

    attn = (mine, far)
    x = x0_full
    kept, pairs = [], []
    owns = [own_rows(x0_full)]
    for layer in range(2):
        last = layer == 1
        vec = wide_vectors[layer]
        (full, normed, heads, o, lse, hidden, second_own), (other,) = attend_call(
            2 + 3 * layer, not last, x, attn, vec, attend_biases[layer], rows, width, [mats[layer][1]]
        )
        expand = (mats[layer][1], other)
        outs, others = widen_call(
            3 + 3 * layer, second_own, expand, expand_biases[layer],
            gy_full if last else None, [] if last else [mats[0][2]],
        )
        second, active, slope = outs[:3]
        contract = (mats[layer][2], mats[layer][2] if last else others[0])
        if last:
            c1 = outs[3]
        outs, others = contract_call(
            4 + 3 * layer, active, hidden, contract, vec, [] if last else [mats[1][0]]
        )
        pairs.append((attn, expand, contract))
        kept.append((normed, heads, o, lse, hidden, second, active, slope))
        x = outs[0]
        owns.append(x)
        if not last:
            attn = (mats[1][0], others[0])
    y0 = own_features(full)

    def add(keep, got, then):
        total = (keep.astype(WIDE) + got.astype(WIDE)).astype(LOW)
        return lax.optimization_barrier((total, then))

    def scatter(total):
        return lax.psum_scatter(total, "row", scatter_dimension=0, tiled=True)

    def tie(value, then):
        return lax.optimization_barrier((value, then))

    attn, expand, contract = pairs[1]
    normed, heads, o, lse, hidden, second, active, slope = kept[1]
    (before, bend_sums1, y1), _ = bend_call(8, True, gy_full, contract, slope, owns[2], size, rows, [])
    layer_low, layer_high = pick(y0, y1), pick(y1, y0)
    (grad_hidden, low, narrow_sums1, e1, _), _ = narrow_call(
        9, True, before, own_rows(gy_full), expand, second, hidden, wide_vectors[1], []
    )
    (mixed, outer), (layer_got,) = scores_back_call(10, low, attn, heads, o, lse, [layer_high])
    part_c1, mixed = tie(scatter(c1), mixed)
    (w1, gx1_own, attend_sums1), (far_c1,) = attend_back_call(
        11, True, mixed, outer, grad_hidden, owns[1], attn, normed, wide_vectors[1], [part_c1]
    )
    layer_outputs = jnp.concatenate([pick(layer_low, layer_got), pick(layer_got, layer_low)], 0)

    attn, expand, contract = pairs[0]
    normed, heads, o, lse, hidden, second, active, slope = kept[0]
    part_e1 = scatter(e1)
    (before, bend_sums0, gx1_full, ck0, cs0), (far_e1,) = bend_call(
        12, False, gx1_own, contract, slope, active, size, rows, [part_e1]
    )
    (grad_hidden, low, narrow_sums0, ek0, es0), (ct0,) = narrow_call(
        13, False, before, gx1_own, expand, second, hidden, wide_vectors[0], [cs0]
    )
    total_c0, low = add(ck0, ct0, low)
    (mixed, outer), (et0,) = scores_back_call(14, low, attn, heads, o, lse, [es0])
    total_e0, mixed = add(ek0, et0, mixed)
    part_w1, mixed = tie(scatter(w1), mixed)
    part_c0, mixed = tie(scatter(total_c0), mixed)
    (wk0, gx0_own, attend_sums0, wt0), _ = attend_back_call(
        15, False, mixed, outer, grad_hidden, owns[0], attn, normed, wide_vectors[0], []
    )
    total_w0, gx0_own = add(wk0, wt0, gx0_own)
    part_e0 = scatter(total_e0)
    input_grads, small_grads, far_w1, far_c0, far_e0 = finish_call(
        16,
        part_w1,
        part_c0,
        part_e0,
        gx0_own,
        own_features(gx1_full),
        (attend_sums0, narrow_sums0, bend_sums0, attend_sums1, narrow_sums1, bend_sums1),
        lax.axis_size("row"),
    )

    late = [part_w1, part_e1, part_c1]
    part_w0, small_grads = tie(scatter(total_w0), small_grads)
    far_w0 = lax.ppermute(part_w0, "section", [(1, 0)])

    units = []
    for late, far_late, early, far_early in (
        (part_w1, far_w1, part_w0, far_w0),
        (part_e1, far_e1, part_e0, far_e0),
        (part_c1, far_c1, part_c0, far_c0),
    ):
        whole = jnp.concatenate([early, far_early], 1).astype(WIDE)
        units.append(pick(whole, late.astype(WIDE) + far_late.astype(WIDE)))
    attn_part, expand_part, contract_part = units

    return (
        layer_outputs[None],
        input_grads[None],
        small_grads[0:1],
        small_grads[1:2],
        attn_part[:, : 3 * width].reshape(block_rows, 3, width)[None],
        small_grads[8:10][None],
        attn_part[:, 3 * width :].T[None],
        small_grads[2:3],
        small_grads[3:4],
        small_grads[4:5],
        expand_part[None],
        small_grads[10 : 10 + expand_bias.shape[1] // width].reshape(1, -1),
        contract_part.T[None],
        small_grads[5:6],
    )


def solution(mesh):
    return jax.shard_map(
        on_device,
        mesh=mesh,
        in_specs=(
            P("row", "col"),
            P("row", "col"),
            P("section", "col"),
            P("section", "col"),
            P("section", "row", None, "col"),
            P("section", None, "col"),
            P("section", "col", "row"),
            P("section", "col"),
            P("section", "col"),
            P("section", "col"),
            P("section", "row", "col"),
            P("section", "col"),
            P("section", "col", "row"),
            P("section", "col"),
        ),
        out_specs=(
            P("section", "row", "col"),
            P("section", "row", "col"),
            P("section", "col"),
            P("section", "col"),
            P("section", "row", None, "col"),
            P("section", None, "col"),
            P("section", "col", "row"),
            P("section", "col"),
            P("section", "col"),
            P("section", "col"),
            P("section", "row", "col"),
            P("section", "col"),
            P("section", "col", "row"),
            P("section", "col"),
        ),
        check_vma=False,
    )
```

```python
import functools

import jax
import jax.numpy as jnp
from jax import lax
from jax.experimental import pallas as pl
from jax.experimental.pallas import tpu as pltpu
from jax.sharding import PartitionSpec as P

HEAD = 64
LENGTH = 1024
EPS = 1e-05
LOW = jnp.bfloat16
WIDE = jnp.float32
MESH = pl.DeviceIdType.MESH
PARTS = 2
TILE = 256
MEBI = 1024 * 1024
GRANT = 58 * MEBI


def nn(left, right):
    return lax.dot_general(left, right, (((1,), (0,)), ((), ())), preferred_element_type=WIDE)


def nt(left, right):
    return lax.dot_general(left, right, (((1,), (1,)), ((), ())), preferred_element_type=WIDE)


def tn(left, right):
    return lax.dot_general(left, right, (((0,), (0,)), ((), ())), preferred_element_type=WIDE)


def normalise(values):
    center = jnp.mean(values, axis=1, keepdims=True)
    centred = values - center
    scale = lax.rsqrt(jnp.mean(centred * centred, axis=1, keepdims=True) + EPS)
    return centred * scale, scale


def norm_backward(grad, hat, scale, gain):
    scaled = grad * gain
    mean_one = jnp.mean(scaled, axis=1, keepdims=True)
    mean_two = jnp.mean(scaled * hat, axis=1, keepdims=True)
    return scale * (scaled - mean_one - hat * mean_two)


class Group:
    def __init__(self, rows):
        self.me = lax.axis_index("col")
        chip, core = self.me // 2, self.me % 2
        self.sib = chip * 2 + 1 - core
        self.peer = (1 - chip) * 2 + core
        self.diag = (1 - chip) * 2 + 1 - core
        self.rows = rows
        self.part = rows // PARTS
        self.loads, self.stores, self.begun = {}, {}, set()

    def need(self, *places):
        for place in places:
            self.loads[place].wait()

    def emit(self, *places):
        for place in places:
            self.stores[place].start()
            self.begun.add(place)

    def greet(self, swaps, diagonal, rows=()):
        barrier = pltpu.get_barrier_semaphore()
        others = [{"col": self.sib}, {"col": self.peer}]
        if diagonal:
            others.append({"col": self.diag})
        if swaps:
            others.append({"section": 1 - lax.axis_index("section")})
        others += [{"row": row} for row in rows]
        for other in others:
            pl.semaphore_signal(barrier, inc=1, device_id=other, device_id_type=MESH)
        pl.semaphore_wait(barrier, len(others))

    def slab(self, owner, j):
        return pl.ds(pl.multiple_of(owner * self.rows + j * self.part, self.part), self.part)

    def chunk(self, owner):
        return pl.ds(pl.multiple_of(owner * self.rows, self.rows), self.rows)


def push(src, dst, sems, slot, target, axis="col"):
    return pltpu.make_async_remote_copy(
        src_ref=src,
        dst_ref=dst,
        send_sem=sems.at[0, slot],
        recv_sem=sems.at[1, slot],
        device_id={axis: target},
        device_id_type=MESH,
    )


class Gather:
    def __init__(self, group, full, sems, blocks=False):
        self.group, self.full, self.sems, self.blocks = group, full, sems, blocks

    def piece(self, owner, j):
        if not self.blocks:
            return self.full.at[self.group.slab(owner, j)]
        part = self.full.shape[1] // PARTS
        return self.full.at[owner, pl.ds(j * part, part)]

    def start(self):
        g = self.group
        self.over, self.near, self.relayed = [], [], []
        for j in range(PARTS):
            piece = self.piece(g.me, j)
            self.over.append(push(piece, piece, self.sems, j, g.peer))
            self.over[-1].start()
        for j in range(PARTS):
            piece = self.piece(g.me, j)
            self.near.append(push(piece, piece, self.sems, PARTS + j, g.sib))
            self.near[-1].start()

    def sibling(self):
        for copy in self.near:
            copy.wait_recv()

    def relay(self):
        g = self.group
        for j in range(PARTS):
            self.over[j].wait_recv()
            piece = self.piece(g.peer, j)
            self.relayed.append(push(piece, piece, self.sems, 2 * PARTS + j, g.sib))
            self.relayed[-1].start()

    def diagonal(self):
        for copy in self.relayed:
            copy.wait_recv()

    def done(self):
        for copy in self.over + self.near + self.relayed:
            copy.wait_send()

    def each(self, body, first=None):
        g = self.group
        self.start()
        if first is not None:
            first()
        body(g.chunk(g.me))
        self.sibling()
        body(g.chunk(g.sib))
        self.relay()
        body(g.chunk(g.peer))
        self.diagonal()
        body(g.chunk(g.diag))
        self.done()


class Scatter:
    def __init__(self, group, stage, land, total, sems):
        self.group, self.stage, self.land, self.total, self.sems = group, stage, land, total, sems

    def start(self, part):
        g, stage, land = self.group, self.stage, self.land
        self.first, self.over, self.near = [], [], []
        def split(owner):
            whole = part(g.chunk(owner))
            return [whole[j * g.part : (j + 1) * g.part] for j in range(PARTS)]

        for j, mine in enumerate(split(g.diag)):
            stage[0, j] = mine.astype(LOW)
            self.first.append(push(stage.at[0, j], land.at[0, j], self.sems, j, g.sib))
            self.first[-1].start()
        for j, mine in enumerate(split(g.peer)):
            self.first[j].wait_recv()
            stage[1, j] = (mine + land[0, j].astype(WIDE)).astype(LOW)
            self.over.append(push(stage.at[1, j], land.at[1, j], self.sems, PARTS + j, g.peer))
            self.over[-1].start()
        for j, mine in enumerate(split(g.sib)):
            stage[2, j] = mine.astype(LOW)
            self.near.append(push(stage.at[2, j], land.at[2, j], self.sems, 2 * PARTS + j, g.sib))
            self.near[-1].start()
        for j, mine in enumerate(split(g.me)):
            self.total[j] = mine

    def take(self, j):
        self.near[j].wait_recv()
        self.over[j].wait_recv()
        land = self.land
        return self.total[j] + (land[1, j].astype(WIDE) + land[2, j].astype(WIDE))

    def done(self):
        for copy in self.first + self.over + self.near:
            copy.wait_send()


class Deliver:
    def __init__(self, group, stage, out, sems):
        self.group, self.stage, self.out, self.sems = group, stage, out, sems

    def start(self, rows_ref):
        g, width = self.group, self.out.shape[1]
        for c in range(self.stage.shape[0]):
            self.stage[c] = rows_ref[:, c * width : (c + 1) * width]
        place = self.out.at[g.chunk(g.me)]
        self.copies = [
            push(self.stage.at[other], place, self.sems, n, other)
            for n, other in enumerate((g.peer, g.diag, g.sib))
        ]
        for copy in self.copies:
            copy.start()
        self.out[g.chunk(g.me), :] = self.stage[g.me]

    def done(self):
        for copy in self.copies:
            copy.wait()


def scatter_scratch(rows, width):
    part = rows // PARTS
    return [
        pltpu.VMEM((3, PARTS, part, width), LOW),
        pltpu.VMEM((3, PARTS, part, width), LOW),
        pltpu.VMEM((PARTS, part, width), WIDE),
        pltpu.SemaphoreType.DMA((2, 3 * PARTS)),
    ]


class Halves:
    def __init__(self, pair, whole, sems, slot):
        if pair[0].shape[1] == whole.shape[1]:
            self.copies = [pltpu.make_async_copy(pair[0], whole, sems.at[slot])]
            return
        section = lax.axis_index("section")
        half = whole.shape[1] // 2
        self.copies = []
        for n, place in enumerate((section, 1 - section)):
            columns = pl.ds(pl.multiple_of(place * half, half), half)
            self.copies.append(
                pltpu.make_async_copy(pair[n], whole.at[:, columns], sems.at[slot + n])
            )

    def start(self):
        for copy in self.copies:
            copy.start()

    def wait(self):
        for copy in self.copies:
            copy.wait()


def add_into(keep_ref, got_ref):
    @pl.loop(0, keep_ref.shape[0] // TILE)
    def _(n):
        rows = pl.ds(pl.multiple_of(n * TILE, TILE), TILE)
        keep_ref[rows, :] = (keep_ref[rows, :].astype(WIDE) + got_ref[rows, :].astype(WIDE)).astype(LOW)


def attention_out(heads_ref, o3, lse_ref, heads):
    length = heads_ref.shape[1]
    size = min(TILE, length)

    @pl.loop(0, heads)
    def _(h):
        for i in range(length // size):
            rows = slice(i * size, (i + 1) * size)
            finish = (i + 1) * size
            queries = heads_ref[h, rows, :]
            scores = nt(heads_ref[heads + h, :finish, :], queries)
            keep = lax.broadcasted_iota(jnp.int32, (size, size), 0) <= lax.broadcasted_iota(
                jnp.int32, (size, size), 1
            )
            last = jnp.where(keep, scores[finish - size :], -1000000000.0)
            scores = last if i == 0 else jnp.concatenate([scores[: finish - size], last], 0)
            highest = jnp.max(scores, axis=0, keepdims=True)
            powers = jnp.exp(scores - highest)
            summed = jnp.sum(powers, axis=0, keepdims=True)
            mixed = tn(heads_ref[2 * heads + h, :finish, :], powers.astype(LOW))
            o3[h, rows, :] = (mixed / summed).T.astype(LOW)
            lse_ref[pl.ds(h, 1), rows] = highest + jnp.log(summed)


def attention_back(heads_ref, go3, lse_ref, dots_ref, g3, key_acc, value_acc, heads):
    length = heads_ref.shape[1]
    size = min(TILE, length)

    @pl.loop(0, heads)
    def _(h):
        for i in reversed(range(length // size)):
            rows = slice(i * size, (i + 1) * size)
            finish = (i + 1) * size
            queries = heads_ref[h, rows, :]
            keys = heads_ref[heads + h, :finish, :]
            grads = go3[h, rows, :]
            scores = nt(keys, queries) - lse_ref[pl.ds(h, 1), rows]
            keep = lax.broadcasted_iota(jnp.int32, (size, size), 0) <= lax.broadcasted_iota(
                jnp.int32, (size, size), 1
            )
            last = jnp.where(keep, scores[finish - size :], -1000000000.0)
            scores = last if i == 0 else jnp.concatenate([scores[: finish - size], last], 0)
            probs = jnp.exp(scores)
            grad_probs = nt(heads_ref[2 * heads + h, :finish, :], grads)
            grad_scores = (probs * (grad_probs - dots_ref[pl.ds(h, 1), rows])).astype(LOW)
            g3[h, rows, :] = (tn(grad_scores, keys) * HEAD ** (-0.5)).astype(LOW)
            key_part = nn(grad_scores, queries)
            value_part = nn(probs.astype(LOW), grads)
            if finish == length:
                key_acc[...] = key_part
                value_acc[...] = value_part
            else:
                key_acc[:finish, :] += key_part
                value_acc[:finish, :] += value_part
        g3[heads + h] = key_acc[...].astype(LOW)
        g3[2 * heads + h] = value_acc[...].astype(LOW)


def start_kernel(
    tokens_ref, cotangent_ref, small_ref, expand_ref, contract_ref,
    x_ref, g_ref, vectors_ref, got_expand_ref, got_contract_ref,
    x4, g4, s4, other4, x_sems, g_sems, s_sems, local_sems,
):
    section = lax.axis_index("section")
    group = Group(x_ref.shape[0] // 4)
    length = x_ref.shape[0]
    loads = []
    rows = pl.ds(pl.multiple_of(section * length, length), length)
    for n, (source, into) in enumerate(((tokens_ref.at[rows], x4), (cotangent_ref.at[rows], g4), (small_ref, s4))):
        loads.append(pltpu.make_async_copy(source, into.at[group.me], local_sems.at[n]))
        loads[-1].start()
    group.greet(True, False)
    blocks = [
        push(source, into, s_sems, 3 * PARTS + 1 + n, 1 - section, "section")
        for n, (source, into) in enumerate(((expand_ref, got_expand_ref), (contract_ref, got_contract_ref)))
    ]
    for block in blocks:
        block.start()
    gathers = [Gather(group, x4, x_sems, True), Gather(group, s4, s_sems, True), Gather(group, g4, g_sems, True)]
    for gather, load in zip(gathers, (loads[0], loads[2], loads[1])):
        load.wait()
        gather.start()
    for gather in gathers:
        gather.sibling()
        gather.relay()
        gather.diagonal()
    swap = push(s4, other4, s_sems, 3 * PARTS, 1 - section, "section")
    swap.start()
    width = x4.shape[2]
    for c in range(x4.shape[0]):
        x_ref[:, c * width : (c + 1) * width] = x4[c]
        g_ref[:, c * width : (c + 1) * width] = g4[c]
    swap.wait()
    for block in blocks:
        block.wait()
    vectors_ref[section] = s4[...]
    vectors_ref[1 - section] = other4[...]
    for gather in gathers:
        gather.done()


def attend_kernel(
    gathered, heads, group, x_ref, mine_ref, other_ref, vec_ref, bias_ref,
    full_ref, normed_ref, heads_ref, o_ref, lse_ref, hidden_ref, second_ref,
    weight, o3, stage, land, total, scatter_sems, gather_sems, local_sems,
):
    width = o_ref.shape[1]
    halves = Halves((mine_ref, other_ref), weight, local_sems, 0)
    halves.start()
    if not gathered:
        full_ref[group.chunk(group.me), :] = x_ref[...]
    halves.wait()

    def project(rows):
        values = (x_ref if gathered else full_ref)[rows, :].astype(WIDE)
        hat, _ = normalise(values)
        normed = (hat * vec_ref[0:1, :] + vec_ref[1:2, :]).astype(LOW)
        normed_ref[rows, :] = normed
        mixed = nn(normed, weight[:, : 3 * width]) + bias_ref[...]
        for j in range(3 * heads):
            piece = mixed[:, j * HEAD : (j + 1) * HEAD]
            if j < heads:
                piece = piece * HEAD ** (-0.5)
            heads_ref[j, rows, :] = piece.astype(LOW)

    if gathered:
        full_ref[...] = jnp.zeros_like(full_ref)

        @pl.loop(0, LENGTH // group.rows)
        def _(n):
            project(group.chunk(n))
    else:
        Gather(group, full_ref, gather_sems).each(project)
    group.emit(0, 1, 2)

    attention_out(heads_ref, o3, lse_ref, heads)
    for h in range(heads):
        o_ref[:, h * HEAD : (h + 1) * HEAD] = o3[h]
    group.emit(3, 4)

    scatter = Scatter(group, stage, land, total, scatter_sems)
    scatter.start(lambda rows: nt(o_ref[rows, :], weight[:, 3 * width :]))
    for j in range(PARTS):
        rows = slice(j * group.part, (j + 1) * group.part)
        residual = (x_ref if gathered else full_ref)[group.slab(group.me, j), :].astype(WIDE)
        hidden = residual + scatter.take(j) + vec_ref[2:3, :]
        hidden_ref[rows, :] = hidden
        hat, _ = normalise(hidden)
        second_ref[rows, :] = (hat * vec_ref[3:4, :] + vec_ref[4:5, :]).astype(LOW)
    scatter.done()


def outer_whole(left_ref, right_ref, out_ref):
    @pl.loop(0, left_ref.shape[1] // TILE)
    def _(n):
        rows = pl.ds(pl.multiple_of(n * TILE, TILE), TILE)
        out_ref[rows, :] = tn(left_ref[:, rows], right_ref[...]).astype(LOW)


def widen_kernel(last, group, second_ref, em_ref, eo_ref, bias_ref, *refs):
    if last:
        g_ref, *refs = refs
    full_ref, active_ref, slope_ref, *refs = refs
    if last:
        c_ref, *refs = refs
    expand, gather_sems, local_sems = refs
    halves = Halves((em_ref, eo_ref), expand, local_sems, 0)
    halves.start()
    full_ref[group.chunk(group.me), :] = second_ref[...]
    halves.wait()

    def widen(rows):
        t = nn(full_ref[rows, :], expand[...]) + bias_ref[...]
        square = t * t
        bent = jnp.tanh(0.7978845608028654 * t * (1.0 + 0.044715 * square))
        active_ref[rows, :] = (0.5 * t * (1.0 + bent)).astype(LOW)
        slope_ref[rows, :] = (
            0.5 * (1.0 + bent)
            + (0.5 * 0.7978845608028654) * t * (1.0 - bent * bent) * (1.0 + 3 * 0.044715 * square)
        ).astype(LOW)

    Gather(group, full_ref, gather_sems).each(widen)
    if last:
        group.emit(0, 1, 2)
        group.need(4)
        outer_whole(g_ref, active_ref, c_ref)


def outer_halves(left_ref, right_ref, keep_ref, send_ref):
    section = lax.axis_index("section")
    half = right_ref.shape[1] // 2
    for place, out in ((section, keep_ref), (1 - section, send_ref)):
        columns = pl.ds(pl.multiple_of(place * half, half), half)

        @pl.loop(0, left_ref.shape[1] // TILE)
        def _(n):
            rows = pl.ds(pl.multiple_of(n * TILE, TILE), TILE)
            out[rows, :] = tn(left_ref[:, rows], right_ref[:, columns]).astype(LOW)


def contract_kernel(
    group, active_ref, hidden_ref, cm_ref, co_ref, vec_ref, result_ref,
    contract, stage, land, total, scatter_sems, local_sems,
):
    halves = Halves((cm_ref, co_ref), contract, local_sems, 0)
    halves.start()
    halves.wait()
    scatter = Scatter(group, stage, land, total, scatter_sems)
    scatter.start(lambda rows: nt(active_ref[rows, :], contract[...]))
    group.need(1)
    for j in range(PARTS):
        rows = slice(j * group.part, (j + 1) * group.part)
        result = hidden_ref[rows, :] + scatter.take(j) + vec_ref[5:6, :]
        result_ref[rows, :] = result.astype(LOW)
    scatter.done()


def expand_back_kernel(
    last, group, g_ref, cm_ref, co_ref, em_ref, eo_ref, slope_ref, extra_ref, second_ref, hidden_ref, vec_ref, *refs
):
    grad_ref, low_ref, sums_ref, ek_ref, *refs = refs
    if last:
        full_ref = g_ref
        out_ref, *refs = refs
    else:
        es_ref, full_ref, c_ref, *refs = refs
    contract, expand, before, stage, land, total, scatter_sems, gather_sems, local_sems, *refs = refs
    first = Halves((cm_ref, co_ref), contract, local_sems, 0)
    then = Halves((em_ref, eo_ref), expand, local_sems, 2)
    first.start()
    then.start()
    sums_ref[...] = jnp.zeros_like(sums_ref)
    if last:
        stage4, deliver_sems = refs
        deliver = Deliver(group, stage4, out_ref, deliver_sems)
        group.need(6)
        deliver.start(extra_ref)
    else:
        outer, got, swap_sems = refs
        full_ref[group.chunk(group.me), :] = g_ref[...]
    first.wait()

    def bend(rows):
        grad = (nn(full_ref[rows, :], contract[...]) * slope_ref[rows, :].astype(WIDE)).astype(LOW)
        before[rows, :] = grad
        sums_ref[4:5, :] += jnp.sum(grad.astype(WIDE), axis=0, keepdims=True)

    if last:
        group.need(5)

        @pl.loop(0, LENGTH // group.rows)
        def _(n):
            bend(group.chunk(n))

        deliver.done()
    else:
        Gather(group, full_ref, gather_sems).each(bend, lambda: group.need(5))
        group.emit(5)
    then.wait()
    scatter = Scatter(group, stage, land, total, scatter_sems)
    scatter.start(lambda rows: nt(before[rows, :], expand[...]))
    if last:
        group.need(7)
        outer_whole(second_ref, before, ek_ref)
        group.emit(3)
    else:
        group.need(6)
        outer_halves(full_ref, extra_ref, outer.at[0], outer.at[1])
        swap = push(outer.at[1], got, swap_sems, 0, 1 - lax.axis_index("section"), "section")
        swap.start()
        group.need(7)
        outer_halves(second_ref, before, ek_ref, es_ref)
        group.emit(3, 4)
    group.need(8)
    for j in range(PARTS):
        rows = slice(j * group.part, (j + 1) * group.part)
        grad = scatter.take(j)
        hat, scale = normalise(hidden_ref[rows, :])
        own = full_ref[group.slab(group.me, j), :].astype(WIDE)
        out = own + norm_backward(grad, hat, scale, vec_ref[3:4, :])
        grad_ref[rows, :] = out
        low_ref[rows, :] = out.astype(LOW)
        for n, term in enumerate((grad * hat, grad, own, out)):
            sums_ref[n : n + 1, :] += jnp.sum(term, axis=0, keepdims=True)
    group.emit(0, 1, 2)
    scatter.done()
    if not last:
        swap.wait()
        add_into(outer.at[0], got)
        store = pltpu.make_async_copy(outer.at[0], c_ref, local_sems.at[0])
        store.start()
        store.wait()


def scores_back(group, heads, low_ref, weight, heads_ref, o_ref, lse_ref, full, go3, dots, g3, accs, mixed, gather_sems, needs):
    width = o_ref.shape[1]
    picks = (
        lax.broadcasted_iota(jnp.int32, (8, width), 1) // HEAD
        == lax.broadcasted_iota(jnp.int32, (8, width), 0)
    ).astype(WIDE)

    def spread(rows):
        grads = nn(full[rows, :], weight[:, 3 * width :]).astype(LOW)
        for h in range(heads):
            go3[h, rows, :] = grads[:, h * HEAD : (h + 1) * HEAD]
        term = grads.astype(WIDE) * o_ref[rows, :].astype(WIDE)
        dots[:, rows] = lax.dot_general(
            picks,
            term,
            (((1,), (1,)), ((), ())),
            precision=lax.Precision.HIGHEST,
            preferred_element_type=WIDE,
        )

    full[group.chunk(group.me), :] = low_ref[...]
    Gather(group, full, gather_sems).each(spread, lambda: group.need(needs[0]))
    group.need(*needs[1:])
    attention_back(heads_ref, go3, lse_ref, dots, g3, *accs, heads)
    for j in range(3 * heads):
        mixed[:, j * HEAD : (j + 1) * HEAD] = g3[j]


def outer_out(full, o_ref, outer_ref):
    @pl.loop(0, outer_ref.shape[0] // TILE)
    def _(n):
        rows = pl.ds(pl.multiple_of(n * TILE, TILE), TILE)
        outer_ref[rows, :] = tn(full[:, rows], o_ref[...]).astype(LOW)


def attend_grads(group, scatter, x_ref, grad_ref, vec_ref, mixed, width, out_ref, sums_ref):
    sums_ref[2:3, : 3 * width] = jnp.sum(mixed[...].astype(WIDE), axis=0, keepdims=True)
    for j in range(PARTS):
        rows = slice(j * group.part, (j + 1) * group.part)
        grad = scatter.take(j)
        hat, scale = normalise(x_ref[rows, :].astype(WIDE))
        out = grad_ref[rows, :] + norm_backward(grad, hat, scale, vec_ref[0:1, :])
        out_ref[rows, :] = out.astype(LOW)
        for n, term in enumerate((grad * hat, grad)):
            sums_ref[n : n + 1, :] += jnp.sum(term, axis=0, keepdims=True)


def late_attend_kernel(
    heads, group, low_ref, grad_ref, x_ref, mine_ref, other_ref, normed_ref, heads_ref, o_ref, lse_ref, vec_ref,
    out_ref, sums_ref, w_ref,
    weight, full, go3, dots, g3, key_acc, value_acc, mixed, outer, outer_o,
    stage, land, total, scatter_sems, gather_sems, local_sems,
):
    width = o_ref.shape[1]
    halves = Halves((mine_ref, other_ref), weight, local_sems, 0)
    halves.start()
    sums_ref[...] = jnp.zeros_like(sums_ref)
    halves.wait()
    scores_back(
        group, heads, low_ref, weight, heads_ref, o_ref, lse_ref, full, go3, dots, g3,
        (key_acc, value_acc), mixed, gather_sems, (7, 6, 8),
    )
    scatter = Scatter(group, stage, land, total, scatter_sems)
    scatter.start(lambda rows: nt(mixed[rows, :], weight[:, : 3 * width]))
    outer_out(full, o_ref, outer_o)
    group.need(5)

    @pl.loop(0, weight.shape[0] // TILE)
    def _(n):
        rows = pl.ds(pl.multiple_of(n * TILE, TILE), TILE)
        outer[rows, : 3 * width] = tn(normed_ref[:, rows], mixed[...]).astype(LOW)
        outer[rows, 3 * width :] = outer_o[rows, :]

    store = pltpu.make_async_copy(outer, w_ref, local_sems.at[2])
    store.start()
    group.need(1, 2)
    attend_grads(group, scatter, x_ref, grad_ref, vec_ref, mixed, width, out_ref, sums_ref)
    scatter.done()
    store.wait()


def scores_back_kernel(
    heads, group, low_ref, mine_ref, other_ref, heads_ref, o_ref, lse_ref, ek_ref, es_ref,
    mixed, outer_ref, e_ref,
    weight, full, go3, dots, g3, key_acc, value_acc, got, gather_sems, local_sems, swap_sems,
):
    swap = push(es_ref, got, swap_sems, 0, 1 - lax.axis_index("section"), "section")
    swap.start()
    halves = Halves((mine_ref, other_ref), weight, local_sems, 0)
    halves.start()
    halves.wait()
    scores_back(
        group, heads, low_ref, weight, heads_ref, o_ref, lse_ref, full, go3, dots, g3,
        (key_acc, value_acc), mixed, gather_sems, (4, 3, 5),
    )
    group.emit(0)
    outer_out(full, o_ref, outer_ref)
    group.emit(1)
    group.need(6)
    swap.wait()
    add_into(ek_ref, got)
    store = pltpu.make_async_copy(ek_ref, e_ref, local_sems.at[0])
    store.start()
    store.wait()


def attend_back_kernel(
    group, mixed, outer_ref, grad_ref, x_ref, mine_ref, other_ref, normed_ref, vec_ref,
    w_ref, out_ref, sums_ref,
    weight, outer, got, stage, land, total, scatter_sems, local_sems, swap_sems,
):
    width = outer_ref.shape[1]
    section = lax.axis_index("section")
    halves = Halves((mine_ref, other_ref), weight, local_sems, 0)
    halves.start()
    sums_ref[...] = jnp.zeros_like(sums_ref)
    half = weight.shape[1] // 2
    scatter = Scatter(group, stage, land, total, scatter_sems)
    group.need(1, 6)

    @pl.loop(0, weight.shape[0] // TILE)
    def _(n):
        rows = pl.ds(pl.multiple_of(n * TILE, TILE), TILE)
        outer[section, rows, :] = tn(normed_ref[:, rows], mixed[:, :half]).astype(LOW)
        outer[1 - section, rows, : 3 * width - half] = tn(
            normed_ref[:, rows], mixed[:, half:]
        ).astype(LOW)
        outer[1 - section, rows, 3 * width - half :] = outer_ref[rows, :]

    swap = push(outer.at[1], got, swap_sems, 0, 1 - section, "section")
    swap.start()
    halves.wait()
    scatter.start(lambda rows: nt(mixed[rows, :], weight[:, : 3 * width]))
    group.need(2, 3)
    attend_grads(group, scatter, x_ref, grad_ref, vec_ref, mixed, width, out_ref, sums_ref)
    group.emit(1, 2)
    scatter.done()
    swap.wait()
    add_into(outer.at[0], got)
    store = pltpu.make_async_copy(outer.at[0], w_ref, local_sems.at[2])
    store.start()
    store.wait()


def finish_kernel(
    late_ref, early1_ref, early2_ref, near_ref, far_ref, a0, n0, a1, n1,
    grads_ref, sums_ref, got_late, got_early1, got_early2,
    mine, stage4, block, land_col, land_x, land_z, send, land,
    deliver_sems, col_sems, x_sems, z_sems, part_sems,
):
    section, row = lax.axis_index("section"), lax.axis_index("row")
    group = Group(near_ref.shape[0])
    length, width = far_ref.shape
    others = [lax.rem(row + d, land_z.shape[0]) for d in range(1, land_z.shape[0])]
    group.greet(True, True, others)
    parts = [
        push(source, into, part_sems, n, 1 - section, "section")
        for n, (source, into) in enumerate(
            ((late_ref, got_late), (early1_ref, got_early1), (early2_ref, got_early2))
        )
    ]

    @pl.when(section == 0)
    def _():
        parts[0].start()

    @pl.when(section == 1)
    def _():
        parts[1].start()
        parts[2].start()

    deliver = Deliver(group, stage4, mine, deliver_sems)
    deliver.start(near_ref)

    block[...] = jnp.zeros_like(block)
    for layer, (attn, narrow) in enumerate(((a0, n0), (a1, n1))):
        wide = [attn[0:1, :], attn[1:2, :], narrow[3:4, :], narrow[0:1, :], narrow[1:2, :], narrow[2:3, :]]
        for c in range(block.shape[0]):
            columns = slice(c * width, (c + 1) * width)
            for n, term in enumerate(wide):
                block[c, layer, n : n + 1, :] = term[:, columns]
            for n, term in enumerate((attn[2:3, :width], attn[2:3, 2 * width : 3 * width])):
                block[c, layer, 8 + n : 9 + n, :] = term
            for n in range(narrow.shape[1] // width):
                block[c, layer, 10 + n : 11 + n, :] = narrow[4:5, n * width : (n + 1) * width]
    copies = [
        push(block.at[other, :, pl.ds(0, 8)], land_col.at[n], col_sems, n, other)
        for n, other in enumerate((group.peer, group.diag, group.sib))
    ]
    for copy in copies:
        copy.start()
    for copy in copies:
        copy.wait()
    me = group.me
    block[me, :, :8] = block[me, :, :8] + (land_col[0] + (land_col[1] + land_col[2]))
    swap = push(block.at[me, 1 - section], land_x, x_sems, 0, 1 - section, "section")
    swap.start()
    swap.wait()
    land_z[row] = block[me, section] + land_x[...]
    copies = [
        push(land_z.at[row], land_z.at[row], z_sems, n, other, "row")
        for n, other in enumerate(others)
    ]
    for copy in copies:
        copy.start()

    deliver.done()

    @pl.when(section == 0)
    def _():
        send[...] = far_ref[...]

    @pl.when(section == 1)
    def _():
        send[...] = mine[...]

    swap = push(send, land, x_sems, 1, 1 - section, "section")
    swap.start()
    own = pl.ds(pl.multiple_of(section * length, length), length)
    away = pl.ds(pl.multiple_of((1 - section) * length, length), length)

    @pl.when(section == 0)
    def _():
        grads_ref[own, :] = mine[...].astype(WIDE)

    @pl.when(section == 1)
    def _():
        grads_ref[own, :] = far_ref[...].astype(WIDE)

    for copy in copies:
        copy.wait()
    result = land_z[0]
    for n in range(1, land_z.shape[0]):
        result = result + land_z[n]
    sums_ref[...] = result
    swap.wait()
    grads_ref[away, :] = land[...].astype(WIDE)

    @pl.when(section == 0)
    def _():
        parts[0].wait_send()
        parts[1].wait_recv()
        parts[2].wait_recv()

    @pl.when(section == 1)
    def _():
        parts[1].wait_send()
        parts[2].wait_send()
        parts[0].wait_recv()


VM = pl.BlockSpec(memory_space=pltpu.VMEM)
ANY = pl.BlockSpec(memory_space=pl.ANY)
PAIRS = pltpu.SemaphoreType.DMA((2, 3 * PARTS))
LOCAL = pltpu.SemaphoreType.DMA((4,))


def shape(dims, kind=LOW):
    return jax.ShapeDtypeStruct(dims, kind)


def launch(
    body, number, rows, in_specs, ins, outs, out_specs, scratch, swaps=(), diagonal=False, across=False, late=(),
):
    n_in, n_out, n = len(ins), len(outs), len(swaps)
    held_in = [i for i in range(n_in) if in_specs[i] is VM]
    held_out = [i for i in range(n_out) if out_specs[i] is VM]

    def kernel(*refs):
        refs = list(refs)
        takes, sources = refs[:n_in], refs[n_in : n_in + n]
        gives = refs[n_in + n : n_in + n + n_out]
        lands = refs[n_in + n + n_out : n_in + 2 * n + n_out]
        rest = refs[n_in + 2 * n + n_out :]
        own, rest = rest[: len(scratch)], rest[len(scratch) :]
        in_held, rest = rest[: len(held_in)], rest[len(held_in) :]
        out_held, rest = rest[: len(held_out)], rest[len(held_out) :]
        in_sems, out_sems, swap_sems = rest
        group = Group(rows)
        for k, i in enumerate(held_in):
            group.loads[i] = pltpu.make_async_copy(takes[i], in_held[k], in_sems.at[k])
            group.loads[i].start()
            takes[i] = in_held[k]
        for k, i in enumerate(held_out):
            group.stores[i] = pltpu.make_async_copy(out_held[k], gives[i], out_sems.at[k])
            gives[i] = out_held[k]
        group.greet(n or across, diagonal)
        other = 1 - lax.axis_index("section")
        copies = [
            push(source, land, swap_sems, i, other, "section")
            for i, (source, land) in enumerate(zip(sources, lands))
        ]
        for copy in copies:
            copy.start()
        group.need(*[i for i in held_in if i not in late])
        body(group, *takes, *gives, *own)
        group.emit(*[i for i in held_out if i not in group.begun])
        for copy in copies:
            copy.wait()
        for i in held_out:
            group.stores[i].wait()

    results = pl.pallas_call(
        kernel,
        out_shape=(*outs, *[shape(s.shape, s.dtype) for s in swaps]),
        in_specs=[ANY] * (n_in + n),
        out_specs=(ANY,) * (n_out + n),
        scratch_shapes=[
            *scratch,
            *[pltpu.VMEM(ins[i].shape, ins[i].dtype) for i in held_in],
            *[pltpu.VMEM(outs[i].shape, outs[i].dtype) for i in held_out],
            pltpu.SemaphoreType.DMA((len(held_in),)),
            pltpu.SemaphoreType.DMA((len(held_out),)),
            pltpu.SemaphoreType.DMA((2, max(n, 1))),
        ],
        compiler_params=pltpu.CompilerParams(
            collective_id=number, has_side_effects=True, vmem_limit_bytes=GRANT
        ),
        cost_estimate=pl.CostEstimate(flops=int(3e10), bytes_accessed=30 * MEBI, transcendentals=0),
    )(*ins, *swaps)
    return results[:n_out], results[n_out:]


def start_call(number, tokens, cotangent, small, expand, contract, columns):
    width = tokens.shape[1]
    size = width * columns
    kinds = small.shape[0]
    outs = (shape((LENGTH, size)), shape((LENGTH, size)), shape((2, columns, kinds, width)), shape(expand.shape), shape(contract.shape))
    blocks = pltpu.VMEM((columns, LENGTH, width), LOW)
    vectors = pltpu.VMEM((columns, kinds, width), LOW)
    return pl.pallas_call(
        start_kernel,
        out_shape=outs,
        in_specs=[ANY] * 5,
        out_specs=(VM, VM, VM, ANY, ANY),
        scratch_shapes=[
            blocks, blocks, vectors, vectors, PAIRS, PAIRS,
            pltpu.SemaphoreType.DMA((2, 3 * PARTS + 3)), LOCAL,
        ],
        compiler_params=pltpu.CompilerParams(
            collective_id=number, has_side_effects=True, vmem_limit_bytes=GRANT
        ),
        cost_estimate=pl.CostEstimate(flops=int(3e10), bytes_accessed=30 * MEBI, transcendentals=0),
    )(tokens, cotangent, small, expand, contract)


def attend_call(number, gathered, x, pair, vec, bias, rows, width, swaps):
    size = vec.shape[1]
    heads = width // HEAD
    outs = (
        shape((LENGTH, size) if not gathered else (16, 128)),
        shape((LENGTH, size)),
        shape((3 * heads, LENGTH, HEAD)),
        shape((LENGTH, width)),
        shape((8, LENGTH), WIDE),
        shape((rows, size), WIDE),
        shape((rows, size)),
    )
    scratch = [
        pltpu.VMEM((size, 4 * width), LOW),
        pltpu.VMEM((heads, LENGTH, HEAD), LOW),
        *scatter_scratch(rows, size), PAIRS, LOCAL,
    ]
    return launch(
        functools.partial(attend_kernel, gathered, heads),
        number, rows, [VM, ANY, ANY, VM, VM], (x, *pair, vec, bias), outs, (VM,) * 7, scratch, swaps,
    )


def widen_call(number, second, pair, bias, grad, swaps):
    rows, size = second.shape
    wide = bias.shape[1]
    last = grad is not None
    ins, in_specs = [second, *pair, bias], [VM, ANY, ANY, VM]
    outs = [shape((LENGTH, size)), shape((LENGTH, wide)), shape((LENGTH, wide))]
    if last:
        ins, in_specs, outs = ins + [grad], in_specs + [VM], outs + [shape((size, wide))]
    scratch = [pltpu.VMEM((size, wide), LOW), PAIRS, LOCAL]
    return launch(
        functools.partial(widen_kernel, last),
        number, rows, in_specs, ins, outs, (VM,) * len(outs), scratch, swaps, late=(4,),
    )


def contract_call(number, active, hidden, pair, vec, swaps):
    rows, size = hidden.shape
    wide = active.shape[1]
    scratch = [pltpu.VMEM((size, wide), LOW), *scatter_scratch(rows, size), LOCAL]
    return launch(
        contract_kernel, number, rows, [VM, VM, ANY, ANY, VM], (active, hidden, *pair, vec),
        [shape((rows, size))], (VM,), scratch, swaps, late=(1,),
    )


def expand_back_call(number, last, grad, contract, expand, slope, extra, second, hidden, vec, swaps):
    rows, size = hidden.shape
    wide = slope.shape[1]
    columns = LENGTH // rows
    outs = [shape((rows, size), WIDE), shape((rows, size)), shape((8, size), WIDE)]
    scratch = [
        pltpu.VMEM((size, wide), LOW),
        pltpu.VMEM((size, wide), LOW),
        pltpu.VMEM((LENGTH, wide), LOW),
        *scatter_scratch(rows, size), PAIRS, LOCAL,
    ]
    if last:
        outs += [shape((size, wide)), shape((LENGTH, size // columns))]
        out_specs = [VM] * 5
        scratch += [pltpu.VMEM((columns, rows, size // columns), LOW), pltpu.SemaphoreType.DMA((2, 3))]
    else:
        outs += [shape((size, wide // 2))] * 2 + [shape((LENGTH, size)), shape((size, wide // 2))]
        out_specs = [VM] * 6 + [ANY]
        scratch += [
            pltpu.VMEM((2, size, wide // 2), LOW), pltpu.VMEM((size, wide // 2), LOW),
            pltpu.SemaphoreType.DMA((2, 1)),
        ]
    return launch(
        functools.partial(expand_back_kernel, last),
        number, rows, [VM, ANY, ANY, ANY, ANY, VM, VM, VM, VM, VM],
        (grad, *contract, *expand, slope, extra, second, hidden, vec),
        outs, out_specs, scratch, swaps, last, not last, late=(5, 6, 7, 8),
    )


def scores_scratch(size, width, heads):
    return [
        pltpu.VMEM((size, 4 * width), LOW),
        pltpu.VMEM((LENGTH, size), LOW),
        pltpu.VMEM((heads, LENGTH, HEAD), LOW),
        pltpu.VMEM((8, LENGTH), WIDE),
        pltpu.VMEM((3 * heads, LENGTH, HEAD), LOW),
        pltpu.VMEM((LENGTH, HEAD), WIDE),
        pltpu.VMEM((LENGTH, HEAD), WIDE),
    ]


def late_attend_call(number, low, grad, x_own, pair, normed, heads_all, o, lse, vec, swaps):
    rows, size = grad.shape
    width = o.shape[1]
    heads = width // HEAD
    outs = (shape((rows, size)), shape((8, size), WIDE), shape((size, 4 * width)))
    scratch = [
        *scores_scratch(size, width, heads),
        pltpu.VMEM((LENGTH, 3 * width), LOW),
        pltpu.VMEM((size, 4 * width), LOW),
        pltpu.VMEM((size, width), LOW),
        *scatter_scratch(rows, size), PAIRS, LOCAL,
    ]
    return launch(
        functools.partial(late_attend_kernel, heads),
        number, rows, [VM, VM, VM, ANY, ANY, VM, VM, VM, VM, VM],
        (low, grad, x_own, *pair, normed, heads_all, o, lse, vec),
        outs, (VM, VM, ANY), scratch, swaps, late=(1, 2, 5, 6, 7, 8),
    )


def scores_back_call(number, low, pair, heads_all, o, lse, keep, send):
    rows, size = low.shape
    width = o.shape[1]
    heads = width // HEAD
    outs = (shape((LENGTH, 3 * width)), shape((size, width)), shape(keep.shape))
    scratch = [
        *scores_scratch(size, width, heads),
        pltpu.VMEM(keep.shape, LOW),
        PAIRS, LOCAL, pltpu.SemaphoreType.DMA((2, 1)),
    ]
    return launch(
        functools.partial(scores_back_kernel, heads),
        number, rows, [VM, ANY, ANY, VM, VM, VM, VM, ANY], (low, *pair, heads_all, o, lse, keep, send),
        outs, (VM, VM, ANY), scratch, (), False, True, late=(3, 4, 5, 6),
    )[0]


def attend_back_call(number, mixed, outer, grad, x_own, pair, normed, vec):
    rows, size = grad.shape
    width = outer.shape[1]
    half = 2 * width
    outs = (shape((size, half)), shape((rows, size)), shape((8, size), WIDE))
    scratch = [
        pltpu.VMEM((size, 4 * width), LOW),
        pltpu.VMEM((2, size, half), LOW),
        pltpu.VMEM((size, half), LOW),
        *scatter_scratch(rows, size), LOCAL, pltpu.SemaphoreType.DMA((2, 1)),
    ]
    return launch(
        attend_back_kernel,
        number, rows, [VM, VM, VM, VM, ANY, ANY, VM, VM],
        (mixed, outer, grad, x_own, *pair, normed, vec), outs, (ANY, VM, VM), scratch, (), False, True,
        late=(1, 2, 3, 6),
    )[0]


def finish_call(number, late, early1, early2, near, far, sums, row_count):
    rows, size = near.shape
    length, width = far.shape
    columns = length // rows
    outs = (
        shape((2 * length, width), WIDE),
        shape((16, width), WIDE),
        *[shape(part.shape) for part in (late, early1, early2)],
    )
    scratch = [
        pltpu.VMEM((length, width), LOW),
        pltpu.VMEM((columns, rows, width), LOW),
        pltpu.VMEM((columns, 2, 16, width), WIDE),
        pltpu.VMEM((3, 2, 8, width), WIDE),
        pltpu.VMEM((16, width), WIDE),
        pltpu.VMEM((row_count, 16, width), WIDE),
        pltpu.VMEM((length, width), LOW),
        pltpu.VMEM((length, width), LOW),
        pltpu.SemaphoreType.DMA((2, 3)),
        pltpu.SemaphoreType.DMA((2, 3)),
        pltpu.SemaphoreType.DMA((2, 2)),
        pltpu.SemaphoreType.DMA((2, row_count)),
        pltpu.SemaphoreType.DMA((2, 3)),
    ]
    return pl.pallas_call(
        finish_kernel,
        out_shape=outs,
        in_specs=[ANY] * 3 + [VM] * 6,
        out_specs=(VM, VM, ANY, ANY, ANY),
        scratch_shapes=scratch,
        compiler_params=pltpu.CompilerParams(
            collective_id=number, has_side_effects=True, vmem_limit_bytes=GRANT
        ),
        cost_estimate=pl.CostEstimate(flops=int(3e10), bytes_accessed=30 * MEBI, transcendentals=0),
    )(late, early1, early2, near, far, *sums)


def swap_sections(value):
    return lax.ppermute(value, "section", [(0, 1), (1, 0)])


def on_device(
    tokens,
    cotangent,
    first_gain,
    first_shift,
    attend_weight,
    attend_bias,
    output_weight,
    output_bias,
    second_gain,
    second_shift,
    expand_weight,
    expand_bias,
    contract_weight,
    contract_bias,
):
    section = lax.axis_index("section")
    column = lax.axis_index("col")
    first_section = section == 0
    columns = lax.axis_size("col")
    width = tokens.shape[1]
    size = width * columns
    rows = LENGTH // columns

    def pick(early, later):
        return jnp.where(first_section, early, later)

    block_rows = attend_weight.shape[1]
    units = (
        jnp.concatenate(
            [attend_weight[0].reshape(block_rows, 3 * width), output_weight[0].T], axis=1
        ),
        expand_weight[0],
        contract_weight[0].T,
    )
    kept_blocks, sent_blocks = [], []
    for unit in units:
        half = unit.shape[1] // 2
        low, high = unit[:, :half], unit[:, half:]
        kept_blocks.append(pick(low, high))
        sent_blocks.append(pick(high, low))

    small = jnp.concatenate(
        [
            first_gain,
            first_shift,
            output_bias,
            second_gain,
            second_shift,
            contract_bias,
            attend_bias[0],
            expand_bias[0].reshape(-1, width),
        ],
        0,
    )
    filled = small.shape[0]
    small = jnp.pad(small, ((0, -filled % 16), (0, 0)))
    got_attend = swap_sections(sent_blocks[0])
    got_attend, sent_expand = lax.optimization_barrier((got_attend, sent_blocks[1]))
    x0_full, gy_full, vectors, got_expand, got_contract = start_call(
        1, tokens, cotangent, small, sent_expand, units[2], columns
    )

    def gather_blocks(block):
        return lax.all_gather(block, "row", axis=0, tiled=True)

    half = units[2].shape[1] // 2
    mats = [[], []]
    for own, got in ((kept_blocks[0], got_attend), (kept_blocks[1], got_expand)):
        for layer, block in enumerate((pick(own, got), pick(got, own))):
            mats[layer].append(gather_blocks(block))
    mats[0].append(gather_blocks(pick(kept_blocks[2], got_contract[:, half:])))
    mats[1].append(gather_blocks(pick(got_contract, units[2])))
    vectors = vectors.astype(WIDE)
    wide_vectors = jnp.swapaxes(vectors[:, :, :6], 1, 2).reshape(2, 6, size)
    wide_vectors = jnp.pad(wide_vectors, ((0, 0), (0, 2), (0, 0)))
    own_vectors = lax.dynamic_index_in_dim(vectors, column, 1, keepdims=False)
    attend_biases = jnp.stack(
        [own_vectors[:, 6], jnp.zeros_like(own_vectors[:, 6]), own_vectors[:, 7]], 1
    ).reshape(2, 1, 3 * width)
    expand_biases = own_vectors[:, 8:filled].reshape(2, 1, -1)

    def own_rows(full):
        return lax.dynamic_slice_in_dim(full, column * rows, rows, 0)

    def own_features(full):
        return lax.dynamic_slice_in_dim(full, column * width, width, 1)

    attn = (mats[0][0], swap_sections(mats[0][0]))
    x = x0_full
    kept, pairs = [], []
    owns = [own_rows(x0_full)]
    for layer in range(2):
        last = layer == 1
        vec = wide_vectors[layer]
        (full, normed, heads, o, lse, hidden, second_own), (other,) = attend_call(
            2 + 3 * layer, not last, x, attn, vec, attend_biases[layer], rows, width, [mats[layer][1]]
        )
        expand = (mats[layer][1], other)
        outs, others = widen_call(
            3 + 3 * layer, second_own, expand, expand_biases[layer],
            gy_full if last else None, [] if last else [mats[0][2]],
        )
        second, active, slope = outs[:3]
        contract = (mats[layer][2], mats[layer][2] if last else others[0])
        if last:
            c1 = outs[3]
        outs, others = contract_call(
            4 + 3 * layer, active, hidden, contract, vec, [] if last else [mats[1][0]]
        )
        pairs.append((attn, expand, contract))
        kept.append((normed, heads, o, lse, hidden, second, active, slope))
        x = outs[0]
        owns.append(x)
        if not last:
            attn = (mats[1][0], others[0])
    y0 = own_features(full)

    def scatter(total):
        return lax.psum_scatter(total, "row", scatter_dimension=0, tiled=True)

    def tie(value, then):
        return lax.optimization_barrier((value, then))

    attn, expand, contract = pairs[1]
    normed, heads, o, lse, hidden, second, active, slope = kept[1]
    (grad_hidden, low, expand_sums1, e1, y1), _ = expand_back_call(
        8, True, gy_full, contract, expand, slope, owns[2], second, hidden, wide_vectors[1], []
    )
    layer_low, layer_high = pick(y0, y1), pick(y1, y0)
    part_c1, low = tie(scatter(c1), low)
    (gx1_own, attend_sums1, w1), (layer_got, far_c1) = late_attend_call(
        10, low, grad_hidden, owns[1], attn, normed, heads, o, lse, wide_vectors[1], [layer_high, part_c1]
    )
    layer_outputs = jnp.concatenate([pick(layer_low, layer_got), pick(layer_got, layer_low)], 0)

    attn, expand, contract = pairs[0]
    normed, heads, o, lse, hidden, second, active, slope = kept[0]
    part_e1 = scatter(e1)
    (grad_hidden, low, expand_sums0, ek0, es0, gx1_full, total_c0), (far_e1,) = expand_back_call(
        12, False, gx1_own, contract, expand, slope, active, second, hidden, wide_vectors[0], [part_e1]
    )
    mixed, outer, total_e0 = scores_back_call(14, low, attn, heads, o, lse, ek0, es0)
    part_w1, mixed = tie(scatter(w1), mixed)
    part_c0, mixed = tie(scatter(total_c0), mixed)
    total_w0, gx0_own, attend_sums0 = attend_back_call(
        15, mixed, outer, grad_hidden, owns[0], attn, normed, wide_vectors[0]
    )
    part_e0 = scatter(total_e0)
    input_grads, small_grads, far_w1, far_c0, far_e0 = finish_call(
        16,
        part_w1,
        part_c0,
        part_e0,
        gx0_own,
        own_features(gx1_full),
        (attend_sums0, expand_sums0, attend_sums1, expand_sums1),
        lax.axis_size("row"),
    )

    part_w0, small_grads = tie(scatter(total_w0), small_grads)
    far_w0 = lax.ppermute(part_w0, "section", [(1, 0)])

    units = []
    for late, far_late, early, far_early in (
        (part_w1, far_w1, part_w0, far_w0),
        (part_e1, far_e1, part_e0, far_e0),
        (part_c1, far_c1, part_c0, far_c0),
    ):
        whole = jnp.concatenate([early, far_early], 1).astype(WIDE)
        units.append(pick(whole, late.astype(WIDE) + far_late.astype(WIDE)))
    attn_part, expand_part, contract_part = units

    return (
        layer_outputs[None],
        input_grads[None],
        small_grads[0:1],
        small_grads[1:2],
        attn_part[:, : 3 * width].reshape(block_rows, 3, width)[None],
        small_grads[8:10][None],
        attn_part[:, 3 * width :].T[None],
        small_grads[2:3],
        small_grads[3:4],
        small_grads[4:5],
        expand_part[None],
        small_grads[10 : 10 + expand_bias.shape[1] // width].reshape(1, -1),
        contract_part.T[None],
        small_grads[5:6],
    )


def solution(mesh):
    return jax.shard_map(
        on_device,
        mesh=mesh,
        in_specs=(
            P("row", "col"),
            P("row", "col"),
            P("section", "col"),
            P("section", "col"),
            P("section", "row", None, "col"),
            P("section", None, "col"),
            P("section", "col", "row"),
            P("section", "col"),
            P("section", "col"),
            P("section", "col"),
            P("section", "row", "col"),
            P("section", "col"),
            P("section", "col", "row"),
            P("section", "col"),
        ),
        out_specs=(
            P("section", "row", "col"),
            P("section", "row", "col"),
            P("section", "col"),
            P("section", "col"),
            P("section", "row", None, "col"),
            P("section", None, "col"),
            P("section", "col", "row"),
            P("section", "col"),
            P("section", "col"),
            P("section", "col"),
            P("section", "row", "col"),
            P("section", "col"),
            P("section", "col", "row"),
            P("section", "col"),
        ),
        check_vma=False,
    )
```

```python
import functools

import jax
import jax.numpy as jnp
from jax import lax
from jax.experimental import pallas as pl
from jax.experimental.pallas import tpu as pltpu
from jax.sharding import PartitionSpec as P

HEAD = 64
LENGTH = 1024
EPS = 1e-05
LOW = jnp.bfloat16
WIDE = jnp.float32
MESH = pl.DeviceIdType.MESH
PARTS = 2
TILE = 256
MEBI = 1024 * 1024
GRANT = 58 * MEBI


def nn(left, right):
    return lax.dot_general(left, right, (((1,), (0,)), ((), ())), preferred_element_type=WIDE)


def nt(left, right):
    return lax.dot_general(left, right, (((1,), (1,)), ((), ())), preferred_element_type=WIDE)


def tn(left, right):
    return lax.dot_general(left, right, (((0,), (0,)), ((), ())), preferred_element_type=WIDE)


def normalise(values):
    center = jnp.mean(values, axis=1, keepdims=True)
    centred = values - center
    scale = lax.rsqrt(jnp.mean(centred * centred, axis=1, keepdims=True) + EPS)
    return centred * scale, scale


def norm_backward(grad, hat, scale, gain):
    scaled = grad * gain
    mean_one = jnp.mean(scaled, axis=1, keepdims=True)
    mean_two = jnp.mean(scaled * hat, axis=1, keepdims=True)
    return scale * (scaled - mean_one - hat * mean_two)


class Group:
    def __init__(self, rows):
        self.me = lax.axis_index("col")
        chip, core = self.me // 2, self.me % 2
        self.sib = chip * 2 + 1 - core
        self.peer = (1 - chip) * 2 + core
        self.diag = (1 - chip) * 2 + 1 - core
        self.rows = rows
        self.part = rows // PARTS
        self.loads, self.stores, self.begun = {}, {}, set()

    def need(self, *places):
        for place in places:
            self.loads[place].wait()

    def emit(self, *places):
        for place in places:
            self.stores[place].start()
            self.begun.add(place)

    def greet(self, swaps, diagonal, rows=()):
        barrier = pltpu.get_barrier_semaphore()
        others = [{"col": self.sib}, {"col": self.peer}]
        if diagonal:
            others.append({"col": self.diag})
        if swaps:
            others.append({"section": 1 - lax.axis_index("section")})
        others += [{"row": row} for row in rows]
        for other in others:
            pl.semaphore_signal(barrier, inc=1, device_id=other, device_id_type=MESH)
        pl.semaphore_wait(barrier, len(others))

    def slab(self, owner, j):
        return pl.ds(pl.multiple_of(owner * self.rows + j * self.part, self.part), self.part)

    def chunk(self, owner):
        return pl.ds(pl.multiple_of(owner * self.rows, self.rows), self.rows)


def push(src, dst, sems, slot, target, axis="col"):
    return pltpu.make_async_remote_copy(
        src_ref=src,
        dst_ref=dst,
        send_sem=sems.at[0, slot],
        recv_sem=sems.at[1, slot],
        device_id={axis: target},
        device_id_type=MESH,
    )


class Gather:
    def __init__(self, group, full, sems, blocks=False):
        self.group, self.full, self.sems, self.blocks = group, full, sems, blocks

    def piece(self, owner, j):
        if not self.blocks:
            return self.full.at[self.group.slab(owner, j)]
        part = self.full.shape[1] // PARTS
        return self.full.at[owner, pl.ds(j * part, part)]

    def start(self):
        g = self.group
        self.over, self.near, self.relayed = [], [], []
        for j in range(PARTS):
            piece = self.piece(g.me, j)
            self.over.append(push(piece, piece, self.sems, j, g.peer))
            self.over[-1].start()
        for j in range(PARTS):
            piece = self.piece(g.me, j)
            self.near.append(push(piece, piece, self.sems, PARTS + j, g.sib))
            self.near[-1].start()

    def sibling(self):
        for copy in self.near:
            copy.wait_recv()

    def relay(self):
        g = self.group
        for j in range(PARTS):
            self.over[j].wait_recv()
            piece = self.piece(g.peer, j)
            self.relayed.append(push(piece, piece, self.sems, 2 * PARTS + j, g.sib))
            self.relayed[-1].start()

    def diagonal(self):
        for copy in self.relayed:
            copy.wait_recv()

    def done(self):
        for copy in self.over + self.near + self.relayed:
            copy.wait_send()

    def each(self, body, first=None):
        g = self.group
        self.start()
        if first is not None:
            first()
        body(g.chunk(g.me))
        self.sibling()
        body(g.chunk(g.sib))
        self.relay()
        body(g.chunk(g.peer))
        self.diagonal()
        body(g.chunk(g.diag))
        self.done()


class Scatter:
    def __init__(self, group, stage, land, total, sems):
        self.group, self.stage, self.land, self.total, self.sems = group, stage, land, total, sems

    def start(self, part):
        g, stage, land = self.group, self.stage, self.land
        self.first, self.over, self.near = [], [], []
        def split(owner):
            whole = part(g.chunk(owner))
            return [whole[j * g.part : (j + 1) * g.part] for j in range(PARTS)]

        for j, mine in enumerate(split(g.diag)):
            stage[0, j] = mine.astype(LOW)
            self.first.append(push(stage.at[0, j], land.at[0, j], self.sems, j, g.sib))
            self.first[-1].start()
        for j, mine in enumerate(split(g.peer)):
            self.first[j].wait_recv()
            stage[1, j] = (mine + land[0, j].astype(WIDE)).astype(LOW)
            self.over.append(push(stage.at[1, j], land.at[1, j], self.sems, PARTS + j, g.peer))
            self.over[-1].start()
        for j, mine in enumerate(split(g.sib)):
            stage[2, j] = mine.astype(LOW)
            self.near.append(push(stage.at[2, j], land.at[2, j], self.sems, 2 * PARTS + j, g.sib))
            self.near[-1].start()
        for j, mine in enumerate(split(g.me)):
            self.total[j] = mine

    def take(self, j):
        self.near[j].wait_recv()
        self.over[j].wait_recv()
        land = self.land
        return self.total[j] + (land[1, j].astype(WIDE) + land[2, j].astype(WIDE))

    def done(self):
        for copy in self.first + self.over + self.near:
            copy.wait_send()


class Deliver:
    def __init__(self, group, stage, out, sems):
        self.group, self.stage, self.out, self.sems = group, stage, out, sems

    def start(self, rows_ref):
        g, width = self.group, self.out.shape[1]
        for c in range(self.stage.shape[0]):
            self.stage[c] = rows_ref[:, c * width : (c + 1) * width]
        place = self.out.at[g.chunk(g.me)]
        self.copies = [
            push(self.stage.at[other], place, self.sems, n, other)
            for n, other in enumerate((g.peer, g.diag, g.sib))
        ]
        for copy in self.copies:
            copy.start()
        self.out[g.chunk(g.me), :] = self.stage[g.me]

    def done(self):
        for copy in self.copies:
            copy.wait()


def scatter_scratch(rows, width):
    part = rows // PARTS
    return [
        pltpu.VMEM((3, PARTS, part, width), LOW),
        pltpu.VMEM((3, PARTS, part, width), LOW),
        pltpu.VMEM((PARTS, part, width), WIDE),
        pltpu.SemaphoreType.DMA((2, 3 * PARTS)),
    ]


class Halves:
    def __init__(self, pair, whole, sems, slot):
        if pair[0].shape[1] == whole.shape[1]:
            self.copies = [pltpu.make_async_copy(pair[0], whole, sems.at[slot])]
            return
        section = lax.axis_index("section")
        half = whole.shape[1] // 2
        self.copies = []
        for n, place in enumerate((section, 1 - section)):
            columns = pl.ds(pl.multiple_of(place * half, half), half)
            self.copies.append(
                pltpu.make_async_copy(pair[n], whole.at[:, columns], sems.at[slot + n])
            )

    def start(self):
        for copy in self.copies:
            copy.start()

    def wait(self):
        for copy in self.copies:
            copy.wait()


class Trade:
    def __init__(self, keep, send, got, sems):
        self.keep, self.send, self.got, self.sems = keep, send, got, sems
        self.tiles = keep.shape[0] // TILE

    def copy(self, n):
        rows = pl.ds(pl.multiple_of(n * TILE, TILE), TILE)
        return push(
            self.send.at[rows], self.got.at[rows], self.sems, n, 1 - lax.axis_index("section"), "section"
        )

    def start(self, make):
        @pl.loop(0, self.tiles)
        def _(n):
            make(pl.ds(pl.multiple_of(n * TILE, TILE), TILE))
            self.copy(n).start()

    def finish(self):
        @pl.loop(0, self.tiles)
        def _(n):
            self.copy(n).wait()

        add_into(self.keep, self.got)


def add_into(keep_ref, got_ref):
    @pl.loop(0, keep_ref.shape[0] // TILE)
    def _(n):
        rows = pl.ds(pl.multiple_of(n * TILE, TILE), TILE)
        keep_ref[rows, :] = (keep_ref[rows, :].astype(WIDE) + got_ref[rows, :].astype(WIDE)).astype(LOW)


def attention_out(heads_ref, o3, lse_ref, heads):
    length = heads_ref.shape[1]
    size = min(TILE, length)

    @pl.loop(0, heads)
    def _(h):
        for i in range(length // size):
            rows = slice(i * size, (i + 1) * size)
            finish = (i + 1) * size
            queries = heads_ref[h, rows, :]
            scores = nt(heads_ref[heads + h, :finish, :], queries)
            keep = lax.broadcasted_iota(jnp.int32, (size, size), 0) <= lax.broadcasted_iota(
                jnp.int32, (size, size), 1
            )
            last = jnp.where(keep, scores[finish - size :], -1000000000.0)
            scores = last if i == 0 else jnp.concatenate([scores[: finish - size], last], 0)
            highest = jnp.max(scores, axis=0, keepdims=True)
            powers = jnp.exp(scores - highest)
            summed = jnp.sum(powers, axis=0, keepdims=True)
            mixed = tn(heads_ref[2 * heads + h, :finish, :], powers.astype(LOW))
            o3[h, rows, :] = (mixed / summed).T.astype(LOW)
            lse_ref[pl.ds(h, 1), rows] = highest + jnp.log(summed)


def attention_back(heads_ref, go3, lse_ref, dots_ref, g3, key_acc, value_acc, heads):
    length = heads_ref.shape[1]
    size = min(TILE, length)

    @pl.loop(0, heads)
    def _(h):
        for i in reversed(range(length // size)):
            rows = slice(i * size, (i + 1) * size)
            finish = (i + 1) * size
            queries = heads_ref[h, rows, :]
            keys = heads_ref[heads + h, :finish, :]
            grads = go3[h, rows, :]
            scores = nt(keys, queries) - lse_ref[pl.ds(h, 1), rows]
            keep = lax.broadcasted_iota(jnp.int32, (size, size), 0) <= lax.broadcasted_iota(
                jnp.int32, (size, size), 1
            )
            last = jnp.where(keep, scores[finish - size :], -1000000000.0)
            scores = last if i == 0 else jnp.concatenate([scores[: finish - size], last], 0)
            probs = jnp.exp(scores)
            grad_probs = nt(heads_ref[2 * heads + h, :finish, :], grads)
            grad_scores = (probs * (grad_probs - dots_ref[pl.ds(h, 1), rows])).astype(LOW)
            g3[h, rows, :] = (tn(grad_scores, keys) * HEAD ** (-0.5)).astype(LOW)
            key_part = nn(grad_scores, queries)
            value_part = nn(probs.astype(LOW), grads)
            if finish == length:
                key_acc[...] = key_part
                value_acc[...] = value_part
            else:
                key_acc[:finish, :] += key_part
                value_acc[:finish, :] += value_part
        g3[heads + h] = key_acc[...].astype(LOW)
        g3[2 * heads + h] = value_acc[...].astype(LOW)


def start_kernel(
    tokens_ref, cotangent_ref, small_ref, expand_ref, contract_ref,
    x_ref, g_ref, vectors_ref, got_expand_ref, got_contract_ref,
    x4, g4, s4, other4, x_sems, g_sems, s_sems, local_sems,
):
    section = lax.axis_index("section")
    group = Group(x_ref.shape[0] // 4)
    length = x_ref.shape[0]
    loads = []
    rows = pl.ds(pl.multiple_of(section * length, length), length)
    for n, (source, into) in enumerate(((tokens_ref.at[rows], x4), (cotangent_ref.at[rows], g4), (small_ref, s4))):
        loads.append(pltpu.make_async_copy(source, into.at[group.me], local_sems.at[n]))
        loads[-1].start()
    group.greet(True, False)
    blocks = [
        push(source, into, s_sems, 3 * PARTS + 1 + n, 1 - section, "section")
        for n, (source, into) in enumerate(((expand_ref, got_expand_ref), (contract_ref, got_contract_ref)))
    ]
    for block in blocks:
        block.start()
    gathers = [Gather(group, x4, x_sems, True), Gather(group, s4, s_sems, True), Gather(group, g4, g_sems, True)]
    for gather, load in zip(gathers, (loads[0], loads[2], loads[1])):
        load.wait()
        gather.start()
    for gather in gathers:
        gather.sibling()
        gather.relay()
        gather.diagonal()
    swap = push(s4, other4, s_sems, 3 * PARTS, 1 - section, "section")
    swap.start()
    width = x4.shape[2]
    for c in range(x4.shape[0]):
        x_ref[:, c * width : (c + 1) * width] = x4[c]
        g_ref[:, c * width : (c + 1) * width] = g4[c]
    swap.wait()
    for block in blocks:
        block.wait()
    vectors_ref[section] = s4[...]
    vectors_ref[1 - section] = other4[...]
    for gather in gathers:
        gather.done()


def attend_kernel(
    gathered, heads, group, x_ref, mine_ref, other_ref, vec_ref, bias_ref,
    full_ref, normed_ref, heads_ref, o_ref, lse_ref, hidden_ref, second_ref,
    weight, o3, stage, land, total, scatter_sems, gather_sems, local_sems,
):
    width = o_ref.shape[1]
    halves = Halves((mine_ref, other_ref), weight, local_sems, 0)
    halves.start()
    if not gathered:
        full_ref[group.chunk(group.me), :] = x_ref[...]
    halves.wait()

    def project(rows):
        values = (x_ref if gathered else full_ref)[rows, :].astype(WIDE)
        hat, _ = normalise(values)
        normed = (hat * vec_ref[0:1, :] + vec_ref[1:2, :]).astype(LOW)
        normed_ref[rows, :] = normed
        mixed = nn(normed, weight[:, : 3 * width]) + bias_ref[...]
        for j in range(3 * heads):
            piece = mixed[:, j * HEAD : (j + 1) * HEAD]
            if j < heads:
                piece = piece * HEAD ** (-0.5)
            heads_ref[j, rows, :] = piece.astype(LOW)

    if gathered:
        full_ref[...] = jnp.zeros_like(full_ref)

        @pl.loop(0, LENGTH // group.rows)
        def _(n):
            project(group.chunk(n))
    else:
        Gather(group, full_ref, gather_sems).each(project)
    group.emit(0, 1, 2)

    attention_out(heads_ref, o3, lse_ref, heads)
    for h in range(heads):
        o_ref[:, h * HEAD : (h + 1) * HEAD] = o3[h]
    group.emit(3, 4)

    scatter = Scatter(group, stage, land, total, scatter_sems)
    scatter.start(lambda rows: nt(o_ref[rows, :], weight[:, 3 * width :]))
    for j in range(PARTS):
        rows = slice(j * group.part, (j + 1) * group.part)
        residual = (x_ref if gathered else full_ref)[group.slab(group.me, j), :].astype(WIDE)
        hidden = residual + scatter.take(j) + vec_ref[2:3, :]
        hidden_ref[rows, :] = hidden
        hat, _ = normalise(hidden)
        second_ref[rows, :] = (hat * vec_ref[3:4, :] + vec_ref[4:5, :]).astype(LOW)
    scatter.done()


def outer_whole(left_ref, right_ref, out_ref):
    @pl.loop(0, left_ref.shape[1] // TILE)
    def _(n):
        rows = pl.ds(pl.multiple_of(n * TILE, TILE), TILE)
        out_ref[rows, :] = tn(left_ref[:, rows], right_ref[...]).astype(LOW)


def widen_kernel(last, group, second_ref, em_ref, eo_ref, bias_ref, *refs):
    if last:
        g_ref, *refs = refs
    full_ref, active_ref, slope_ref, *refs = refs
    if last:
        c_ref, *refs = refs
    expand, gather_sems, local_sems = refs
    halves = Halves((em_ref, eo_ref), expand, local_sems, 0)
    halves.start()
    full_ref[group.chunk(group.me), :] = second_ref[...]
    halves.wait()

    def widen(rows):
        t = nn(full_ref[rows, :], expand[...]) + bias_ref[...]
        square = t * t
        bent = jnp.tanh(0.7978845608028654 * t * (1.0 + 0.044715 * square))
        active_ref[rows, :] = (0.5 * t * (1.0 + bent)).astype(LOW)
        slope_ref[rows, :] = (
            0.5 * (1.0 + bent)
            + (0.5 * 0.7978845608028654) * t * (1.0 - bent * bent) * (1.0 + 3 * 0.044715 * square)
        ).astype(LOW)

    Gather(group, full_ref, gather_sems).each(widen)
    if last:
        group.emit(0, 1, 2)
        group.need(4)
        outer_whole(g_ref, active_ref, c_ref)


def outer_halves(left_ref, right_ref, keep_ref, send_ref):
    section = lax.axis_index("section")
    half = right_ref.shape[1] // 2
    for place, out in ((section, keep_ref), (1 - section, send_ref)):
        columns = pl.ds(pl.multiple_of(place * half, half), half)

        @pl.loop(0, left_ref.shape[1] // TILE)
        def _(n):
            rows = pl.ds(pl.multiple_of(n * TILE, TILE), TILE)
            out[rows, :] = tn(left_ref[:, rows], right_ref[:, columns]).astype(LOW)


def contract_kernel(
    group, active_ref, hidden_ref, cm_ref, co_ref, vec_ref, result_ref,
    contract, stage, land, total, scatter_sems, local_sems,
):
    halves = Halves((cm_ref, co_ref), contract, local_sems, 0)
    halves.start()
    halves.wait()
    scatter = Scatter(group, stage, land, total, scatter_sems)
    scatter.start(lambda rows: nt(active_ref[rows, :], contract[...]))
    group.need(1)
    for j in range(PARTS):
        rows = slice(j * group.part, (j + 1) * group.part)
        result = hidden_ref[rows, :] + scatter.take(j) + vec_ref[5:6, :]
        result_ref[rows, :] = result.astype(LOW)
    scatter.done()


def narrow_grads(group, scatter, full_ref, hidden_ref, vec_ref, grad_ref, low_ref, sums_ref):
    for j in range(PARTS):
        rows = slice(j * group.part, (j + 1) * group.part)
        grad = scatter.take(j)
        hat, scale = normalise(hidden_ref[rows, :])
        own = full_ref[group.slab(group.me, j), :].astype(WIDE)
        out = own + norm_backward(grad, hat, scale, vec_ref[3:4, :])
        grad_ref[rows, :] = out
        low_ref[rows, :] = out.astype(LOW)
        for n, term in enumerate((grad * hat, grad, own, out)):
            sums_ref[n : n + 1, :] += jnp.sum(term, axis=0, keepdims=True)


def bend(rows, full_ref, contract, slope_ref, before, sums_ref):
    grad = (nn(full_ref[rows, :], contract[...]) * slope_ref[rows, :].astype(WIDE)).astype(LOW)
    before[rows, :] = grad
    sums_ref[4:5, :] += jnp.sum(grad.astype(WIDE), axis=0, keepdims=True)


def late_expand_kernel(
    group, active_ref, hidden_ref, cm_ref, co_ref, em_ref, eo_ref, g_ref, slope_ref, second_ref, vec_ref,
    grad_ref, low_ref, sums_ref, e_ref, out_ref,
    contract, expand, before, result, stage4,
    stage_a, land_a, total_a, sems_a, stage, land, total, scatter_sems, deliver_sems, local_sems,
):
    first = Halves((cm_ref, co_ref), contract, local_sems, 0)
    then = Halves((em_ref, eo_ref), expand, local_sems, 2)
    first.start()
    then.start()
    sums_ref[...] = jnp.zeros_like(sums_ref)
    first.wait()
    forward = Scatter(group, stage_a, land_a, total_a, sems_a)
    forward.start(lambda rows: nt(active_ref[rows, :], contract[...]))
    group.need(6, 7)

    @pl.loop(0, LENGTH // group.rows)
    def _(n):
        bend(group.chunk(n), g_ref, contract, slope_ref, before, sums_ref)

    then.wait()
    scatter = Scatter(group, stage, land, total, scatter_sems)
    scatter.start(lambda rows: nt(before[rows, :], expand[...]))
    group.need(1)
    for j in range(PARTS):
        rows = slice(j * group.part, (j + 1) * group.part)
        result[rows, :] = (hidden_ref[rows, :] + forward.take(j) + vec_ref[5:6, :]).astype(LOW)
    deliver = Deliver(group, stage4, out_ref, deliver_sems)
    deliver.start(result)
    group.need(8)
    outer_whole(second_ref, before, e_ref)
    group.emit(3)
    narrow_grads(group, scatter, g_ref, hidden_ref, vec_ref, grad_ref, low_ref, sums_ref)
    group.emit(0, 1, 2)
    forward.done()
    scatter.done()
    deliver.done()


def expand_back_kernel(
    group, g_ref, cm_ref, co_ref, em_ref, eo_ref, slope_ref, active_ref, second_ref, hidden_ref, vec_ref,
    grad_ref, low_ref, sums_ref, ek_ref, es_ref, full_ref, c_ref,
    contract, expand, before, stage, land, total, scatter_sems, gather_sems, local_sems, outer, got, trade_sems,
):
    section = lax.axis_index("section")
    first = Halves((cm_ref, co_ref), contract, local_sems, 0)
    then = Halves((em_ref, eo_ref), expand, local_sems, 2)
    first.start()
    then.start()
    sums_ref[...] = jnp.zeros_like(sums_ref)
    full_ref[group.chunk(group.me), :] = g_ref[...]
    first.wait()
    Gather(group, full_ref, gather_sems).each(
        lambda rows: bend(rows, full_ref, contract, slope_ref, before, sums_ref), lambda: group.need(5)
    )
    group.emit(5)
    group.need(6)
    half = active_ref.shape[1] // 2

    def columns(place):
        return pl.ds(pl.multiple_of(place * half, half), half)

    def make(n):
        def tile(rows):
            place = section if n == 0 else 1 - section
            outer[n, rows, :] = tn(full_ref[:, rows], active_ref[:, columns(place)]).astype(LOW)

        return tile

    trade = Trade(outer.at[0], outer.at[1], got, trade_sems)
    trade.start(make(1))
    then.wait()
    scatter = Scatter(group, stage, land, total, scatter_sems)
    scatter.start(lambda rows: nt(before[rows, :], expand[...]))
    group.need(7)
    outer_halves(second_ref, before, ek_ref, es_ref)
    group.emit(3, 4)
    keep = make(0)

    @pl.loop(0, outer.shape[1] // TILE)
    def _(n):
        keep(pl.ds(pl.multiple_of(n * TILE, TILE), TILE))

    group.need(8)
    narrow_grads(group, scatter, full_ref, hidden_ref, vec_ref, grad_ref, low_ref, sums_ref)
    group.emit(0, 1, 2)
    scatter.done()
    trade.finish()
    store = pltpu.make_async_copy(outer.at[0], c_ref, local_sems.at[0])
    store.start()
    store.wait()


def scores_back(group, heads, low_ref, weight, heads_ref, o_ref, lse_ref, full, go3, dots, g3, accs, mixed, gather_sems, needs):
    width = o_ref.shape[1]
    picks = (
        lax.broadcasted_iota(jnp.int32, (8, width), 1) // HEAD
        == lax.broadcasted_iota(jnp.int32, (8, width), 0)
    ).astype(WIDE)

    def spread(rows):
        grads = nn(full[rows, :], weight[:, 3 * width :]).astype(LOW)
        for h in range(heads):
            go3[h, rows, :] = grads[:, h * HEAD : (h + 1) * HEAD]
        term = grads.astype(WIDE) * o_ref[rows, :].astype(WIDE)
        dots[:, rows] = lax.dot_general(
            picks,
            term,
            (((1,), (1,)), ((), ())),
            precision=lax.Precision.HIGHEST,
            preferred_element_type=WIDE,
        )

    full[group.chunk(group.me), :] = low_ref[...]
    Gather(group, full, gather_sems).each(spread, lambda: group.need(needs[0]))
    group.need(*needs[1:])
    attention_back(heads_ref, go3, lse_ref, dots, g3, *accs, heads)
    for j in range(3 * heads):
        mixed[:, j * HEAD : (j + 1) * HEAD] = g3[j]


def outer_out(full, o_ref, outer_ref):
    @pl.loop(0, outer_ref.shape[0] // TILE)
    def _(n):
        rows = pl.ds(pl.multiple_of(n * TILE, TILE), TILE)
        outer_ref[rows, :] = tn(full[:, rows], o_ref[...]).astype(LOW)


def attend_grads(group, scatter, x_ref, grad_ref, vec_ref, mixed, width, out_ref, sums_ref):
    sums_ref[2:3, : 3 * width] = jnp.sum(mixed[...].astype(WIDE), axis=0, keepdims=True)
    for j in range(PARTS):
        rows = slice(j * group.part, (j + 1) * group.part)
        grad = scatter.take(j)
        hat, scale = normalise(x_ref[rows, :].astype(WIDE))
        out = grad_ref[rows, :] + norm_backward(grad, hat, scale, vec_ref[0:1, :])
        out_ref[rows, :] = out.astype(LOW)
        for n, term in enumerate((grad * hat, grad)):
            sums_ref[n : n + 1, :] += jnp.sum(term, axis=0, keepdims=True)


def late_attend_kernel(
    heads, group, low_ref, grad_ref, x_ref, mine_ref, other_ref, normed_ref, heads_ref, o_ref, lse_ref, vec_ref,
    out_ref, sums_ref, w_ref,
    weight, full, go3, dots, g3, key_acc, value_acc, mixed, outer, outer_o,
    stage, land, total, scatter_sems, gather_sems, local_sems,
):
    width = o_ref.shape[1]
    halves = Halves((mine_ref, other_ref), weight, local_sems, 0)
    halves.start()
    sums_ref[...] = jnp.zeros_like(sums_ref)
    halves.wait()
    scores_back(
        group, heads, low_ref, weight, heads_ref, o_ref, lse_ref, full, go3, dots, g3,
        (key_acc, value_acc), mixed, gather_sems, (7, 6, 8),
    )
    scatter = Scatter(group, stage, land, total, scatter_sems)
    scatter.start(lambda rows: nt(mixed[rows, :], weight[:, : 3 * width]))
    outer_out(full, o_ref, outer_o)
    group.need(5)

    @pl.loop(0, weight.shape[0] // TILE)
    def _(n):
        rows = pl.ds(pl.multiple_of(n * TILE, TILE), TILE)
        outer[rows, : 3 * width] = tn(normed_ref[:, rows], mixed[...]).astype(LOW)
        outer[rows, 3 * width :] = outer_o[rows, :]

    store = pltpu.make_async_copy(outer, w_ref, local_sems.at[2])
    store.start()
    group.need(1, 2)
    attend_grads(group, scatter, x_ref, grad_ref, vec_ref, mixed, width, out_ref, sums_ref)
    scatter.done()
    store.wait()


def scores_back_kernel(
    heads, group, low_ref, mine_ref, other_ref, heads_ref, o_ref, lse_ref, ek_ref, es_ref,
    mixed, outer_ref, e_ref,
    weight, full, go3, dots, g3, key_acc, value_acc, got, gather_sems, local_sems, swap_sems,
):
    swap = push(es_ref, got, swap_sems, 0, 1 - lax.axis_index("section"), "section")
    swap.start()
    halves = Halves((mine_ref, other_ref), weight, local_sems, 0)
    halves.start()
    halves.wait()
    scores_back(
        group, heads, low_ref, weight, heads_ref, o_ref, lse_ref, full, go3, dots, g3,
        (key_acc, value_acc), mixed, gather_sems, (4, 3, 5),
    )
    group.emit(0)
    outer_out(full, o_ref, outer_ref)
    group.emit(1)
    group.need(6)
    swap.wait()
    add_into(ek_ref, got)
    store = pltpu.make_async_copy(ek_ref, e_ref, local_sems.at[0])
    store.start()
    store.wait()


def attend_back_kernel(
    group, mixed, outer_ref, grad_ref, x_ref, mine_ref, other_ref, normed_ref, vec_ref,
    w_ref, out_ref, sums_ref,
    weight, outer, got, stage, land, total, scatter_sems, local_sems, swap_sems,
):
    width = outer_ref.shape[1]
    section = lax.axis_index("section")
    halves = Halves((mine_ref, other_ref), weight, local_sems, 0)
    halves.start()
    sums_ref[...] = jnp.zeros_like(sums_ref)
    half = weight.shape[1] // 2
    scatter = Scatter(group, stage, land, total, scatter_sems)
    group.need(1, 6)

    def make(n):
        place = section if n == 0 else 1 - section

        def tile(rows):
            @pl.when(place == 0)
            def _():
                outer[n, rows, :] = tn(normed_ref[:, rows], mixed[:, :half]).astype(LOW)

            @pl.when(place == 1)
            def _():
                outer[n, rows, : 3 * width - half] = tn(normed_ref[:, rows], mixed[:, half:]).astype(LOW)
                outer[n, rows, 3 * width - half :] = outer_ref[rows, :]

        return tile

    trade = Trade(outer.at[0], outer.at[1], got, swap_sems)
    trade.start(make(1))
    halves.wait()
    scatter.start(lambda rows: nt(mixed[rows, :], weight[:, : 3 * width]))
    keep = make(0)

    @pl.loop(0, outer.shape[1] // TILE)
    def _(n):
        keep(pl.ds(pl.multiple_of(n * TILE, TILE), TILE))

    group.need(2, 3)
    attend_grads(group, scatter, x_ref, grad_ref, vec_ref, mixed, width, out_ref, sums_ref)
    group.emit(1, 2)
    scatter.done()
    trade.finish()
    store = pltpu.make_async_copy(outer.at[0], w_ref, local_sems.at[2])
    store.start()
    store.wait()


def finish_kernel(
    late1_ref, late2_ref, early1_ref, early2_ref, near_ref, far_ref, a0, n0, a1, n1,
    grads_ref, sums_ref, got_late1, got_late2, got_early1, got_early2,
    mine, stage4, block, land_col, land_x, land_z, land,
    deliver_sems, col_sems, x_sems, z_sems, part_sems,
):
    section, row = lax.axis_index("section"), lax.axis_index("row")
    group = Group(near_ref.shape[0])
    length, width = far_ref.shape
    others = [lax.rem(row + d, land_z.shape[0]) for d in range(1, land_z.shape[0])]
    group.greet(True, True, others)
    parts = [
        push(source, into, part_sems, n, 1 - section, "section")
        for n, (source, into) in enumerate(
            (
                (late1_ref, got_late1), (late2_ref, got_late2),
                (early1_ref, got_early1), (early2_ref, got_early2),
            )
        )
    ]

    swap_far = push(far_ref, land, x_sems, 1, 1 - section, "section")
    swap_near = push(mine, land, x_sems, 1, 1 - section, "section")

    @pl.when(section == 0)
    def _():
        parts[0].start()
        parts[1].start()
        swap_far.start()

    @pl.when(section == 1)
    def _():
        parts[2].start()
        parts[3].start()

    deliver = Deliver(group, stage4, mine, deliver_sems)
    deliver.start(near_ref)

    block[...] = jnp.zeros_like(block)
    for layer, (attn, narrow) in enumerate(((a0, n0), (a1, n1))):
        wide = [attn[0:1, :], attn[1:2, :], narrow[3:4, :], narrow[0:1, :], narrow[1:2, :], narrow[2:3, :]]
        for c in range(block.shape[0]):
            columns = slice(c * width, (c + 1) * width)
            for n, term in enumerate(wide):
                block[c, layer, n : n + 1, :] = term[:, columns]
            for n, term in enumerate((attn[2:3, :width], attn[2:3, 2 * width : 3 * width])):
                block[c, layer, 8 + n : 9 + n, :] = term
            for n in range(narrow.shape[1] // width):
                block[c, layer, 10 + n : 11 + n, :] = narrow[4:5, n * width : (n + 1) * width]
    copies = [
        push(block.at[other, :, pl.ds(0, 8)], land_col.at[n], col_sems, n, other)
        for n, other in enumerate((group.peer, group.diag, group.sib))
    ]
    for copy in copies:
        copy.start()
    for copy in copies:
        copy.wait()
    me = group.me
    block[me, :, :8] = block[me, :, :8] + (land_col[0] + (land_col[1] + land_col[2]))
    swap = push(block.at[me, 1 - section], land_x, x_sems, 0, 1 - section, "section")
    swap.start()
    swap.wait()
    land_z[row] = block[me, section] + land_x[...]
    copies = [
        push(land_z.at[row], land_z.at[row], z_sems, n, other, "row")
        for n, other in enumerate(others)
    ]
    for copy in copies:
        copy.start()

    deliver.done()

    @pl.when(section == 1)
    def _():
        swap_near.start()

    own = pl.ds(pl.multiple_of(section * length, length), length)
    away = pl.ds(pl.multiple_of((1 - section) * length, length), length)

    @pl.when(section == 0)
    def _():
        grads_ref[own, :] = mine[...].astype(WIDE)

    @pl.when(section == 1)
    def _():
        grads_ref[own, :] = far_ref[...].astype(WIDE)

    for copy in copies:
        copy.wait()
    result = land_z[0]
    for n in range(1, land_z.shape[0]):
        result = result + land_z[n]
    sums_ref[...] = result
    @pl.when(section == 0)
    def _():
        swap_far.wait()

    @pl.when(section == 1)
    def _():
        swap_near.wait()

    grads_ref[away, :] = land[...].astype(WIDE)

    @pl.when(section == 0)
    def _():
        parts[0].wait_send()
        parts[1].wait_send()
        parts[2].wait_recv()
        parts[3].wait_recv()

    @pl.when(section == 1)
    def _():
        parts[2].wait_send()
        parts[3].wait_send()
        parts[0].wait_recv()
        parts[1].wait_recv()


VM = pl.BlockSpec(memory_space=pltpu.VMEM)
ANY = pl.BlockSpec(memory_space=pl.ANY)
PAIRS = pltpu.SemaphoreType.DMA((2, 3 * PARTS))
LOCAL = pltpu.SemaphoreType.DMA((4,))


def shape(dims, kind=LOW):
    return jax.ShapeDtypeStruct(dims, kind)


def launch(
    body, number, rows, in_specs, ins, outs, out_specs, scratch, swaps=(), diagonal=False, across=False, late=(),
):
    n_in, n_out, n = len(ins), len(outs), len(swaps)
    held_in = [i for i in range(n_in) if in_specs[i] is VM]
    held_out = [i for i in range(n_out) if out_specs[i] is VM]

    def kernel(*refs):
        refs = list(refs)
        takes, sources = refs[:n_in], refs[n_in : n_in + n]
        gives = refs[n_in + n : n_in + n + n_out]
        lands = refs[n_in + n + n_out : n_in + 2 * n + n_out]
        rest = refs[n_in + 2 * n + n_out :]
        own, rest = rest[: len(scratch)], rest[len(scratch) :]
        in_held, rest = rest[: len(held_in)], rest[len(held_in) :]
        out_held, rest = rest[: len(held_out)], rest[len(held_out) :]
        in_sems, out_sems, swap_sems = rest
        group = Group(rows)
        for k, i in enumerate(held_in):
            group.loads[i] = pltpu.make_async_copy(takes[i], in_held[k], in_sems.at[k])
            group.loads[i].start()
            takes[i] = in_held[k]
        for k, i in enumerate(held_out):
            group.stores[i] = pltpu.make_async_copy(out_held[k], gives[i], out_sems.at[k])
            gives[i] = out_held[k]
        group.greet(n or across, diagonal)
        other = 1 - lax.axis_index("section")
        copies = [
            push(source, land, swap_sems, i, other, "section")
            for i, (source, land) in enumerate(zip(sources, lands))
        ]
        for copy in copies:
            copy.start()
        group.need(*[i for i in held_in if i not in late])
        body(group, *takes, *gives, *own)
        group.emit(*[i for i in held_out if i not in group.begun])
        for copy in copies:
            copy.wait()
        for i in held_out:
            group.stores[i].wait()

    results = pl.pallas_call(
        kernel,
        out_shape=(*outs, *[shape(s.shape, s.dtype) for s in swaps]),
        in_specs=[ANY] * (n_in + n),
        out_specs=(ANY,) * (n_out + n),
        scratch_shapes=[
            *scratch,
            *[pltpu.VMEM(ins[i].shape, ins[i].dtype) for i in held_in],
            *[pltpu.VMEM(outs[i].shape, outs[i].dtype) for i in held_out],
            pltpu.SemaphoreType.DMA((len(held_in),)),
            pltpu.SemaphoreType.DMA((len(held_out),)),
            pltpu.SemaphoreType.DMA((2, max(n, 1))),
        ],
        compiler_params=pltpu.CompilerParams(
            collective_id=number, has_side_effects=True, vmem_limit_bytes=GRANT
        ),
        cost_estimate=pl.CostEstimate(flops=int(3e10), bytes_accessed=30 * MEBI, transcendentals=0),
    )(*ins, *swaps)
    return results[:n_out], results[n_out:]


def start_call(number, tokens, cotangent, small, expand, contract, columns):
    width = tokens.shape[1]
    size = width * columns
    kinds = small.shape[0]
    outs = (shape((LENGTH, size)), shape((LENGTH, size)), shape((2, columns, kinds, width)), shape(expand.shape), shape(contract.shape))
    blocks = pltpu.VMEM((columns, LENGTH, width), LOW)
    vectors = pltpu.VMEM((columns, kinds, width), LOW)
    return pl.pallas_call(
        start_kernel,
        out_shape=outs,
        in_specs=[ANY] * 5,
        out_specs=(VM, VM, VM, ANY, ANY),
        scratch_shapes=[
            blocks, blocks, vectors, vectors, PAIRS, PAIRS,
            pltpu.SemaphoreType.DMA((2, 3 * PARTS + 3)), LOCAL,
        ],
        compiler_params=pltpu.CompilerParams(
            collective_id=number, has_side_effects=True, vmem_limit_bytes=GRANT
        ),
        cost_estimate=pl.CostEstimate(flops=int(3e10), bytes_accessed=30 * MEBI, transcendentals=0),
    )(tokens, cotangent, small, expand, contract)


def attend_call(number, gathered, x, pair, vec, bias, rows, width, swaps):
    size = vec.shape[1]
    heads = width // HEAD
    outs = (
        shape((LENGTH, size) if not gathered else (16, 128)),
        shape((LENGTH, size)),
        shape((3 * heads, LENGTH, HEAD)),
        shape((LENGTH, width)),
        shape((8, LENGTH), WIDE),
        shape((rows, size), WIDE),
        shape((rows, size)),
    )
    scratch = [
        pltpu.VMEM((size, 4 * width), LOW),
        pltpu.VMEM((heads, LENGTH, HEAD), LOW),
        *scatter_scratch(rows, size), PAIRS, LOCAL,
    ]
    return launch(
        functools.partial(attend_kernel, gathered, heads),
        number, rows, [VM, ANY, ANY, VM, VM], (x, *pair, vec, bias), outs, (VM,) * 7, scratch, swaps,
    )


def widen_call(number, second, pair, bias, grad, swaps):
    rows, size = second.shape
    wide = bias.shape[1]
    last = grad is not None
    ins, in_specs = [second, *pair, bias], [VM, ANY, ANY, VM]
    outs = [shape((LENGTH, size)), shape((LENGTH, wide)), shape((LENGTH, wide))]
    if last:
        ins, in_specs, outs = ins + [grad], in_specs + [VM], outs + [shape((size, wide))]
    scratch = [pltpu.VMEM((size, wide), LOW), PAIRS, LOCAL]
    return launch(
        functools.partial(widen_kernel, last),
        number, rows, in_specs, ins, outs, (VM,) * len(outs), scratch, swaps, late=(4,),
    )


def contract_call(number, active, hidden, pair, vec, swaps):
    rows, size = hidden.shape
    wide = active.shape[1]
    scratch = [pltpu.VMEM((size, wide), LOW), *scatter_scratch(rows, size), LOCAL]
    return launch(
        contract_kernel, number, rows, [VM, VM, ANY, ANY, VM], (active, hidden, *pair, vec),
        [shape((rows, size))], (VM,), scratch, swaps, late=(1,),
    )


def late_expand_call(number, active, hidden, contract, expand, grad, slope, second, vec, swaps):
    rows, size = hidden.shape
    wide = slope.shape[1]
    columns = LENGTH // rows
    outs = [
        shape((rows, size), WIDE), shape((rows, size)), shape((8, size), WIDE),
        shape((size, wide)), shape((LENGTH, size // columns)),
    ]
    scratch = [
        pltpu.VMEM((size, wide), LOW),
        pltpu.VMEM((size, wide), LOW),
        pltpu.VMEM((LENGTH, wide), LOW),
        pltpu.VMEM((rows, size), LOW),
        pltpu.VMEM((columns, rows, size // columns), LOW),
        *scatter_scratch(rows, size), *scatter_scratch(rows, size),
        pltpu.SemaphoreType.DMA((2, 3)), LOCAL,
    ]
    return launch(
        late_expand_kernel,
        number, rows, [VM, VM, ANY, ANY, ANY, ANY, VM, VM, VM, VM],
        (active, hidden, *contract, *expand, grad, slope, second, vec),
        outs, [VM] * 5, scratch, swaps, True, late=(1, 6, 7, 8),
    )


def expand_back_call(number, grad, contract, expand, slope, active, second, hidden, vec, swaps):
    rows, size = hidden.shape
    wide = slope.shape[1]
    half = wide // 2
    outs = [
        shape((rows, size), WIDE), shape((rows, size)), shape((8, size), WIDE),
        shape((size, half)), shape((size, half)), shape((LENGTH, size)), shape((size, half)),
    ]
    scratch = [
        pltpu.VMEM((size, wide), LOW),
        pltpu.VMEM((size, wide), LOW),
        pltpu.VMEM((LENGTH, wide), LOW),
        *scatter_scratch(rows, size), PAIRS, LOCAL,
        pltpu.VMEM((2, size, half), LOW), pltpu.VMEM((size, half), LOW),
        pltpu.SemaphoreType.DMA((2, size // TILE)),
    ]
    return launch(
        expand_back_kernel,
        number, rows, [VM, ANY, ANY, ANY, ANY, VM, VM, VM, VM, VM],
        (grad, *contract, *expand, slope, active, second, hidden, vec),
        outs, [VM] * 6 + [ANY], scratch, swaps, False, True, late=(5, 6, 7, 8),
    )


def scores_scratch(size, width, heads):
    return [
        pltpu.VMEM((size, 4 * width), LOW),
        pltpu.VMEM((LENGTH, size), LOW),
        pltpu.VMEM((heads, LENGTH, HEAD), LOW),
        pltpu.VMEM((8, LENGTH), WIDE),
        pltpu.VMEM((3 * heads, LENGTH, HEAD), LOW),
        pltpu.VMEM((LENGTH, HEAD), WIDE),
        pltpu.VMEM((LENGTH, HEAD), WIDE),
    ]


def late_attend_call(number, low, grad, x_own, pair, normed, heads_all, o, lse, vec, swaps):
    rows, size = grad.shape
    width = o.shape[1]
    heads = width // HEAD
    outs = (shape((rows, size)), shape((8, size), WIDE), shape((size, 4 * width)))
    scratch = [
        *scores_scratch(size, width, heads),
        pltpu.VMEM((LENGTH, 3 * width), LOW),
        pltpu.VMEM((size, 4 * width), LOW),
        pltpu.VMEM((size, width), LOW),
        *scatter_scratch(rows, size), PAIRS, LOCAL,
    ]
    return launch(
        functools.partial(late_attend_kernel, heads),
        number, rows, [VM, VM, VM, ANY, ANY, VM, VM, VM, VM, VM],
        (low, grad, x_own, *pair, normed, heads_all, o, lse, vec),
        outs, (VM, VM, ANY), scratch, swaps, late=(1, 2, 5, 6, 7, 8),
    )


def scores_back_call(number, low, pair, heads_all, o, lse, keep, send):
    rows, size = low.shape
    width = o.shape[1]
    heads = width // HEAD
    outs = (shape((LENGTH, 3 * width)), shape((size, width)), shape(keep.shape))
    scratch = [
        *scores_scratch(size, width, heads),
        pltpu.VMEM(keep.shape, LOW),
        PAIRS, LOCAL, pltpu.SemaphoreType.DMA((2, 1)),
    ]
    return launch(
        functools.partial(scores_back_kernel, heads),
        number, rows, [VM, ANY, ANY, VM, VM, VM, VM, ANY], (low, *pair, heads_all, o, lse, keep, send),
        outs, (VM, VM, ANY), scratch, (), False, True, late=(3, 4, 5, 6),
    )[0]


def attend_back_call(number, mixed, outer, grad, x_own, pair, normed, vec):
    rows, size = grad.shape
    width = outer.shape[1]
    half = 2 * width
    outs = (shape((size, half)), shape((rows, size)), shape((8, size), WIDE))
    scratch = [
        pltpu.VMEM((size, 4 * width), LOW),
        pltpu.VMEM((2, size, half), LOW),
        pltpu.VMEM((size, half), LOW),
        *scatter_scratch(rows, size), LOCAL, pltpu.SemaphoreType.DMA((2, size // TILE)),
    ]
    return launch(
        attend_back_kernel,
        number, rows, [VM, VM, VM, VM, ANY, ANY, VM, VM],
        (mixed, outer, grad, x_own, *pair, normed, vec), outs, (ANY, VM, VM), scratch, (), False, True,
        late=(1, 2, 3, 6),
    )[0]


def finish_call(number, late, early, near, far, sums, row_count):
    rows, size = near.shape
    length, width = far.shape
    columns = length // rows
    outs = (
        shape((2 * length, width), WIDE),
        shape((16, width), WIDE),
        *[shape(part.shape) for part in (*late, *early)],
    )
    scratch = [
        pltpu.VMEM((length, width), LOW),
        pltpu.VMEM((columns, rows, width), LOW),
        pltpu.VMEM((columns, 2, 16, width), WIDE),
        pltpu.VMEM((3, 2, 8, width), WIDE),
        pltpu.VMEM((16, width), WIDE),
        pltpu.VMEM((row_count, 16, width), WIDE),
        pltpu.VMEM((length, width), LOW),
        pltpu.SemaphoreType.DMA((2, 3)),
        pltpu.SemaphoreType.DMA((2, 3)),
        pltpu.SemaphoreType.DMA((2, 2)),
        pltpu.SemaphoreType.DMA((2, row_count)),
        pltpu.SemaphoreType.DMA((2, 4)),
    ]
    return pl.pallas_call(
        finish_kernel,
        out_shape=outs,
        in_specs=[ANY] * 4 + [VM] * 6,
        out_specs=(VM, VM) + (ANY,) * 4,
        scratch_shapes=scratch,
        compiler_params=pltpu.CompilerParams(
            collective_id=number, has_side_effects=True, vmem_limit_bytes=GRANT
        ),
        cost_estimate=pl.CostEstimate(flops=int(3e10), bytes_accessed=30 * MEBI, transcendentals=0),
    )(*late, *early, near, far, *sums)


def swap_sections(value):
    return lax.ppermute(value, "section", [(0, 1), (1, 0)])


def on_device(
    tokens,
    cotangent,
    first_gain,
    first_shift,
    attend_weight,
    attend_bias,
    output_weight,
    output_bias,
    second_gain,
    second_shift,
    expand_weight,
    expand_bias,
    contract_weight,
    contract_bias,
):
    section = lax.axis_index("section")
    column = lax.axis_index("col")
    first_section = section == 0
    columns = lax.axis_size("col")
    width = tokens.shape[1]
    size = width * columns
    rows = LENGTH // columns

    def pick(early, later):
        return jnp.where(first_section, early, later)

    block_rows = attend_weight.shape[1]
    units = (
        jnp.concatenate(
            [attend_weight[0].reshape(block_rows, 3 * width), output_weight[0].T], axis=1
        ),
        expand_weight[0],
        contract_weight[0].T,
    )
    kept_blocks, sent_blocks = [], []
    for unit in units:
        half = unit.shape[1] // 2
        low, high = unit[:, :half], unit[:, half:]
        kept_blocks.append(pick(low, high))
        sent_blocks.append(pick(high, low))

    small = jnp.concatenate(
        [
            first_gain,
            first_shift,
            output_bias,
            second_gain,
            second_shift,
            contract_bias,
            attend_bias[0],
            expand_bias[0].reshape(-1, width),
        ],
        0,
    )
    filled = small.shape[0]
    small = jnp.pad(small, ((0, -filled % 16), (0, 0)))
    got_attend = swap_sections(sent_blocks[0])
    got_attend, sent_expand = lax.optimization_barrier((got_attend, sent_blocks[1]))
    x0_full, gy_full, vectors, got_expand, got_contract = start_call(
        1, tokens, cotangent, small, sent_expand, units[2], columns
    )

    def gather_blocks(block):
        return lax.all_gather(block, "row", axis=0, tiled=True)

    half = units[2].shape[1] // 2
    mats = [[], []]
    for own, got in ((kept_blocks[0], got_attend), (kept_blocks[1], got_expand)):
        for layer, block in enumerate((pick(own, got), pick(got, own))):
            mats[layer].append(gather_blocks(block))
    mats[0].append(gather_blocks(pick(kept_blocks[2], got_contract[:, half:])))
    mats[1].append(gather_blocks(pick(got_contract, units[2])))
    vectors = vectors.astype(WIDE)
    wide_vectors = jnp.swapaxes(vectors[:, :, :6], 1, 2).reshape(2, 6, size)
    wide_vectors = jnp.pad(wide_vectors, ((0, 0), (0, 2), (0, 0)))
    own_vectors = lax.dynamic_index_in_dim(vectors, column, 1, keepdims=False)
    attend_biases = jnp.stack(
        [own_vectors[:, 6], jnp.zeros_like(own_vectors[:, 6]), own_vectors[:, 7]], 1
    ).reshape(2, 1, 3 * width)
    expand_biases = own_vectors[:, 8:filled].reshape(2, 1, -1)

    def own_rows(full):
        return lax.dynamic_slice_in_dim(full, column * rows, rows, 0)

    def own_features(full):
        return lax.dynamic_slice_in_dim(full, column * width, width, 1)

    attn = (mats[0][0], swap_sections(mats[0][0]))
    x = x0_full
    kept, pairs = [], []
    owns = [own_rows(x0_full)]
    for layer in range(2):
        last = layer == 1
        vec = wide_vectors[layer]
        (full, normed, heads, o, lse, hidden, second_own), (other,) = attend_call(
            2 + 3 * layer, not last, x, attn, vec, attend_biases[layer], rows, width, [mats[layer][1]]
        )
        expand = (mats[layer][1], other)
        outs, others = widen_call(
            3 + 3 * layer, second_own, expand, expand_biases[layer],
            gy_full if last else None, [] if last else [mats[0][2]],
        )
        second, active, slope = outs[:3]
        contract = (mats[layer][2], mats[layer][2] if last else others[0])
        if last:
            c1 = outs[3]
        pairs.append((attn, expand, contract))
        kept.append((normed, heads, o, lse, hidden, second, active, slope))
        if not last:
            (x,), others = contract_call(4, active, hidden, contract, vec, [mats[1][0]])
            owns.append(x)
            attn = (mats[1][0], others[0])
    y0 = own_features(full)

    def scatter(total):
        return lax.psum_scatter(total, "row", scatter_dimension=0, tiled=True)

    def tie(value, then):
        return lax.optimization_barrier((value, then))

    attn, expand, contract = pairs[1]
    normed, heads, o, lse, hidden, second, active, slope = kept[1]
    (grad_hidden, low, expand_sums1, e1, y1), _ = late_expand_call(
        8, active, hidden, contract, expand, gy_full, slope, second, wide_vectors[1], []
    )
    layer_low, layer_high = pick(y0, y1), pick(y1, y0)
    (gx1_own, attend_sums1, w1), (layer_got,) = late_attend_call(
        10, low, grad_hidden, owns[1], attn, normed, heads, o, lse, wide_vectors[1], [layer_high]
    )
    layer_outputs = jnp.concatenate([pick(layer_low, layer_got), pick(layer_got, layer_low)], 0)

    attn, expand, contract = pairs[0]
    normed, heads, o, lse, hidden, second, active, slope = kept[0]
    part_c1 = scatter(c1)
    (grad_hidden, low, expand_sums0, ek0, es0, gx1_full, total_c0), (far_c1,) = expand_back_call(
        12, gx1_own, contract, expand, slope, active, second, hidden, wide_vectors[0], [part_c1]
    )
    part_e1, low = tie(scatter(e1), low)
    mixed, outer, total_e0 = scores_back_call(14, low, attn, heads, o, lse, ek0, es0)
    part_w1, mixed = tie(scatter(w1), mixed)
    part_c0, mixed = tie(scatter(total_c0), mixed)
    total_w0, gx0_own, attend_sums0 = attend_back_call(
        15, mixed, outer, grad_hidden, owns[0], attn, normed, wide_vectors[0]
    )
    part_e0 = scatter(total_e0)
    input_grads, small_grads, far_e1, far_w1, far_c0, far_e0 = finish_call(
        16,
        (part_e1, part_w1),
        (part_c0, part_e0),
        gx0_own,
        own_features(gx1_full),
        (attend_sums0, expand_sums0, attend_sums1, expand_sums1),
        lax.axis_size("row"),
    )

    part_w0, small_grads = tie(scatter(total_w0), small_grads)
    far_w0 = lax.ppermute(part_w0, "section", [(1, 0)])

    units = []
    for late, far_late, early, far_early in (
        (part_w1, far_w1, part_w0, far_w0),
        (part_e1, far_e1, part_e0, far_e0),
        (part_c1, far_c1, part_c0, far_c0),
    ):
        whole = jnp.concatenate([early, far_early], 1).astype(WIDE)
        units.append(pick(whole, late.astype(WIDE) + far_late.astype(WIDE)))
    attn_part, expand_part, contract_part = units

    return (
        layer_outputs[None],
        input_grads[None],
        small_grads[0:1],
        small_grads[1:2],
        attn_part[:, : 3 * width].reshape(block_rows, 3, width)[None],
        small_grads[8:10][None],
        attn_part[:, 3 * width :].T[None],
        small_grads[2:3],
        small_grads[3:4],
        small_grads[4:5],
        expand_part[None],
        small_grads[10 : 10 + expand_bias.shape[1] // width].reshape(1, -1),
        contract_part.T[None],
        small_grads[5:6],
    )


def solution(mesh):
    return jax.shard_map(
        on_device,
        mesh=mesh,
        in_specs=(
            P("row", "col"),
            P("row", "col"),
            P("section", "col"),
            P("section", "col"),
            P("section", "row", None, "col"),
            P("section", None, "col"),
            P("section", "col", "row"),
            P("section", "col"),
            P("section", "col"),
            P("section", "col"),
            P("section", "row", "col"),
            P("section", "col"),
            P("section", "col", "row"),
            P("section", "col"),
        ),
        out_specs=(
            P("section", "row", "col"),
            P("section", "row", "col"),
            P("section", "col"),
            P("section", "col"),
            P("section", "row", None, "col"),
            P("section", None, "col"),
            P("section", "col", "row"),
            P("section", "col"),
            P("section", "col"),
            P("section", "col"),
            P("section", "row", "col"),
            P("section", "col"),
            P("section", "col", "row"),
            P("section", "col"),
        ),
        check_vma=False,
    )
```

```python
import functools

import jax
import jax.numpy as jnp
from jax import lax
from jax.experimental import pallas as pl
from jax.experimental.pallas import tpu as pltpu
from jax.sharding import PartitionSpec as P

HEAD = 64
LENGTH = 1024
EPS = 1e-05
LOW = jnp.bfloat16
WIDE = jnp.float32
MESH = pl.DeviceIdType.MESH
PARTS = 2
TILE = 256
MEBI = 1024 * 1024
GRANT = 58 * MEBI


def nn(left, right):
    return lax.dot_general(left, right, (((1,), (0,)), ((), ())), preferred_element_type=WIDE)


def nt(left, right):
    return lax.dot_general(left, right, (((1,), (1,)), ((), ())), preferred_element_type=WIDE)


def tn(left, right):
    return lax.dot_general(left, right, (((0,), (0,)), ((), ())), preferred_element_type=WIDE)


def normalise(values):
    center = jnp.mean(values, axis=1, keepdims=True)
    centred = values - center
    scale = lax.rsqrt(jnp.mean(centred * centred, axis=1, keepdims=True) + EPS)
    return centred * scale, scale


def norm_backward(grad, hat, scale, gain):
    scaled = grad * gain
    mean_one = jnp.mean(scaled, axis=1, keepdims=True)
    mean_two = jnp.mean(scaled * hat, axis=1, keepdims=True)
    return scale * (scaled - mean_one - hat * mean_two)


class Group:
    def __init__(self, rows):
        self.me = lax.axis_index("col")
        chip, core = self.me // 2, self.me % 2
        self.sib = chip * 2 + 1 - core
        self.peer = (1 - chip) * 2 + core
        self.diag = (1 - chip) * 2 + 1 - core
        self.rows = rows
        self.part = rows // PARTS
        self.loads, self.stores, self.begun = {}, {}, set()

    def need(self, *places):
        for place in places:
            self.loads[place].wait()

    def emit(self, *places):
        for place in places:
            self.stores[place].start()
            self.begun.add(place)

    def greet(self, swaps, diagonal, rows=()):
        barrier = pltpu.get_barrier_semaphore()
        others = [{"col": self.sib}, {"col": self.peer}]
        if diagonal:
            others.append({"col": self.diag})
        if swaps:
            others.append({"section": 1 - lax.axis_index("section")})
        others += [{"row": row} for row in rows]
        for other in others:
            pl.semaphore_signal(barrier, inc=1, device_id=other, device_id_type=MESH)
        pl.semaphore_wait(barrier, len(others))

    def slab(self, owner, j):
        return pl.ds(pl.multiple_of(owner * self.rows + j * self.part, self.part), self.part)

    def chunk(self, owner):
        return pl.ds(pl.multiple_of(owner * self.rows, self.rows), self.rows)


def push(src, dst, sems, slot, target, axis="col"):
    return pltpu.make_async_remote_copy(
        src_ref=src,
        dst_ref=dst,
        send_sem=sems.at[0, slot],
        recv_sem=sems.at[1, slot],
        device_id={axis: target},
        device_id_type=MESH,
    )


class Gather:
    def __init__(self, group, full, sems, blocks=False):
        self.group, self.full, self.sems, self.blocks = group, full, sems, blocks

    def piece(self, owner, j):
        if not self.blocks:
            return self.full.at[self.group.slab(owner, j)]
        part = self.full.shape[1] // PARTS
        return self.full.at[owner, pl.ds(j * part, part)]

    def start(self):
        g = self.group
        self.over, self.near, self.relayed = [], [], []
        for j in range(PARTS):
            piece = self.piece(g.me, j)
            self.over.append(push(piece, piece, self.sems, j, g.peer))
            self.over[-1].start()
        for j in range(PARTS):
            piece = self.piece(g.me, j)
            self.near.append(push(piece, piece, self.sems, PARTS + j, g.sib))
            self.near[-1].start()

    def sibling(self):
        for copy in self.near:
            copy.wait_recv()

    def relay(self):
        g = self.group
        for j in range(PARTS):
            self.over[j].wait_recv()
            piece = self.piece(g.peer, j)
            self.relayed.append(push(piece, piece, self.sems, 2 * PARTS + j, g.sib))
            self.relayed[-1].start()

    def diagonal(self):
        for copy in self.relayed:
            copy.wait_recv()

    def done(self):
        for copy in self.over + self.near + self.relayed:
            copy.wait_send()

    def each(self, body, first=None):
        g = self.group
        self.start()
        if first is not None:
            first()
        body(g.chunk(g.me))
        self.sibling()
        body(g.chunk(g.sib))
        self.relay()
        body(g.chunk(g.peer))
        self.diagonal()
        body(g.chunk(g.diag))
        self.done()


class Scatter:
    def __init__(self, group, stage, land, total, sems):
        self.group, self.stage, self.land, self.total, self.sems = group, stage, land, total, sems

    def start(self, part):
        g, stage, land = self.group, self.stage, self.land
        self.first, self.over, self.near = [], [], []
        def split(owner):
            whole = part(g.chunk(owner))
            return [whole[j * g.part : (j + 1) * g.part] for j in range(PARTS)]

        for j, mine in enumerate(split(g.diag)):
            stage[0, j] = mine.astype(LOW)
            self.first.append(push(stage.at[0, j], land.at[0, j], self.sems, j, g.sib))
            self.first[-1].start()
        for j, mine in enumerate(split(g.peer)):
            self.first[j].wait_recv()
            stage[1, j] = (mine + land[0, j].astype(WIDE)).astype(LOW)
            self.over.append(push(stage.at[1, j], land.at[1, j], self.sems, PARTS + j, g.peer))
            self.over[-1].start()
        for j, mine in enumerate(split(g.sib)):
            stage[2, j] = mine.astype(LOW)
            self.near.append(push(stage.at[2, j], land.at[2, j], self.sems, 2 * PARTS + j, g.sib))
            self.near[-1].start()
        for j, mine in enumerate(split(g.me)):
            self.total[j] = mine

    def take(self, j):
        self.near[j].wait_recv()
        self.over[j].wait_recv()
        land = self.land
        return self.total[j] + (land[1, j].astype(WIDE) + land[2, j].astype(WIDE))

    def done(self):
        for copy in self.first + self.over + self.near:
            copy.wait_send()


class Deliver:
    def __init__(self, group, stage, out, sems):
        self.group, self.stage, self.out, self.sems = group, stage, out, sems

    def start(self, rows_ref):
        g, width = self.group, self.out.shape[1]
        for c in range(self.stage.shape[0]):
            self.stage[c] = rows_ref[:, c * width : (c + 1) * width]
        place = self.out.at[g.chunk(g.me)]
        self.copies = [
            push(self.stage.at[other], place, self.sems, n, other)
            for n, other in enumerate((g.peer, g.diag, g.sib))
        ]
        for copy in self.copies:
            copy.start()
        self.out[g.chunk(g.me), :] = self.stage[g.me]

    def done(self):
        for copy in self.copies:
            copy.wait()


def scatter_scratch(rows, width):
    part = rows // PARTS
    return [
        pltpu.VMEM((3, PARTS, part, width), LOW),
        pltpu.VMEM((3, PARTS, part, width), LOW),
        pltpu.VMEM((PARTS, part, width), WIDE),
        pltpu.SemaphoreType.DMA((2, 3 * PARTS)),
    ]


class Halves:
    def __init__(self, pair, whole, sems, slot):
        if pair[0].shape[1] == whole.shape[1]:
            self.copies = [pltpu.make_async_copy(pair[0], whole, sems.at[slot])]
            return
        section = lax.axis_index("section")
        half = whole.shape[1] // 2
        self.copies = []
        for n, place in enumerate((section, 1 - section)):
            columns = pl.ds(pl.multiple_of(place * half, half), half)
            self.copies.append(
                pltpu.make_async_copy(pair[n], whole.at[:, columns], sems.at[slot + n])
            )

    def start(self):
        for copy in self.copies:
            copy.start()

    def wait(self):
        for copy in self.copies:
            copy.wait()


class Trade:
    def __init__(self, keep, send, got, sems):
        self.keep, self.send, self.got, self.sems = keep, send, got, sems
        self.tiles = keep.shape[0] // TILE

    def copy(self, n):
        rows = pl.ds(pl.multiple_of(n * TILE, TILE), TILE)
        return push(
            self.send.at[rows], self.got.at[rows], self.sems, n, 1 - lax.axis_index("section"), "section"
        )

    def start(self, make):
        @pl.loop(0, self.tiles)
        def _(n):
            make(pl.ds(pl.multiple_of(n * TILE, TILE), TILE))
            self.copy(n).start()

    def finish(self):
        @pl.loop(0, self.tiles)
        def _(n):
            self.copy(n).wait()

        add_into(self.keep, self.got)


def add_into(keep_ref, got_ref):
    @pl.loop(0, keep_ref.shape[0] // TILE)
    def _(n):
        rows = pl.ds(pl.multiple_of(n * TILE, TILE), TILE)
        keep_ref[rows, :] = (keep_ref[rows, :].astype(WIDE) + got_ref[rows, :].astype(WIDE)).astype(LOW)


def attention_out(heads_ref, o3, lse_ref, heads):
    length = heads_ref.shape[1]
    size = min(TILE, length)

    @pl.loop(0, heads)
    def _(h):
        for i in range(length // size):
            rows = slice(i * size, (i + 1) * size)
            finish = (i + 1) * size
            queries = heads_ref[h, rows, :]
            scores = nt(heads_ref[heads + h, :finish, :], queries)
            keep = lax.broadcasted_iota(jnp.int32, (size, size), 0) <= lax.broadcasted_iota(
                jnp.int32, (size, size), 1
            )
            last = jnp.where(keep, scores[finish - size :], -1000000000.0)
            scores = last if i == 0 else jnp.concatenate([scores[: finish - size], last], 0)
            highest = jnp.max(scores, axis=0, keepdims=True)
            powers = jnp.exp(scores - highest)
            summed = jnp.sum(powers, axis=0, keepdims=True)
            mixed = tn(heads_ref[2 * heads + h, :finish, :], powers.astype(LOW))
            o3[h, rows, :] = (mixed / summed).T.astype(LOW)
            lse_ref[pl.ds(h, 1), rows] = highest + jnp.log(summed)


def attention_back(heads_ref, go3, lse_ref, dots_ref, g3, key_acc, value_acc, heads):
    length = heads_ref.shape[1]
    size = min(TILE, length)

    @pl.loop(0, heads)
    def _(h):
        for i in reversed(range(length // size)):
            rows = slice(i * size, (i + 1) * size)
            finish = (i + 1) * size
            queries = heads_ref[h, rows, :]
            keys = heads_ref[heads + h, :finish, :]
            grads = go3[h, rows, :]
            scores = nt(keys, queries) - lse_ref[pl.ds(h, 1), rows]
            keep = lax.broadcasted_iota(jnp.int32, (size, size), 0) <= lax.broadcasted_iota(
                jnp.int32, (size, size), 1
            )
            last = jnp.where(keep, scores[finish - size :], -1000000000.0)
            scores = last if i == 0 else jnp.concatenate([scores[: finish - size], last], 0)
            probs = jnp.exp(scores)
            grad_probs = nt(heads_ref[2 * heads + h, :finish, :], grads)
            grad_scores = (probs * (grad_probs - dots_ref[pl.ds(h, 1), rows])).astype(LOW)
            g3[h, rows, :] = (tn(grad_scores, keys) * HEAD ** (-0.5)).astype(LOW)
            key_part = nn(grad_scores, queries)
            value_part = nn(probs.astype(LOW), grads)
            if finish == length:
                key_acc[...] = key_part
                value_acc[...] = value_part
            else:
                key_acc[:finish, :] += key_part
                value_acc[:finish, :] += value_part
        g3[heads + h] = key_acc[...].astype(LOW)
        g3[2 * heads + h] = value_acc[...].astype(LOW)


def start_kernel(
    tokens_ref, cotangent_ref, small_ref, expand_ref, contract_ref,
    x_ref, g_ref, vectors_ref, got_expand_ref, got_contract_ref,
    x4, g4, s4, other4, x_sems, g_sems, s_sems, local_sems,
):
    section = lax.axis_index("section")
    group = Group(x_ref.shape[0] // 4)
    length = x_ref.shape[0]
    loads = []
    rows = pl.ds(pl.multiple_of(section * length, length), length)
    for n, (source, into) in enumerate(((tokens_ref.at[rows], x4), (cotangent_ref.at[rows], g4), (small_ref, s4))):
        loads.append(pltpu.make_async_copy(source, into.at[group.me], local_sems.at[n]))
        loads[-1].start()
    group.greet(True, False)
    blocks = [
        push(source, into, s_sems, 3 * PARTS + 1 + n, 1 - section, "section")
        for n, (source, into) in enumerate(((expand_ref, got_expand_ref), (contract_ref, got_contract_ref)))
    ]
    for block in blocks:
        block.start()
    gathers = [Gather(group, x4, x_sems, True), Gather(group, s4, s_sems, True), Gather(group, g4, g_sems, True)]
    for gather, load in zip(gathers, (loads[0], loads[2], loads[1])):
        load.wait()
        gather.start()
    for gather in gathers:
        gather.sibling()
        gather.relay()
        gather.diagonal()
    swap = push(s4, other4, s_sems, 3 * PARTS, 1 - section, "section")
    swap.start()
    width = x4.shape[2]
    for c in range(x4.shape[0]):
        x_ref[:, c * width : (c + 1) * width] = x4[c]
        g_ref[:, c * width : (c + 1) * width] = g4[c]
    swap.wait()
    for block in blocks:
        block.wait()
    vectors_ref[section] = s4[...]
    vectors_ref[1 - section] = other4[...]
    for gather in gathers:
        gather.done()


def attend_kernel(
    gathered, heads, group, x_ref, mine_ref, other_ref, vec_ref, bias_ref,
    full_ref, normed_ref, heads_ref, o_ref, lse_ref, hidden_ref, second_ref,
    weight, o3, stage, land, total, scatter_sems, gather_sems, local_sems,
):
    width = o_ref.shape[1]
    halves = Halves((mine_ref, other_ref), weight, local_sems, 0)
    halves.start()
    if not gathered:
        full_ref[group.chunk(group.me), :] = x_ref[...]
    halves.wait()

    def project(rows):
        values = (x_ref if gathered else full_ref)[rows, :].astype(WIDE)
        hat, _ = normalise(values)
        normed = (hat * vec_ref[0:1, :] + vec_ref[1:2, :]).astype(LOW)
        normed_ref[rows, :] = normed
        mixed = nn(normed, weight[:, : 3 * width]) + bias_ref[...]
        for j in range(3 * heads):
            piece = mixed[:, j * HEAD : (j + 1) * HEAD]
            if j < heads:
                piece = piece * HEAD ** (-0.5)
            heads_ref[j, rows, :] = piece.astype(LOW)

    if gathered:
        full_ref[...] = jnp.zeros_like(full_ref)

        @pl.loop(0, LENGTH // group.rows)
        def _(n):
            project(group.chunk(n))
    else:
        Gather(group, full_ref, gather_sems).each(project)
    group.emit(0, 1, 2)

    attention_out(heads_ref, o3, lse_ref, heads)
    for h in range(heads):
        o_ref[:, h * HEAD : (h + 1) * HEAD] = o3[h]
    group.emit(3, 4)

    scatter = Scatter(group, stage, land, total, scatter_sems)
    scatter.start(lambda rows: nt(o_ref[rows, :], weight[:, 3 * width :]))
    for j in range(PARTS):
        rows = slice(j * group.part, (j + 1) * group.part)
        residual = (x_ref if gathered else full_ref)[group.slab(group.me, j), :].astype(WIDE)
        hidden = residual + scatter.take(j) + vec_ref[2:3, :]
        hidden_ref[rows, :] = hidden
        hat, _ = normalise(hidden)
        second_ref[rows, :] = (hat * vec_ref[3:4, :] + vec_ref[4:5, :]).astype(LOW)
    scatter.done()


def outer_whole(left_ref, right_ref, out_ref):
    @pl.loop(0, left_ref.shape[1] // TILE)
    def _(n):
        rows = pl.ds(pl.multiple_of(n * TILE, TILE), TILE)
        out_ref[rows, :] = tn(left_ref[:, rows], right_ref[...]).astype(LOW)


def widen_kernel(last, group, second_ref, em_ref, eo_ref, bias_ref, *refs):
    if last:
        g_ref, *refs = refs
    full_ref, active_ref, slope_ref, *refs = refs
    if last:
        c_ref, *refs = refs
    expand, gather_sems, local_sems = refs
    halves = Halves((em_ref, eo_ref), expand, local_sems, 0)
    halves.start()
    full_ref[group.chunk(group.me), :] = second_ref[...]
    halves.wait()

    def widen(rows):
        t = nn(full_ref[rows, :], expand[...]) + bias_ref[...]
        square = t * t
        bent = jnp.tanh(0.7978845608028654 * t * (1.0 + 0.044715 * square))
        active_ref[rows, :] = (0.5 * t * (1.0 + bent)).astype(LOW)
        slope_ref[rows, :] = (
            0.5 * (1.0 + bent)
            + (0.5 * 0.7978845608028654) * t * (1.0 - bent * bent) * (1.0 + 3 * 0.044715 * square)
        ).astype(LOW)

    Gather(group, full_ref, gather_sems).each(widen)
    if last:
        group.emit(0, 1, 2)
        group.need(4)
        outer_whole(g_ref, active_ref, c_ref)


def outer_halves(left_ref, right_ref, keep_ref, send_ref):
    section = lax.axis_index("section")
    half = right_ref.shape[1] // 2
    for place, out in ((section, keep_ref), (1 - section, send_ref)):
        columns = pl.ds(pl.multiple_of(place * half, half), half)

        @pl.loop(0, left_ref.shape[1] // TILE)
        def _(n):
            rows = pl.ds(pl.multiple_of(n * TILE, TILE), TILE)
            out[rows, :] = tn(left_ref[:, rows], right_ref[:, columns]).astype(LOW)


def contract_kernel(
    group, active_ref, hidden_ref, cm_ref, co_ref, vec_ref, result_ref,
    contract, stage, land, total, scatter_sems, local_sems,
):
    halves = Halves((cm_ref, co_ref), contract, local_sems, 0)
    halves.start()
    halves.wait()
    scatter = Scatter(group, stage, land, total, scatter_sems)
    scatter.start(lambda rows: nt(active_ref[rows, :], contract[...]))
    group.need(1)
    for j in range(PARTS):
        rows = slice(j * group.part, (j + 1) * group.part)
        result = hidden_ref[rows, :] + scatter.take(j) + vec_ref[5:6, :]
        result_ref[rows, :] = result.astype(LOW)
    scatter.done()


def narrow_grads(group, scatter, full_ref, hidden_ref, vec_ref, grad_ref, low_ref, sums_ref):
    for j in range(PARTS):
        rows = slice(j * group.part, (j + 1) * group.part)
        grad = scatter.take(j)
        hat, scale = normalise(hidden_ref[rows, :])
        own = full_ref[group.slab(group.me, j), :].astype(WIDE)
        out = own + norm_backward(grad, hat, scale, vec_ref[3:4, :])
        grad_ref[rows, :] = out
        low_ref[rows, :] = out.astype(LOW)
        for n, term in enumerate((grad * hat, grad, own, out)):
            sums_ref[n : n + 1, :] += jnp.sum(term, axis=0, keepdims=True)


def bend(rows, full_ref, contract, slope_ref, before, sums_ref):
    grad = (nn(full_ref[rows, :], contract[...]) * slope_ref[rows, :].astype(WIDE)).astype(LOW)
    before[rows, :] = grad
    sums_ref[4:5, :] += jnp.sum(grad.astype(WIDE), axis=0, keepdims=True)


def late_expand_kernel(
    group, active_ref, hidden_ref, cm_ref, co_ref, em_ref, eo_ref, g_ref, slope_ref, second_ref, vec_ref,
    grad_ref, low_ref, sums_ref, e_ref, out_ref,
    contract, expand, before, result, stage4,
    stage_a, land_a, total_a, sems_a, stage, land, total, scatter_sems, deliver_sems, local_sems,
):
    first = Halves((cm_ref, co_ref), contract, local_sems, 0)
    then = Halves((em_ref, eo_ref), expand, local_sems, 2)
    first.start()
    then.start()
    sums_ref[...] = jnp.zeros_like(sums_ref)
    first.wait()
    forward = Scatter(group, stage_a, land_a, total_a, sems_a)
    forward.start(lambda rows: nt(active_ref[rows, :], contract[...]))
    group.need(6, 7)

    @pl.loop(0, LENGTH // group.rows)
    def _(n):
        bend(group.chunk(n), g_ref, contract, slope_ref, before, sums_ref)

    then.wait()
    scatter = Scatter(group, stage, land, total, scatter_sems)
    scatter.start(lambda rows: nt(before[rows, :], expand[...]))
    group.need(1)
    for j in range(PARTS):
        rows = slice(j * group.part, (j + 1) * group.part)
        result[rows, :] = (hidden_ref[rows, :] + forward.take(j) + vec_ref[5:6, :]).astype(LOW)
    deliver = Deliver(group, stage4, out_ref, deliver_sems)
    deliver.start(result)
    group.need(8)
    outer_whole(second_ref, before, e_ref)
    group.emit(3)
    narrow_grads(group, scatter, g_ref, hidden_ref, vec_ref, grad_ref, low_ref, sums_ref)
    group.emit(0, 1, 2)
    forward.done()
    scatter.done()
    deliver.done()


def expand_back_kernel(
    group, g_ref, cm_ref, co_ref, em_ref, eo_ref, slope_ref, active_ref, second_ref, hidden_ref, vec_ref,
    grad_ref, low_ref, sums_ref, ek_ref, es_ref, full_ref, c_ref,
    contract, expand, before, stage, land, total, scatter_sems, gather_sems, local_sems, outer, got, trade_sems,
):
    section = lax.axis_index("section")
    first = Halves((cm_ref, co_ref), contract, local_sems, 0)
    then = Halves((em_ref, eo_ref), expand, local_sems, 2)
    first.start()
    then.start()
    sums_ref[...] = jnp.zeros_like(sums_ref)
    full_ref[group.chunk(group.me), :] = g_ref[...]
    first.wait()
    Gather(group, full_ref, gather_sems).each(
        lambda rows: bend(rows, full_ref, contract, slope_ref, before, sums_ref), lambda: group.need(5)
    )
    group.emit(5)
    group.need(6)
    half = active_ref.shape[1] // 2

    def columns(place):
        return pl.ds(pl.multiple_of(place * half, half), half)

    def make(n):
        def tile(rows):
            place = section if n == 0 else 1 - section
            outer[n, rows, :] = tn(full_ref[:, rows], active_ref[:, columns(place)]).astype(LOW)

        return tile

    trade = Trade(outer.at[0], outer.at[1], got, trade_sems)
    trade.start(make(1))
    then.wait()
    scatter = Scatter(group, stage, land, total, scatter_sems)
    scatter.start(lambda rows: nt(before[rows, :], expand[...]))
    group.need(7)
    outer_halves(second_ref, before, ek_ref, es_ref)
    group.emit(3, 4)
    keep = make(0)

    @pl.loop(0, outer.shape[1] // TILE)
    def _(n):
        keep(pl.ds(pl.multiple_of(n * TILE, TILE), TILE))

    group.need(8)
    narrow_grads(group, scatter, full_ref, hidden_ref, vec_ref, grad_ref, low_ref, sums_ref)
    group.emit(0, 1, 2)
    scatter.done()
    trade.finish()
    store = pltpu.make_async_copy(outer.at[0], c_ref, local_sems.at[0])
    store.start()
    store.wait()


def scores_back(group, heads, low_ref, weight, heads_ref, o_ref, lse_ref, full, go3, dots, g3, accs, mixed, gather_sems, needs):
    width = o_ref.shape[1]
    picks = (
        lax.broadcasted_iota(jnp.int32, (8, width), 1) // HEAD
        == lax.broadcasted_iota(jnp.int32, (8, width), 0)
    ).astype(WIDE)

    def spread(rows):
        grads = nn(full[rows, :], weight[:, 3 * width :]).astype(LOW)
        for h in range(heads):
            go3[h, rows, :] = grads[:, h * HEAD : (h + 1) * HEAD]
        term = grads.astype(WIDE) * o_ref[rows, :].astype(WIDE)
        dots[:, rows] = lax.dot_general(
            picks,
            term,
            (((1,), (1,)), ((), ())),
            precision=lax.Precision.HIGHEST,
            preferred_element_type=WIDE,
        )

    full[group.chunk(group.me), :] = low_ref[...]
    Gather(group, full, gather_sems).each(spread, lambda: group.need(needs[0]))
    group.need(*needs[1:])
    attention_back(heads_ref, go3, lse_ref, dots, g3, *accs, heads)
    for j in range(3 * heads):
        mixed[:, j * HEAD : (j + 1) * HEAD] = g3[j]


def outer_out(full, o_ref, outer_ref):
    @pl.loop(0, outer_ref.shape[0] // TILE)
    def _(n):
        rows = pl.ds(pl.multiple_of(n * TILE, TILE), TILE)
        outer_ref[rows, :] = tn(full[:, rows], o_ref[...]).astype(LOW)


def attend_grads(group, scatter, x_ref, grad_ref, vec_ref, mixed, width, out_ref, sums_ref):
    sums_ref[2:3, : 3 * width] = jnp.sum(mixed[...].astype(WIDE), axis=0, keepdims=True)
    for j in range(PARTS):
        rows = slice(j * group.part, (j + 1) * group.part)
        grad = scatter.take(j)
        hat, scale = normalise(x_ref[rows, :].astype(WIDE))
        out = grad_ref[rows, :] + norm_backward(grad, hat, scale, vec_ref[0:1, :])
        out_ref[rows, :] = out.astype(LOW)
        for n, term in enumerate((grad * hat, grad)):
            sums_ref[n : n + 1, :] += jnp.sum(term, axis=0, keepdims=True)


def late_attend_kernel(
    heads, group, low_ref, grad_ref, x_ref, mine_ref, other_ref, normed_ref, heads_ref, o_ref, lse_ref, vec_ref,
    out_ref, sums_ref, w_ref,
    weight, full, go3, dots, g3, key_acc, value_acc, mixed, outer, outer_o,
    stage, land, total, scatter_sems, gather_sems, local_sems,
):
    width = o_ref.shape[1]
    halves = Halves((mine_ref, other_ref), weight, local_sems, 0)
    halves.start()
    sums_ref[...] = jnp.zeros_like(sums_ref)
    halves.wait()
    scores_back(
        group, heads, low_ref, weight, heads_ref, o_ref, lse_ref, full, go3, dots, g3,
        (key_acc, value_acc), mixed, gather_sems, (7, 6, 8),
    )
    scatter = Scatter(group, stage, land, total, scatter_sems)
    scatter.start(lambda rows: nt(mixed[rows, :], weight[:, : 3 * width]))
    outer_out(full, o_ref, outer_o)
    group.need(5)

    @pl.loop(0, weight.shape[0] // TILE)
    def _(n):
        rows = pl.ds(pl.multiple_of(n * TILE, TILE), TILE)
        outer[rows, : 3 * width] = tn(normed_ref[:, rows], mixed[...]).astype(LOW)
        outer[rows, 3 * width :] = outer_o[rows, :]

    store = pltpu.make_async_copy(outer, w_ref, local_sems.at[2])
    store.start()
    group.need(1, 2)
    attend_grads(group, scatter, x_ref, grad_ref, vec_ref, mixed, width, out_ref, sums_ref)
    scatter.done()
    store.wait()


def scores_back_kernel(
    heads, group, low_ref, mine_ref, other_ref, heads_ref, o_ref, lse_ref, ek_ref, es_ref,
    mixed, outer_ref, e_ref,
    weight, full, go3, dots, g3, key_acc, value_acc, got, gather_sems, local_sems, swap_sems,
):
    swap = push(es_ref, got, swap_sems, 0, 1 - lax.axis_index("section"), "section")
    swap.start()
    halves = Halves((mine_ref, other_ref), weight, local_sems, 0)
    halves.start()
    halves.wait()
    scores_back(
        group, heads, low_ref, weight, heads_ref, o_ref, lse_ref, full, go3, dots, g3,
        (key_acc, value_acc), mixed, gather_sems, (4, 3, 5),
    )
    group.emit(0)
    outer_out(full, o_ref, outer_ref)
    group.emit(1)
    group.need(6)
    swap.wait()
    add_into(ek_ref, got)
    store = pltpu.make_async_copy(ek_ref, e_ref, local_sems.at[0])
    store.start()
    store.wait()


def attend_back_kernel(
    group, mixed, outer_ref, grad_ref, x_ref, mine_ref, other_ref, normed_ref, vec_ref,
    w_ref, out_ref, sums_ref,
    weight, outer, got, stage, land, total, scatter_sems, local_sems, swap_sems,
):
    width = outer_ref.shape[1]
    section = lax.axis_index("section")
    halves = Halves((mine_ref, other_ref), weight, local_sems, 0)
    halves.start()
    sums_ref[...] = jnp.zeros_like(sums_ref)
    half = weight.shape[1] // 2
    scatter = Scatter(group, stage, land, total, scatter_sems)
    group.need(1, 6)

    def make(n):
        place = section if n == 0 else 1 - section

        def tile(rows):
            @pl.when(place == 0)
            def _():
                outer[n, rows, :] = tn(normed_ref[:, rows], mixed[:, :half]).astype(LOW)

            @pl.when(place == 1)
            def _():
                outer[n, rows, : 3 * width - half] = tn(normed_ref[:, rows], mixed[:, half:]).astype(LOW)
                outer[n, rows, 3 * width - half :] = outer_ref[rows, :]

        return tile

    trade = Trade(outer.at[0], outer.at[1], got, swap_sems)
    trade.start(make(1))
    halves.wait()
    scatter.start(lambda rows: nt(mixed[rows, :], weight[:, : 3 * width]))
    keep = make(0)

    @pl.loop(0, outer.shape[1] // TILE)
    def _(n):
        keep(pl.ds(pl.multiple_of(n * TILE, TILE), TILE))

    group.need(2, 3)
    attend_grads(group, scatter, x_ref, grad_ref, vec_ref, mixed, width, out_ref, sums_ref)
    group.emit(1, 2)
    scatter.done()
    trade.finish()
    store = pltpu.make_async_copy(outer.at[0], w_ref, local_sems.at[2])
    store.start()
    store.wait()


class OneWay:
    def __init__(self, up, down, sems):
        self.section = lax.axis_index("section")
        both = [*up, *down]
        copies = [
            push(source, into, sems, n, 1 - self.section, "section")
            for n, (source, into) in enumerate(both)
        ]
        self.up, self.down = copies[: len(up)], copies[len(up) :]

    def each(self, first, second):
        @pl.when(self.section == 0)
        def _():
            first(self.up)
            second(self.down)

        @pl.when(self.section == 1)
        def _():
            first(self.down)
            second(self.up)

    def start(self):
        self.each(lambda copies: [copy.start() for copy in copies], lambda copies: None)

    def wait(self):
        self.each(
            lambda copies: [copy.wait_send() for copy in copies],
            lambda copies: [copy.wait_recv() for copy in copies],
        )


def finish_kernel(
    late_ref, early1_ref, early2_ref, near_ref, far_ref, a0, n0, a1, n1,
    grads_ref, sums_ref, got_late, got_early1, got_early2,
    mine, stage4, block, land_col, land_x, land_z, land,
    deliver_sems, col_sems, x_sems, z_sems, part_sems,
):
    section, row = lax.axis_index("section"), lax.axis_index("row")
    away = 1 - section
    group = Group(near_ref.shape[0])
    length, width = far_ref.shape
    others = [lax.rem(row + d, land_z.shape[0]) for d in range(1, land_z.shape[0])]
    group.greet(True, True, others)
    gradient_up = OneWay([(far_ref, land)], [], x_sems.at[:, pl.ds(1, 1)])
    gradient_down = OneWay([], [(mine, land)], x_sems.at[:, pl.ds(2, 1)])
    parts = OneWay(
        [(late_ref, got_late)], [(early1_ref, got_early1), (early2_ref, got_early2)], part_sems
    )
    deliver = Deliver(group, stage4, mine, deliver_sems)
    deliver.start(near_ref)
    gradient_up.start()

    block[...] = jnp.zeros_like(block)
    for layer, (attn, narrow) in enumerate(((a0, n0), (a1, n1))):
        wide = [attn[0:1, :], attn[1:2, :], narrow[3:4, :], narrow[0:1, :], narrow[1:2, :], narrow[2:3, :]]
        for c in range(block.shape[0]):
            columns = slice(c * width, (c + 1) * width)
            for n, term in enumerate(wide):
                block[c, layer, n : n + 1, :] = term[:, columns]
            for n, term in enumerate((attn[2:3, :width], attn[2:3, 2 * width : 3 * width])):
                block[c, layer, 8 + n : 9 + n, :] = term
            for n in range(narrow.shape[1] // width):
                block[c, layer, 10 + n : 11 + n, :] = narrow[4:5, n * width : (n + 1) * width]
    copies = [
        push(block.at[other, :, pl.ds(0, 8)], land_col.at[n], col_sems, n, other)
        for n, other in enumerate((group.peer, group.diag, group.sib))
    ]
    for copy in copies:
        copy.start()
    for copy in copies:
        copy.wait()
    me = group.me
    block[me, :, :8] = block[me, :, :8] + (land_col[0] + (land_col[1] + land_col[2]))
    swap = push(block.at[me, away], land_x, x_sems, 0, away, "section")
    swap.start()
    deliver.done()
    gradient_down.start()
    parts.start()
    own = pl.ds(pl.multiple_of(section * length, length), length)

    @pl.when(section == 0)
    def _():
        grads_ref[own, :] = mine[...].astype(WIDE)

    @pl.when(section == 1)
    def _():
        grads_ref[own, :] = far_ref[...].astype(WIDE)

    swap.wait()
    land_z[row] = block[me, section] + land_x[...]
    copies = [
        push(land_z.at[row], land_z.at[row], z_sems, n, other, "row")
        for n, other in enumerate(others)
    ]
    for copy in copies:
        copy.start()
    for copy in copies:
        copy.wait()
    result = land_z[0]
    for n in range(1, land_z.shape[0]):
        result = result + land_z[n]
    sums_ref[...] = result
    gradient_up.wait()
    gradient_down.wait()
    grads_ref[pl.ds(pl.multiple_of(away * length, length), length), :] = land[...].astype(WIDE)
    parts.wait()


def last_kernel(up_ref, down_ref, got_up, got_down, sems):
    barrier = pltpu.get_barrier_semaphore()
    other = 1 - lax.axis_index("section")
    pl.semaphore_signal(barrier, inc=1, device_id={"section": other}, device_id_type=MESH)
    pl.semaphore_wait(barrier, 1)
    parts = OneWay([(up_ref, got_up)], [(down_ref, got_down)], sems)
    parts.start()
    parts.wait()


VM = pl.BlockSpec(memory_space=pltpu.VMEM)
ANY = pl.BlockSpec(memory_space=pl.ANY)
PAIRS = pltpu.SemaphoreType.DMA((2, 3 * PARTS))
LOCAL = pltpu.SemaphoreType.DMA((4,))


def shape(dims, kind=LOW):
    return jax.ShapeDtypeStruct(dims, kind)


def launch(
    body, number, rows, in_specs, ins, outs, out_specs, scratch, swaps=(), diagonal=False, across=False, late=(),
):
    n_in, n_out, n = len(ins), len(outs), len(swaps)
    held_in = [i for i in range(n_in) if in_specs[i] is VM]
    held_out = [i for i in range(n_out) if out_specs[i] is VM]

    def kernel(*refs):
        refs = list(refs)
        takes, sources = refs[:n_in], refs[n_in : n_in + n]
        gives = refs[n_in + n : n_in + n + n_out]
        lands = refs[n_in + n + n_out : n_in + 2 * n + n_out]
        rest = refs[n_in + 2 * n + n_out :]
        own, rest = rest[: len(scratch)], rest[len(scratch) :]
        in_held, rest = rest[: len(held_in)], rest[len(held_in) :]
        out_held, rest = rest[: len(held_out)], rest[len(held_out) :]
        in_sems, out_sems, swap_sems = rest
        group = Group(rows)
        for k, i in enumerate(held_in):
            group.loads[i] = pltpu.make_async_copy(takes[i], in_held[k], in_sems.at[k])
            group.loads[i].start()
            takes[i] = in_held[k]
        for k, i in enumerate(held_out):
            group.stores[i] = pltpu.make_async_copy(out_held[k], gives[i], out_sems.at[k])
            gives[i] = out_held[k]
        group.greet(n or across, diagonal)
        other = 1 - lax.axis_index("section")
        copies = [
            push(source, land, swap_sems, i, other, "section")
            for i, (source, land) in enumerate(zip(sources, lands))
        ]
        for copy in copies:
            copy.start()
        group.need(*[i for i in held_in if i not in late])
        body(group, *takes, *gives, *own)
        group.emit(*[i for i in held_out if i not in group.begun])
        for copy in copies:
            copy.wait()
        for i in held_out:
            group.stores[i].wait()

    results = pl.pallas_call(
        kernel,
        out_shape=(*outs, *[shape(s.shape, s.dtype) for s in swaps]),
        in_specs=[ANY] * (n_in + n),
        out_specs=(ANY,) * (n_out + n),
        scratch_shapes=[
            *scratch,
            *[pltpu.VMEM(ins[i].shape, ins[i].dtype) for i in held_in],
            *[pltpu.VMEM(outs[i].shape, outs[i].dtype) for i in held_out],
            pltpu.SemaphoreType.DMA((len(held_in),)),
            pltpu.SemaphoreType.DMA((len(held_out),)),
            pltpu.SemaphoreType.DMA((2, max(n, 1))),
        ],
        compiler_params=pltpu.CompilerParams(
            collective_id=number, has_side_effects=True, vmem_limit_bytes=GRANT
        ),
        cost_estimate=pl.CostEstimate(flops=int(3e10), bytes_accessed=30 * MEBI, transcendentals=0),
    )(*ins, *swaps)
    return results[:n_out], results[n_out:]


def start_call(number, tokens, cotangent, small, expand, contract, columns):
    width = tokens.shape[1]
    size = width * columns
    kinds = small.shape[0]
    outs = (shape((LENGTH, size)), shape((LENGTH, size)), shape((2, columns, kinds, width)), shape(expand.shape), shape(contract.shape))
    blocks = pltpu.VMEM((columns, LENGTH, width), LOW)
    vectors = pltpu.VMEM((columns, kinds, width), LOW)
    return pl.pallas_call(
        start_kernel,
        out_shape=outs,
        in_specs=[ANY] * 5,
        out_specs=(VM, VM, VM, ANY, ANY),
        scratch_shapes=[
            blocks, blocks, vectors, vectors, PAIRS, PAIRS,
            pltpu.SemaphoreType.DMA((2, 3 * PARTS + 3)), LOCAL,
        ],
        compiler_params=pltpu.CompilerParams(
            collective_id=number, has_side_effects=True, vmem_limit_bytes=GRANT
        ),
        cost_estimate=pl.CostEstimate(flops=int(3e10), bytes_accessed=30 * MEBI, transcendentals=0),
    )(tokens, cotangent, small, expand, contract)


def attend_call(number, gathered, x, pair, vec, bias, rows, width, swaps):
    size = vec.shape[1]
    heads = width // HEAD
    outs = (
        shape((LENGTH, size) if not gathered else (16, 128)),
        shape((LENGTH, size)),
        shape((3 * heads, LENGTH, HEAD)),
        shape((LENGTH, width)),
        shape((8, LENGTH), WIDE),
        shape((rows, size), WIDE),
        shape((rows, size)),
    )
    scratch = [
        pltpu.VMEM((size, 4 * width), LOW),
        pltpu.VMEM((heads, LENGTH, HEAD), LOW),
        *scatter_scratch(rows, size), PAIRS, LOCAL,
    ]
    return launch(
        functools.partial(attend_kernel, gathered, heads),
        number, rows, [VM, ANY, ANY, VM, VM], (x, *pair, vec, bias), outs, (VM,) * 7, scratch, swaps,
    )


def widen_call(number, second, pair, bias, grad, swaps):
    rows, size = second.shape
    wide = bias.shape[1]
    last = grad is not None
    ins, in_specs = [second, *pair, bias], [VM, ANY, ANY, VM]
    outs = [shape((LENGTH, size)), shape((LENGTH, wide)), shape((LENGTH, wide))]
    if last:
        ins, in_specs, outs = ins + [grad], in_specs + [VM], outs + [shape((size, wide))]
    scratch = [pltpu.VMEM((size, wide), LOW), PAIRS, LOCAL]
    return launch(
        functools.partial(widen_kernel, last),
        number, rows, in_specs, ins, outs, (VM,) * len(outs), scratch, swaps, late=(4,),
    )


def contract_call(number, active, hidden, pair, vec, swaps):
    rows, size = hidden.shape
    wide = active.shape[1]
    scratch = [pltpu.VMEM((size, wide), LOW), *scatter_scratch(rows, size), LOCAL]
    return launch(
        contract_kernel, number, rows, [VM, VM, ANY, ANY, VM], (active, hidden, *pair, vec),
        [shape((rows, size))], (VM,), scratch, swaps, late=(1,),
    )


def late_expand_call(number, active, hidden, contract, expand, grad, slope, second, vec, swaps):
    rows, size = hidden.shape
    wide = slope.shape[1]
    columns = LENGTH // rows
    outs = [
        shape((rows, size), WIDE), shape((rows, size)), shape((8, size), WIDE),
        shape((size, wide)), shape((LENGTH, size // columns)),
    ]
    scratch = [
        pltpu.VMEM((size, wide), LOW),
        pltpu.VMEM((size, wide), LOW),
        pltpu.VMEM((LENGTH, wide), LOW),
        pltpu.VMEM((rows, size), LOW),
        pltpu.VMEM((columns, rows, size // columns), LOW),
        *scatter_scratch(rows, size), *scatter_scratch(rows, size),
        pltpu.SemaphoreType.DMA((2, 3)), LOCAL,
    ]
    return launch(
        late_expand_kernel,
        number, rows, [VM, VM, ANY, ANY, ANY, ANY, VM, VM, VM, VM],
        (active, hidden, *contract, *expand, grad, slope, second, vec),
        outs, [VM] * 5, scratch, swaps, True, late=(1, 6, 7, 8),
    )


def expand_back_call(number, grad, contract, expand, slope, active, second, hidden, vec, swaps):
    rows, size = hidden.shape
    wide = slope.shape[1]
    half = wide // 2
    outs = [
        shape((rows, size), WIDE), shape((rows, size)), shape((8, size), WIDE),
        shape((size, half)), shape((size, half)), shape((LENGTH, size)), shape((size, half)),
    ]
    scratch = [
        pltpu.VMEM((size, wide), LOW),
        pltpu.VMEM((size, wide), LOW),
        pltpu.VMEM((LENGTH, wide), LOW),
        *scatter_scratch(rows, size), PAIRS, LOCAL,
        pltpu.VMEM((2, size, half), LOW), pltpu.VMEM((size, half), LOW),
        pltpu.SemaphoreType.DMA((2, size // TILE)),
    ]
    return launch(
        expand_back_kernel,
        number, rows, [VM, ANY, ANY, ANY, ANY, VM, VM, VM, VM, VM],
        (grad, *contract, *expand, slope, active, second, hidden, vec),
        outs, [VM] * 6 + [ANY], scratch, swaps, False, True, late=(5, 6, 7, 8),
    )


def scores_scratch(size, width, heads):
    return [
        pltpu.VMEM((size, 4 * width), LOW),
        pltpu.VMEM((LENGTH, size), LOW),
        pltpu.VMEM((heads, LENGTH, HEAD), LOW),
        pltpu.VMEM((8, LENGTH), WIDE),
        pltpu.VMEM((3 * heads, LENGTH, HEAD), LOW),
        pltpu.VMEM((LENGTH, HEAD), WIDE),
        pltpu.VMEM((LENGTH, HEAD), WIDE),
    ]


def late_attend_call(number, low, grad, x_own, pair, normed, heads_all, o, lse, vec, swaps):
    rows, size = grad.shape
    width = o.shape[1]
    heads = width // HEAD
    outs = (shape((rows, size)), shape((8, size), WIDE), shape((size, 4 * width)))
    scratch = [
        *scores_scratch(size, width, heads),
        pltpu.VMEM((LENGTH, 3 * width), LOW),
        pltpu.VMEM((size, 4 * width), LOW),
        pltpu.VMEM((size, width), LOW),
        *scatter_scratch(rows, size), PAIRS, LOCAL,
    ]
    return launch(
        functools.partial(late_attend_kernel, heads),
        number, rows, [VM, VM, VM, ANY, ANY, VM, VM, VM, VM, VM],
        (low, grad, x_own, *pair, normed, heads_all, o, lse, vec),
        outs, (VM, VM, ANY), scratch, swaps, late=(1, 2, 5, 6, 7, 8),
    )


def scores_back_call(number, low, pair, heads_all, o, lse, keep, send):
    rows, size = low.shape
    width = o.shape[1]
    heads = width // HEAD
    outs = (shape((LENGTH, 3 * width)), shape((size, width)), shape(keep.shape))
    scratch = [
        *scores_scratch(size, width, heads),
        pltpu.VMEM(keep.shape, LOW),
        PAIRS, LOCAL, pltpu.SemaphoreType.DMA((2, 1)),
    ]
    return launch(
        functools.partial(scores_back_kernel, heads),
        number, rows, [VM, ANY, ANY, VM, VM, VM, VM, ANY], (low, *pair, heads_all, o, lse, keep, send),
        outs, (VM, VM, ANY), scratch, (), False, True, late=(3, 4, 5, 6),
    )[0]


def attend_back_call(number, mixed, outer, grad, x_own, pair, normed, vec):
    rows, size = grad.shape
    width = outer.shape[1]
    half = 2 * width
    outs = (shape((size, half)), shape((rows, size)), shape((8, size), WIDE))
    scratch = [
        pltpu.VMEM((size, 4 * width), LOW),
        pltpu.VMEM((2, size, half), LOW),
        pltpu.VMEM((size, half), LOW),
        *scatter_scratch(rows, size), LOCAL, pltpu.SemaphoreType.DMA((2, size // TILE)),
    ]
    return launch(
        attend_back_kernel,
        number, rows, [VM, VM, VM, VM, ANY, ANY, VM, VM],
        (mixed, outer, grad, x_own, *pair, normed, vec), outs, (ANY, VM, VM), scratch, (), False, True,
        late=(1, 2, 3, 6),
    )[0]


def finish_call(number, late, early, near, far, sums, row_count):
    rows, size = near.shape
    length, width = far.shape
    columns = length // rows
    outs = (
        shape((2 * length, width), WIDE),
        shape((16, width), WIDE),
        *[shape(part.shape) for part in (*late, *early)],
    )
    scratch = [
        pltpu.VMEM((length, width), LOW),
        pltpu.VMEM((columns, rows, width), LOW),
        pltpu.VMEM((columns, 2, 16, width), WIDE),
        pltpu.VMEM((3, 2, 8, width), WIDE),
        pltpu.VMEM((16, width), WIDE),
        pltpu.VMEM((row_count, 16, width), WIDE),
        pltpu.VMEM((length, width), LOW),
        pltpu.SemaphoreType.DMA((2, 3)),
        pltpu.SemaphoreType.DMA((2, 3)),
        pltpu.SemaphoreType.DMA((2, 3)),
        pltpu.SemaphoreType.DMA((2, row_count)),
        pltpu.SemaphoreType.DMA((2, 3)),
    ]
    return pl.pallas_call(
        finish_kernel,
        out_shape=outs,
        in_specs=[ANY] * 3 + [VM] * 6,
        out_specs=(VM, VM) + (ANY,) * 3,
        scratch_shapes=scratch,
        compiler_params=pltpu.CompilerParams(
            collective_id=number, has_side_effects=True, vmem_limit_bytes=GRANT
        ),
        cost_estimate=pl.CostEstimate(flops=int(3e10), bytes_accessed=30 * MEBI, transcendentals=0),
    )(*late, *early, near, far, *sums)


def last_call(number, up, down):
    return pl.pallas_call(
        last_kernel,
        out_shape=(shape(up.shape), shape(down.shape)),
        in_specs=[ANY] * 2,
        out_specs=(ANY,) * 2,
        scratch_shapes=[pltpu.SemaphoreType.DMA((2, 2))],
        compiler_params=pltpu.CompilerParams(collective_id=number, has_side_effects=True),
    )(up, down)


def swap_sections(value):
    return lax.ppermute(value, "section", [(0, 1), (1, 0)])


def on_device(
    tokens,
    cotangent,
    first_gain,
    first_shift,
    attend_weight,
    attend_bias,
    output_weight,
    output_bias,
    second_gain,
    second_shift,
    expand_weight,
    expand_bias,
    contract_weight,
    contract_bias,
):
    section = lax.axis_index("section")
    column = lax.axis_index("col")
    first_section = section == 0
    columns = lax.axis_size("col")
    width = tokens.shape[1]
    size = width * columns
    rows = LENGTH // columns

    def pick(early, later):
        return jnp.where(first_section, early, later)

    block_rows = attend_weight.shape[1]
    units = (
        jnp.concatenate(
            [attend_weight[0].reshape(block_rows, 3 * width), output_weight[0].T], axis=1
        ),
        expand_weight[0],
        contract_weight[0].T,
    )
    kept_blocks, sent_blocks = [], []
    for unit in units:
        half = unit.shape[1] // 2
        low, high = unit[:, :half], unit[:, half:]
        kept_blocks.append(pick(low, high))
        sent_blocks.append(pick(high, low))

    small = jnp.concatenate(
        [
            first_gain,
            first_shift,
            output_bias,
            second_gain,
            second_shift,
            contract_bias,
            attend_bias[0],
            expand_bias[0].reshape(-1, width),
        ],
        0,
    )
    filled = small.shape[0]
    small = jnp.pad(small, ((0, -filled % 16), (0, 0)))
    got_attend = swap_sections(sent_blocks[0])
    got_attend, sent_expand = lax.optimization_barrier((got_attend, sent_blocks[1]))
    x0_full, gy_full, vectors, got_expand, got_contract = start_call(
        1, tokens, cotangent, small, sent_expand, units[2], columns
    )

    def gather_blocks(block):
        return lax.all_gather(block, "row", axis=0, tiled=True)

    half = units[2].shape[1] // 2
    mats = [[], []]
    for own, got in ((kept_blocks[0], got_attend), (kept_blocks[1], got_expand)):
        for layer, block in enumerate((pick(own, got), pick(got, own))):
            mats[layer].append(gather_blocks(block))
    mats[0].append(gather_blocks(pick(kept_blocks[2], got_contract[:, half:])))
    mats[1].append(gather_blocks(pick(got_contract, units[2])))
    vectors = vectors.astype(WIDE)
    wide_vectors = jnp.swapaxes(vectors[:, :, :6], 1, 2).reshape(2, 6, size)
    wide_vectors = jnp.pad(wide_vectors, ((0, 0), (0, 2), (0, 0)))
    own_vectors = lax.dynamic_index_in_dim(vectors, column, 1, keepdims=False)
    attend_biases = jnp.stack(
        [own_vectors[:, 6], jnp.zeros_like(own_vectors[:, 6]), own_vectors[:, 7]], 1
    ).reshape(2, 1, 3 * width)
    expand_biases = own_vectors[:, 8:filled].reshape(2, 1, -1)

    def own_rows(full):
        return lax.dynamic_slice_in_dim(full, column * rows, rows, 0)

    def own_features(full):
        return lax.dynamic_slice_in_dim(full, column * width, width, 1)

    attn = (mats[0][0], swap_sections(mats[0][0]))
    x = x0_full
    kept, pairs = [], []
    owns = [own_rows(x0_full)]
    for layer in range(2):
        last = layer == 1
        vec = wide_vectors[layer]
        (full, normed, heads, o, lse, hidden, second_own), (other,) = attend_call(
            2 + 3 * layer, not last, x, attn, vec, attend_biases[layer], rows, width, [mats[layer][1]]
        )
        expand = (mats[layer][1], other)
        outs, others = widen_call(
            3 + 3 * layer, second_own, expand, expand_biases[layer],
            gy_full if last else None, [] if last else [mats[0][2]],
        )
        second, active, slope = outs[:3]
        contract = (mats[layer][2], mats[layer][2] if last else others[0])
        if last:
            c1 = outs[3]
        pairs.append((attn, expand, contract))
        kept.append((normed, heads, o, lse, hidden, second, active, slope))
        if not last:
            (x,), others = contract_call(4, active, hidden, contract, vec, [mats[1][0]])
            owns.append(x)
            attn = (mats[1][0], others[0])
    y0 = own_features(full)

    def scatter(total):
        return lax.psum_scatter(total, "row", scatter_dimension=0, tiled=True)

    def tie(value, then):
        return lax.optimization_barrier((value, then))

    attn, expand, contract = pairs[1]
    normed, heads, o, lse, hidden, second, active, slope = kept[1]
    (grad_hidden, low, expand_sums1, e1, y1), _ = late_expand_call(
        8, active, hidden, contract, expand, gy_full, slope, second, wide_vectors[1], []
    )
    layer_low, layer_high = pick(y0, y1), pick(y1, y0)
    (gx1_own, attend_sums1, w1), (layer_got,) = late_attend_call(
        10, low, grad_hidden, owns[1], attn, normed, heads, o, lse, wide_vectors[1], [layer_high]
    )
    layer_outputs = jnp.concatenate([pick(layer_low, layer_got), pick(layer_got, layer_low)], 0)

    attn, expand, contract = pairs[0]
    normed, heads, o, lse, hidden, second, active, slope = kept[0]
    part_c1 = scatter(c1)
    (grad_hidden, low, expand_sums0, ek0, es0, gx1_full, total_c0), (far_c1,) = expand_back_call(
        12, gx1_own, contract, expand, slope, active, second, hidden, wide_vectors[0], [part_c1]
    )
    part_e1, low = tie(scatter(e1), low)
    mixed, outer, total_e0 = scores_back_call(14, low, attn, heads, o, lse, ek0, es0)
    part_w1, mixed = tie(scatter(w1), mixed)
    part_c0, mixed = tie(scatter(total_c0), mixed)
    total_w0, gx0_own, attend_sums0 = attend_back_call(
        15, mixed, outer, grad_hidden, owns[0], attn, normed, wide_vectors[0]
    )
    part_e0 = scatter(total_e0)
    input_grads, small_grads, far_e1, far_c0, far_e0 = finish_call(
        16,
        (part_e1,),
        (part_c0, part_e0),
        gx0_own,
        own_features(gx1_full),
        (attend_sums0, expand_sums0, attend_sums1, expand_sums1),
        lax.axis_size("row"),
    )

    part_w0, small_grads = tie(scatter(total_w0), small_grads)
    far_w1, far_w0 = last_call(17, part_w1, part_w0)

    units = []
    for late, far_late, early, far_early in (
        (part_w1, far_w1, part_w0, far_w0),
        (part_e1, far_e1, part_e0, far_e0),
        (part_c1, far_c1, part_c0, far_c0),
    ):
        whole = jnp.concatenate([early, far_early], 1).astype(WIDE)
        units.append(pick(whole, late.astype(WIDE) + far_late.astype(WIDE)))
    attn_part, expand_part, contract_part = units

    return (
        layer_outputs[None],
        input_grads[None],
        small_grads[0:1],
        small_grads[1:2],
        attn_part[:, : 3 * width].reshape(block_rows, 3, width)[None],
        small_grads[8:10][None],
        attn_part[:, 3 * width :].T[None],
        small_grads[2:3],
        small_grads[3:4],
        small_grads[4:5],
        expand_part[None],
        small_grads[10 : 10 + expand_bias.shape[1] // width].reshape(1, -1),
        contract_part.T[None],
        small_grads[5:6],
    )


def solution(mesh):
    return jax.shard_map(
        on_device,
        mesh=mesh,
        in_specs=(
            P("row", "col"),
            P("row", "col"),
            P("section", "col"),
            P("section", "col"),
            P("section", "row", None, "col"),
            P("section", None, "col"),
            P("section", "col", "row"),
            P("section", "col"),
            P("section", "col"),
            P("section", "col"),
            P("section", "row", "col"),
            P("section", "col"),
            P("section", "col", "row"),
            P("section", "col"),
        ),
        out_specs=(
            P("section", "row", "col"),
            P("section", "row", "col"),
            P("section", "col"),
            P("section", "col"),
            P("section", "row", None, "col"),
            P("section", None, "col"),
            P("section", "col", "row"),
            P("section", "col"),
            P("section", "col"),
            P("section", "col"),
            P("section", "row", "col"),
            P("section", "col"),
            P("section", "col", "row"),
            P("section", "col"),
        ),
        check_vma=False,
    )
```

```python
import functools

import jax
import jax.numpy as jnp
from jax import lax
from jax.experimental import pallas as pl
from jax.experimental.pallas import tpu as pltpu
from jax.sharding import PartitionSpec as P

HEAD = 64
LENGTH = 1024
EPS = 1e-05
LOW = jnp.bfloat16
WIDE = jnp.float32
MESH = pl.DeviceIdType.MESH
PARTS = 2
TILE = 256
MEBI = 1024 * 1024
GRANT = 58 * MEBI


def nn(left, right):
    return lax.dot_general(left, right, (((1,), (0,)), ((), ())), preferred_element_type=WIDE)


def nt(left, right):
    return lax.dot_general(left, right, (((1,), (1,)), ((), ())), preferred_element_type=WIDE)


def tn(left, right):
    return lax.dot_general(left, right, (((0,), (0,)), ((), ())), preferred_element_type=WIDE)


def normalise(values):
    center = jnp.mean(values, axis=1, keepdims=True)
    centred = values - center
    scale = lax.rsqrt(jnp.mean(centred * centred, axis=1, keepdims=True) + EPS)
    return centred * scale, scale


def norm_backward(grad, hat, scale, gain):
    scaled = grad * gain
    mean_one = jnp.mean(scaled, axis=1, keepdims=True)
    mean_two = jnp.mean(scaled * hat, axis=1, keepdims=True)
    return scale * (scaled - mean_one - hat * mean_two)


class Group:
    def __init__(self, rows):
        self.me = lax.axis_index("col")
        chip, core = self.me // 2, self.me % 2
        self.sib = chip * 2 + 1 - core
        self.peer = (1 - chip) * 2 + core
        self.diag = (1 - chip) * 2 + 1 - core
        self.rows = rows
        self.part = rows // PARTS
        self.loads, self.stores, self.begun = {}, {}, set()

    def need(self, *places):
        for place in places:
            self.loads[place].wait()

    def emit(self, *places):
        for place in places:
            self.stores[place].start()
            self.begun.add(place)

    def greet(self, swaps, diagonal, rows=()):
        barrier = pltpu.get_barrier_semaphore()
        others = [{"col": self.sib}, {"col": self.peer}]
        if diagonal:
            others.append({"col": self.diag})
        if swaps:
            others.append({"section": 1 - lax.axis_index("section")})
        others += [{"row": row} for row in rows]
        for other in others:
            pl.semaphore_signal(barrier, inc=1, device_id=other, device_id_type=MESH)
        pl.semaphore_wait(barrier, len(others))

    def slab(self, owner, j):
        return pl.ds(pl.multiple_of(owner * self.rows + j * self.part, self.part), self.part)

    def chunk(self, owner):
        return pl.ds(pl.multiple_of(owner * self.rows, self.rows), self.rows)


def push(src, dst, sems, slot, target, axis="col"):
    return pltpu.make_async_remote_copy(
        src_ref=src,
        dst_ref=dst,
        send_sem=sems.at[0, slot],
        recv_sem=sems.at[1, slot],
        device_id={axis: target},
        device_id_type=MESH,
    )


class Gather:
    def __init__(self, group, full, sems, blocks=False):
        self.group, self.full, self.sems, self.blocks = group, full, sems, blocks

    def piece(self, owner, j):
        if not self.blocks:
            return self.full.at[self.group.slab(owner, j)]
        part = self.full.shape[1] // PARTS
        return self.full.at[owner, pl.ds(j * part, part)]

    def start(self):
        g = self.group
        self.over, self.near, self.relayed = [], [], []
        for j in range(PARTS):
            piece = self.piece(g.me, j)
            self.over.append(push(piece, piece, self.sems, j, g.peer))
            self.over[-1].start()
        for j in range(PARTS):
            piece = self.piece(g.me, j)
            self.near.append(push(piece, piece, self.sems, PARTS + j, g.sib))
            self.near[-1].start()

    def sibling(self):
        for copy in self.near:
            copy.wait_recv()

    def relay(self):
        g = self.group
        for j in range(PARTS):
            self.over[j].wait_recv()
            piece = self.piece(g.peer, j)
            self.relayed.append(push(piece, piece, self.sems, 2 * PARTS + j, g.sib))
            self.relayed[-1].start()

    def diagonal(self):
        for copy in self.relayed:
            copy.wait_recv()

    def done(self):
        for copy in self.over + self.near + self.relayed:
            copy.wait_send()

    def each(self, body, first=None):
        g = self.group
        self.start()
        if first is not None:
            first()
        body(g.me)
        self.sibling()
        body(g.sib)
        self.relay()
        body(g.peer)
        self.diagonal()
        body(g.diag)
        self.done()


class Scatter:
    def __init__(self, group, stage, land, total, sems):
        self.group, self.stage, self.land, self.total, self.sems = group, stage, land, total, sems

    def start(self, part):
        g, stage, land = self.group, self.stage, self.land
        self.first, self.over, self.near = [], [], []
        def split(owner):
            whole = part(owner)
            return [whole[j * g.part : (j + 1) * g.part] for j in range(PARTS)]

        for j, mine in enumerate(split(g.diag)):
            stage[0, j] = mine.astype(LOW)
            self.first.append(push(stage.at[0, j], land.at[0, j], self.sems, j, g.sib))
            self.first[-1].start()
        for j, mine in enumerate(split(g.peer)):
            self.first[j].wait_recv()
            stage[1, j] = (mine + land[0, j].astype(WIDE)).astype(LOW)
            self.over.append(push(stage.at[1, j], land.at[1, j], self.sems, PARTS + j, g.peer))
            self.over[-1].start()
        for j, mine in enumerate(split(g.sib)):
            stage[2, j] = mine.astype(LOW)
            self.near.append(push(stage.at[2, j], land.at[2, j], self.sems, 2 * PARTS + j, g.sib))
            self.near[-1].start()
        for j, mine in enumerate(split(g.me)):
            self.total[j] = mine

    def take(self, j):
        self.near[j].wait_recv()
        self.over[j].wait_recv()
        land = self.land
        return self.total[j] + (land[1, j].astype(WIDE) + land[2, j].astype(WIDE))

    def done(self):
        for copy in self.first + self.over + self.near:
            copy.wait_send()


class Deliver:
    def __init__(self, group, stage, out, sems):
        self.group, self.stage, self.out, self.sems = group, stage, out, sems

    def start(self, rows_ref):
        g, width = self.group, self.out.shape[1]
        for c in range(self.stage.shape[0]):
            self.stage[c] = rows_ref[:, c * width : (c + 1) * width]
        place = self.out.at[g.chunk(g.me)]
        self.copies = [
            push(self.stage.at[other], place, self.sems, n, other)
            for n, other in enumerate((g.peer, g.diag, g.sib))
        ]
        for copy in self.copies:
            copy.start()
        self.out[g.chunk(g.me), :] = self.stage[g.me]

    def done(self):
        for copy in self.copies:
            copy.wait()


class OneWay:
    def __init__(self, up, down, sems):
        self.section = lax.axis_index("section")
        both = [*up, *down]
        copies = [
            push(source, into, sems, n, 1 - self.section, "section")
            for n, (source, into) in enumerate(both)
        ]
        self.up, self.down = copies[: len(up)], copies[len(up) :]

    def each(self, first, second):
        @pl.when(self.section == 0)
        def _():
            first(self.up)
            second(self.down)

        @pl.when(self.section == 1)
        def _():
            first(self.down)
            second(self.up)

    def start(self):
        self.each(lambda copies: [copy.start() for copy in copies], lambda copies: None)

    def wait(self):
        self.each(
            lambda copies: [copy.wait_send() for copy in copies],
            lambda copies: [copy.wait_recv() for copy in copies],
        )


def scatter_scratch(rows, width):
    part = rows // PARTS
    return [
        pltpu.VMEM((3, PARTS, part, width), LOW),
        pltpu.VMEM((3, PARTS, part, width), LOW),
        pltpu.VMEM((PARTS, part, width), WIDE),
        pltpu.SemaphoreType.DMA((2, 3 * PARTS)),
    ]


class Halves:
    def __init__(self, pair, whole, sems, slot):
        if pair[0].shape[1] == whole.shape[1]:
            self.copies = [pltpu.make_async_copy(pair[0], whole, sems.at[slot])]
            return
        section = lax.axis_index("section")
        half = whole.shape[1] // 2
        self.copies = []
        for n, place in enumerate((section, 1 - section)):
            columns = pl.ds(pl.multiple_of(place * half, half), half)
            self.copies.append(
                pltpu.make_async_copy(pair[n], whole.at[:, columns], sems.at[slot + n])
            )

    def start(self):
        for copy in self.copies:
            copy.start()

    def wait(self):
        for copy in self.copies:
            copy.wait()


class Trade:
    def __init__(self, keep, send, got, sems):
        self.keep, self.send, self.got, self.sems = keep, send, got, sems
        self.tiles = keep.shape[0] // TILE

    def copy(self, n):
        rows = pl.ds(pl.multiple_of(n * TILE, TILE), TILE)
        return push(
            self.send.at[rows], self.got.at[rows], self.sems, n, 1 - lax.axis_index("section"), "section"
        )

    def start(self, make):
        @pl.loop(0, self.tiles)
        def _(n):
            make(pl.ds(pl.multiple_of(n * TILE, TILE), TILE))
            self.copy(n).start()

    def finish(self):
        @pl.loop(0, self.tiles)
        def _(n):
            self.copy(n).wait()

        add_into(self.keep, self.got)


def add_into(keep_ref, got_ref):
    @pl.loop(0, keep_ref.shape[0] // TILE)
    def _(n):
        rows = pl.ds(pl.multiple_of(n * TILE, TILE), TILE)
        keep_ref[rows, :] = (keep_ref[rows, :].astype(WIDE) + got_ref[rows, :].astype(WIDE)).astype(LOW)


def causal_scores(scores):
    size = scores.shape[1]
    keep = lax.broadcasted_iota(jnp.int32, (size, size), 0) <= lax.broadcasted_iota(
        jnp.int32, (size, size), 1
    )
    begin = scores.shape[0] - size
    last = jnp.where(keep, scores[begin:], -1000000000.0)
    return last if begin == 0 else jnp.concatenate([scores[:begin], last], 0)


def attention_out(owner, size, heads_ref, o3, lse_ref, heads):
    for i in range(heads_ref.shape[1] // size):
        rows, finish = slice(i * size, (i + 1) * size), (i + 1) * size

        @pl.when(owner == i)
        def _():
            @pl.loop(0, heads)
            def _(h):
                scores = causal_scores(nt(heads_ref[heads + h, :finish, :], heads_ref[h, rows, :]))
                highest = jnp.max(scores, axis=0, keepdims=True)
                powers = jnp.exp(scores - highest)
                summed = jnp.sum(powers, axis=0, keepdims=True)
                mixed = tn(heads_ref[2 * heads + h, :finish, :], powers.astype(LOW))
                o3[h, rows, :] = (mixed / summed).T.astype(LOW)
                lse_ref[pl.ds(h, 1), rows] = highest + jnp.log(summed)


def attention_back(owner, size, heads_ref, go3, lse_ref, dots_ref, g3, key_acc, value_acc, heads):
    for i in range(heads_ref.shape[1] // size):
        rows, finish = slice(i * size, (i + 1) * size), (i + 1) * size

        @pl.when(owner == i)
        def _():
            @pl.loop(0, heads)
            def _(h):
                queries = heads_ref[h, rows, :]
                keys = heads_ref[heads + h, :finish, :]
                grads = go3[h, rows, :]
                probs = jnp.exp(causal_scores(nt(keys, queries) - lse_ref[pl.ds(h, 1), rows]))
                grad_probs = nt(heads_ref[2 * heads + h, :finish, :], grads)
                grad_scores = (probs * (grad_probs - dots_ref[pl.ds(h, 1), rows])).astype(LOW)
                g3[h, rows, :] = (tn(grad_scores, keys) * HEAD ** (-0.5)).astype(LOW)
                key_acc[h, :finish, :] += nn(grad_scores, queries)
                value_acc[h, :finish, :] += nn(probs.astype(LOW), grads)


def start_kernel(
    tokens_ref, cotangent_ref, small_ref, expand_ref, contract_ref,
    x_ref, g_ref, vectors_ref, got_expand_ref, got_contract_ref,
    x4, g4, s4, other4, x_sems, g_sems, s_sems, local_sems,
):
    section = lax.axis_index("section")
    group = Group(x_ref.shape[0] // 4)
    length = x_ref.shape[0]
    loads = []
    rows = pl.ds(pl.multiple_of(section * length, length), length)
    for n, (source, into) in enumerate(((tokens_ref.at[rows], x4), (cotangent_ref.at[rows], g4), (small_ref, s4))):
        loads.append(pltpu.make_async_copy(source, into.at[group.me], local_sems.at[n]))
        loads[-1].start()
    group.greet(True, False)
    blocks = [
        push(source, into, s_sems, 3 * PARTS + 1 + n, 1 - section, "section")
        for n, (source, into) in enumerate(((expand_ref, got_expand_ref), (contract_ref, got_contract_ref)))
    ]
    for block in blocks:
        block.start()
    gathers = [Gather(group, x4, x_sems, True), Gather(group, s4, s_sems, True), Gather(group, g4, g_sems, True)]
    for gather, load in zip(gathers, (loads[0], loads[2], loads[1])):
        load.wait()
        gather.start()
    for gather in gathers:
        gather.sibling()
        gather.relay()
        gather.diagonal()
    swap = push(s4, other4, s_sems, 3 * PARTS, 1 - section, "section")
    swap.start()
    width = x4.shape[2]
    for c in range(x4.shape[0]):
        x_ref[:, c * width : (c + 1) * width] = x4[c]
        g_ref[:, c * width : (c + 1) * width] = g4[c]
    swap.wait()
    for block in blocks:
        block.wait()
    vectors_ref[section] = s4[...]
    vectors_ref[1 - section] = other4[...]
    for gather in gathers:
        gather.done()


def attend_kernel(
    gathered, heads, group, x_ref, mine_ref, other_ref, vec_ref, bias_ref,
    full_ref, normed_ref, heads_ref, o_ref, lse_ref, hidden_ref, second_ref,
    weight, o3, stage, land, total, scatter_sems, gather_sems, local_sems,
):
    width = o_ref.shape[1]
    halves = Halves((mine_ref, other_ref), weight, local_sems, 0)
    halves.start()
    if not gathered:
        full_ref[group.chunk(group.me), :] = x_ref[...]
    halves.wait()

    def project(owner):
        rows = group.chunk(owner)
        values = (x_ref if gathered else full_ref)[rows, :].astype(WIDE)
        hat, _ = normalise(values)
        normed = (hat * vec_ref[0:1, :] + vec_ref[1:2, :]).astype(LOW)
        normed_ref[rows, :] = normed
        mixed = nn(normed, weight[:, : 3 * width]) + bias_ref[...]
        for j in range(3 * heads):
            piece = mixed[:, j * HEAD : (j + 1) * HEAD]
            if j < heads:
                piece = piece * HEAD ** (-0.5)
            heads_ref[j, rows, :] = piece.astype(LOW)

    if gathered:
        full_ref[...] = jnp.zeros_like(full_ref)

        @pl.loop(0, LENGTH // group.rows)
        def _(n):
            project(n)
    else:
        Gather(group, full_ref, gather_sems).each(project)
    group.emit(0, 1, 2)
    lse_ref[...] = jnp.zeros_like(lse_ref)

    def attend(owner):
        rows = group.chunk(owner)
        attention_out(owner, group.rows, heads_ref, o3, lse_ref, heads)
        for h in range(heads):
            o_ref[rows, h * HEAD : (h + 1) * HEAD] = o3[h, rows, :]
        return nt(o_ref[rows, :], weight[:, 3 * width :])

    scatter = Scatter(group, stage, land, total, scatter_sems)
    scatter.start(attend)
    group.emit(3, 4)
    for j in range(PARTS):
        rows = slice(j * group.part, (j + 1) * group.part)
        residual = (x_ref if gathered else full_ref)[group.slab(group.me, j), :].astype(WIDE)
        hidden = residual + scatter.take(j) + vec_ref[2:3, :]
        hidden_ref[rows, :] = hidden
        hat, _ = normalise(hidden)
        second_ref[rows, :] = (hat * vec_ref[3:4, :] + vec_ref[4:5, :]).astype(LOW)
    scatter.done()


def outer_whole(left_ref, right_ref, out_ref):
    @pl.loop(0, left_ref.shape[1] // TILE)
    def _(n):
        rows = pl.ds(pl.multiple_of(n * TILE, TILE), TILE)
        out_ref[rows, :] = tn(left_ref[:, rows], right_ref[...]).astype(LOW)


def widen_kernel(last, group, second_ref, em_ref, eo_ref, bias_ref, *refs):
    if last:
        g_ref, *refs = refs
    full_ref, active_ref, slope_ref, *refs = refs
    if last:
        c_ref, *refs = refs
    expand, gather_sems, local_sems = refs
    halves = Halves((em_ref, eo_ref), expand, local_sems, 0)
    halves.start()
    full_ref[group.chunk(group.me), :] = second_ref[...]
    halves.wait()

    def widen(owner):
        rows = group.chunk(owner)
        t = nn(full_ref[rows, :], expand[...]) + bias_ref[...]
        square = t * t
        bent = jnp.tanh(0.7978845608028654 * t * (1.0 + 0.044715 * square))
        active_ref[rows, :] = (0.5 * t * (1.0 + bent)).astype(LOW)
        slope_ref[rows, :] = (
            0.5 * (1.0 + bent)
            + (0.5 * 0.7978845608028654) * t * (1.0 - bent * bent) * (1.0 + 3 * 0.044715 * square)
        ).astype(LOW)

    Gather(group, full_ref, gather_sems).each(widen)
    if last:
        group.emit(0, 1, 2)
        group.need(4)
        outer_whole(g_ref, active_ref, c_ref)


def outer_halves(left_ref, right_ref, keep_ref, send_ref):
    section = lax.axis_index("section")
    half = right_ref.shape[1] // 2
    for place, out in ((section, keep_ref), (1 - section, send_ref)):
        columns = pl.ds(pl.multiple_of(place * half, half), half)

        @pl.loop(0, left_ref.shape[1] // TILE)
        def _(n):
            rows = pl.ds(pl.multiple_of(n * TILE, TILE), TILE)
            out[rows, :] = tn(left_ref[:, rows], right_ref[:, columns]).astype(LOW)


def contract_kernel(
    group, active_ref, hidden_ref, cm_ref, co_ref, vec_ref, result_ref,
    contract, stage, land, total, scatter_sems, local_sems,
):
    halves = Halves((cm_ref, co_ref), contract, local_sems, 0)
    halves.start()
    halves.wait()
    scatter = Scatter(group, stage, land, total, scatter_sems)
    scatter.start(lambda owner: nt(active_ref[group.chunk(owner), :], contract[...]))
    group.need(1)
    for j in range(PARTS):
        rows = slice(j * group.part, (j + 1) * group.part)
        result = hidden_ref[rows, :] + scatter.take(j) + vec_ref[5:6, :]
        result_ref[rows, :] = result.astype(LOW)
    scatter.done()


def narrow_grads(group, scatter, full_ref, hidden_ref, vec_ref, grad_ref, low_ref, sums_ref):
    for j in range(PARTS):
        rows = slice(j * group.part, (j + 1) * group.part)
        grad = scatter.take(j)
        hat, scale = normalise(hidden_ref[rows, :])
        own = full_ref[group.slab(group.me, j), :].astype(WIDE)
        out = own + norm_backward(grad, hat, scale, vec_ref[3:4, :])
        grad_ref[rows, :] = out
        low_ref[rows, :] = out.astype(LOW)
        for n, term in enumerate((grad * hat, grad, own, out)):
            sums_ref[n : n + 1, :] += jnp.sum(term, axis=0, keepdims=True)


def bend(rows, full_ref, contract, slope_ref, before, sums_ref):
    grad = (nn(full_ref[rows, :], contract[...]) * slope_ref[rows, :].astype(WIDE)).astype(LOW)
    before[rows, :] = grad
    sums_ref[4:5, :] += jnp.sum(grad.astype(WIDE), axis=0, keepdims=True)


def late_expand_kernel(
    group, active_ref, hidden_ref, cm_ref, co_ref, em_ref, eo_ref, g_ref, slope_ref, second_ref, vec_ref,
    grad_ref, low_ref, sums_ref, e_ref, result,
    contract, expand, before,
    stage_a, land_a, total_a, sems_a, stage, land, total, scatter_sems, local_sems,
):
    first = Halves((cm_ref, co_ref), contract, local_sems, 0)
    then = Halves((em_ref, eo_ref), expand, local_sems, 2)
    first.start()
    then.start()
    sums_ref[...] = jnp.zeros_like(sums_ref)
    first.wait()
    forward = Scatter(group, stage_a, land_a, total_a, sems_a)
    forward.start(lambda owner: nt(active_ref[group.chunk(owner), :], contract[...]))
    group.need(6, 7)

    @pl.loop(0, LENGTH // group.rows)
    def _(n):
        bend(group.chunk(n), g_ref, contract, slope_ref, before, sums_ref)

    then.wait()
    scatter = Scatter(group, stage, land, total, scatter_sems)
    scatter.start(lambda owner: nt(before[group.chunk(owner), :], expand[...]))
    group.need(1)
    for j in range(PARTS):
        rows = slice(j * group.part, (j + 1) * group.part)
        result[rows, :] = (hidden_ref[rows, :] + forward.take(j) + vec_ref[5:6, :]).astype(LOW)
    group.emit(4)
    group.need(8)
    outer_whole(second_ref, before, e_ref)
    group.emit(3)
    narrow_grads(group, scatter, g_ref, hidden_ref, vec_ref, grad_ref, low_ref, sums_ref)
    group.emit(0, 1, 2)
    forward.done()
    scatter.done()


def expand_back_kernel(
    group, g_ref, cm_ref, co_ref, em_ref, eo_ref, slope_ref, active_ref, second_ref, hidden_ref, vec_ref,
    grad_ref, low_ref, sums_ref, ek_ref, es_ref, full_ref, c_ref,
    contract, expand, before, stage, land, total, scatter_sems, gather_sems, local_sems, outer, got, trade_sems,
):
    section = lax.axis_index("section")
    first = Halves((cm_ref, co_ref), contract, local_sems, 0)
    then = Halves((em_ref, eo_ref), expand, local_sems, 2)
    first.start()
    then.start()
    sums_ref[...] = jnp.zeros_like(sums_ref)
    full_ref[group.chunk(group.me), :] = g_ref[...]
    first.wait()
    Gather(group, full_ref, gather_sems).each(
        lambda owner: bend(group.chunk(owner), full_ref, contract, slope_ref, before, sums_ref),
        lambda: group.need(5),
    )
    group.emit(5)
    group.need(6)
    half = active_ref.shape[1] // 2

    def columns(place):
        return pl.ds(pl.multiple_of(place * half, half), half)

    def make(n):
        def tile(rows):
            place = section if n == 0 else 1 - section
            outer[n, rows, :] = tn(full_ref[:, rows], active_ref[:, columns(place)]).astype(LOW)

        return tile

    trade = Trade(outer.at[0], outer.at[1], got, trade_sems)
    trade.start(make(1))
    then.wait()
    scatter = Scatter(group, stage, land, total, scatter_sems)
    scatter.start(lambda owner: nt(before[group.chunk(owner), :], expand[...]))
    group.need(7)
    outer_halves(second_ref, before, ek_ref, es_ref)
    group.emit(3, 4)
    keep = make(0)

    @pl.loop(0, outer.shape[1] // TILE)
    def _(n):
        keep(pl.ds(pl.multiple_of(n * TILE, TILE), TILE))

    group.need(8)
    narrow_grads(group, scatter, full_ref, hidden_ref, vec_ref, grad_ref, low_ref, sums_ref)
    group.emit(0, 1, 2)
    scatter.done()
    trade.finish()
    store = pltpu.make_async_copy(outer.at[0], c_ref, local_sems.at[0])
    store.start()
    store.wait()


def scores_back(group, heads, low_ref, weight, heads_ref, o_ref, lse_ref, full, go3, dots, g3, accs, mixed, gather_sems, first):
    width = o_ref.shape[1]
    picks = (
        lax.broadcasted_iota(jnp.int32, (8, width), 1) // HEAD
        == lax.broadcasted_iota(jnp.int32, (8, width), 0)
    ).astype(WIDE)
    for acc in accs:
        acc[...] = jnp.zeros_like(acc)

    def spread(owner):
        rows = group.chunk(owner)
        grads = nn(full[rows, :], weight[:, 3 * width :]).astype(LOW)
        for h in range(heads):
            go3[h, rows, :] = grads[:, h * HEAD : (h + 1) * HEAD]
        term = grads.astype(WIDE) * o_ref[rows, :].astype(WIDE)
        dots[:, rows] = lax.dot_general(
            picks,
            term,
            (((1,), (1,)), ((), ())),
            precision=lax.Precision.HIGHEST,
            preferred_element_type=WIDE,
        )
        attention_back(owner, group.rows, heads_ref, go3, lse_ref, dots, g3, *accs, heads)

    full[group.chunk(group.me), :] = low_ref[...]
    Gather(group, full, gather_sems).each(spread, first)
    for j in range(3 * heads):
        source = g3[j] if j < heads else accs[j // heads - 1][j % heads].astype(LOW)
        mixed[:, j * HEAD : (j + 1) * HEAD] = source


def outer_out(full, o_ref, outer_ref):
    @pl.loop(0, outer_ref.shape[0] // TILE)
    def _(n):
        rows = pl.ds(pl.multiple_of(n * TILE, TILE), TILE)
        outer_ref[rows, :] = tn(full[:, rows], o_ref[...]).astype(LOW)


def attend_grads(group, scatter, x_ref, grad_ref, vec_ref, mixed, width, out_ref, sums_ref):
    sums_ref[2:3, : 3 * width] = jnp.sum(mixed[...].astype(WIDE), axis=0, keepdims=True)
    for j in range(PARTS):
        rows = slice(j * group.part, (j + 1) * group.part)
        grad = scatter.take(j)
        hat, scale = normalise(x_ref[rows, :].astype(WIDE))
        out = grad_ref[rows, :] + norm_backward(grad, hat, scale, vec_ref[0:1, :])
        out_ref[rows, :] = out.astype(LOW)
        for n, term in enumerate((grad * hat, grad)):
            sums_ref[n : n + 1, :] += jnp.sum(term, axis=0, keepdims=True)


def late_attend_kernel(
    heads, group, low_ref, grad_ref, x_ref, mine_ref, other_ref, normed_ref, heads_ref, o_ref, lse_ref, vec_ref,
    result_ref, y_ref,
    out_ref, sums_ref, results_ref, w_ref,
    weight, full, go3, dots, g3, key_acc, value_acc, mixed, outer, outer_o, late, y_land, stage4,
    stage, land, total, scatter_sems, gather_sems, deliver_sems, y_sems, local_sems,
):
    width = o_ref.shape[1]
    section = lax.axis_index("section")
    halves = Halves((mine_ref, other_ref), weight, local_sems, 0)
    halves.start()
    sums_ref[...] = jnp.zeros_like(sums_ref)
    halves.wait()
    deliver = Deliver(group, stage4, late, deliver_sems)

    def first():
        group.need(6, 7, 8, 10)
        deliver.start(result_ref)

    scores_back(
        group, heads, low_ref, weight, heads_ref, o_ref, lse_ref, full, go3, dots, g3,
        (key_acc, value_acc), mixed, gather_sems, first,
    )
    deliver.done()
    group.need(11)
    results = OneWay([(late, y_land)], [(y_ref, y_land)], y_sems)
    results.start()
    scatter = Scatter(group, stage, land, total, scatter_sems)
    scatter.start(lambda owner: nt(mixed[group.chunk(owner), :], weight[:, : 3 * width]))
    outer_out(full, o_ref, outer_o)
    group.need(5)

    @pl.loop(0, weight.shape[0] // TILE)
    def _(n):
        rows = pl.ds(pl.multiple_of(n * TILE, TILE), TILE)
        outer[rows, : 3 * width] = tn(normed_ref[:, rows], mixed[...]).astype(LOW)
        outer[rows, 3 * width :] = outer_o[rows, :]

    store = pltpu.make_async_copy(outer, w_ref, local_sems.at[2])
    store.start()
    length = y_ref.shape[0]
    own = pl.ds(pl.multiple_of(section * length, length), length)

    @pl.when(section == 0)
    def _():
        results_ref[own, :] = y_ref[...]

    @pl.when(section == 1)
    def _():
        results_ref[own, :] = late[...]

    group.need(1, 2)
    attend_grads(group, scatter, x_ref, grad_ref, vec_ref, mixed, width, out_ref, sums_ref)
    results.wait()
    results_ref[pl.ds(pl.multiple_of((1 - section) * length, length), length), :] = y_land[...]
    scatter.done()
    store.wait()


def scores_back_kernel(
    heads, group, low_ref, mine_ref, other_ref, heads_ref, o_ref, lse_ref, ek_ref, es_ref,
    mixed, outer_ref, e_ref,
    weight, full, go3, dots, g3, key_acc, value_acc, got, gather_sems, local_sems, swap_sems,
):
    swap = push(es_ref, got, swap_sems, 0, 1 - lax.axis_index("section"), "section")
    swap.start()
    halves = Halves((mine_ref, other_ref), weight, local_sems, 0)
    halves.start()
    halves.wait()
    scores_back(
        group, heads, low_ref, weight, heads_ref, o_ref, lse_ref, full, go3, dots, g3,
        (key_acc, value_acc), mixed, gather_sems, lambda: group.need(3, 4, 5),
    )
    group.emit(0)
    outer_out(full, o_ref, outer_ref)
    group.emit(1)
    group.need(6)
    swap.wait()
    add_into(ek_ref, got)
    store = pltpu.make_async_copy(ek_ref, e_ref, local_sems.at[0])
    store.start()
    store.wait()


def attend_back_kernel(
    group, mixed, outer_ref, grad_ref, x_ref, mine_ref, other_ref, normed_ref, vec_ref,
    w_ref, out_ref, sums_ref,
    weight, outer, got, stage, land, total, scatter_sems, local_sems, swap_sems,
):
    width = outer_ref.shape[1]
    section = lax.axis_index("section")
    halves = Halves((mine_ref, other_ref), weight, local_sems, 0)
    halves.start()
    sums_ref[...] = jnp.zeros_like(sums_ref)
    half = weight.shape[1] // 2
    scatter = Scatter(group, stage, land, total, scatter_sems)
    group.need(1, 6)

    def make(n):
        place = section if n == 0 else 1 - section

        def tile(rows):
            @pl.when(place == 0)
            def _():
                outer[n, rows, :] = tn(normed_ref[:, rows], mixed[:, :half]).astype(LOW)

            @pl.when(place == 1)
            def _():
                outer[n, rows, : 3 * width - half] = tn(normed_ref[:, rows], mixed[:, half:]).astype(LOW)
                outer[n, rows, 3 * width - half :] = outer_ref[rows, :]

        return tile

    trade = Trade(outer.at[0], outer.at[1], got, swap_sems)
    trade.start(make(1))
    halves.wait()
    scatter.start(lambda owner: nt(mixed[group.chunk(owner), :], weight[:, : 3 * width]))
    keep = make(0)

    @pl.loop(0, outer.shape[1] // TILE)
    def _(n):
        keep(pl.ds(pl.multiple_of(n * TILE, TILE), TILE))

    group.need(2, 3)
    attend_grads(group, scatter, x_ref, grad_ref, vec_ref, mixed, width, out_ref, sums_ref)
    group.emit(1, 2)
    scatter.done()
    trade.finish()
    store = pltpu.make_async_copy(outer.at[0], w_ref, local_sems.at[2])
    store.start()
    store.wait()


def finish_kernel(
    late_ref, early_ref, near_ref, far_ref, a0, n0, a1, n1,
    grads_ref, sums_ref, got_late, got_early,
    mine, stage4, block, land_col, land_x, land_z, land,
    deliver_sems, col_sems, x_sems, z_sems, part_sems,
):
    section, row = lax.axis_index("section"), lax.axis_index("row")
    away = 1 - section
    group = Group(near_ref.shape[0])
    length, width = far_ref.shape
    others = [lax.rem(row + d, land_z.shape[0]) for d in range(1, land_z.shape[0])]
    group.greet(True, True, others)
    gradient_up = OneWay([(far_ref, land)], [], x_sems.at[:, pl.ds(1, 1)])
    gradient_down = OneWay([], [(mine, land)], x_sems.at[:, pl.ds(2, 1)])
    parts = OneWay([(late_ref, got_late)], [(early_ref, got_early)], part_sems)
    deliver = Deliver(group, stage4, mine, deliver_sems)
    deliver.start(near_ref)
    gradient_up.start()
    parts.start()

    block[...] = jnp.zeros_like(block)
    for layer, (attn, narrow) in enumerate(((a0, n0), (a1, n1))):
        wide = [attn[0:1, :], attn[1:2, :], narrow[3:4, :], narrow[0:1, :], narrow[1:2, :], narrow[2:3, :]]
        for c in range(block.shape[0]):
            columns = slice(c * width, (c + 1) * width)
            for n, term in enumerate(wide):
                block[c, layer, n : n + 1, :] = term[:, columns]
            for n, term in enumerate((attn[2:3, :width], attn[2:3, 2 * width : 3 * width])):
                block[c, layer, 8 + n : 9 + n, :] = term
            for n in range(narrow.shape[1] // width):
                block[c, layer, 10 + n : 11 + n, :] = narrow[4:5, n * width : (n + 1) * width]
    copies = [
        push(block.at[other, :, pl.ds(0, 8)], land_col.at[n], col_sems, n, other)
        for n, other in enumerate((group.peer, group.diag, group.sib))
    ]
    for copy in copies:
        copy.start()
    for copy in copies:
        copy.wait()
    me = group.me
    block[me, :, :8] = block[me, :, :8] + (land_col[0] + (land_col[1] + land_col[2]))
    swap = push(block.at[me, away], land_x, x_sems, 0, away, "section")
    swap.start()
    deliver.done()
    gradient_down.start()
    own = pl.ds(pl.multiple_of(section * length, length), length)

    @pl.when(section == 0)
    def _():
        grads_ref[own, :] = mine[...].astype(WIDE)

    @pl.when(section == 1)
    def _():
        grads_ref[own, :] = far_ref[...].astype(WIDE)

    swap.wait()
    land_z[row] = block[me, section] + land_x[...]
    copies = [
        push(land_z.at[row], land_z.at[row], z_sems, n, other, "row")
        for n, other in enumerate(others)
    ]
    for copy in copies:
        copy.start()
    for copy in copies:
        copy.wait()
    result = land_z[0]
    for n in range(1, land_z.shape[0]):
        result = result + land_z[n]
    sums_ref[...] = result
    gradient_up.wait()
    gradient_down.wait()
    grads_ref[pl.ds(pl.multiple_of(away * length, length), length), :] = land[...].astype(WIDE)
    parts.wait()


def last_kernel(up_ref, down1_ref, down2_ref, got_up, got_down1, got_down2, sems):
    barrier = pltpu.get_barrier_semaphore()
    other = 1 - lax.axis_index("section")
    pl.semaphore_signal(barrier, inc=1, device_id={"section": other}, device_id_type=MESH)
    pl.semaphore_wait(barrier, 1)
    parts = OneWay([(up_ref, got_up)], [(down1_ref, got_down1), (down2_ref, got_down2)], sems)
    parts.start()
    parts.wait()


VM = pl.BlockSpec(memory_space=pltpu.VMEM)
ANY = pl.BlockSpec(memory_space=pl.ANY)
PAIRS = pltpu.SemaphoreType.DMA((2, 3 * PARTS))
LOCAL = pltpu.SemaphoreType.DMA((4,))


def shape(dims, kind=LOW):
    return jax.ShapeDtypeStruct(dims, kind)


def launch(
    body, number, rows, in_specs, ins, outs, out_specs, scratch, swaps=(), diagonal=False, across=False, late=(),
):
    n_in, n_out, n = len(ins), len(outs), len(swaps)
    held_in = [i for i in range(n_in) if in_specs[i] is VM]
    held_out = [i for i in range(n_out) if out_specs[i] is VM]

    def kernel(*refs):
        refs = list(refs)
        takes, sources = refs[:n_in], refs[n_in : n_in + n]
        gives = refs[n_in + n : n_in + n + n_out]
        lands = refs[n_in + n + n_out : n_in + 2 * n + n_out]
        rest = refs[n_in + 2 * n + n_out :]
        own, rest = rest[: len(scratch)], rest[len(scratch) :]
        in_held, rest = rest[: len(held_in)], rest[len(held_in) :]
        out_held, rest = rest[: len(held_out)], rest[len(held_out) :]
        in_sems, out_sems, swap_sems = rest
        group = Group(rows)
        for k, i in enumerate(held_in):
            group.loads[i] = pltpu.make_async_copy(takes[i], in_held[k], in_sems.at[k])
            group.loads[i].start()
            takes[i] = in_held[k]
        for k, i in enumerate(held_out):
            group.stores[i] = pltpu.make_async_copy(out_held[k], gives[i], out_sems.at[k])
            gives[i] = out_held[k]
        group.greet(n or across, diagonal)
        other = 1 - lax.axis_index("section")
        copies = [
            push(source, land, swap_sems, i, other, "section")
            for i, (source, land) in enumerate(zip(sources, lands))
        ]
        for copy in copies:
            copy.start()
        group.need(*[i for i in held_in if i not in late])
        body(group, *takes, *gives, *own)
        group.emit(*[i for i in held_out if i not in group.begun])
        for copy in copies:
            copy.wait()
        for i in held_out:
            group.stores[i].wait()

    results = pl.pallas_call(
        kernel,
        out_shape=(*outs, *[shape(s.shape, s.dtype) for s in swaps]),
        in_specs=[ANY] * (n_in + n),
        out_specs=(ANY,) * (n_out + n),
        scratch_shapes=[
            *scratch,
            *[pltpu.VMEM(ins[i].shape, ins[i].dtype) for i in held_in],
            *[pltpu.VMEM(outs[i].shape, outs[i].dtype) for i in held_out],
            pltpu.SemaphoreType.DMA((len(held_in),)),
            pltpu.SemaphoreType.DMA((len(held_out),)),
            pltpu.SemaphoreType.DMA((2, max(n, 1))),
        ],
        compiler_params=pltpu.CompilerParams(
            collective_id=number, has_side_effects=True, vmem_limit_bytes=GRANT
        ),
        cost_estimate=pl.CostEstimate(flops=int(3e10), bytes_accessed=30 * MEBI, transcendentals=0),
    )(*ins, *swaps)
    return results[:n_out], results[n_out:]


def start_call(number, tokens, cotangent, small, expand, contract, columns):
    width = tokens.shape[1]
    size = width * columns
    kinds = small.shape[0]
    outs = (shape((LENGTH, size)), shape((LENGTH, size)), shape((2, columns, kinds, width)), shape(expand.shape), shape(contract.shape))
    blocks = pltpu.VMEM((columns, LENGTH, width), LOW)
    vectors = pltpu.VMEM((columns, kinds, width), LOW)
    return pl.pallas_call(
        start_kernel,
        out_shape=outs,
        in_specs=[ANY] * 5,
        out_specs=(VM, VM, VM, ANY, ANY),
        scratch_shapes=[
            blocks, blocks, vectors, vectors, PAIRS, PAIRS,
            pltpu.SemaphoreType.DMA((2, 3 * PARTS + 3)), LOCAL,
        ],
        compiler_params=pltpu.CompilerParams(
            collective_id=number, has_side_effects=True, vmem_limit_bytes=GRANT
        ),
        cost_estimate=pl.CostEstimate(flops=int(3e10), bytes_accessed=30 * MEBI, transcendentals=0),
    )(tokens, cotangent, small, expand, contract)


def attend_call(number, gathered, x, pair, vec, bias, rows, width, swaps):
    size = vec.shape[1]
    heads = width // HEAD
    outs = (
        shape((LENGTH, size) if not gathered else (16, 128)),
        shape((LENGTH, size)),
        shape((3 * heads, LENGTH, HEAD)),
        shape((LENGTH, width)),
        shape((8, LENGTH), WIDE),
        shape((rows, size), WIDE),
        shape((rows, size)),
    )
    scratch = [
        pltpu.VMEM((size, 4 * width), LOW),
        pltpu.VMEM((heads, LENGTH, HEAD), LOW),
        *scatter_scratch(rows, size), PAIRS, LOCAL,
    ]
    return launch(
        functools.partial(attend_kernel, gathered, heads),
        number, rows, [VM, ANY, ANY, VM, VM], (x, *pair, vec, bias), outs, (VM,) * 7, scratch, swaps,
    )


def widen_call(number, second, pair, bias, grad, swaps):
    rows, size = second.shape
    wide = bias.shape[1]
    last = grad is not None
    ins, in_specs = [second, *pair, bias], [VM, ANY, ANY, VM]
    outs = [shape((LENGTH, size)), shape((LENGTH, wide)), shape((LENGTH, wide))]
    if last:
        ins, in_specs, outs = ins + [grad], in_specs + [VM], outs + [shape((size, wide))]
    scratch = [pltpu.VMEM((size, wide), LOW), PAIRS, LOCAL]
    return launch(
        functools.partial(widen_kernel, last),
        number, rows, in_specs, ins, outs, (VM,) * len(outs), scratch, swaps, late=(4,),
    )


def contract_call(number, active, hidden, pair, vec, swaps):
    rows, size = hidden.shape
    wide = active.shape[1]
    scratch = [pltpu.VMEM((size, wide), LOW), *scatter_scratch(rows, size), LOCAL]
    return launch(
        contract_kernel, number, rows, [VM, VM, ANY, ANY, VM], (active, hidden, *pair, vec),
        [shape((rows, size))], (VM,), scratch, swaps, late=(1,),
    )


def late_expand_call(number, active, hidden, contract, expand, grad, slope, second, vec, swaps):
    rows, size = hidden.shape
    wide = slope.shape[1]
    outs = [
        shape((rows, size), WIDE), shape((rows, size)), shape((8, size), WIDE),
        shape((size, wide)), shape((rows, size)),
    ]
    scratch = [
        pltpu.VMEM((size, wide), LOW),
        pltpu.VMEM((size, wide), LOW),
        pltpu.VMEM((LENGTH, wide), LOW),
        *scatter_scratch(rows, size), *scatter_scratch(rows, size), LOCAL,
    ]
    return launch(
        late_expand_kernel,
        number, rows, [VM, VM, ANY, ANY, ANY, ANY, VM, VM, VM, VM],
        (active, hidden, *contract, *expand, grad, slope, second, vec),
        outs, [VM] * 5, scratch, swaps, late=(1, 6, 7, 8),
    )


def expand_back_call(number, grad, contract, expand, slope, active, second, hidden, vec, swaps):
    rows, size = hidden.shape
    wide = slope.shape[1]
    half = wide // 2
    outs = [
        shape((rows, size), WIDE), shape((rows, size)), shape((8, size), WIDE),
        shape((size, half)), shape((size, half)), shape((LENGTH, size)), shape((size, half)),
    ]
    scratch = [
        pltpu.VMEM((size, wide), LOW),
        pltpu.VMEM((size, wide), LOW),
        pltpu.VMEM((LENGTH, wide), LOW),
        *scatter_scratch(rows, size), PAIRS, LOCAL,
        pltpu.VMEM((2, size, half), LOW), pltpu.VMEM((size, half), LOW),
        pltpu.SemaphoreType.DMA((2, size // TILE)),
    ]
    return launch(
        expand_back_kernel,
        number, rows, [VM, ANY, ANY, ANY, ANY, VM, VM, VM, VM, VM],
        (grad, *contract, *expand, slope, active, second, hidden, vec),
        outs, [VM] * 6 + [ANY], scratch, swaps, False, True, late=(5, 6, 7, 8),
    )


def scores_scratch(size, width, heads):
    return [
        pltpu.VMEM((size, 4 * width), LOW),
        pltpu.VMEM((LENGTH, size), LOW),
        pltpu.VMEM((heads, LENGTH, HEAD), LOW),
        pltpu.VMEM((8, LENGTH), WIDE),
        pltpu.VMEM((heads, LENGTH, HEAD), LOW),
        pltpu.VMEM((heads, LENGTH, HEAD), WIDE),
        pltpu.VMEM((heads, LENGTH, HEAD), WIDE),
    ]


def late_attend_call(number, low, grad, x_own, pair, normed, heads_all, o, lse, vec, result, y, swaps):
    rows, size = grad.shape
    width = o.shape[1]
    heads = width // HEAD
    outs = (shape((rows, size)), shape((8, size), WIDE), shape((2 * LENGTH, width)), shape((size, 4 * width)))
    scratch = [
        *scores_scratch(size, width, heads),
        pltpu.VMEM((LENGTH, 3 * width), LOW),
        pltpu.VMEM((size, 4 * width), LOW),
        pltpu.VMEM((size, width), LOW),
        pltpu.VMEM((LENGTH, width), LOW),
        pltpu.VMEM((LENGTH, width), LOW),
        pltpu.VMEM((LENGTH // rows, rows, width), LOW),
        *scatter_scratch(rows, size), PAIRS,
        pltpu.SemaphoreType.DMA((2, 3)), pltpu.SemaphoreType.DMA((2, 2)), LOCAL,
    ]
    return launch(
        functools.partial(late_attend_kernel, heads),
        number, rows, [VM, VM, VM, ANY, ANY, VM, VM, VM, VM, VM, VM, VM],
        (low, grad, x_own, *pair, normed, heads_all, o, lse, vec, result, y),
        outs, (VM, VM, VM, ANY), scratch, swaps, True, True, late=(1, 2, 5, 6, 7, 8, 10, 11),
    )


def scores_back_call(number, low, pair, heads_all, o, lse, keep, send):
    rows, size = low.shape
    width = o.shape[1]
    heads = width // HEAD
    outs = (shape((LENGTH, 3 * width)), shape((size, width)), shape(keep.shape))
    scratch = [
        *scores_scratch(size, width, heads),
        pltpu.VMEM(keep.shape, LOW),
        PAIRS, LOCAL, pltpu.SemaphoreType.DMA((2, 1)),
    ]
    return launch(
        functools.partial(scores_back_kernel, heads),
        number, rows, [VM, ANY, ANY, VM, VM, VM, VM, ANY], (low, *pair, heads_all, o, lse, keep, send),
        outs, (VM, VM, ANY), scratch, (), False, True, late=(3, 4, 5, 6),
    )[0]


def attend_back_call(number, mixed, outer, grad, x_own, pair, normed, vec):
    rows, size = grad.shape
    width = outer.shape[1]
    half = 2 * width
    outs = (shape((size, half)), shape((rows, size)), shape((8, size), WIDE))
    scratch = [
        pltpu.VMEM((size, 4 * width), LOW),
        pltpu.VMEM((2, size, half), LOW),
        pltpu.VMEM((size, half), LOW),
        *scatter_scratch(rows, size), LOCAL, pltpu.SemaphoreType.DMA((2, size // TILE)),
    ]
    return launch(
        attend_back_kernel,
        number, rows, [VM, VM, VM, VM, ANY, ANY, VM, VM],
        (mixed, outer, grad, x_own, *pair, normed, vec), outs, (ANY, VM, VM), scratch, (), False, True,
        late=(1, 2, 3, 6),
    )[0]


def finish_call(number, late, early, near, far, sums, row_count):
    rows, size = near.shape
    length, width = far.shape
    columns = length // rows
    outs = (
        shape((2 * length, width), WIDE),
        shape((16, width), WIDE),
        *[shape(part.shape) for part in (*late, *early)],
    )
    scratch = [
        pltpu.VMEM((length, width), LOW),
        pltpu.VMEM((columns, rows, width), LOW),
        pltpu.VMEM((columns, 2, 16, width), WIDE),
        pltpu.VMEM((3, 2, 8, width), WIDE),
        pltpu.VMEM((16, width), WIDE),
        pltpu.VMEM((row_count, 16, width), WIDE),
        pltpu.VMEM((length, width), LOW),
        pltpu.SemaphoreType.DMA((2, 3)),
        pltpu.SemaphoreType.DMA((2, 3)),
        pltpu.SemaphoreType.DMA((2, 3)),
        pltpu.SemaphoreType.DMA((2, row_count)),
        pltpu.SemaphoreType.DMA((2, 2)),
    ]
    return pl.pallas_call(
        finish_kernel,
        out_shape=outs,
        in_specs=[ANY] * 2 + [VM] * 6,
        out_specs=(VM, VM) + (ANY,) * 2,
        scratch_shapes=scratch,
        compiler_params=pltpu.CompilerParams(
            collective_id=number, has_side_effects=True, vmem_limit_bytes=GRANT
        ),
        cost_estimate=pl.CostEstimate(flops=int(3e10), bytes_accessed=30 * MEBI, transcendentals=0),
    )(*late, *early, near, far, *sums)


def last_call(number, *parts):
    return pl.pallas_call(
        last_kernel,
        out_shape=[shape(part.shape) for part in parts],
        in_specs=[ANY] * 3,
        out_specs=[ANY] * 3,
        scratch_shapes=[pltpu.SemaphoreType.DMA((2, 3))],
        compiler_params=pltpu.CompilerParams(collective_id=number, has_side_effects=True),
    )(*parts)


def swap_sections(value):
    return lax.ppermute(value, "section", [(0, 1), (1, 0)])


def on_device(
    tokens,
    cotangent,
    first_gain,
    first_shift,
    attend_weight,
    attend_bias,
    output_weight,
    output_bias,
    second_gain,
    second_shift,
    expand_weight,
    expand_bias,
    contract_weight,
    contract_bias,
):
    section = lax.axis_index("section")
    column = lax.axis_index("col")
    first_section = section == 0
    columns = lax.axis_size("col")
    width = tokens.shape[1]
    size = width * columns
    rows = LENGTH // columns

    def pick(early, later):
        return jnp.where(first_section, early, later)

    block_rows = attend_weight.shape[1]
    units = (
        jnp.concatenate(
            [attend_weight[0].reshape(block_rows, 3 * width), output_weight[0].T], axis=1
        ),
        expand_weight[0],
        contract_weight[0].T,
    )
    kept_blocks, sent_blocks = [], []
    for unit in units:
        half = unit.shape[1] // 2
        low, high = unit[:, :half], unit[:, half:]
        kept_blocks.append(pick(low, high))
        sent_blocks.append(pick(high, low))

    small = jnp.concatenate(
        [
            first_gain,
            first_shift,
            output_bias,
            second_gain,
            second_shift,
            contract_bias,
            attend_bias[0],
            expand_bias[0].reshape(-1, width),
        ],
        0,
    )
    filled = small.shape[0]
    small = jnp.pad(small, ((0, -filled % 16), (0, 0)))
    got_attend = swap_sections(sent_blocks[0])
    got_attend, sent_expand = lax.optimization_barrier((got_attend, sent_blocks[1]))
    x0_full, gy_full, vectors, got_expand, got_contract = start_call(
        1, tokens, cotangent, small, sent_expand, units[2], columns
    )

    def gather_blocks(block):
        return lax.all_gather(block, "row", axis=0, tiled=True)

    half = units[2].shape[1] // 2
    mats = [[], []]
    for own, got in ((kept_blocks[0], got_attend), (kept_blocks[1], got_expand)):
        for layer, block in enumerate((pick(own, got), pick(got, own))):
            mats[layer].append(gather_blocks(block))
    mats[0].append(gather_blocks(pick(kept_blocks[2], got_contract[:, half:])))
    mats[1].append(gather_blocks(pick(got_contract, units[2])))
    vectors = vectors.astype(WIDE)
    wide_vectors = jnp.swapaxes(vectors[:, :, :6], 1, 2).reshape(2, 6, size)
    wide_vectors = jnp.pad(wide_vectors, ((0, 0), (0, 2), (0, 0)))
    own_vectors = lax.dynamic_index_in_dim(vectors, column, 1, keepdims=False)
    attend_biases = jnp.stack(
        [own_vectors[:, 6], jnp.zeros_like(own_vectors[:, 6]), own_vectors[:, 7]], 1
    ).reshape(2, 1, 3 * width)
    expand_biases = own_vectors[:, 8:filled].reshape(2, 1, -1)

    def own_rows(full):
        return lax.dynamic_slice_in_dim(full, column * rows, rows, 0)

    def own_features(full):
        return lax.dynamic_slice_in_dim(full, column * width, width, 1)

    attn = (mats[0][0], swap_sections(mats[0][0]))
    x = x0_full
    kept, pairs = [], []
    owns = [own_rows(x0_full)]
    for layer in range(2):
        last = layer == 1
        vec = wide_vectors[layer]
        (full, normed, heads, o, lse, hidden, second_own), (other,) = attend_call(
            2 + 3 * layer, not last, x, attn, vec, attend_biases[layer], rows, width, [mats[layer][1]]
        )
        expand = (mats[layer][1], other)
        outs, others = widen_call(
            3 + 3 * layer, second_own, expand, expand_biases[layer],
            gy_full if last else None, [] if last else [mats[0][2]],
        )
        second, active, slope = outs[:3]
        contract = (mats[layer][2], mats[layer][2] if last else others[0])
        if last:
            c1 = outs[3]
        pairs.append((attn, expand, contract))
        kept.append((normed, heads, o, lse, hidden, second, active, slope))
        if not last:
            (x,), others = contract_call(4, active, hidden, contract, vec, [mats[1][0]])
            owns.append(x)
            attn = (mats[1][0], others[0])
    y0 = own_features(full)

    def scatter(total):
        return lax.psum_scatter(total, "row", scatter_dimension=0, tiled=True)

    def tie(value, then):
        return lax.optimization_barrier((value, then))

    attn, expand, contract = pairs[1]
    normed, heads, o, lse, hidden, second, active, slope = kept[1]
    (grad_hidden, low, expand_sums1, e1, result), _ = late_expand_call(
        8, active, hidden, contract, expand, gy_full, slope, second, wide_vectors[1], []
    )
    (gx1_own, attend_sums1, layer_outputs, w1), _ = late_attend_call(
        10, low, grad_hidden, owns[1], attn, normed, heads, o, lse, wide_vectors[1], result, y0, []
    )

    attn, expand, contract = pairs[0]
    normed, heads, o, lse, hidden, second, active, slope = kept[0]
    part_c1 = scatter(c1)
    (grad_hidden, low, expand_sums0, ek0, es0, gx1_full, total_c0), (far_c1,) = expand_back_call(
        12, gx1_own, contract, expand, slope, active, second, hidden, wide_vectors[0], [part_c1]
    )
    part_e1, low = tie(scatter(e1), low)
    mixed, outer, total_e0 = scores_back_call(14, low, attn, heads, o, lse, ek0, es0)
    part_w1, mixed = tie(scatter(w1), mixed)
    part_c0, mixed = tie(scatter(total_c0), mixed)
    total_w0, gx0_own, attend_sums0 = attend_back_call(
        15, mixed, outer, grad_hidden, owns[0], attn, normed, wide_vectors[0]
    )
    part_e0, gx0_own = tie(scatter(total_e0), gx0_own)
    input_grads, small_grads, far_e1, far_c0 = finish_call(
        16,
        (part_e1,),
        (part_c0,),
        gx0_own,
        own_features(gx1_full),
        (attend_sums0, expand_sums0, attend_sums1, expand_sums1),
        lax.axis_size("row"),
    )

    part_w0, small_grads = tie(scatter(total_w0), small_grads)
    far_w1, far_e0, far_w0 = last_call(17, part_w1, part_e0, part_w0)

    units = []
    for late, far_late, early, far_early in (
        (part_w1, far_w1, part_w0, far_w0),
        (part_e1, far_e1, part_e0, far_e0),
        (part_c1, far_c1, part_c0, far_c0),
    ):
        whole = jnp.concatenate([early, far_early], 1).astype(WIDE)
        units.append(pick(whole, late.astype(WIDE) + far_late.astype(WIDE)))
    attn_part, expand_part, contract_part = units

    return (
        layer_outputs[None],
        input_grads[None],
        small_grads[0:1],
        small_grads[1:2],
        attn_part[:, : 3 * width].reshape(block_rows, 3, width)[None],
        small_grads[8:10][None],
        attn_part[:, 3 * width :].T[None],
        small_grads[2:3],
        small_grads[3:4],
        small_grads[4:5],
        expand_part[None],
        small_grads[10 : 10 + expand_bias.shape[1] // width].reshape(1, -1),
        contract_part.T[None],
        small_grads[5:6],
    )


def solution(mesh):
    return jax.shard_map(
        on_device,
        mesh=mesh,
        in_specs=(
            P("row", "col"),
            P("row", "col"),
            P("section", "col"),
            P("section", "col"),
            P("section", "row", None, "col"),
            P("section", None, "col"),
            P("section", "col", "row"),
            P("section", "col"),
            P("section", "col"),
            P("section", "col"),
            P("section", "row", "col"),
            P("section", "col"),
            P("section", "col", "row"),
            P("section", "col"),
        ),
        out_specs=(
            P("section", "row", "col"),
            P("section", "row", "col"),
            P("section", "col"),
            P("section", "col"),
            P("section", "row", None, "col"),
            P("section", None, "col"),
            P("section", "col", "row"),
            P("section", "col"),
            P("section", "col"),
            P("section", "col"),
            P("section", "row", "col"),
            P("section", "col"),
            P("section", "col", "row"),
            P("section", "col"),
        ),
        check_vma=False,
    )
```

```python
import functools

import jax
import jax.numpy as jnp
from jax import lax
from jax.experimental import pallas as pl
from jax.experimental.pallas import tpu as pltpu
from jax.sharding import PartitionSpec as P

HEAD = 64
LENGTH = 1024
EPS = 1e-05
LOW = jnp.bfloat16
WIDE = jnp.float32
MESH = pl.DeviceIdType.MESH
PARTS = 2
TILE = 256
MEBI = 1024 * 1024
GRANT = 58 * MEBI


def nn(left, right):
    return lax.dot_general(left, right, (((1,), (0,)), ((), ())), preferred_element_type=WIDE)


def nt(left, right):
    return lax.dot_general(left, right, (((1,), (1,)), ((), ())), preferred_element_type=WIDE)


def tn(left, right):
    return lax.dot_general(left, right, (((0,), (0,)), ((), ())), preferred_element_type=WIDE)


def turned(values):
    width = values.shape[1]
    unit = (
        lax.broadcasted_iota(jnp.int32, (width, width), 0) == lax.broadcasted_iota(jnp.int32, (width, width), 1)
    ).astype(LOW)
    return nt(unit, values)


def normalise(values):
    center = jnp.mean(values, axis=1, keepdims=True)
    centred = values - center
    scale = lax.rsqrt(jnp.mean(centred * centred, axis=1, keepdims=True) + EPS)
    return centred * scale, scale


def norm_backward(grad, hat, scale, gain):
    scaled = grad * gain
    mean_one = jnp.mean(scaled, axis=1, keepdims=True)
    mean_two = jnp.mean(scaled * hat, axis=1, keepdims=True)
    return scale * (scaled - mean_one - hat * mean_two)


class Group:
    def __init__(self, rows):
        self.me = lax.axis_index("col")
        chip, core = self.me // 2, self.me % 2
        self.sib = chip * 2 + 1 - core
        self.peer = (1 - chip) * 2 + core
        self.diag = (1 - chip) * 2 + 1 - core
        self.rows = rows
        self.part = rows // PARTS
        self.loads, self.stores, self.begun = {}, {}, set()

    def need(self, *places):
        for place in places:
            self.loads[place].wait()

    def emit(self, *places):
        for place in places:
            self.stores[place].start()
            self.begun.add(place)

    def greet(self, swaps, diagonal, rows=()):
        barrier = pltpu.get_barrier_semaphore()
        others = [{"col": self.sib}, {"col": self.peer}]
        if diagonal:
            others.append({"col": self.diag})
        if swaps:
            others.append({"section": 1 - lax.axis_index("section")})
        others += [{"row": row} for row in rows]
        for other in others:
            pl.semaphore_signal(barrier, inc=1, device_id=other, device_id_type=MESH)
        pl.semaphore_wait(barrier, len(others))

    def slab(self, owner, j):
        return pl.ds(pl.multiple_of(owner * self.rows + j * self.part, self.part), self.part)

    def chunk(self, owner):
        return pl.ds(pl.multiple_of(owner * self.rows, self.rows), self.rows)


def push(src, dst, sems, slot, target, axis="col"):
    return pltpu.make_async_remote_copy(
        src_ref=src,
        dst_ref=dst,
        send_sem=sems.at[0, slot],
        recv_sem=sems.at[1, slot],
        device_id={axis: target},
        device_id_type=MESH,
    )


class Gather:
    def __init__(self, group, full, sems, blocks=False):
        self.group, self.full, self.sems, self.blocks = group, full, sems, blocks

    def piece(self, owner, j):
        if not self.blocks:
            return self.full.at[self.group.slab(owner, j)]
        part = self.full.shape[1] // PARTS
        return self.full.at[owner, pl.ds(j * part, part)]

    def start(self):
        g = self.group
        self.over, self.near, self.relayed = [], [], []
        for j in range(PARTS):
            piece = self.piece(g.me, j)
            self.over.append(push(piece, piece, self.sems, j, g.peer))
            self.over[-1].start()
        for j in range(PARTS):
            piece = self.piece(g.me, j)
            self.near.append(push(piece, piece, self.sems, PARTS + j, g.sib))
            self.near[-1].start()

    def sibling(self):
        for copy in self.near:
            copy.wait_recv()

    def relay(self):
        g = self.group
        for j in range(PARTS):
            self.over[j].wait_recv()
            piece = self.piece(g.peer, j)
            self.relayed.append(push(piece, piece, self.sems, 2 * PARTS + j, g.sib))
            self.relayed[-1].start()

    def diagonal(self):
        for copy in self.relayed:
            copy.wait_recv()

    def done(self):
        for copy in self.over + self.near + self.relayed:
            copy.wait_send()

    def each(self, body, first=None):
        g = self.group
        self.start()
        if first is not None:
            first()
        body(g.me)
        self.sibling()
        body(g.sib)
        self.relay()
        body(g.peer)
        self.diagonal()
        body(g.diag)
        self.done()


class Scatter:
    def __init__(self, group, stage, land, total, sems):
        self.group, self.stage, self.land, self.total, self.sems = group, stage, land, total, sems

    def start(self, part):
        g, stage, land = self.group, self.stage, self.land
        self.first, self.over, self.near = [], [], []
        def split(owner):
            whole = part(owner)
            return [whole[j * g.part : (j + 1) * g.part] for j in range(PARTS)]

        for j, mine in enumerate(split(g.diag)):
            stage[0, j] = mine.astype(LOW)
            self.first.append(push(stage.at[0, j], land.at[0, j], self.sems, j, g.sib))
            self.first[-1].start()
        for j, mine in enumerate(split(g.peer)):
            self.first[j].wait_recv()
            stage[1, j] = (mine + land[0, j].astype(WIDE)).astype(LOW)
            self.over.append(push(stage.at[1, j], land.at[1, j], self.sems, PARTS + j, g.peer))
            self.over[-1].start()
        for j, mine in enumerate(split(g.sib)):
            stage[2, j] = mine.astype(LOW)
            self.near.append(push(stage.at[2, j], land.at[2, j], self.sems, 2 * PARTS + j, g.sib))
            self.near[-1].start()
        for j, mine in enumerate(split(g.me)):
            self.total[j] = mine

    def take(self, j):
        self.near[j].wait_recv()
        self.over[j].wait_recv()
        land = self.land
        return self.total[j] + (land[1, j].astype(WIDE) + land[2, j].astype(WIDE))

    def done(self):
        for copy in self.first + self.over + self.near:
            copy.wait_send()


class Deliver:
    def __init__(self, group, stage, out, sems):
        self.group, self.stage, self.out, self.sems = group, stage, out, sems

    def start(self, rows_ref):
        g, width = self.group, self.out.shape[1]
        for c in range(self.stage.shape[0]):
            self.stage[c] = rows_ref[:, c * width : (c + 1) * width]
        place = self.out.at[g.chunk(g.me)]
        self.copies = [
            push(self.stage.at[other], place, self.sems, n, other)
            for n, other in enumerate((g.peer, g.diag, g.sib))
        ]
        for copy in self.copies:
            copy.start()
        self.out[g.chunk(g.me), :] = self.stage[g.me]

    def done(self):
        for copy in self.copies:
            copy.wait()


class OneWay:
    def __init__(self, up, down, sems):
        self.section = lax.axis_index("section")
        both = [*up, *down]
        copies = [
            push(source, into, sems, n, 1 - self.section, "section")
            for n, (source, into) in enumerate(both)
        ]
        self.up, self.down = copies[: len(up)], copies[len(up) :]

    def each(self, first, second):
        @pl.when(self.section == 0)
        def _():
            first(self.up)
            second(self.down)

        @pl.when(self.section == 1)
        def _():
            first(self.down)
            second(self.up)

    def start(self):
        self.each(lambda copies: [copy.start() for copy in copies], lambda copies: None)

    def wait(self):
        self.each(
            lambda copies: [copy.wait_send() for copy in copies],
            lambda copies: [copy.wait_recv() for copy in copies],
        )


def scatter_scratch(rows, width):
    part = rows // PARTS
    return [
        pltpu.VMEM((3, PARTS, part, width), LOW),
        pltpu.VMEM((3, PARTS, part, width), LOW),
        pltpu.VMEM((PARTS, part, width), WIDE),
        pltpu.SemaphoreType.DMA((2, 3 * PARTS)),
    ]


class Halves:
    def __init__(self, pair, whole, sems, slot):
        if pair[0].shape[1] == whole.shape[1]:
            self.copies = [pltpu.make_async_copy(pair[0], whole, sems.at[slot])]
            return
        section = lax.axis_index("section")
        half = whole.shape[1] // 2
        self.copies = []
        for n, place in enumerate((section, 1 - section)):
            columns = pl.ds(pl.multiple_of(place * half, half), half)
            self.copies.append(
                pltpu.make_async_copy(pair[n], whole.at[:, columns], sems.at[slot + n])
            )

    def start(self):
        for copy in self.copies:
            copy.start()

    def wait(self):
        for copy in self.copies:
            copy.wait()


class Trade:
    def __init__(self, keep, send, got, sems):
        self.keep, self.send, self.got, self.sems = keep, send, got, sems
        self.tiles = keep.shape[0] // TILE

    def copy(self, n):
        rows = pl.ds(pl.multiple_of(n * TILE, TILE), TILE)
        return push(
            self.send.at[rows], self.got.at[rows], self.sems, n, 1 - lax.axis_index("section"), "section"
        )

    def start(self, make):
        @pl.loop(0, self.tiles)
        def _(n):
            make(pl.ds(pl.multiple_of(n * TILE, TILE), TILE))
            self.copy(n).start()

    def finish(self):
        @pl.loop(0, self.tiles)
        def _(n):
            self.copy(n).wait()

        add_into(self.keep, self.got)


def add_into(keep_ref, got_ref):
    @pl.loop(0, keep_ref.shape[0] // TILE)
    def _(n):
        rows = pl.ds(pl.multiple_of(n * TILE, TILE), TILE)
        keep_ref[rows, :] = (keep_ref[rows, :].astype(WIDE) + got_ref[rows, :].astype(WIDE)).astype(LOW)


def causal_scores(scores):
    size = scores.shape[1]
    keep = lax.broadcasted_iota(jnp.int32, (size, size), 0) <= lax.broadcasted_iota(
        jnp.int32, (size, size), 1
    )
    begin = scores.shape[0] - size
    last = jnp.where(keep, scores[begin:], -1000000000.0)
    return last if begin == 0 else jnp.concatenate([scores[:begin], last], 0)


def attention_out(owner, size, heads_ref, o3, lse_ref, heads):
    for i in range(heads_ref.shape[1] // size):
        rows, finish = slice(i * size, (i + 1) * size), (i + 1) * size

        @pl.when(owner == i)
        def _():
            @pl.loop(0, heads)
            def _(h):
                scores = causal_scores(nt(heads_ref[heads + h, :finish, :], heads_ref[h, rows, :]))
                highest = jnp.max(scores, axis=0, keepdims=True)
                powers = jnp.exp(scores - highest)
                summed = jnp.sum(powers, axis=0, keepdims=True)
                mixed = tn(heads_ref[2 * heads + h, :finish, :], powers.astype(LOW))
                o3[h, rows, :] = (mixed / summed).T.astype(LOW)
                lse_ref[pl.ds(h, 1), rows] = highest + jnp.log(summed)


def attention_back(owner, size, heads_ref, go3, lse_ref, dots_ref, g3, key_acc, value_acc, heads):
    for i in range(heads_ref.shape[1] // size):
        rows, finish = slice(i * size, (i + 1) * size), (i + 1) * size

        @pl.when(owner == i)
        def _():
            @pl.loop(0, heads)
            def _(h):
                queries = heads_ref[h, rows, :]
                keys = heads_ref[heads + h, :finish, :]
                grads = go3[h, rows, :]
                probs = jnp.exp(causal_scores(nt(keys, queries) - lse_ref[pl.ds(h, 1), rows]))
                grad_probs = nt(heads_ref[2 * heads + h, :finish, :], grads)
                grad_scores = (probs * (grad_probs - dots_ref[pl.ds(h, 1), rows])).astype(LOW)
                g3[h, rows, :] = (tn(grad_scores, keys) * HEAD ** (-0.5)).astype(LOW)
                key_acc[h, :finish, :] += nn(grad_scores, queries)
                value_acc[h, :finish, :] += nn(probs.astype(LOW), grads)


def start_kernel(
    tokens_ref, cotangent_ref, small_ref, expand_ref, contract_ref,
    x_ref, g_ref, vectors_ref, got_expand_ref, got_contract_ref,
    x4, g4, s4, other4, x_sems, g_sems, s_sems, local_sems,
):
    section = lax.axis_index("section")
    group = Group(x_ref.shape[0] // 4)
    length = x_ref.shape[0]
    loads = []
    rows = pl.ds(pl.multiple_of(section * length, length), length)
    for n, (source, into) in enumerate(((tokens_ref.at[rows], x4), (cotangent_ref.at[rows], g4), (small_ref, s4))):
        loads.append(pltpu.make_async_copy(source, into.at[group.me], local_sems.at[n]))
        loads[-1].start()
    group.greet(True, False)
    blocks = [
        push(source, into, s_sems, 3 * PARTS + 1 + n, 1 - section, "section")
        for n, (source, into) in enumerate(((expand_ref, got_expand_ref), (contract_ref, got_contract_ref)))
    ]
    for block in blocks:
        block.start()
    gathers = [Gather(group, x4, x_sems, True), Gather(group, s4, s_sems, True), Gather(group, g4, g_sems, True)]
    for gather, load in zip(gathers, (loads[0], loads[2], loads[1])):
        load.wait()
        gather.start()
    for gather in gathers:
        gather.sibling()
        gather.relay()
        gather.diagonal()
    swap = push(s4, other4, s_sems, 3 * PARTS, 1 - section, "section")
    swap.start()
    width = x4.shape[2]
    for c in range(x4.shape[0]):
        x_ref[:, c * width : (c + 1) * width] = x4[c]
        g_ref[:, c * width : (c + 1) * width] = g4[c]
    swap.wait()
    for block in blocks:
        block.wait()
    vectors_ref[section] = s4[...]
    vectors_ref[1 - section] = other4[...]
    for gather in gathers:
        gather.done()


def attend_kernel(
    gathered, heads, group, x_ref, mine_ref, other_ref, vec_ref, bias_ref,
    full_ref, normed_ref, heads_ref, o_ref, lse_ref, hidden_ref, second_ref,
    weight, o3, stage, land, total, scatter_sems, gather_sems, local_sems,
):
    width = o_ref.shape[1]
    halves = Halves((mine_ref, other_ref), weight, local_sems, 0)
    halves.start()
    if not gathered:
        full_ref[group.chunk(group.me), :] = x_ref[...]
    halves.wait()

    def project(owner):
        rows = group.chunk(owner)
        values = (x_ref if gathered else full_ref)[rows, :].astype(WIDE)
        hat, _ = normalise(values)
        normed = (hat * vec_ref[0:1, :] + vec_ref[1:2, :]).astype(LOW)
        normed_ref[rows, :] = normed
        mixed = nn(normed, weight[:, : 3 * width]) + bias_ref[...]
        for j in range(3 * heads):
            piece = mixed[:, j * HEAD : (j + 1) * HEAD]
            if j < heads:
                piece = piece * HEAD ** (-0.5)
            heads_ref[j, rows, :] = piece.astype(LOW)

    if gathered:
        full_ref[...] = jnp.zeros_like(full_ref)

        @pl.loop(0, LENGTH // group.rows)
        def _(n):
            project(n)
    else:
        Gather(group, full_ref, gather_sems).each(project)
    group.emit(0, 1, 2)
    lse_ref[...] = jnp.zeros_like(lse_ref)

    def attend(owner):
        rows = group.chunk(owner)
        attention_out(owner, group.rows, heads_ref, o3, lse_ref, heads)
        for h in range(heads):
            o_ref[rows, h * HEAD : (h + 1) * HEAD] = o3[h, rows, :]
        return nt(o_ref[rows, :], weight[:, 3 * width :])

    scatter = Scatter(group, stage, land, total, scatter_sems)
    scatter.start(attend)
    group.emit(3, 4)
    for j in range(PARTS):
        rows = slice(j * group.part, (j + 1) * group.part)
        residual = (x_ref if gathered else full_ref)[group.slab(group.me, j), :].astype(WIDE)
        hidden = residual + scatter.take(j) + vec_ref[2:3, :]
        hidden_ref[rows, :] = hidden
        hat, _ = normalise(hidden)
        second_ref[rows, :] = (hat * vec_ref[3:4, :] + vec_ref[4:5, :]).astype(LOW)
    scatter.done()


def outer_whole(left_ref, right_ref, out_ref):
    @pl.loop(0, left_ref.shape[1] // TILE)
    def _(n):
        rows = pl.ds(pl.multiple_of(n * TILE, TILE), TILE)
        out_ref[rows, :] = tn(left_ref[:, rows], right_ref[...]).astype(LOW)


def widen_kernel(last, group, second_ref, em_ref, eo_ref, bias_ref, *refs):
    if last:
        g_ref, *refs = refs
    full_ref, active_ref, slope_ref, *refs = refs
    if last:
        c_ref, *refs = refs
    expand, gather_sems, local_sems = refs
    halves = Halves((em_ref, eo_ref), expand, local_sems, 0)
    halves.start()
    full_ref[group.chunk(group.me), :] = second_ref[...]
    halves.wait()

    def widen(owner):
        rows = group.chunk(owner)
        t = nn(full_ref[rows, :], expand[...]) + bias_ref[...]
        square = t * t
        bent = jnp.tanh(0.7978845608028654 * t * (1.0 + 0.044715 * square))
        active_ref[rows, :] = (0.5 * t * (1.0 + bent)).astype(LOW)
        slope_ref[rows, :] = (
            0.5 * (1.0 + bent)
            + (0.5 * 0.7978845608028654) * t * (1.0 - bent * bent) * (1.0 + 3 * 0.044715 * square)
        ).astype(LOW)

    Gather(group, full_ref, gather_sems).each(widen)
    if last:
        group.emit(0, 1, 2)
        group.need(4)
        outer_whole(g_ref, active_ref, c_ref)


def outer_halves(left_ref, right_ref, keep_ref, send_ref):
    section = lax.axis_index("section")
    half = right_ref.shape[1] // 2
    for place, out in ((section, keep_ref), (1 - section, send_ref)):
        columns = pl.ds(pl.multiple_of(place * half, half), half)

        @pl.loop(0, left_ref.shape[1] // TILE)
        def _(n):
            rows = pl.ds(pl.multiple_of(n * TILE, TILE), TILE)
            out[rows, :] = tn(left_ref[:, rows], right_ref[:, columns]).astype(LOW)


def contract_kernel(
    group, active_ref, hidden_ref, cm_ref, co_ref, vec_ref, result_ref,
    contract, stage, land, total, scatter_sems, local_sems,
):
    halves = Halves((cm_ref, co_ref), contract, local_sems, 0)
    halves.start()
    halves.wait()
    scatter = Scatter(group, stage, land, total, scatter_sems)
    scatter.start(lambda owner: nt(active_ref[group.chunk(owner), :], contract[...]))
    group.need(1)
    for j in range(PARTS):
        rows = slice(j * group.part, (j + 1) * group.part)
        result = hidden_ref[rows, :] + scatter.take(j) + vec_ref[5:6, :]
        result_ref[rows, :] = result.astype(LOW)
    scatter.done()


def narrow_grads(group, scatter, full_ref, hidden_ref, vec_ref, grad_ref, low_ref, sums_ref):
    for j in range(PARTS):
        rows = slice(j * group.part, (j + 1) * group.part)
        grad = scatter.take(j)
        hat, scale = normalise(hidden_ref[rows, :])
        own = full_ref[group.slab(group.me, j), :].astype(WIDE)
        out = own + norm_backward(grad, hat, scale, vec_ref[3:4, :])
        grad_ref[rows, :] = out
        low_ref[rows, :] = out.astype(LOW)
        for n, term in enumerate((grad * hat, grad, own, out)):
            sums_ref[n : n + 1, :] += jnp.sum(term, axis=0, keepdims=True)


def bend(rows, full_ref, contract, slope_ref, before, sums_ref):
    grad = (nn(full_ref[rows, :], contract[...]) * slope_ref[rows, :].astype(WIDE)).astype(LOW)
    before[rows, :] = grad
    sums_ref[4:5, :] += jnp.sum(grad.astype(WIDE), axis=0, keepdims=True)


def late_expand_kernel(
    group, active_ref, hidden_ref, cm_ref, co_ref, em_ref, eo_ref, g_ref, slope_ref, second_ref, vec_ref,
    grad_ref, low_ref, sums_ref, e_ref, result,
    contract, expand, before,
    stage_a, land_a, total_a, sems_a, stage, land, total, scatter_sems, local_sems,
):
    first = Halves((cm_ref, co_ref), contract, local_sems, 0)
    then = Halves((em_ref, eo_ref), expand, local_sems, 2)
    first.start()
    then.start()
    sums_ref[...] = jnp.zeros_like(sums_ref)
    first.wait()
    forward = Scatter(group, stage_a, land_a, total_a, sems_a)
    forward.start(lambda owner: nt(active_ref[group.chunk(owner), :], contract[...]))
    group.need(6, 7)

    @pl.loop(0, LENGTH // group.rows)
    def _(n):
        bend(group.chunk(n), g_ref, contract, slope_ref, before, sums_ref)

    then.wait()
    scatter = Scatter(group, stage, land, total, scatter_sems)
    scatter.start(lambda owner: nt(before[group.chunk(owner), :], expand[...]))
    group.need(1)
    for j in range(PARTS):
        rows = slice(j * group.part, (j + 1) * group.part)
        result[rows, :] = (hidden_ref[rows, :] + forward.take(j) + vec_ref[5:6, :]).astype(LOW)
    group.emit(4)
    group.need(8)
    outer_whole(second_ref, before, e_ref)
    group.emit(3)
    narrow_grads(group, scatter, g_ref, hidden_ref, vec_ref, grad_ref, low_ref, sums_ref)
    group.emit(0, 1, 2)
    forward.done()
    scatter.done()


def expand_back_kernel(
    group, g_ref, cm_ref, co_ref, em_ref, eo_ref, slope_ref, active_ref, second_ref, hidden_ref, vec_ref,
    grad_ref, low_ref, sums_ref, ek_ref, es_ref, full_ref, c_ref,
    contract, expand, before, stage, land, total, scatter_sems, gather_sems, local_sems, outer, got, trade_sems,
):
    section = lax.axis_index("section")
    first = Halves((cm_ref, co_ref), contract, local_sems, 0)
    then = Halves((em_ref, eo_ref), expand, local_sems, 2)
    first.start()
    then.start()
    sums_ref[...] = jnp.zeros_like(sums_ref)
    full_ref[group.chunk(group.me), :] = g_ref[...]
    first.wait()
    Gather(group, full_ref, gather_sems).each(
        lambda owner: bend(group.chunk(owner), full_ref, contract, slope_ref, before, sums_ref),
        lambda: group.need(5),
    )
    group.emit(5)
    group.need(6)
    half = active_ref.shape[1] // 2

    def columns(place):
        return pl.ds(pl.multiple_of(place * half, half), half)

    def make(n):
        def tile(rows):
            place = section if n == 0 else 1 - section
            outer[n, rows, :] = tn(full_ref[:, rows], active_ref[:, columns(place)]).astype(LOW)

        return tile

    trade = Trade(outer.at[0], outer.at[1], got, trade_sems)
    trade.start(make(1))
    then.wait()
    scatter = Scatter(group, stage, land, total, scatter_sems)
    scatter.start(lambda owner: nt(before[group.chunk(owner), :], expand[...]))
    group.need(7)
    outer_halves(second_ref, before, ek_ref, es_ref)
    group.emit(3, 4)
    keep = make(0)

    @pl.loop(0, outer.shape[1] // TILE)
    def _(n):
        keep(pl.ds(pl.multiple_of(n * TILE, TILE), TILE))

    group.need(8)
    narrow_grads(group, scatter, full_ref, hidden_ref, vec_ref, grad_ref, low_ref, sums_ref)
    group.emit(0, 1, 2)
    scatter.done()
    trade.finish()
    store = pltpu.make_async_copy(outer.at[0], c_ref, local_sems.at[0])
    store.start()
    store.wait()


def scores_back(group, heads, low_ref, weight, heads_ref, o_ref, lse_ref, full, go3, dots, g3, accs, mixed, gather_sems, first):
    width = o_ref.shape[1]
    picks = (
        lax.broadcasted_iota(jnp.int32, (8, width), 1) // HEAD
        == lax.broadcasted_iota(jnp.int32, (8, width), 0)
    ).astype(WIDE)
    for acc in accs:
        acc[...] = jnp.zeros_like(acc)

    def spread(owner):
        rows = group.chunk(owner)
        grads = nn(full[rows, :], weight[:, 3 * width :]).astype(LOW)
        for h in range(heads):
            go3[h, rows, :] = grads[:, h * HEAD : (h + 1) * HEAD]
        term = grads.astype(WIDE) * o_ref[rows, :].astype(WIDE)
        dots[:, rows] = lax.dot_general(
            picks,
            term,
            (((1,), (1,)), ((), ())),
            precision=lax.Precision.HIGHEST,
            preferred_element_type=WIDE,
        )
        attention_back(owner, group.rows, heads_ref, go3, lse_ref, dots, g3, *accs, heads)

    full[group.chunk(group.me), :] = low_ref[...]
    Gather(group, full, gather_sems).each(spread, first)
    for j in range(3 * heads):
        source = g3[j] if j < heads else accs[j // heads - 1][j % heads].astype(LOW)
        mixed[:, j * HEAD : (j + 1) * HEAD] = source


def outer_out(full, o_ref, outer_ref):
    @pl.loop(0, outer_ref.shape[0] // TILE)
    def _(n):
        rows = pl.ds(pl.multiple_of(n * TILE, TILE), TILE)
        outer_ref[rows, :] = tn(full[:, rows], o_ref[...]).astype(LOW)


def attend_grads(group, scatter, x_ref, grad_ref, vec_ref, mixed, width, out_ref, sums_ref):
    sums_ref[2:3, : 3 * width] = jnp.sum(mixed[...].astype(WIDE), axis=0, keepdims=True)
    for j in range(PARTS):
        rows = slice(j * group.part, (j + 1) * group.part)
        grad = scatter.take(j)
        hat, scale = normalise(x_ref[rows, :].astype(WIDE))
        out = grad_ref[rows, :] + norm_backward(grad, hat, scale, vec_ref[0:1, :])
        out_ref[rows, :] = out.astype(LOW)
        for n, term in enumerate((grad * hat, grad)):
            sums_ref[n : n + 1, :] += jnp.sum(term, axis=0, keepdims=True)


def late_attend_kernel(
    heads, group, low_ref, grad_ref, x_ref, mine_ref, other_ref, normed_ref, heads_ref, o_ref, lse_ref, vec_ref,
    result_ref, y_ref,
    out_ref, sums_ref, results_ref, w_ref,
    weight, full, go3, dots, g3, key_acc, value_acc, mixed, outer, outer_o, late, y_land, stage4,
    stage, land, total, scatter_sems, gather_sems, deliver_sems, y_sems, local_sems,
):
    width = o_ref.shape[1]
    section = lax.axis_index("section")
    halves = Halves((mine_ref, other_ref), weight, local_sems, 0)
    halves.start()
    sums_ref[...] = jnp.zeros_like(sums_ref)
    halves.wait()
    deliver = Deliver(group, stage4, late, deliver_sems)

    def first():
        group.need(6, 7, 8, 10)
        deliver.start(result_ref)

    scores_back(
        group, heads, low_ref, weight, heads_ref, o_ref, lse_ref, full, go3, dots, g3,
        (key_acc, value_acc), mixed, gather_sems, first,
    )
    deliver.done()
    group.need(11)
    results = OneWay([(late, y_land)], [(y_ref, y_land)], y_sems)
    results.start()
    scatter = Scatter(group, stage, land, total, scatter_sems)
    scatter.start(lambda owner: nt(mixed[group.chunk(owner), :], weight[:, : 3 * width]))
    outer_out(full, o_ref, outer_o)
    group.need(5)

    @pl.loop(0, weight.shape[0] // TILE)
    def _(n):
        rows = pl.ds(pl.multiple_of(n * TILE, TILE), TILE)
        outer[rows, : 3 * width] = tn(normed_ref[:, rows], mixed[...]).astype(LOW)
        outer[rows, 3 * width :] = outer_o[rows, :]

    store = pltpu.make_async_copy(outer, w_ref, local_sems.at[2])
    store.start()
    length = y_ref.shape[0]
    own = pl.ds(pl.multiple_of(section * length, length), length)

    @pl.when(section == 0)
    def _():
        results_ref[:, own] = turned(y_ref[...]).astype(LOW)

    @pl.when(section == 1)
    def _():
        results_ref[:, own] = turned(late[...]).astype(LOW)

    group.need(1, 2)
    attend_grads(group, scatter, x_ref, grad_ref, vec_ref, mixed, width, out_ref, sums_ref)
    results.wait()
    away = pl.ds(pl.multiple_of((1 - section) * length, length), length)
    results_ref[:, away] = turned(y_land[...]).astype(LOW)
    scatter.done()
    store.wait()


def scores_back_kernel(
    heads, group, low_ref, mine_ref, other_ref, heads_ref, o_ref, lse_ref, ek_ref, es_ref,
    mixed, outer_ref, e_ref,
    weight, full, go3, dots, g3, key_acc, value_acc, got, gather_sems, local_sems, swap_sems,
):
    swap = push(es_ref, got, swap_sems, 0, 1 - lax.axis_index("section"), "section")
    swap.start()
    halves = Halves((mine_ref, other_ref), weight, local_sems, 0)
    halves.start()
    halves.wait()
    scores_back(
        group, heads, low_ref, weight, heads_ref, o_ref, lse_ref, full, go3, dots, g3,
        (key_acc, value_acc), mixed, gather_sems, lambda: group.need(3, 4, 5),
    )
    group.emit(0)
    outer_out(full, o_ref, outer_ref)
    group.emit(1)
    group.need(6)
    swap.wait()
    add_into(ek_ref, got)
    store = pltpu.make_async_copy(ek_ref, e_ref, local_sems.at[0])
    store.start()
    store.wait()


def attend_back_kernel(
    group, mixed, outer_ref, grad_ref, x_ref, mine_ref, other_ref, normed_ref, vec_ref,
    w_ref, out_ref, sums_ref,
    weight, outer, got, stage, land, total, scatter_sems, local_sems, swap_sems,
):
    width = outer_ref.shape[1]
    section = lax.axis_index("section")
    halves = Halves((mine_ref, other_ref), weight, local_sems, 0)
    halves.start()
    sums_ref[...] = jnp.zeros_like(sums_ref)
    half = weight.shape[1] // 2
    scatter = Scatter(group, stage, land, total, scatter_sems)
    group.need(1, 6)

    def make(n):
        place = section if n == 0 else 1 - section

        def tile(rows):
            @pl.when(place == 0)
            def _():
                outer[n, rows, :] = tn(normed_ref[:, rows], mixed[:, :half]).astype(LOW)

            @pl.when(place == 1)
            def _():
                outer[n, rows, : 3 * width - half] = tn(normed_ref[:, rows], mixed[:, half:]).astype(LOW)
                outer[n, rows, 3 * width - half :] = outer_ref[rows, :]

        return tile

    trade = Trade(outer.at[0], outer.at[1], got, swap_sems)
    trade.start(make(1))
    halves.wait()
    scatter.start(lambda owner: nt(mixed[group.chunk(owner), :], weight[:, : 3 * width]))
    keep = make(0)

    @pl.loop(0, outer.shape[1] // TILE)
    def _(n):
        keep(pl.ds(pl.multiple_of(n * TILE, TILE), TILE))

    group.need(2, 3)
    attend_grads(group, scatter, x_ref, grad_ref, vec_ref, mixed, width, out_ref, sums_ref)
    group.emit(1, 2)
    scatter.done()
    trade.finish()
    store = pltpu.make_async_copy(outer.at[0], w_ref, local_sems.at[2])
    store.start()
    store.wait()


def finish_kernel(
    early_ref, near_ref, far_ref, a0, n0, a1, n1,
    grads_ref, sums_ref, got_early,
    mine, stage4, block, land_col, land_x, land_z, land,
    deliver_sems, col_sems, x_sems, z_sems, part_sems,
):
    section, row = lax.axis_index("section"), lax.axis_index("row")
    away = 1 - section
    group = Group(near_ref.shape[0])
    length, width = far_ref.shape
    others = [lax.rem(row + d, land_z.shape[0]) for d in range(1, land_z.shape[0])]
    group.greet(True, True, others)
    gradient_up = OneWay([(far_ref, land)], [], x_sems.at[:, pl.ds(1, 1)])
    gradient_down = OneWay([], [(mine, land)], x_sems.at[:, pl.ds(2, 1)])
    parts = OneWay([], [(early_ref, got_early)], part_sems)
    deliver = Deliver(group, stage4, mine, deliver_sems)
    deliver.start(near_ref)
    gradient_up.start()
    parts.start()

    block[...] = jnp.zeros_like(block)
    for layer, (attn, narrow) in enumerate(((a0, n0), (a1, n1))):
        wide = [attn[0:1, :], attn[1:2, :], narrow[3:4, :], narrow[0:1, :], narrow[1:2, :], narrow[2:3, :]]
        for c in range(block.shape[0]):
            columns = slice(c * width, (c + 1) * width)
            for n, term in enumerate(wide):
                block[c, layer, n : n + 1, :] = term[:, columns]
            for n, term in enumerate((attn[2:3, :width], attn[2:3, 2 * width : 3 * width])):
                block[c, layer, 8 + n : 9 + n, :] = term
            for n in range(narrow.shape[1] // width):
                block[c, layer, 10 + n : 11 + n, :] = narrow[4:5, n * width : (n + 1) * width]
    copies = [
        push(block.at[other, :, pl.ds(0, 8)], land_col.at[n], col_sems, n, other)
        for n, other in enumerate((group.peer, group.diag, group.sib))
    ]
    for copy in copies:
        copy.start()
    for copy in copies:
        copy.wait()
    me = group.me
    block[me, :, :8] = block[me, :, :8] + (land_col[0] + (land_col[1] + land_col[2]))
    swap = push(block.at[me, away], land_x, x_sems, 0, away, "section")
    swap.start()
    deliver.done()
    gradient_down.start()
    own = pl.ds(pl.multiple_of(section * length, length), length)

    @pl.when(section == 0)
    def _():
        grads_ref[:, own] = turned(mine[...])

    @pl.when(section == 1)
    def _():
        grads_ref[:, own] = turned(far_ref[...])

    swap.wait()
    land_z[row] = block[me, section] + land_x[...]
    copies = [
        push(land_z.at[row], land_z.at[row], z_sems, n, other, "row")
        for n, other in enumerate(others)
    ]
    for copy in copies:
        copy.start()
    for copy in copies:
        copy.wait()
    result = land_z[0]
    for n in range(1, land_z.shape[0]):
        result = result + land_z[n]
    sums_ref[...] = result
    gradient_up.wait()
    gradient_down.wait()
    grads_ref[:, pl.ds(pl.multiple_of(away * length, length), length)] = turned(land[...])
    parts.wait()


def greet_section():
    barrier = pltpu.get_barrier_semaphore()
    other = 1 - lax.axis_index("section")
    pl.semaphore_signal(barrier, inc=1, device_id={"section": other}, device_id_type=MESH)
    pl.semaphore_wait(barrier, 1)


def up_kernel(up_ref, got_ref, sems):
    greet_section()
    part = OneWay([(up_ref, got_ref)], [], sems)
    part.start()
    part.wait()


def last_kernel(
    late1_ref, early1_ref, late2_ref, early2_ref, far2_ref, attend_ref, output_ref, expand_ref,
    own1, far1, own2, far2, sems, local_sems,
):
    section = lax.axis_index("section")
    half = early1_ref.shape[1]
    width = output_ref.shape[1]
    greet_section()
    parts = OneWay(
        [(late1_ref, far1)],
        [(early1_ref, own1.at[:, pl.ds(half, half)]), (early2_ref, own2.at[:, pl.ds(half, half)])],
        sems,
    )
    parts.start()

    def load(pairs):
        copies = [
            pltpu.make_async_copy(source, into, local_sems.at[n]) for n, (source, into) in enumerate(pairs)
        ]
        for copy in copies:
            copy.start()
        for copy in copies:
            copy.wait()

    @pl.when(section == 0)
    def _():
        load(((early1_ref, own1.at[:, pl.ds(0, half)]), (early2_ref, own2.at[:, pl.ds(0, half)])))

    @pl.when(section == 1)
    def _():
        load(((late1_ref, own1), (late2_ref, own2), (far2_ref, far2)))

    parts.wait()

    def give(first, second):
        for j in range(3):
            attend_ref[j] = first[:, j * width : (j + 1) * width]
        output_ref[...] = first[:, 3 * width :]
        expand_ref[...] = second

    @pl.when(section == 0)
    def _():
        give(own1[...].astype(WIDE), own2[...].astype(WIDE))

    @pl.when(section == 1)
    def _():
        give(
            own1[...].astype(WIDE) + far1[...].astype(WIDE),
            own2[...].astype(WIDE) + far2[...].astype(WIDE),
        )


VM = pl.BlockSpec(memory_space=pltpu.VMEM)
ANY = pl.BlockSpec(memory_space=pl.ANY)
PAIRS = pltpu.SemaphoreType.DMA((2, 3 * PARTS))
LOCAL = pltpu.SemaphoreType.DMA((4,))


def shape(dims, kind=LOW):
    return jax.ShapeDtypeStruct(dims, kind)


def launch(
    body, number, rows, in_specs, ins, outs, out_specs, scratch, swaps=(), diagonal=False, across=False, late=(),
):
    n_in, n_out, n = len(ins), len(outs), len(swaps)
    held_in = [i for i in range(n_in) if in_specs[i] is VM]
    held_out = [i for i in range(n_out) if out_specs[i] is VM]

    def kernel(*refs):
        refs = list(refs)
        takes, sources = refs[:n_in], refs[n_in : n_in + n]
        gives = refs[n_in + n : n_in + n + n_out]
        lands = refs[n_in + n + n_out : n_in + 2 * n + n_out]
        rest = refs[n_in + 2 * n + n_out :]
        own, rest = rest[: len(scratch)], rest[len(scratch) :]
        in_held, rest = rest[: len(held_in)], rest[len(held_in) :]
        out_held, rest = rest[: len(held_out)], rest[len(held_out) :]
        in_sems, out_sems, swap_sems = rest
        group = Group(rows)
        for k, i in enumerate(held_in):
            group.loads[i] = pltpu.make_async_copy(takes[i], in_held[k], in_sems.at[k])
            group.loads[i].start()
            takes[i] = in_held[k]
        for k, i in enumerate(held_out):
            group.stores[i] = pltpu.make_async_copy(out_held[k], gives[i], out_sems.at[k])
            gives[i] = out_held[k]
        group.greet(n or across, diagonal)
        other = 1 - lax.axis_index("section")
        copies = [
            push(source, land, swap_sems, i, other, "section")
            for i, (source, land) in enumerate(zip(sources, lands))
        ]
        for copy in copies:
            copy.start()
        group.need(*[i for i in held_in if i not in late])
        body(group, *takes, *gives, *own)
        group.emit(*[i for i in held_out if i not in group.begun])
        for copy in copies:
            copy.wait()
        for i in held_out:
            group.stores[i].wait()

    results = pl.pallas_call(
        kernel,
        out_shape=(*outs, *[shape(s.shape, s.dtype) for s in swaps]),
        in_specs=[ANY] * (n_in + n),
        out_specs=(ANY,) * (n_out + n),
        scratch_shapes=[
            *scratch,
            *[pltpu.VMEM(ins[i].shape, ins[i].dtype) for i in held_in],
            *[pltpu.VMEM(outs[i].shape, outs[i].dtype) for i in held_out],
            pltpu.SemaphoreType.DMA((len(held_in),)),
            pltpu.SemaphoreType.DMA((len(held_out),)),
            pltpu.SemaphoreType.DMA((2, max(n, 1))),
        ],
        compiler_params=pltpu.CompilerParams(
            collective_id=number, has_side_effects=True, vmem_limit_bytes=GRANT
        ),
        cost_estimate=pl.CostEstimate(flops=int(3e10), bytes_accessed=30 * MEBI, transcendentals=0),
    )(*ins, *swaps)
    return results[:n_out], results[n_out:]


def start_call(number, tokens, cotangent, small, expand, contract, columns):
    width = tokens.shape[1]
    size = width * columns
    kinds = small.shape[0]
    outs = (shape((LENGTH, size)), shape((LENGTH, size)), shape((2, columns, kinds, width)), shape(expand.shape), shape(contract.shape))
    blocks = pltpu.VMEM((columns, LENGTH, width), LOW)
    vectors = pltpu.VMEM((columns, kinds, width), LOW)
    return pl.pallas_call(
        start_kernel,
        out_shape=outs,
        in_specs=[ANY] * 5,
        out_specs=(VM, VM, VM, ANY, ANY),
        scratch_shapes=[
            blocks, blocks, vectors, vectors, PAIRS, PAIRS,
            pltpu.SemaphoreType.DMA((2, 3 * PARTS + 3)), LOCAL,
        ],
        compiler_params=pltpu.CompilerParams(
            collective_id=number, has_side_effects=True, vmem_limit_bytes=GRANT
        ),
        cost_estimate=pl.CostEstimate(flops=int(3e10), bytes_accessed=30 * MEBI, transcendentals=0),
    )(tokens, cotangent, small, expand, contract)


def attend_call(number, gathered, x, pair, vec, bias, rows, width, swaps):
    size = vec.shape[1]
    heads = width // HEAD
    outs = (
        shape((LENGTH, size) if not gathered else (16, 128)),
        shape((LENGTH, size)),
        shape((3 * heads, LENGTH, HEAD)),
        shape((LENGTH, width)),
        shape((8, LENGTH), WIDE),
        shape((rows, size), WIDE),
        shape((rows, size)),
    )
    scratch = [
        pltpu.VMEM((size, 4 * width), LOW),
        pltpu.VMEM((heads, LENGTH, HEAD), LOW),
        *scatter_scratch(rows, size), PAIRS, LOCAL,
    ]
    return launch(
        functools.partial(attend_kernel, gathered, heads),
        number, rows, [VM, ANY, ANY, VM, VM], (x, *pair, vec, bias), outs, (VM,) * 7, scratch, swaps,
    )


def widen_call(number, second, pair, bias, grad, swaps):
    rows, size = second.shape
    wide = bias.shape[1]
    last = grad is not None
    ins, in_specs = [second, *pair, bias], [VM, ANY, ANY, VM]
    outs = [shape((LENGTH, size)), shape((LENGTH, wide)), shape((LENGTH, wide))]
    if last:
        ins, in_specs, outs = ins + [grad], in_specs + [VM], outs + [shape((size, wide))]
    scratch = [pltpu.VMEM((size, wide), LOW), PAIRS, LOCAL]
    return launch(
        functools.partial(widen_kernel, last),
        number, rows, in_specs, ins, outs, (VM,) * len(outs), scratch, swaps, late=(4,),
    )


def contract_call(number, active, hidden, pair, vec, swaps):
    rows, size = hidden.shape
    wide = active.shape[1]
    scratch = [pltpu.VMEM((size, wide), LOW), *scatter_scratch(rows, size), LOCAL]
    return launch(
        contract_kernel, number, rows, [VM, VM, ANY, ANY, VM], (active, hidden, *pair, vec),
        [shape((rows, size))], (VM,), scratch, swaps, late=(1,),
    )


def late_expand_call(number, active, hidden, contract, expand, grad, slope, second, vec, swaps):
    rows, size = hidden.shape
    wide = slope.shape[1]
    outs = [
        shape((rows, size), WIDE), shape((rows, size)), shape((8, size), WIDE),
        shape((size, wide)), shape((rows, size)),
    ]
    scratch = [
        pltpu.VMEM((size, wide), LOW),
        pltpu.VMEM((size, wide), LOW),
        pltpu.VMEM((LENGTH, wide), LOW),
        *scatter_scratch(rows, size), *scatter_scratch(rows, size), LOCAL,
    ]
    return launch(
        late_expand_kernel,
        number, rows, [VM, VM, ANY, ANY, ANY, ANY, VM, VM, VM, VM],
        (active, hidden, *contract, *expand, grad, slope, second, vec),
        outs, [VM] * 5, scratch, swaps, late=(1, 6, 7, 8),
    )


def expand_back_call(number, grad, contract, expand, slope, active, second, hidden, vec, swaps):
    rows, size = hidden.shape
    wide = slope.shape[1]
    half = wide // 2
    outs = [
        shape((rows, size), WIDE), shape((rows, size)), shape((8, size), WIDE),
        shape((size, half)), shape((size, half)), shape((LENGTH, size)), shape((size, half)),
    ]
    scratch = [
        pltpu.VMEM((size, wide), LOW),
        pltpu.VMEM((size, wide), LOW),
        pltpu.VMEM((LENGTH, wide), LOW),
        *scatter_scratch(rows, size), PAIRS, LOCAL,
        pltpu.VMEM((2, size, half), LOW), pltpu.VMEM((size, half), LOW),
        pltpu.SemaphoreType.DMA((2, size // TILE)),
    ]
    return launch(
        expand_back_kernel,
        number, rows, [VM, ANY, ANY, ANY, ANY, VM, VM, VM, VM, VM],
        (grad, *contract, *expand, slope, active, second, hidden, vec),
        outs, [VM] * 6 + [ANY], scratch, swaps, False, True, late=(5, 6, 7, 8),
    )


def scores_scratch(size, width, heads):
    return [
        pltpu.VMEM((size, 4 * width), LOW),
        pltpu.VMEM((LENGTH, size), LOW),
        pltpu.VMEM((heads, LENGTH, HEAD), LOW),
        pltpu.VMEM((8, LENGTH), WIDE),
        pltpu.VMEM((heads, LENGTH, HEAD), LOW),
        pltpu.VMEM((heads, LENGTH, HEAD), WIDE),
        pltpu.VMEM((heads, LENGTH, HEAD), WIDE),
    ]


def late_attend_call(number, low, grad, x_own, pair, normed, heads_all, o, lse, vec, result, y, swaps):
    rows, size = grad.shape
    width = o.shape[1]
    heads = width // HEAD
    outs = (shape((rows, size)), shape((8, size), WIDE), shape((width, 2 * LENGTH)), shape((size, 4 * width)))
    scratch = [
        *scores_scratch(size, width, heads),
        pltpu.VMEM((LENGTH, 3 * width), LOW),
        pltpu.VMEM((size, 4 * width), LOW),
        pltpu.VMEM((size, width), LOW),
        pltpu.VMEM((LENGTH, width), LOW),
        pltpu.VMEM((LENGTH, width), LOW),
        pltpu.VMEM((LENGTH // rows, rows, width), LOW),
        *scatter_scratch(rows, size), PAIRS,
        pltpu.SemaphoreType.DMA((2, 3)), pltpu.SemaphoreType.DMA((2, 2)), LOCAL,
    ]
    return launch(
        functools.partial(late_attend_kernel, heads),
        number, rows, [VM, VM, VM, ANY, ANY, VM, VM, VM, VM, VM, VM, VM],
        (low, grad, x_own, *pair, normed, heads_all, o, lse, vec, result, y),
        outs, (VM, VM, VM, ANY), scratch, swaps, True, True, late=(1, 2, 5, 6, 7, 8, 10, 11),
    )


def scores_back_call(number, low, pair, heads_all, o, lse, keep, send):
    rows, size = low.shape
    width = o.shape[1]
    heads = width // HEAD
    outs = (shape((LENGTH, 3 * width)), shape((size, width)), shape(keep.shape))
    scratch = [
        *scores_scratch(size, width, heads),
        pltpu.VMEM(keep.shape, LOW),
        PAIRS, LOCAL, pltpu.SemaphoreType.DMA((2, 1)),
    ]
    return launch(
        functools.partial(scores_back_kernel, heads),
        number, rows, [VM, ANY, ANY, VM, VM, VM, VM, ANY], (low, *pair, heads_all, o, lse, keep, send),
        outs, (VM, VM, ANY), scratch, (), False, True, late=(3, 4, 5, 6),
    )[0]


def attend_back_call(number, mixed, outer, grad, x_own, pair, normed, vec):
    rows, size = grad.shape
    width = outer.shape[1]
    half = 2 * width
    outs = (shape((size, half)), shape((rows, size)), shape((8, size), WIDE))
    scratch = [
        pltpu.VMEM((size, 4 * width), LOW),
        pltpu.VMEM((2, size, half), LOW),
        pltpu.VMEM((size, half), LOW),
        *scatter_scratch(rows, size), LOCAL, pltpu.SemaphoreType.DMA((2, size // TILE)),
    ]
    return launch(
        attend_back_kernel,
        number, rows, [VM, VM, VM, VM, ANY, ANY, VM, VM],
        (mixed, outer, grad, x_own, *pair, normed, vec), outs, (ANY, VM, VM), scratch, (), False, True,
        late=(1, 2, 3, 6),
    )[0]


def finish_call(number, early, near, far, sums, row_count):
    rows, size = near.shape
    length, width = far.shape
    columns = length // rows
    outs = (
        shape((width, 2 * length), WIDE),
        shape((16, width), WIDE),
        shape(early.shape),
    )
    scratch = [
        pltpu.VMEM((length, width), LOW),
        pltpu.VMEM((columns, rows, width), LOW),
        pltpu.VMEM((columns, 2, 16, width), WIDE),
        pltpu.VMEM((3, 2, 8, width), WIDE),
        pltpu.VMEM((16, width), WIDE),
        pltpu.VMEM((row_count, 16, width), WIDE),
        pltpu.VMEM((length, width), LOW),
        pltpu.SemaphoreType.DMA((2, 3)),
        pltpu.SemaphoreType.DMA((2, 3)),
        pltpu.SemaphoreType.DMA((2, 3)),
        pltpu.SemaphoreType.DMA((2, row_count)),
        pltpu.SemaphoreType.DMA((2, 2)),
    ]
    return pl.pallas_call(
        finish_kernel,
        out_shape=outs,
        in_specs=[ANY] + [VM] * 6,
        out_specs=(VM, VM, ANY),
        scratch_shapes=scratch,
        compiler_params=pltpu.CompilerParams(
            collective_id=number, has_side_effects=True, vmem_limit_bytes=GRANT
        ),
        cost_estimate=pl.CostEstimate(flops=int(3e10), bytes_accessed=30 * MEBI, transcendentals=0),
    )(early, near, far, *sums)


def up_call(number, part):
    return pl.pallas_call(
        up_kernel,
        out_shape=shape(part.shape),
        in_specs=[ANY],
        out_specs=ANY,
        scratch_shapes=[pltpu.SemaphoreType.DMA((2, 1))],
        compiler_params=pltpu.CompilerParams(collective_id=number, has_side_effects=True),
        cost_estimate=pl.CostEstimate(flops=int(1e10), bytes_accessed=10 * MEBI, transcendentals=0),
    )(part)


def last_call(number, width, *parts):
    rows, size = parts[0].shape
    return pl.pallas_call(
        last_kernel,
        out_shape=(shape((3, rows, width), WIDE), shape((rows, width), WIDE), shape((rows, size), WIDE)),
        in_specs=[ANY] * 5,
        out_specs=(VM,) * 3,
        scratch_shapes=[pltpu.VMEM((rows, size), LOW)] * 4
        + [pltpu.SemaphoreType.DMA((2, 3)), pltpu.SemaphoreType.DMA((3,))],
        compiler_params=pltpu.CompilerParams(
            collective_id=number, has_side_effects=True, vmem_limit_bytes=32 * MEBI
        ),
    )(*parts)


def swap_sections(value):
    return lax.ppermute(value, "section", [(0, 1), (1, 0)])


def on_device(
    tokens,
    cotangent,
    first_gain,
    first_shift,
    attend_weight,
    attend_bias,
    output_weight,
    output_bias,
    second_gain,
    second_shift,
    expand_weight,
    expand_bias,
    contract_weight,
    contract_bias,
):
    section = lax.axis_index("section")
    column = lax.axis_index("col")
    first_section = section == 0
    columns = lax.axis_size("col")
    width = tokens.shape[1]
    size = width * columns
    rows = LENGTH // columns

    def pick(early, later):
        return jnp.where(first_section, early, later)

    block_rows = attend_weight.shape[1]
    units = (
        jnp.concatenate(
            [attend_weight[0].reshape(block_rows, 3 * width), output_weight[0].T], axis=1
        ),
        expand_weight[0],
        contract_weight[0].T,
    )
    kept_blocks, sent_blocks = [], []
    for unit in units:
        half = unit.shape[1] // 2
        low, high = unit[:, :half], unit[:, half:]
        kept_blocks.append(pick(low, high))
        sent_blocks.append(pick(high, low))

    small = jnp.concatenate(
        [
            first_gain,
            first_shift,
            output_bias,
            second_gain,
            second_shift,
            contract_bias,
            attend_bias[0],
            expand_bias[0].reshape(-1, width),
        ],
        0,
    )
    filled = small.shape[0]
    small = jnp.pad(small, ((0, -filled % 16), (0, 0)))
    got_attend = swap_sections(sent_blocks[0])
    got_attend, sent_expand = lax.optimization_barrier((got_attend, sent_blocks[1]))
    x0_full, gy_full, vectors, got_expand, got_contract = start_call(
        1, tokens, cotangent, small, sent_expand, units[2], columns
    )

    def gather_blocks(block):
        return lax.all_gather(block, "row", axis=0, tiled=True)

    half = units[2].shape[1] // 2
    mats = [[], []]
    for own, got in ((kept_blocks[0], got_attend), (kept_blocks[1], got_expand)):
        for layer, block in enumerate((pick(own, got), pick(got, own))):
            mats[layer].append(gather_blocks(block))
    mats[0].append(gather_blocks(pick(kept_blocks[2], got_contract[:, half:])))
    mats[1].append(gather_blocks(pick(got_contract, units[2])))
    vectors = vectors.astype(WIDE)
    wide_vectors = jnp.swapaxes(vectors[:, :, :6], 1, 2).reshape(2, 6, size)
    wide_vectors = jnp.pad(wide_vectors, ((0, 0), (0, 2), (0, 0)))
    own_vectors = lax.dynamic_index_in_dim(vectors, column, 1, keepdims=False)
    attend_biases = jnp.stack(
        [own_vectors[:, 6], jnp.zeros_like(own_vectors[:, 6]), own_vectors[:, 7]], 1
    ).reshape(2, 1, 3 * width)
    expand_biases = own_vectors[:, 8:filled].reshape(2, 1, -1)

    def own_rows(full):
        return lax.dynamic_slice_in_dim(full, column * rows, rows, 0)

    def own_features(full):
        return lax.dynamic_slice_in_dim(full, column * width, width, 1)

    attn = (mats[0][0], swap_sections(mats[0][0]))
    x = x0_full
    kept, pairs = [], []
    owns = [own_rows(x0_full)]
    for layer in range(2):
        last = layer == 1
        vec = wide_vectors[layer]
        (full, normed, heads, o, lse, hidden, second_own), (other,) = attend_call(
            2 + 3 * layer, not last, x, attn, vec, attend_biases[layer], rows, width, [mats[layer][1]]
        )
        expand = (mats[layer][1], other)
        outs, others = widen_call(
            3 + 3 * layer, second_own, expand, expand_biases[layer],
            gy_full if last else None, [] if last else [mats[0][2]],
        )
        second, active, slope = outs[:3]
        contract = (mats[layer][2], mats[layer][2] if last else others[0])
        if last:
            c1 = outs[3]
        pairs.append((attn, expand, contract))
        kept.append((normed, heads, o, lse, hidden, second, active, slope))
        if not last:
            (x,), others = contract_call(4, active, hidden, contract, vec, [mats[1][0]])
            owns.append(x)
            attn = (mats[1][0], others[0])
    y0 = own_features(full)

    def scatter(total):
        return lax.psum_scatter(total, "row", scatter_dimension=0, tiled=True)

    def tie(value, then):
        return lax.optimization_barrier((value, then))

    attn, expand, contract = pairs[1]
    normed, heads, o, lse, hidden, second, active, slope = kept[1]
    (grad_hidden, low, expand_sums1, e1, result), _ = late_expand_call(
        8, active, hidden, contract, expand, gy_full, slope, second, wide_vectors[1], []
    )
    (gx1_own, attend_sums1, layer_outputs, w1), _ = late_attend_call(
        10, low, grad_hidden, owns[1], attn, normed, heads, o, lse, wide_vectors[1], result, y0, []
    )

    attn, expand, contract = pairs[0]
    normed, heads, o, lse, hidden, second, active, slope = kept[0]
    part_c1 = scatter(c1)
    (grad_hidden, low, expand_sums0, ek0, es0, gx1_full, total_c0), (far_c1,) = expand_back_call(
        12, gx1_own, contract, expand, slope, active, second, hidden, wide_vectors[0], [part_c1]
    )
    part_e1, low = tie(scatter(e1), low)
    mixed, outer, total_e0 = scores_back_call(14, low, attn, heads, o, lse, ek0, es0)
    part_w1, mixed = tie(scatter(w1), mixed)
    part_e1, mixed = tie(part_e1, mixed)
    far_e1, mixed = tie(up_call(18, part_e1), mixed)
    part_c0, mixed = tie(scatter(total_c0), mixed)
    total_w0, gx0_own, attend_sums0 = attend_back_call(
        15, mixed, outer, grad_hidden, owns[0], attn, normed, wide_vectors[0]
    )
    part_e0, gx0_own = tie(scatter(total_e0), gx0_own)
    input_grads, small_grads, far_c0 = finish_call(
        16,
        part_c0,
        gx0_own,
        own_features(gx1_full),
        (attend_sums0, expand_sums0, attend_sums1, expand_sums1),
        lax.axis_size("row"),
    )

    part_w0, small_grads = tie(scatter(total_w0), small_grads)
    attend_part, output_part, expand_part = last_call(
        17, width, part_w1, part_w0, part_e1, part_e0, far_e1
    )
    contract_part = pick(
        jnp.concatenate([part_c0, far_c0], 1).astype(WIDE), part_c1.astype(WIDE) + far_c1.astype(WIDE)
    )
    return (
        layer_outputs.T[None],
        input_grads.T[None],
        small_grads[0:1],
        small_grads[1:2],
        jnp.swapaxes(attend_part, 0, 1)[None],
        small_grads[8:10][None],
        output_part.T[None],
        small_grads[2:3],
        small_grads[3:4],
        small_grads[4:5],
        expand_part[None],
        small_grads[10 : 10 + expand_bias.shape[1] // width].reshape(1, -1),
        contract_part.T[None],
        small_grads[5:6],
    )


def solution(mesh):
    return jax.shard_map(
        on_device,
        mesh=mesh,
        in_specs=(
            P("row", "col"),
            P("row", "col"),
            P("section", "col"),
            P("section", "col"),
            P("section", "row", None, "col"),
            P("section", None, "col"),
            P("section", "col", "row"),
            P("section", "col"),
            P("section", "col"),
            P("section", "col"),
            P("section", "row", "col"),
            P("section", "col"),
            P("section", "col", "row"),
            P("section", "col"),
        ),
        out_specs=(
            P("section", "row", "col"),
            P("section", "row", "col"),
            P("section", "col"),
            P("section", "col"),
            P("section", "row", None, "col"),
            P("section", None, "col"),
            P("section", "col", "row"),
            P("section", "col"),
            P("section", "col"),
            P("section", "col"),
            P("section", "row", "col"),
            P("section", "col"),
            P("section", "col", "row"),
            P("section", "col"),
        ),
        check_vma=False,
    )
```

```python
import functools

import jax
import jax.numpy as jnp
from jax import lax
from jax.experimental import pallas as pl
from jax.experimental.pallas import tpu as pltpu
from jax.sharding import PartitionSpec as P

HEAD = 64
LENGTH = 1024
EPS = 1e-05
LOW = jnp.bfloat16
WIDE = jnp.float32
MESH = pl.DeviceIdType.MESH
PARTS = 2
TILE = 256
MEBI = 1024 * 1024
GRANT = 58 * MEBI


def nn(left, right):
    return lax.dot_general(left, right, (((1,), (0,)), ((), ())), preferred_element_type=WIDE)


def nt(left, right):
    return lax.dot_general(left, right, (((1,), (1,)), ((), ())), preferred_element_type=WIDE)


def tn(left, right):
    return lax.dot_general(left, right, (((0,), (0,)), ((), ())), preferred_element_type=WIDE)


def turned(values):
    width = values.shape[1]
    unit = (
        lax.broadcasted_iota(jnp.int32, (width, width), 0) == lax.broadcasted_iota(jnp.int32, (width, width), 1)
    ).astype(LOW)
    return nt(unit, values)


def normalise(values):
    center = jnp.mean(values, axis=1, keepdims=True)
    centred = values - center
    scale = lax.rsqrt(jnp.mean(centred * centred, axis=1, keepdims=True) + EPS)
    return centred * scale, scale


def norm_backward(grad, hat, scale, gain):
    scaled = grad * gain
    mean_one = jnp.mean(scaled, axis=1, keepdims=True)
    mean_two = jnp.mean(scaled * hat, axis=1, keepdims=True)
    return scale * (scaled - mean_one - hat * mean_two)


class Group:
    def __init__(self, rows):
        self.me = lax.axis_index("col")
        chip, core = self.me // 2, self.me % 2
        self.sib = chip * 2 + 1 - core
        self.peer = (1 - chip) * 2 + core
        self.diag = (1 - chip) * 2 + 1 - core
        self.rows = rows
        self.part = rows // PARTS
        self.loads, self.stores, self.begun = {}, {}, set()

    def need(self, *places):
        for place in places:
            self.loads[place].wait()

    def emit(self, *places):
        for place in places:
            self.stores[place].start()
            self.begun.add(place)

    def greet(self, swaps, diagonal, rows=()):
        barrier = pltpu.get_barrier_semaphore()
        others = [{"col": self.sib}, {"col": self.peer}]
        if diagonal:
            others.append({"col": self.diag})
        if swaps:
            others.append({"section": 1 - lax.axis_index("section")})
        others += [{"row": row} for row in rows]
        for other in others:
            pl.semaphore_signal(barrier, inc=1, device_id=other, device_id_type=MESH)
        pl.semaphore_wait(barrier, len(others))

    def slab(self, owner, j):
        return pl.ds(pl.multiple_of(owner * self.rows + j * self.part, self.part), self.part)

    def chunk(self, owner):
        return pl.ds(pl.multiple_of(owner * self.rows, self.rows), self.rows)


def push(src, dst, sems, slot, target, axis="col"):
    return pltpu.make_async_remote_copy(
        src_ref=src,
        dst_ref=dst,
        send_sem=sems.at[0, slot],
        recv_sem=sems.at[1, slot],
        device_id={axis: target},
        device_id_type=MESH,
    )


class Gather:
    def __init__(self, group, full, sems, blocks=False):
        self.group, self.full, self.sems, self.blocks = group, full, sems, blocks

    def piece(self, owner, j):
        if not self.blocks:
            return self.full.at[self.group.slab(owner, j)]
        part = self.full.shape[1] // PARTS
        return self.full.at[owner, pl.ds(j * part, part)]

    def start(self):
        g = self.group
        self.over, self.near, self.relayed = [], [], []
        for j in range(PARTS):
            piece = self.piece(g.me, j)
            self.over.append(push(piece, piece, self.sems, j, g.peer))
            self.over[-1].start()
        for j in range(PARTS):
            piece = self.piece(g.me, j)
            self.near.append(push(piece, piece, self.sems, PARTS + j, g.sib))
            self.near[-1].start()

    def sibling(self):
        for copy in self.near:
            copy.wait_recv()

    def relay(self):
        g = self.group
        for j in range(PARTS):
            self.over[j].wait_recv()
            piece = self.piece(g.peer, j)
            self.relayed.append(push(piece, piece, self.sems, 2 * PARTS + j, g.sib))
            self.relayed[-1].start()

    def diagonal(self):
        for copy in self.relayed:
            copy.wait_recv()

    def done(self):
        for copy in self.over + self.near + self.relayed:
            copy.wait_send()

    def each(self, body, first=None):
        g = self.group
        self.start()
        if first is not None:
            first()
        body(g.me)
        self.sibling()
        body(g.sib)
        self.relay()
        body(g.peer)
        self.diagonal()
        body(g.diag)
        self.done()


class Scatter:
    def __init__(self, group, stage, land, total, sems):
        self.group, self.stage, self.land, self.total, self.sems = group, stage, land, total, sems

    def start(self, part):
        g, stage, land = self.group, self.stage, self.land
        self.first, self.over, self.near = [], [], []
        def split(owner):
            whole = part(owner)
            return [whole[j * g.part : (j + 1) * g.part] for j in range(PARTS)]

        for j, mine in enumerate(split(g.diag)):
            stage[0, j] = mine.astype(LOW)
            self.first.append(push(stage.at[0, j], land.at[0, j], self.sems, j, g.sib))
            self.first[-1].start()
        for j, mine in enumerate(split(g.peer)):
            self.first[j].wait_recv()
            stage[1, j] = (mine + land[0, j].astype(WIDE)).astype(LOW)
            self.over.append(push(stage.at[1, j], land.at[1, j], self.sems, PARTS + j, g.peer))
            self.over[-1].start()
        for j, mine in enumerate(split(g.sib)):
            stage[2, j] = mine.astype(LOW)
            self.near.append(push(stage.at[2, j], land.at[2, j], self.sems, 2 * PARTS + j, g.sib))
            self.near[-1].start()
        for j, mine in enumerate(split(g.me)):
            self.total[j] = mine

    def take(self, j):
        self.near[j].wait_recv()
        self.over[j].wait_recv()
        land = self.land
        return self.total[j] + (land[1, j].astype(WIDE) + land[2, j].astype(WIDE))

    def done(self):
        for copy in self.first + self.over + self.near:
            copy.wait_send()


class Deliver:
    def __init__(self, group, stage, out, sems):
        self.group, self.stage, self.out, self.sems = group, stage, out, sems

    def start(self, rows_ref):
        g, width = self.group, self.out.shape[1]
        for c in range(self.stage.shape[0]):
            self.stage[c] = rows_ref[:, c * width : (c + 1) * width]
        place = self.out.at[g.chunk(g.me)]
        self.copies = [
            push(self.stage.at[other], place, self.sems, n, other)
            for n, other in enumerate((g.peer, g.diag, g.sib))
        ]
        for copy in self.copies:
            copy.start()
        self.out[g.chunk(g.me), :] = self.stage[g.me]

    def done(self):
        for copy in self.copies:
            copy.wait()


class OneWay:
    def __init__(self, up, down, sems):
        self.section = lax.axis_index("section")
        both = [*up, *down]
        copies = [
            push(source, into, sems, n, 1 - self.section, "section")
            for n, (source, into) in enumerate(both)
        ]
        self.up, self.down = copies[: len(up)], copies[len(up) :]

    def each(self, first, second):
        @pl.when(self.section == 0)
        def _():
            first(self.up)
            second(self.down)

        @pl.when(self.section == 1)
        def _():
            first(self.down)
            second(self.up)

    def start(self):
        self.each(lambda copies: [copy.start() for copy in copies], lambda copies: None)

    def wait(self):
        self.each(
            lambda copies: [copy.wait_send() for copy in copies],
            lambda copies: [copy.wait_recv() for copy in copies],
        )


def scatter_scratch(rows, width):
    part = rows // PARTS
    return [
        pltpu.VMEM((3, PARTS, part, width), LOW),
        pltpu.VMEM((3, PARTS, part, width), LOW),
        pltpu.VMEM((PARTS, part, width), WIDE),
        pltpu.SemaphoreType.DMA((2, 3 * PARTS)),
    ]


class Halves:
    def __init__(self, pair, whole, sems, slot):
        if pair[0].shape[1] == whole.shape[1]:
            self.copies = [pltpu.make_async_copy(pair[0], whole, sems.at[slot])]
            return
        section = lax.axis_index("section")
        half = whole.shape[1] // 2
        self.copies = []
        for n, place in enumerate((section, 1 - section)):
            columns = pl.ds(pl.multiple_of(place * half, half), half)
            self.copies.append(
                pltpu.make_async_copy(pair[n], whole.at[:, columns], sems.at[slot + n])
            )

    def start(self):
        for copy in self.copies:
            copy.start()

    def wait(self):
        for copy in self.copies:
            copy.wait()


class Trade:
    def __init__(self, keep, send, got, sems):
        self.keep, self.send, self.got, self.sems = keep, send, got, sems
        self.tiles = keep.shape[0] // TILE

    def copy(self, n):
        rows = pl.ds(pl.multiple_of(n * TILE, TILE), TILE)
        return push(
            self.send.at[rows], self.got.at[rows], self.sems, n, 1 - lax.axis_index("section"), "section"
        )

    def start(self, make):
        @pl.loop(0, self.tiles)
        def _(n):
            make(pl.ds(pl.multiple_of(n * TILE, TILE), TILE))
            self.copy(n).start()

    def finish(self):
        @pl.loop(0, self.tiles)
        def _(n):
            self.copy(n).wait()

        add_into(self.keep, self.got)


def add_into(keep_ref, got_ref):
    @pl.loop(0, keep_ref.shape[0] // TILE)
    def _(n):
        rows = pl.ds(pl.multiple_of(n * TILE, TILE), TILE)
        keep_ref[rows, :] = (keep_ref[rows, :].astype(WIDE) + got_ref[rows, :].astype(WIDE)).astype(LOW)


def causal_scores(scores):
    size = scores.shape[1]
    keep = lax.broadcasted_iota(jnp.int32, (size, size), 0) <= lax.broadcasted_iota(
        jnp.int32, (size, size), 1
    )
    begin = scores.shape[0] - size
    last = jnp.where(keep, scores[begin:], -1000000000.0)
    return last if begin == 0 else jnp.concatenate([scores[:begin], last], 0)


def attention_out(owner, size, heads_ref, o3, lse_ref, heads):
    for i in range(heads_ref.shape[1] // size):
        rows, finish = slice(i * size, (i + 1) * size), (i + 1) * size

        @pl.when(owner == i)
        def _():
            @pl.loop(0, heads)
            def _(h):
                scores = causal_scores(nt(heads_ref[heads + h, :finish, :], heads_ref[h, rows, :]))
                highest = jnp.max(scores, axis=0, keepdims=True)
                powers = jnp.exp(scores - highest)
                summed = jnp.sum(powers, axis=0, keepdims=True)
                mixed = tn(heads_ref[2 * heads + h, :finish, :], powers.astype(LOW))
                o3[h, rows, :] = (mixed / summed).T.astype(LOW)
                lse_ref[pl.ds(h, 1), rows] = highest + jnp.log(summed)


def attention_back(owner, size, heads_ref, go3, lse_ref, dots_ref, g3, key_acc, value_acc, heads):
    for i in range(heads_ref.shape[1] // size):
        rows, finish = slice(i * size, (i + 1) * size), (i + 1) * size

        @pl.when(owner == i)
        def _():
            @pl.loop(0, heads)
            def _(h):
                queries = heads_ref[h, rows, :]
                keys = heads_ref[heads + h, :finish, :]
                grads = go3[h, rows, :]
                probs = jnp.exp(causal_scores(nt(keys, queries) - lse_ref[pl.ds(h, 1), rows]))
                grad_probs = nt(heads_ref[2 * heads + h, :finish, :], grads)
                grad_scores = (probs * (grad_probs - dots_ref[pl.ds(h, 1), rows])).astype(LOW)
                g3[h, rows, :] = (tn(grad_scores, keys) * HEAD ** (-0.5)).astype(LOW)
                key_acc[h, :finish, :] += nn(grad_scores, queries)
                value_acc[h, :finish, :] += nn(probs.astype(LOW), grads)


def start_kernel(
    tokens_ref, cotangent_ref, small_ref, expand_ref, contract_ref,
    x_ref, g_ref, vectors_ref, got_expand_ref, got_contract_ref,
    x4, g4, s4, other4, x_sems, g_sems, s_sems, local_sems,
):
    section = lax.axis_index("section")
    group = Group(x_ref.shape[0] // 4)
    length = x_ref.shape[0]
    loads = []
    rows = pl.ds(pl.multiple_of(section * length, length), length)
    for n, (source, into) in enumerate(((tokens_ref.at[rows], x4), (cotangent_ref.at[rows], g4), (small_ref, s4))):
        loads.append(pltpu.make_async_copy(source, into.at[group.me], local_sems.at[n]))
        loads[-1].start()
    group.greet(True, False)
    blocks = [
        push(source, into, s_sems, 3 * PARTS + 1 + n, 1 - section, "section")
        for n, (source, into) in enumerate(((expand_ref, got_expand_ref), (contract_ref, got_contract_ref)))
    ]
    for block in blocks:
        block.start()
    gathers = [Gather(group, x4, x_sems, True), Gather(group, s4, s_sems, True), Gather(group, g4, g_sems, True)]
    for gather, load in zip(gathers, (loads[0], loads[2], loads[1])):
        load.wait()
        gather.start()
    for gather in gathers:
        gather.sibling()
        gather.relay()
        gather.diagonal()
    swap = push(s4, other4, s_sems, 3 * PARTS, 1 - section, "section")
    swap.start()
    width = x4.shape[2]
    for c in range(x4.shape[0]):
        x_ref[:, c * width : (c + 1) * width] = x4[c]
        g_ref[:, c * width : (c + 1) * width] = g4[c]
    swap.wait()
    for block in blocks:
        block.wait()
    vectors_ref[section] = s4[...]
    vectors_ref[1 - section] = other4[...]
    for gather in gathers:
        gather.done()


def attend_kernel(
    heads, group, x_ref, mine_ref, other_ref, vec_ref, bias_ref,
    normed_ref, heads_ref, o_ref, lse_ref, hidden_ref, second_ref,
    weight, o3, stage, land, total, scatter_sems, local_sems,
):
    width = o_ref.shape[1]
    halves = Halves((mine_ref, other_ref), weight, local_sems, 0)
    halves.start()
    lse_ref[...] = jnp.zeros_like(lse_ref)
    halves.wait()

    @pl.loop(0, LENGTH // group.rows)
    def _(owner):
        rows = group.chunk(owner)
        hat, _ = normalise(x_ref[rows, :].astype(WIDE))
        normed = (hat * vec_ref[0:1, :] + vec_ref[1:2, :]).astype(LOW)
        normed_ref[rows, :] = normed
        mixed = nn(normed, weight[:, : 3 * width]) + bias_ref[...]
        for j in range(3 * heads):
            piece = mixed[:, j * HEAD : (j + 1) * HEAD]
            if j < heads:
                piece = piece * HEAD ** (-0.5)
            heads_ref[j, rows, :] = piece.astype(LOW)

    group.emit(0, 1)

    def attend(owner):
        rows = group.chunk(owner)
        attention_out(owner, group.rows, heads_ref, o3, lse_ref, heads)
        for h in range(heads):
            o_ref[rows, h * HEAD : (h + 1) * HEAD] = o3[h, rows, :]
        return nt(o_ref[rows, :], weight[:, 3 * width :])

    scatter = Scatter(group, stage, land, total, scatter_sems)
    scatter.start(attend)
    group.emit(2, 3)
    for j in range(PARTS):
        rows = slice(j * group.part, (j + 1) * group.part)
        residual = x_ref[group.slab(group.me, j), :].astype(WIDE)
        hidden = residual + scatter.take(j) + vec_ref[2:3, :]
        hidden_ref[rows, :] = hidden
        hat, _ = normalise(hidden)
        second_ref[rows, :] = (hat * vec_ref[3:4, :] + vec_ref[4:5, :]).astype(LOW)
    scatter.done()


def outer_whole(left_ref, right_ref, out_ref):
    @pl.loop(0, left_ref.shape[1] // TILE)
    def _(n):
        rows = pl.ds(pl.multiple_of(n * TILE, TILE), TILE)
        out_ref[rows, :] = tn(left_ref[:, rows], right_ref[...]).astype(LOW)


def widen_kernel(last, group, second_ref, em_ref, eo_ref, bias_ref, *refs):
    if last:
        g_ref, *refs = refs
    full_ref, active_ref, slope_ref, *refs = refs
    if last:
        c_ref, *refs = refs
    expand, gather_sems, local_sems = refs
    halves = Halves((em_ref, eo_ref), expand, local_sems, 0)
    halves.start()
    full_ref[group.chunk(group.me), :] = second_ref[...]
    halves.wait()

    def widen(owner):
        rows = group.chunk(owner)
        t = nn(full_ref[rows, :], expand[...]) + bias_ref[...]
        square = t * t
        bent = jnp.tanh(0.7978845608028654 * t * (1.0 + 0.044715 * square))
        active_ref[rows, :] = (0.5 * t * (1.0 + bent)).astype(LOW)
        slope_ref[rows, :] = (
            0.5 * (1.0 + bent)
            + (0.5 * 0.7978845608028654) * t * (1.0 - bent * bent) * (1.0 + 3 * 0.044715 * square)
        ).astype(LOW)

    Gather(group, full_ref, gather_sems).each(widen)
    if last:
        group.emit(0, 1, 2)
        group.need(4)
        outer_whole(g_ref, active_ref, c_ref)


def outer_halves(left_ref, right_ref, keep_ref, send_ref):
    section = lax.axis_index("section")
    half = right_ref.shape[1] // 2
    for place, out in ((section, keep_ref), (1 - section, send_ref)):
        columns = pl.ds(pl.multiple_of(place * half, half), half)

        @pl.loop(0, left_ref.shape[1] // TILE)
        def _(n):
            rows = pl.ds(pl.multiple_of(n * TILE, TILE), TILE)
            out[rows, :] = tn(left_ref[:, rows], right_ref[:, columns]).astype(LOW)


def contract_kernel(
    group, active_ref, hidden_ref, cm_ref, co_ref, vec_ref, result_ref, full_ref,
    contract, stage, land, total, scatter_sems, gather_sems, local_sems,
):
    halves = Halves((cm_ref, co_ref), contract, local_sems, 0)
    halves.start()
    halves.wait()
    scatter = Scatter(group, stage, land, total, scatter_sems)
    scatter.start(lambda owner: nt(active_ref[group.chunk(owner), :], contract[...]))
    group.need(1)
    for j in range(PARTS):
        rows = slice(j * group.part, (j + 1) * group.part)
        result = (hidden_ref[rows, :] + scatter.take(j) + vec_ref[5:6, :]).astype(LOW)
        result_ref[rows, :] = result
        full_ref[group.slab(group.me, j), :] = result
    Gather(group, full_ref, gather_sems).each(lambda owner: None)
    scatter.done()


def narrow_grads(group, scatter, full_ref, hidden_ref, vec_ref, grad_ref, low_ref, sums_ref):
    for j in range(PARTS):
        rows = slice(j * group.part, (j + 1) * group.part)
        grad = scatter.take(j)
        hat, scale = normalise(hidden_ref[rows, :])
        own = full_ref[group.slab(group.me, j), :].astype(WIDE)
        out = own + norm_backward(grad, hat, scale, vec_ref[3:4, :])
        grad_ref[rows, :] = out
        low_ref[rows, :] = out.astype(LOW)
        for n, term in enumerate((grad * hat, grad, own, out)):
            sums_ref[n : n + 1, :] += jnp.sum(term, axis=0, keepdims=True)


def bend(rows, full_ref, contract, slope_ref, before, sums_ref):
    grad = (nn(full_ref[rows, :], contract[...]) * slope_ref[rows, :].astype(WIDE)).astype(LOW)
    before[rows, :] = grad
    sums_ref[4:5, :] += jnp.sum(grad.astype(WIDE), axis=0, keepdims=True)


def late_expand_kernel(
    group, active_ref, hidden_ref, cm_ref, co_ref, em_ref, eo_ref, g_ref, slope_ref, second_ref, vec_ref,
    grad_ref, low_ref, sums_ref, e_ref, result,
    contract, expand, before,
    stage_a, land_a, total_a, sems_a, stage, land, total, scatter_sems, local_sems,
):
    first = Halves((cm_ref, co_ref), contract, local_sems, 0)
    then = Halves((em_ref, eo_ref), expand, local_sems, 2)
    first.start()
    then.start()
    sums_ref[...] = jnp.zeros_like(sums_ref)
    first.wait()
    forward = Scatter(group, stage_a, land_a, total_a, sems_a)
    forward.start(lambda owner: nt(active_ref[group.chunk(owner), :], contract[...]))
    group.need(6, 7)

    @pl.loop(0, LENGTH // group.rows)
    def _(n):
        bend(group.chunk(n), g_ref, contract, slope_ref, before, sums_ref)

    then.wait()
    scatter = Scatter(group, stage, land, total, scatter_sems)
    scatter.start(lambda owner: nt(before[group.chunk(owner), :], expand[...]))
    group.need(1)
    for j in range(PARTS):
        rows = slice(j * group.part, (j + 1) * group.part)
        result[rows, :] = (hidden_ref[rows, :] + forward.take(j) + vec_ref[5:6, :]).astype(LOW)
    group.emit(4)
    group.need(8)
    outer_whole(second_ref, before, e_ref)
    group.emit(3)
    narrow_grads(group, scatter, g_ref, hidden_ref, vec_ref, grad_ref, low_ref, sums_ref)
    group.emit(0, 1, 2)
    forward.done()
    scatter.done()


def expand_back_kernel(
    group, g_ref, cm_ref, co_ref, em_ref, eo_ref, slope_ref, active_ref, second_ref, hidden_ref, vec_ref,
    grad_ref, low_ref, sums_ref, ek_ref, es_ref, full_ref, c_ref,
    contract, expand, before, stage, land, total, scatter_sems, gather_sems, local_sems, outer, got, trade_sems,
):
    section = lax.axis_index("section")
    first = Halves((cm_ref, co_ref), contract, local_sems, 0)
    then = Halves((em_ref, eo_ref), expand, local_sems, 2)
    first.start()
    then.start()
    sums_ref[...] = jnp.zeros_like(sums_ref)
    full_ref[group.chunk(group.me), :] = g_ref[...]
    first.wait()
    Gather(group, full_ref, gather_sems).each(
        lambda owner: bend(group.chunk(owner), full_ref, contract, slope_ref, before, sums_ref),
        lambda: group.need(5),
    )
    group.emit(5)
    group.need(6)
    half = active_ref.shape[1] // 2

    def columns(place):
        return pl.ds(pl.multiple_of(place * half, half), half)

    def make(n):
        def tile(rows):
            place = section if n == 0 else 1 - section
            outer[n, rows, :] = tn(full_ref[:, rows], active_ref[:, columns(place)]).astype(LOW)

        return tile

    trade = Trade(outer.at[0], outer.at[1], got, trade_sems)
    trade.start(make(1))
    then.wait()
    scatter = Scatter(group, stage, land, total, scatter_sems)
    scatter.start(lambda owner: nt(before[group.chunk(owner), :], expand[...]))
    group.need(7)
    outer_halves(second_ref, before, ek_ref, es_ref)
    group.emit(3, 4)
    keep = make(0)

    @pl.loop(0, outer.shape[1] // TILE)
    def _(n):
        keep(pl.ds(pl.multiple_of(n * TILE, TILE), TILE))

    group.need(8)
    narrow_grads(group, scatter, full_ref, hidden_ref, vec_ref, grad_ref, low_ref, sums_ref)
    group.emit(0, 1, 2)
    scatter.done()
    trade.finish()
    store = pltpu.make_async_copy(outer.at[0], c_ref, local_sems.at[0])
    store.start()
    store.wait()


def scores_back(group, heads, low_ref, weight, heads_ref, o_ref, lse_ref, full, go3, dots, g3, accs, mixed, gather_sems, first):
    width = o_ref.shape[1]
    picks = (
        lax.broadcasted_iota(jnp.int32, (8, width), 1) // HEAD
        == lax.broadcasted_iota(jnp.int32, (8, width), 0)
    ).astype(WIDE)
    for acc in accs:
        acc[...] = jnp.zeros_like(acc)

    def spread(owner):
        rows = group.chunk(owner)
        grads = nn(full[rows, :], weight[:, 3 * width :]).astype(LOW)
        for h in range(heads):
            go3[h, rows, :] = grads[:, h * HEAD : (h + 1) * HEAD]
        term = grads.astype(WIDE) * o_ref[rows, :].astype(WIDE)
        dots[:, rows] = lax.dot_general(
            picks,
            term,
            (((1,), (1,)), ((), ())),
            precision=lax.Precision.HIGHEST,
            preferred_element_type=WIDE,
        )
        attention_back(owner, group.rows, heads_ref, go3, lse_ref, dots, g3, *accs, heads)

    full[group.chunk(group.me), :] = low_ref[...]
    Gather(group, full, gather_sems).each(spread, first)
    for j in range(3 * heads):
        source = g3[j] if j < heads else accs[j // heads - 1][j % heads].astype(LOW)
        mixed[:, j * HEAD : (j + 1) * HEAD] = source


def outer_out(full, o_ref, outer_ref):
    @pl.loop(0, outer_ref.shape[0] // TILE)
    def _(n):
        rows = pl.ds(pl.multiple_of(n * TILE, TILE), TILE)
        outer_ref[rows, :] = tn(full[:, rows], o_ref[...]).astype(LOW)


def attend_grads(group, scatter, x_ref, grad_ref, vec_ref, mixed, width, out_ref, sums_ref):
    sums_ref[2:3, : 3 * width] = jnp.sum(mixed[...].astype(WIDE), axis=0, keepdims=True)
    for j in range(PARTS):
        rows = slice(j * group.part, (j + 1) * group.part)
        grad = scatter.take(j)
        hat, scale = normalise(x_ref[rows, :].astype(WIDE))
        out = grad_ref[rows, :] + norm_backward(grad, hat, scale, vec_ref[0:1, :])
        out_ref[rows, :] = out.astype(LOW)
        for n, term in enumerate((grad * hat, grad)):
            sums_ref[n : n + 1, :] += jnp.sum(term, axis=0, keepdims=True)


def late_attend_kernel(
    heads, group, low_ref, grad_ref, x_ref, mine_ref, other_ref, normed_ref, heads_ref, o_ref, lse_ref, vec_ref,
    result_ref, y_ref,
    out_ref, sums_ref, results_ref, w_ref,
    weight, full, go3, dots, g3, key_acc, value_acc, mixed, outer, outer_o, late, y_land, stage4,
    stage, land, total, scatter_sems, gather_sems, deliver_sems, y_sems, local_sems,
):
    width = o_ref.shape[1]
    section = lax.axis_index("section")
    halves = Halves((mine_ref, other_ref), weight, local_sems, 0)
    halves.start()
    sums_ref[...] = jnp.zeros_like(sums_ref)
    halves.wait()
    deliver = Deliver(group, stage4, late, deliver_sems)

    def first():
        group.need(6, 7, 8, 10)
        deliver.start(result_ref)

    scores_back(
        group, heads, low_ref, weight, heads_ref, o_ref, lse_ref, full, go3, dots, g3,
        (key_acc, value_acc), mixed, gather_sems, first,
    )
    deliver.done()
    group.need(11)
    results = OneWay([(late, y_land)], [(y_ref, y_land)], y_sems)
    results.start()
    scatter = Scatter(group, stage, land, total, scatter_sems)
    scatter.start(lambda owner: nt(mixed[group.chunk(owner), :], weight[:, : 3 * width]))
    outer_out(full, o_ref, outer_o)
    group.need(5)

    @pl.loop(0, weight.shape[0] // TILE)
    def _(n):
        rows = pl.ds(pl.multiple_of(n * TILE, TILE), TILE)
        outer[rows, : 3 * width] = tn(normed_ref[:, rows], mixed[...]).astype(LOW)
        outer[rows, 3 * width :] = outer_o[rows, :]

    store = pltpu.make_async_copy(outer, w_ref, local_sems.at[2])
    store.start()
    @pl.when(section == 0)
    def _():
        results_ref[section] = turned(y_ref[...]).astype(LOW)

    @pl.when(section == 1)
    def _():
        results_ref[section] = turned(late[...]).astype(LOW)

    group.need(1, 2)
    attend_grads(group, scatter, x_ref, grad_ref, vec_ref, mixed, width, out_ref, sums_ref)
    results.wait()
    results_ref[1 - section] = turned(y_land[...]).astype(LOW)
    scatter.done()
    store.wait()


def scores_back_kernel(
    heads, group, low_ref, mine_ref, other_ref, heads_ref, o_ref, lse_ref, ek_ref, es_ref,
    mixed, outer_ref, e_ref,
    weight, full, go3, dots, g3, key_acc, value_acc, got, gather_sems, local_sems, swap_sems,
):
    swap = push(es_ref, got, swap_sems, 0, 1 - lax.axis_index("section"), "section")
    swap.start()
    halves = Halves((mine_ref, other_ref), weight, local_sems, 0)
    halves.start()
    halves.wait()
    scores_back(
        group, heads, low_ref, weight, heads_ref, o_ref, lse_ref, full, go3, dots, g3,
        (key_acc, value_acc), mixed, gather_sems, lambda: group.need(3, 4, 5),
    )
    group.emit(0)
    outer_out(full, o_ref, outer_ref)
    group.emit(1)
    group.need(6)
    swap.wait()
    add_into(ek_ref, got)
    store = pltpu.make_async_copy(ek_ref, e_ref, local_sems.at[0])
    store.start()
    store.wait()


def attend_back_kernel(
    group, mixed, outer_ref, grad_ref, x_ref, mine_ref, other_ref, normed_ref, vec_ref,
    w_ref, out_ref, sums_ref,
    weight, outer, got, stage, land, total, scatter_sems, local_sems, swap_sems,
):
    width = outer_ref.shape[1]
    section = lax.axis_index("section")
    halves = Halves((mine_ref, other_ref), weight, local_sems, 0)
    halves.start()
    sums_ref[...] = jnp.zeros_like(sums_ref)
    half = weight.shape[1] // 2
    scatter = Scatter(group, stage, land, total, scatter_sems)
    group.need(1, 6)

    def make(n):
        place = section if n == 0 else 1 - section

        def tile(rows):
            @pl.when(place == 0)
            def _():
                outer[n, rows, :] = tn(normed_ref[:, rows], mixed[:, :half]).astype(LOW)

            @pl.when(place == 1)
            def _():
                outer[n, rows, : 3 * width - half] = tn(normed_ref[:, rows], mixed[:, half:]).astype(LOW)
                outer[n, rows, 3 * width - half :] = outer_ref[rows, :]

        return tile

    trade = Trade(outer.at[0], outer.at[1], got, swap_sems)
    trade.start(make(1))
    halves.wait()
    scatter.start(lambda owner: nt(mixed[group.chunk(owner), :], weight[:, : 3 * width]))
    keep = make(0)

    @pl.loop(0, outer.shape[1] // TILE)
    def _(n):
        keep(pl.ds(pl.multiple_of(n * TILE, TILE), TILE))

    group.need(2, 3)
    attend_grads(group, scatter, x_ref, grad_ref, vec_ref, mixed, width, out_ref, sums_ref)
    group.emit(1, 2)
    scatter.done()
    trade.finish()
    store = pltpu.make_async_copy(outer.at[0], w_ref, local_sems.at[2])
    store.start()
    store.wait()


def finish_kernel(
    late_ref, early1_ref, early2_ref, near_ref, far_ref, a0, n0, a1, n1,
    grads_ref, sums_ref, got_late, got_early1, got_early2,
    mine, stage4, block, land_col, land_x, land_z, land,
    deliver_sems, col_sems, x_sems, z_sems, part_sems,
):
    section, row = lax.axis_index("section"), lax.axis_index("row")
    away = 1 - section
    group = Group(near_ref.shape[0])
    length, width = far_ref.shape
    others = [lax.rem(row + d, land_z.shape[0]) for d in range(1, land_z.shape[0])]
    group.greet(True, True, others)
    gradient_up = OneWay([(far_ref, land)], [], x_sems.at[:, pl.ds(1, 1)])
    gradient_down = OneWay([], [(mine, land)], x_sems.at[:, pl.ds(2, 1)])
    parts = OneWay(
        [(late_ref, got_late)], [(early1_ref, got_early1), (early2_ref, got_early2)], part_sems
    )
    deliver = Deliver(group, stage4, mine, deliver_sems)
    deliver.start(near_ref)
    gradient_up.start()
    parts.start()

    block[...] = jnp.zeros_like(block)
    for layer, (attn, narrow) in enumerate(((a0, n0), (a1, n1))):
        wide = [attn[0:1, :], attn[1:2, :], narrow[3:4, :], narrow[0:1, :], narrow[1:2, :], narrow[2:3, :]]
        for c in range(block.shape[0]):
            columns = slice(c * width, (c + 1) * width)
            for n, term in enumerate(wide):
                block[c, layer, n : n + 1, :] = term[:, columns]
            for n, term in enumerate((attn[2:3, :width], attn[2:3, 2 * width : 3 * width])):
                block[c, layer, 8 + n : 9 + n, :] = term
            for n in range(narrow.shape[1] // width):
                block[c, layer, 10 + n : 11 + n, :] = narrow[4:5, n * width : (n + 1) * width]
    copies = [
        push(block.at[other, :, pl.ds(0, 8)], land_col.at[n], col_sems, n, other)
        for n, other in enumerate((group.peer, group.diag, group.sib))
    ]
    for copy in copies:
        copy.start()
    for copy in copies:
        copy.wait()
    me = group.me
    block[me, :, :8] = block[me, :, :8] + (land_col[0] + (land_col[1] + land_col[2]))
    swap = push(block.at[me, away], land_x, x_sems, 0, away, "section")
    swap.start()
    deliver.done()
    gradient_down.start()

    @pl.when(section == 0)
    def _():
        grads_ref[section] = turned(mine[...]).astype(LOW)

    @pl.when(section == 1)
    def _():
        grads_ref[section] = turned(far_ref[...]).astype(LOW)

    swap.wait()
    land_z[row] = block[me, section] + land_x[...]
    copies = [
        push(land_z.at[row], land_z.at[row], z_sems, n, other, "row")
        for n, other in enumerate(others)
    ]
    for copy in copies:
        copy.start()
    for copy in copies:
        copy.wait()
    result = land_z[0]
    for n in range(1, land_z.shape[0]):
        result = result + land_z[n]
    sums_ref[...] = result
    gradient_up.wait()
    gradient_down.wait()
    grads_ref[away] = turned(land[...]).astype(LOW)
    parts.wait()


def greet_section():
    barrier = pltpu.get_barrier_semaphore()
    other = 1 - lax.axis_index("section")
    pl.semaphore_signal(barrier, inc=1, device_id={"section": other}, device_id_type=MESH)
    pl.semaphore_wait(barrier, 1)


def cross_kernel(up, part_ref, got_ref, sems):
    greet_section()
    pair = [(part_ref, got_ref)]
    part = OneWay(pair, [], sems) if up else OneWay([], pair, sems)
    part.start()
    part.wait()


def write_kernel(*refs):
    (late, far_late, early, far_early), (attend_ref, output_ref, expand_ref, contract_ref) = (
        [refs[n : n + 3] for n in (0, 3, 6, 9)],
        refs[12:16],
    )
    own, far, sems = refs[16:]
    half = early[0].shape[1]
    width = output_ref.shape[1]
    section = lax.axis_index("section")

    def load(firsts, seconds):
        copies = [
            pltpu.make_async_copy(source, into, sems.at[n])
            for n, (source, into) in enumerate((*firsts, *seconds))
        ]
        for copy in copies:
            copy.start()
        for copy in copies:
            copy.wait()

    @pl.when(section == 0)
    def _():
        load(
            [(early[n], own.at[n, :, pl.ds(0, half)]) for n in range(3)],
            [(far_early[n], own.at[n, :, pl.ds(half, half)]) for n in range(3)],
        )
        far[...] = jnp.zeros_like(far)

    @pl.when(section == 1)
    def _():
        load([(late[n], own.at[n]) for n in range(3)], [(far_late[n], far.at[n]) for n in range(3)])

    first = own[0].astype(WIDE) + far[0].astype(WIDE)
    for j in range(3):
        attend_ref[j] = first[:, j * width : (j + 1) * width]
    output_ref[...] = first[:, 3 * width :]
    expand_ref[...] = own[1].astype(WIDE) + far[1].astype(WIDE)
    contract_ref[...] = own[2].astype(WIDE) + far[2].astype(WIDE)


VM = pl.BlockSpec(memory_space=pltpu.VMEM)
ANY = pl.BlockSpec(memory_space=pl.ANY)
PAIRS = pltpu.SemaphoreType.DMA((2, 3 * PARTS))
LOCAL = pltpu.SemaphoreType.DMA((4,))


def shape(dims, kind=LOW):
    return jax.ShapeDtypeStruct(dims, kind)


def launch(
    body, number, rows, in_specs, ins, outs, out_specs, scratch, swaps=(), diagonal=False, across=False, late=(),
):
    n_in, n_out, n = len(ins), len(outs), len(swaps)
    held_in = [i for i in range(n_in) if in_specs[i] is VM]
    held_out = [i for i in range(n_out) if out_specs[i] is VM]

    def kernel(*refs):
        refs = list(refs)
        takes, sources = refs[:n_in], refs[n_in : n_in + n]
        gives = refs[n_in + n : n_in + n + n_out]
        lands = refs[n_in + n + n_out : n_in + 2 * n + n_out]
        rest = refs[n_in + 2 * n + n_out :]
        own, rest = rest[: len(scratch)], rest[len(scratch) :]
        in_held, rest = rest[: len(held_in)], rest[len(held_in) :]
        out_held, rest = rest[: len(held_out)], rest[len(held_out) :]
        in_sems, out_sems, swap_sems = rest
        group = Group(rows)
        for k, i in enumerate(held_in):
            group.loads[i] = pltpu.make_async_copy(takes[i], in_held[k], in_sems.at[k])
            group.loads[i].start()
            takes[i] = in_held[k]
        for k, i in enumerate(held_out):
            group.stores[i] = pltpu.make_async_copy(out_held[k], gives[i], out_sems.at[k])
            gives[i] = out_held[k]
        group.greet(n or across, diagonal)
        other = 1 - lax.axis_index("section")
        copies = [
            push(source, land, swap_sems, i, other, "section")
            for i, (source, land) in enumerate(zip(sources, lands))
        ]
        for copy in copies:
            copy.start()
        group.need(*[i for i in held_in if i not in late])
        body(group, *takes, *gives, *own)
        group.emit(*[i for i in held_out if i not in group.begun])
        for copy in copies:
            copy.wait()
        for i in held_out:
            group.stores[i].wait()

    results = pl.pallas_call(
        kernel,
        out_shape=(*outs, *[shape(s.shape, s.dtype) for s in swaps]),
        in_specs=[ANY] * (n_in + n),
        out_specs=(ANY,) * (n_out + n),
        scratch_shapes=[
            *scratch,
            *[pltpu.VMEM(ins[i].shape, ins[i].dtype) for i in held_in],
            *[pltpu.VMEM(outs[i].shape, outs[i].dtype) for i in held_out],
            pltpu.SemaphoreType.DMA((len(held_in),)),
            pltpu.SemaphoreType.DMA((len(held_out),)),
            pltpu.SemaphoreType.DMA((2, max(n, 1))),
        ],
        compiler_params=pltpu.CompilerParams(
            collective_id=number, has_side_effects=True, vmem_limit_bytes=GRANT
        ),
        cost_estimate=pl.CostEstimate(flops=int(3e10), bytes_accessed=30 * MEBI, transcendentals=0),
    )(*ins, *swaps)
    return results[:n_out], results[n_out:]


def start_call(number, tokens, cotangent, small, expand, contract, columns):
    width = tokens.shape[1]
    size = width * columns
    kinds = small.shape[0]
    outs = (shape((LENGTH, size)), shape((LENGTH, size)), shape((2, columns, kinds, width)), shape(expand.shape), shape(contract.shape))
    blocks = pltpu.VMEM((columns, LENGTH, width), LOW)
    vectors = pltpu.VMEM((columns, kinds, width), LOW)
    return pl.pallas_call(
        start_kernel,
        out_shape=outs,
        in_specs=[ANY] * 5,
        out_specs=(VM, VM, VM, ANY, ANY),
        scratch_shapes=[
            blocks, blocks, vectors, vectors, PAIRS, PAIRS,
            pltpu.SemaphoreType.DMA((2, 3 * PARTS + 3)), LOCAL,
        ],
        compiler_params=pltpu.CompilerParams(
            collective_id=number, has_side_effects=True, vmem_limit_bytes=GRANT
        ),
        cost_estimate=pl.CostEstimate(flops=int(3e10), bytes_accessed=30 * MEBI, transcendentals=0),
    )(tokens, cotangent, small, expand, contract)


def attend_call(number, x, pair, vec, bias, rows, width, swaps):
    size = vec.shape[1]
    heads = width // HEAD
    outs = (
        shape((LENGTH, size)),
        shape((3 * heads, LENGTH, HEAD)),
        shape((LENGTH, width)),
        shape((8, LENGTH), WIDE),
        shape((rows, size), WIDE),
        shape((rows, size)),
    )
    scratch = [
        pltpu.VMEM((size, 4 * width), LOW),
        pltpu.VMEM((heads, LENGTH, HEAD), LOW),
        *scatter_scratch(rows, size), LOCAL,
    ]
    return launch(
        functools.partial(attend_kernel, heads),
        number, rows, [VM, ANY, ANY, VM, VM], (x, *pair, vec, bias), outs, (VM,) * 6, scratch, swaps,
    )


def widen_call(number, second, pair, bias, grad, swaps):
    rows, size = second.shape
    wide = bias.shape[1]
    last = grad is not None
    ins, in_specs = [second, *pair, bias], [VM, ANY, ANY, VM]
    outs = [shape((LENGTH, size)), shape((LENGTH, wide)), shape((LENGTH, wide))]
    if last:
        ins, in_specs, outs = ins + [grad], in_specs + [VM], outs + [shape((size, wide))]
    scratch = [pltpu.VMEM((size, wide), LOW), PAIRS, LOCAL]
    return launch(
        functools.partial(widen_kernel, last),
        number, rows, in_specs, ins, outs, (VM,) * len(outs), scratch, swaps, late=(4,),
    )


def contract_call(number, active, hidden, pair, vec, swaps):
    rows, size = hidden.shape
    wide = active.shape[1]
    scratch = [pltpu.VMEM((size, wide), LOW), *scatter_scratch(rows, size), PAIRS, LOCAL]
    return launch(
        contract_kernel, number, rows, [VM, VM, ANY, ANY, VM], (active, hidden, *pair, vec),
        [shape((rows, size)), shape((LENGTH, size))], (VM, VM), scratch, swaps, late=(1,),
    )


def late_expand_call(number, active, hidden, contract, expand, grad, slope, second, vec, swaps):
    rows, size = hidden.shape
    wide = slope.shape[1]
    outs = [
        shape((rows, size), WIDE), shape((rows, size)), shape((8, size), WIDE),
        shape((size, wide)), shape((rows, size)),
    ]
    scratch = [
        pltpu.VMEM((size, wide), LOW),
        pltpu.VMEM((size, wide), LOW),
        pltpu.VMEM((LENGTH, wide), LOW),
        *scatter_scratch(rows, size), *scatter_scratch(rows, size), LOCAL,
    ]
    return launch(
        late_expand_kernel,
        number, rows, [VM, VM, ANY, ANY, ANY, ANY, VM, VM, VM, VM],
        (active, hidden, *contract, *expand, grad, slope, second, vec),
        outs, [VM] * 5, scratch, swaps, late=(1, 6, 7, 8),
    )


def expand_back_call(number, grad, contract, expand, slope, active, second, hidden, vec, swaps):
    rows, size = hidden.shape
    wide = slope.shape[1]
    half = wide // 2
    outs = [
        shape((rows, size), WIDE), shape((rows, size)), shape((8, size), WIDE),
        shape((size, half)), shape((size, half)), shape((LENGTH, size)), shape((size, half)),
    ]
    scratch = [
        pltpu.VMEM((size, wide), LOW),
        pltpu.VMEM((size, wide), LOW),
        pltpu.VMEM((LENGTH, wide), LOW),
        *scatter_scratch(rows, size), PAIRS, LOCAL,
        pltpu.VMEM((2, size, half), LOW), pltpu.VMEM((size, half), LOW),
        pltpu.SemaphoreType.DMA((2, size // TILE)),
    ]
    return launch(
        expand_back_kernel,
        number, rows, [VM, ANY, ANY, ANY, ANY, VM, VM, VM, VM, VM],
        (grad, *contract, *expand, slope, active, second, hidden, vec),
        outs, [VM] * 6 + [ANY], scratch, swaps, False, True, late=(5, 6, 7, 8),
    )


def scores_scratch(size, width, heads):
    return [
        pltpu.VMEM((size, 4 * width), LOW),
        pltpu.VMEM((LENGTH, size), LOW),
        pltpu.VMEM((heads, LENGTH, HEAD), LOW),
        pltpu.VMEM((8, LENGTH), WIDE),
        pltpu.VMEM((heads, LENGTH, HEAD), LOW),
        pltpu.VMEM((heads, LENGTH, HEAD), WIDE),
        pltpu.VMEM((heads, LENGTH, HEAD), WIDE),
    ]


def late_attend_call(number, low, grad, x_own, pair, normed, heads_all, o, lse, vec, result, y, swaps):
    rows, size = grad.shape
    width = o.shape[1]
    heads = width // HEAD
    outs = (shape((rows, size)), shape((8, size), WIDE), shape((2, width, LENGTH)), shape((size, 4 * width)))
    scratch = [
        *scores_scratch(size, width, heads),
        pltpu.VMEM((LENGTH, 3 * width), LOW),
        pltpu.VMEM((size, 4 * width), LOW),
        pltpu.VMEM((size, width), LOW),
        pltpu.VMEM((LENGTH, width), LOW),
        pltpu.VMEM((LENGTH, width), LOW),
        pltpu.VMEM((LENGTH // rows, rows, width), LOW),
        *scatter_scratch(rows, size), PAIRS,
        pltpu.SemaphoreType.DMA((2, 3)), pltpu.SemaphoreType.DMA((2, 2)), LOCAL,
    ]
    return launch(
        functools.partial(late_attend_kernel, heads),
        number, rows, [VM, VM, VM, ANY, ANY, VM, VM, VM, VM, VM, VM, VM],
        (low, grad, x_own, *pair, normed, heads_all, o, lse, vec, result, y),
        outs, (VM, VM, VM, ANY), scratch, swaps, True, True, late=(1, 2, 5, 6, 7, 8, 10, 11),
    )


def scores_back_call(number, low, pair, heads_all, o, lse, keep, send):
    rows, size = low.shape
    width = o.shape[1]
    heads = width // HEAD
    outs = (shape((LENGTH, 3 * width)), shape((size, width)), shape(keep.shape))
    scratch = [
        *scores_scratch(size, width, heads),
        pltpu.VMEM(keep.shape, LOW),
        PAIRS, LOCAL, pltpu.SemaphoreType.DMA((2, 1)),
    ]
    return launch(
        functools.partial(scores_back_kernel, heads),
        number, rows, [VM, ANY, ANY, VM, VM, VM, VM, ANY], (low, *pair, heads_all, o, lse, keep, send),
        outs, (VM, VM, ANY), scratch, (), False, True, late=(3, 4, 5, 6),
    )[0]


def attend_back_call(number, mixed, outer, grad, x_own, pair, normed, vec):
    rows, size = grad.shape
    width = outer.shape[1]
    half = 2 * width
    outs = (shape((size, half)), shape((rows, size)), shape((8, size), WIDE))
    scratch = [
        pltpu.VMEM((size, 4 * width), LOW),
        pltpu.VMEM((2, size, half), LOW),
        pltpu.VMEM((size, half), LOW),
        *scatter_scratch(rows, size), LOCAL, pltpu.SemaphoreType.DMA((2, size // TILE)),
    ]
    return launch(
        attend_back_kernel,
        number, rows, [VM, VM, VM, VM, ANY, ANY, VM, VM],
        (mixed, outer, grad, x_own, *pair, normed, vec), outs, (ANY, VM, VM), scratch, (), False, True,
        late=(1, 2, 3, 6),
    )[0]


def finish_call(number, parts, near, far, sums, row_count):
    rows, size = near.shape
    length, width = far.shape
    columns = length // rows
    outs = (
        shape((2, width, length)),
        shape((16, width), WIDE),
        *[shape(part.shape) for part in parts],
    )
    scratch = [
        pltpu.VMEM((length, width), LOW),
        pltpu.VMEM((columns, rows, width), LOW),
        pltpu.VMEM((columns, 2, 16, width), WIDE),
        pltpu.VMEM((3, 2, 8, width), WIDE),
        pltpu.VMEM((16, width), WIDE),
        pltpu.VMEM((row_count, 16, width), WIDE),
        pltpu.VMEM((length, width), LOW),
        pltpu.SemaphoreType.DMA((2, 3)),
        pltpu.SemaphoreType.DMA((2, 3)),
        pltpu.SemaphoreType.DMA((2, 3)),
        pltpu.SemaphoreType.DMA((2, row_count)),
        pltpu.SemaphoreType.DMA((2, 3)),
    ]
    return pl.pallas_call(
        finish_kernel,
        out_shape=outs,
        in_specs=[ANY] * 3 + [VM] * 6,
        out_specs=(VM, VM) + (ANY,) * 3,
        scratch_shapes=scratch,
        compiler_params=pltpu.CompilerParams(
            collective_id=number, has_side_effects=True, vmem_limit_bytes=GRANT
        ),
        cost_estimate=pl.CostEstimate(flops=int(3e10), bytes_accessed=30 * MEBI, transcendentals=0),
    )(*parts, near, far, *sums)


def cross_call(number, up, part):
    return pl.pallas_call(
        functools.partial(cross_kernel, up),
        out_shape=shape(part.shape),
        in_specs=[ANY],
        out_specs=ANY,
        scratch_shapes=[pltpu.SemaphoreType.DMA((2, 1))],
        compiler_params=pltpu.CompilerParams(
            collective_id=number, has_side_effects=True, vmem_limit_bytes=GRANT
        ),
        cost_estimate=pl.CostEstimate(flops=int(1e10), bytes_accessed=10 * MEBI, transcendentals=0),
    )(part)


def write_call(width, late, far_late, early, far_early):
    rows, size = late[0].shape
    return pl.pallas_call(
        write_kernel,
        out_shape=(
            shape((3, rows, width), WIDE), shape((rows, width), WIDE), shape((rows, size), WIDE), shape((rows, size), WIDE)
        ),
        in_specs=[ANY] * 12,
        out_specs=(VM,) * 4,
        scratch_shapes=[pltpu.VMEM((3, rows, size), LOW)] * 2 + [pltpu.SemaphoreType.DMA((6,))],
        compiler_params=pltpu.CompilerParams(vmem_limit_bytes=GRANT),
    )(*late, *far_late, *early, *far_early)


def swap_sections(value):
    return lax.ppermute(value, "section", [(0, 1), (1, 0)])


def on_device(
    tokens,
    cotangent,
    first_gain,
    first_shift,
    attend_weight,
    attend_bias,
    output_weight,
    output_bias,
    second_gain,
    second_shift,
    expand_weight,
    expand_bias,
    contract_weight,
    contract_bias,
):
    section = lax.axis_index("section")
    column = lax.axis_index("col")
    first_section = section == 0
    columns = lax.axis_size("col")
    width = tokens.shape[1]
    size = width * columns
    rows = LENGTH // columns

    def pick(early, later):
        return jnp.where(first_section, early, later)

    block_rows = attend_weight.shape[1]
    units = (
        jnp.concatenate(
            [attend_weight[0].reshape(block_rows, 3 * width), output_weight[0].T], axis=1
        ),
        expand_weight[0],
        contract_weight[0].T,
    )
    kept_blocks, sent_blocks = [], []
    for unit in units:
        half = unit.shape[1] // 2
        low, high = unit[:, :half], unit[:, half:]
        kept_blocks.append(pick(low, high))
        sent_blocks.append(pick(high, low))

    small = jnp.concatenate(
        [
            first_gain,
            first_shift,
            output_bias,
            second_gain,
            second_shift,
            contract_bias,
            attend_bias[0],
            expand_bias[0].reshape(-1, width),
        ],
        0,
    )
    filled = small.shape[0]
    small = jnp.pad(small, ((0, -filled % 16), (0, 0)))
    got_attend = swap_sections(sent_blocks[0])
    got_attend, sent_expand = lax.optimization_barrier((got_attend, sent_blocks[1]))
    x0_full, gy_full, vectors, got_expand, got_contract = start_call(
        1, tokens, cotangent, small, sent_expand, units[2], columns
    )

    def gather_blocks(block):
        return lax.all_gather(block, "row", axis=0, tiled=True)

    half = units[2].shape[1] // 2
    mats = [[], []]
    for own, got in ((kept_blocks[0], got_attend), (kept_blocks[1], got_expand)):
        for layer, block in enumerate((pick(own, got), pick(got, own))):
            mats[layer].append(gather_blocks(block))
    mats[0].append(gather_blocks(pick(kept_blocks[2], got_contract[:, half:])))
    mats[1].append(gather_blocks(pick(got_contract, units[2])))
    vectors = vectors.astype(WIDE)
    wide_vectors = jnp.swapaxes(vectors[:, :, :6], 1, 2).reshape(2, 6, size)
    wide_vectors = jnp.pad(wide_vectors, ((0, 0), (0, 2), (0, 0)))
    own_vectors = lax.dynamic_index_in_dim(vectors, column, 1, keepdims=False)
    attend_biases = jnp.stack(
        [own_vectors[:, 6], jnp.zeros_like(own_vectors[:, 6]), own_vectors[:, 7]], 1
    ).reshape(2, 1, 3 * width)
    expand_biases = own_vectors[:, 8:filled].reshape(2, 1, -1)

    def own_rows(full):
        return lax.dynamic_slice_in_dim(full, column * rows, rows, 0)

    def own_features(full):
        return lax.dynamic_slice_in_dim(full, column * width, width, 1)

    attn = (mats[0][0], swap_sections(mats[0][0]))
    x = x0_full
    kept, pairs = [], []
    owns = [own_rows(x0_full)]
    for layer in range(2):
        last = layer == 1
        vec = wide_vectors[layer]
        (normed, heads, o, lse, hidden, second_own), (other,) = attend_call(
            2 + 3 * layer, x, attn, vec, attend_biases[layer], rows, width, [mats[layer][1]]
        )
        expand = (mats[layer][1], other)
        outs, others = widen_call(
            3 + 3 * layer, second_own, expand, expand_biases[layer],
            gy_full if last else None, [] if last else [mats[0][2]],
        )
        second, active, slope = outs[:3]
        contract = (mats[layer][2], mats[layer][2] if last else others[0])
        if last:
            c1 = outs[3]
        pairs.append((attn, expand, contract))
        kept.append((normed, heads, o, lse, hidden, second, active, slope))
        if not last:
            (own, x), others = contract_call(4, active, hidden, contract, vec, [mats[1][0]])
            owns.append(own)
            attn = (mats[1][0], others[0])
    y0 = own_features(x)

    def scatter(total):
        return lax.psum_scatter(total, "row", scatter_dimension=0, tiled=True)

    def tie(value, then):
        return lax.optimization_barrier((value, then))

    attn, expand, contract = pairs[1]
    normed, heads, o, lse, hidden, second, active, slope = kept[1]
    (grad_hidden, low, expand_sums1, e1, result), _ = late_expand_call(
        8, active, hidden, contract, expand, gy_full, slope, second, wide_vectors[1], []
    )
    (gx1_own, attend_sums1, layer_outputs, w1), _ = late_attend_call(
        10, low, grad_hidden, owns[1], attn, normed, heads, o, lse, wide_vectors[1], result, y0, []
    )

    attn, expand, contract = pairs[0]
    normed, heads, o, lse, hidden, second, active, slope = kept[0]
    part_c1 = scatter(c1)
    (grad_hidden, low, expand_sums0, ek0, es0, gx1_full, total_c0), (far_c1,) = expand_back_call(
        12, gx1_own, contract, expand, slope, active, second, hidden, wide_vectors[0], [part_c1]
    )
    part_e1, low = tie(scatter(e1), low)
    mixed, outer, total_e0 = scores_back_call(14, low, attn, heads, o, lse, ek0, es0)
    part_w1, mixed = tie(scatter(w1), mixed)
    part_e1, mixed = tie(part_e1, mixed)
    far_e1, mixed = tie(cross_call(18, True, part_e1), mixed)
    part_c0, mixed = tie(scatter(total_c0), mixed)
    total_w0, gx0_own, attend_sums0 = attend_back_call(
        15, mixed, outer, grad_hidden, owns[0], attn, normed, wide_vectors[0]
    )
    part_e0, gx0_own = tie(scatter(total_e0), gx0_own)
    input_grads, small_grads, far_w1, far_c0, far_e0 = finish_call(
        16,
        (part_w1, part_c0, part_e0),
        gx0_own,
        own_features(gx1_full),
        (attend_sums0, expand_sums0, attend_sums1, expand_sums1),
        lax.axis_size("row"),
    )

    part_w0, small_grads = tie(scatter(total_w0), small_grads)
    far_w0 = cross_call(17, False, part_w0)
    attend_part, output_part, expand_part, contract_part = write_call(
        width,
        (part_w1, part_e1, part_c1),
        (far_w1, far_e1, far_c1),
        (part_w0, part_e0, part_c0),
        (far_w0, far_e0, far_c0),
    )
    return (
        jnp.concatenate([layer_outputs[0], layer_outputs[1]], 1).T[None],
        jnp.concatenate([input_grads[0], input_grads[1]], 1).astype(WIDE).T[None],
        small_grads[0:1],
        small_grads[1:2],
        jnp.swapaxes(attend_part, 0, 1)[None],
        small_grads[8:10][None],
        output_part.T[None],
        small_grads[2:3],
        small_grads[3:4],
        small_grads[4:5],
        expand_part[None],
        small_grads[10 : 10 + expand_bias.shape[1] // width].reshape(1, -1),
        contract_part.T[None],
        small_grads[5:6],
    )


def solution(mesh):
    return jax.shard_map(
        on_device,
        mesh=mesh,
        in_specs=(
            P("row", "col"),
            P("row", "col"),
            P("section", "col"),
            P("section", "col"),
            P("section", "row", None, "col"),
            P("section", None, "col"),
            P("section", "col", "row"),
            P("section", "col"),
            P("section", "col"),
            P("section", "col"),
            P("section", "row", "col"),
            P("section", "col"),
            P("section", "col", "row"),
            P("section", "col"),
        ),
        out_specs=(
            P("section", "row", "col"),
            P("section", "row", "col"),
            P("section", "col"),
            P("section", "col"),
            P("section", "row", None, "col"),
            P("section", None, "col"),
            P("section", "col", "row"),
            P("section", "col"),
            P("section", "col"),
            P("section", "col"),
            P("section", "row", "col"),
            P("section", "col"),
            P("section", "col", "row"),
            P("section", "col"),
        ),
        check_vma=False,
    )
```

```python
import functools

import jax
import jax.numpy as jnp
from jax import lax
from jax.experimental import pallas as pl
from jax.experimental.pallas import tpu as pltpu
from jax.sharding import PartitionSpec as P

HEAD = 64
LENGTH = 1024
EPS = 1e-05
LOW = jnp.bfloat16
WIDE = jnp.float32
MESH = pl.DeviceIdType.MESH
PARTS = 2
TILE = 256
MEBI = 1024 * 1024
GRANT = 58 * MEBI


def nn(left, right):
    return lax.dot_general(left, right, (((1,), (0,)), ((), ())), preferred_element_type=WIDE)


def nt(left, right):
    return lax.dot_general(left, right, (((1,), (1,)), ((), ())), preferred_element_type=WIDE)


def tn(left, right):
    return lax.dot_general(left, right, (((0,), (0,)), ((), ())), preferred_element_type=WIDE)


def turned(values):
    width = values.shape[1]
    unit = (
        lax.broadcasted_iota(jnp.int32, (width, width), 0) == lax.broadcasted_iota(jnp.int32, (width, width), 1)
    ).astype(LOW)
    return nt(unit, values)


def normalise(values):
    center = jnp.mean(values, axis=1, keepdims=True)
    centred = values - center
    scale = lax.rsqrt(jnp.mean(centred * centred, axis=1, keepdims=True) + EPS)
    return centred * scale, scale


def norm_backward(grad, hat, scale, gain):
    scaled = grad * gain
    mean_one = jnp.mean(scaled, axis=1, keepdims=True)
    mean_two = jnp.mean(scaled * hat, axis=1, keepdims=True)
    return scale * (scaled - mean_one - hat * mean_two)


class Group:
    def __init__(self, rows):
        self.me = lax.axis_index("col")
        chip, core = self.me // 2, self.me % 2
        self.sib = chip * 2 + 1 - core
        self.peer = (1 - chip) * 2 + core
        self.diag = (1 - chip) * 2 + 1 - core
        self.rows = rows
        self.part = rows // PARTS
        self.loads, self.stores, self.begun = {}, {}, set()

    def need(self, *places):
        for place in places:
            self.loads[place].wait()

    def emit(self, *places):
        for place in places:
            self.stores[place].start()
            self.begun.add(place)

    def greet(self, swaps, diagonal, rows=()):
        barrier = pltpu.get_barrier_semaphore()
        others = [{"col": self.sib}, {"col": self.peer}]
        if diagonal:
            others.append({"col": self.diag})
        if swaps:
            others.append({"section": 1 - lax.axis_index("section")})
        others += [{"row": row} for row in rows]
        for other in others:
            pl.semaphore_signal(barrier, inc=1, device_id=other, device_id_type=MESH)
        pl.semaphore_wait(barrier, len(others))

    def slab(self, owner, j):
        return pl.ds(pl.multiple_of(owner * self.rows + j * self.part, self.part), self.part)

    def chunk(self, owner):
        return pl.ds(pl.multiple_of(owner * self.rows, self.rows), self.rows)


def push(src, dst, sems, slot, target, axis="col"):
    return pltpu.make_async_remote_copy(
        src_ref=src,
        dst_ref=dst,
        send_sem=sems.at[0, slot],
        recv_sem=sems.at[1, slot],
        device_id={axis: target},
        device_id_type=MESH,
    )


class Gather:
    def __init__(self, group, full, sems, blocks=False):
        self.group, self.full, self.sems, self.blocks = group, full, sems, blocks

    def piece(self, owner, j):
        if not self.blocks:
            return self.full.at[self.group.slab(owner, j)]
        part = self.full.shape[1] // PARTS
        return self.full.at[owner, pl.ds(j * part, part)]

    def start(self):
        g = self.group
        self.over, self.near, self.relayed = [], [], []
        for j in range(PARTS):
            piece = self.piece(g.me, j)
            self.over.append(push(piece, piece, self.sems, j, g.peer))
            self.over[-1].start()
        for j in range(PARTS):
            piece = self.piece(g.me, j)
            self.near.append(push(piece, piece, self.sems, PARTS + j, g.sib))
            self.near[-1].start()

    def sibling(self):
        for copy in self.near:
            copy.wait_recv()

    def relay(self):
        g = self.group
        for j in range(PARTS):
            self.over[j].wait_recv()
            piece = self.piece(g.peer, j)
            self.relayed.append(push(piece, piece, self.sems, 2 * PARTS + j, g.sib))
            self.relayed[-1].start()

    def diagonal(self):
        for copy in self.relayed:
            copy.wait_recv()

    def done(self):
        for copy in self.over + self.near + self.relayed:
            copy.wait_send()

    def each(self, body, first=None):
        g = self.group
        self.start()
        if first is not None:
            first()
        body(g.me)
        self.sibling()
        body(g.sib)
        self.relay()
        body(g.peer)
        self.diagonal()
        body(g.diag)
        self.done()


class Scatter:
    def __init__(self, group, stage, land, total, sems):
        self.group, self.stage, self.land, self.total, self.sems = group, stage, land, total, sems

    def start(self, part):
        g, stage, land = self.group, self.stage, self.land
        self.first, self.over, self.near = [], [], []
        def split(owner):
            whole = part(owner)
            return [whole[j * g.part : (j + 1) * g.part] for j in range(PARTS)]

        for j, mine in enumerate(split(g.diag)):
            stage[0, j] = mine.astype(LOW)
            self.first.append(push(stage.at[0, j], land.at[0, j], self.sems, j, g.sib))
            self.first[-1].start()
        for j, mine in enumerate(split(g.peer)):
            self.first[j].wait_recv()
            stage[1, j] = (mine + land[0, j].astype(WIDE)).astype(LOW)
            self.over.append(push(stage.at[1, j], land.at[1, j], self.sems, PARTS + j, g.peer))
            self.over[-1].start()
        for j, mine in enumerate(split(g.sib)):
            stage[2, j] = mine.astype(LOW)
            self.near.append(push(stage.at[2, j], land.at[2, j], self.sems, 2 * PARTS + j, g.sib))
            self.near[-1].start()
        for j, mine in enumerate(split(g.me)):
            self.total[j] = mine

    def take(self, j):
        self.near[j].wait_recv()
        self.over[j].wait_recv()
        land = self.land
        return self.total[j] + (land[1, j].astype(WIDE) + land[2, j].astype(WIDE))

    def done(self):
        for copy in self.first + self.over + self.near:
            copy.wait_send()


class Deliver:
    def __init__(self, group, stage, out, sems):
        self.group, self.stage, self.out, self.sems = group, stage, out, sems

    def start(self, rows_ref):
        g, width = self.group, self.out.shape[1]
        for c in range(self.stage.shape[0]):
            self.stage[c] = rows_ref[:, c * width : (c + 1) * width]
        place = self.out.at[g.chunk(g.me)]
        self.copies = [
            push(self.stage.at[other], place, self.sems, n, other)
            for n, other in enumerate((g.peer, g.diag, g.sib))
        ]
        for copy in self.copies:
            copy.start()
        self.out[g.chunk(g.me), :] = self.stage[g.me]

    def done(self):
        for copy in self.copies:
            copy.wait()


class OneWay:
    def __init__(self, up, down, sems):
        self.section = lax.axis_index("section")
        both = [*up, *down]
        copies = [
            push(source, into, sems, n, 1 - self.section, "section")
            for n, (source, into) in enumerate(both)
        ]
        self.up, self.down = copies[: len(up)], copies[len(up) :]

    def each(self, first, second):
        @pl.when(self.section == 0)
        def _():
            first(self.up)
            second(self.down)

        @pl.when(self.section == 1)
        def _():
            first(self.down)
            second(self.up)

    def start(self):
        self.each(lambda copies: [copy.start() for copy in copies], lambda copies: None)

    def wait(self):
        self.each(
            lambda copies: [copy.wait_send() for copy in copies],
            lambda copies: [copy.wait_recv() for copy in copies],
        )


def scatter_scratch(rows, width):
    part = rows // PARTS
    return [
        pltpu.VMEM((3, PARTS, part, width), LOW),
        pltpu.VMEM((3, PARTS, part, width), LOW),
        pltpu.VMEM((PARTS, part, width), WIDE),
        pltpu.SemaphoreType.DMA((2, 3 * PARTS)),
    ]


class Halves:
    def __init__(self, pair, whole, sems, slot):
        if pair[0].shape[1] == whole.shape[1]:
            self.copies = [pltpu.make_async_copy(pair[0], whole, sems.at[slot])]
            return
        section = lax.axis_index("section")
        half = whole.shape[1] // 2
        self.copies = []
        for n, place in enumerate((section, 1 - section)):
            columns = pl.ds(pl.multiple_of(place * half, half), half)
            self.copies.append(
                pltpu.make_async_copy(pair[n], whole.at[:, columns], sems.at[slot + n])
            )

    def start(self):
        for copy in self.copies:
            copy.start()

    def wait(self):
        for copy in self.copies:
            copy.wait()


class Trade:
    def __init__(self, keep, send, got, sems):
        self.keep, self.send, self.got, self.sems = keep, send, got, sems
        self.tiles = keep.shape[0] // TILE

    def copy(self, n):
        rows = pl.ds(pl.multiple_of(n * TILE, TILE), TILE)
        return push(
            self.send.at[rows], self.got.at[rows], self.sems, n, 1 - lax.axis_index("section"), "section"
        )

    def start(self, make):
        @pl.loop(0, self.tiles)
        def _(n):
            make(pl.ds(pl.multiple_of(n * TILE, TILE), TILE))
            self.copy(n).start()

    def finish(self):
        @pl.loop(0, self.tiles)
        def _(n):
            self.copy(n).wait()

        add_into(self.keep, self.got)


def add_into(keep_ref, got_ref):
    @pl.loop(0, keep_ref.shape[0] // TILE)
    def _(n):
        rows = pl.ds(pl.multiple_of(n * TILE, TILE), TILE)
        keep_ref[rows, :] = (keep_ref[rows, :].astype(WIDE) + got_ref[rows, :].astype(WIDE)).astype(LOW)


def causal_scores(scores):
    size = scores.shape[1]
    keep = lax.broadcasted_iota(jnp.int32, (size, size), 0) <= lax.broadcasted_iota(
        jnp.int32, (size, size), 1
    )
    begin = scores.shape[0] - size
    last = jnp.where(keep, scores[begin:], -1000000000.0)
    return last if begin == 0 else jnp.concatenate([scores[:begin], last], 0)


def attention_out(owner, size, heads_ref, o3, lse_ref, heads):
    for i in range(heads_ref.shape[1] // size):
        rows, finish = slice(i * size, (i + 1) * size), (i + 1) * size

        @pl.when(owner == i)
        def _():
            @pl.loop(0, heads)
            def _(h):
                scores = causal_scores(nt(heads_ref[heads + h, :finish, :], heads_ref[h, rows, :]))
                highest = jnp.max(scores, axis=0, keepdims=True)
                powers = jnp.exp(scores - highest)
                summed = jnp.sum(powers, axis=0, keepdims=True)
                mixed = tn(heads_ref[2 * heads + h, :finish, :], powers.astype(LOW))
                o3[h, rows, :] = (mixed / summed).T.astype(LOW)
                lse_ref[pl.ds(h, 1), rows] = highest + jnp.log(summed)


def attention_back(owner, size, heads_ref, go3, lse_ref, dots_ref, g3, key_acc, value_acc, heads):
    for i in range(heads_ref.shape[1] // size):
        rows, finish = slice(i * size, (i + 1) * size), (i + 1) * size

        @pl.when(owner == i)
        def _():
            @pl.loop(0, heads)
            def _(h):
                queries = heads_ref[h, rows, :]
                keys = heads_ref[heads + h, :finish, :]
                grads = go3[h, rows, :]
                probs = jnp.exp(causal_scores(nt(keys, queries) - lse_ref[pl.ds(h, 1), rows]))
                grad_probs = nt(heads_ref[2 * heads + h, :finish, :], grads)
                grad_scores = (probs * (grad_probs - dots_ref[pl.ds(h, 1), rows])).astype(LOW)
                g3[h, rows, :] = (tn(grad_scores, keys) * HEAD ** (-0.5)).astype(LOW)
                key_acc[h, :finish, :] += nn(grad_scores, queries)
                value_acc[h, :finish, :] += nn(probs.astype(LOW), grads)


def start_kernel(
    tokens_ref, cotangent_ref, small_ref, expand_ref, contract_ref,
    x_ref, g_ref, vectors_ref, got_expand_ref, got_contract_ref,
    x4, g4, s4, other4, x_sems, g_sems, s_sems, local_sems,
):
    section = lax.axis_index("section")
    group = Group(x_ref.shape[0] // 4)
    length = x_ref.shape[0]
    loads = []
    rows = pl.ds(pl.multiple_of(section * length, length), length)
    for n, (source, into) in enumerate(((tokens_ref.at[rows], x4), (cotangent_ref.at[rows], g4), (small_ref, s4))):
        loads.append(pltpu.make_async_copy(source, into.at[group.me], local_sems.at[n]))
        loads[-1].start()
    group.greet(True, False)
    blocks = [
        push(source, into, s_sems, 3 * PARTS + 1 + n, 1 - section, "section")
        for n, (source, into) in enumerate(((expand_ref, got_expand_ref), (contract_ref, got_contract_ref)))
    ]
    for block in blocks:
        block.start()
    gathers = [Gather(group, x4, x_sems, True), Gather(group, s4, s_sems, True), Gather(group, g4, g_sems, True)]
    for gather, load in zip(gathers, (loads[0], loads[2], loads[1])):
        load.wait()
        gather.start()
    width = x4.shape[2]
    for gather, blocks4, full_ref in ((gathers[0], x4, x_ref), (gathers[1], None, None), (gathers[2], g4, g_ref)):
        gather.sibling()
        gather.relay()
        gather.diagonal()
        if blocks4 is None:
            swap = push(s4, other4, s_sems, 3 * PARTS, 1 - section, "section")
            swap.start()
        else:
            for c in range(blocks4.shape[0]):
                full_ref[:, c * width : (c + 1) * width] = blocks4[c]
    swap.wait()
    for block in blocks:
        block.wait()
    vectors_ref[section] = s4[...]
    vectors_ref[1 - section] = other4[...]
    for gather in gathers:
        gather.done()


def attend_kernel(
    heads, group, x_ref, mine_ref, other_ref, vec_ref, bias_ref,
    normed_ref, heads_ref, o_ref, lse_ref, hidden_ref, second_ref,
    weight, o3, stage, land, total, scatter_sems, local_sems,
):
    width = o_ref.shape[1]
    halves = Halves((mine_ref, other_ref), weight, local_sems, 0)
    halves.start()
    lse_ref[...] = jnp.zeros_like(lse_ref)
    halves.wait()

    @pl.loop(0, LENGTH // group.rows)
    def _(owner):
        rows = group.chunk(owner)
        hat, _ = normalise(x_ref[rows, :].astype(WIDE))
        normed = (hat * vec_ref[0:1, :] + vec_ref[1:2, :]).astype(LOW)
        normed_ref[rows, :] = normed
        mixed = nn(normed, weight[:, : 3 * width]) + bias_ref[...]
        for j in range(3 * heads):
            piece = mixed[:, j * HEAD : (j + 1) * HEAD]
            if j < heads:
                piece = piece * HEAD ** (-0.5)
            heads_ref[j, rows, :] = piece.astype(LOW)

    group.emit(0, 1)

    def attend(owner):
        rows = group.chunk(owner)
        attention_out(owner, group.rows, heads_ref, o3, lse_ref, heads)
        for h in range(heads):
            o_ref[rows, h * HEAD : (h + 1) * HEAD] = o3[h, rows, :]
        return nt(o_ref[rows, :], weight[:, 3 * width :])

    scatter = Scatter(group, stage, land, total, scatter_sems)
    scatter.start(attend)
    group.emit(2, 3)
    for j in range(PARTS):
        rows = slice(j * group.part, (j + 1) * group.part)
        residual = x_ref[group.slab(group.me, j), :].astype(WIDE)
        hidden = residual + scatter.take(j) + vec_ref[2:3, :]
        hidden_ref[rows, :] = hidden
        hat, _ = normalise(hidden)
        second_ref[rows, :] = (hat * vec_ref[3:4, :] + vec_ref[4:5, :]).astype(LOW)
    scatter.done()


def outer_whole(left_ref, right_ref, out_ref):
    @pl.loop(0, left_ref.shape[1] // TILE)
    def _(n):
        rows = pl.ds(pl.multiple_of(n * TILE, TILE), TILE)
        out_ref[rows, :] = tn(left_ref[:, rows], right_ref[...]).astype(LOW)


def widen_kernel(last, group, second_ref, em_ref, eo_ref, bias_ref, *refs):
    if last:
        g_ref, *refs = refs
    full_ref, active_ref, slope_ref, *refs = refs
    if last:
        c_ref, *refs = refs
    expand, gather_sems, local_sems = refs
    halves = Halves((em_ref, eo_ref), expand, local_sems, 0)
    halves.start()
    full_ref[group.chunk(group.me), :] = second_ref[...]
    halves.wait()

    def widen(owner):
        rows = group.chunk(owner)
        t = nn(full_ref[rows, :], expand[...]) + bias_ref[...]
        square = t * t
        bent = jnp.tanh(0.7978845608028654 * t * (1.0 + 0.044715 * square))
        active_ref[rows, :] = (0.5 * t * (1.0 + bent)).astype(LOW)
        slope_ref[rows, :] = (
            0.5 * (1.0 + bent)
            + (0.5 * 0.7978845608028654) * t * (1.0 - bent * bent) * (1.0 + 3 * 0.044715 * square)
        ).astype(LOW)

    Gather(group, full_ref, gather_sems).each(widen)
    if last:
        group.emit(0, 1, 2)
        group.need(4)
        outer_whole(g_ref, active_ref, c_ref)


def outer_halves(left_ref, right_ref, keep_ref, send_ref):
    section = lax.axis_index("section")
    half = right_ref.shape[1] // 2
    for place, out in ((section, keep_ref), (1 - section, send_ref)):
        columns = pl.ds(pl.multiple_of(place * half, half), half)

        @pl.loop(0, left_ref.shape[1] // TILE)
        def _(n):
            rows = pl.ds(pl.multiple_of(n * TILE, TILE), TILE)
            out[rows, :] = tn(left_ref[:, rows], right_ref[:, columns]).astype(LOW)


def contract_kernel(
    group, active_ref, hidden_ref, cm_ref, co_ref, vec_ref, result_ref, full_ref,
    contract, stage, land, total, scatter_sems, gather_sems, local_sems,
):
    halves = Halves((cm_ref, co_ref), contract, local_sems, 0)
    halves.start()
    halves.wait()
    scatter = Scatter(group, stage, land, total, scatter_sems)
    scatter.start(lambda owner: nt(active_ref[group.chunk(owner), :], contract[...]))
    group.need(1)
    for j in range(PARTS):
        rows = slice(j * group.part, (j + 1) * group.part)
        result = (hidden_ref[rows, :] + scatter.take(j) + vec_ref[5:6, :]).astype(LOW)
        result_ref[rows, :] = result
        full_ref[group.slab(group.me, j), :] = result
    Gather(group, full_ref, gather_sems).each(lambda owner: None)
    scatter.done()


def narrow_grads(group, scatter, full_ref, hidden_ref, vec_ref, grad_ref, low_ref, sums_ref):
    for j in range(PARTS):
        rows = slice(j * group.part, (j + 1) * group.part)
        grad = scatter.take(j)
        hat, scale = normalise(hidden_ref[rows, :])
        own = full_ref[group.slab(group.me, j), :].astype(WIDE)
        out = own + norm_backward(grad, hat, scale, vec_ref[3:4, :])
        grad_ref[rows, :] = out
        low_ref[rows, :] = out.astype(LOW)
        for n, term in enumerate((grad * hat, grad, own, out)):
            sums_ref[n : n + 1, :] += jnp.sum(term, axis=0, keepdims=True)


def bend(rows, full_ref, contract, slope_ref, before, sums_ref):
    grad = (nn(full_ref[rows, :], contract[...]) * slope_ref[rows, :].astype(WIDE)).astype(LOW)
    before[rows, :] = grad
    sums_ref[4:5, :] += jnp.sum(grad.astype(WIDE), axis=0, keepdims=True)


def late_expand_kernel(
    group, active_ref, hidden_ref, cm_ref, co_ref, em_ref, eo_ref, g_ref, slope_ref, second_ref, vec_ref,
    grad_ref, low_ref, sums_ref, e_ref, result,
    contract, expand, before,
    stage_a, land_a, total_a, sems_a, stage, land, total, scatter_sems, local_sems,
):
    first = Halves((cm_ref, co_ref), contract, local_sems, 0)
    then = Halves((em_ref, eo_ref), expand, local_sems, 2)
    first.start()
    then.start()
    sums_ref[...] = jnp.zeros_like(sums_ref)
    first.wait()
    forward = Scatter(group, stage_a, land_a, total_a, sems_a)
    forward.start(lambda owner: nt(active_ref[group.chunk(owner), :], contract[...]))
    group.need(6, 7)

    @pl.loop(0, LENGTH // group.rows)
    def _(n):
        bend(group.chunk(n), g_ref, contract, slope_ref, before, sums_ref)

    then.wait()
    scatter = Scatter(group, stage, land, total, scatter_sems)
    scatter.start(lambda owner: nt(before[group.chunk(owner), :], expand[...]))
    group.need(1)
    for j in range(PARTS):
        rows = slice(j * group.part, (j + 1) * group.part)
        result[rows, :] = (hidden_ref[rows, :] + forward.take(j) + vec_ref[5:6, :]).astype(LOW)
    group.emit(4)
    group.need(8)
    outer_whole(second_ref, before, e_ref)
    group.emit(3)
    narrow_grads(group, scatter, g_ref, hidden_ref, vec_ref, grad_ref, low_ref, sums_ref)
    group.emit(0, 1, 2)
    forward.done()
    scatter.done()


def expand_back_kernel(
    group, g_ref, cm_ref, co_ref, em_ref, eo_ref, slope_ref, active_ref, second_ref, hidden_ref, vec_ref,
    grad_ref, low_ref, sums_ref, ek_ref, es_ref, full_ref, c_ref,
    contract, expand, before, stage, land, total, scatter_sems, gather_sems, local_sems, outer, got, trade_sems,
):
    section = lax.axis_index("section")
    first = Halves((cm_ref, co_ref), contract, local_sems, 0)
    then = Halves((em_ref, eo_ref), expand, local_sems, 2)
    first.start()
    then.start()
    sums_ref[...] = jnp.zeros_like(sums_ref)
    full_ref[group.chunk(group.me), :] = g_ref[...]
    first.wait()
    Gather(group, full_ref, gather_sems).each(
        lambda owner: bend(group.chunk(owner), full_ref, contract, slope_ref, before, sums_ref),
        lambda: group.need(5),
    )
    group.emit(5)
    group.need(6)
    half = active_ref.shape[1] // 2

    def columns(place):
        return pl.ds(pl.multiple_of(place * half, half), half)

    def make(n):
        def tile(rows):
            place = section if n == 0 else 1 - section
            outer[n, rows, :] = tn(full_ref[:, rows], active_ref[:, columns(place)]).astype(LOW)

        return tile

    trade = Trade(outer.at[0], outer.at[1], got, trade_sems)
    trade.start(make(1))
    then.wait()
    scatter = Scatter(group, stage, land, total, scatter_sems)
    scatter.start(lambda owner: nt(before[group.chunk(owner), :], expand[...]))
    group.need(7)
    outer_halves(second_ref, before, ek_ref, es_ref)
    group.emit(3, 4)
    keep = make(0)

    @pl.loop(0, outer.shape[1] // TILE)
    def _(n):
        keep(pl.ds(pl.multiple_of(n * TILE, TILE), TILE))

    group.need(8)
    narrow_grads(group, scatter, full_ref, hidden_ref, vec_ref, grad_ref, low_ref, sums_ref)
    group.emit(0, 1, 2)
    scatter.done()
    trade.finish()
    store = pltpu.make_async_copy(outer.at[0], c_ref, local_sems.at[0])
    store.start()
    store.wait()


def scores_back(group, heads, low_ref, weight, heads_ref, o_ref, lse_ref, full, go3, dots, g3, accs, mixed, gather_sems, first):
    width = o_ref.shape[1]
    picks = (
        lax.broadcasted_iota(jnp.int32, (8, width), 1) // HEAD
        == lax.broadcasted_iota(jnp.int32, (8, width), 0)
    ).astype(WIDE)
    for acc in accs:
        acc[...] = jnp.zeros_like(acc)

    def spread(owner):
        rows = group.chunk(owner)
        grads = nn(full[rows, :], weight[:, 3 * width :]).astype(LOW)
        for h in range(heads):
            go3[h, rows, :] = grads[:, h * HEAD : (h + 1) * HEAD]
        term = grads.astype(WIDE) * o_ref[rows, :].astype(WIDE)
        dots[:, rows] = lax.dot_general(
            picks,
            term,
            (((1,), (1,)), ((), ())),
            precision=lax.Precision.HIGHEST,
            preferred_element_type=WIDE,
        )
        attention_back(owner, group.rows, heads_ref, go3, lse_ref, dots, g3, *accs, heads)

    full[group.chunk(group.me), :] = low_ref[...]
    Gather(group, full, gather_sems).each(spread, first)
    for j in range(3 * heads):
        source = g3[j] if j < heads else accs[j // heads - 1][j % heads].astype(LOW)
        mixed[:, j * HEAD : (j + 1) * HEAD] = source


def outer_out(full, o_ref, outer_ref):
    @pl.loop(0, outer_ref.shape[0] // TILE)
    def _(n):
        rows = pl.ds(pl.multiple_of(n * TILE, TILE), TILE)
        outer_ref[rows, :] = tn(full[:, rows], o_ref[...]).astype(LOW)


def attend_grads(group, scatter, x_ref, grad_ref, vec_ref, mixed, width, out_ref, sums_ref):
    sums_ref[2:3, : 3 * width] = jnp.sum(mixed[...].astype(WIDE), axis=0, keepdims=True)
    for j in range(PARTS):
        rows = slice(j * group.part, (j + 1) * group.part)
        grad = scatter.take(j)
        hat, scale = normalise(x_ref[rows, :].astype(WIDE))
        out = grad_ref[rows, :] + norm_backward(grad, hat, scale, vec_ref[0:1, :])
        out_ref[rows, :] = out.astype(LOW)
        for n, term in enumerate((grad * hat, grad)):
            sums_ref[n : n + 1, :] += jnp.sum(term, axis=0, keepdims=True)


def late_attend_kernel(
    heads, group, low_ref, grad_ref, x_ref, mine_ref, other_ref, normed_ref, heads_ref, o_ref, lse_ref, vec_ref,
    result_ref, y_ref,
    out_ref, sums_ref, results_ref, w_ref,
    weight, full, go3, dots, g3, key_acc, value_acc, mixed, outer, outer_o, late, y_land, stage4,
    stage, land, total, scatter_sems, gather_sems, deliver_sems, y_sems, local_sems,
):
    width = o_ref.shape[1]
    section = lax.axis_index("section")
    halves = Halves((mine_ref, other_ref), weight, local_sems, 0)
    halves.start()
    sums_ref[...] = jnp.zeros_like(sums_ref)
    halves.wait()
    deliver = Deliver(group, stage4, late, deliver_sems)

    def first():
        group.need(6, 7, 8, 10)
        deliver.start(result_ref)

    scores_back(
        group, heads, low_ref, weight, heads_ref, o_ref, lse_ref, full, go3, dots, g3,
        (key_acc, value_acc), mixed, gather_sems, first,
    )
    deliver.done()
    group.need(11)
    results = OneWay([(late, y_land)], [(y_ref, y_land)], y_sems)
    results.start()
    scatter = Scatter(group, stage, land, total, scatter_sems)
    scatter.start(lambda owner: nt(mixed[group.chunk(owner), :], weight[:, : 3 * width]))
    outer_out(full, o_ref, outer_o)
    group.need(5)

    @pl.loop(0, weight.shape[0] // TILE)
    def _(n):
        rows = pl.ds(pl.multiple_of(n * TILE, TILE), TILE)
        outer[rows, : 3 * width] = tn(normed_ref[:, rows], mixed[...]).astype(LOW)
        outer[rows, 3 * width :] = outer_o[rows, :]

    store = pltpu.make_async_copy(outer, w_ref, local_sems.at[2])
    store.start()
    @pl.when(section == 0)
    def _():
        results_ref[section] = turned(y_ref[...]).astype(LOW)

    @pl.when(section == 1)
    def _():
        results_ref[section] = turned(late[...]).astype(LOW)

    group.need(1, 2)
    attend_grads(group, scatter, x_ref, grad_ref, vec_ref, mixed, width, out_ref, sums_ref)
    results.wait()
    results_ref[1 - section] = turned(y_land[...]).astype(LOW)
    scatter.done()
    store.wait()


def scores_back_kernel(
    heads, group, low_ref, mine_ref, other_ref, heads_ref, o_ref, lse_ref, ek_ref, es_ref,
    mixed, outer_ref, e_ref,
    weight, full, go3, dots, g3, key_acc, value_acc, got, gather_sems, local_sems, swap_sems,
):
    swap = push(es_ref, got, swap_sems, 0, 1 - lax.axis_index("section"), "section")
    swap.start()
    halves = Halves((mine_ref, other_ref), weight, local_sems, 0)
    halves.start()
    halves.wait()
    scores_back(
        group, heads, low_ref, weight, heads_ref, o_ref, lse_ref, full, go3, dots, g3,
        (key_acc, value_acc), mixed, gather_sems, lambda: group.need(3, 4, 5),
    )
    group.emit(0)
    outer_out(full, o_ref, outer_ref)
    group.emit(1)
    group.need(6)
    swap.wait()
    add_into(ek_ref, got)
    store = pltpu.make_async_copy(ek_ref, e_ref, local_sems.at[0])
    store.start()
    store.wait()


def attend_back_kernel(
    group, mixed, outer_ref, grad_ref, x_ref, mine_ref, other_ref, normed_ref, vec_ref,
    w_ref, out_ref, sums_ref,
    weight, outer, got, stage, land, total, scatter_sems, local_sems, swap_sems,
):
    width = outer_ref.shape[1]
    section = lax.axis_index("section")
    halves = Halves((mine_ref, other_ref), weight, local_sems, 0)
    halves.start()
    sums_ref[...] = jnp.zeros_like(sums_ref)
    half = weight.shape[1] // 2
    scatter = Scatter(group, stage, land, total, scatter_sems)
    group.need(1, 6)

    def make(n):
        place = section if n == 0 else 1 - section

        def tile(rows):
            @pl.when(place == 0)
            def _():
                outer[n, rows, :] = tn(normed_ref[:, rows], mixed[:, :half]).astype(LOW)

            @pl.when(place == 1)
            def _():
                outer[n, rows, : 3 * width - half] = tn(normed_ref[:, rows], mixed[:, half:]).astype(LOW)
                outer[n, rows, 3 * width - half :] = outer_ref[rows, :]

        return tile

    trade = Trade(outer.at[0], outer.at[1], got, swap_sems)
    trade.start(make(1))
    halves.wait()
    scatter.start(lambda owner: nt(mixed[group.chunk(owner), :], weight[:, : 3 * width]))
    keep = make(0)

    @pl.loop(0, outer.shape[1] // TILE)
    def _(n):
        keep(pl.ds(pl.multiple_of(n * TILE, TILE), TILE))

    group.need(2, 3)
    attend_grads(group, scatter, x_ref, grad_ref, vec_ref, mixed, width, out_ref, sums_ref)
    group.emit(1, 2)
    scatter.done()
    trade.finish()
    store = pltpu.make_async_copy(outer.at[0], w_ref, local_sems.at[2])
    store.start()
    store.wait()


def finish_kernel(
    late_ref, early1_ref, early2_ref, near_hbm, far_hbm, a0_hbm, n0_hbm, a1_hbm, n1_hbm,
    grads_ref, sums_ref, got_late, got_early1, got_early2,
    near_ref, far_ref, a0, n0, a1, n1, mine, stage4, block, land_col, land_x, land_z, send,
    deliver_sems, col_sems, x_sems, z_sems, part_sems, local_sems,
):
    section, row = lax.axis_index("section"), lax.axis_index("row")
    away = 1 - section
    group = Group(near_ref.shape[0])
    width = far_ref.shape[1]
    others = [lax.rem(row + d, land_z.shape[0]) for d in range(1, land_z.shape[0])]
    loads = [
        pltpu.make_async_copy(source, into, local_sems.at[n])
        for n, (source, into) in enumerate(
            (
                (near_hbm, near_ref), (far_hbm, far_ref),
                (a0_hbm, a0), (n0_hbm, n0), (a1_hbm, a1), (n1_hbm, n1),
            )
        )
    ]
    for copy in loads:
        copy.start()
    group.greet(True, True, others)
    parts = OneWay(
        [(late_ref, got_late)], [(early1_ref, got_early1), (early2_ref, got_early2)], part_sems
    )
    parts.start()
    for copy in loads:
        copy.wait()
    deliver = Deliver(group, stage4, mine, deliver_sems)
    deliver.start(near_ref)
    gradients = push(send, grads_ref.at[section], x_sems, 1, away, "section")

    @pl.when(section == 0)
    def _():
        send[...] = turned(far_ref[...]).astype(LOW)
        gradients.start()

    block[...] = jnp.zeros_like(block)
    for layer, (attn, narrow) in enumerate(((a0, n0), (a1, n1))):
        wide = [attn[0:1, :], attn[1:2, :], narrow[3:4, :], narrow[0:1, :], narrow[1:2, :], narrow[2:3, :]]
        for c in range(block.shape[0]):
            columns = slice(c * width, (c + 1) * width)
            for n, term in enumerate(wide):
                block[c, layer, n : n + 1, :] = term[:, columns]
            for n, term in enumerate((attn[2:3, :width], attn[2:3, 2 * width : 3 * width])):
                block[c, layer, 8 + n : 9 + n, :] = term
            for n in range(narrow.shape[1] // width):
                block[c, layer, 10 + n : 11 + n, :] = narrow[4:5, n * width : (n + 1) * width]
    copies = [
        push(block.at[other, :, pl.ds(0, 8)], land_col.at[n], col_sems, n, other)
        for n, other in enumerate((group.peer, group.diag, group.sib))
    ]
    for copy in copies:
        copy.start()
    for copy in copies:
        copy.wait()
    me = group.me
    block[me, :, :8] = block[me, :, :8] + (land_col[0] + (land_col[1] + land_col[2]))
    swap = push(block.at[me, away], land_x, x_sems, 0, away, "section")
    swap.start()
    deliver.done()

    @pl.when(section == 0)
    def _():
        grads_ref[section] = turned(mine[...]).astype(LOW)

    @pl.when(section == 1)
    def _():
        send[...] = turned(mine[...]).astype(LOW)
        gradients.start()
        grads_ref[section] = turned(far_ref[...]).astype(LOW)

    swap.wait()
    land_z[row] = block[me, section] + land_x[...]
    copies = [
        push(land_z.at[row], land_z.at[row], z_sems, n, other, "row")
        for n, other in enumerate(others)
    ]
    for copy in copies:
        copy.start()
    for copy in copies:
        copy.wait()
    result = land_z[0]
    for n in range(1, land_z.shape[0]):
        result = result + land_z[n]
    sums_ref[...] = result
    gradients.wait()
    parts.wait()


def greet_section():
    barrier = pltpu.get_barrier_semaphore()
    other = 1 - lax.axis_index("section")
    pl.semaphore_signal(barrier, inc=1, device_id={"section": other}, device_id_type=MESH)
    pl.semaphore_wait(barrier, 1)


def cross_kernel(up, part_ref, got_ref, sems):
    greet_section()
    pair = [(part_ref, got_ref)]
    part = OneWay(pair, [], sems) if up else OneWay([], pair, sems)
    part.start()
    part.wait()


def write_kernel(*refs):
    late, far_late, early, far_early = [refs[n : n + 3] for n in (0, 3, 6, 9)]
    sums_ref, attend_ref, output_ref, expand_ref, contract_ref, *vector_refs = refs[12:-3]
    own, far, sems = refs[-3:]
    half = early[0].shape[1]
    width = output_ref.shape[0]
    section = lax.axis_index("section")

    def load(firsts, seconds):
        copies = [
            pltpu.make_async_copy(source, into, sems.at[n])
            for n, (source, into) in enumerate((*firsts, *seconds))
        ]
        for copy in copies:
            copy.start()
        for copy in copies:
            copy.wait()

    @pl.when(section == 0)
    def _():
        load(
            [(early[n], own.at[n, :, pl.ds(0, half)]) for n in range(3)],
            [(far_early[n], own.at[n, :, pl.ds(half, half)]) for n in range(3)],
        )
        far[...] = jnp.zeros_like(far)

    @pl.when(section == 1)
    def _():
        load([(late[n], own.at[n]) for n in range(3)], [(far_late[n], far.at[n]) for n in range(3)])

    first = own[0].astype(WIDE) + far[0].astype(WIDE)
    for j in range(3):
        attend_ref[j] = first[:, j * width : (j + 1) * width]
    corner = first[:, 3 * width :]
    high = corner.astype(LOW)
    output_ref[...] = turned(high) + turned((corner - high.astype(WIDE)).astype(LOW))
    expand_ref[...] = own[1].astype(WIDE) + far[1].astype(WIDE)
    contract_ref[...] = own[2].astype(WIDE) + far[2].astype(WIDE)
    for n in range(6):
        vector_refs[n][...] = sums_ref[n : n + 1, :]
    vector_refs[6][...] = sums_ref[8:10, :][None]
    for n in range(vector_refs[7].shape[1] // width):
        vector_refs[7][:, n * width : (n + 1) * width] = sums_ref[10 + n : 11 + n, :]


VM = pl.BlockSpec(memory_space=pltpu.VMEM)
ANY = pl.BlockSpec(memory_space=pl.ANY)
PAIRS = pltpu.SemaphoreType.DMA((2, 3 * PARTS))
LOCAL = pltpu.SemaphoreType.DMA((4,))


def shape(dims, kind=LOW):
    return jax.ShapeDtypeStruct(dims, kind)


def launch(
    body, number, rows, in_specs, ins, outs, out_specs, scratch, swaps=(), diagonal=False, across=False, late=(),
):
    n_in, n_out, n = len(ins), len(outs), len(swaps)
    held_in = [i for i in range(n_in) if in_specs[i] is VM]
    held_out = [i for i in range(n_out) if out_specs[i] is VM]

    def kernel(*refs):
        refs = list(refs)
        takes, sources = refs[:n_in], refs[n_in : n_in + n]
        gives = refs[n_in + n : n_in + n + n_out]
        lands = refs[n_in + n + n_out : n_in + 2 * n + n_out]
        rest = refs[n_in + 2 * n + n_out :]
        own, rest = rest[: len(scratch)], rest[len(scratch) :]
        in_held, rest = rest[: len(held_in)], rest[len(held_in) :]
        out_held, rest = rest[: len(held_out)], rest[len(held_out) :]
        in_sems, out_sems, swap_sems = rest
        group = Group(rows)
        for k, i in enumerate(held_in):
            group.loads[i] = pltpu.make_async_copy(takes[i], in_held[k], in_sems.at[k])
            group.loads[i].start()
            takes[i] = in_held[k]
        for k, i in enumerate(held_out):
            group.stores[i] = pltpu.make_async_copy(out_held[k], gives[i], out_sems.at[k])
            gives[i] = out_held[k]
        group.greet(n or across, diagonal)
        other = 1 - lax.axis_index("section")
        copies = [
            push(source, land, swap_sems, i, other, "section")
            for i, (source, land) in enumerate(zip(sources, lands))
        ]
        for copy in copies:
            copy.start()
        group.need(*[i for i in held_in if i not in late])
        body(group, *takes, *gives, *own)
        group.emit(*[i for i in held_out if i not in group.begun])
        for copy in copies:
            copy.wait()
        for i in held_out:
            group.stores[i].wait()

    results = pl.pallas_call(
        kernel,
        out_shape=(*outs, *[shape(s.shape, s.dtype) for s in swaps]),
        in_specs=[ANY] * (n_in + n),
        out_specs=(ANY,) * (n_out + n),
        scratch_shapes=[
            *scratch,
            *[pltpu.VMEM(ins[i].shape, ins[i].dtype) for i in held_in],
            *[pltpu.VMEM(outs[i].shape, outs[i].dtype) for i in held_out],
            pltpu.SemaphoreType.DMA((len(held_in),)),
            pltpu.SemaphoreType.DMA((len(held_out),)),
            pltpu.SemaphoreType.DMA((2, max(n, 1))),
        ],
        compiler_params=pltpu.CompilerParams(
            collective_id=number, has_side_effects=True, vmem_limit_bytes=GRANT
        ),
        cost_estimate=pl.CostEstimate(flops=int(3e10), bytes_accessed=30 * MEBI, transcendentals=0),
    )(*ins, *swaps)
    return results[:n_out], results[n_out:]


def start_call(number, tokens, cotangent, small, expand, contract, columns):
    width = tokens.shape[1]
    size = width * columns
    kinds = small.shape[0]
    outs = (shape((LENGTH, size)), shape((LENGTH, size)), shape((2, columns, kinds, width)), shape(expand.shape), shape(contract.shape))
    blocks = pltpu.VMEM((columns, LENGTH, width), LOW)
    vectors = pltpu.VMEM((columns, kinds, width), LOW)
    return pl.pallas_call(
        start_kernel,
        out_shape=outs,
        in_specs=[ANY] * 5,
        out_specs=(VM, VM, VM, ANY, ANY),
        scratch_shapes=[
            blocks, blocks, vectors, vectors, PAIRS, PAIRS,
            pltpu.SemaphoreType.DMA((2, 3 * PARTS + 3)), LOCAL,
        ],
        compiler_params=pltpu.CompilerParams(
            collective_id=number, has_side_effects=True, vmem_limit_bytes=GRANT
        ),
        cost_estimate=pl.CostEstimate(flops=int(3e10), bytes_accessed=30 * MEBI, transcendentals=0),
    )(tokens, cotangent, small, expand, contract)


def attend_call(number, x, pair, vec, bias, rows, width, swaps):
    size = vec.shape[1]
    heads = width // HEAD
    outs = (
        shape((LENGTH, size)),
        shape((3 * heads, LENGTH, HEAD)),
        shape((LENGTH, width)),
        shape((8, LENGTH), WIDE),
        shape((rows, size), WIDE),
        shape((rows, size)),
    )
    scratch = [
        pltpu.VMEM((size, 4 * width), LOW),
        pltpu.VMEM((heads, LENGTH, HEAD), LOW),
        *scatter_scratch(rows, size), LOCAL,
    ]
    return launch(
        functools.partial(attend_kernel, heads),
        number, rows, [VM, ANY, ANY, VM, VM], (x, *pair, vec, bias), outs, (VM,) * 6, scratch, swaps,
    )


def widen_call(number, second, pair, bias, grad, swaps):
    rows, size = second.shape
    wide = bias.shape[1]
    last = grad is not None
    ins, in_specs = [second, *pair, bias], [VM, ANY, ANY, VM]
    outs = [shape((LENGTH, size)), shape((LENGTH, wide)), shape((LENGTH, wide))]
    if last:
        ins, in_specs, outs = ins + [grad], in_specs + [VM], outs + [shape((size, wide))]
    scratch = [pltpu.VMEM((size, wide), LOW), PAIRS, LOCAL]
    return launch(
        functools.partial(widen_kernel, last),
        number, rows, in_specs, ins, outs, (VM,) * len(outs), scratch, swaps, late=(4,),
    )


def contract_call(number, active, hidden, pair, vec, swaps):
    rows, size = hidden.shape
    wide = active.shape[1]
    scratch = [pltpu.VMEM((size, wide), LOW), *scatter_scratch(rows, size), PAIRS, LOCAL]
    return launch(
        contract_kernel, number, rows, [VM, VM, ANY, ANY, VM], (active, hidden, *pair, vec),
        [shape((rows, size)), shape((LENGTH, size))], (VM, VM), scratch, swaps, late=(1,),
    )


def late_expand_call(number, active, hidden, contract, expand, grad, slope, second, vec, swaps):
    rows, size = hidden.shape
    wide = slope.shape[1]
    outs = [
        shape((rows, size), WIDE), shape((rows, size)), shape((8, size), WIDE),
        shape((size, wide)), shape((rows, size)),
    ]
    scratch = [
        pltpu.VMEM((size, wide), LOW),
        pltpu.VMEM((size, wide), LOW),
        pltpu.VMEM((LENGTH, wide), LOW),
        *scatter_scratch(rows, size), *scatter_scratch(rows, size), LOCAL,
    ]
    return launch(
        late_expand_kernel,
        number, rows, [VM, VM, ANY, ANY, ANY, ANY, VM, VM, VM, VM],
        (active, hidden, *contract, *expand, grad, slope, second, vec),
        outs, [VM] * 5, scratch, swaps, late=(1, 6, 7, 8),
    )


def expand_back_call(number, grad, contract, expand, slope, active, second, hidden, vec, swaps):
    rows, size = hidden.shape
    wide = slope.shape[1]
    half = wide // 2
    outs = [
        shape((rows, size), WIDE), shape((rows, size)), shape((8, size), WIDE),
        shape((size, half)), shape((size, half)), shape((LENGTH, size)), shape((size, half)),
    ]
    scratch = [
        pltpu.VMEM((size, wide), LOW),
        pltpu.VMEM((size, wide), LOW),
        pltpu.VMEM((LENGTH, wide), LOW),
        *scatter_scratch(rows, size), PAIRS, LOCAL,
        pltpu.VMEM((2, size, half), LOW), pltpu.VMEM((size, half), LOW),
        pltpu.SemaphoreType.DMA((2, size // TILE)),
    ]
    return launch(
        expand_back_kernel,
        number, rows, [VM, ANY, ANY, ANY, ANY, VM, VM, VM, VM, VM],
        (grad, *contract, *expand, slope, active, second, hidden, vec),
        outs, [VM] * 6 + [ANY], scratch, swaps, False, True, late=(5, 6, 7, 8),
    )


def scores_scratch(size, width, heads):
    return [
        pltpu.VMEM((size, 4 * width), LOW),
        pltpu.VMEM((LENGTH, size), LOW),
        pltpu.VMEM((heads, LENGTH, HEAD), LOW),
        pltpu.VMEM((8, LENGTH), WIDE),
        pltpu.VMEM((heads, LENGTH, HEAD), LOW),
        pltpu.VMEM((heads, LENGTH, HEAD), WIDE),
        pltpu.VMEM((heads, LENGTH, HEAD), WIDE),
    ]


def late_attend_call(number, low, grad, x_own, pair, normed, heads_all, o, lse, vec, result, y, swaps):
    rows, size = grad.shape
    width = o.shape[1]
    heads = width // HEAD
    outs = (shape((rows, size)), shape((8, size), WIDE), shape((2, width, LENGTH)), shape((size, 4 * width)))
    scratch = [
        *scores_scratch(size, width, heads),
        pltpu.VMEM((LENGTH, 3 * width), LOW),
        pltpu.VMEM((size, 4 * width), LOW),
        pltpu.VMEM((size, width), LOW),
        pltpu.VMEM((LENGTH, width), LOW),
        pltpu.VMEM((LENGTH, width), LOW),
        pltpu.VMEM((LENGTH // rows, rows, width), LOW),
        *scatter_scratch(rows, size), PAIRS,
        pltpu.SemaphoreType.DMA((2, 3)), pltpu.SemaphoreType.DMA((2, 2)), LOCAL,
    ]
    return launch(
        functools.partial(late_attend_kernel, heads),
        number, rows, [VM, VM, VM, ANY, ANY, VM, VM, VM, VM, VM, VM, VM],
        (low, grad, x_own, *pair, normed, heads_all, o, lse, vec, result, y),
        outs, (VM, VM, VM, ANY), scratch, swaps, True, True, late=(1, 2, 5, 6, 7, 8, 10, 11),
    )


def scores_back_call(number, low, pair, heads_all, o, lse, keep, send):
    rows, size = low.shape
    width = o.shape[1]
    heads = width // HEAD
    outs = (shape((LENGTH, 3 * width)), shape((size, width)), shape(keep.shape))
    scratch = [
        *scores_scratch(size, width, heads),
        pltpu.VMEM(keep.shape, LOW),
        PAIRS, LOCAL, pltpu.SemaphoreType.DMA((2, 1)),
    ]
    return launch(
        functools.partial(scores_back_kernel, heads),
        number, rows, [VM, ANY, ANY, VM, VM, VM, VM, ANY], (low, *pair, heads_all, o, lse, keep, send),
        outs, (VM, VM, ANY), scratch, (), False, True, late=(3, 4, 5, 6),
    )[0]


def attend_back_call(number, mixed, outer, grad, x_own, pair, normed, vec):
    rows, size = grad.shape
    width = outer.shape[1]
    half = 2 * width
    outs = (shape((size, half)), shape((rows, size)), shape((8, size), WIDE))
    scratch = [
        pltpu.VMEM((size, 4 * width), LOW),
        pltpu.VMEM((2, size, half), LOW),
        pltpu.VMEM((size, half), LOW),
        *scatter_scratch(rows, size), LOCAL, pltpu.SemaphoreType.DMA((2, size // TILE)),
    ]
    return launch(
        attend_back_kernel,
        number, rows, [VM, VM, VM, VM, ANY, ANY, VM, VM],
        (mixed, outer, grad, x_own, *pair, normed, vec), outs, (ANY, VM, VM), scratch, (), False, True,
        late=(1, 2, 3, 6),
    )[0]


def finish_call(number, parts, near, far, sums, row_count):
    rows, size = near.shape
    length, width = far.shape
    columns = length // rows
    outs = (
        shape((2, width, length)),
        shape((16, width), WIDE),
        *[shape(part.shape) for part in parts],
    )
    scratch = [
        pltpu.VMEM(near.shape, LOW),
        pltpu.VMEM(far.shape, LOW),
        *[pltpu.VMEM(s.shape, WIDE) for s in sums],
        pltpu.VMEM((length, width), LOW),
        pltpu.VMEM((columns, rows, width), LOW),
        pltpu.VMEM((columns, 2, 16, width), WIDE),
        pltpu.VMEM((3, 2, 8, width), WIDE),
        pltpu.VMEM((16, width), WIDE),
        pltpu.VMEM((row_count, 16, width), WIDE),
        pltpu.VMEM((width, length), LOW),
        pltpu.SemaphoreType.DMA((2, 3)),
        pltpu.SemaphoreType.DMA((2, 3)),
        pltpu.SemaphoreType.DMA((2, 2)),
        pltpu.SemaphoreType.DMA((2, row_count)),
        pltpu.SemaphoreType.DMA((2, 3)),
        pltpu.SemaphoreType.DMA((6,)),
    ]
    return pl.pallas_call(
        finish_kernel,
        out_shape=outs,
        in_specs=[ANY] * 9,
        out_specs=(VM, VM) + (ANY,) * 3,
        scratch_shapes=scratch,
        compiler_params=pltpu.CompilerParams(
            collective_id=number, has_side_effects=True, vmem_limit_bytes=GRANT
        ),
        cost_estimate=pl.CostEstimate(flops=int(3e10), bytes_accessed=30 * MEBI, transcendentals=0),
    )(*parts, near, far, *sums)


def cross_call(number, up, part):
    return pl.pallas_call(
        functools.partial(cross_kernel, up),
        out_shape=shape(part.shape),
        in_specs=[ANY],
        out_specs=ANY,
        scratch_shapes=[pltpu.SemaphoreType.DMA((2, 1))],
        compiler_params=pltpu.CompilerParams(
            collective_id=number, has_side_effects=True, vmem_limit_bytes=GRANT
        ),
        cost_estimate=pl.CostEstimate(flops=int(1e10), bytes_accessed=10 * MEBI, transcendentals=0),
    )(part)


def write_call(late, far_late, early, far_early, sums, wide):
    rows, size = late[0].shape
    width = sums.shape[1]
    return pl.pallas_call(
        write_kernel,
        out_shape=(
            shape((3, rows, width), WIDE), shape((width, rows), WIDE), shape((rows, size), WIDE), shape((rows, size), WIDE),
            *[shape((1, width), WIDE)] * 6, shape((1, 2, width), WIDE), shape((1, wide), WIDE),
        ),
        in_specs=[ANY] * 12 + [VM],
        out_specs=(VM,) * 12,
        scratch_shapes=[pltpu.VMEM((3, rows, size), LOW)] * 2 + [pltpu.SemaphoreType.DMA((6,))],
        compiler_params=pltpu.CompilerParams(vmem_limit_bytes=GRANT),
    )(*late, *far_late, *early, *far_early, sums)


def swap_sections(value):
    return lax.ppermute(value, "section", [(0, 1), (1, 0)])


def on_device(
    tokens,
    cotangent,
    first_gain,
    first_shift,
    attend_weight,
    attend_bias,
    output_weight,
    output_bias,
    second_gain,
    second_shift,
    expand_weight,
    expand_bias,
    contract_weight,
    contract_bias,
):
    section = lax.axis_index("section")
    column = lax.axis_index("col")
    first_section = section == 0
    columns = lax.axis_size("col")
    width = tokens.shape[1]
    size = width * columns
    rows = LENGTH // columns

    def pick(early, later):
        return jnp.where(first_section, early, later)

    block_rows = attend_weight.shape[1]
    units = (
        jnp.concatenate(
            [attend_weight[0].reshape(block_rows, 3 * width), output_weight[0].T], axis=1
        ),
        expand_weight[0],
        contract_weight[0].T,
    )
    kept_blocks, sent_blocks = [], []
    for unit in units:
        half = unit.shape[1] // 2
        low, high = unit[:, :half], unit[:, half:]
        kept_blocks.append(pick(low, high))
        sent_blocks.append(pick(high, low))

    small = jnp.concatenate(
        [
            first_gain,
            first_shift,
            output_bias,
            second_gain,
            second_shift,
            contract_bias,
            attend_bias[0],
            expand_bias[0].reshape(-1, width),
        ],
        0,
    )
    filled = small.shape[0]
    small = jnp.pad(small, ((0, -filled % 16), (0, 0)))
    got_attend = swap_sections(sent_blocks[0])
    got_attend, sent_expand = lax.optimization_barrier((got_attend, sent_blocks[1]))
    x0_full, gy_full, vectors, got_expand, got_contract = start_call(
        1, tokens, cotangent, small, sent_expand, units[2], columns
    )

    def gather_blocks(block):
        return lax.all_gather(block, "row", axis=0, tiled=True)

    half = units[2].shape[1] // 2
    mats = [[], []]
    for own, got in ((kept_blocks[0], got_attend), (kept_blocks[1], got_expand)):
        for layer, block in enumerate((pick(own, got), pick(got, own))):
            mats[layer].append(gather_blocks(block))
    mats[0].append(gather_blocks(pick(kept_blocks[2], got_contract[:, half:])))
    mats[1].append(gather_blocks(pick(got_contract, units[2])))
    vectors = vectors.astype(WIDE)
    wide_vectors = jnp.swapaxes(vectors[:, :, :6], 1, 2).reshape(2, 6, size)
    wide_vectors = jnp.pad(wide_vectors, ((0, 0), (0, 2), (0, 0)))
    own_vectors = lax.dynamic_index_in_dim(vectors, column, 1, keepdims=False)
    attend_biases = jnp.stack(
        [own_vectors[:, 6], jnp.zeros_like(own_vectors[:, 6]), own_vectors[:, 7]], 1
    ).reshape(2, 1, 3 * width)
    expand_biases = own_vectors[:, 8:filled].reshape(2, 1, -1)

    def own_rows(full):
        return lax.dynamic_slice_in_dim(full, column * rows, rows, 0)

    def own_features(full):
        return lax.dynamic_slice_in_dim(full, column * width, width, 1)

    attn = (mats[0][0], swap_sections(mats[0][0]))
    x = x0_full
    kept, pairs = [], []
    owns = [own_rows(x0_full)]
    for layer in range(2):
        last = layer == 1
        vec = wide_vectors[layer]
        (normed, heads, o, lse, hidden, second_own), (other,) = attend_call(
            2 + 3 * layer, x, attn, vec, attend_biases[layer], rows, width, [mats[layer][1]]
        )
        expand = (mats[layer][1], other)
        outs, others = widen_call(
            3 + 3 * layer, second_own, expand, expand_biases[layer],
            gy_full if last else None, [] if last else [mats[0][2]],
        )
        second, active, slope = outs[:3]
        contract = (mats[layer][2], mats[layer][2] if last else others[0])
        if last:
            c1 = outs[3]
        pairs.append((attn, expand, contract))
        kept.append((normed, heads, o, lse, hidden, second, active, slope))
        if not last:
            (own, x), others = contract_call(4, active, hidden, contract, vec, [mats[1][0]])
            owns.append(own)
            attn = (mats[1][0], others[0])
    y0 = own_features(x)

    def scatter(total):
        return lax.psum_scatter(total, "row", scatter_dimension=0, tiled=True)

    def tie(value, then):
        return lax.optimization_barrier((value, then))

    attn, expand, contract = pairs[1]
    normed, heads, o, lse, hidden, second, active, slope = kept[1]
    (grad_hidden, low, expand_sums1, e1, result), _ = late_expand_call(
        8, active, hidden, contract, expand, gy_full, slope, second, wide_vectors[1], []
    )
    (gx1_own, attend_sums1, layer_outputs, w1), _ = late_attend_call(
        10, low, grad_hidden, owns[1], attn, normed, heads, o, lse, wide_vectors[1], result, y0, []
    )

    attn, expand, contract = pairs[0]
    normed, heads, o, lse, hidden, second, active, slope = kept[0]
    part_c1 = scatter(c1)
    (grad_hidden, low, expand_sums0, ek0, es0, gx1_full, total_c0), (far_c1,) = expand_back_call(
        12, gx1_own, contract, expand, slope, active, second, hidden, wide_vectors[0], [part_c1]
    )
    part_e1, low = tie(scatter(e1), low)
    mixed, outer, total_e0 = scores_back_call(14, low, attn, heads, o, lse, ek0, es0)
    part_w1, mixed = tie(scatter(w1), mixed)
    part_e1, mixed = tie(part_e1, mixed)
    far_e1, mixed = tie(cross_call(18, True, part_e1), mixed)
    part_c0, mixed = tie(scatter(total_c0), mixed)
    total_w0, gx0_own, attend_sums0 = attend_back_call(
        15, mixed, outer, grad_hidden, owns[0], attn, normed, wide_vectors[0]
    )
    part_e0, gx0_own = tie(scatter(total_e0), gx0_own)
    input_grads, small_grads, far_w1, far_c0, far_e0 = finish_call(
        16,
        (part_w1, part_c0, part_e0),
        gx0_own,
        own_features(gx1_full),
        (attend_sums0, expand_sums0, attend_sums1, expand_sums1),
        lax.axis_size("row"),
    )

    part_w0, small_grads = tie(scatter(total_w0), small_grads)
    far_w0 = cross_call(17, False, part_w0)
    attend_part, output_part, expand_part, contract_part, *vector_grads = write_call(
        (part_w1, part_e1, part_c1),
        (far_w1, far_e1, far_c1),
        (part_w0, part_e0, part_c0),
        (far_w0, far_e0, far_c0),
        small_grads,
        expand_bias.shape[1],
    )
    return (
        jnp.concatenate([layer_outputs[0], layer_outputs[1]], 1).T[None],
        jnp.concatenate([input_grads[0], input_grads[1]], 1).astype(WIDE).T[None],
        vector_grads[0],
        vector_grads[1],
        jnp.swapaxes(attend_part, 0, 1)[None],
        vector_grads[6],
        output_part[None],
        vector_grads[2],
        vector_grads[3],
        vector_grads[4],
        expand_part[None],
        vector_grads[7],
        contract_part.T[None],
        vector_grads[5],
    )


def solution(mesh):
    return jax.shard_map(
        on_device,
        mesh=mesh,
        in_specs=(
            P("row", "col"),
            P("row", "col"),
            P("section", "col"),
            P("section", "col"),
            P("section", "row", None, "col"),
            P("section", None, "col"),
            P("section", "col", "row"),
            P("section", "col"),
            P("section", "col"),
            P("section", "col"),
            P("section", "row", "col"),
            P("section", "col"),
            P("section", "col", "row"),
            P("section", "col"),
        ),
        out_specs=(
            P("section", "row", "col"),
            P("section", "row", "col"),
            P("section", "col"),
            P("section", "col"),
            P("section", "row", None, "col"),
            P("section", None, "col"),
            P("section", "col", "row"),
            P("section", "col"),
            P("section", "col"),
            P("section", "col"),
            P("section", "row", "col"),
            P("section", "col"),
            P("section", "col", "row"),
            P("section", "col"),
        ),
        check_vma=False,
    )
```

```python
import functools

import jax
import jax.numpy as jnp
from jax import lax
from jax.experimental import pallas as pl
from jax.experimental.pallas import tpu as pltpu
from jax.sharding import PartitionSpec as P

HEAD = 64
LENGTH = 1024
EPS = 1e-05
LOW = jnp.bfloat16
WIDE = jnp.float32
MESH = pl.DeviceIdType.MESH
PARTS = 2
TILE = 256
MEBI = 1024 * 1024
GRANT = 58 * MEBI


def nn(left, right):
    return lax.dot_general(left, right, (((1,), (0,)), ((), ())), preferred_element_type=WIDE)


def nt(left, right):
    return lax.dot_general(left, right, (((1,), (1,)), ((), ())), preferred_element_type=WIDE)


def tn(left, right):
    return lax.dot_general(left, right, (((0,), (0,)), ((), ())), preferred_element_type=WIDE)


def turned(values):
    width = values.shape[1]
    unit = (
        lax.broadcasted_iota(jnp.int32, (width, width), 0) == lax.broadcasted_iota(jnp.int32, (width, width), 1)
    ).astype(LOW)
    return nt(unit, values)


def turned_back(values):
    height = values.shape[0]
    unit = (
        lax.broadcasted_iota(jnp.int32, (height, height), 0) == lax.broadcasted_iota(jnp.int32, (height, height), 1)
    ).astype(LOW)
    return tn(values, unit)


def normalise(values):
    center = jnp.mean(values, axis=1, keepdims=True)
    centred = values - center
    scale = lax.rsqrt(jnp.mean(centred * centred, axis=1, keepdims=True) + EPS)
    return centred * scale, scale


def norm_backward(grad, hat, scale, gain):
    scaled = grad * gain
    mean_one = jnp.mean(scaled, axis=1, keepdims=True)
    mean_two = jnp.mean(scaled * hat, axis=1, keepdims=True)
    return scale * (scaled - mean_one - hat * mean_two)


class Group:
    def __init__(self, rows):
        self.me = lax.axis_index("col")
        chip, core = self.me // 2, self.me % 2
        self.sib = chip * 2 + 1 - core
        self.peer = (1 - chip) * 2 + core
        self.diag = (1 - chip) * 2 + 1 - core
        self.rows = rows
        self.part = rows // PARTS
        self.loads, self.stores, self.begun = {}, {}, set()

    def need(self, *places):
        for place in places:
            self.loads[place].wait()

    def emit(self, *places):
        for place in places:
            self.stores[place].start()
            self.begun.add(place)

    def greet(self, swaps, diagonal, rows=()):
        barrier = pltpu.get_barrier_semaphore()
        others = [{"col": self.sib}, {"col": self.peer}]
        if diagonal:
            others.append({"col": self.diag})
        if swaps:
            others.append({"section": 1 - lax.axis_index("section")})
        others += [{"row": row} for row in rows]
        for other in others:
            pl.semaphore_signal(barrier, inc=1, device_id=other, device_id_type=MESH)
        pl.semaphore_wait(barrier, len(others))

    def slab(self, owner, j):
        return pl.ds(pl.multiple_of(owner * self.rows + j * self.part, self.part), self.part)

    def chunk(self, owner):
        return pl.ds(pl.multiple_of(owner * self.rows, self.rows), self.rows)


def push(src, dst, sems, slot, target, axis="col"):
    return pltpu.make_async_remote_copy(
        src_ref=src,
        dst_ref=dst,
        send_sem=sems.at[0, slot],
        recv_sem=sems.at[1, slot],
        device_id={axis: target},
        device_id_type=MESH,
    )


class Gather:
    def __init__(self, group, full, sems, blocks=False):
        self.group, self.full, self.sems, self.blocks = group, full, sems, blocks
        self.over, self.near, self.relayed = [], [], []

    def piece(self, owner, j):
        if not self.blocks:
            return self.full.at[self.group.slab(owner, j)]
        part = self.full.shape[1] // PARTS
        return self.full.at[owner, pl.ds(j * part, part)]

    def start_part(self, j):
        g = self.group
        piece = self.piece(g.me, j)
        self.over.append(push(piece, piece, self.sems, j, g.peer))
        self.near.append(push(piece, piece, self.sems, PARTS + j, g.sib))
        self.over[-1].start()
        self.near[-1].start()

    def start(self):
        for j in range(PARTS):
            self.start_part(j)

    def sibling(self):
        for copy in self.near:
            copy.wait_recv()

    def relay(self):
        g = self.group
        for j in range(PARTS):
            self.over[j].wait_recv()
            piece = self.piece(g.peer, j)
            self.relayed.append(push(piece, piece, self.sems, 2 * PARTS + j, g.sib))
            self.relayed[-1].start()

    def diagonal(self):
        for copy in self.relayed:
            copy.wait_recv()

    def done(self):
        for copy in self.over + self.near + self.relayed:
            copy.wait_send()

    def each(self, body, first=None):
        g = self.group
        if not self.over:
            self.start()
        if first is not None:
            first()
        body(g.me)
        self.sibling()
        body(g.sib)
        self.relay()
        body(g.peer)
        self.diagonal()
        body(g.diag)
        self.done()


class Scatter:
    def __init__(self, group, stage, land, total, sems):
        self.group, self.stage, self.land, self.total, self.sems = group, stage, land, total, sems

    def start(self, part):
        g, stage, land = self.group, self.stage, self.land
        self.first, self.over, self.near = [], [], []
        def split(owner):
            whole = part(owner)
            return [whole[j * g.part : (j + 1) * g.part] for j in range(PARTS)]

        for j, mine in enumerate(split(g.diag)):
            stage[0, j] = mine.astype(LOW)
            self.first.append(push(stage.at[0, j], land.at[0, j], self.sems, j, g.sib))
            self.first[-1].start()
        for j, mine in enumerate(split(g.peer)):
            self.first[j].wait_recv()
            stage[1, j] = (mine + land[0, j].astype(WIDE)).astype(LOW)
            self.over.append(push(stage.at[1, j], land.at[1, j], self.sems, PARTS + j, g.peer))
            self.over[-1].start()
        for j, mine in enumerate(split(g.sib)):
            stage[2, j] = mine.astype(LOW)
            self.near.append(push(stage.at[2, j], land.at[2, j], self.sems, 2 * PARTS + j, g.sib))
            self.near[-1].start()
        for j, mine in enumerate(split(g.me)):
            self.total[j] = mine

    def take(self, j):
        self.near[j].wait_recv()
        self.over[j].wait_recv()
        land = self.land
        return self.total[j] + (land[1, j].astype(WIDE) + land[2, j].astype(WIDE))

    def done(self):
        for copy in self.first + self.over + self.near:
            copy.wait_send()


class Deliver:
    def __init__(self, group, stage, out, sems):
        self.group, self.stage, self.out, self.sems = group, stage, out, sems

    def start(self, rows_ref):
        g, width = self.group, self.out.shape[1]
        for c in range(self.stage.shape[0]):
            self.stage[c] = rows_ref[:, c * width : (c + 1) * width]
        place = self.out.at[g.chunk(g.me)]
        self.copies = [
            push(self.stage.at[other], place, self.sems, n, other)
            for n, other in enumerate((g.peer, g.diag, g.sib))
        ]
        for copy in self.copies:
            copy.start()
        self.out[g.chunk(g.me), :] = self.stage[g.me]

    def done(self):
        for copy in self.copies:
            copy.wait()


class OneWay:
    def __init__(self, up, down, sems):
        self.section = lax.axis_index("section")
        both = [*up, *down]
        copies = [
            push(source, into, sems, n, 1 - self.section, "section")
            for n, (source, into) in enumerate(both)
        ]
        self.up, self.down = copies[: len(up)], copies[len(up) :]

    def each(self, first, second):
        @pl.when(self.section == 0)
        def _():
            first(self.up)
            second(self.down)

        @pl.when(self.section == 1)
        def _():
            first(self.down)
            second(self.up)

    def start(self):
        self.each(lambda copies: [copy.start() for copy in copies], lambda copies: None)

    def wait(self):
        self.each(
            lambda copies: [copy.wait_send() for copy in copies],
            lambda copies: [copy.wait_recv() for copy in copies],
        )


def scatter_scratch(rows, width):
    part = rows // PARTS
    return [
        pltpu.VMEM((3, PARTS, part, width), LOW),
        pltpu.VMEM((3, PARTS, part, width), LOW),
        pltpu.VMEM((PARTS, part, width), WIDE),
        pltpu.SemaphoreType.DMA((2, 3 * PARTS)),
    ]


class Halves:
    def __init__(self, pair, whole, sems, slot):
        if pair[0].shape[1] == whole.shape[1]:
            self.copies = [pltpu.make_async_copy(pair[0], whole, sems.at[slot])]
            return
        section = lax.axis_index("section")
        half = whole.shape[1] // 2
        self.copies = []
        for n, place in enumerate((section, 1 - section)):
            columns = pl.ds(pl.multiple_of(place * half, half), half)
            self.copies.append(
                pltpu.make_async_copy(pair[n], whole.at[:, columns], sems.at[slot + n])
            )

    def start(self):
        for copy in self.copies:
            copy.start()

    def wait(self):
        for copy in self.copies:
            copy.wait()


class Trade:
    def __init__(self, keep, send, got, sems):
        self.keep, self.send, self.got, self.sems = keep, send, got, sems
        self.tiles = keep.shape[0] // TILE

    def copy(self, n):
        rows = pl.ds(pl.multiple_of(n * TILE, TILE), TILE)
        return push(
            self.send.at[rows], self.got.at[rows], self.sems, n, 1 - lax.axis_index("section"), "section"
        )

    def start(self, make):
        @pl.loop(0, self.tiles)
        def _(n):
            make(pl.ds(pl.multiple_of(n * TILE, TILE), TILE))
            self.copy(n).start()

    def finish(self):
        @pl.loop(0, self.tiles)
        def _(n):
            self.copy(n).wait()

        add_into(self.keep, self.got)


def add_into(keep_ref, got_ref):
    @pl.loop(0, keep_ref.shape[0] // TILE)
    def _(n):
        rows = pl.ds(pl.multiple_of(n * TILE, TILE), TILE)
        keep_ref[rows, :] = (keep_ref[rows, :].astype(WIDE) + got_ref[rows, :].astype(WIDE)).astype(LOW)


def causal_scores(scores):
    size = scores.shape[1]
    keep = lax.broadcasted_iota(jnp.int32, (size, size), 0) <= lax.broadcasted_iota(
        jnp.int32, (size, size), 1
    )
    begin = scores.shape[0] - size
    last = jnp.where(keep, scores[begin:], -1000000000.0)
    return last if begin == 0 else jnp.concatenate([scores[:begin], last], 0)


def attention_out(owner, size, heads_ref, o3, lse_ref, heads):
    for i in range(heads_ref.shape[1] // size):
        rows, finish = slice(i * size, (i + 1) * size), (i + 1) * size

        @pl.when(owner == i)
        def _():
            @pl.loop(0, heads)
            def _(h):
                scores = causal_scores(nt(heads_ref[heads + h, :finish, :], heads_ref[h, rows, :]))
                highest = jnp.max(scores, axis=0, keepdims=True)
                powers = jnp.exp(scores - highest)
                summed = jnp.sum(powers, axis=0, keepdims=True)
                mixed = tn(heads_ref[2 * heads + h, :finish, :], powers.astype(LOW))
                o3[h, rows, :] = (mixed / summed).T.astype(LOW)
                lse_ref[pl.ds(h, 1), rows] = highest + jnp.log(summed)


def attention_back(owner, size, heads_ref, go3, lse_ref, dots_ref, g3, key_acc, value_acc, heads):
    for i in range(heads_ref.shape[1] // size):
        rows, finish = slice(i * size, (i + 1) * size), (i + 1) * size

        @pl.when(owner == i)
        def _():
            @pl.loop(0, heads)
            def _(h):
                queries = heads_ref[h, rows, :]
                keys = heads_ref[heads + h, :finish, :]
                grads = go3[h, rows, :]
                probs = jnp.exp(causal_scores(nt(keys, queries) - lse_ref[pl.ds(h, 1), rows]))
                grad_probs = nt(heads_ref[2 * heads + h, :finish, :], grads)
                grad_scores = (probs * (grad_probs - dots_ref[pl.ds(h, 1), rows])).astype(LOW)
                g3[h, rows, :] = (tn(grad_scores, keys) * HEAD ** (-0.5)).astype(LOW)
                key_acc[h, :finish, :] += nn(grad_scores, queries)
                value_acc[h, :finish, :] += nn(probs.astype(LOW), grads)


def start_kernel(
    tokens_ref, cotangent_ref, small_ref, contract_ref,
    x_ref, g_ref, vectors_ref, got_contract_ref,
    x4, g4, s4, other4, x_sems, g_sems, s_sems, local_sems,
):
    section = lax.axis_index("section")
    group = Group(x_ref.shape[0] // 4)
    length = x_ref.shape[0]
    loads = []
    rows = pl.ds(pl.multiple_of(section * length, length), length)
    sources = ((tokens_ref.at[:, rows], x4), (cotangent_ref.at[:, rows], g4), (small_ref, s4))
    for n, (source, into) in enumerate(sources):
        loads.append(pltpu.make_async_copy(source, into.at[group.me], local_sems.at[n]))
        loads[-1].start()
    group.greet(True, False)
    blocks = push(contract_ref, got_contract_ref, s_sems, 3 * PARTS + 1, 1 - section, "section")
    gathers = [Gather(group, s4, s_sems, True), Gather(group, x4, x_sems, True), Gather(group, g4, g_sems, True)]
    for gather, load in zip(gathers, (loads[2], loads[0], loads[1])):
        load.wait()
        gather.start()
    width = x4.shape[1]
    for gather, blocks4, full_ref in ((gathers[0], None, None), (gathers[1], x4, x_ref), (gathers[2], g4, g_ref)):
        gather.sibling()
        gather.relay()
        gather.diagonal()
        if blocks4 is None:
            swap = push(s4, other4, s_sems, 3 * PARTS, 1 - section, "section")
            swap.start()
            blocks.start()
        else:
            for c in range(blocks4.shape[0]):
                full_ref[:, c * width : (c + 1) * width] = turned_back(blocks4[c]).astype(LOW)
    swap.wait()
    blocks.wait()
    vectors_ref[section] = s4[...]
    vectors_ref[1 - section] = other4[...]
    for gather in gathers:
        gather.done()


def attend_kernel(
    heads, group, x_ref, mine_ref, other_ref, vec_ref, bias_ref,
    normed_ref, heads_ref, o_ref, lse_ref, hidden_ref, second_ref,
    weight, o3, stage, land, total, scatter_sems, local_sems,
):
    width = o_ref.shape[1]
    halves = Halves((mine_ref, other_ref), weight, local_sems, 0)
    halves.start()
    lse_ref[...] = jnp.zeros_like(lse_ref)
    halves.wait()

    @pl.loop(0, LENGTH // group.rows)
    def _(owner):
        rows = group.chunk(owner)
        hat, _ = normalise(x_ref[rows, :].astype(WIDE))
        normed = (hat * vec_ref[0:1, :] + vec_ref[1:2, :]).astype(LOW)
        normed_ref[rows, :] = normed
        mixed = nn(normed, weight[:, : 3 * width]) + bias_ref[...]
        for j in range(3 * heads):
            piece = mixed[:, j * HEAD : (j + 1) * HEAD]
            if j < heads:
                piece = piece * HEAD ** (-0.5)
            heads_ref[j, rows, :] = piece.astype(LOW)

    group.emit(0, 1)

    def attend(owner):
        rows = group.chunk(owner)
        attention_out(owner, group.rows, heads_ref, o3, lse_ref, heads)
        for h in range(heads):
            o_ref[rows, h * HEAD : (h + 1) * HEAD] = o3[h, rows, :]
        return nt(o_ref[rows, :], weight[:, 3 * width :])

    scatter = Scatter(group, stage, land, total, scatter_sems)
    scatter.start(attend)
    group.emit(2, 3)
    for j in range(PARTS):
        rows = slice(j * group.part, (j + 1) * group.part)
        residual = x_ref[group.slab(group.me, j), :].astype(WIDE)
        hidden = residual + scatter.take(j) + vec_ref[2:3, :]
        hidden_ref[rows, :] = hidden
        hat, _ = normalise(hidden)
        second_ref[rows, :] = (hat * vec_ref[3:4, :] + vec_ref[4:5, :]).astype(LOW)
    scatter.done()


def outer_whole(left_ref, right_ref, out_ref):
    @pl.loop(0, left_ref.shape[1] // TILE)
    def _(n):
        rows = pl.ds(pl.multiple_of(n * TILE, TILE), TILE)
        out_ref[rows, :] = tn(left_ref[:, rows], right_ref[...]).astype(LOW)


def widen_kernel(last, group, second_ref, em_ref, eo_ref, bias_ref, *refs):
    if last:
        g_ref, *refs = refs
    full_ref, active_ref, slope_ref, *refs = refs
    if last:
        c_ref, *refs = refs
    expand, gather_sems, local_sems = refs
    halves = Halves((em_ref, eo_ref), expand, local_sems, 0)
    halves.start()
    full_ref[group.chunk(group.me), :] = second_ref[...]
    halves.wait()

    def widen(owner):
        rows = group.chunk(owner)
        t = nn(full_ref[rows, :], expand[...]) + bias_ref[...]
        square = t * t
        bent = jnp.tanh(0.7978845608028654 * t * (1.0 + 0.044715 * square))
        active_ref[rows, :] = (0.5 * t * (1.0 + bent)).astype(LOW)
        slope_ref[rows, :] = (
            0.5 * (1.0 + bent)
            + (0.5 * 0.7978845608028654) * t * (1.0 - bent * bent) * (1.0 + 3 * 0.044715 * square)
        ).astype(LOW)

    Gather(group, full_ref, gather_sems).each(widen)
    if last:
        group.emit(0, 1, 2)
        group.need(4)
        outer_whole(g_ref, active_ref, c_ref)


def outer_halves(left_ref, right_ref, keep_ref, send_ref):
    section = lax.axis_index("section")
    half = right_ref.shape[1] // 2
    for place, out in ((section, keep_ref), (1 - section, send_ref)):
        columns = pl.ds(pl.multiple_of(place * half, half), half)

        @pl.loop(0, left_ref.shape[1] // TILE)
        def _(n):
            rows = pl.ds(pl.multiple_of(n * TILE, TILE), TILE)
            out[rows, :] = tn(left_ref[:, rows], right_ref[:, columns]).astype(LOW)


def contract_kernel(
    group, active_ref, hidden_ref, cm_ref, co_ref, vec_ref, result_ref, full_ref,
    contract, stage, land, total, scatter_sems, gather_sems, local_sems,
):
    halves = Halves((cm_ref, co_ref), contract, local_sems, 0)
    halves.start()
    halves.wait()
    scatter = Scatter(group, stage, land, total, scatter_sems)
    scatter.start(lambda owner: nt(active_ref[group.chunk(owner), :], contract[...]))
    group.need(1)
    gather = Gather(group, full_ref, gather_sems)
    for j in range(PARTS):
        rows = slice(j * group.part, (j + 1) * group.part)
        result = (hidden_ref[rows, :] + scatter.take(j) + vec_ref[5:6, :]).astype(LOW)
        result_ref[rows, :] = result
        full_ref[group.slab(group.me, j), :] = result
        gather.start_part(j)
    gather.each(lambda owner: None)
    scatter.done()


def narrow_grads(group, scatter, full_ref, hidden_ref, vec_ref, grad_ref, low_ref, sums_ref):
    for j in range(PARTS):
        rows = slice(j * group.part, (j + 1) * group.part)
        grad = scatter.take(j)
        hat, scale = normalise(hidden_ref[rows, :])
        own = full_ref[group.slab(group.me, j), :].astype(WIDE)
        out = own + norm_backward(grad, hat, scale, vec_ref[3:4, :])
        grad_ref[rows, :] = out
        low_ref[rows, :] = out.astype(LOW)
        for n, term in enumerate((grad * hat, grad, own, out)):
            sums_ref[n : n + 1, :] += jnp.sum(term, axis=0, keepdims=True)


def bend(rows, full_ref, contract, slope_ref, before, sums_ref):
    grad = (nn(full_ref[rows, :], contract[...]) * slope_ref[rows, :].astype(WIDE)).astype(LOW)
    before[rows, :] = grad
    sums_ref[4:5, :] += jnp.sum(grad.astype(WIDE), axis=0, keepdims=True)


def late_expand_kernel(
    group, active_ref, hidden_ref, cm_ref, co_ref, em_ref, eo_ref, g_ref, slope_ref, second_ref, vec_ref,
    grad_ref, low_ref, sums_ref, e_ref, result,
    contract, expand, before,
    stage_a, land_a, total_a, sems_a, stage, land, total, scatter_sems, local_sems,
):
    first = Halves((cm_ref, co_ref), contract, local_sems, 0)
    then = Halves((em_ref, eo_ref), expand, local_sems, 2)
    first.start()
    then.start()
    sums_ref[...] = jnp.zeros_like(sums_ref)
    first.wait()
    forward = Scatter(group, stage_a, land_a, total_a, sems_a)
    forward.start(lambda owner: nt(active_ref[group.chunk(owner), :], contract[...]))
    group.need(6, 7)

    @pl.loop(0, LENGTH // group.rows)
    def _(n):
        bend(group.chunk(n), g_ref, contract, slope_ref, before, sums_ref)

    then.wait()
    scatter = Scatter(group, stage, land, total, scatter_sems)
    scatter.start(lambda owner: nt(before[group.chunk(owner), :], expand[...]))
    group.need(1)
    for j in range(PARTS):
        rows = slice(j * group.part, (j + 1) * group.part)
        result[rows, :] = (hidden_ref[rows, :] + forward.take(j) + vec_ref[5:6, :]).astype(LOW)
    group.emit(4)
    group.need(8)
    outer_whole(second_ref, before, e_ref)
    group.emit(3)
    narrow_grads(group, scatter, g_ref, hidden_ref, vec_ref, grad_ref, low_ref, sums_ref)
    group.emit(0, 1, 2)
    forward.done()
    scatter.done()


def expand_back_kernel(
    group, g_ref, cm_ref, co_ref, em_ref, eo_ref, slope_ref, active_ref, second_ref, hidden_ref, vec_ref,
    grad_ref, low_ref, sums_ref, ek_ref, es_ref, full_ref, c_ref,
    contract, expand, before, stage, land, total, scatter_sems, gather_sems, local_sems, outer, got, trade_sems,
):
    section = lax.axis_index("section")
    first = Halves((cm_ref, co_ref), contract, local_sems, 0)
    then = Halves((em_ref, eo_ref), expand, local_sems, 2)
    first.start()
    then.start()
    sums_ref[...] = jnp.zeros_like(sums_ref)
    full_ref[group.chunk(group.me), :] = g_ref[...]
    first.wait()
    Gather(group, full_ref, gather_sems).each(
        lambda owner: bend(group.chunk(owner), full_ref, contract, slope_ref, before, sums_ref),
        lambda: group.need(5),
    )
    group.emit(5)
    group.need(6)
    half = active_ref.shape[1] // 2

    def columns(place):
        return pl.ds(pl.multiple_of(place * half, half), half)

    def make(n):
        def tile(rows):
            place = section if n == 0 else 1 - section
            outer[n, rows, :] = tn(full_ref[:, rows], active_ref[:, columns(place)]).astype(LOW)

        return tile

    trade = Trade(outer.at[0], outer.at[1], got, trade_sems)
    trade.start(make(1))
    then.wait()
    scatter = Scatter(group, stage, land, total, scatter_sems)
    scatter.start(lambda owner: nt(before[group.chunk(owner), :], expand[...]))
    group.need(7)
    outer_halves(second_ref, before, ek_ref, es_ref)
    group.emit(3, 4)
    keep = make(0)

    @pl.loop(0, outer.shape[1] // TILE)
    def _(n):
        keep(pl.ds(pl.multiple_of(n * TILE, TILE), TILE))

    group.need(8)
    narrow_grads(group, scatter, full_ref, hidden_ref, vec_ref, grad_ref, low_ref, sums_ref)
    group.emit(0, 1, 2)
    scatter.done()
    trade.finish()
    store = pltpu.make_async_copy(outer.at[0], c_ref, local_sems.at[0])
    store.start()
    store.wait()


def scores_back(group, heads, low_ref, weight, heads_ref, o_ref, lse_ref, full, go3, dots, g3, accs, mixed, gather_sems, first):
    width = o_ref.shape[1]
    picks = (
        lax.broadcasted_iota(jnp.int32, (8, width), 1) // HEAD
        == lax.broadcasted_iota(jnp.int32, (8, width), 0)
    ).astype(WIDE)
    for acc in accs:
        acc[...] = jnp.zeros_like(acc)

    def spread(owner):
        rows = group.chunk(owner)
        grads = nn(full[rows, :], weight[:, 3 * width :]).astype(LOW)
        for h in range(heads):
            go3[h, rows, :] = grads[:, h * HEAD : (h + 1) * HEAD]
        term = grads.astype(WIDE) * o_ref[rows, :].astype(WIDE)
        dots[:, rows] = lax.dot_general(
            picks,
            term,
            (((1,), (1,)), ((), ())),
            precision=lax.Precision.HIGHEST,
            preferred_element_type=WIDE,
        )
        attention_back(owner, group.rows, heads_ref, go3, lse_ref, dots, g3, *accs, heads)

    full[group.chunk(group.me), :] = low_ref[...]
    Gather(group, full, gather_sems).each(spread, first)
    for j in range(3 * heads):
        source = g3[j] if j < heads else accs[j // heads - 1][j % heads].astype(LOW)
        mixed[:, j * HEAD : (j + 1) * HEAD] = source


def outer_out(full, o_ref, outer_ref):
    @pl.loop(0, outer_ref.shape[0] // TILE)
    def _(n):
        rows = pl.ds(pl.multiple_of(n * TILE, TILE), TILE)
        outer_ref[rows, :] = tn(full[:, rows], o_ref[...]).astype(LOW)


def attend_grads(group, scatter, x_ref, grad_ref, vec_ref, mixed, width, out_ref, sums_ref):
    sums_ref[2:3, : 3 * width] = jnp.sum(mixed[...].astype(WIDE), axis=0, keepdims=True)
    for j in range(PARTS):
        rows = slice(j * group.part, (j + 1) * group.part)
        grad = scatter.take(j)
        hat, scale = normalise(x_ref[rows, :].astype(WIDE))
        out = grad_ref[rows, :] + norm_backward(grad, hat, scale, vec_ref[0:1, :])
        out_ref[rows, :] = out.astype(LOW)
        for n, term in enumerate((grad * hat, grad)):
            sums_ref[n : n + 1, :] += jnp.sum(term, axis=0, keepdims=True)


def late_attend_kernel(
    heads, group, low_ref, grad_ref, x_ref, mine_ref, other_ref, normed_ref, heads_ref, o_ref, lse_ref, vec_ref,
    result_ref, y_ref,
    out_ref, sums_ref, results_ref, w_ref,
    weight, full, go3, dots, g3, key_acc, value_acc, mixed, outer, outer_o, late, y_land, stage4,
    stage, land, total, scatter_sems, gather_sems, deliver_sems, y_sems, local_sems,
):
    width = o_ref.shape[1]
    section = lax.axis_index("section")
    halves = Halves((mine_ref, other_ref), weight, local_sems, 0)
    halves.start()
    sums_ref[...] = jnp.zeros_like(sums_ref)
    halves.wait()
    deliver = Deliver(group, stage4, late, deliver_sems)

    def first():
        group.need(6, 7, 8, 10)
        deliver.start(result_ref)

    scores_back(
        group, heads, low_ref, weight, heads_ref, o_ref, lse_ref, full, go3, dots, g3,
        (key_acc, value_acc), mixed, gather_sems, first,
    )
    deliver.done()
    group.need(11)
    results = OneWay([(late, y_land)], [(y_ref, y_land)], y_sems)
    results.start()
    scatter = Scatter(group, stage, land, total, scatter_sems)
    scatter.start(lambda owner: nt(mixed[group.chunk(owner), :], weight[:, : 3 * width]))
    outer_out(full, o_ref, outer_o)
    group.need(5)

    @pl.loop(0, weight.shape[0] // TILE)
    def _(n):
        rows = pl.ds(pl.multiple_of(n * TILE, TILE), TILE)
        outer[rows, : 3 * width] = tn(normed_ref[:, rows], mixed[...]).astype(LOW)
        outer[rows, 3 * width :] = outer_o[rows, :]

    store = pltpu.make_async_copy(outer, w_ref, local_sems.at[2])
    store.start()
    @pl.when(section == 0)
    def _():
        results_ref[section] = turned(y_ref[...]).astype(LOW)

    @pl.when(section == 1)
    def _():
        results_ref[section] = turned(late[...]).astype(LOW)

    group.need(1, 2)
    attend_grads(group, scatter, x_ref, grad_ref, vec_ref, mixed, width, out_ref, sums_ref)
    results.wait()
    results_ref[1 - section] = turned(y_land[...]).astype(LOW)
    scatter.done()
    store.wait()


def scores_back_kernel(
    heads, group, low_ref, mine_ref, other_ref, heads_ref, o_ref, lse_ref, ek_ref, es_ref,
    mixed, outer_ref, e_ref,
    weight, full, go3, dots, g3, key_acc, value_acc, got, gather_sems, local_sems, swap_sems,
):
    swap = push(es_ref, got, swap_sems, 0, 1 - lax.axis_index("section"), "section")
    swap.start()
    halves = Halves((mine_ref, other_ref), weight, local_sems, 0)
    halves.start()
    halves.wait()
    scores_back(
        group, heads, low_ref, weight, heads_ref, o_ref, lse_ref, full, go3, dots, g3,
        (key_acc, value_acc), mixed, gather_sems, lambda: group.need(3, 4, 5),
    )
    group.emit(0)
    outer_out(full, o_ref, outer_ref)
    group.emit(1)
    group.need(6)
    swap.wait()
    add_into(ek_ref, got)
    store = pltpu.make_async_copy(ek_ref, e_ref, local_sems.at[0])
    store.start()
    store.wait()


def attend_back_kernel(
    group, mixed, outer_ref, grad_ref, x_ref, mine_ref, other_ref, normed_ref, vec_ref,
    w_ref, out_ref, sums_ref,
    weight, outer, got, stage, land, total, scatter_sems, local_sems, swap_sems,
):
    width = outer_ref.shape[1]
    section = lax.axis_index("section")
    halves = Halves((mine_ref, other_ref), weight, local_sems, 0)
    halves.start()
    sums_ref[...] = jnp.zeros_like(sums_ref)
    half = weight.shape[1] // 2
    scatter = Scatter(group, stage, land, total, scatter_sems)
    group.need(1, 6)

    def make(n):
        place = section if n == 0 else 1 - section

        def tile(rows):
            @pl.when(place == 0)
            def _():
                outer[n, rows, :] = tn(normed_ref[:, rows], mixed[:, :half]).astype(LOW)

            @pl.when(place == 1)
            def _():
                outer[n, rows, : 3 * width - half] = tn(normed_ref[:, rows], mixed[:, half:]).astype(LOW)
                outer[n, rows, 3 * width - half :] = outer_ref[rows, :]

        return tile

    trade = Trade(outer.at[0], outer.at[1], got, swap_sems)
    trade.start(make(1))
    halves.wait()
    scatter.start(lambda owner: nt(mixed[group.chunk(owner), :], weight[:, : 3 * width]))
    keep = make(0)

    @pl.loop(0, outer.shape[1] // TILE)
    def _(n):
        keep(pl.ds(pl.multiple_of(n * TILE, TILE), TILE))

    group.need(2, 3)
    attend_grads(group, scatter, x_ref, grad_ref, vec_ref, mixed, width, out_ref, sums_ref)
    group.emit(1, 2)
    scatter.done()
    trade.finish()
    store = pltpu.make_async_copy(outer.at[0], w_ref, local_sems.at[2])
    store.start()
    store.wait()


def finish_kernel(
    late_ref, early1_ref, early2_ref, near_hbm, far_hbm, a0_hbm, n0_hbm, a1_hbm, n1_hbm,
    grads_ref, sums_ref, got_late, got_early1, got_early2,
    near_ref, far_ref, a0, n0, a1, n1, mine, stage4, block, land_col, land_x, land_z, send,
    deliver_sems, col_sems, x_sems, z_sems, part_sems, local_sems,
):
    section, row = lax.axis_index("section"), lax.axis_index("row")
    away = 1 - section
    group = Group(near_ref.shape[0])
    width = far_ref.shape[1]
    others = [lax.rem(row + d, land_z.shape[0]) for d in range(1, land_z.shape[0])]
    loads = [
        pltpu.make_async_copy(source, into, local_sems.at[n])
        for n, (source, into) in enumerate(
            (
                (near_hbm, near_ref), (far_hbm, far_ref),
                (a0_hbm, a0), (n0_hbm, n0), (a1_hbm, a1), (n1_hbm, n1),
            )
        )
    ]
    for copy in loads:
        copy.start()
    group.greet(True, True, others)
    parts = OneWay(
        [(late_ref, got_late)], [(early1_ref, got_early1), (early2_ref, got_early2)], part_sems
    )
    parts.start()
    for copy in loads:
        copy.wait()
    deliver = Deliver(group, stage4, mine, deliver_sems)
    deliver.start(near_ref)
    gradients = push(send, grads_ref.at[section], x_sems, 1, away, "section")

    @pl.when(section == 0)
    def _():
        send[...] = turned(far_ref[...]).astype(LOW)
        gradients.start()

    block[...] = jnp.zeros_like(block)
    for layer, (attn, narrow) in enumerate(((a0, n0), (a1, n1))):
        wide = [attn[0:1, :], attn[1:2, :], narrow[3:4, :], narrow[0:1, :], narrow[1:2, :], narrow[2:3, :]]
        for c in range(block.shape[0]):
            columns = slice(c * width, (c + 1) * width)
            for n, term in enumerate(wide):
                block[c, layer, n : n + 1, :] = term[:, columns]
            for n, term in enumerate((attn[2:3, :width], attn[2:3, 2 * width : 3 * width])):
                block[c, layer, 8 + n : 9 + n, :] = term
            for n in range(narrow.shape[1] // width):
                block[c, layer, 10 + n : 11 + n, :] = narrow[4:5, n * width : (n + 1) * width]
    copies = [
        push(block.at[other, :, pl.ds(0, 8)], land_col.at[n], col_sems, n, other)
        for n, other in enumerate((group.peer, group.diag, group.sib))
    ]
    for copy in copies:
        copy.start()
    for copy in copies:
        copy.wait()
    me = group.me
    block[me, :, :8] = block[me, :, :8] + (land_col[0] + (land_col[1] + land_col[2]))
    swap = push(block.at[me, away], land_x, x_sems, 0, away, "section")
    swap.start()
    deliver.done()

    @pl.when(section == 0)
    def _():
        grads_ref[section] = turned(mine[...]).astype(LOW)

    @pl.when(section == 1)
    def _():
        send[...] = turned(mine[...]).astype(LOW)
        gradients.start()
        grads_ref[section] = turned(far_ref[...]).astype(LOW)

    swap.wait()
    land_z[row] = block[me, section] + land_x[...]
    copies = [
        push(land_z.at[row], land_z.at[row], z_sems, n, other, "row")
        for n, other in enumerate(others)
    ]
    for copy in copies:
        copy.start()
    for copy in copies:
        copy.wait()
    result = land_z[0]
    for n in range(1, land_z.shape[0]):
        result = result + land_z[n]
    sums_ref[...] = result
    gradients.wait()
    parts.wait()


def greet_section():
    barrier = pltpu.get_barrier_semaphore()
    other = 1 - lax.axis_index("section")
    pl.semaphore_signal(barrier, inc=1, device_id={"section": other}, device_id_type=MESH)
    pl.semaphore_wait(barrier, 1)


def cross_kernel(up, part_ref, got_ref, sems):
    greet_section()
    pair = [(part_ref, got_ref)]
    part = OneWay(pair, [], sems) if up else OneWay([], pair, sems)
    part.start()
    part.wait()


def write_kernel(*refs):
    late, far_late, early, far_early = [refs[n : n + 3] for n in (0, 3, 6, 9)]
    sums_ref, results_ref, grads_ref, attend_ref, output_ref, expand_ref, contract_ref, *vector_refs = refs[12:-4]
    *vector_refs, outputs_ref, inputs_ref = vector_refs
    own, far, low, sems = refs[-4:]
    length = low.shape[2]
    moves = [pltpu.make_async_copy(grads_ref, low, sems.at[6])] + [
        pltpu.make_async_copy(results_ref.at[n], outputs_ref.at[:, pl.ds(n * length, length)], sems.at[7 + n])
        for n in range(2)
    ]
    for move in moves:
        move.start()
    half = early[0].shape[1]
    width = output_ref.shape[0]
    section = lax.axis_index("section")

    def load(firsts, seconds):
        copies = [
            pltpu.make_async_copy(source, into, sems.at[n])
            for n, (source, into) in enumerate((*firsts, *seconds))
        ]
        for copy in copies:
            copy.start()
        for copy in copies:
            copy.wait()

    @pl.when(section == 0)
    def _():
        load(
            [(early[n], own.at[n, :, pl.ds(0, half)]) for n in range(3)],
            [(far_early[n], own.at[n, :, pl.ds(half, half)]) for n in range(3)],
        )
        far[...] = jnp.zeros_like(far)

    @pl.when(section == 1)
    def _():
        load([(late[n], own.at[n]) for n in range(3)], [(far_late[n], far.at[n]) for n in range(3)])

    moves[0].wait()
    for n in range(2):
        inputs_ref[:, n * length : (n + 1) * length] = low[n].astype(WIDE)
    first = own[0].astype(WIDE) + far[0].astype(WIDE)
    for j in range(3):
        attend_ref[j] = first[:, j * width : (j + 1) * width]
    corner = first[:, 3 * width :]
    high = corner.astype(LOW)
    output_ref[...] = turned(high) + turned((corner - high.astype(WIDE)).astype(LOW))
    expand_ref[...] = own[1].astype(WIDE) + far[1].astype(WIDE)
    contract_ref[...] = own[2].astype(WIDE) + far[2].astype(WIDE)
    for n in range(6):
        vector_refs[n][...] = sums_ref[n : n + 1, :]
    vector_refs[6][...] = sums_ref[8:10, :][None]
    for n in range(vector_refs[7].shape[1] // width):
        vector_refs[7][:, n * width : (n + 1) * width] = sums_ref[10 + n : 11 + n, :]
    for move in moves[1:]:
        move.wait()


VM = pl.BlockSpec(memory_space=pltpu.VMEM)
ANY = pl.BlockSpec(memory_space=pl.ANY)
PAIRS = pltpu.SemaphoreType.DMA((2, 3 * PARTS))
LOCAL = pltpu.SemaphoreType.DMA((4,))


def shape(dims, kind=LOW):
    return jax.ShapeDtypeStruct(dims, kind)


def launch(
    body, number, rows, in_specs, ins, outs, out_specs, scratch, swaps=(), diagonal=False, across=False, late=(),
):
    n_in, n_out, n = len(ins), len(outs), len(swaps)
    held_in = [i for i in range(n_in) if in_specs[i] is VM]
    held_out = [i for i in range(n_out) if out_specs[i] is VM]

    def kernel(*refs):
        refs = list(refs)
        takes, sources = refs[:n_in], refs[n_in : n_in + n]
        gives = refs[n_in + n : n_in + n + n_out]
        lands = refs[n_in + n + n_out : n_in + 2 * n + n_out]
        rest = refs[n_in + 2 * n + n_out :]
        own, rest = rest[: len(scratch)], rest[len(scratch) :]
        in_held, rest = rest[: len(held_in)], rest[len(held_in) :]
        out_held, rest = rest[: len(held_out)], rest[len(held_out) :]
        in_sems, out_sems, swap_sems = rest
        group = Group(rows)
        for k, i in enumerate(held_in):
            group.loads[i] = pltpu.make_async_copy(takes[i], in_held[k], in_sems.at[k])
            group.loads[i].start()
            takes[i] = in_held[k]
        for k, i in enumerate(held_out):
            group.stores[i] = pltpu.make_async_copy(out_held[k], gives[i], out_sems.at[k])
            gives[i] = out_held[k]
        group.greet(n or across, diagonal)
        other = 1 - lax.axis_index("section")
        copies = [
            push(source, land, swap_sems, i, other, "section")
            for i, (source, land) in enumerate(zip(sources, lands))
        ]
        for copy in copies:
            copy.start()
        group.need(*[i for i in held_in if i not in late])
        body(group, *takes, *gives, *own)
        group.emit(*[i for i in held_out if i not in group.begun])
        for copy in copies:
            copy.wait()
        for i in held_out:
            group.stores[i].wait()

    results = pl.pallas_call(
        kernel,
        out_shape=(*outs, *[shape(s.shape, s.dtype) for s in swaps]),
        in_specs=[ANY] * (n_in + n),
        out_specs=(ANY,) * (n_out + n),
        scratch_shapes=[
            *scratch,
            *[pltpu.VMEM(ins[i].shape, ins[i].dtype) for i in held_in],
            *[pltpu.VMEM(outs[i].shape, outs[i].dtype) for i in held_out],
            pltpu.SemaphoreType.DMA((len(held_in),)),
            pltpu.SemaphoreType.DMA((len(held_out),)),
            pltpu.SemaphoreType.DMA((2, max(n, 1))),
        ],
        compiler_params=pltpu.CompilerParams(
            collective_id=number, has_side_effects=True, vmem_limit_bytes=GRANT
        ),
        cost_estimate=pl.CostEstimate(flops=int(3e10), bytes_accessed=30 * MEBI, transcendentals=0),
    )(*ins, *swaps)
    return results[:n_out], results[n_out:]


def start_call(number, tokens, cotangent, small, contract, columns):
    width = tokens.shape[0]
    size = width * columns
    kinds = small.shape[0]
    outs = (shape((LENGTH, size)), shape((LENGTH, size)), shape((2, columns, kinds, width)), shape(contract.shape))
    blocks = pltpu.VMEM((columns, width, LENGTH), LOW)
    vectors = pltpu.VMEM((columns, kinds, width), LOW)
    return pl.pallas_call(
        start_kernel,
        out_shape=outs,
        in_specs=[ANY] * 4,
        out_specs=(VM, VM, VM, ANY),
        scratch_shapes=[
            blocks, blocks, vectors, vectors, PAIRS, PAIRS,
            pltpu.SemaphoreType.DMA((2, 3 * PARTS + 2)), LOCAL,
        ],
        compiler_params=pltpu.CompilerParams(
            collective_id=number, has_side_effects=True, vmem_limit_bytes=GRANT
        ),
        cost_estimate=pl.CostEstimate(flops=int(3e10), bytes_accessed=30 * MEBI, transcendentals=0),
    )(tokens, cotangent, small, contract)


def attend_call(number, x, pair, vec, bias, rows, width, swaps):
    size = vec.shape[1]
    heads = width // HEAD
    outs = (
        shape((LENGTH, size)),
        shape((3 * heads, LENGTH, HEAD)),
        shape((LENGTH, width)),
        shape((8, LENGTH), WIDE),
        shape((rows, size), WIDE),
        shape((rows, size)),
    )
    scratch = [
        pltpu.VMEM((size, 4 * width), LOW),
        pltpu.VMEM((heads, LENGTH, HEAD), LOW),
        *scatter_scratch(rows, size), LOCAL,
    ]
    return launch(
        functools.partial(attend_kernel, heads),
        number, rows, [VM, ANY, ANY, VM, VM], (x, *pair, vec, bias), outs, (VM,) * 6, scratch, swaps,
    )


def widen_call(number, second, pair, bias, grad, swaps):
    rows, size = second.shape
    wide = bias.shape[1]
    last = grad is not None
    ins, in_specs = [second, *pair, bias], [VM, ANY, ANY, VM]
    outs = [shape((LENGTH, size)), shape((LENGTH, wide)), shape((LENGTH, wide))]
    if last:
        ins, in_specs, outs = ins + [grad], in_specs + [VM], outs + [shape((size, wide))]
    scratch = [pltpu.VMEM((size, wide), LOW), PAIRS, LOCAL]
    return launch(
        functools.partial(widen_kernel, last),
        number, rows, in_specs, ins, outs, (VM,) * len(outs), scratch, swaps, late=(4,),
    )


def contract_call(number, active, hidden, pair, vec, swaps):
    rows, size = hidden.shape
    wide = active.shape[1]
    scratch = [pltpu.VMEM((size, wide), LOW), *scatter_scratch(rows, size), PAIRS, LOCAL]
    return launch(
        contract_kernel, number, rows, [VM, VM, ANY, ANY, VM], (active, hidden, *pair, vec),
        [shape((rows, size)), shape((LENGTH, size))], (VM, VM), scratch, swaps, late=(1,),
    )


def late_expand_call(number, active, hidden, contract, expand, grad, slope, second, vec, swaps):
    rows, size = hidden.shape
    wide = slope.shape[1]
    outs = [
        shape((rows, size), WIDE), shape((rows, size)), shape((8, size), WIDE),
        shape((size, wide)), shape((rows, size)),
    ]
    scratch = [
        pltpu.VMEM((size, wide), LOW),
        pltpu.VMEM((size, wide), LOW),
        pltpu.VMEM((LENGTH, wide), LOW),
        *scatter_scratch(rows, size), *scatter_scratch(rows, size), LOCAL,
    ]
    return launch(
        late_expand_kernel,
        number, rows, [VM, VM, ANY, ANY, ANY, ANY, VM, VM, VM, VM],
        (active, hidden, *contract, *expand, grad, slope, second, vec),
        outs, [VM] * 5, scratch, swaps, late=(1, 6, 7, 8),
    )


def expand_back_call(number, grad, contract, expand, slope, active, second, hidden, vec, swaps):
    rows, size = hidden.shape
    wide = slope.shape[1]
    half = wide // 2
    outs = [
        shape((rows, size), WIDE), shape((rows, size)), shape((8, size), WIDE),
        shape((size, half)), shape((size, half)), shape((LENGTH, size)), shape((size, half)),
    ]
    scratch = [
        pltpu.VMEM((size, wide), LOW),
        pltpu.VMEM((size, wide), LOW),
        pltpu.VMEM((LENGTH, wide), LOW),
        *scatter_scratch(rows, size), PAIRS, LOCAL,
        pltpu.VMEM((2, size, half), LOW), pltpu.VMEM((size, half), LOW),
        pltpu.SemaphoreType.DMA((2, size // TILE)),
    ]
    return launch(
        expand_back_kernel,
        number, rows, [VM, ANY, ANY, ANY, ANY, VM, VM, VM, VM, VM],
        (grad, *contract, *expand, slope, active, second, hidden, vec),
        outs, [VM] * 6 + [ANY], scratch, swaps, False, True, late=(5, 6, 7, 8),
    )


def scores_scratch(size, width, heads):
    return [
        pltpu.VMEM((size, 4 * width), LOW),
        pltpu.VMEM((LENGTH, size), LOW),
        pltpu.VMEM((heads, LENGTH, HEAD), LOW),
        pltpu.VMEM((8, LENGTH), WIDE),
        pltpu.VMEM((heads, LENGTH, HEAD), LOW),
        pltpu.VMEM((heads, LENGTH, HEAD), WIDE),
        pltpu.VMEM((heads, LENGTH, HEAD), WIDE),
    ]


def late_attend_call(number, low, grad, x_own, pair, normed, heads_all, o, lse, vec, result, y, swaps):
    rows, size = grad.shape
    width = o.shape[1]
    heads = width // HEAD
    outs = (shape((rows, size)), shape((8, size), WIDE), shape((2, width, LENGTH)), shape((size, 4 * width)))
    scratch = [
        *scores_scratch(size, width, heads),
        pltpu.VMEM((LENGTH, 3 * width), LOW),
        pltpu.VMEM((size, 4 * width), LOW),
        pltpu.VMEM((size, width), LOW),
        pltpu.VMEM((LENGTH, width), LOW),
        pltpu.VMEM((LENGTH, width), LOW),
        pltpu.VMEM((LENGTH // rows, rows, width), LOW),
        *scatter_scratch(rows, size), PAIRS,
        pltpu.SemaphoreType.DMA((2, 3)), pltpu.SemaphoreType.DMA((2, 2)), LOCAL,
    ]
    return launch(
        functools.partial(late_attend_kernel, heads),
        number, rows, [VM, VM, VM, ANY, ANY, VM, VM, VM, VM, VM, VM, VM],
        (low, grad, x_own, *pair, normed, heads_all, o, lse, vec, result, y),
        outs, (VM, VM, VM, ANY), scratch, swaps, True, True, late=(1, 2, 5, 6, 7, 8, 10, 11),
    )


def scores_back_call(number, low, pair, heads_all, o, lse, keep, send):
    rows, size = low.shape
    width = o.shape[1]
    heads = width // HEAD
    outs = (shape((LENGTH, 3 * width)), shape((size, width)), shape(keep.shape))
    scratch = [
        *scores_scratch(size, width, heads),
        pltpu.VMEM(keep.shape, LOW),
        PAIRS, LOCAL, pltpu.SemaphoreType.DMA((2, 1)),
    ]
    return launch(
        functools.partial(scores_back_kernel, heads),
        number, rows, [VM, ANY, ANY, VM, VM, VM, VM, ANY], (low, *pair, heads_all, o, lse, keep, send),
        outs, (VM, VM, ANY), scratch, (), False, True, late=(3, 4, 5, 6),
    )[0]


def attend_back_call(number, mixed, outer, grad, x_own, pair, normed, vec):
    rows, size = grad.shape
    width = outer.shape[1]
    half = 2 * width
    outs = (shape((size, half)), shape((rows, size)), shape((8, size), WIDE))
    scratch = [
        pltpu.VMEM((size, 4 * width), LOW),
        pltpu.VMEM((2, size, half), LOW),
        pltpu.VMEM((size, half), LOW),
        *scatter_scratch(rows, size), LOCAL, pltpu.SemaphoreType.DMA((2, size // TILE)),
    ]
    return launch(
        attend_back_kernel,
        number, rows, [VM, VM, VM, VM, ANY, ANY, VM, VM],
        (mixed, outer, grad, x_own, *pair, normed, vec), outs, (ANY, VM, VM), scratch, (), False, True,
        late=(1, 2, 3, 6),
    )[0]


def finish_call(number, parts, near, far, sums, row_count):
    rows, size = near.shape
    length, width = far.shape
    columns = length // rows
    outs = (
        shape((2, width, length)),
        shape((16, width), WIDE),
        *[shape(part.shape) for part in parts],
    )
    scratch = [
        pltpu.VMEM(near.shape, LOW),
        pltpu.VMEM(far.shape, LOW),
        *[pltpu.VMEM(s.shape, WIDE) for s in sums],
        pltpu.VMEM((length, width), LOW),
        pltpu.VMEM((columns, rows, width), LOW),
        pltpu.VMEM((columns, 2, 16, width), WIDE),
        pltpu.VMEM((3, 2, 8, width), WIDE),
        pltpu.VMEM((16, width), WIDE),
        pltpu.VMEM((row_count, 16, width), WIDE),
        pltpu.VMEM((width, length), LOW),
        pltpu.SemaphoreType.DMA((2, 3)),
        pltpu.SemaphoreType.DMA((2, 3)),
        pltpu.SemaphoreType.DMA((2, 2)),
        pltpu.SemaphoreType.DMA((2, row_count)),
        pltpu.SemaphoreType.DMA((2, 3)),
        pltpu.SemaphoreType.DMA((6,)),
    ]
    return pl.pallas_call(
        finish_kernel,
        out_shape=outs,
        in_specs=[ANY] * 9,
        out_specs=(VM, VM) + (ANY,) * 3,
        scratch_shapes=scratch,
        compiler_params=pltpu.CompilerParams(
            collective_id=number, has_side_effects=True, vmem_limit_bytes=GRANT
        ),
        cost_estimate=pl.CostEstimate(flops=int(3e10), bytes_accessed=30 * MEBI, transcendentals=0),
    )(*parts, near, far, *sums)


def cross_call(number, up, part):
    return pl.pallas_call(
        functools.partial(cross_kernel, up),
        out_shape=shape(part.shape),
        in_specs=[ANY],
        out_specs=ANY,
        scratch_shapes=[pltpu.SemaphoreType.DMA((2, 1))],
        compiler_params=pltpu.CompilerParams(
            collective_id=number, has_side_effects=True, vmem_limit_bytes=GRANT
        ),
        cost_estimate=pl.CostEstimate(flops=int(1e10), bytes_accessed=10 * MEBI, transcendentals=0),
    )(part)


def write_call(late, far_late, early, far_early, sums, wide, results, grads):
    rows, size = late[0].shape
    _, width, length = grads.shape
    return pl.pallas_call(
        write_kernel,
        out_shape=(
            shape((3, rows, width), WIDE), shape((width, rows), WIDE), shape((rows, size), WIDE), shape((rows, size), WIDE),
            *[shape((1, width), WIDE)] * 6, shape((1, 2, width), WIDE), shape((1, wide), WIDE),
            shape((width, 2 * length)), shape((width, 2 * length), WIDE),
        ),
        in_specs=[ANY] * 12 + [VM, ANY, ANY],
        out_specs=(VM,) * 12 + (ANY, VM),
        scratch_shapes=[pltpu.VMEM((3, rows, size), LOW)] * 2
        + [pltpu.VMEM(grads.shape, LOW), pltpu.SemaphoreType.DMA((9,))],
        compiler_params=pltpu.CompilerParams(vmem_limit_bytes=GRANT),
    )(*late, *far_late, *early, *far_early, sums, results, grads)


def swap_sections(value):
    return lax.ppermute(value, "section", [(0, 1), (1, 0)])


def on_device(
    tokens,
    cotangent,
    first_gain,
    first_shift,
    attend_weight,
    attend_bias,
    output_weight,
    output_bias,
    second_gain,
    second_shift,
    expand_weight,
    expand_bias,
    contract_weight,
    contract_bias,
):
    section = lax.axis_index("section")
    column = lax.axis_index("col")
    first_section = section == 0
    columns = lax.axis_size("col")
    width = tokens.shape[1]
    size = width * columns
    rows = LENGTH // columns

    def pick(early, later):
        return jnp.where(first_section, early, later)

    block_rows = attend_weight.shape[1]
    units = (
        jnp.concatenate(
            [attend_weight[0].reshape(block_rows, 3 * width), output_weight[0].T], axis=1
        ),
        expand_weight[0],
        contract_weight[0].T,
    )
    kept_blocks, sent_blocks = [], []
    for unit in units:
        half = unit.shape[1] // 2
        low, high = unit[:, :half], unit[:, half:]
        kept_blocks.append(pick(low, high))
        sent_blocks.append(pick(high, low))

    small = jnp.concatenate(
        [
            first_gain,
            first_shift,
            output_bias,
            second_gain,
            second_shift,
            contract_bias,
            attend_bias[0],
            expand_bias[0].reshape(-1, width),
        ],
        0,
    )
    filled = small.shape[0]
    small = jnp.pad(small, ((0, -filled % (16 * PARTS)), (0, 0)))
    got_attend = swap_sections(sent_blocks[0])
    got_expand = swap_sections(sent_blocks[1])
    got_attend, got_expand, sent_contract = lax.optimization_barrier((got_attend, got_expand, units[2]))
    x0_full, gy_full, vectors, got_contract = start_call(
        1, tokens.T, cotangent.T, small, sent_contract, columns
    )

    def gather_blocks(block):
        return lax.all_gather(block, "row", axis=0, tiled=True)

    half = units[2].shape[1] // 2
    mats = [[], []]
    for own, got in ((kept_blocks[0], got_attend), (kept_blocks[1], got_expand)):
        for layer, block in enumerate((pick(own, got), pick(got, own))):
            mats[layer].append(gather_blocks(block))
    mats[0].append(gather_blocks(pick(kept_blocks[2], got_contract[:, half:])))
    mats[1].append(gather_blocks(pick(got_contract, units[2])))
    vectors = vectors.astype(WIDE)
    wide_vectors = jnp.swapaxes(vectors[:, :, :6], 1, 2).reshape(2, 6, size)
    wide_vectors = jnp.pad(wide_vectors, ((0, 0), (0, 2), (0, 0)))
    own_vectors = lax.dynamic_index_in_dim(vectors, column, 1, keepdims=False)
    attend_biases = jnp.stack(
        [own_vectors[:, 6], jnp.zeros_like(own_vectors[:, 6]), own_vectors[:, 7]], 1
    ).reshape(2, 1, 3 * width)
    expand_biases = own_vectors[:, 8:filled].reshape(2, 1, -1)

    def own_rows(full):
        return lax.dynamic_slice_in_dim(full, column * rows, rows, 0)

    def own_features(full):
        return lax.dynamic_slice_in_dim(full, column * width, width, 1)

    attn = (mats[0][0], swap_sections(mats[0][0]))
    x = x0_full
    kept, pairs = [], []
    owns = [own_rows(x0_full)]
    for layer in range(2):
        last = layer == 1
        vec = wide_vectors[layer]
        (normed, heads, o, lse, hidden, second_own), (other,) = attend_call(
            2 + 3 * layer, x, attn, vec, attend_biases[layer], rows, width, [mats[layer][1]]
        )
        expand = (mats[layer][1], other)
        outs, others = widen_call(
            3 + 3 * layer, second_own, expand, expand_biases[layer],
            gy_full if last else None, [] if last else [mats[0][2]],
        )
        second, active, slope = outs[:3]
        contract = (mats[layer][2], mats[layer][2] if last else others[0])
        if last:
            c1 = outs[3]
        pairs.append((attn, expand, contract))
        kept.append((normed, heads, o, lse, hidden, second, active, slope))
        if not last:
            (own, x), others = contract_call(4, active, hidden, contract, vec, [mats[1][0]])
            owns.append(own)
            attn = (mats[1][0], others[0])
    y0 = own_features(x)

    def scatter(total):
        return lax.psum_scatter(total, "row", scatter_dimension=0, tiled=True)

    def tie(value, then):
        return lax.optimization_barrier((value, then))

    attn, expand, contract = pairs[1]
    normed, heads, o, lse, hidden, second, active, slope = kept[1]
    (grad_hidden, low, expand_sums1, e1, result), _ = late_expand_call(
        8, active, hidden, contract, expand, gy_full, slope, second, wide_vectors[1], []
    )
    (gx1_own, attend_sums1, layer_outputs, w1), _ = late_attend_call(
        10, low, grad_hidden, owns[1], attn, normed, heads, o, lse, wide_vectors[1], result, y0, []
    )

    attn, expand, contract = pairs[0]
    normed, heads, o, lse, hidden, second, active, slope = kept[0]
    part_c1 = scatter(c1)
    (grad_hidden, low, expand_sums0, ek0, es0, gx1_full, total_c0), (far_c1,) = expand_back_call(
        12, gx1_own, contract, expand, slope, active, second, hidden, wide_vectors[0], [part_c1]
    )
    part_e1, low = tie(scatter(e1), low)
    mixed, outer, total_e0 = scores_back_call(14, low, attn, heads, o, lse, ek0, es0)
    part_w1, mixed = tie(scatter(w1), mixed)
    part_e1, mixed = tie(part_e1, mixed)
    far_e1, mixed = tie(cross_call(18, True, part_e1), mixed)
    part_c0, mixed = tie(scatter(total_c0), mixed)
    total_w0, gx0_own, attend_sums0 = attend_back_call(
        15, mixed, outer, grad_hidden, owns[0], attn, normed, wide_vectors[0]
    )
    part_e0, gx0_own = tie(scatter(total_e0), gx0_own)
    input_grads, small_grads, far_w1, far_c0, far_e0 = finish_call(
        16,
        (part_w1, part_c0, part_e0),
        gx0_own,
        own_features(gx1_full),
        (attend_sums0, expand_sums0, attend_sums1, expand_sums1),
        lax.axis_size("row"),
    )

    part_w0, small_grads = tie(scatter(total_w0), small_grads)
    far_w0 = cross_call(17, False, part_w0)
    attend_part, output_part, expand_part, contract_part, *vector_grads, layer_outputs, input_grads = write_call(
        (part_w1, part_e1, part_c1),
        (far_w1, far_e1, far_c1),
        (part_w0, part_e0, part_c0),
        (far_w0, far_e0, far_c0),
        small_grads,
        expand_bias.shape[1],
        layer_outputs,
        input_grads,
    )
    return (
        layer_outputs.T[None],
        input_grads.T[None],
        vector_grads[0],
        vector_grads[1],
        jnp.swapaxes(attend_part, 0, 1)[None],
        vector_grads[6],
        output_part[None],
        vector_grads[2],
        vector_grads[3],
        vector_grads[4],
        expand_part[None],
        vector_grads[7],
        contract_part.T[None],
        vector_grads[5],
    )


def solution(mesh):
    return jax.shard_map(
        on_device,
        mesh=mesh,
        in_specs=(
            P("row", "col"),
            P("row", "col"),
            P("section", "col"),
            P("section", "col"),
            P("section", "row", None, "col"),
            P("section", None, "col"),
            P("section", "col", "row"),
            P("section", "col"),
            P("section", "col"),
            P("section", "col"),
            P("section", "row", "col"),
            P("section", "col"),
            P("section", "col", "row"),
            P("section", "col"),
        ),
        out_specs=(
            P("section", "row", "col"),
            P("section", "row", "col"),
            P("section", "col"),
            P("section", "col"),
            P("section", "row", None, "col"),
            P("section", None, "col"),
            P("section", "col", "row"),
            P("section", "col"),
            P("section", "col"),
            P("section", "col"),
            P("section", "row", "col"),
            P("section", "col"),
            P("section", "col", "row"),
            P("section", "col"),
        ),
        check_vma=False,
    )
```

```python
import functools

import jax
import jax.numpy as jnp
from jax import lax
from jax.experimental import pallas as pl
from jax.experimental.pallas import tpu as pltpu
from jax.sharding import PartitionSpec as P

HEAD = 64
LENGTH = 1024
EPS = 1e-05
LOW = jnp.bfloat16
WIDE = jnp.float32
MESH = pl.DeviceIdType.MESH
PARTS = 2
TILE = 256
MEBI = 1024 * 1024
GRANT = 58 * MEBI


def nn(left, right):
    return lax.dot_general(left, right, (((1,), (0,)), ((), ())), preferred_element_type=WIDE)


def nt(left, right):
    return lax.dot_general(left, right, (((1,), (1,)), ((), ())), preferred_element_type=WIDE)


def tn(left, right):
    return lax.dot_general(left, right, (((0,), (0,)), ((), ())), preferred_element_type=WIDE)


def turned(values):
    width = values.shape[1]
    unit = (
        lax.broadcasted_iota(jnp.int32, (width, width), 0) == lax.broadcasted_iota(jnp.int32, (width, width), 1)
    ).astype(LOW)
    return nt(unit, values)


def turned_back(values):
    height = values.shape[0]
    unit = (
        lax.broadcasted_iota(jnp.int32, (height, height), 0) == lax.broadcasted_iota(jnp.int32, (height, height), 1)
    ).astype(LOW)
    return tn(values, unit)


def normalise(values):
    center = jnp.mean(values, axis=1, keepdims=True)
    centred = values - center
    scale = lax.rsqrt(jnp.mean(centred * centred, axis=1, keepdims=True) + EPS)
    return centred * scale, scale


def norm_backward(grad, hat, scale, gain):
    scaled = grad * gain
    mean_one = jnp.mean(scaled, axis=1, keepdims=True)
    mean_two = jnp.mean(scaled * hat, axis=1, keepdims=True)
    return scale * (scaled - mean_one - hat * mean_two)


class Group:
    def __init__(self, rows):
        self.me = lax.axis_index("col")
        chip, core = self.me // 2, self.me % 2
        self.sib = chip * 2 + 1 - core
        self.peer = (1 - chip) * 2 + core
        self.diag = (1 - chip) * 2 + 1 - core
        self.rows = rows
        self.part = rows // PARTS
        self.loads, self.stores, self.begun = {}, {}, set()

    def need(self, *places):
        for place in places:
            self.loads[place].wait()

    def emit(self, *places):
        for place in places:
            self.stores[place].start()
            self.begun.add(place)

    def greet(self, swaps, diagonal, rows=()):
        barrier = pltpu.get_barrier_semaphore()
        others = [{"col": self.sib}, {"col": self.peer}]
        if diagonal:
            others.append({"col": self.diag})
        if swaps:
            others.append({"section": 1 - lax.axis_index("section")})
        others += [{"row": row} for row in rows]
        for other in others:
            pl.semaphore_signal(barrier, inc=1, device_id=other, device_id_type=MESH)
        pl.semaphore_wait(barrier, len(others))

    def slab(self, owner, j):
        return pl.ds(pl.multiple_of(owner * self.rows + j * self.part, self.part), self.part)

    def chunk(self, owner):
        return pl.ds(pl.multiple_of(owner * self.rows, self.rows), self.rows)


def push(src, dst, sems, slot, target, axis="col"):
    return pltpu.make_async_remote_copy(
        src_ref=src,
        dst_ref=dst,
        send_sem=sems.at[0, slot],
        recv_sem=sems.at[1, slot],
        device_id={axis: target},
        device_id_type=MESH,
    )


class Gather:
    def __init__(self, group, full, sems, blocks=False):
        self.group, self.full, self.sems, self.blocks = group, full, sems, blocks
        self.over, self.near, self.relayed = [], [], []

    def piece(self, owner, j):
        if not self.blocks:
            return self.full.at[self.group.slab(owner, j)]
        part = self.full.shape[1] // PARTS
        return self.full.at[owner, pl.ds(j * part, part)]

    def start_part(self, j):
        g = self.group
        piece = self.piece(g.me, j)
        self.over.append(push(piece, piece, self.sems, j, g.peer))
        self.near.append(push(piece, piece, self.sems, PARTS + j, g.sib))
        self.over[-1].start()
        self.near[-1].start()

    def start(self):
        for j in range(PARTS):
            self.start_part(j)

    def sibling(self):
        for copy in self.near:
            copy.wait_recv()

    def relay(self):
        g = self.group
        for j in range(PARTS):
            self.over[j].wait_recv()
            piece = self.piece(g.peer, j)
            self.relayed.append(push(piece, piece, self.sems, 2 * PARTS + j, g.sib))
            self.relayed[-1].start()

    def diagonal(self):
        for copy in self.relayed:
            copy.wait_recv()

    def done(self):
        for copy in self.over + self.near + self.relayed:
            copy.wait_send()

    def each(self, body, first=None):
        g = self.group
        if not self.over:
            self.start()
        if first is not None:
            first()
        body(g.me)
        self.sibling()
        body(g.sib)
        self.relay()
        body(g.peer)
        self.diagonal()
        body(g.diag)
        self.done()


class Scatter:
    def __init__(self, group, stage, land, total, sems):
        self.group, self.stage, self.land, self.total, self.sems = group, stage, land, total, sems

    def start(self, part):
        g, stage, land = self.group, self.stage, self.land
        self.first, self.over, self.near = [], [], []
        def split(owner):
            whole = part(owner)
            return [whole[j * g.part : (j + 1) * g.part] for j in range(PARTS)]

        for j, mine in enumerate(split(g.diag)):
            stage[0, j] = mine.astype(LOW)
            self.first.append(push(stage.at[0, j], land.at[0, j], self.sems, j, g.sib))
            self.first[-1].start()
        for j, mine in enumerate(split(g.peer)):
            self.first[j].wait_recv()
            stage[1, j] = (mine + land[0, j].astype(WIDE)).astype(LOW)
            self.over.append(push(stage.at[1, j], land.at[1, j], self.sems, PARTS + j, g.peer))
            self.over[-1].start()
        for j, mine in enumerate(split(g.sib)):
            stage[2, j] = mine.astype(LOW)
            self.near.append(push(stage.at[2, j], land.at[2, j], self.sems, 2 * PARTS + j, g.sib))
            self.near[-1].start()
        for j, mine in enumerate(split(g.me)):
            self.total[j] = mine

    def take(self, j):
        self.near[j].wait_recv()
        self.over[j].wait_recv()
        land = self.land
        return self.total[j] + (land[1, j].astype(WIDE) + land[2, j].astype(WIDE))

    def done(self):
        for copy in self.first + self.over + self.near:
            copy.wait_send()


class Deliver:
    def __init__(self, group, stage, out, sems):
        self.group, self.stage, self.out, self.sems = group, stage, out, sems

    def start(self, rows_ref):
        g, width = self.group, self.out.shape[1]
        for c in range(self.stage.shape[0]):
            self.stage[c] = rows_ref[:, c * width : (c + 1) * width]
        place = self.out.at[g.chunk(g.me)]
        self.copies = [
            push(self.stage.at[other], place, self.sems, n, other)
            for n, other in enumerate((g.peer, g.diag, g.sib))
        ]
        for copy in self.copies:
            copy.start()
        self.out[g.chunk(g.me), :] = self.stage[g.me]

    def done(self):
        for copy in self.copies:
            copy.wait()


class OneWay:
    def __init__(self, up, down, sems):
        self.section = lax.axis_index("section")
        both = [*up, *down]
        copies = [
            push(source, into, sems, n, 1 - self.section, "section")
            for n, (source, into) in enumerate(both)
        ]
        self.up, self.down = copies[: len(up)], copies[len(up) :]

    def each(self, first, second):
        @pl.when(self.section == 0)
        def _():
            first(self.up)
            second(self.down)

        @pl.when(self.section == 1)
        def _():
            first(self.down)
            second(self.up)

    def start(self):
        self.each(lambda copies: [copy.start() for copy in copies], lambda copies: None)

    def wait(self):
        self.each(
            lambda copies: [copy.wait_send() for copy in copies],
            lambda copies: [copy.wait_recv() for copy in copies],
        )


def scatter_scratch(rows, width):
    part = rows // PARTS
    return [
        pltpu.VMEM((3, PARTS, part, width), LOW),
        pltpu.VMEM((3, PARTS, part, width), LOW),
        pltpu.VMEM((PARTS, part, width), WIDE),
        pltpu.SemaphoreType.DMA((2, 3 * PARTS)),
    ]


class Halves:
    def __init__(self, pair, whole, sems, slot):
        if pair[0].shape[1] == whole.shape[1]:
            self.copies = [pltpu.make_async_copy(pair[0], whole, sems.at[slot])]
            return
        section = lax.axis_index("section")
        half = whole.shape[1] // 2
        self.copies = []
        for n, place in enumerate((section, 1 - section)):
            columns = pl.ds(pl.multiple_of(place * half, half), half)
            self.copies.append(
                pltpu.make_async_copy(pair[n], whole.at[:, columns], sems.at[slot + n])
            )

    def start(self):
        for copy in self.copies:
            copy.start()

    def wait(self):
        for copy in self.copies:
            copy.wait()


class Trade:
    def __init__(self, keep, send, got, sems):
        self.keep, self.send, self.got, self.sems = keep, send, got, sems
        self.tiles = keep.shape[0] // TILE

    def copy(self, n):
        rows = pl.ds(pl.multiple_of(n * TILE, TILE), TILE)
        return push(
            self.send.at[rows], self.got.at[rows], self.sems, n, 1 - lax.axis_index("section"), "section"
        )

    def start(self, make):
        @pl.loop(0, self.tiles)
        def _(n):
            make(pl.ds(pl.multiple_of(n * TILE, TILE), TILE))
            self.copy(n).start()

    def finish(self):
        @pl.loop(0, self.tiles)
        def _(n):
            self.copy(n).wait()

        add_into(self.keep, self.got)


def add_into(keep_ref, got_ref):
    @pl.loop(0, keep_ref.shape[0] // TILE)
    def _(n):
        rows = pl.ds(pl.multiple_of(n * TILE, TILE), TILE)
        keep_ref[rows, :] = (keep_ref[rows, :].astype(WIDE) + got_ref[rows, :].astype(WIDE)).astype(LOW)


def causal_scores(scores):
    size = scores.shape[1]
    keep = lax.broadcasted_iota(jnp.int32, (size, size), 0) <= lax.broadcasted_iota(
        jnp.int32, (size, size), 1
    )
    begin = scores.shape[0] - size
    last = jnp.where(keep, scores[begin:], -1000000000.0)
    return last if begin == 0 else jnp.concatenate([scores[:begin], last], 0)


def attention_out(owner, size, heads_ref, o3, lse_ref, heads):
    for i in range(heads_ref.shape[1] // size):
        rows, finish = slice(i * size, (i + 1) * size), (i + 1) * size

        @pl.when(owner == i)
        def _():
            @pl.loop(0, heads)
            def _(h):
                scores = causal_scores(nt(heads_ref[heads + h, :finish, :], heads_ref[h, rows, :]))
                highest = jnp.max(scores, axis=0, keepdims=True)
                powers = jnp.exp(scores - highest)
                summed = jnp.sum(powers, axis=0, keepdims=True)
                mixed = tn(heads_ref[2 * heads + h, :finish, :], powers.astype(LOW))
                o3[h, rows, :] = (mixed / summed).T.astype(LOW)
                lse_ref[pl.ds(h, 1), rows] = highest + jnp.log(summed)


def attention_back(owner, size, heads_ref, go3, lse_ref, dots_ref, g3, key_acc, value_acc, heads):
    for i in range(heads_ref.shape[1] // size):
        rows, finish = slice(i * size, (i + 1) * size), (i + 1) * size

        @pl.when(owner == i)
        def _():
            @pl.loop(0, heads)
            def _(h):
                queries = heads_ref[h, rows, :]
                keys = heads_ref[heads + h, :finish, :]
                grads = go3[h, rows, :]
                probs = jnp.exp(causal_scores(nt(keys, queries) - lse_ref[pl.ds(h, 1), rows]))
                grad_probs = nt(heads_ref[2 * heads + h, :finish, :], grads)
                grad_scores = (probs * (grad_probs - dots_ref[pl.ds(h, 1), rows])).astype(LOW)
                g3[h, rows, :] = (tn(grad_scores, keys) * HEAD ** (-0.5)).astype(LOW)
                key_acc[h, :finish, :] += nn(grad_scores, queries)
                value_acc[h, :finish, :] += nn(probs.astype(LOW), grads)


def start_kernel(
    tokens_ref, cotangent_ref, small_ref, expand_ref, contract_ref,
    x_ref, g_ref, vectors_ref, got_expand_ref, got_contract_ref,
    x4, g4, s4, other4, x_sems, g_sems, s_sems, local_sems,
):
    section = lax.axis_index("section")
    group = Group(x_ref.shape[0] // 4)
    length = x_ref.shape[0]
    loads = []
    rows = pl.ds(pl.multiple_of(section * length, length), length)
    sources = ((tokens_ref.at[:, rows], x4), (cotangent_ref.at[rows], g4), (small_ref, s4))
    for n, (source, into) in enumerate(sources):
        loads.append(pltpu.make_async_copy(source, into.at[group.me], local_sems.at[n]))
        loads[-1].start()
    group.greet(True, False)
    blocks = [
        push(source, into, s_sems, 3 * PARTS + 1 + n, 1 - section, "section")
        for n, (source, into) in enumerate(((expand_ref, got_expand_ref), (contract_ref, got_contract_ref)))
    ]
    blocks[0].start()
    gathers = [Gather(group, s4, s_sems, True), Gather(group, x4, x_sems, True), Gather(group, g4, g_sems, True)]
    for gather, load in zip(gathers, (loads[2], loads[0], loads[1])):
        load.wait()
        gather.start()
    width = x_ref.shape[1] // 4
    for gather, blocks4, full_ref in ((gathers[0], None, None), (gathers[1], x4, x_ref), (gathers[2], g4, g_ref)):
        gather.sibling()
        gather.relay()
        gather.diagonal()
        if blocks4 is None:
            swap = push(s4, other4, s_sems, 3 * PARTS, 1 - section, "section")
            swap.start()
            blocks[1].start()
        else:
            for c in range(blocks4.shape[0]):
                block = blocks4[c]
                if block.shape[0] == width:
                    block = turned_back(block).astype(LOW)
                full_ref[:, c * width : (c + 1) * width] = block
    swap.wait()
    for block in blocks:
        block.wait()
    vectors_ref[section] = s4[...]
    vectors_ref[1 - section] = other4[...]
    for gather in gathers:
        gather.done()


def attend_kernel(
    heads, group, x_ref, mine_ref, other_ref, vec_ref, bias_ref,
    normed_ref, heads_ref, o_ref, lse_ref, hidden_ref, second_ref,
    weight, o3, stage, land, total, scatter_sems, local_sems,
):
    width = o_ref.shape[1]
    halves = Halves((mine_ref, other_ref), weight, local_sems, 0)
    halves.start()
    lse_ref[...] = jnp.zeros_like(lse_ref)
    halves.wait()

    @pl.loop(0, LENGTH // group.rows)
    def _(owner):
        rows = group.chunk(owner)
        hat, _ = normalise(x_ref[rows, :].astype(WIDE))
        normed = (hat * vec_ref[0:1, :] + vec_ref[1:2, :]).astype(LOW)
        normed_ref[rows, :] = normed
        mixed = nn(normed, weight[:, : 3 * width]) + bias_ref[...]
        for j in range(3 * heads):
            piece = mixed[:, j * HEAD : (j + 1) * HEAD]
            if j < heads:
                piece = piece * HEAD ** (-0.5)
            heads_ref[j, rows, :] = piece.astype(LOW)

    group.emit(0, 1)

    def attend(owner):
        rows = group.chunk(owner)
        attention_out(owner, group.rows, heads_ref, o3, lse_ref, heads)
        for h in range(heads):
            o_ref[rows, h * HEAD : (h + 1) * HEAD] = o3[h, rows, :]
        return nt(o_ref[rows, :], weight[:, 3 * width :])

    scatter = Scatter(group, stage, land, total, scatter_sems)
    scatter.start(attend)
    group.emit(2, 3)
    for j in range(PARTS):
        rows = slice(j * group.part, (j + 1) * group.part)
        residual = x_ref[group.slab(group.me, j), :].astype(WIDE)
        hidden = residual + scatter.take(j) + vec_ref[2:3, :]
        hidden_ref[rows, :] = hidden
        hat, _ = normalise(hidden)
        second_ref[rows, :] = (hat * vec_ref[3:4, :] + vec_ref[4:5, :]).astype(LOW)
    scatter.done()


def outer_whole(left_ref, right_ref, out_ref):
    @pl.loop(0, left_ref.shape[1] // TILE)
    def _(n):
        rows = pl.ds(pl.multiple_of(n * TILE, TILE), TILE)
        out_ref[rows, :] = tn(left_ref[:, rows], right_ref[...]).astype(LOW)


def widen_kernel(last, group, second_ref, em_ref, eo_ref, bias_ref, *refs):
    if last:
        g_ref, *refs = refs
    full_ref, active_ref, slope_ref, *refs = refs
    if last:
        c_ref, *refs = refs
    expand, gather_sems, local_sems = refs
    halves = Halves((em_ref, eo_ref), expand, local_sems, 0)
    halves.start()
    full_ref[group.chunk(group.me), :] = second_ref[...]
    halves.wait()

    def widen(owner):
        rows = group.chunk(owner)
        t = nn(full_ref[rows, :], expand[...]) + bias_ref[...]
        square = t * t
        bent = jnp.tanh(0.7978845608028654 * t * (1.0 + 0.044715 * square))
        active_ref[rows, :] = (0.5 * t * (1.0 + bent)).astype(LOW)
        slope_ref[rows, :] = (
            0.5 * (1.0 + bent)
            + (0.5 * 0.7978845608028654) * t * (1.0 - bent * bent) * (1.0 + 3 * 0.044715 * square)
        ).astype(LOW)

    Gather(group, full_ref, gather_sems).each(widen)
    if last:
        group.emit(0, 1, 2)
        group.need(4)
        outer_whole(g_ref, active_ref, c_ref)


def outer_halves(left_ref, right_ref, keep_ref, send_ref):
    section = lax.axis_index("section")
    half = right_ref.shape[1] // 2
    for place, out in ((section, keep_ref), (1 - section, send_ref)):
        columns = pl.ds(pl.multiple_of(place * half, half), half)

        @pl.loop(0, left_ref.shape[1] // TILE)
        def _(n):
            rows = pl.ds(pl.multiple_of(n * TILE, TILE), TILE)
            out[rows, :] = tn(left_ref[:, rows], right_ref[:, columns]).astype(LOW)


def contract_kernel(
    group, active_ref, hidden_ref, cm_ref, co_ref, vec_ref, result_ref, full_ref,
    contract, stage, land, total, scatter_sems, gather_sems, local_sems,
):
    halves = Halves((cm_ref, co_ref), contract, local_sems, 0)
    halves.start()
    halves.wait()
    scatter = Scatter(group, stage, land, total, scatter_sems)
    scatter.start(lambda owner: nt(active_ref[group.chunk(owner), :], contract[...]))
    group.need(1)
    gather = Gather(group, full_ref, gather_sems)
    for j in range(PARTS):
        rows = slice(j * group.part, (j + 1) * group.part)
        result = (hidden_ref[rows, :] + scatter.take(j) + vec_ref[5:6, :]).astype(LOW)
        result_ref[rows, :] = result
        full_ref[group.slab(group.me, j), :] = result
        gather.start_part(j)
    gather.each(lambda owner: None)
    scatter.done()


def narrow_grads(group, scatter, full_ref, hidden_ref, vec_ref, grad_ref, low_ref, sums_ref):
    for j in range(PARTS):
        rows = slice(j * group.part, (j + 1) * group.part)
        grad = scatter.take(j)
        hat, scale = normalise(hidden_ref[rows, :])
        own = full_ref[group.slab(group.me, j), :].astype(WIDE)
        out = own + norm_backward(grad, hat, scale, vec_ref[3:4, :])
        grad_ref[rows, :] = out
        low_ref[rows, :] = out.astype(LOW)
        for n, term in enumerate((grad * hat, grad, own, out)):
            sums_ref[n : n + 1, :] += jnp.sum(term, axis=0, keepdims=True)


def bend(rows, full_ref, contract, slope_ref, before, sums_ref):
    grad = (nn(full_ref[rows, :], contract[...]) * slope_ref[rows, :].astype(WIDE)).astype(LOW)
    before[rows, :] = grad
    sums_ref[4:5, :] += jnp.sum(grad.astype(WIDE), axis=0, keepdims=True)


def late_expand_kernel(
    group, active_ref, hidden_ref, cm_ref, co_ref, em_ref, eo_ref, g_ref, slope_ref, second_ref, vec_ref,
    grad_ref, low_ref, sums_ref, e_ref, result,
    contract, expand, before,
    stage_a, land_a, total_a, sems_a, stage, land, total, scatter_sems, local_sems,
):
    first = Halves((cm_ref, co_ref), contract, local_sems, 0)
    then = Halves((em_ref, eo_ref), expand, local_sems, 2)
    first.start()
    then.start()
    sums_ref[...] = jnp.zeros_like(sums_ref)
    first.wait()
    forward = Scatter(group, stage_a, land_a, total_a, sems_a)
    forward.start(lambda owner: nt(active_ref[group.chunk(owner), :], contract[...]))
    group.need(6, 7)

    @pl.loop(0, LENGTH // group.rows)
    def _(n):
        bend(group.chunk(n), g_ref, contract, slope_ref, before, sums_ref)

    then.wait()
    scatter = Scatter(group, stage, land, total, scatter_sems)
    scatter.start(lambda owner: nt(before[group.chunk(owner), :], expand[...]))
    group.need(1)
    for j in range(PARTS):
        rows = slice(j * group.part, (j + 1) * group.part)
        result[rows, :] = (hidden_ref[rows, :] + forward.take(j) + vec_ref[5:6, :]).astype(LOW)
    group.emit(4)
    group.need(8)
    outer_whole(second_ref, before, e_ref)
    group.emit(3)
    narrow_grads(group, scatter, g_ref, hidden_ref, vec_ref, grad_ref, low_ref, sums_ref)
    group.emit(0, 1, 2)
    forward.done()
    scatter.done()


def expand_back_kernel(
    group, g_ref, cm_ref, co_ref, em_ref, eo_ref, slope_ref, active_ref, second_ref, hidden_ref, vec_ref,
    grad_ref, low_ref, sums_ref, ek_ref, es_ref, full_ref, c_ref,
    contract, expand, before, stage, land, total, scatter_sems, gather_sems, local_sems, outer, got, trade_sems,
):
    section = lax.axis_index("section")
    first = Halves((cm_ref, co_ref), contract, local_sems, 0)
    then = Halves((em_ref, eo_ref), expand, local_sems, 2)
    first.start()
    then.start()
    sums_ref[...] = jnp.zeros_like(sums_ref)
    full_ref[group.chunk(group.me), :] = g_ref[...]
    first.wait()
    Gather(group, full_ref, gather_sems).each(
        lambda owner: bend(group.chunk(owner), full_ref, contract, slope_ref, before, sums_ref),
        lambda: group.need(5),
    )
    group.emit(5)
    group.need(6)
    half = active_ref.shape[1] // 2

    def columns(place):
        return pl.ds(pl.multiple_of(place * half, half), half)

    def make(n):
        def tile(rows):
            place = section if n == 0 else 1 - section
            outer[n, rows, :] = tn(full_ref[:, rows], active_ref[:, columns(place)]).astype(LOW)

        return tile

    trade = Trade(outer.at[0], outer.at[1], got, trade_sems)
    trade.start(make(1))
    then.wait()
    scatter = Scatter(group, stage, land, total, scatter_sems)
    scatter.start(lambda owner: nt(before[group.chunk(owner), :], expand[...]))
    group.need(7)
    outer_halves(second_ref, before, ek_ref, es_ref)
    group.emit(3, 4)
    keep = make(0)

    @pl.loop(0, outer.shape[1] // TILE)
    def _(n):
        keep(pl.ds(pl.multiple_of(n * TILE, TILE), TILE))

    group.need(8)
    narrow_grads(group, scatter, full_ref, hidden_ref, vec_ref, grad_ref, low_ref, sums_ref)
    group.emit(0, 1, 2)
    scatter.done()
    trade.finish()
    store = pltpu.make_async_copy(outer.at[0], c_ref, local_sems.at[0])
    store.start()
    store.wait()


def scores_back(group, heads, low_ref, weight, heads_ref, o_ref, lse_ref, full, go3, dots, g3, accs, mixed, gather_sems, first):
    width = o_ref.shape[1]
    picks = (
        lax.broadcasted_iota(jnp.int32, (8, width), 1) // HEAD
        == lax.broadcasted_iota(jnp.int32, (8, width), 0)
    ).astype(WIDE)
    for acc in accs:
        acc[...] = jnp.zeros_like(acc)

    def spread(owner):
        rows = group.chunk(owner)
        grads = nn(full[rows, :], weight[:, 3 * width :]).astype(LOW)
        for h in range(heads):
            go3[h, rows, :] = grads[:, h * HEAD : (h + 1) * HEAD]
        term = grads.astype(WIDE) * o_ref[rows, :].astype(WIDE)
        dots[:, rows] = lax.dot_general(
            picks,
            term,
            (((1,), (1,)), ((), ())),
            precision=lax.Precision.HIGHEST,
            preferred_element_type=WIDE,
        )
        attention_back(owner, group.rows, heads_ref, go3, lse_ref, dots, g3, *accs, heads)

    full[group.chunk(group.me), :] = low_ref[...]
    Gather(group, full, gather_sems).each(spread, first)
    for j in range(3 * heads):
        source = g3[j] if j < heads else accs[j // heads - 1][j % heads].astype(LOW)
        mixed[:, j * HEAD : (j + 1) * HEAD] = source


def outer_out(full, o_ref, outer_ref):
    @pl.loop(0, outer_ref.shape[0] // TILE)
    def _(n):
        rows = pl.ds(pl.multiple_of(n * TILE, TILE), TILE)
        outer_ref[rows, :] = tn(full[:, rows], o_ref[...]).astype(LOW)


def attend_grads(group, scatter, x_ref, grad_ref, vec_ref, mixed, width, out_ref, sums_ref):
    sums_ref[2:3, : 3 * width] = jnp.sum(mixed[...].astype(WIDE), axis=0, keepdims=True)
    for j in range(PARTS):
        rows = slice(j * group.part, (j + 1) * group.part)
        grad = scatter.take(j)
        hat, scale = normalise(x_ref[rows, :].astype(WIDE))
        out = grad_ref[rows, :] + norm_backward(grad, hat, scale, vec_ref[0:1, :])
        out_ref[rows, :] = out.astype(LOW)
        for n, term in enumerate((grad * hat, grad)):
            sums_ref[n : n + 1, :] += jnp.sum(term, axis=0, keepdims=True)


def late_attend_kernel(
    heads, group, low_ref, grad_ref, x_ref, mine_ref, other_ref, normed_ref, heads_ref, o_ref, lse_ref, vec_ref,
    result_ref, y_ref,
    out_ref, sums_ref, results_ref, w_ref,
    weight, full, go3, dots, g3, key_acc, value_acc, mixed, outer, outer_o, late, y_land, stage4,
    stage, land, total, scatter_sems, gather_sems, deliver_sems, y_sems, local_sems,
):
    width = o_ref.shape[1]
    section = lax.axis_index("section")
    halves = Halves((mine_ref, other_ref), weight, local_sems, 0)
    halves.start()
    sums_ref[...] = jnp.zeros_like(sums_ref)
    halves.wait()
    deliver = Deliver(group, stage4, late, deliver_sems)

    def first():
        group.need(6, 7, 8, 10)
        deliver.start(result_ref)

    scores_back(
        group, heads, low_ref, weight, heads_ref, o_ref, lse_ref, full, go3, dots, g3,
        (key_acc, value_acc), mixed, gather_sems, first,
    )
    deliver.done()
    group.need(11)
    results = OneWay([(late, y_land)], [(y_ref, y_land)], y_sems)
    results.start()
    scatter = Scatter(group, stage, land, total, scatter_sems)
    scatter.start(lambda owner: nt(mixed[group.chunk(owner), :], weight[:, : 3 * width]))
    outer_out(full, o_ref, outer_o)
    group.need(5)

    @pl.loop(0, weight.shape[0] // TILE)
    def _(n):
        rows = pl.ds(pl.multiple_of(n * TILE, TILE), TILE)
        outer[rows, : 3 * width] = tn(normed_ref[:, rows], mixed[...]).astype(LOW)
        outer[rows, 3 * width :] = outer_o[rows, :]

    store = pltpu.make_async_copy(outer, w_ref, local_sems.at[2])
    store.start()
    @pl.when(section == 0)
    def _():
        results_ref[section] = turned(y_ref[...]).astype(LOW)

    @pl.when(section == 1)
    def _():
        results_ref[section] = turned(late[...]).astype(LOW)

    group.need(1, 2)
    attend_grads(group, scatter, x_ref, grad_ref, vec_ref, mixed, width, out_ref, sums_ref)
    results.wait()
    results_ref[1 - section] = turned(y_land[...]).astype(LOW)
    scatter.done()
    store.wait()


def scores_back_kernel(
    heads, group, low_ref, mine_ref, other_ref, heads_ref, o_ref, lse_ref, ek_ref, es_ref,
    mixed, outer_ref, e_ref,
    weight, full, go3, dots, g3, key_acc, value_acc, got, gather_sems, local_sems, swap_sems,
):
    swap = push(es_ref, got, swap_sems, 0, 1 - lax.axis_index("section"), "section")
    swap.start()
    halves = Halves((mine_ref, other_ref), weight, local_sems, 0)
    halves.start()
    halves.wait()
    scores_back(
        group, heads, low_ref, weight, heads_ref, o_ref, lse_ref, full, go3, dots, g3,
        (key_acc, value_acc), mixed, gather_sems, lambda: group.need(3, 4, 5),
    )
    group.emit(0)
    outer_out(full, o_ref, outer_ref)
    group.emit(1)
    group.need(6)
    swap.wait()
    add_into(ek_ref, got)
    store = pltpu.make_async_copy(ek_ref, e_ref, local_sems.at[0])
    store.start()
    store.wait()


def attend_back_kernel(
    group, mixed, outer_ref, grad_ref, x_ref, mine_ref, other_ref, normed_ref, vec_ref,
    w_ref, out_ref, sums_ref,
    weight, outer, got, stage, land, total, scatter_sems, local_sems, swap_sems,
):
    width = outer_ref.shape[1]
    section = lax.axis_index("section")
    halves = Halves((mine_ref, other_ref), weight, local_sems, 0)
    halves.start()
    sums_ref[...] = jnp.zeros_like(sums_ref)
    half = weight.shape[1] // 2
    scatter = Scatter(group, stage, land, total, scatter_sems)
    group.need(1, 6)

    def make(n):
        place = section if n == 0 else 1 - section

        def tile(rows):
            @pl.when(place == 0)
            def _():
                outer[n, rows, :] = tn(normed_ref[:, rows], mixed[:, :half]).astype(LOW)

            @pl.when(place == 1)
            def _():
                outer[n, rows, : 3 * width - half] = tn(normed_ref[:, rows], mixed[:, half:]).astype(LOW)
                outer[n, rows, 3 * width - half :] = outer_ref[rows, :]

        return tile

    trade = Trade(outer.at[0], outer.at[1], got, swap_sems)
    trade.start(make(1))
    halves.wait()
    scatter.start(lambda owner: nt(mixed[group.chunk(owner), :], weight[:, : 3 * width]))
    keep = make(0)

    @pl.loop(0, outer.shape[1] // TILE)
    def _(n):
        keep(pl.ds(pl.multiple_of(n * TILE, TILE), TILE))

    group.need(2, 3)
    attend_grads(group, scatter, x_ref, grad_ref, vec_ref, mixed, width, out_ref, sums_ref)
    group.emit(1, 2)
    scatter.done()
    trade.finish()
    store = pltpu.make_async_copy(outer.at[0], w_ref, local_sems.at[2])
    store.start()
    store.wait()


def finish_kernel(
    late_ref, early1_ref, early2_ref, near_hbm, far_hbm, a0_hbm, n0_hbm, a1_hbm, n1_hbm,
    grads_ref, sums_ref, got_late, got_early1, got_early2,
    near_ref, far_ref, a0, n0, a1, n1, mine, stage4, block, land_col, land_x, land_z, send,
    deliver_sems, col_sems, x_sems, z_sems, part_sems, local_sems,
):
    section, row = lax.axis_index("section"), lax.axis_index("row")
    away = 1 - section
    group = Group(near_ref.shape[0])
    width = far_ref.shape[1]
    others = [lax.rem(row + d, land_z.shape[0]) for d in range(1, land_z.shape[0])]
    loads = [
        pltpu.make_async_copy(source, into, local_sems.at[n])
        for n, (source, into) in enumerate(
            (
                (near_hbm, near_ref), (far_hbm, far_ref),
                (a0_hbm, a0), (n0_hbm, n0), (a1_hbm, a1), (n1_hbm, n1),
            )
        )
    ]
    for copy in loads:
        copy.start()
    group.greet(True, True, others)
    parts = OneWay(
        [(late_ref, got_late)], [(early1_ref, got_early1), (early2_ref, got_early2)], part_sems
    )
    parts.start()
    for copy in loads:
        copy.wait()
    deliver = Deliver(group, stage4, mine, deliver_sems)
    deliver.start(near_ref)
    gradients = push(send, grads_ref.at[section], x_sems, 1, away, "section")

    @pl.when(section == 0)
    def _():
        send[...] = turned(far_ref[...]).astype(LOW)
        gradients.start()

    block[...] = jnp.zeros_like(block)
    for layer, (attn, narrow) in enumerate(((a0, n0), (a1, n1))):
        wide = [attn[0:1, :], attn[1:2, :], narrow[3:4, :], narrow[0:1, :], narrow[1:2, :], narrow[2:3, :]]
        for c in range(block.shape[0]):
            columns = slice(c * width, (c + 1) * width)
            for n, term in enumerate(wide):
                block[c, layer, n : n + 1, :] = term[:, columns]
            for n, term in enumerate((attn[2:3, :width], attn[2:3, 2 * width : 3 * width])):
                block[c, layer, 8 + n : 9 + n, :] = term
            for n in range(narrow.shape[1] // width):
                block[c, layer, 10 + n : 11 + n, :] = narrow[4:5, n * width : (n + 1) * width]
    copies = [
        push(block.at[other, :, pl.ds(0, 8)], land_col.at[n], col_sems, n, other)
        for n, other in enumerate((group.peer, group.diag, group.sib))
    ]
    for copy in copies:
        copy.start()
    for copy in copies:
        copy.wait()
    me = group.me
    block[me, :, :8] = block[me, :, :8] + (land_col[0] + (land_col[1] + land_col[2]))
    swap = push(block.at[me, away], land_x, x_sems, 0, away, "section")
    swap.start()
    deliver.done()

    @pl.when(section == 0)
    def _():
        grads_ref[section] = turned(mine[...]).astype(LOW)

    @pl.when(section == 1)
    def _():
        send[...] = turned(mine[...]).astype(LOW)
        gradients.start()
        grads_ref[section] = turned(far_ref[...]).astype(LOW)

    swap.wait()
    land_z[row] = block[me, section] + land_x[...]
    copies = [
        push(land_z.at[row], land_z.at[row], z_sems, n, other, "row")
        for n, other in enumerate(others)
    ]
    for copy in copies:
        copy.start()
    for copy in copies:
        copy.wait()
    result = land_z[0]
    for n in range(1, land_z.shape[0]):
        result = result + land_z[n]
    sums_ref[...] = result
    gradients.wait()
    parts.wait()


def greet_section():
    barrier = pltpu.get_barrier_semaphore()
    other = 1 - lax.axis_index("section")
    pl.semaphore_signal(barrier, inc=1, device_id={"section": other}, device_id_type=MESH)
    pl.semaphore_wait(barrier, 1)


def cross_kernel(up, part_ref, got_ref, sems):
    greet_section()
    pair = [(part_ref, got_ref)]
    part = OneWay(pair, [], sems) if up else OneWay([], pair, sems)
    part.start()
    part.wait()


def write_kernel(*refs):
    late, far_late, early, far_early = [refs[n : n + 3] for n in (0, 3, 6, 9)]
    sums_ref, results_ref, grads_ref, output_ref, *vector_refs = refs[12:24]
    homes, (own, far, low, results, *held, sems, out_sems) = refs[24:29], refs[29:]
    attend, expand, contract, outputs, inputs = held
    stores = [pltpu.make_async_copy(held[n], homes[n], out_sems.at[n]) for n in range(5)]
    length, width = low.shape[2], output_ref.shape[0]
    moves = [
        pltpu.make_async_copy(grads_ref, low, sems.at[6]),
        pltpu.make_async_copy(results_ref, results, sems.at[7]),
    ]
    for move in moves:
        move.start()
    half = early[0].shape[1]
    section = lax.axis_index("section")

    def pairs(which):
        if which == 0:
            firsts = [(early[n], own.at[n, :, pl.ds(0, half)]) for n in range(3)]
            seconds = [(far_early[n], own.at[n, :, pl.ds(half, half)]) for n in range(3)]
        else:
            firsts = [(late[n], own.at[n]) for n in range(3)]
            seconds = [(far_late[n], far.at[n]) for n in range(3)]
        return [
            pltpu.make_async_copy(source, into, sems.at[n])
            for n, (source, into) in enumerate((*firsts, *seconds))
        ]

    @pl.when(section == 0)
    def _():
        for copy in pairs(0):
            copy.start()
        far[...] = jnp.zeros_like(far)

    @pl.when(section == 1)
    def _():
        for copy in pairs(1):
            copy.start()

    moves[0].wait()
    for n in range(2):
        inputs[:, n * length : (n + 1) * length] = low[n].astype(WIDE)
    stores[4].start()
    moves[1].wait()
    for n in range(2):
        outputs[:, n * length : (n + 1) * length] = results[n]
    stores[3].start()

    @pl.when(section == 0)
    def _():
        for copy in pairs(0):
            copy.wait()

    @pl.when(section == 1)
    def _():
        for copy in pairs(1):
            copy.wait()

    contract[...] = own[2].astype(WIDE) + far[2].astype(WIDE)
    stores[2].start()
    expand[...] = own[1].astype(WIDE) + far[1].astype(WIDE)
    stores[1].start()
    first = own[0].astype(WIDE) + far[0].astype(WIDE)
    for j in range(3):
        attend[j] = first[:, j * width : (j + 1) * width]
    stores[0].start()
    corner = first[:, 3 * width :]
    high = corner.astype(LOW)
    output_ref[...] = turned(high) + turned((corner - high.astype(WIDE)).astype(LOW))
    for n in range(6):
        vector_refs[n][...] = sums_ref[n : n + 1, :]
    vector_refs[6][...] = sums_ref[8:10, :][None]
    for n in range(vector_refs[7].shape[1] // width):
        vector_refs[7][:, n * width : (n + 1) * width] = sums_ref[10 + n : 11 + n, :]
    for store in stores:
        store.wait()


VM = pl.BlockSpec(memory_space=pltpu.VMEM)
ANY = pl.BlockSpec(memory_space=pl.ANY)
PAIRS = pltpu.SemaphoreType.DMA((2, 3 * PARTS))
LOCAL = pltpu.SemaphoreType.DMA((4,))


def shape(dims, kind=LOW):
    return jax.ShapeDtypeStruct(dims, kind)


def launch(
    body, number, rows, in_specs, ins, outs, out_specs, scratch, swaps=(), diagonal=False, across=False, late=(),
):
    n_in, n_out, n = len(ins), len(outs), len(swaps)
    held_in = [i for i in range(n_in) if in_specs[i] is VM]
    held_out = [i for i in range(n_out) if out_specs[i] is VM]

    def kernel(*refs):
        refs = list(refs)
        takes, sources = refs[:n_in], refs[n_in : n_in + n]
        gives = refs[n_in + n : n_in + n + n_out]
        lands = refs[n_in + n + n_out : n_in + 2 * n + n_out]
        rest = refs[n_in + 2 * n + n_out :]
        own, rest = rest[: len(scratch)], rest[len(scratch) :]
        in_held, rest = rest[: len(held_in)], rest[len(held_in) :]
        out_held, rest = rest[: len(held_out)], rest[len(held_out) :]
        in_sems, out_sems, swap_sems = rest
        group = Group(rows)
        for k, i in enumerate(held_in):
            group.loads[i] = pltpu.make_async_copy(takes[i], in_held[k], in_sems.at[k])
            group.loads[i].start()
            takes[i] = in_held[k]
        for k, i in enumerate(held_out):
            group.stores[i] = pltpu.make_async_copy(out_held[k], gives[i], out_sems.at[k])
            gives[i] = out_held[k]
        group.greet(n or across, diagonal)
        other = 1 - lax.axis_index("section")
        copies = [
            push(source, land, swap_sems, i, other, "section")
            for i, (source, land) in enumerate(zip(sources, lands))
        ]
        for copy in copies:
            copy.start()
        group.need(*[i for i in held_in if i not in late])
        body(group, *takes, *gives, *own)
        group.emit(*[i for i in held_out if i not in group.begun])
        for copy in copies:
            copy.wait()
        for i in held_out:
            group.stores[i].wait()

    results = pl.pallas_call(
        kernel,
        out_shape=(*outs, *[shape(s.shape, s.dtype) for s in swaps]),
        in_specs=[ANY] * (n_in + n),
        out_specs=(ANY,) * (n_out + n),
        scratch_shapes=[
            *scratch,
            *[pltpu.VMEM(ins[i].shape, ins[i].dtype) for i in held_in],
            *[pltpu.VMEM(outs[i].shape, outs[i].dtype) for i in held_out],
            pltpu.SemaphoreType.DMA((len(held_in),)),
            pltpu.SemaphoreType.DMA((len(held_out),)),
            pltpu.SemaphoreType.DMA((2, max(n, 1))),
        ],
        compiler_params=pltpu.CompilerParams(
            collective_id=number, has_side_effects=True, vmem_limit_bytes=GRANT
        ),
        cost_estimate=pl.CostEstimate(flops=int(3e10), bytes_accessed=30 * MEBI, transcendentals=0),
    )(*ins, *swaps)
    return results[:n_out], results[n_out:]


def start_call(number, tokens, cotangent, small, expand, contract, columns):
    width = small.shape[1]
    size = width * columns
    kinds = small.shape[0]
    outs = (shape((LENGTH, size)), shape((LENGTH, size)), shape((2, columns, kinds, width)), shape(expand.shape), shape(contract.shape))
    low = pltpu.VMEM((columns, width, LENGTH), LOW)
    high = pltpu.VMEM((columns, LENGTH, width), LOW)
    vectors = pltpu.VMEM((columns, kinds, width), LOW)
    return pl.pallas_call(
        start_kernel,
        out_shape=outs,
        in_specs=[ANY] * 5,
        out_specs=(VM, VM, VM, ANY, ANY),
        scratch_shapes=[
            low, high, vectors, vectors, PAIRS, PAIRS,
            pltpu.SemaphoreType.DMA((2, 3 * PARTS + 3)), LOCAL,
        ],
        compiler_params=pltpu.CompilerParams(
            collective_id=number, has_side_effects=True, vmem_limit_bytes=GRANT
        ),
        cost_estimate=pl.CostEstimate(flops=int(3e10), bytes_accessed=30 * MEBI, transcendentals=0),
    )(tokens, cotangent, small, expand, contract)


def attend_call(number, x, pair, vec, bias, rows, width, swaps):
    size = vec.shape[1]
    heads = width // HEAD
    outs = (
        shape((LENGTH, size)),
        shape((3 * heads, LENGTH, HEAD)),
        shape((LENGTH, width)),
        shape((8, LENGTH), WIDE),
        shape((rows, size), WIDE),
        shape((rows, size)),
    )
    scratch = [
        pltpu.VMEM((size, 4 * width), LOW),
        pltpu.VMEM((heads, LENGTH, HEAD), LOW),
        *scatter_scratch(rows, size), LOCAL,
    ]
    return launch(
        functools.partial(attend_kernel, heads),
        number, rows, [VM, ANY, ANY, VM, VM], (x, *pair, vec, bias), outs, (VM,) * 6, scratch, swaps,
    )


def widen_call(number, second, pair, bias, grad, swaps):
    rows, size = second.shape
    wide = bias.shape[1]
    last = grad is not None
    ins, in_specs = [second, *pair, bias], [VM, ANY, ANY, VM]
    outs = [shape((LENGTH, size)), shape((LENGTH, wide)), shape((LENGTH, wide))]
    if last:
        ins, in_specs, outs = ins + [grad], in_specs + [VM], outs + [shape((size, wide))]
    scratch = [pltpu.VMEM((size, wide), LOW), PAIRS, LOCAL]
    return launch(
        functools.partial(widen_kernel, last),
        number, rows, in_specs, ins, outs, (VM,) * len(outs), scratch, swaps, late=(4,),
    )


def contract_call(number, active, hidden, pair, vec, swaps):
    rows, size = hidden.shape
    wide = active.shape[1]
    scratch = [pltpu.VMEM((size, wide), LOW), *scatter_scratch(rows, size), PAIRS, LOCAL]
    return launch(
        contract_kernel, number, rows, [VM, VM, ANY, ANY, VM], (active, hidden, *pair, vec),
        [shape((rows, size)), shape((LENGTH, size))], (VM, VM), scratch, swaps, late=(1,),
    )


def late_expand_call(number, active, hidden, contract, expand, grad, slope, second, vec, swaps):
    rows, size = hidden.shape
    wide = slope.shape[1]
    outs = [
        shape((rows, size), WIDE), shape((rows, size)), shape((8, size), WIDE),
        shape((size, wide)), shape((rows, size)),
    ]
    scratch = [
        pltpu.VMEM((size, wide), LOW),
        pltpu.VMEM((size, wide), LOW),
        pltpu.VMEM((LENGTH, wide), LOW),
        *scatter_scratch(rows, size), *scatter_scratch(rows, size), LOCAL,
    ]
    return launch(
        late_expand_kernel,
        number, rows, [VM, VM, ANY, ANY, ANY, ANY, VM, VM, VM, VM],
        (active, hidden, *contract, *expand, grad, slope, second, vec),
        outs, [VM] * 5, scratch, swaps, late=(1, 6, 7, 8),
    )


def expand_back_call(number, grad, contract, expand, slope, active, second, hidden, vec, swaps):
    rows, size = hidden.shape
    wide = slope.shape[1]
    half = wide // 2
    outs = [
        shape((rows, size), WIDE), shape((rows, size)), shape((8, size), WIDE),
        shape((size, half)), shape((size, half)), shape((LENGTH, size)), shape((size, half)),
    ]
    scratch = [
        pltpu.VMEM((size, wide), LOW),
        pltpu.VMEM((size, wide), LOW),
        pltpu.VMEM((LENGTH, wide), LOW),
        *scatter_scratch(rows, size), PAIRS, LOCAL,
        pltpu.VMEM((2, size, half), LOW), pltpu.VMEM((size, half), LOW),
        pltpu.SemaphoreType.DMA((2, size // TILE)),
    ]
    return launch(
        expand_back_kernel,
        number, rows, [VM, ANY, ANY, ANY, ANY, VM, VM, VM, VM, VM],
        (grad, *contract, *expand, slope, active, second, hidden, vec),
        outs, [VM] * 6 + [ANY], scratch, swaps, False, True, late=(5, 6, 7, 8),
    )


def scores_scratch(size, width, heads):
    return [
        pltpu.VMEM((size, 4 * width), LOW),
        pltpu.VMEM((LENGTH, size), LOW),
        pltpu.VMEM((heads, LENGTH, HEAD), LOW),
        pltpu.VMEM((8, LENGTH), WIDE),
        pltpu.VMEM((heads, LENGTH, HEAD), LOW),
        pltpu.VMEM((heads, LENGTH, HEAD), WIDE),
        pltpu.VMEM((heads, LENGTH, HEAD), WIDE),
    ]


def late_attend_call(number, low, grad, x_own, pair, normed, heads_all, o, lse, vec, result, y, swaps):
    rows, size = grad.shape
    width = o.shape[1]
    heads = width // HEAD
    outs = (shape((rows, size)), shape((8, size), WIDE), shape((2, width, LENGTH)), shape((size, 4 * width)))
    scratch = [
        *scores_scratch(size, width, heads),
        pltpu.VMEM((LENGTH, 3 * width), LOW),
        pltpu.VMEM((size, 4 * width), LOW),
        pltpu.VMEM((size, width), LOW),
        pltpu.VMEM((LENGTH, width), LOW),
        pltpu.VMEM((LENGTH, width), LOW),
        pltpu.VMEM((LENGTH // rows, rows, width), LOW),
        *scatter_scratch(rows, size), PAIRS,
        pltpu.SemaphoreType.DMA((2, 3)), pltpu.SemaphoreType.DMA((2, 2)), LOCAL,
    ]
    return launch(
        functools.partial(late_attend_kernel, heads),
        number, rows, [VM, VM, VM, ANY, ANY, VM, VM, VM, VM, VM, VM, VM],
        (low, grad, x_own, *pair, normed, heads_all, o, lse, vec, result, y),
        outs, (VM, VM, VM, ANY), scratch, swaps, True, True, late=(1, 2, 5, 6, 7, 8, 10, 11),
    )


def scores_back_call(number, low, pair, heads_all, o, lse, keep, send):
    rows, size = low.shape
    width = o.shape[1]
    heads = width // HEAD
    outs = (shape((LENGTH, 3 * width)), shape((size, width)), shape(keep.shape))
    scratch = [
        *scores_scratch(size, width, heads),
        pltpu.VMEM(keep.shape, LOW),
        PAIRS, LOCAL, pltpu.SemaphoreType.DMA((2, 1)),
    ]
    return launch(
        functools.partial(scores_back_kernel, heads),
        number, rows, [VM, ANY, ANY, VM, VM, VM, VM, ANY], (low, *pair, heads_all, o, lse, keep, send),
        outs, (VM, VM, ANY), scratch, (), False, True, late=(3, 4, 5, 6),
    )[0]


def attend_back_call(number, mixed, outer, grad, x_own, pair, normed, vec):
    rows, size = grad.shape
    width = outer.shape[1]
    half = 2 * width
    outs = (shape((size, half)), shape((rows, size)), shape((8, size), WIDE))
    scratch = [
        pltpu.VMEM((size, 4 * width), LOW),
        pltpu.VMEM((2, size, half), LOW),
        pltpu.VMEM((size, half), LOW),
        *scatter_scratch(rows, size), LOCAL, pltpu.SemaphoreType.DMA((2, size // TILE)),
    ]
    return launch(
        attend_back_kernel,
        number, rows, [VM, VM, VM, VM, ANY, ANY, VM, VM],
        (mixed, outer, grad, x_own, *pair, normed, vec), outs, (ANY, VM, VM), scratch, (), False, True,
        late=(1, 2, 3, 6),
    )[0]


def finish_call(number, parts, near, far, sums, row_count):
    rows, size = near.shape
    length, width = far.shape
    columns = length // rows
    outs = (
        shape((2, width, length)),
        shape((16, width), WIDE),
        *[shape(part.shape) for part in parts],
    )
    scratch = [
        pltpu.VMEM(near.shape, LOW),
        pltpu.VMEM(far.shape, LOW),
        *[pltpu.VMEM(s.shape, WIDE) for s in sums],
        pltpu.VMEM((length, width), LOW),
        pltpu.VMEM((columns, rows, width), LOW),
        pltpu.VMEM((columns, 2, 16, width), WIDE),
        pltpu.VMEM((3, 2, 8, width), WIDE),
        pltpu.VMEM((16, width), WIDE),
        pltpu.VMEM((row_count, 16, width), WIDE),
        pltpu.VMEM((width, length), LOW),
        pltpu.SemaphoreType.DMA((2, 3)),
        pltpu.SemaphoreType.DMA((2, 3)),
        pltpu.SemaphoreType.DMA((2, 2)),
        pltpu.SemaphoreType.DMA((2, row_count)),
        pltpu.SemaphoreType.DMA((2, 3)),
        pltpu.SemaphoreType.DMA((6,)),
    ]
    return pl.pallas_call(
        finish_kernel,
        out_shape=outs,
        in_specs=[ANY] * 9,
        out_specs=(VM, VM) + (ANY,) * 3,
        scratch_shapes=scratch,
        compiler_params=pltpu.CompilerParams(
            collective_id=number, has_side_effects=True, vmem_limit_bytes=GRANT
        ),
        cost_estimate=pl.CostEstimate(flops=int(3e10), bytes_accessed=30 * MEBI, transcendentals=0),
    )(*parts, near, far, *sums)


def cross_call(number, up, part):
    return pl.pallas_call(
        functools.partial(cross_kernel, up),
        out_shape=shape(part.shape),
        in_specs=[ANY],
        out_specs=ANY,
        scratch_shapes=[pltpu.SemaphoreType.DMA((2, 1))],
        compiler_params=pltpu.CompilerParams(
            collective_id=number, has_side_effects=True, vmem_limit_bytes=GRANT
        ),
        cost_estimate=pl.CostEstimate(flops=int(1e10), bytes_accessed=10 * MEBI, transcendentals=0),
    )(part)


def write_call(late, far_late, early, far_early, sums, wide, results, grads):
    rows, size = late[0].shape
    _, width, length = grads.shape
    large = (
        shape((3, rows, width), WIDE), shape((rows, size), WIDE), shape((rows, size), WIDE),
        shape((width, 2 * length)), shape((width, 2 * length), WIDE),
    )
    return pl.pallas_call(
        write_kernel,
        out_shape=(
            shape((width, rows), WIDE),
            *[shape((1, width), WIDE)] * 6, shape((1, 2, width), WIDE), shape((1, wide), WIDE), *large,
        ),
        in_specs=[ANY] * 12 + [VM, ANY, ANY],
        out_specs=(VM,) * 9 + (ANY,) * 5,
        scratch_shapes=[pltpu.VMEM((3, rows, size), LOW)] * 2
        + [pltpu.VMEM(grads.shape, LOW), pltpu.VMEM(results.shape, LOW)]
        + [pltpu.VMEM(s.shape, s.dtype) for s in large]
        + [pltpu.SemaphoreType.DMA((8,)), pltpu.SemaphoreType.DMA((5,))],
        compiler_params=pltpu.CompilerParams(vmem_limit_bytes=GRANT),
    )(*late, *far_late, *early, *far_early, sums, results, grads)


def swap_sections(value):
    return lax.ppermute(value, "section", [(0, 1), (1, 0)])


def on_device(
    tokens,
    cotangent,
    first_gain,
    first_shift,
    attend_weight,
    attend_bias,
    output_weight,
    output_bias,
    second_gain,
    second_shift,
    expand_weight,
    expand_bias,
    contract_weight,
    contract_bias,
):
    section = lax.axis_index("section")
    column = lax.axis_index("col")
    first_section = section == 0
    columns = lax.axis_size("col")
    width = tokens.shape[1]
    size = width * columns
    rows = LENGTH // columns

    def pick(early, later):
        return jnp.where(first_section, early, later)

    block_rows = attend_weight.shape[1]
    units = (
        jnp.concatenate(
            [attend_weight[0].reshape(block_rows, 3 * width), output_weight[0].T], axis=1
        ),
        expand_weight[0],
        contract_weight[0].T,
    )
    kept_blocks, sent_blocks = [], []
    for unit in units:
        half = unit.shape[1] // 2
        low, high = unit[:, :half], unit[:, half:]
        kept_blocks.append(pick(low, high))
        sent_blocks.append(pick(high, low))

    small = jnp.concatenate(
        [
            first_gain,
            first_shift,
            output_bias,
            second_gain,
            second_shift,
            contract_bias,
            attend_bias[0],
            expand_bias[0].reshape(-1, width),
        ],
        0,
    )
    filled = small.shape[0]
    small = jnp.pad(small, ((0, -filled % (16 * PARTS)), (0, 0)))
    got_attend = swap_sections(sent_blocks[0])
    got_attend, sent_expand = lax.optimization_barrier((got_attend, sent_blocks[1]))
    x0_full, gy_full, vectors, got_expand, got_contract = start_call(
        1, tokens.T, cotangent, small, sent_expand, units[2], columns
    )

    def gather_blocks(block):
        return lax.all_gather(block, "row", axis=0, tiled=True)

    half = units[2].shape[1] // 2
    mats = [[], []]
    for own, got in ((kept_blocks[0], got_attend), (kept_blocks[1], got_expand)):
        for layer, block in enumerate((pick(own, got), pick(got, own))):
            mats[layer].append(gather_blocks(block))
    mats[0].append(gather_blocks(pick(kept_blocks[2], got_contract[:, half:])))
    mats[1].append(gather_blocks(pick(got_contract, units[2])))
    vectors = vectors.astype(WIDE)
    wide_vectors = jnp.swapaxes(vectors[:, :, :6], 1, 2).reshape(2, 6, size)
    wide_vectors = jnp.pad(wide_vectors, ((0, 0), (0, 2), (0, 0)))
    own_vectors = lax.dynamic_index_in_dim(vectors, column, 1, keepdims=False)
    attend_biases = jnp.stack(
        [own_vectors[:, 6], jnp.zeros_like(own_vectors[:, 6]), own_vectors[:, 7]], 1
    ).reshape(2, 1, 3 * width)
    expand_biases = own_vectors[:, 8:filled].reshape(2, 1, -1)

    def own_rows(full):
        return lax.dynamic_slice_in_dim(full, column * rows, rows, 0)

    def own_features(full):
        return lax.dynamic_slice_in_dim(full, column * width, width, 1)

    attn = (mats[0][0], swap_sections(mats[0][0]))
    x = x0_full
    kept, pairs = [], []
    owns = [own_rows(x0_full)]
    for layer in range(2):
        last = layer == 1
        vec = wide_vectors[layer]
        (normed, heads, o, lse, hidden, second_own), (other,) = attend_call(
            2 + 3 * layer, x, attn, vec, attend_biases[layer], rows, width, [mats[layer][1]]
        )
        expand = (mats[layer][1], other)
        outs, others = widen_call(
            3 + 3 * layer, second_own, expand, expand_biases[layer],
            gy_full if last else None, [] if last else [mats[0][2]],
        )
        second, active, slope = outs[:3]
        contract = (mats[layer][2], mats[layer][2] if last else others[0])
        if last:
            c1 = outs[3]
        pairs.append((attn, expand, contract))
        kept.append((normed, heads, o, lse, hidden, second, active, slope))
        if not last:
            (own, x), others = contract_call(4, active, hidden, contract, vec, [mats[1][0]])
            owns.append(own)
            attn = (mats[1][0], others[0])
    y0 = own_features(x)

    def scatter(total):
        return lax.psum_scatter(total, "row", scatter_dimension=0, tiled=True)

    def tie(value, then):
        return lax.optimization_barrier((value, then))

    attn, expand, contract = pairs[1]
    normed, heads, o, lse, hidden, second, active, slope = kept[1]
    (grad_hidden, low, expand_sums1, e1, result), _ = late_expand_call(
        8, active, hidden, contract, expand, gy_full, slope, second, wide_vectors[1], []
    )
    (gx1_own, attend_sums1, layer_outputs, w1), _ = late_attend_call(
        10, low, grad_hidden, owns[1], attn, normed, heads, o, lse, wide_vectors[1], result, y0, []
    )

    attn, expand, contract = pairs[0]
    normed, heads, o, lse, hidden, second, active, slope = kept[0]
    part_c1 = scatter(c1)
    (grad_hidden, low, expand_sums0, ek0, es0, gx1_full, total_c0), (far_c1,) = expand_back_call(
        12, gx1_own, contract, expand, slope, active, second, hidden, wide_vectors[0], [part_c1]
    )
    part_e1, low = tie(scatter(e1), low)
    mixed, outer, total_e0 = scores_back_call(14, low, attn, heads, o, lse, ek0, es0)
    part_w1, mixed = tie(scatter(w1), mixed)
    part_e1, mixed = tie(part_e1, mixed)
    far_e1, mixed = tie(cross_call(18, True, part_e1), mixed)
    part_c0, mixed = tie(scatter(total_c0), mixed)
    total_w0, gx0_own, attend_sums0 = attend_back_call(
        15, mixed, outer, grad_hidden, owns[0], attn, normed, wide_vectors[0]
    )
    part_e0, gx0_own = tie(scatter(total_e0), gx0_own)
    input_grads, small_grads, far_w1, far_c0, far_e0 = finish_call(
        16,
        (part_w1, part_c0, part_e0),
        gx0_own,
        own_features(gx1_full),
        (attend_sums0, expand_sums0, attend_sums1, expand_sums1),
        lax.axis_size("row"),
    )

    part_w0, small_grads = tie(scatter(total_w0), small_grads)
    far_w0 = cross_call(17, False, part_w0)
    output_part, *vector_grads, attend_part, expand_part, contract_part, layer_outputs, input_grads = write_call(
        (part_w1, part_e1, part_c1),
        (far_w1, far_e1, far_c1),
        (part_w0, part_e0, part_c0),
        (far_w0, far_e0, far_c0),
        small_grads,
        expand_bias.shape[1],
        layer_outputs,
        input_grads,
    )
    return (
        layer_outputs.T[None],
        input_grads.T[None],
        vector_grads[0],
        vector_grads[1],
        jnp.swapaxes(attend_part, 0, 1)[None],
        vector_grads[6],
        output_part[None],
        vector_grads[2],
        vector_grads[3],
        vector_grads[4],
        expand_part[None],
        vector_grads[7],
        contract_part.T[None],
        vector_grads[5],
    )


def solution(mesh):
    return jax.shard_map(
        on_device,
        mesh=mesh,
        in_specs=(
            P("row", "col"),
            P("row", "col"),
            P("section", "col"),
            P("section", "col"),
            P("section", "row", None, "col"),
            P("section", None, "col"),
            P("section", "col", "row"),
            P("section", "col"),
            P("section", "col"),
            P("section", "col"),
            P("section", "row", "col"),
            P("section", "col"),
            P("section", "col", "row"),
            P("section", "col"),
        ),
        out_specs=(
            P("section", "row", "col"),
            P("section", "row", "col"),
            P("section", "col"),
            P("section", "col"),
            P("section", "row", None, "col"),
            P("section", None, "col"),
            P("section", "col", "row"),
            P("section", "col"),
            P("section", "col"),
            P("section", "col"),
            P("section", "row", "col"),
            P("section", "col"),
            P("section", "col", "row"),
            P("section", "col"),
        ),
        check_vma=False,
    )
```

```python
import functools

import jax
import jax.numpy as jnp
from jax import lax
from jax.experimental import pallas as pl
from jax.experimental.pallas import tpu as pltpu
from jax.sharding import PartitionSpec as P

HEAD = 64
LENGTH = 1024
EPS = 1e-05
LOW = jnp.bfloat16
WIDE = jnp.float32
MESH = pl.DeviceIdType.MESH
PARTS = 2
TILE = 256
MEBI = 1024 * 1024
GRANT = 58 * MEBI


def nn(left, right):
    return lax.dot_general(left, right, (((1,), (0,)), ((), ())), preferred_element_type=WIDE)


def nt(left, right):
    return lax.dot_general(left, right, (((1,), (1,)), ((), ())), preferred_element_type=WIDE)


def tn(left, right):
    return lax.dot_general(left, right, (((0,), (0,)), ((), ())), preferred_element_type=WIDE)


def turned(values):
    width = values.shape[1]
    unit = (
        lax.broadcasted_iota(jnp.int32, (width, width), 0) == lax.broadcasted_iota(jnp.int32, (width, width), 1)
    ).astype(LOW)
    return nt(unit, values)


def turned_back(values):
    height = values.shape[0]
    unit = (
        lax.broadcasted_iota(jnp.int32, (height, height), 0) == lax.broadcasted_iota(jnp.int32, (height, height), 1)
    ).astype(LOW)
    return tn(values, unit)


def normalise(values):
    center = jnp.mean(values, axis=1, keepdims=True)
    centred = values - center
    scale = lax.rsqrt(jnp.mean(centred * centred, axis=1, keepdims=True) + EPS)
    return centred * scale, scale


def norm_backward(grad, hat, scale, gain):
    scaled = grad * gain
    mean_one = jnp.mean(scaled, axis=1, keepdims=True)
    mean_two = jnp.mean(scaled * hat, axis=1, keepdims=True)
    return scale * (scaled - mean_one - hat * mean_two)


class Group:
    def __init__(self, rows):
        self.me = lax.axis_index("col")
        chip, core = self.me // 2, self.me % 2
        self.sib = chip * 2 + 1 - core
        self.peer = (1 - chip) * 2 + core
        self.diag = (1 - chip) * 2 + 1 - core
        self.rows = rows
        self.part = rows // PARTS
        self.loads, self.stores, self.begun = {}, {}, set()

    def need(self, *places):
        for place in places:
            self.loads[place].wait()

    def emit(self, *places):
        for place in places:
            self.stores[place].start()
            self.begun.add(place)

    def greet(self, swaps, diagonal, rows=()):
        barrier = pltpu.get_barrier_semaphore()
        others = [{"col": self.sib}, {"col": self.peer}]
        if diagonal:
            others.append({"col": self.diag})
        if swaps:
            others.append({"section": 1 - lax.axis_index("section")})
        others += [{"row": row} for row in rows]
        for other in others:
            pl.semaphore_signal(barrier, inc=1, device_id=other, device_id_type=MESH)
        pl.semaphore_wait(barrier, len(others))

    def slab(self, owner, j):
        return pl.ds(pl.multiple_of(owner * self.rows + j * self.part, self.part), self.part)

    def chunk(self, owner):
        return pl.ds(pl.multiple_of(owner * self.rows, self.rows), self.rows)


def push(src, dst, sems, slot, target, axis="col"):
    return pltpu.make_async_remote_copy(
        src_ref=src,
        dst_ref=dst,
        send_sem=sems.at[0, slot],
        recv_sem=sems.at[1, slot],
        device_id={axis: target},
        device_id_type=MESH,
    )


class Gather:
    def __init__(self, group, full, sems, blocks=False):
        self.group, self.full, self.sems, self.blocks = group, full, sems, blocks
        self.over, self.near, self.relayed = [], [], []

    def piece(self, owner, j):
        if not self.blocks:
            return self.full.at[self.group.slab(owner, j)]
        part = self.full.shape[1] // PARTS
        return self.full.at[owner, pl.ds(j * part, part)]

    def start_part(self, j):
        g = self.group
        piece = self.piece(g.me, j)
        self.over.append(push(piece, piece, self.sems, j, g.peer))
        self.near.append(push(piece, piece, self.sems, PARTS + j, g.sib))
        self.over[-1].start()
        self.near[-1].start()

    def start(self):
        for j in range(PARTS):
            self.start_part(j)

    def sibling(self):
        for copy in self.near:
            copy.wait_recv()

    def relay(self):
        g = self.group
        for j in range(PARTS):
            self.over[j].wait_recv()
            piece = self.piece(g.peer, j)
            self.relayed.append(push(piece, piece, self.sems, 2 * PARTS + j, g.sib))
            self.relayed[-1].start()

    def diagonal(self):
        for copy in self.relayed:
            copy.wait_recv()

    def done(self):
        for copy in self.over + self.near + self.relayed:
            copy.wait_send()

    def each(self, body, first=None):
        g = self.group
        if not self.over:
            self.start()
        if first is not None:
            first()
        body(g.me)
        self.sibling()
        body(g.sib)
        self.relay()
        body(g.peer)
        self.diagonal()
        body(g.diag)
        self.done()


class Scatter:
    def __init__(self, group, stage, land, total, sems):
        self.group, self.stage, self.land, self.total, self.sems = group, stage, land, total, sems

    def start(self, part):
        g, stage, land = self.group, self.stage, self.land
        self.first, self.over, self.near = [], [], []
        def split(owner):
            whole = part(owner)
            return [whole[j * g.part : (j + 1) * g.part] for j in range(PARTS)]

        for j, mine in enumerate(split(g.diag)):
            stage[0, j] = mine.astype(LOW)
            self.first.append(push(stage.at[0, j], land.at[0, j], self.sems, j, g.sib))
            self.first[-1].start()
        for j, mine in enumerate(split(g.peer)):
            self.first[j].wait_recv()
            stage[1, j] = (mine + land[0, j].astype(WIDE)).astype(LOW)
            self.over.append(push(stage.at[1, j], land.at[1, j], self.sems, PARTS + j, g.peer))
            self.over[-1].start()
        for j, mine in enumerate(split(g.sib)):
            stage[2, j] = mine.astype(LOW)
            self.near.append(push(stage.at[2, j], land.at[2, j], self.sems, 2 * PARTS + j, g.sib))
            self.near[-1].start()
        for j, mine in enumerate(split(g.me)):
            self.total[j] = mine

    def take(self, j):
        self.near[j].wait_recv()
        self.over[j].wait_recv()
        land = self.land
        return self.total[j] + (land[1, j].astype(WIDE) + land[2, j].astype(WIDE))

    def done(self):
        for copy in self.first + self.over + self.near:
            copy.wait_send()


class Deliver:
    def __init__(self, group, stage, out, sems):
        self.group, self.stage, self.out, self.sems = group, stage, out, sems

    def start(self, rows_ref):
        g, width = self.group, self.out.shape[1]
        for c in range(self.stage.shape[0]):
            self.stage[c] = rows_ref[:, c * width : (c + 1) * width]
        place = self.out.at[g.chunk(g.me)]
        self.copies = [
            push(self.stage.at[other], place, self.sems, n, other)
            for n, other in enumerate((g.peer, g.diag, g.sib))
        ]
        for copy in self.copies:
            copy.start()
        self.out[g.chunk(g.me), :] = self.stage[g.me]

    def done(self):
        for copy in self.copies:
            copy.wait()


class OneWay:
    def __init__(self, up, down, sems):
        self.section = lax.axis_index("section")
        both = [*up, *down]
        copies = [
            push(source, into, sems, n, 1 - self.section, "section")
            for n, (source, into) in enumerate(both)
        ]
        self.up, self.down = copies[: len(up)], copies[len(up) :]

    def each(self, first, second):
        @pl.when(self.section == 0)
        def _():
            first(self.up)
            second(self.down)

        @pl.when(self.section == 1)
        def _():
            first(self.down)
            second(self.up)

    def start(self):
        self.each(lambda copies: [copy.start() for copy in copies], lambda copies: None)

    def wait(self):
        self.each(
            lambda copies: [copy.wait_send() for copy in copies],
            lambda copies: [copy.wait_recv() for copy in copies],
        )


def scatter_scratch(rows, width):
    part = rows // PARTS
    return [
        pltpu.VMEM((3, PARTS, part, width), LOW),
        pltpu.VMEM((3, PARTS, part, width), LOW),
        pltpu.VMEM((PARTS, part, width), WIDE),
        pltpu.SemaphoreType.DMA((2, 3 * PARTS)),
    ]


class Halves:
    def __init__(self, pair, whole, sems, slot):
        if pair[0].shape[1] == whole.shape[1]:
            self.copies = [pltpu.make_async_copy(pair[0], whole, sems.at[slot])]
            return
        section = lax.axis_index("section")
        half = whole.shape[1] // 2
        self.copies = []
        for n, place in enumerate((section, 1 - section)):
            columns = pl.ds(pl.multiple_of(place * half, half), half)
            self.copies.append(
                pltpu.make_async_copy(pair[n], whole.at[:, columns], sems.at[slot + n])
            )

    def start(self):
        for copy in self.copies:
            copy.start()

    def wait(self):
        for copy in self.copies:
            copy.wait()


class Trade:
    def __init__(self, keep, send, got, sems):
        self.keep, self.send, self.got, self.sems = keep, send, got, sems
        self.tiles = keep.shape[0] // TILE

    def copy(self, n):
        rows = pl.ds(pl.multiple_of(n * TILE, TILE), TILE)
        return push(
            self.send.at[rows], self.got.at[rows], self.sems, n, 1 - lax.axis_index("section"), "section"
        )

    def start(self, make):
        @pl.loop(0, self.tiles)
        def _(n):
            make(pl.ds(pl.multiple_of(n * TILE, TILE), TILE))
            self.copy(n).start()

    def finish(self):
        @pl.loop(0, self.tiles)
        def _(n):
            self.copy(n).wait()

        add_into(self.keep, self.got)


def add_into(keep_ref, got_ref):
    @pl.loop(0, keep_ref.shape[0] // TILE)
    def _(n):
        rows = pl.ds(pl.multiple_of(n * TILE, TILE), TILE)
        keep_ref[rows, :] = (keep_ref[rows, :].astype(WIDE) + got_ref[rows, :].astype(WIDE)).astype(LOW)


def causal_scores(scores):
    size = scores.shape[1]
    keep = lax.broadcasted_iota(jnp.int32, (size, size), 0) <= lax.broadcasted_iota(
        jnp.int32, (size, size), 1
    )
    begin = scores.shape[0] - size
    last = jnp.where(keep, scores[begin:], -1000000000.0)
    return last if begin == 0 else jnp.concatenate([scores[:begin], last], 0)


def attention_out(owner, size, heads_ref, o3, lse_ref, heads):
    for i in range(heads_ref.shape[1] // size):
        rows, finish = slice(i * size, (i + 1) * size), (i + 1) * size

        @pl.when(owner == i)
        def _():
            @pl.loop(0, heads)
            def _(h):
                scores = causal_scores(nt(heads_ref[heads + h, :finish, :], heads_ref[h, rows, :]))
                highest = jnp.max(scores, axis=0, keepdims=True)
                powers = jnp.exp(scores - highest)
                summed = jnp.sum(powers, axis=0, keepdims=True)
                mixed = tn(heads_ref[2 * heads + h, :finish, :], powers.astype(LOW))
                o3[h, rows, :] = (mixed / summed).T.astype(LOW)
                lse_ref[pl.ds(h, 1), rows] = highest + jnp.log(summed)


def attention_back(owner, size, heads_ref, go3, lse_ref, dots_ref, g3, key_acc, value_acc, heads):
    for i in range(heads_ref.shape[1] // size):
        rows, finish = slice(i * size, (i + 1) * size), (i + 1) * size

        @pl.when(owner == i)
        def _():
            @pl.loop(0, heads)
            def _(h):
                queries = heads_ref[h, rows, :]
                keys = heads_ref[heads + h, :finish, :]
                grads = go3[h, rows, :]
                probs = jnp.exp(causal_scores(nt(keys, queries) - lse_ref[pl.ds(h, 1), rows]))
                grad_probs = nt(heads_ref[2 * heads + h, :finish, :], grads)
                grad_scores = (probs * (grad_probs - dots_ref[pl.ds(h, 1), rows])).astype(LOW)
                g3[h, rows, :] = (tn(grad_scores, keys) * HEAD ** (-0.5)).astype(LOW)
                key_acc[h, :finish, :] += nn(grad_scores, queries)
                value_acc[h, :finish, :] += nn(probs.astype(LOW), grads)


def start_kernel(
    tokens_ref, cotangent_ref, small_ref, expand_ref, contract_ref,
    x_ref, g_ref, vectors_ref, got_expand_ref, got_contract_ref,
    x4, g4, s4, other4, x_sems, g_sems, s_sems, local_sems,
):
    section = lax.axis_index("section")
    group = Group(x_ref.shape[0] // 4)
    length = x_ref.shape[0]
    loads = []
    rows = pl.ds(pl.multiple_of(section * length, length), length)
    sources = ((tokens_ref.at[:, rows], x4), (cotangent_ref.at[rows], g4), (small_ref, s4))
    for n, (source, into) in enumerate(sources):
        loads.append(pltpu.make_async_copy(source, into.at[group.me], local_sems.at[n]))
        loads[-1].start()
    group.greet(True, False)
    blocks = [
        push(source, into, s_sems, 3 * PARTS + 1 + n, 1 - section, "section")
        for n, (source, into) in enumerate(((expand_ref, got_expand_ref), (contract_ref, got_contract_ref)))
    ]
    blocks[0].start()
    gathers = [Gather(group, s4, s_sems, True), Gather(group, x4, x_sems, True), Gather(group, g4, g_sems, True)]
    for gather, load in zip(gathers, (loads[2], loads[0], loads[1])):
        load.wait()
        gather.start()
    width = x_ref.shape[1] // 4
    for gather, blocks4, full_ref in ((gathers[0], None, None), (gathers[1], x4, x_ref), (gathers[2], g4, g_ref)):
        gather.sibling()
        gather.relay()
        gather.diagonal()
        if blocks4 is None:
            swap = push(s4, other4, s_sems, 3 * PARTS, 1 - section, "section")
            swap.start()
            blocks[1].start()
        else:
            for c in range(blocks4.shape[0]):
                block = blocks4[c]
                if block.shape[0] == width:
                    block = turned_back(block).astype(LOW)
                full_ref[:, c * width : (c + 1) * width] = block
    swap.wait()
    for block in blocks:
        block.wait()
    vectors_ref[section] = s4[...]
    vectors_ref[1 - section] = other4[...]
    for gather in gathers:
        gather.done()


def attend_kernel(
    heads, group, x_ref, mine_ref, other_ref, vec_ref, bias_ref,
    normed_ref, heads_ref, o_ref, lse_ref, hidden_ref, second_ref,
    weight, o3, stage, land, total, scatter_sems, local_sems,
):
    width = o_ref.shape[1]
    halves = Halves((mine_ref, other_ref), weight, local_sems, 0)
    halves.start()
    lse_ref[...] = jnp.zeros_like(lse_ref)
    halves.wait()

    @pl.loop(0, LENGTH // group.rows)
    def _(owner):
        rows = group.chunk(owner)
        hat, _ = normalise(x_ref[rows, :].astype(WIDE))
        normed = (hat * vec_ref[0:1, :] + vec_ref[1:2, :]).astype(LOW)
        normed_ref[rows, :] = normed
        mixed = nn(normed, weight[:, : 3 * width]) + bias_ref[...]
        for j in range(3 * heads):
            piece = mixed[:, j * HEAD : (j + 1) * HEAD]
            if j < heads:
                piece = piece * HEAD ** (-0.5)
            heads_ref[j, rows, :] = piece.astype(LOW)

    group.emit(0, 1)

    def attend(owner):
        rows = group.chunk(owner)
        attention_out(owner, group.rows, heads_ref, o3, lse_ref, heads)
        for h in range(heads):
            o_ref[rows, h * HEAD : (h + 1) * HEAD] = o3[h, rows, :]
        return nt(o_ref[rows, :], weight[:, 3 * width :])

    scatter = Scatter(group, stage, land, total, scatter_sems)
    scatter.start(attend)
    group.emit(2, 3)
    for j in range(PARTS):
        rows = slice(j * group.part, (j + 1) * group.part)
        residual = x_ref[group.slab(group.me, j), :].astype(WIDE)
        hidden = residual + scatter.take(j) + vec_ref[2:3, :]
        hidden_ref[rows, :] = hidden
        hat, _ = normalise(hidden)
        second_ref[rows, :] = (hat * vec_ref[3:4, :] + vec_ref[4:5, :]).astype(LOW)
    scatter.done()


def outer_whole(left_ref, right_ref, out_ref):
    @pl.loop(0, left_ref.shape[1] // TILE)
    def _(n):
        rows = pl.ds(pl.multiple_of(n * TILE, TILE), TILE)
        out_ref[rows, :] = tn(left_ref[:, rows], right_ref[...]).astype(LOW)


def widen_kernel(last, group, second_ref, em_ref, eo_ref, bias_ref, *refs):
    if last:
        g_ref, *refs = refs
    full_ref, active_ref, slope_ref, *refs = refs
    if last:
        c_ref, *refs = refs
    expand, gather_sems, local_sems = refs
    halves = Halves((em_ref, eo_ref), expand, local_sems, 0)
    halves.start()
    full_ref[group.chunk(group.me), :] = second_ref[...]
    halves.wait()

    def widen(owner):
        rows = group.chunk(owner)
        t = nn(full_ref[rows, :], expand[...]) + bias_ref[...]
        square = t * t
        bent = jnp.tanh(0.7978845608028654 * t * (1.0 + 0.044715 * square))
        active_ref[rows, :] = (0.5 * t * (1.0 + bent)).astype(LOW)
        slope_ref[rows, :] = (
            0.5 * (1.0 + bent)
            + (0.5 * 0.7978845608028654) * t * (1.0 - bent * bent) * (1.0 + 3 * 0.044715 * square)
        ).astype(LOW)

    Gather(group, full_ref, gather_sems).each(widen)
    if last:
        group.emit(0, 1, 2)
        group.need(4)
        outer_whole(g_ref, active_ref, c_ref)


def outer_halves(left_ref, right_ref, keep_ref, send_ref):
    section = lax.axis_index("section")
    half = right_ref.shape[1] // 2
    for place, out in ((section, keep_ref), (1 - section, send_ref)):
        columns = pl.ds(pl.multiple_of(place * half, half), half)

        @pl.loop(0, left_ref.shape[1] // TILE)
        def _(n):
            rows = pl.ds(pl.multiple_of(n * TILE, TILE), TILE)
            out[rows, :] = tn(left_ref[:, rows], right_ref[:, columns]).astype(LOW)


def contract_kernel(
    group, active_ref, hidden_ref, cm_ref, co_ref, vec_ref, result_ref, full_ref,
    contract, stage, land, total, scatter_sems, gather_sems, local_sems,
):
    halves = Halves((cm_ref, co_ref), contract, local_sems, 0)
    halves.start()
    halves.wait()
    scatter = Scatter(group, stage, land, total, scatter_sems)
    scatter.start(lambda owner: nt(active_ref[group.chunk(owner), :], contract[...]))
    group.need(1)
    gather = Gather(group, full_ref, gather_sems)
    for j in range(PARTS):
        rows = slice(j * group.part, (j + 1) * group.part)
        result = (hidden_ref[rows, :] + scatter.take(j) + vec_ref[5:6, :]).astype(LOW)
        result_ref[rows, :] = result
        full_ref[group.slab(group.me, j), :] = result
        gather.start_part(j)
    gather.each(lambda owner: None)
    scatter.done()


def narrow_grads(group, scatter, full_ref, hidden_ref, vec_ref, grad_ref, low_ref, sums_ref):
    for j in range(PARTS):
        rows = slice(j * group.part, (j + 1) * group.part)
        grad = scatter.take(j)
        hat, scale = normalise(hidden_ref[rows, :])
        own = full_ref[group.slab(group.me, j), :].astype(WIDE)
        out = own + norm_backward(grad, hat, scale, vec_ref[3:4, :])
        grad_ref[rows, :] = out
        low_ref[rows, :] = out.astype(LOW)
        for n, term in enumerate((grad * hat, grad, own, out)):
            sums_ref[n : n + 1, :] += jnp.sum(term, axis=0, keepdims=True)


def bend(rows, full_ref, contract, slope_ref, before, sums_ref):
    grad = (nn(full_ref[rows, :], contract[...]) * slope_ref[rows, :].astype(WIDE)).astype(LOW)
    before[rows, :] = grad
    sums_ref[4:5, :] += jnp.sum(grad.astype(WIDE), axis=0, keepdims=True)


def late_expand_kernel(
    group, active_ref, hidden_ref, cm_ref, co_ref, em_ref, eo_ref, g_ref, slope_ref, second_ref, vec_ref,
    grad_ref, low_ref, sums_ref, e_ref, result,
    contract, expand, before,
    stage_a, land_a, total_a, sems_a, stage, land, total, scatter_sems, local_sems,
):
    first = Halves((cm_ref, co_ref), contract, local_sems, 0)
    then = Halves((em_ref, eo_ref), expand, local_sems, 2)
    first.start()
    then.start()
    sums_ref[...] = jnp.zeros_like(sums_ref)
    first.wait()
    forward = Scatter(group, stage_a, land_a, total_a, sems_a)
    forward.start(lambda owner: nt(active_ref[group.chunk(owner), :], contract[...]))
    group.need(6, 7)

    @pl.loop(0, LENGTH // group.rows)
    def _(n):
        bend(group.chunk(n), g_ref, contract, slope_ref, before, sums_ref)

    then.wait()
    scatter = Scatter(group, stage, land, total, scatter_sems)
    scatter.start(lambda owner: nt(before[group.chunk(owner), :], expand[...]))
    group.need(1)
    for j in range(PARTS):
        rows = slice(j * group.part, (j + 1) * group.part)
        result[rows, :] = (hidden_ref[rows, :] + forward.take(j) + vec_ref[5:6, :]).astype(LOW)
    group.emit(4)
    group.need(8)
    outer_whole(second_ref, before, e_ref)
    group.emit(3)
    narrow_grads(group, scatter, g_ref, hidden_ref, vec_ref, grad_ref, low_ref, sums_ref)
    group.emit(0, 1, 2)
    forward.done()
    scatter.done()


def expand_back_kernel(
    group, g_ref, cm_ref, co_ref, em_ref, eo_ref, slope_ref, active_ref, second_ref, hidden_ref, vec_ref,
    grad_ref, low_ref, sums_ref, ek_ref, es_ref, full_ref, c_ref,
    contract, expand, before, stage, land, total, scatter_sems, gather_sems, local_sems, outer, got, trade_sems,
):
    section = lax.axis_index("section")
    first = Halves((cm_ref, co_ref), contract, local_sems, 0)
    then = Halves((em_ref, eo_ref), expand, local_sems, 2)
    first.start()
    then.start()
    sums_ref[...] = jnp.zeros_like(sums_ref)
    full_ref[group.chunk(group.me), :] = g_ref[...]
    first.wait()
    Gather(group, full_ref, gather_sems).each(
        lambda owner: bend(group.chunk(owner), full_ref, contract, slope_ref, before, sums_ref),
        lambda: group.need(5),
    )
    group.emit(5)
    group.need(6)
    half = active_ref.shape[1] // 2

    def columns(place):
        return pl.ds(pl.multiple_of(place * half, half), half)

    def make(n):
        def tile(rows):
            place = section if n == 0 else 1 - section
            outer[n, rows, :] = tn(full_ref[:, rows], active_ref[:, columns(place)]).astype(LOW)

        return tile

    trade = Trade(outer.at[0], outer.at[1], got, trade_sems)
    trade.start(make(1))
    then.wait()
    scatter = Scatter(group, stage, land, total, scatter_sems)
    scatter.start(lambda owner: nt(before[group.chunk(owner), :], expand[...]))
    group.need(7)
    outer_halves(second_ref, before, ek_ref, es_ref)
    group.emit(3, 4)
    keep = make(0)

    @pl.loop(0, outer.shape[1] // TILE)
    def _(n):
        keep(pl.ds(pl.multiple_of(n * TILE, TILE), TILE))

    group.need(8)
    narrow_grads(group, scatter, full_ref, hidden_ref, vec_ref, grad_ref, low_ref, sums_ref)
    group.emit(0, 1, 2)
    scatter.done()
    trade.finish()
    store = pltpu.make_async_copy(outer.at[0], c_ref, local_sems.at[0])
    store.start()
    store.wait()


def scores_back(group, heads, low_ref, weight, heads_ref, o_ref, lse_ref, full, go3, dots, g3, accs, mixed, gather_sems, first):
    width = o_ref.shape[1]
    picks = (
        lax.broadcasted_iota(jnp.int32, (8, width), 1) // HEAD
        == lax.broadcasted_iota(jnp.int32, (8, width), 0)
    ).astype(WIDE)
    for acc in accs:
        acc[...] = jnp.zeros_like(acc)

    def spread(owner):
        rows = group.chunk(owner)
        grads = nn(full[rows, :], weight[:, 3 * width :]).astype(LOW)
        for h in range(heads):
            go3[h, rows, :] = grads[:, h * HEAD : (h + 1) * HEAD]
        term = grads.astype(WIDE) * o_ref[rows, :].astype(WIDE)
        dots[:, rows] = lax.dot_general(
            picks,
            term,
            (((1,), (1,)), ((), ())),
            precision=lax.Precision.HIGHEST,
            preferred_element_type=WIDE,
        )
        attention_back(owner, group.rows, heads_ref, go3, lse_ref, dots, g3, *accs, heads)

    full[group.chunk(group.me), :] = low_ref[...]
    Gather(group, full, gather_sems).each(spread, first)
    for j in range(3 * heads):
        source = g3[j] if j < heads else accs[j // heads - 1][j % heads].astype(LOW)
        mixed[:, j * HEAD : (j + 1) * HEAD] = source


def outer_out(full, o_ref, outer_ref):
    @pl.loop(0, outer_ref.shape[0] // TILE)
    def _(n):
        rows = pl.ds(pl.multiple_of(n * TILE, TILE), TILE)
        outer_ref[rows, :] = tn(full[:, rows], o_ref[...]).astype(LOW)


def attend_grads(group, scatter, x_ref, grad_ref, vec_ref, mixed, width, out_ref, sums_ref):
    sums_ref[2:3, : 3 * width] = jnp.sum(mixed[...].astype(WIDE), axis=0, keepdims=True)
    for j in range(PARTS):
        rows = slice(j * group.part, (j + 1) * group.part)
        grad = scatter.take(j)
        hat, scale = normalise(x_ref[rows, :].astype(WIDE))
        out = grad_ref[rows, :] + norm_backward(grad, hat, scale, vec_ref[0:1, :])
        out_ref[rows, :] = out.astype(LOW)
        for n, term in enumerate((grad * hat, grad)):
            sums_ref[n : n + 1, :] += jnp.sum(term, axis=0, keepdims=True)


def late_attend_kernel(
    heads, group, low_ref, grad_ref, x_ref, mine_ref, other_ref, normed_ref, heads_ref, o_ref, lse_ref, vec_ref,
    result_ref, y_ref,
    out_ref, sums_ref, results_ref, w_ref,
    weight, full, go3, dots, g3, key_acc, value_acc, mixed, outer, outer_o, late, y_land, stage4,
    stage, land, total, scatter_sems, gather_sems, deliver_sems, y_sems, local_sems,
):
    width = o_ref.shape[1]
    section = lax.axis_index("section")
    halves = Halves((mine_ref, other_ref), weight, local_sems, 0)
    halves.start()
    sums_ref[...] = jnp.zeros_like(sums_ref)
    halves.wait()
    deliver = Deliver(group, stage4, late, deliver_sems)

    def first():
        group.need(6, 7, 8, 10)
        deliver.start(result_ref)

    scores_back(
        group, heads, low_ref, weight, heads_ref, o_ref, lse_ref, full, go3, dots, g3,
        (key_acc, value_acc), mixed, gather_sems, first,
    )
    deliver.done()
    group.need(11)
    results = OneWay([(late, y_land)], [(y_ref, y_land)], y_sems)
    results.start()
    scatter = Scatter(group, stage, land, total, scatter_sems)
    scatter.start(lambda owner: nt(mixed[group.chunk(owner), :], weight[:, : 3 * width]))
    outer_out(full, o_ref, outer_o)
    group.need(5)

    @pl.loop(0, weight.shape[0] // TILE)
    def _(n):
        rows = pl.ds(pl.multiple_of(n * TILE, TILE), TILE)
        outer[rows, : 3 * width] = tn(normed_ref[:, rows], mixed[...]).astype(LOW)
        outer[rows, 3 * width :] = outer_o[rows, :]

    store = pltpu.make_async_copy(outer, w_ref, local_sems.at[2])
    store.start()
    @pl.when(section == 0)
    def _():
        results_ref[section] = turned(y_ref[...]).astype(LOW)

    @pl.when(section == 1)
    def _():
        results_ref[section] = turned(late[...]).astype(LOW)

    group.need(1, 2)
    attend_grads(group, scatter, x_ref, grad_ref, vec_ref, mixed, width, out_ref, sums_ref)
    results.wait()
    results_ref[1 - section] = turned(y_land[...]).astype(LOW)
    scatter.done()
    store.wait()


def scores_back_kernel(
    heads, group, low_ref, mine_ref, other_ref, heads_ref, o_ref, lse_ref, ek_ref, es_ref,
    mixed, outer_ref, e_ref,
    weight, full, go3, dots, g3, key_acc, value_acc, got, gather_sems, local_sems, swap_sems,
):
    swap = push(es_ref, got, swap_sems, 0, 1 - lax.axis_index("section"), "section")
    swap.start()
    halves = Halves((mine_ref, other_ref), weight, local_sems, 0)
    halves.start()
    halves.wait()
    scores_back(
        group, heads, low_ref, weight, heads_ref, o_ref, lse_ref, full, go3, dots, g3,
        (key_acc, value_acc), mixed, gather_sems, lambda: group.need(3, 4, 5),
    )
    group.emit(0)
    outer_out(full, o_ref, outer_ref)
    group.emit(1)
    group.need(6)
    swap.wait()
    add_into(ek_ref, got)
    store = pltpu.make_async_copy(ek_ref, e_ref, local_sems.at[0])
    store.start()
    store.wait()


def attend_back_kernel(
    group, mixed, outer_ref, grad_ref, x_ref, mine_ref, other_ref, normed_ref, vec_ref,
    w_ref, out_ref, sums_ref,
    weight, outer, got, stage, land, total, scatter_sems, local_sems, swap_sems,
):
    width = outer_ref.shape[1]
    section = lax.axis_index("section")
    halves = Halves((mine_ref, other_ref), weight, local_sems, 0)
    halves.start()
    sums_ref[...] = jnp.zeros_like(sums_ref)
    half = weight.shape[1] // 2
    scatter = Scatter(group, stage, land, total, scatter_sems)
    group.need(1, 6)

    def make(n):
        place = section if n == 0 else 1 - section

        def tile(rows):
            @pl.when(place == 0)
            def _():
                outer[n, rows, :] = tn(normed_ref[:, rows], mixed[:, :half]).astype(LOW)

            @pl.when(place == 1)
            def _():
                outer[n, rows, : 3 * width - half] = tn(normed_ref[:, rows], mixed[:, half:]).astype(LOW)
                outer[n, rows, 3 * width - half :] = outer_ref[rows, :]

        return tile

    trade = Trade(outer.at[0], outer.at[1], got, swap_sems)
    trade.start(make(1))
    halves.wait()
    scatter.start(lambda owner: nt(mixed[group.chunk(owner), :], weight[:, : 3 * width]))
    keep = make(0)

    @pl.loop(0, outer.shape[1] // TILE)
    def _(n):
        keep(pl.ds(pl.multiple_of(n * TILE, TILE), TILE))

    group.need(2, 3)
    attend_grads(group, scatter, x_ref, grad_ref, vec_ref, mixed, width, out_ref, sums_ref)
    group.emit(1, 2)
    scatter.done()
    trade.finish()
    store = pltpu.make_async_copy(outer.at[0], w_ref, local_sems.at[2])
    store.start()
    store.wait()


def finish_kernel(
    late_ref, early1_ref, early2_ref, near_hbm, far_hbm, a0_hbm, n0_hbm, a1_hbm, n1_hbm,
    grads_ref, sums_ref, got_late, got_early1, got_early2,
    near_ref, far_ref, a0, n0, a1, n1, mine, stage4, block, land_col, land_x, land_z, send,
    deliver_sems, col_sems, x_sems, z_sems, part_sems, local_sems,
):
    section, row = lax.axis_index("section"), lax.axis_index("row")
    away = 1 - section
    group = Group(near_ref.shape[0])
    width = far_ref.shape[1]
    others = [lax.rem(row + d, land_z.shape[0]) for d in range(1, land_z.shape[0])]
    loads = [
        pltpu.make_async_copy(source, into, local_sems.at[n])
        for n, (source, into) in enumerate(
            (
                (near_hbm, near_ref), (far_hbm, far_ref),
                (a0_hbm, a0), (n0_hbm, n0), (a1_hbm, a1), (n1_hbm, n1),
            )
        )
    ]
    for copy in loads:
        copy.start()
    group.greet(True, True, others)
    parts = OneWay(
        [(late_ref, got_late)], [(early1_ref, got_early1), (early2_ref, got_early2)], part_sems
    )
    parts.start()
    for copy in loads:
        copy.wait()
    deliver = Deliver(group, stage4, mine, deliver_sems)
    deliver.start(near_ref)
    gradients = push(send, grads_ref.at[section], x_sems, 1, away, "section")

    @pl.when(section == 0)
    def _():
        send[...] = turned(far_ref[...]).astype(LOW)
        gradients.start()

    block[...] = jnp.zeros_like(block)
    for layer, (attn, narrow) in enumerate(((a0, n0), (a1, n1))):
        wide = [attn[0:1, :], attn[1:2, :], narrow[3:4, :], narrow[0:1, :], narrow[1:2, :], narrow[2:3, :]]
        for c in range(block.shape[0]):
            columns = slice(c * width, (c + 1) * width)
            for n, term in enumerate(wide):
                block[c, layer, n : n + 1, :] = term[:, columns]
            for n, term in enumerate((attn[2:3, :width], attn[2:3, 2 * width : 3 * width])):
                block[c, layer, 8 + n : 9 + n, :] = term
            for n in range(narrow.shape[1] // width):
                block[c, layer, 10 + n : 11 + n, :] = narrow[4:5, n * width : (n + 1) * width]
    copies = [
        push(block.at[other, :, pl.ds(0, 8)], land_col.at[n], col_sems, n, other)
        for n, other in enumerate((group.peer, group.diag, group.sib))
    ]
    for copy in copies:
        copy.start()
    for copy in copies:
        copy.wait()
    me = group.me
    block[me, :, :8] = block[me, :, :8] + (land_col[0] + (land_col[1] + land_col[2]))
    swap = push(block.at[me, away], land_x, x_sems, 0, away, "section")
    swap.start()
    deliver.done()

    @pl.when(section == 0)
    def _():
        grads_ref[section] = turned(mine[...]).astype(LOW)

    @pl.when(section == 1)
    def _():
        send[...] = turned(mine[...]).astype(LOW)
        gradients.start()
        grads_ref[section] = turned(far_ref[...]).astype(LOW)

    swap.wait()
    land_z[row] = block[me, section] + land_x[...]
    copies = [
        push(land_z.at[row], land_z.at[row], z_sems, n, other, "row")
        for n, other in enumerate(others)
    ]
    for copy in copies:
        copy.start()
    for copy in copies:
        copy.wait()
    result = land_z[0]
    for n in range(1, land_z.shape[0]):
        result = result + land_z[n]
    sums_ref[...] = result
    gradients.wait()
    parts.wait()


def greet_section():
    barrier = pltpu.get_barrier_semaphore()
    other = 1 - lax.axis_index("section")
    pl.semaphore_signal(barrier, inc=1, device_id={"section": other}, device_id_type=MESH)
    pl.semaphore_wait(barrier, 1)


def cross_kernel(up, part_ref, got_ref, sems):
    greet_section()
    pair = [(part_ref, got_ref)]
    part = OneWay(pair, [], sems) if up else OneWay([], pair, sems)
    part.start()
    part.wait()


def write_kernel(*refs):
    late, far_late, early, far_early = [refs[n : n + 3] for n in (0, 3, 6, 9)]
    sums_ref, results_ref, grads_ref, output_ref, *vector_refs = refs[12:24]
    homes, (own, far, low, results, *held, sems, out_sems) = refs[24:29], refs[29:]
    attend, expand, contract, outputs, inputs = held
    stores = [pltpu.make_async_copy(held[n], homes[n], out_sems.at[n]) for n in range(5)]
    length, width = low.shape[2], output_ref.shape[0]
    moves = [
        pltpu.make_async_copy(grads_ref, low, sems.at[6]),
        pltpu.make_async_copy(results_ref, results, sems.at[7]),
    ]
    for move in moves:
        move.start()
    half = early[0].shape[1]
    section = lax.axis_index("section")

    def pairs(which):
        if which == 0:
            firsts = [(early[n], own.at[n, :, pl.ds(0, half)]) for n in range(3)]
            seconds = [(far_early[n], own.at[n, :, pl.ds(half, half)]) for n in range(3)]
        else:
            firsts = [(late[n], own.at[n]) for n in range(3)]
            seconds = [(far_late[n], far.at[n]) for n in range(3)]
        return [
            pltpu.make_async_copy(source, into, sems.at[n])
            for n, (source, into) in enumerate((*firsts, *seconds))
        ]

    @pl.when(section == 0)
    def _():
        for copy in pairs(0):
            copy.start()
        far[...] = jnp.zeros_like(far)

    @pl.when(section == 1)
    def _():
        for copy in pairs(1):
            copy.start()

    moves[0].wait()
    for n in range(2):
        inputs[:, n * length : (n + 1) * length] = low[n].astype(WIDE)
    stores[4].start()
    moves[1].wait()
    for n in range(2):
        outputs[:, n * length : (n + 1) * length] = results[n]
    stores[3].start()

    @pl.when(section == 0)
    def _():
        for copy in pairs(0):
            copy.wait()

    @pl.when(section == 1)
    def _():
        for copy in pairs(1):
            copy.wait()

    contract[...] = own[2].astype(WIDE) + far[2].astype(WIDE)
    stores[2].start()
    expand[...] = own[1].astype(WIDE) + far[1].astype(WIDE)
    stores[1].start()
    first = own[0].astype(WIDE) + far[0].astype(WIDE)
    for j in range(3):
        attend[j] = first[:, j * width : (j + 1) * width]
    stores[0].start()
    corner = first[:, 3 * width :]
    high = corner.astype(LOW)
    output_ref[...] = turned(high) + turned((corner - high.astype(WIDE)).astype(LOW))
    for n in range(6):
        vector_refs[n][...] = sums_ref[n : n + 1, :]
    vector_refs[6][...] = sums_ref[8:10, :][None]
    for n in range(vector_refs[7].shape[1] // width):
        vector_refs[7][:, n * width : (n + 1) * width] = sums_ref[10 + n : 11 + n, :]
    for store in stores:
        store.wait()


VM = pl.BlockSpec(memory_space=pltpu.VMEM)
ANY = pl.BlockSpec(memory_space=pl.ANY)
PAIRS = pltpu.SemaphoreType.DMA((2, 3 * PARTS))
LOCAL = pltpu.SemaphoreType.DMA((4,))


def shape(dims, kind=LOW):
    return jax.ShapeDtypeStruct(dims, kind)


def launch(
    body, number, rows, in_specs, ins, outs, out_specs, scratch, swaps=(), diagonal=False, across=False, late=(),
):
    n_in, n_out, n = len(ins), len(outs), len(swaps)
    held_in = [i for i in range(n_in) if in_specs[i] is VM]
    held_out = [i for i in range(n_out) if out_specs[i] is VM]

    def kernel(*refs):
        refs = list(refs)
        takes, sources = refs[:n_in], refs[n_in : n_in + n]
        gives = refs[n_in + n : n_in + n + n_out]
        lands = refs[n_in + n + n_out : n_in + 2 * n + n_out]
        rest = refs[n_in + 2 * n + n_out :]
        own, rest = rest[: len(scratch)], rest[len(scratch) :]
        in_held, rest = rest[: len(held_in)], rest[len(held_in) :]
        out_held, rest = rest[: len(held_out)], rest[len(held_out) :]
        in_sems, out_sems, swap_sems = rest
        group = Group(rows)
        for k, i in enumerate(held_in):
            group.loads[i] = pltpu.make_async_copy(takes[i], in_held[k], in_sems.at[k])
            group.loads[i].start()
            takes[i] = in_held[k]
        for k, i in enumerate(held_out):
            group.stores[i] = pltpu.make_async_copy(out_held[k], gives[i], out_sems.at[k])
            gives[i] = out_held[k]
        group.greet(n or across, diagonal)
        other = 1 - lax.axis_index("section")
        copies = [
            push(source, land, swap_sems, i, other, "section")
            for i, (source, land) in enumerate(zip(sources, lands))
        ]
        for copy in copies:
            copy.start()
        group.need(*[i for i in held_in if i not in late])
        body(group, *takes, *gives, *own)
        group.emit(*[i for i in held_out if i not in group.begun])
        for copy in copies:
            copy.wait()
        for i in held_out:
            group.stores[i].wait()

    results = pl.pallas_call(
        kernel,
        out_shape=(*outs, *[shape(s.shape, s.dtype) for s in swaps]),
        in_specs=[ANY] * (n_in + n),
        out_specs=(ANY,) * (n_out + n),
        scratch_shapes=[
            *scratch,
            *[pltpu.VMEM(ins[i].shape, ins[i].dtype) for i in held_in],
            *[pltpu.VMEM(outs[i].shape, outs[i].dtype) for i in held_out],
            pltpu.SemaphoreType.DMA((len(held_in),)),
            pltpu.SemaphoreType.DMA((len(held_out),)),
            pltpu.SemaphoreType.DMA((2, max(n, 1))),
        ],
        compiler_params=pltpu.CompilerParams(
            collective_id=number, has_side_effects=True, vmem_limit_bytes=GRANT
        ),
        cost_estimate=pl.CostEstimate(flops=int(3e10), bytes_accessed=30 * MEBI, transcendentals=0),
    )(*ins, *swaps)
    return results[:n_out], results[n_out:]


def start_call(number, tokens, cotangent, small, expand, contract, columns):
    width = small.shape[1]
    size = width * columns
    kinds = small.shape[0]
    outs = (shape((LENGTH, size)), shape((LENGTH, size)), shape((2, columns, kinds, width)), shape(expand.shape), shape(contract.shape))
    low = pltpu.VMEM((columns, width, LENGTH), LOW)
    high = pltpu.VMEM((columns, LENGTH, width), LOW)
    vectors = pltpu.VMEM((columns, kinds, width), LOW)
    return pl.pallas_call(
        start_kernel,
        out_shape=outs,
        in_specs=[ANY] * 5,
        out_specs=(VM, VM, VM, ANY, ANY),
        scratch_shapes=[
            low, high, vectors, vectors, PAIRS, PAIRS,
            pltpu.SemaphoreType.DMA((2, 3 * PARTS + 3)), LOCAL,
        ],
        compiler_params=pltpu.CompilerParams(
            collective_id=number, has_side_effects=True, vmem_limit_bytes=GRANT
        ),
        cost_estimate=pl.CostEstimate(flops=int(3e10), bytes_accessed=30 * MEBI, transcendentals=0),
    )(tokens, cotangent, small, expand, contract)


def attend_call(number, x, pair, vec, bias, rows, width, swaps):
    size = vec.shape[1]
    heads = width // HEAD
    outs = (
        shape((LENGTH, size)),
        shape((3 * heads, LENGTH, HEAD)),
        shape((LENGTH, width)),
        shape((8, LENGTH), WIDE),
        shape((rows, size), WIDE),
        shape((rows, size)),
    )
    scratch = [
        pltpu.VMEM((size, 4 * width), LOW),
        pltpu.VMEM((heads, LENGTH, HEAD), LOW),
        *scatter_scratch(rows, size), LOCAL,
    ]
    return launch(
        functools.partial(attend_kernel, heads),
        number, rows, [VM, ANY, ANY, VM, VM], (x, *pair, vec, bias), outs, (VM,) * 6, scratch, swaps,
    )


def widen_call(number, second, pair, bias, grad, swaps):
    rows, size = second.shape
    wide = bias.shape[1]
    last = grad is not None
    ins, in_specs = [second, *pair, bias], [VM, ANY, ANY, VM]
    outs = [shape((LENGTH, size)), shape((LENGTH, wide)), shape((LENGTH, wide))]
    if last:
        ins, in_specs, outs = ins + [grad], in_specs + [VM], outs + [shape((size, wide))]
    scratch = [pltpu.VMEM((size, wide), LOW), PAIRS, LOCAL]
    return launch(
        functools.partial(widen_kernel, last),
        number, rows, in_specs, ins, outs, (VM,) * len(outs), scratch, swaps, late=(4,),
    )


def contract_call(number, active, hidden, pair, vec, swaps):
    rows, size = hidden.shape
    wide = active.shape[1]
    scratch = [pltpu.VMEM((size, wide), LOW), *scatter_scratch(rows, size), PAIRS, LOCAL]
    return launch(
        contract_kernel, number, rows, [VM, VM, ANY, ANY, VM], (active, hidden, *pair, vec),
        [shape((rows, size)), shape((LENGTH, size))], (VM, VM), scratch, swaps, late=(1,),
    )


def late_expand_call(number, active, hidden, contract, expand, grad, slope, second, vec, swaps):
    rows, size = hidden.shape
    wide = slope.shape[1]
    outs = [
        shape((rows, size), WIDE), shape((rows, size)), shape((8, size), WIDE),
        shape((size, wide)), shape((rows, size)),
    ]
    scratch = [
        pltpu.VMEM((size, wide), LOW),
        pltpu.VMEM((size, wide), LOW),
        pltpu.VMEM((LENGTH, wide), LOW),
        *scatter_scratch(rows, size), *scatter_scratch(rows, size), LOCAL,
    ]
    return launch(
        late_expand_kernel,
        number, rows, [VM, VM, ANY, ANY, ANY, ANY, VM, VM, VM, VM],
        (active, hidden, *contract, *expand, grad, slope, second, vec),
        outs, [VM] * 5, scratch, swaps, late=(1, 6, 7, 8),
    )


def expand_back_call(number, grad, contract, expand, slope, active, second, hidden, vec, swaps):
    rows, size = hidden.shape
    wide = slope.shape[1]
    half = wide // 2
    outs = [
        shape((rows, size), WIDE), shape((rows, size)), shape((8, size), WIDE),
        shape((size, half)), shape((size, half)), shape((LENGTH, size)), shape((size, half)),
    ]
    scratch = [
        pltpu.VMEM((size, wide), LOW),
        pltpu.VMEM((size, wide), LOW),
        pltpu.VMEM((LENGTH, wide), LOW),
        *scatter_scratch(rows, size), PAIRS, LOCAL,
        pltpu.VMEM((2, size, half), LOW), pltpu.VMEM((size, half), LOW),
        pltpu.SemaphoreType.DMA((2, size // TILE)),
    ]
    return launch(
        expand_back_kernel,
        number, rows, [VM, ANY, ANY, ANY, ANY, VM, VM, VM, VM, VM],
        (grad, *contract, *expand, slope, active, second, hidden, vec),
        outs, [VM] * 6 + [ANY], scratch, swaps, False, True, late=(5, 6, 7, 8),
    )


def scores_scratch(size, width, heads):
    return [
        pltpu.VMEM((size, 4 * width), LOW),
        pltpu.VMEM((LENGTH, size), LOW),
        pltpu.VMEM((heads, LENGTH, HEAD), LOW),
        pltpu.VMEM((8, LENGTH), WIDE),
        pltpu.VMEM((heads, LENGTH, HEAD), LOW),
        pltpu.VMEM((heads, LENGTH, HEAD), WIDE),
        pltpu.VMEM((heads, LENGTH, HEAD), WIDE),
    ]


def late_attend_call(number, low, grad, x_own, pair, normed, heads_all, o, lse, vec, result, y, swaps):
    rows, size = grad.shape
    width = o.shape[1]
    heads = width // HEAD
    outs = (shape((rows, size)), shape((8, size), WIDE), shape((2, width, LENGTH)), shape((size, 4 * width)))
    scratch = [
        *scores_scratch(size, width, heads),
        pltpu.VMEM((LENGTH, 3 * width), LOW),
        pltpu.VMEM((size, 4 * width), LOW),
        pltpu.VMEM((size, width), LOW),
        pltpu.VMEM((LENGTH, width), LOW),
        pltpu.VMEM((LENGTH, width), LOW),
        pltpu.VMEM((LENGTH // rows, rows, width), LOW),
        *scatter_scratch(rows, size), PAIRS,
        pltpu.SemaphoreType.DMA((2, 3)), pltpu.SemaphoreType.DMA((2, 2)), LOCAL,
    ]
    return launch(
        functools.partial(late_attend_kernel, heads),
        number, rows, [VM, VM, VM, ANY, ANY, VM, VM, VM, VM, VM, VM, VM],
        (low, grad, x_own, *pair, normed, heads_all, o, lse, vec, result, y),
        outs, (VM, VM, VM, ANY), scratch, swaps, True, True, late=(1, 2, 5, 6, 7, 8, 10, 11),
    )


def scores_back_call(number, low, pair, heads_all, o, lse, keep, send):
    rows, size = low.shape
    width = o.shape[1]
    heads = width // HEAD
    outs = (shape((LENGTH, 3 * width)), shape((size, width)), shape(keep.shape))
    scratch = [
        *scores_scratch(size, width, heads),
        pltpu.VMEM(keep.shape, LOW),
        PAIRS, LOCAL, pltpu.SemaphoreType.DMA((2, 1)),
    ]
    return launch(
        functools.partial(scores_back_kernel, heads),
        number, rows, [VM, ANY, ANY, VM, VM, VM, VM, ANY], (low, *pair, heads_all, o, lse, keep, send),
        outs, (VM, VM, ANY), scratch, (), False, True, late=(3, 4, 5, 6),
    )[0]


def attend_back_call(number, mixed, outer, grad, x_own, pair, normed, vec):
    rows, size = grad.shape
    width = outer.shape[1]
    half = 2 * width
    outs = (shape((size, half)), shape((rows, size)), shape((8, size), WIDE))
    scratch = [
        pltpu.VMEM((size, 4 * width), LOW),
        pltpu.VMEM((2, size, half), LOW),
        pltpu.VMEM((size, half), LOW),
        *scatter_scratch(rows, size), LOCAL, pltpu.SemaphoreType.DMA((2, size // TILE)),
    ]
    return launch(
        attend_back_kernel,
        number, rows, [VM, VM, VM, VM, ANY, ANY, VM, VM],
        (mixed, outer, grad, x_own, *pair, normed, vec), outs, (ANY, VM, VM), scratch, (), False, True,
        late=(1, 2, 3, 6),
    )[0]


def finish_call(number, parts, near, far, sums, row_count):
    rows, size = near.shape
    length, width = far.shape
    columns = length // rows
    outs = (
        shape((2, width, length)),
        shape((16, width), WIDE),
        *[shape(part.shape) for part in parts],
    )
    scratch = [
        pltpu.VMEM(near.shape, LOW),
        pltpu.VMEM(far.shape, LOW),
        *[pltpu.VMEM(s.shape, WIDE) for s in sums],
        pltpu.VMEM((length, width), LOW),
        pltpu.VMEM((columns, rows, width), LOW),
        pltpu.VMEM((columns, 2, 16, width), WIDE),
        pltpu.VMEM((3, 2, 8, width), WIDE),
        pltpu.VMEM((16, width), WIDE),
        pltpu.VMEM((row_count, 16, width), WIDE),
        pltpu.VMEM((width, length), LOW),
        pltpu.SemaphoreType.DMA((2, 3)),
        pltpu.SemaphoreType.DMA((2, 3)),
        pltpu.SemaphoreType.DMA((2, 2)),
        pltpu.SemaphoreType.DMA((2, row_count)),
        pltpu.SemaphoreType.DMA((2, 3)),
        pltpu.SemaphoreType.DMA((6,)),
    ]
    return pl.pallas_call(
        finish_kernel,
        out_shape=outs,
        in_specs=[ANY] * 9,
        out_specs=(VM, VM) + (ANY,) * 3,
        scratch_shapes=scratch,
        compiler_params=pltpu.CompilerParams(
            collective_id=number, has_side_effects=True, vmem_limit_bytes=GRANT
        ),
        cost_estimate=pl.CostEstimate(flops=int(3e10), bytes_accessed=30 * MEBI, transcendentals=0),
    )(*parts, near, far, *sums)


def cross_call(number, up, part):
    return pl.pallas_call(
        functools.partial(cross_kernel, up),
        out_shape=shape(part.shape),
        in_specs=[ANY],
        out_specs=ANY,
        scratch_shapes=[pltpu.SemaphoreType.DMA((2, 1))],
        compiler_params=pltpu.CompilerParams(
            collective_id=number, has_side_effects=True, vmem_limit_bytes=GRANT
        ),
        cost_estimate=pl.CostEstimate(flops=int(1e10), bytes_accessed=10 * MEBI, transcendentals=0),
    )(part)


def write_call(late, far_late, early, far_early, sums, wide, results, grads):
    rows, size = late[0].shape
    _, width, length = grads.shape
    large = (
        shape((3, rows, width), WIDE), shape((rows, size), WIDE), shape((rows, size), WIDE),
        shape((width, 2 * length)), shape((width, 2 * length), WIDE),
    )
    return pl.pallas_call(
        write_kernel,
        out_shape=(
            shape((width, rows), WIDE),
            *[shape((1, width), WIDE)] * 6, shape((1, 2, width), WIDE), shape((1, wide), WIDE), *large,
        ),
        in_specs=[ANY] * 12 + [VM, ANY, ANY],
        out_specs=(VM,) * 9 + (ANY,) * 5,
        scratch_shapes=[pltpu.VMEM((3, rows, size), LOW)] * 2
        + [pltpu.VMEM(grads.shape, LOW), pltpu.VMEM(results.shape, LOW)]
        + [pltpu.VMEM(s.shape, s.dtype) for s in large]
        + [pltpu.SemaphoreType.DMA((8,)), pltpu.SemaphoreType.DMA((5,))],
        compiler_params=pltpu.CompilerParams(vmem_limit_bytes=GRANT),
    )(*late, *far_late, *early, *far_early, sums, results, grads)


def swap_sections(value):
    return lax.ppermute(value, "section", [(0, 1), (1, 0)])


def on_device(
    tokens,
    cotangent,
    first_gain,
    first_shift,
    attend_weight,
    attend_bias,
    output_weight,
    output_bias,
    second_gain,
    second_shift,
    expand_weight,
    expand_bias,
    contract_weight,
    contract_bias,
):
    section = lax.axis_index("section")
    column = lax.axis_index("col")
    first_section = section == 0
    columns = lax.axis_size("col")
    width = tokens.shape[1]
    size = width * columns
    rows = LENGTH // columns

    def pick(early, later):
        return jnp.where(first_section, early, later)

    block_rows = attend_weight.shape[1]
    units = (
        jnp.concatenate(
            [attend_weight[0].reshape(block_rows, 3 * width), output_weight[0].T], axis=1
        ),
        expand_weight[0],
        contract_weight[0].T,
    )
    kept_blocks, sent_blocks = [], []
    for unit in units:
        half = unit.shape[1] // 2
        low, high = unit[:, :half], unit[:, half:]
        kept_blocks.append(pick(low, high))
        sent_blocks.append(pick(high, low))

    small = jnp.concatenate(
        [
            first_gain,
            first_shift,
            output_bias,
            second_gain,
            second_shift,
            contract_bias,
            attend_bias[0],
            expand_bias[0].reshape(-1, width),
        ],
        0,
    )
    filled = small.shape[0]
    small = jnp.pad(small, ((0, -filled % (16 * PARTS)), (0, 0)))
    got_attend = swap_sections(sent_blocks[0])
    got_attend, sent_expand = lax.optimization_barrier((got_attend, sent_blocks[1]))
    x0_full, gy_full, vectors, got_expand, got_contract = start_call(
        1, tokens.T, cotangent, small, sent_expand, units[2], columns
    )

    def gather_blocks(block):
        return lax.all_gather(block, "row", axis=0, tiled=True)

    half = units[2].shape[1] // 2
    mats = [[], []]
    for own, got in ((kept_blocks[0], got_attend), (kept_blocks[1], got_expand)):
        for layer, block in enumerate((pick(own, got), pick(got, own))):
            mats[layer].append(gather_blocks(block))
    mats[0].append(gather_blocks(pick(kept_blocks[2], got_contract[:, half:])))
    mats[1].append(gather_blocks(pick(got_contract, units[2])))
    vectors = vectors.astype(WIDE)
    wide_vectors = jnp.swapaxes(vectors[:, :, :6], 1, 2).reshape(2, 6, size)
    wide_vectors = jnp.pad(wide_vectors, ((0, 0), (0, 2), (0, 0)))
    own_vectors = lax.dynamic_index_in_dim(vectors, column, 1, keepdims=False)
    attend_biases = jnp.stack(
        [own_vectors[:, 6], jnp.zeros_like(own_vectors[:, 6]), own_vectors[:, 7]], 1
    ).reshape(2, 1, 3 * width)
    expand_biases = own_vectors[:, 8:filled].reshape(2, 1, -1)

    def own_rows(full):
        return lax.dynamic_slice_in_dim(full, column * rows, rows, 0)

    def own_features(full):
        return lax.dynamic_slice_in_dim(full, column * width, width, 1)

    attn = (mats[0][0], swap_sections(mats[0][0]))
    x = x0_full
    kept, pairs = [], []
    owns = [own_rows(x0_full)]
    for layer in range(2):
        last = layer == 1
        vec = wide_vectors[layer]
        (normed, heads, o, lse, hidden, second_own), (other,) = attend_call(
            2 + 3 * layer, x, attn, vec, attend_biases[layer], rows, width, [mats[layer][1]]
        )
        expand = (mats[layer][1], other)
        outs, others = widen_call(
            3 + 3 * layer, second_own, expand, expand_biases[layer],
            gy_full if last else None, [] if last else [mats[0][2]],
        )
        second, active, slope = outs[:3]
        contract = (mats[layer][2], mats[layer][2] if last else others[0])
        if last:
            c1 = outs[3]
        pairs.append((attn, expand, contract))
        kept.append((normed, heads, o, lse, hidden, second, active, slope))
        if not last:
            (own, x), others = contract_call(4, active, hidden, contract, vec, [mats[1][0]])
            owns.append(own)
            attn = (mats[1][0], others[0])
    y0 = own_features(x)

    def scatter(total):
        return lax.psum_scatter(total, "row", scatter_dimension=0, tiled=True)

    def tie(value, then):
        return lax.optimization_barrier((value, then))

    attn, expand, contract = pairs[1]
    normed, heads, o, lse, hidden, second, active, slope = kept[1]
    (grad_hidden, low, expand_sums1, e1, result), _ = late_expand_call(
        8, active, hidden, contract, expand, gy_full, slope, second, wide_vectors[1], []
    )
    (gx1_own, attend_sums1, layer_outputs, w1), _ = late_attend_call(
        10, low, grad_hidden, owns[1], attn, normed, heads, o, lse, wide_vectors[1], result, y0, []
    )

    attn, expand, contract = pairs[0]
    normed, heads, o, lse, hidden, second, active, slope = kept[0]
    part_c1 = scatter(c1)
    (grad_hidden, low, expand_sums0, ek0, es0, gx1_full, total_c0), (far_c1,) = expand_back_call(
        12, gx1_own, contract, expand, slope, active, second, hidden, wide_vectors[0], [part_c1]
    )
    part_e1, low = tie(scatter(e1), low)
    mixed, outer, total_e0 = scores_back_call(14, low, attn, heads, o, lse, ek0, es0)
    part_w1, mixed = tie(scatter(w1), mixed)
    gx1_columns, part_e1, mixed = lax.optimization_barrier((own_features(gx1_full), part_e1, mixed))
    far_e1, mixed = tie(cross_call(18, True, part_e1), mixed)
    part_c0, mixed = tie(scatter(total_c0), mixed)
    total_w0, gx0_own, attend_sums0 = attend_back_call(
        15, mixed, outer, grad_hidden, owns[0], attn, normed, wide_vectors[0]
    )
    part_e0, gx0_own = tie(scatter(total_e0), gx0_own)
    input_grads, small_grads, far_w1, far_c0, far_e0 = finish_call(
        16,
        (part_w1, part_c0, part_e0),
        gx0_own,
        gx1_columns,
        (attend_sums0, expand_sums0, attend_sums1, expand_sums1),
        lax.axis_size("row"),
    )

    part_w0, small_grads = tie(scatter(total_w0), small_grads)
    far_w0 = cross_call(17, False, part_w0)
    output_part, *vector_grads, attend_part, expand_part, contract_part, layer_outputs, input_grads = write_call(
        (part_w1, part_e1, part_c1),
        (far_w1, far_e1, far_c1),
        (part_w0, part_e0, part_c0),
        (far_w0, far_e0, far_c0),
        small_grads,
        expand_bias.shape[1],
        layer_outputs,
        input_grads,
    )
    return (
        layer_outputs.T[None],
        input_grads.T[None],
        vector_grads[0],
        vector_grads[1],
        jnp.swapaxes(attend_part, 0, 1)[None],
        vector_grads[6],
        output_part[None],
        vector_grads[2],
        vector_grads[3],
        vector_grads[4],
        expand_part[None],
        vector_grads[7],
        contract_part.T[None],
        vector_grads[5],
    )


def solution(mesh):
    return jax.shard_map(
        on_device,
        mesh=mesh,
        in_specs=(
            P("row", "col"),
            P("row", "col"),
            P("section", "col"),
            P("section", "col"),
            P("section", "row", None, "col"),
            P("section", None, "col"),
            P("section", "col", "row"),
            P("section", "col"),
            P("section", "col"),
            P("section", "col"),
            P("section", "row", "col"),
            P("section", "col"),
            P("section", "col", "row"),
            P("section", "col"),
        ),
        out_specs=(
            P("section", "row", "col"),
            P("section", "row", "col"),
            P("section", "col"),
            P("section", "col"),
            P("section", "row", None, "col"),
            P("section", None, "col"),
            P("section", "col", "row"),
            P("section", "col"),
            P("section", "col"),
            P("section", "col"),
            P("section", "row", "col"),
            P("section", "col"),
            P("section", "col", "row"),
            P("section", "col"),
        ),
        check_vma=False,
    )
```
